32 devices in a mesh: rep: 4 (over z), ctx: 4 (over y, core), shard: 2 (over x).
Axes of the slice: x: 2, y: 2, z: 4, core: 2. Of those that a mesh axis runs over, the one named last changes fastest.
Arguments:
- tokens: bfloat16 [4, 512, 2, 2048], P('rep', 'ctx', 'shard'), may hold values from -6 to 6
- cotangent: bfloat16 [4, 512, 2, 2048], P('rep', 'ctx', 'shard'), may hold values from -6 to 6
- span_order: int32 [4, 2, 8], P('rep', 'shard'), may hold values from 0 to 7, each once within a row
- w_qkv: float32 [2048, 6144], P(('ctx', 'shard')), may hold values from -0.125 to 0.125
- w_out: float32 [2048, 2048], P(('ctx', 'shard')), may hold values from -0.75 to 0.75
- w_up: float32 [2048, 11264], P(('ctx', 'shard')), may hold values from -0.125 to 0.125
- w_down: float32 [5632, 2048], P(('ctx', 'shard')), may hold values from -0.078125 to 0.078125
- norm_params: float32 [7, 2048], replicated, may hold values from -2 to 2, as said below
- m_qkv: float32 [2048, 6144], P(('ctx', 'shard')), may hold values from -64 to 64
- v_qkv: float32 [2048, 6144], P(('ctx', 'shard')), may hold values from 4.096 to 65.536
- m_out: float32 [2048, 2048], P(('ctx', 'shard')), may hold values from -6 to 6
- v_out: float32 [2048, 2048], P(('ctx', 'shard')), may hold values from 0.08192 to 1.2288
- m_up: float32 [2048, 11264], P(('ctx', 'shard')), may hold values from -16 to 16
- v_up: float32 [2048, 11264], P(('ctx', 'shard')), may hold values from 0.32768 to 5.3248
- m_down: float32 [5632, 2048], P(('ctx', 'shard')), may hold values from -24 to 24
- v_down: float32 [5632, 2048], P(('ctx', 'shard')), may hold values from 0.73728 to 12.288
- m_norm: float32 [7, 2048], replicated, may hold values from -80 to 80
- v_norm: float32 [7, 2048], replicated, may hold values from 4.096 to 65.536
Outputs:
- block_output: bfloat16 [4, 512, 2, 2048], P('rep', 'ctx', 'shard')
- input_grad: float32 [4, 512, 2, 2048], P('rep', 'ctx', 'shard')
- new_m_qkv: float32 [2048, 6144], P(('ctx', 'shard'))
- new_v_qkv: float32 [2048, 6144], P(('ctx', 'shard'))
- new_w_qkv: float32 [2048, 6144], P(('ctx', 'shard'))
- new_m_out: float32 [2048, 2048], P(('ctx', 'shard'))
- new_v_out: float32 [2048, 2048], P(('ctx', 'shard'))
- new_w_out: float32 [2048, 2048], P(('ctx', 'shard'))
- new_m_up: float32 [2048, 11264], P(('ctx', 'shard'))
- new_v_up: float32 [2048, 11264], P(('ctx', 'shard'))
- new_w_up: float32 [2048, 11264], P(('ctx', 'shard'))
- new_m_down: float32 [5632, 2048], P(('ctx', 'shard'))
- new_v_down: float32 [5632, 2048], P(('ctx', 'shard'))
- new_w_down: float32 [5632, 2048], P(('ctx', 'shard'))
- new_m_norm: float32 [7, 2048], replicated
- new_v_norm: float32 [7, 2048], replicated
- new_norm_params: float32 [7, 2048], replicated
The draws below stay inside these ranges and needn't reach their ends.
Inputs may be any that keep to these rules, and one draw needn't show every extreme that they name: `span_order`: each row is a permutation of 0 to 7. `norm_params`: rows 0 and 2 lie between 0.4 and 1.6.
All inputs are finite; a program needn't handle non-finite values.
Results may differ from the reference program's by a relative error of at most 0.018.
Values may be sent and summed in bfloat16 or wider, within the bound.
No kernel may reach another device: no remote copies, remote signals or barrier semaphores. Data moves between devices by JAX's collectives and lax.ppermute only.
A program may use at most 832 MiB of HBM per device.

```python
import math
from functools import partial
import jax
import jax.numpy as jnp
from jax import lax

D = 2048
HEADS = 32
HEAD_DIM = 64
FF = 5632
ROTARY = 16
STEP = 10
TOK_DEV = 128
SEQ = 512
SPANS = 8
TOKENS = 4096
N_REP = 4
N_SHARD = 2


def draw_norm_params(key, part):
    key = jax.random.fold_in(key, 11)
    keys = jax.random.split(key, 3)
    gains = jnp.clip(1.0 + 0.2 * jax.random.normal(keys[0], (2, D), jnp.float32), 0.4, 1.6)
    shifts = jnp.clip(0.3 * jax.random.normal(keys[1], (2, D), jnp.float32), -2.0, 2.0)
    biases = jnp.clip(0.5 * jax.random.normal(keys[2], (3, D), jnp.float32), -2.0, 2.0)
    return jnp.stack([gains[0], shifts[0], gains[1], shifts[1], biases[0], biases[1], biases[2]])


def shard_levels(own_key, dims, cuts, low, top_value):
    loudness = 1.0
    for position, parts in cuts:
        draws = jax.random.uniform(jax.random.fold_in(jax.random.fold_in(own_key, 6), position), (parts,), jnp.float32, low / len(cuts), top_value / len(cuts))
        loudness = loudness * jnp.repeat(jnp.exp(draws), dims[position] // parts).reshape((-1,) + (1,) * (len(dims) - 1 - position))
    return loudness


def bell_draw(stream_key, extent, scale, limit, cuts=(), held_as=jnp.bfloat16):
    entries = jax.random.normal(stream_key, extent, jnp.float32) * scale
    if len(cuts) > 0:
        entries = shard_levels(stream_key, extent, cuts, -0.22, 0.18) * entries
    return jnp.clip(entries, min=-limit, max=limit).astype(held_as)


def setup_inputs(seed: int = 0) -> dict:
    key_of = jax.random.split(jax.random.key(seed), 19)
    tokens = bell_draw(key_of[0], (N_REP, SEQ, N_SHARD, D), 1.0, 6.0, ((0, 4), (1, 4), (2, 2)))
    cotangent = bell_draw(key_of[1], (N_REP, SEQ, N_SHARD, D), 1.0, 6.0, ((0, 4), (1, 4), (2, 2)))
    span_order = jax.vmap(lambda own: jax.random.permutation(own, SPANS))(jax.random.split(key_of[2], N_REP * N_SHARD)).reshape((N_REP, N_SHARD, SPANS)).astype(jnp.int32)
    w_qkv = bell_draw(key_of[3], (D, 3 * D), D ** -0.5, 0.125, ((0, 8),), jnp.float32)
    w_out = bell_draw(key_of[4], (D, D), (D * 16 // SEQ) ** -0.5, 0.75, ((0, 8),), jnp.float32)
    w_up = bell_draw(key_of[5], (D, 2 * FF), D ** -0.5, 0.125, ((0, 8),), jnp.float32)
    w_down = bell_draw(key_of[6], (FF, D), FF ** -0.5, 0.078125, ((0, 8),), jnp.float32)
    norm_params = draw_norm_params(jax.random.fold_in(key_of[18], 71), 0)
    m_qkv = bell_draw(key_of[8], (D, 3 * D), (0.16 * TOKENS ** 0.5), 64.0, ((0, 8),), jnp.float32)
    v_qkv = jnp.clip(jnp.exp(math.log(65.536) - 2.7725887 * jax.random.uniform(key_of[9], (D, 3 * D), jnp.float32) ** shard_levels(key_of[9], (D, 3 * D), ((0, 8),), -0.2, 0.2)), 4.096, 65.536)
    m_out = bell_draw(key_of[10], (D, D), (0.022 * TOKENS ** 0.5), 6.0, ((0, 8),), jnp.float32)
    v_out = jnp.clip(jnp.exp(math.log(1.2288) - 2.7080503 * jax.random.uniform(key_of[11], (D, D), jnp.float32) ** shard_levels(key_of[11], (D, D), ((0, 8),), -0.2, 0.2)), 0.08192, 1.2288)
    m_up = bell_draw(key_of[12], (D, 2 * FF), (0.044 * TOKENS ** 0.5), 16.0, ((0, 8),), jnp.float32)
    v_up = jnp.clip(jnp.exp(math.log(5.3248) - 2.7880929 * jax.random.uniform(key_of[13], (D, 2 * FF), jnp.float32) ** shard_levels(key_of[13], (D, 2 * FF), ((0, 8),), -0.2, 0.2)), 0.32768, 5.3248)
    m_down = bell_draw(key_of[14], (FF, D), (0.066 * TOKENS ** 0.5), 24.0, ((0, 8),), jnp.float32)
    v_down = jnp.clip(jnp.exp(math.log(12.288) - 2.8134107 * jax.random.uniform(key_of[15], (FF, D), jnp.float32) ** shard_levels(key_of[15], (FF, D), ((0, 8),), -0.2, 0.2)), 0.73728, 12.288)
    m_norm = bell_draw(key_of[16], (7, D), (0.2 * TOKENS ** 0.5), 80.0, (), jnp.float32)
    v_norm = jnp.clip(jnp.exp(jax.random.uniform(key_of[17], (7, D), jnp.float32, math.log(4.096), math.log(65.536))), 4.096, 65.536)
    return dict(tokens=tokens, cotangent=cotangent, span_order=span_order, w_qkv=w_qkv, w_out=w_out, w_up=w_up, w_down=w_down, norm_params=norm_params, m_qkv=m_qkv, v_qkv=v_qkv, m_out=m_out, v_out=v_out, m_up=m_up, v_up=v_up, m_down=m_down, v_down=v_down, m_norm=m_norm, v_norm=v_norm)


@jax.custom_vjp
def low(v):
    return lax.optimization_barrier(v.astype(jnp.bfloat16)).astype(jnp.float32)

@jax.custom_vjp
def low_back(v):
    return v

def low_keep(v):
    return (low(v), None)

def low_pass(kept, grad):
    return (grad,)

def back_keep(v):
    return (v, None)

def back_low(kept, grad):
    return (low(grad),)
low.defvjp(low_keep, low_pass)
low_back.defvjp(back_keep, back_low)
eps_norm = 1e-05
masked_score = -1e+30
beta_one = 0.9
beta_two = 0.999
adam_eps = 1e-08
weight_decay = 0.1

def matmul(left_rows, right_cols):
    return jnp.dot(left_rows, right_cols, precision=lax.Precision.HIGHEST, preferred_element_type=jnp.float32)

def layer_norm(hidden, gain_row, shift_row):
    centred = hidden - lax.optimization_barrier(jnp.mean(hidden, axis=-1, keepdims=True))
    variance = lax.optimization_barrier(jnp.mean(centred * centred, axis=-1, keepdims=True))
    return centred * lax.rsqrt(variance + eps_norm) * gain_row + shift_row

def rotary_tables(positions):
    exponent = jnp.arange(ROTARY // 2, dtype=jnp.float32)
    inverse = 10000.0 ** (-2.0 * exponent / ROTARY)
    angles = positions.astype(jnp.float32)[:, None] * inverse[None, :]
    return (jnp.cos(angles)[:, None, :], jnp.sin(angles)[:, None, :])

def rotate(values, cosine_table, sine_table):
    half_rot = ROTARY // 2
    lower_half = values[..., :half_rot]
    upper_half = values[..., half_rot:ROTARY]
    return jnp.concatenate([lower_half * cosine_table - upper_half * sine_table, upper_half * cosine_table + lower_half * sine_table, values[..., ROTARY:]], axis=-1)

def head_attention(triple, allowed):
    query_h, key_h, value_h = triple
    scores = low_back(matmul(query_h, key_h.T) * HEAD_DIM ** (-0.5))
    scores = jnp.where(allowed, scores, masked_score)
    prob_rows = low(jax.nn.softmax(scores, axis=-1))
    return matmul(prob_rows, value_h)

def sequence_forward(params, sequence_in, positions):
    w_qkv, w_out, w_up, w_down, norm_params = params
    normed_one = low(layer_norm(sequence_in, norm_params[0], norm_params[1]))
    qkv_linear = low_back(matmul(normed_one, low(w_qkv)) + norm_params[4:7].reshape(-1))
    heads_shape = (SEQ, HEADS, HEAD_DIM)
    cosine_table, sine_table = rotary_tables(positions)
    query_r = low(rotate(qkv_linear[:, :D].reshape(heads_shape), cosine_table, sine_table))
    key_r = low(rotate(qkv_linear[:, D:2 * D].reshape(heads_shape), cosine_table, sine_table))
    value_r = low(qkv_linear[:, 2 * D:].reshape(heads_shape))
    allowed = positions[None, :] <= positions[:, None]
    head_fn = jax.checkpoint(partial(head_attention, allowed=allowed))
    head_outs = lax.map(head_fn, (query_r.transpose(1, 0, 2), key_r.transpose(1, 0, 2), value_r.transpose(1, 0, 2)))
    attended = low(low_back(head_outs.transpose(1, 0, 2).reshape(SEQ, D)))
    branch = low_back(matmul(attended, low(w_out)))
    hidden_one = sequence_in + branch
    normed_two = low(layer_norm(hidden_one, norm_params[2], norm_params[3]))
    gate_up = low_back(matmul(normed_two, low(w_up)))
    act_rows = low(jax.nn.silu(gate_up[:, :FF]) * gate_up[:, FF:])
    return hidden_one + matmul(act_rows, low(w_down))

def adam_update(weight, moment_one, moment_two, grad, step_rate, decay_rate):
    first_new = beta_one * moment_one + (1.0 - beta_one) * grad
    second_new = beta_two * moment_two + (1.0 - beta_two) * grad * grad
    first_hat = first_new / (1.0 - beta_one ** STEP)
    second_hat = second_new / (1.0 - beta_two ** STEP)
    weight_new = weight - step_rate * (first_hat / (jnp.sqrt(second_hat) + adam_eps) + decay_rate * weight)
    return (first_new, second_new, weight_new)

def reference(tokens, cotangent, span_order, w_qkv, w_out, w_up, w_down, norm_params, m_qkv, v_qkv, m_out, v_out, m_up, v_up, m_down, v_down, m_norm, v_norm):
    seq_count = N_REP * N_SHARD
    inputs_all = tokens.astype(jnp.float32).transpose(0, 2, 1, 3).reshape(seq_count, SEQ, D)
    grads_all = cotangent.astype(jnp.float32).transpose(0, 2, 1, 3).reshape(seq_count, SEQ, D)
    orders = span_order.reshape(seq_count, SPANS)
    params = (w_qkv, w_out, w_up, w_down, norm_params)
    half_rows = TOK_DEV // 2
    slot_ids = jnp.arange(SEQ, dtype=jnp.int32)

    def one_sequence(totals, inputs):
        sequence_in, sequence_grad, order_row = inputs
        positions = (order_row[slot_ids // half_rows] * half_rows + slot_ids % half_rows).astype(jnp.int32)
        result, pullback = jax.vjp(lambda weights_in, values_in: sequence_forward(weights_in, values_in, positions), params, sequence_in)
        grad_params, grad_in = pullback(sequence_grad)
        totals = jax.tree.map(jnp.add, totals, grad_params)
        return (totals, (result.astype(jnp.bfloat16), grad_in))
    zero_grads = jax.tree.map(jnp.zeros_like, params)
    totals, (outputs, grads_in) = lax.scan(one_sequence, zero_grads, (inputs_all, grads_all, orders))
    block_output = outputs.reshape(N_REP, N_SHARD, SEQ, D).transpose(0, 2, 1, 3)
    input_grad = grads_in.reshape(N_REP, N_SHARD, SEQ, D).transpose(0, 2, 1, 3)
    g_qkv, g_out, g_up, g_down, g_norm = totals
    mq, vq, wq = adam_update(w_qkv, m_qkv, v_qkv, g_qkv, 0.03, weight_decay)
    mo, vo, wo = adam_update(w_out, m_out, v_out, g_out, 0.2, weight_decay)
    mu_new, vu_new, wu_new = adam_update(w_up, m_up, v_up, g_up, 0.03, weight_decay)
    md, vd, wd_new = adam_update(w_down, m_down, v_down, g_down, 0.02, weight_decay)
    mn, vn, wn = adam_update(norm_params, m_norm, v_norm, g_norm, 0.3, 0.0)
    return (block_output, input_grad, mq, vq, wq, mo, vo, wo, mu_new, vu_new, wu_new, md, vd, wd_new, mn, vn, wn)
```

```python
import functools

import jax
import jax.numpy as jnp
from jax import lax
from jax.experimental import pallas as pl
from jax.experimental.pallas import tpu as pltpu
from jax.sharding import PartitionSpec as P

HEADS = 32
HEAD_DIM = 64
FF = 5632
ROTARY = 16
STEP = 10

eps_norm = 1e-05
masked_score = -1e30
beta_one = 0.9
beta_two = 0.999
adam_eps = 1e-08
weight_decay = 0.1
score_scale = HEAD_DIM ** (-0.5)
FIRST = (((0,), (0,)), ((), ()))
LAST = (((1,), (1,)), ((), ()))
PLAIN = (((1,), (0,)), ((), ()))
bf16 = jnp.bfloat16
f32 = jnp.float32


def dot(a, b, dims):
    return lax.dot_general(a, b, dims, preferred_element_type=f32)


def adam_update(weight, moment_one, moment_two, grad, step_rate, decay_rate):
    first_new = beta_one * moment_one + (1.0 - beta_one) * grad
    second_new = beta_two * moment_two + (1.0 - beta_two) * grad * grad
    first_hat = first_new / (1.0 - beta_one**STEP)
    second_hat = second_new / (1.0 - beta_two**STEP)
    weight_new = weight - step_rate * (
        first_hat / (jnp.sqrt(second_hat) + adam_eps) + decay_rate * weight
    )
    return (first_new, second_new, weight_new)


class Plane:
    def __init__(self):
        self.s_size = lax.axis_size("shard")
        self.ctx_size = lax.axis_size("ctx")
        self.y_size = self.ctx_size // 2
        self.ctx = lax.axis_index("ctx")
        self.s = lax.axis_index("shard")
        self.y = self.ctx // 2
        self.c = self.ctx % 2
        self.blocks = self.ctx_size * self.s_size

    def core(self, x):
        return lax.ppermute(x, "ctx", [(i, i ^ 1) for i in range(self.ctx_size)])

    def along(self, x, axis, step):
        if axis == "y":
            return lax.ppermute(x, "ctx", [(i, i ^ (2 * step)) for i in range(self.ctx_size)])
        return lax.ppermute(x, "shard", [(i, i ^ step) for i in range(self.s_size)])

    def index(self, axis):
        return self.y if axis == "y" else self.s

    def steps(self, flip):
        ys = []
        k = self.y_size // 2
        while k:
            ys.append(("y", k))
            k //= 2
        ss = []
        k = self.s_size // 2
        while k:
            ss.append(("s", k))
            k //= 2
        return ys + ss if flip else ss + ys

    def chip_exchange(self, x, take):
        out = [(self.y, self.s, take(self.y, self.s))]
        for ry in range(self.y_size):
            for rs in range(self.s_size):
                if ry or rs:
                    y, s = self.y ^ ry, self.s ^ rs
                    mask = 2 * ry * self.s_size + rs
                    perm = [(i, i ^ mask) for i in range(self.blocks)]
                    out.append((y, s, lax.ppermute(take(y, s), ("ctx", "shard"), perm)))
        return out

    def sum_all(self, x):
        for axis, step in self.steps(False):
            x = x + self.along(x, axis, step)
        return x + self.core(x)

    def scatter_sum(self, p, flip):
        axes = {"y": 1, "s": 2}
        steps = self.steps(flip)
        kept = got = None
        for n, (axis, step) in enumerate(steps):
            ax = axes[axis]
            bit = (self.index(axis) // step) % 2
            kept = lax.dynamic_slice_in_dim(p, bit * step, step, ax)
            send = lax.dynamic_slice_in_dim(p, (1 - bit) * step, step, ax)
            got = self.along(send, axis, step)
            if n + 1 < len(steps):
                p = (kept.astype(f32) + got.astype(f32)).astype(bf16)
        return kept[:, 0, 0], got[:, 0, 0]

    def gather(self, p, flip):
        axes = {"y": 1, "s": 2}
        p = p[:, None, None]
        for axis, step in reversed(self.steps(flip)):
            ax = axes[axis]
            bit = (self.index(axis) // step) % 2
            got = self.along(p, axis, step)
            first = bit == 0
            p = jnp.concatenate([jnp.where(first, p, got), jnp.where(first, got, p)], ax)
        return p


def chain_sum(parts):
    size = lax.axis_size("rep")
    z = lax.axis_index("rep")
    end = (z == 0) | (z == size - 1)
    n = len(parts)
    first, sums, totals, outs = [None] * n, [None] * n, [None] * n, [None] * n
    for k in range(n + 2):
        if k < n:
            g = parts[k]
            r = lax.ppermute(g, "rep", [(0, 1), (3, 2)])
            sums[k] = lax.reduce_precision(g.astype(f32) + r.astype(f32), 8, 7).astype(bf16)
        j = k - 1
        if 0 <= j < n:
            r = lax.ppermute(sums[j], "rep", [(1, 2), (2, 1)])
            totals[j] = lax.reduce_precision(sums[j].astype(f32) + r.astype(f32), 8, 7).astype(bf16)
        j = k - 2
        if 0 <= j < n:
            r = lax.ppermute(totals[j], "rep", [(1, 0), (2, 3)])
            outs[j] = jnp.where(end, r, totals[j])
    return outs


def attend_kernel(kept_ref, got_ref, bias_ref, cos_ref, sin_ref, prow_ref, pcol_ref, qkv_ref, out_ref, peak_ref, total_ref):
    cos, sin = cos_ref[0], sin_ref[0]
    half = ROTARY // 2
    parts = []
    for i in range(3):
        v = kept_ref[i, 0].astype(f32) + got_ref[i, 0].astype(f32) + bias_ref[i, 0]
        if i < 2:
            a, b = v[:half], v[half:ROTARY]
            v = jnp.concatenate([a * cos - b * sin, b * cos + a * sin, v[ROTARY:]], axis=0)
        v = v.astype(bf16)
        qkv_ref[i, 0] = v
        parts.append(v)
    q, k, v = parts
    scores = dot(k, q, FIRST) * score_scale
    scores = jnp.where(pcol_ref[0] <= prow_ref[0], scores, masked_score)
    peak = jnp.max(scores, axis=0, keepdims=True)
    e = jnp.exp(scores - peak)
    total = jnp.sum(e, axis=0, keepdims=True)
    p = (e / total).astype(bf16)
    out_ref[0] = dot(v, p, PLAIN).astype(bf16)
    peak_ref[0, 0] = peak
    total_ref[0, 0] = total


def attend(kept, got, bias, cos, sin, prow, pcol):
    _, heads, hd, t = kept.shape
    seqs, _, seq = prow.shape
    big = pl.BlockSpec((3, 1, hd, seq), lambda s, h: (0, h, 0, s))
    table = pl.BlockSpec((1, ROTARY // 2, seq), lambda s, h: (s, 0, 0))
    stat = pl.BlockSpec((1, 1, 1, seq), lambda s, h: (s, h, 0, 0))
    return pl.pallas_call(
        attend_kernel,
        grid=(seqs, heads),
        in_specs=[
            big,
            big,
            pl.BlockSpec((3, 1, hd, 1), lambda s, h: (0, h, 0, 0)),
            table,
            table,
            pl.BlockSpec((1, 1, seq), lambda s, h: (s, 0, 0)),
            pl.BlockSpec((1, seq, 1), lambda s, h: (s, 0, 0)),
        ],
        out_specs=[big, pl.BlockSpec((1, hd, seq), lambda s, h: (h, 0, s)), stat, stat],
        out_shape=[
            jax.ShapeDtypeStruct((3, heads, hd, t), bf16),
            jax.ShapeDtypeStruct((heads, hd, t), bf16),
            jax.ShapeDtypeStruct((seqs, heads, 1, seq), f32),
            jax.ShapeDtypeStruct((seqs, heads, 1, seq), f32),
        ],
        compiler_params=pltpu.CompilerParams(vmem_limit_bytes=32 * 1024 * 1024),
        cost_estimate=pl.CostEstimate(
            flops=4 * seqs * heads * seq * seq * hd,
            bytes_accessed=16 * 3 * heads * hd * t,
            transcendentals=seqs * heads * seq * seq,
        ),
    )(kept, got, bias, cos, sin, prow, pcol)


def attend_back_kernel(qkv_ref, dout_ref, peak_ref, total_ref, cos_ref, sin_ref, prow_ref, pcol_ref, out_ref):
    cos, sin = cos_ref[0], sin_ref[0]
    half = ROTARY // 2
    q, k, v = qkv_ref[0, 0], qkv_ref[1, 0], qkv_ref[2, 0]
    dout = dout_ref[0]
    scores = dot(k, q, FIRST) * score_scale
    scores = jnp.where(pcol_ref[0] <= prow_ref[0], scores, masked_score)
    p = jnp.exp(scores - peak_ref[0, 0]) / total_ref[0, 0]
    dp = dot(v, dout, FIRST)
    inner = jnp.sum(p * dp, axis=0, keepdims=True)
    ds = (p * (dp - inner)).astype(bf16)

    def back(x):
        a, b = x[:half], x[half:ROTARY]
        return jnp.concatenate([a * cos + b * sin, b * cos - a * sin, x[ROTARY:]], axis=0)

    out_ref[0, 0] = back(dot(k, ds, PLAIN) * score_scale).astype(bf16)
    out_ref[1, 0] = back(dot(q, ds, LAST) * score_scale).astype(bf16)
    out_ref[2, 0] = dot(dout, p.astype(bf16), LAST).astype(bf16)


def attend_back(qkv, dout, peak, total, cos, sin, prow, pcol):
    _, heads, hd, t = qkv.shape
    seqs, _, seq = prow.shape
    big = pl.BlockSpec((3, 1, hd, seq), lambda s, h: (0, h, 0, s))
    table = pl.BlockSpec((1, ROTARY // 2, seq), lambda s, h: (s, 0, 0))
    stat = pl.BlockSpec((1, 1, 1, seq), lambda s, h: (s, h, 0, 0))
    return pl.pallas_call(
        attend_back_kernel,
        grid=(seqs, heads),
        in_specs=[
            big,
            pl.BlockSpec((1, hd, seq), lambda s, h: (h, 0, s)),
            stat,
            stat,
            table,
            table,
            pl.BlockSpec((1, 1, seq), lambda s, h: (s, 0, 0)),
            pl.BlockSpec((1, seq, 1), lambda s, h: (s, 0, 0)),
        ],
        out_specs=big,
        out_shape=jax.ShapeDtypeStruct((3, heads, hd, t), bf16),
        compiler_params=pltpu.CompilerParams(vmem_limit_bytes=32 * 1024 * 1024),
        cost_estimate=pl.CostEstimate(
            flops=10 * seqs * heads * seq * seq * hd,
            bytes_accessed=16 * 3 * heads * hd * t,
            transcendentals=seqs * heads * seq * seq,
        ),
    )(qkv, dout, peak, total, cos, sin, prow, pcol)


def body(
    tokens,
    cotangent,
    span_order,
    w_qkv,
    w_out,
    w_up,
    w_down,
    norm_params,
    m_qkv,
    v_qkv,
    m_out,
    v_out,
    m_up,
    v_up,
    m_down,
    v_down,
    m_norm,
    v_norm,
):
    at = Plane()
    width = tokens.shape[3]
    rows = tokens.shape[1]
    S, Y, nb = at.s_size, at.y_size, at.blocks
    blk = width // nb
    ffb = FF // nb
    heads = blk // HEAD_DIM
    seq = rows * at.ctx_size
    T = S * seq
    H = T // 2
    first = at.c == 0
    my_block = at.ctx * S + at.s

    def pick(pair_axis_array, axis, which):
        return lax.dynamic_index_in_dim(pair_axis_array, which, axis, keepdims=False)

    def chip_rows(w, lead, unit):
        r = w.shape[0]
        w = w.reshape(r, lead * Y, 2, S * unit)
        a, b = w[:, :, 0], w[:, :, 1]
        mine = jnp.where(first, a, b).astype(bf16).reshape(r, -1)
        theirs = jnp.where(first, b, a).astype(bf16).reshape(r, -1)
        return jnp.concatenate([mine, at.core(theirs)], axis=0)

    wq = chip_rows(w_qkv, 3, blk)
    wo = chip_rows(w_out, 1, blk)
    wu = chip_rows(w_up, 2, ffb)
    wo_own = w_out.astype(bf16)
    wd_own = w_down.astype(bf16)

    order = span_order.reshape(1, -1).astype(f32)
    orders = [(at.s, order)]
    for rs in range(1, S):
        orders.append((at.s ^ rs, lax.ppermute(order, "shard", [(i, i ^ rs) for i in range(S)])))
    order_all = jnp.zeros((S, order.shape[1]), f32)
    for s, o in orders:
        order_all = lax.dynamic_update_slice(order_all, o, (s, 0))
    span = rows // 2
    pos = (order_all[:, :, None] * span + jnp.arange(span, dtype=f32)[None, None, :]).reshape(S, seq)
    prow = pos.reshape(S, 1, seq)
    pcol = pos.reshape(S, seq, 1)
    exponent = jnp.arange(ROTARY // 2, dtype=f32)
    inverse = 10000.0 ** (-2.0 * exponent / ROTARY)
    angles = prow * inverse[None, :, None]
    cos, sin = jnp.cos(angles), jnp.sin(angles)

    norm_cols = norm_params.reshape(7, nb, blk).transpose(1, 2, 0)
    own_cols = pick(norm_cols, 0, my_block)
    other_cols = pick(norm_cols, 0, (at.ctx ^ 1) * S + at.s)
    pair_cols = jnp.concatenate([own_cols, other_cols], axis=0)

    x_rows = tokens.reshape(rows, width)
    x_f = x_rows.astype(f32)
    mean = jnp.mean(x_f, axis=1)
    centred = x_f - mean[:, None]
    inv = lax.rsqrt(jnp.mean(centred * centred, axis=1) + eps_norm)
    stats = jnp.stack([mean, inv])

    def to_columns(take, tail):
        got = at.chip_exchange(None, take)
        buf = jnp.zeros((S, Y) + tail, got[0][2].dtype)
        for y, s, v in got:
            buf = lax.dynamic_update_slice(buf, v[None, None], (s, y) + (0,) * len(tail))
        other = at.core(buf)
        return jnp.stack([jnp.where(first, buf, other), jnp.where(first, other, buf)], axis=2)

    xt = x_rows.T.reshape(Y, 2, S, blk, rows)
    x_all = to_columns(
        lambda y, s: lax.dynamic_slice(xt, (y, 0, s, 0, 0), (1, 2, 1, blk, rows)).reshape(2, blk, rows),
        (2, blk, rows),
    )
    st_all = to_columns(lambda y, s: stats, (2, rows))
    x_all = x_all.transpose(3, 4, 0, 1, 2, 5).reshape(2, blk, T)
    x_own = pick(x_all, 0, at.c).astype(f32)
    x_other = pick(x_all, 0, 1 - at.c).astype(f32)
    st_all = st_all.transpose(3, 0, 1, 2, 4).reshape(2, T)
    mean1, inv1 = st_all[0:1], st_all[1:2]
    x_pair = jnp.concatenate([x_own, x_other], axis=0)
    xn1 = ((x_pair - mean1) * inv1 * pair_cols[:, 0:1] + pair_cols[:, 1:2]).astype(bf16)

    cot = cotangent.reshape(2, rows // 2, width)
    cot_parts = [at.gather(cot[k][None], bool(k))[0] for k in range(2)]
    cot_c = jnp.stack(cot_parts, axis=2)
    cot_o = at.core(cot_c)
    cot_all = jnp.stack([jnp.where(first, cot_c, cot_o), jnp.where(first, cot_o, cot_c)], axis=2)
    cot_all = cot_all.transpose(1, 0, 2, 3, 4, 5).reshape(T, width)

    bias = own_cols[:, 4:7].T.reshape(3, heads, HEAD_DIM, 1)
    halves = (slice(0, H), slice(H, T))
    seqs = (slice(0, S // 2), slice(S // 2, S))
    qkvs, attns, peaks, totals = [], [], [], []
    for k in range(2):
        p = dot(wq, xn1[:, halves[k]], FIRST).astype(bf16).reshape(3, Y, S, blk, H)
        kept, got = at.scatter_sum(p, bool(k))
        sq = seqs[k]
        qkv, attn, peak, total = attend(
            kept.reshape(3, heads, HEAD_DIM, H),
            got.reshape(3, heads, HEAD_DIM, H),
            bias,
            cos[sq],
            sin[sq],
            prow[sq],
            pcol[sq],
        )
        qkvs.append(qkv)
        attns.append(attn.reshape(blk, H))
        peaks.append(peak)
        totals.append(total)

    hiddens = []
    for k in range(2):
        pair = jnp.concatenate([attns[k], at.core(attns[k])], axis=0)
        p = dot(wo, pair, FIRST).astype(bf16).reshape(1, Y, S, blk, H)
        kept, got = at.scatter_sum(p, bool(k))
        hiddens.append(x_own[:, halves[k]] + (kept[0].astype(f32) + got[0].astype(f32)))
    hidden = jnp.concatenate(hiddens, axis=1)
    local_mean = jnp.mean(hidden, axis=0, keepdims=True)
    dev = hidden - local_mean
    moments = jnp.concatenate([local_mean, jnp.sum(dev * dev, axis=0, keepdims=True)], axis=0)
    count = blk
    for axis, step in at.steps(False) + [("core", 1)]:
        other = at.core(moments) if axis == "core" else at.along(moments, axis, step)
        gap = moments[0:1] - other[0:1]
        moments = jnp.concatenate(
            [
                0.5 * (moments[0:1] + other[0:1]),
                moments[1:2] + other[1:2] + gap * gap * (count / 2.0),
            ],
            axis=0,
        )
        count *= 2
    mean2 = moments[0:1]
    inv2 = lax.rsqrt(moments[1:2] / width + eps_norm)
    z2 = (hidden - mean2) * inv2
    xn2_own = (z2 * own_cols[:, 2:3] + own_cols[:, 3:4]).astype(bf16)
    xn2 = jnp.concatenate([xn2_own, at.core(xn2_own)], axis=0)

    acts, ggus = [], []
    for k in range(2):
        p = dot(wu, xn2[:, halves[k]], FIRST).astype(bf16).reshape(2, Y, S, ffb, H)
        kept, got = at.scatter_sum(p, bool(k))
        gate = kept[0].astype(f32) + got[0].astype(f32)
        up = kept[1].astype(f32) + got[1].astype(f32)
        sig = jax.nn.sigmoid(gate)
        silu = gate * sig
        acts.append((silu * up).astype(bf16))
        grad_act = dot(wd_own, cot_all[halves[k]], LAST)
        grad_gate = grad_act * up * sig * (1.0 + gate * (1.0 - sig))
        ggus.append(jnp.stack([grad_gate, grad_act * silu]).astype(bf16))
    act = jnp.concatenate(acts, axis=1)
    g_down = dot(act, cot_all, PLAIN).astype(bf16)

    ggu = jnp.concatenate([at.gather(ggus[k], bool(k)) for k in range(2)], axis=4)
    ggu = ggu.reshape(2 * Y * S * ffb, T)
    part = dot(wu, ggu, PLAIN)
    gxn2 = part[:blk] + at.core(part[blk:])
    g_up = dot(xn2, ggu, LAST).astype(bf16)

    def norm_back(grad, z, scale, gain):
        e = grad * gain
        sums = jnp.concatenate(
            [jnp.sum(e, axis=0, keepdims=True), jnp.sum(e * z, axis=0, keepdims=True)], axis=0
        )
        sums = at.sum_all(sums) / width
        return scale * (e - sums[0:1] - z * sums[1:2])

    cot_cols = lax.dynamic_slice_in_dim(cot_all, my_block * blk, blk, 1).T
    grad_hidden = cot_cols.astype(f32) + norm_back(gxn2, z2, inv2, own_cols[:, 2:3])
    grad_branch = grad_hidden.astype(bf16)
    gbrs = [at.gather(grad_branch[:, halves[k]][None], bool(k))[0] for k in range(2)]
    gbr_c = jnp.concatenate(gbrs, axis=3)
    gbr_o = at.core(gbr_c)
    gbr = jnp.stack([jnp.where(first, gbr_c, gbr_o), jnp.where(first, gbr_o, gbr_c)], axis=1)
    gbr = gbr.reshape(width, T)
    attn = jnp.concatenate(attns, axis=1)
    g_out = dot(attn, gbr, LAST).astype(bf16)
    grad_attn = dot(wo_own, gbr, PLAIN).astype(bf16)

    gqkvs = []
    for k in range(2):
        sq = seqs[k]
        gqkvs.append(
            attend_back(
                qkvs[k],
                grad_attn[:, halves[k]].reshape(heads, HEAD_DIM, H),
                peaks[k],
                totals[k],
                cos[sq],
                sin[sq],
                prow[sq],
                pcol[sq],
            ).reshape(3, blk, H)
        )
    gqkv_own = jnp.concatenate(gqkvs, axis=2)
    bias_grad = jnp.sum(gqkv_own.astype(f32), axis=2)
    gqkv = jnp.concatenate([at.gather(gqkvs[k], bool(k)) for k in range(2)], axis=4)
    gqkv = gqkv.reshape(3 * Y * S * blk, T)
    g_qkv = dot(xn1, gqkv, LAST).astype(bf16)
    part = dot(wq, gqkv, PLAIN)
    gxn1 = part[:blk] + at.core(part[blk:])
    z1 = (x_own - mean1) * inv1
    input_grad = grad_hidden + norm_back(gxn1, z1, inv1, own_cols[:, 0:1])

    p = dot(wd_own, act, FIRST).astype(bf16).reshape(Y, 2, S, blk, T)
    theirs = at.core(pick(p, 1, 1 - at.c))
    p = (pick(p, 1, at.c).astype(f32) + theirs.astype(f32)).astype(bf16)[None]
    outs = []
    for k in range(2):
        kept, got = at.scatter_sum(p[..., halves[k]], bool(k))
        outs.append(hiddens[k] + (kept[0].astype(f32) + got[0].astype(f32)))
    out_cols = jnp.concatenate(outs, axis=1).astype(bf16)

    def to_rows(cols):
        split = cols.reshape(blk, S, Y, 2, rows).transpose(1, 2, 3, 0, 4)
        theirs = at.core(pick(split, 2, 1 - at.c))
        mine = pick(split, 2, at.c)
        both = jnp.stack([jnp.where(first, mine, theirs), jnp.where(first, theirs, mine)], axis=2)
        got = at.chip_exchange(
            None,
            lambda y, s: lax.dynamic_slice(both, (s, y, 0, 0, 0), (1, 1, 2, blk, rows)).reshape(2, blk, rows),
        )
        buf = jnp.zeros((Y, 2, S, blk, rows), cols.dtype)
        for y, s, v in got:
            buf = lax.dynamic_update_slice(buf, v[None, :, None], (y, 0, s, 0, 0))
        return buf.reshape(width, rows).T

    block_output = to_rows(out_cols)
    input_rows = to_rows(input_grad)

    def cut(g, n):
        r = g.shape[0] // n
        return [g[i * r : (i + 1) * r] for i in range(n)]

    g_down = jnp.concatenate(chain_sum(cut(g_down, 2)), axis=0)
    g_up = jnp.concatenate(chain_sum(cut(g_up, 4)), axis=0)
    g_out = jnp.concatenate(chain_sum(cut(g_out, 1)), axis=0)
    g_qkv = jnp.concatenate(chain_sum(cut(g_qkv, 4)), axis=0)

    def own_rows(g, lead, unit):
        r = g.shape[0] // 2
        mine = g[:r].reshape(r, lead * Y, S * unit)
        theirs = at.core(g[r:]).reshape(r, lead * Y, S * unit)
        both = jnp.stack([jnp.where(first, mine, theirs), jnp.where(first, theirs, mine)], axis=2)
        return both.reshape(r, -1).astype(f32)

    small = jnp.concatenate(
        [
            jnp.sum(gxn1 * z1, axis=1)[None],
            jnp.sum(gxn1, axis=1)[None],
            jnp.sum(gxn2 * z2, axis=1)[None],
            jnp.sum(gxn2, axis=1)[None],
            bias_grad,
        ],
        axis=0,
    )
    small = small.reshape(7, 1, blk)
    z = lax.axis_index("rep")
    n_rep = lax.axis_size("rep")
    step = 1
    while step < n_rep:
        small = small + lax.ppermute(small, "rep", [(i, i ^ step) for i in range(n_rep)])
        step *= 2
    del z
    got = at.chip_exchange(None, lambda y, s: small)
    buf = jnp.zeros((7, Y, S, blk), f32)
    for y, s, v in got:
        buf = lax.dynamic_update_slice(buf, v[:, None], (0, y, s, 0))
    other = at.core(buf)
    norm_grad = jnp.stack([jnp.where(first, buf, other), jnp.where(first, other, buf)], axis=2)
    norm_grad = norm_grad.reshape(7, width)

    mq, vq, wq_new = adam_update(w_qkv, m_qkv, v_qkv, own_rows(g_qkv, 3, blk), 0.03, weight_decay)
    mo, vo, wo_new = adam_update(w_out, m_out, v_out, g_out.astype(f32), 0.2, weight_decay)
    mu, vu, wu_new = adam_update(w_up, m_up, v_up, own_rows(g_up, 2, ffb), 0.03, weight_decay)
    md, vd, wd_new = adam_update(w_down, m_down, v_down, g_down.astype(f32), 0.02, weight_decay)
    mn, vn, wn = adam_update(norm_params, m_norm, v_norm, norm_grad, 0.3, 0.0)
    return (
        block_output.reshape(tokens.shape),
        input_rows.reshape(tokens.shape),
        mq,
        vq,
        wq_new,
        mo,
        vo,
        wo_new,
        mu,
        vu,
        wu_new,
        md,
        vd,
        wd_new,
        mn,
        vn,
        wn,
    )


def solution(mesh):
    tok = P("rep", "ctx", "shard", None)
    row = P(("ctx", "shard"), None)
    placed = (tok, tok, P("rep", "shard", None)) + (row,) * 4 + (P(),) + (row,) * 8 + (P(), P())
    return jax.shard_map(
        body,
        mesh=mesh,
        in_specs=placed,
        out_specs=(tok, tok) + (row,) * 12 + (P(),) * 3,
        check_vma=False,
    )
```

```python
import functools

import jax
import jax.numpy as jnp
from jax import lax
from jax.experimental import pallas as pl
from jax.experimental.pallas import tpu as pltpu
from jax.sharding import PartitionSpec as P

HEADS = 32
HEAD_DIM = 64
FF = 5632
ROTARY = 16
STEP = 10

eps_norm = 1e-05
masked_score = -1e30
beta_one = 0.9
beta_two = 0.999
adam_eps = 1e-08
weight_decay = 0.1
score_scale = HEAD_DIM ** (-0.5)
FIRST = (((0,), (0,)), ((), ()))
LAST = (((1,), (1,)), ((), ()))
PLAIN = (((1,), (0,)), ((), ()))
bf16 = jnp.bfloat16
f32 = jnp.float32


def dot(a, b, dims):
    return lax.dot_general(a, b, dims, preferred_element_type=f32)


def adam_update(weight, moment_one, moment_two, grad, step_rate, decay_rate):
    first_new = beta_one * moment_one + (1.0 - beta_one) * grad
    second_new = beta_two * moment_two + (1.0 - beta_two) * grad * grad
    first_hat = first_new / (1.0 - beta_one**STEP)
    second_hat = second_new / (1.0 - beta_two**STEP)
    weight_new = weight - step_rate * (
        first_hat / (jnp.sqrt(second_hat) + adam_eps) + decay_rate * weight
    )
    return (first_new, second_new, weight_new)


class Plane:
    def __init__(self):
        self.s_size = lax.axis_size("shard")
        self.ctx_size = lax.axis_size("ctx")
        self.y_size = self.ctx_size // 2
        self.ctx = lax.axis_index("ctx")
        self.s = lax.axis_index("shard")
        self.y = self.ctx // 2
        self.c = self.ctx % 2
        self.blocks = self.ctx_size * self.s_size

    def core(self, x):
        return lax.ppermute(x, "ctx", [(i, i ^ 1) for i in range(self.ctx_size)])

    def along(self, x, axis, step):
        if axis == "y":
            return lax.ppermute(x, "ctx", [(i, i ^ (2 * step)) for i in range(self.ctx_size)])
        return lax.ppermute(x, "shard", [(i, i ^ step) for i in range(self.s_size)])

    def index(self, axis):
        return self.y if axis == "y" else self.s

    def steps(self, flip):
        ys = []
        k = self.y_size // 2
        while k:
            ys.append(("y", k))
            k //= 2
        ss = []
        k = self.s_size // 2
        while k:
            ss.append(("s", k))
            k //= 2
        return ys + ss if flip else ss + ys

    def chip_exchange(self, x, take):
        out = [(self.y, self.s, take(self.y, self.s))]
        for ry in range(self.y_size):
            for rs in range(self.s_size):
                if ry or rs:
                    y, s = self.y ^ ry, self.s ^ rs
                    mask = 2 * ry * self.s_size + rs
                    perm = [(i, i ^ mask) for i in range(self.blocks)]
                    out.append((y, s, lax.ppermute(take(y, s), ("ctx", "shard"), perm)))
        return out

    def sum_all(self, x):
        for axis, step in self.steps(False):
            x = x + self.along(x, axis, step)
        return x + self.core(x)

    def scatter_sum(self, p, flip):
        axes = {"y": 1, "s": 2}
        steps = self.steps(flip)
        kept = got = None
        for n, (axis, step) in enumerate(steps):
            ax = axes[axis]
            bit = (self.index(axis) // step) % 2
            kept = lax.dynamic_slice_in_dim(p, bit * step, step, ax)
            send = lax.dynamic_slice_in_dim(p, (1 - bit) * step, step, ax)
            got = self.along(send, axis, step)
            if n + 1 < len(steps):
                p = (kept.astype(f32) + got.astype(f32)).astype(bf16)
        return kept[:, 0, 0], got[:, 0, 0]

    def gather(self, p, flip):
        axes = {"y": 1, "s": 2}
        p = p[:, None, None]
        for axis, step in reversed(self.steps(flip)):
            ax = axes[axis]
            bit = (self.index(axis) // step) % 2
            got = self.along(p, axis, step)
            first = bit == 0
            p = jnp.concatenate([jnp.where(first, p, got), jnp.where(first, got, p)], ax)
        return p


class Order:
    def __init__(self):
        self.last = None

    def __call__(self, stage, *args):
        if self.last is not None:
            args, self.last = lax.optimization_barrier((args, self.last))
        out = stage(*args)
        self.last = jax.tree.leaves(out)[0]
        return out


class RepSum:
    def __init__(self, order):
        self.order = order
        size = lax.axis_size("rep")
        z = lax.axis_index("rep")
        self.end = (z == 0) | (z == size - 1)
        self.queue = []
        self.one = self.two = self.three = None
        self.done = {}

    def push(self, name, g):
        self.queue.append((name, g))

    def add(self, a, b):
        return self.order(
            lambda a, b: lax.reduce_precision(a.astype(f32) + b.astype(f32), 8, 7).astype(bf16), a, b
        )

    def tick(self):
        if self.three:
            name, total, got = self.three
            self.done[name] = jnp.where(self.end, got, total)
            self.three = None
        if self.two:
            name, part, got = self.two
            total = self.add(part, got)
            self.three = (name, total, lax.ppermute(total, "rep", [(1, 0), (2, 3)]))
            self.two = None
        if self.one:
            name, part, got = self.one
            part = self.add(part, got)
            self.two = (name, part, lax.ppermute(part, "rep", [(1, 2), (2, 1)]))
            self.one = None
        if self.queue:
            name, g = self.queue.pop(0)
            self.one = (name, g, lax.ppermute(g, "rep", [(0, 1), (3, 2)]))

    def drain(self, name):
        while name not in self.done:
            self.tick()
        return self.done[name]


def split_kernel(core_ref, w_ref, mine_ref, theirs_ref):
    unit = mine_ref.shape[1]
    w = w_ref[...].astype(bf16)
    first = core_ref[0] == 0
    a, b = w[:, :unit], w[:, unit:]
    mine_ref[...] = jnp.where(first, a, b)
    theirs_ref[...] = jnp.where(first, b, a)


def split_columns(w, core, lead, unit, count):
    rows = w.shape[0]
    half = pl.BlockSpec((rows, unit), lambda j, core: (0, j))
    out = jax.ShapeDtypeStruct((rows, count * unit), bf16)
    return pl.pallas_call(
        split_kernel,
        grid_spec=pltpu.PrefetchScalarGridSpec(
            num_scalar_prefetch=1,
            grid=(count,),
            in_specs=[pl.BlockSpec((rows, 2 * unit), lambda j, core: (0, lead + j))],
            out_specs=[half, half],
        ),
        out_shape=[out, out],
        compiler_params=pltpu.CompilerParams(vmem_limit_bytes=32 * 1024 * 1024),
        cost_estimate=pl.CostEstimate(flops=0, bytes_accessed=12 * rows * count * unit, transcendentals=0),
    )(core, w)


def adam_kernel(rate, core_ref, w_ref, m_ref, v_ref, mine_ref, theirs_ref, new_m_ref, new_v_ref, new_w_ref):
    mine = core_ref[0] == pl.program_id(2)
    grad = jnp.where(mine, mine_ref[...], theirs_ref[...]).astype(f32)
    new_m, new_v, new_w = adam_update(w_ref[...], m_ref[...], v_ref[...], grad, rate, weight_decay)
    new_m_ref[...] = new_m
    new_v_ref[...] = new_v
    new_w_ref[...] = new_w


def adam_columns(w, m, v, mine, theirs, core, unit, rate):
    rows, width = w.shape
    rb = min(rows, 128)
    whole = pl.BlockSpec((rb, unit), lambda i, g, j, core: (i, 2 * g + j))
    half = pl.BlockSpec((rb, unit), lambda i, g, j, core: (i, g))
    out = jax.ShapeDtypeStruct((rows, width), f32)
    return pl.pallas_call(
        functools.partial(adam_kernel, rate),
        grid_spec=pltpu.PrefetchScalarGridSpec(
            num_scalar_prefetch=1,
            grid=(rows // rb, width // (2 * unit), 2),
            in_specs=[whole, whole, whole, half, half],
            out_specs=[whole, whole, whole],
        ),
        out_shape=[out, out, out],
        compiler_params=pltpu.CompilerParams(vmem_limit_bytes=32 * 1024 * 1024),
        cost_estimate=pl.CostEstimate(flops=20 * rows * width, bytes_accessed=28 * rows * width, transcendentals=0),
    )(core, w, m, v, mine, theirs)


def attend_kernel(kept_ref, got_ref, bias_ref, cos_ref, sin_ref, prow_ref, pcol_ref, qkv_ref, out_ref, peak_ref, total_ref):
    cos, sin = cos_ref[0], sin_ref[0]
    half = ROTARY // 2
    parts = []
    for i in range(3):
        v = kept_ref[i, 0].astype(f32) + got_ref[i, 0].astype(f32) + bias_ref[i, 0]
        if i < 2:
            a, b = v[:half], v[half:ROTARY]
            v = jnp.concatenate([a * cos - b * sin, b * cos + a * sin, v[ROTARY:]], axis=0)
        v = v.astype(bf16)
        qkv_ref[i, 0] = v
        parts.append(v)
    q, k, v = parts
    scores = dot(k, q, FIRST) * score_scale
    scores = jnp.where(pcol_ref[0] <= prow_ref[0], scores, masked_score)
    peak = jnp.max(scores, axis=0, keepdims=True)
    e = jnp.exp(scores - peak)
    total = jnp.sum(e, axis=0, keepdims=True)
    p = (e / total).astype(bf16)
    out_ref[0] = dot(v, p, PLAIN).astype(bf16)
    peak_ref[0, 0] = peak
    total_ref[0, 0] = total


def attend(kept, got, bias, cos, sin, prow, pcol):
    _, heads, hd, t = kept.shape
    seqs, _, seq = prow.shape
    big = pl.BlockSpec((3, 1, hd, seq), lambda s, h: (0, h, 0, s))
    table = pl.BlockSpec((1, ROTARY // 2, seq), lambda s, h: (s, 0, 0))
    stat = pl.BlockSpec((1, 1, 1, seq), lambda s, h: (s, h, 0, 0))
    return pl.pallas_call(
        attend_kernel,
        grid=(seqs, heads),
        in_specs=[
            big,
            big,
            pl.BlockSpec((3, 1, hd, 1), lambda s, h: (0, h, 0, 0)),
            table,
            table,
            pl.BlockSpec((1, 1, seq), lambda s, h: (s, 0, 0)),
            pl.BlockSpec((1, seq, 1), lambda s, h: (s, 0, 0)),
        ],
        out_specs=[big, pl.BlockSpec((1, hd, seq), lambda s, h: (h, 0, s)), stat, stat],
        out_shape=[
            jax.ShapeDtypeStruct((3, heads, hd, t), bf16),
            jax.ShapeDtypeStruct((heads, hd, t), bf16),
            jax.ShapeDtypeStruct((seqs, heads, 1, seq), f32),
            jax.ShapeDtypeStruct((seqs, heads, 1, seq), f32),
        ],
        compiler_params=pltpu.CompilerParams(vmem_limit_bytes=32 * 1024 * 1024),
        cost_estimate=pl.CostEstimate(
            flops=4 * seqs * heads * seq * seq * hd,
            bytes_accessed=16 * 3 * heads * hd * t,
            transcendentals=seqs * heads * seq * seq,
        ),
    )(kept, got, bias, cos, sin, prow, pcol)


def attend_back_kernel(qkv_ref, dout_ref, peak_ref, total_ref, cos_ref, sin_ref, prow_ref, pcol_ref, out_ref):
    cos, sin = cos_ref[0], sin_ref[0]
    half = ROTARY // 2
    q, k, v = qkv_ref[0, 0], qkv_ref[1, 0], qkv_ref[2, 0]
    dout = dout_ref[0]
    scores = dot(k, q, FIRST) * score_scale
    scores = jnp.where(pcol_ref[0] <= prow_ref[0], scores, masked_score)
    p = jnp.exp(scores - peak_ref[0, 0]) / total_ref[0, 0]
    dp = dot(v, dout, FIRST)
    inner = jnp.sum(p * dp, axis=0, keepdims=True)
    ds = (p * (dp - inner)).astype(bf16)

    def back(x):
        a, b = x[:half], x[half:ROTARY]
        return jnp.concatenate([a * cos + b * sin, b * cos - a * sin, x[ROTARY:]], axis=0)

    out_ref[0, 0] = back(dot(k, ds, PLAIN) * score_scale).astype(bf16)
    out_ref[1, 0] = back(dot(q, ds, LAST) * score_scale).astype(bf16)
    out_ref[2, 0] = dot(dout, p.astype(bf16), LAST).astype(bf16)


def attend_back(qkv, dout, peak, total, cos, sin, prow, pcol):
    _, heads, hd, t = qkv.shape
    seqs, _, seq = prow.shape
    big = pl.BlockSpec((3, 1, hd, seq), lambda s, h: (0, h, 0, s))
    table = pl.BlockSpec((1, ROTARY // 2, seq), lambda s, h: (s, 0, 0))
    stat = pl.BlockSpec((1, 1, 1, seq), lambda s, h: (s, h, 0, 0))
    return pl.pallas_call(
        attend_back_kernel,
        grid=(seqs, heads),
        in_specs=[
            big,
            pl.BlockSpec((1, hd, seq), lambda s, h: (h, 0, s)),
            stat,
            stat,
            table,
            table,
            pl.BlockSpec((1, 1, seq), lambda s, h: (s, 0, 0)),
            pl.BlockSpec((1, seq, 1), lambda s, h: (s, 0, 0)),
        ],
        out_specs=big,
        out_shape=jax.ShapeDtypeStruct((3, heads, hd, t), bf16),
        compiler_params=pltpu.CompilerParams(vmem_limit_bytes=32 * 1024 * 1024),
        cost_estimate=pl.CostEstimate(
            flops=10 * seqs * heads * seq * seq * hd,
            bytes_accessed=16 * 3 * heads * hd * t,
            transcendentals=seqs * heads * seq * seq,
        ),
    )(qkv, dout, peak, total, cos, sin, prow, pcol)


def body(
    tokens,
    cotangent,
    span_order,
    w_qkv,
    w_out,
    w_up,
    w_down,
    norm_params,
    m_qkv,
    v_qkv,
    m_out,
    v_out,
    m_up,
    v_up,
    m_down,
    v_down,
    m_norm,
    v_norm,
):
    at = Plane()
    do = Order()
    reps = RepSum(do)
    width = tokens.shape[3]
    rows = tokens.shape[1]
    S, Y, nb = at.s_size, at.y_size, at.blocks
    blk = width // nb
    ffb = FF // nb
    heads = blk // HEAD_DIM
    seq = rows * at.ctx_size
    T = S * seq
    H = T // 2
    first = at.c == 0
    core = at.c.reshape(1)
    my_block = at.ctx * S + at.s
    halves = (slice(0, H), slice(H, T))
    seqs = (slice(0, S // 2), slice(S // 2, S))

    def pick(x, axis, which):
        return lax.dynamic_index_in_dim(x, which, axis, keepdims=False)

    def in_order(mine, theirs, axis):
        return jnp.stack([jnp.where(first, mine, theirs), jnp.where(first, theirs, mine)], axis=axis)

    x_rows = tokens.reshape(rows, width)
    xt = do(lambda x: x.T.reshape(Y, 2, S, blk, rows), x_rows)
    x_got = at.chip_exchange(
        None, lambda y, s: lax.dynamic_slice(xt, (y, 0, s, 0, 0), (1, 2, 1, blk, rows)).reshape(2, blk, rows)
    )

    def row_stats(x):
        x = x.astype(f32)
        mean = jnp.mean(x, axis=1)
        centred = x - mean[:, None]
        return jnp.stack([mean, lax.rsqrt(jnp.mean(centred * centred, axis=1) + eps_norm)])

    stats = do(row_stats, x_rows)
    st_got = at.chip_exchange(None, lambda y, s: stats)
    order = span_order.reshape(1, -1).astype(f32)
    orders = [(at.s, order)]
    for rs in range(1, S):
        orders.append((at.s ^ rs, lax.ppermute(order, "shard", [(i, i ^ rs) for i in range(S)])))

    def chip_rows(w, lead, unit, count):
        mine, theirs = do(lambda w: split_columns(w, core, lead, unit, count), w)
        return mine, at.core(theirs)

    wq_mine, wq_got = chip_rows(w_qkv, 0, S * blk, 3 * Y)

    norm_cols = norm_params.reshape(7, nb, blk).transpose(1, 2, 0)
    own_cols = pick(norm_cols, 0, my_block)
    other_cols = pick(norm_cols, 0, (at.ctx ^ 1) * S + at.s)
    pair_cols = jnp.concatenate([own_cols, other_cols], axis=0)
    bias = own_cols[:, 4:7].T.reshape(3, heads, HEAD_DIM, 1)

    def place(got, tail):
        buf = jnp.zeros((S, Y) + tail, got[0][2].dtype)
        for y, s, v in got:
            buf = lax.dynamic_update_slice(buf, v[None, None], (s, y) + (0,) * len(tail))
        return buf

    x_buf, st_buf = do(
        lambda x, st: (place(x, (2, blk, rows)), place(st, (2, rows))), x_got, st_got
    )
    x_other, st_other = at.core(x_buf), at.core(st_buf)
    cot = cotangent.reshape(2, rows // 2, width)
    cot0, cot1, _ = lax.optimization_barrier((cot[0], cot[1], x_buf))
    cot_parts = [at.gather(v[None], bool(k))[0] for k, v in enumerate((cot0, cot1))]
    wq = do(lambda a, b: jnp.concatenate([a, b], axis=0), wq_mine, wq_got)

    def first_norm(mine, theirs, st_mine, st_theirs, cols):
        x = in_order(mine, theirs, 2).transpose(3, 4, 0, 1, 2, 5).reshape(2, blk, T)
        st = in_order(st_mine, st_theirs, 2).transpose(3, 0, 1, 2, 4).reshape(2, T)
        x_own = pick(x, 0, at.c)
        x_pair = jnp.concatenate([x_own, pick(x, 0, 1 - at.c)], axis=0).astype(f32)
        xn = ((x_pair - st[0:1]) * st[1:2] * cols[:, 0:1] + cols[:, 1:2]).astype(bf16)
        return xn, x_own, st

    xn1, x_own, st = do(first_norm, x_buf, x_other, st_buf, st_other, pair_cols)
    mean1, inv1 = st[0:1], st[1:2]

    def split_send(p, flip):
        axis, step = at.steps(flip)[0]
        ax = {"y": 1, "s": 2}[axis]
        bit = (at.index(axis) // step) % 2
        send = lax.dynamic_slice_in_dim(p, (1 - bit) * step, step, ax)
        return lax.dynamic_slice_in_dim(p, bit * step, step, ax), at.along(send, axis, step)

    def scatter_rest(kept, got, flip):
        for axis, step in at.steps(flip)[1:]:
            ax = {"y": 1, "s": 2}[axis]
            bit = (at.index(axis) // step) % 2
            p = do(lambda a, b: (a.astype(f32) + b.astype(f32)).astype(bf16), kept, got)
            send = lax.dynamic_slice_in_dim(p, (1 - bit) * step, step, ax)
            kept, got = lax.dynamic_slice_in_dim(p, bit * step, step, ax), at.along(send, axis, step)
        return kept[:, 0, 0], got[:, 0, 0]

    flying = []
    for k in range(2):
        p = do(lambda w, x: dot(w, x, FIRST).astype(bf16), wq, xn1[:, halves[k]])
        flying.append(split_send(p.reshape(3, Y, S, blk, H), bool(k)))

    wo_mine, wo_got = chip_rows(w_out, 0, S * blk, Y)
    wg_mine, wg_got = chip_rows(w_up, 0, S * ffb, Y)
    wu_mine, wu_got = chip_rows(w_up, Y, S * ffb, Y)
    wo_own = do(lambda w: w.astype(bf16), w_out)
    wd_own = do(lambda w: w.astype(bf16), w_down)
    wo = do(lambda a, b: jnp.concatenate([a, b], axis=0), wo_mine, wo_got)
    wg = do(lambda a, b: jnp.concatenate([a, b], axis=0), wg_mine, wg_got)
    wu = do(lambda a, b: jnp.concatenate([a, b], axis=0), wu_mine, wu_got)

    def positions(orders):
        order_all = jnp.zeros((S, order.shape[1]), f32)
        for s, o in orders:
            order_all = lax.dynamic_update_slice(order_all, o, (s, 0))
        span = rows // 2
        pos = order_all[:, :, None] * span + jnp.arange(span, dtype=f32)[None, None, :]
        pos = pos.reshape(S, seq)
        prow, pcol = pos.reshape(S, 1, seq), pos.reshape(S, seq, 1)
        exponent = jnp.arange(ROTARY // 2, dtype=f32)
        inverse = 10000.0 ** (-2.0 * exponent / ROTARY)
        angles = prow * inverse[None, :, None]
        return jnp.cos(angles), jnp.sin(angles), prow, pcol

    cos, sin, prow, pcol = do(positions, orders)
    flying = [scatter_rest(*flying[k], bool(k)) for k in range(2)]

    qkvs, attns, attn_got, peaks, totals = [], [], [], [], []
    for k in range(2):
        sq = seqs[k]
        shape = (3, heads, HEAD_DIM, H)
        qkv, attn, peak, total = do(
            attend, flying[k][0].reshape(shape), flying[k][1].reshape(shape), bias, cos[sq], sin[sq], prow[sq], pcol[sq]
        )
        qkvs.append(qkv)
        attns.append(attn.reshape(blk, H))
        attn_got.append(at.core(attns[k]))
        peaks.append(peak)
        totals.append(total)

    flying = []
    for k in range(2):
        p = do(
            lambda w, a, b: dot(w, jnp.concatenate([a, b], axis=0), FIRST).astype(bf16), wo, attns[k], attn_got[k]
        )
        flying.append(split_send(p.reshape(1, Y, S, blk, H), bool(k)))
    flying = [scatter_rest(*flying[k], bool(k)) for k in range(2)]

    def residual(x, a0, b0, a1, b1):
        a, b = jnp.concatenate([a0[0], a1[0]], axis=1), jnp.concatenate([b0[0], b1[0]], axis=1)
        hidden = x.astype(f32) + (a.astype(f32) + b.astype(f32))
        local_mean = jnp.mean(hidden, axis=0, keepdims=True)
        dev = hidden - local_mean
        return hidden, jnp.concatenate([local_mean, jnp.sum(dev * dev, axis=0, keepdims=True)], axis=0)

    hidden, moments = do(residual, x_own, *flying[0], *flying[1])
    count = blk
    for axis, step in at.steps(False) + [("core", 1)]:
        other = at.core(moments) if axis == "core" else at.along(moments, axis, step)
        gap = moments[0:1] - other[0:1]
        moments = jnp.concatenate(
            [0.5 * (moments[0:1] + other[0:1]), moments[1:2] + other[1:2] + gap * gap * (count / 2.0)], axis=0
        )
        count *= 2

    def second_norm(hidden, moments, cols):
        inv2 = lax.rsqrt(moments[1:2] / width + eps_norm)
        z2 = (hidden - moments[0:1]) * inv2
        return (z2 * cols[:, 2:3] + cols[:, 3:4]).astype(bf16), z2, inv2

    xn2_own, z2, inv2 = do(second_norm, hidden, moments, own_cols)
    xn2 = do(lambda a, b: jnp.concatenate([a, b], axis=0), xn2_own, at.core(xn2_own))

    flying = []
    for k, w in enumerate((wg, wu)):
        p = do(lambda w, x: dot(w, x, FIRST).astype(bf16), w, xn2)
        flying.append(split_send(p.reshape(1, Y, S, ffb, T), bool(k)))

    cot_c = do(lambda a, b: jnp.stack([a, b], axis=2), *cot_parts)

    def all_cotangents(mine, theirs):
        return in_order(mine, theirs, 2).transpose(1, 0, 2, 3, 4, 5).reshape(T, width)

    cot_all = do(all_cotangents, cot_c, at.core(cot_c))
    grad_act = do(lambda w, c: dot(w, c, LAST), wd_own, cot_all)
    cot_cols = do(lambda c: lax.dynamic_slice_in_dim(c, my_block * blk, blk, 1).T, cot_all)
    flying = [scatter_rest(*flying[k], bool(k)) for k in range(2)]

    def gated(ga, gb, ua, ub, grad_act):
        gate = ga[0].astype(f32) + gb[0].astype(f32)
        up = ua[0].astype(f32) + ub[0].astype(f32)
        sig = jax.nn.sigmoid(gate)
        silu = gate * sig
        grad_gate = grad_act * up * sig * (1.0 + gate * (1.0 - sig))
        return grad_gate.astype(bf16), (grad_act * silu).astype(bf16), (silu * up).astype(bf16)

    ggate, gup, act = do(gated, *flying[0], *flying[1], grad_act)

    def gather_steps(x, hold=None):
        parts = [x[:, halves[k]][None, None] for k in range(2)]
        n = len(at.steps(False))
        state = {"parts": parts, "got": None}

        def start(i):
            got = []
            for k in range(2):
                axis, step = list(reversed(at.steps(bool(k))))[i]
                got.append((axis, step, at.along(state["parts"][k], axis, step)))
            state["got"] = got

        def finish():
            def join(parts, got):
                out = []
                for k in range(2):
                    axis, step, _ = state["got"][k]
                    ax = {"y": 0, "s": 1}[axis]
                    low = (at.index(axis) // step) % 2 == 0
                    a, b = parts[k], got[k]
                    out.append(jnp.concatenate([jnp.where(low, a, b), jnp.where(low, b, a)], ax))
                return out

            state["parts"] = do(join, state["parts"], [g[2] for g in state["got"]])

        def result():
            return jnp.concatenate(state["parts"], axis=3)

        return n, start, finish, result

    def cut(g, n):
        r = g.shape[0] // n
        return [g[i * r : (i + 1) * r] for i in range(n)]

    n, start, finish, gate_all = gather_steps(ggate)
    start(0)
    g_down = do(lambda a, c: dot(a, c, PLAIN).astype(bf16), act, cot_all)
    for i, g in enumerate(cut(g_down, 4)):
        reps.push(("down", i), g)
    reps.tick()
    out_part = do(lambda w, a: dot(w, a, FIRST).astype(bf16), wd_own, act).reshape(Y, 2, S, blk, T)
    out_theirs = at.core(pick(out_part, 1, 1 - at.c))
    finish()
    for i in range(1, n):
        start(i)
        reps.tick()
        if i < n - 1:
            finish()
    n, start_up, finish_up, up_all = gather_steps(gup)
    out_sum = do(
        lambda a, b: (a.astype(f32) + b.astype(f32)).astype(bf16), pick(out_part, 1, at.c), out_theirs
    )
    finish()
    start_up(0)
    ggate_all = do(lambda x: x.reshape(Y * S * ffb, T), gate_all())
    reps.tick()
    part_gate = do(lambda w, g: dot(w, g, PLAIN), wg, ggate_all)
    g_gate = do(lambda x, g: dot(x, g, LAST).astype(bf16), xn2, ggate_all)
    for i, g in enumerate(reversed(cut(g_gate, 4))):
        reps.push(("gate", 3 - i), g)
    finish_up()
    for i in range(1, n):
        start_up(i)
        reps.tick()
        finish_up()
    gup_all = do(lambda x: x.reshape(Y * S * ffb, T), up_all())
    part = do(lambda w, g, p: dot(w, g, PLAIN) + p, wu, gup_all, part_gate)
    part_theirs = at.core(part[blk:])
    reps.tick()
    gxn2 = do(lambda a, b: a + b, part[:blk], part_theirs)

    def norm_sums(grad, z, gain):
        e = grad * gain
        return jnp.concatenate(
            [jnp.sum(e, axis=0, keepdims=True), jnp.sum(e * z, axis=0, keepdims=True)], axis=0
        )

    def norm_back(grad, z, scale, gain, sums):
        e = grad * gain
        return scale * (e - sums[0:1] / width - z * (sums[1:2] / width))

    sums = at.sum_all(do(norm_sums, gxn2, z2, own_cols[:, 2:3]))
    g_up = do(lambda x, g: dot(x, g, LAST).astype(bf16), xn2, gup_all)
    for i, g in enumerate(reversed(cut(g_up, 4))):
        reps.push(("up", 3 - i), g)

    def branch(cot, grad, z, scale, gain, sums):
        grad_hidden = cot.astype(f32) + norm_back(grad, z, scale, gain, sums)
        return grad_hidden.astype(bf16), grad_hidden

    grad_branch, grad_hidden = do(branch, cot_cols, gxn2, z2, inv2, own_cols[:, 2:3], sums)
    n, start, finish, branch_all = gather_steps(grad_branch)
    for i in range(n):
        start(i)
        if i == 0:
            reps.tick()
        finish()
    gbr_c = do(lambda x: x, branch_all())
    gbr_o = at.core(gbr_c)
    gbr = do(lambda a, b: in_order(a, b, 1).reshape(width, T), gbr_c, gbr_o)
    grad_attn = do(lambda w, g: dot(w, g, PLAIN).astype(bf16), wo_own, gbr)

    gqkvs = []
    for k in range(2):
        sq = seqs[k]
        gqkvs.append(
            do(
                attend_back,
                qkvs[k],
                grad_attn[:, halves[k]].reshape(heads, HEAD_DIM, H),
                peaks[k],
                totals[k],
                cos[sq],
                sin[sq],
                prow[sq],
                pcol[sq],
            ).reshape(3, blk, H)
        )
    gqkv_own = jnp.concatenate(gqkvs, axis=2)
    part = None
    for third in (2, 1, 0):
        n, start, finish, third_all = gather_steps(gqkv_own[third])
        start(0)
        if third == 2:
            attn = jnp.concatenate(attns, axis=1)
            g_out = do(lambda a, g: dot(a, g, LAST).astype(bf16), attn, gbr)
            reps.push(("out", 0), g_out)
        reps.tick()
        finish()
        for i in range(1, n):
            start(i)
            reps.tick()
            finish()
        g_all = do(lambda x: x.reshape(Y * S * blk, T), third_all())
        cols = slice(third * Y * S * blk, (third + 1) * Y * S * blk)
        if part is None:
            part = do(lambda w, g: dot(w, g, PLAIN), wq[:, cols], g_all)
        else:
            part = do(lambda w, g, p: dot(w, g, PLAIN) + p, wq[:, cols], g_all, part)
        g = do(lambda x, g: dot(x, g, LAST).astype(bf16), xn1, g_all)
        for i, g in enumerate(reversed(cut(g, 2))):
            reps.push(("qkv", third, 1 - i), g)

    part_theirs = at.core(part[blk:])
    reps.tick()
    gxn1 = do(lambda a, b: a + b, part[:blk], part_theirs)

    def first_sums(x, st, grad, gain):
        z1 = (x.astype(f32) - st[0:1]) * st[1:2]
        return norm_sums(grad, z1, gain), z1

    sums, z1 = do(first_sums, x_own, st, gxn1, own_cols[:, 0:1])
    sums = at.sum_all(sums)

    def small_grads(gxn1, z1, gxn2, z2, gqkv):
        return jnp.concatenate(
            [
                jnp.sum(gxn1 * z1, axis=1)[None],
                jnp.sum(gxn1, axis=1)[None],
                jnp.sum(gxn2 * z2, axis=1)[None],
                jnp.sum(gxn2, axis=1)[None],
                jnp.sum(gqkv.astype(f32), axis=2),
            ],
            axis=0,
        )

    small = do(small_grads, gxn1, z1, gxn2, z2, gqkv_own)
    n_rep = lax.axis_size("rep")
    step = 1
    while step < n_rep:
        small = small + lax.ppermute(small, "rep", [(i, i ^ step) for i in range(n_rep)])
        step *= 2
    small_got = at.chip_exchange(None, lambda y, s: small)
    reps.tick()
    input_grad = do(
        lambda h, grad, z, scale, gain, sums: h + norm_back(grad, z, scale, gain, sums),
        grad_hidden,
        gxn1,
        z1,
        st[1:2],
        own_cols[:, 0:1],
        sums,
    )

    def to_rows(cols):
        split = cols.reshape(blk, S, Y, 2, rows).transpose(1, 2, 3, 0, 4)
        theirs = at.core(pick(split, 2, 1 - at.c))
        both = in_order(pick(split, 2, at.c), theirs, 2)
        return at.chip_exchange(
            None, lambda y, s: lax.dynamic_slice(both, (s, y, 0, 0, 0), (1, 1, 2, blk, rows)).reshape(2, blk, rows)
        )

    def rows_done(got):
        buf = jnp.zeros((Y, 2, S, blk, rows), got[0][2].dtype)
        for y, s, v in got:
            buf = lax.dynamic_update_slice(buf, v[None, :, None], (y, 0, s, 0, 0))
        return buf.reshape(width, rows).T

    in_got = to_rows(input_grad)

    flying = [split_send(out_sum[None][..., halves[k]], bool(k)) for k in range(2)]
    reps.tick()
    flying = [scatter_rest(*flying[k], bool(k)) for k in range(2)]
    reps.tick()

    def output(hidden, a0, b0, a1, b1):
        a, b = jnp.concatenate([a0[0], a1[0]], axis=1), jnp.concatenate([b0[0], b1[0]], axis=1)
        return (hidden + (a.astype(f32) + b.astype(f32))).astype(bf16)

    out_got = to_rows(do(output, hidden, *flying[0], *flying[1]))
    reps.tick()

    down = [reps.drain(("down", i)) for i in range(4)]
    md, vd, wd_new = do(
        lambda g, *a: adam_update(*a, g.astype(f32), 0.02, weight_decay),
        jnp.concatenate(down, axis=0),
        w_down,
        m_down,
        v_down,
    )
    gates = [reps.drain(("gate", i)) for i in (3, 2, 1, 0)][::-1]
    ups = [reps.drain(("up", i)) for i in (3, 2, 1, 0)][::-1]
    g_up_all = do(
        lambda a, b: jnp.concatenate([jnp.concatenate(a, axis=0), jnp.concatenate(b, axis=0)], axis=1), gates, ups
    )
    r = g_up_all.shape[0] // 2
    got = at.core(g_up_all[r:])
    reps.tick()
    mu, vu, wu_new = do(
        lambda w, m, v, a, b: adam_columns(w, m, v, a, b, core, S * ffb, 0.03), w_up, m_up, v_up, g_up_all[:r], got
    )
    g_out = reps.drain(("out", 0))
    mo, vo, wo_new = do(
        lambda g, *a: adam_update(*a, g.astype(f32), 0.2, weight_decay), g_out, w_out, m_out, v_out
    )
    block_output = do(rows_done, out_got)
    input_rows = do(rows_done, in_got)
    buf = jnp.zeros((7, Y, S, blk), f32)
    for y, s, v in small_got:
        buf = lax.dynamic_update_slice(buf, v.reshape(7, 1, 1, blk), (0, y, s, 0))
    norm_grad = in_order(buf, at.core(buf), 2).reshape(7, width)
    mn, vn, wn = do(lambda *a: adam_update(*a, 0.3, 0.0), norm_params, m_norm, v_norm, norm_grad)

    theirs = [reps.drain(("qkv", third, 1)) for third in (2, 1, 0)][::-1]
    mine = [reps.drain(("qkv", third, 0)) for third in (2, 1, 0)][::-1]
    got = at.core(jnp.concatenate(theirs, axis=1))
    mq, vq, wq_new = do(
        lambda w, m, v, a, b: adam_columns(w, m, v, a, b, core, S * blk, 0.03),
        w_qkv,
        m_qkv,
        v_qkv,
        jnp.concatenate(mine, axis=1),
        got,
    )
    return (
        block_output.reshape(tokens.shape),
        input_rows.reshape(tokens.shape),
        mq,
        vq,
        wq_new,
        mo,
        vo,
        wo_new,
        mu,
        vu,
        wu_new,
        md,
        vd,
        wd_new,
        mn,
        vn,
        wn,
    )


def solution(mesh):
    tok = P("rep", "ctx", "shard", None)
    row = P(("ctx", "shard"), None)
    placed = (tok, tok, P("rep", "shard", None)) + (row,) * 4 + (P(),) + (row,) * 8 + (P(), P())
    return jax.shard_map(
        body,
        mesh=mesh,
        in_specs=placed,
        out_specs=(tok, tok) + (row,) * 12 + (P(),) * 3,
        check_vma=False,
    )
```

```python
import functools

import jax
import jax.numpy as jnp
from jax import lax
from jax.experimental import pallas as pl
from jax.experimental.pallas import tpu as pltpu
from jax.sharding import PartitionSpec as P

HEADS = 32
HEAD_DIM = 64
FF = 5632
ROTARY = 16
STEP = 10

eps_norm = 1e-05
masked_score = -1e30
beta_one = 0.9
beta_two = 0.999
adam_eps = 1e-08
weight_decay = 0.1
score_scale = HEAD_DIM ** (-0.5)
FIRST = (((0,), (0,)), ((), ()))
LAST = (((1,), (1,)), ((), ()))
PLAIN = (((1,), (0,)), ((), ()))
bf16 = jnp.bfloat16
f32 = jnp.float32


def dot(a, b, dims):
    return lax.dot_general(a, b, dims, preferred_element_type=f32)


def adam_update(weight, moment_one, moment_two, grad, step_rate, decay_rate):
    first_new = beta_one * moment_one + (1.0 - beta_one) * grad
    second_new = beta_two * moment_two + (1.0 - beta_two) * grad * grad
    first_hat = first_new / (1.0 - beta_one**STEP)
    second_hat = second_new / (1.0 - beta_two**STEP)
    weight_new = weight - step_rate * (
        first_hat / (jnp.sqrt(second_hat) + adam_eps) + decay_rate * weight
    )
    return (first_new, second_new, weight_new)


class Plane:
    def __init__(self):
        self.s_size = lax.axis_size("shard")
        self.ctx_size = lax.axis_size("ctx")
        self.y_size = self.ctx_size // 2
        self.ctx = lax.axis_index("ctx")
        self.s = lax.axis_index("shard")
        self.y = self.ctx // 2
        self.c = self.ctx % 2
        self.blocks = self.ctx_size * self.s_size

    def core(self, x):
        return lax.ppermute(x, "ctx", [(i, i ^ 1) for i in range(self.ctx_size)])

    def along(self, x, axis, step):
        if axis == "y":
            return lax.ppermute(x, "ctx", [(i, i ^ (2 * step)) for i in range(self.ctx_size)])
        return lax.ppermute(x, "shard", [(i, i ^ step) for i in range(self.s_size)])

    def index(self, axis):
        return self.y if axis == "y" else self.s

    def steps(self, flip):
        ys = []
        k = self.y_size // 2
        while k:
            ys.append(("y", k))
            k //= 2
        ss = []
        k = self.s_size // 2
        while k:
            ss.append(("s", k))
            k //= 2
        return ys + ss if flip else ss + ys

    def chip_exchange(self, x, take):
        out = [(self.y, self.s, take(self.y, self.s))]
        for ry in range(self.y_size):
            for rs in range(self.s_size):
                if ry or rs:
                    y, s = self.y ^ ry, self.s ^ rs
                    mask = 2 * ry * self.s_size + rs
                    perm = [(i, i ^ mask) for i in range(self.blocks)]
                    out.append((y, s, lax.ppermute(take(y, s), ("ctx", "shard"), perm)))
        return out

    def sum_all(self, x):
        for axis, step in self.steps(False):
            x = x + self.along(x, axis, step)
        return x + self.core(x)

    def scatter_sum(self, p, flip):
        axes = {"y": 1, "s": 2}
        steps = self.steps(flip)
        kept = got = None
        for n, (axis, step) in enumerate(steps):
            ax = axes[axis]
            bit = (self.index(axis) // step) % 2
            kept = lax.dynamic_slice_in_dim(p, bit * step, step, ax)
            send = lax.dynamic_slice_in_dim(p, (1 - bit) * step, step, ax)
            got = self.along(send, axis, step)
            if n + 1 < len(steps):
                p = (kept.astype(f32) + got.astype(f32)).astype(bf16)
        return kept[:, 0, 0], got[:, 0, 0]

    def gather(self, p, flip):
        axes = {"y": 1, "s": 2}
        p = p[:, None, None]
        for axis, step in reversed(self.steps(flip)):
            ax = axes[axis]
            bit = (self.index(axis) // step) % 2
            got = self.along(p, axis, step)
            first = bit == 0
            p = jnp.concatenate([jnp.where(first, p, got), jnp.where(first, got, p)], ax)
        return p


class Order:
    def __init__(self):
        self.last = None

    def __call__(self, stage, *args):
        if self.last is not None:
            args, self.last = lax.optimization_barrier((args, self.last))
        out = stage(*args)
        self.last = jax.tree.leaves(out)[0]
        return out


class RepSum:
    def __init__(self, order):
        self.order = order
        z = lax.axis_index("rep")
        self.end = (z == 0) | (z == lax.axis_size("rep") - 1)
        self.queue = []
        self.outer = None
        self.inner = None
        self.done = {}

    def push(self, name, g):
        self.queue.append((name, g))

    def busy(self):
        return bool(self.queue or self.outer or self.inner)

    def tick(self):
        outer, inner = self.outer, self.inner
        new = self.queue.pop(0) if self.queue else None
        values = {}
        if outer and outer["in"]:
            values["g"], values["g_got"] = outer["in"][1], outer["in_got"]
        if outer and outer["out"]:
            values["t"], values["t_got"] = outer["out"][1], outer["out_got"]
        if inner:
            values["s"], values["s_got"] = inner[1], inner[2]
        if new:
            values["new"] = new[1]
        both = new and inner and new[1].shape == inner[1].shape

        def stage(v):
            def add(a, b):
                return lax.reduce_precision(a.astype(f32) + b.astype(f32), 8, 7).astype(bf16)

            out = {}
            if "s" in v:
                out["total"] = add(v["s"], v["s_got"])
            if "g" in v:
                out["sum"] = add(v["g"], v["g_got"])
            if "t" in v:
                out["out"] = jnp.where(self.end, v["t_got"], v["t"])
            if both:
                out["send"] = jnp.where(self.end, v["new"], out["total"])
            elif "new" in v:
                out["new"] = v["new"]
            return out

        out = self.order(stage, values)
        if outer and outer["out"]:
            self.done[outer["out"][0]] = out["out"]
        self.outer = None
        if new or inner:
            o = {"in": None, "out": None}
            if both:
                o["in_got"] = o["out_got"] = lax.ppermute(out["send"], "rep", [(0, 1), (1, 0), (2, 3), (3, 2)])
            else:
                if new:
                    o["in_got"] = lax.ppermute(out["new"], "rep", [(0, 1), (3, 2)])
                if inner:
                    o["out_got"] = lax.ppermute(out["total"], "rep", [(1, 0), (2, 3)])
            if new:
                o["in"] = new
            if inner:
                o["out"] = (inner[0], out["total"])
            self.outer = o
        self.inner = None
        if outer and outer["in"]:
            self.inner = (outer["in"][0], out["sum"], lax.ppermute(out["sum"], "rep", [(1, 2), (2, 1)]))


def split_kernel(core_ref, w_ref, mine_ref, theirs_ref):
    unit = mine_ref.shape[0]
    first = core_ref[0] == 0
    a, b = w_ref[:, :unit], w_ref[:, unit:]
    mine_ref[...] = jnp.where(first, a, b).T.astype(bf16)
    theirs_ref[...] = jnp.where(first, b, a).T.astype(bf16)


def split_columns(w, core, lead, unit, count):
    rows = w.shape[0]
    half = pl.BlockSpec((unit, rows), lambda j, core: (j, 0))
    out = jax.ShapeDtypeStruct((count * unit, rows), bf16)
    return pl.pallas_call(
        split_kernel,
        grid_spec=pltpu.PrefetchScalarGridSpec(
            num_scalar_prefetch=1,
            grid=(count,),
            in_specs=[pl.BlockSpec((rows, 2 * unit), lambda j, core: (0, lead + j))],
            out_specs=[half, half],
        ),
        out_shape=[out, out],
        compiler_params=pltpu.CompilerParams(vmem_limit_bytes=32 * 1024 * 1024),
        cost_estimate=pl.CostEstimate(flops=0, bytes_accessed=12 * rows * count * unit, transcendentals=0),
    )(core, w)


def adam_kernel(rate, two, core_ref, w_ref, m_ref, v_ref, *refs):
    if two:
        mine = core_ref[0] == pl.program_id(1)
        grad = jnp.where(mine, refs[0][...], refs[1][...]).astype(f32)
    else:
        grad = refs[0][...].astype(f32)
    new_m_ref, new_v_ref, new_w_ref = refs[-3:]
    new_m, new_v, new_w = adam_update(w_ref[...], m_ref[...], v_ref[...], grad, rate, weight_decay)
    new_m_ref[...] = new_m
    new_v_ref[...] = new_v
    new_w_ref[...] = new_w


def adam_part(state, grads, core, rate, prev, row_block, col_first, unit):
    w, m, v = state
    two = len(grads) == 2
    rb = grads[0].shape[0]
    count = grads[0].shape[1] // unit
    if two:
        grid = (count, 2)
        whole = pl.BlockSpec((rb, unit), lambda g, j, core: (row_block, 2 * (col_first + g) + j))
        half = pl.BlockSpec((rb, unit), lambda g, j, core: (0, g))
    else:
        grid = (count,)
        whole = pl.BlockSpec((rb, unit), lambda g, core: (row_block, g))
        half = pl.BlockSpec((rb, unit), lambda g, core: (0, g))
    out = jax.ShapeDtypeStruct(w.shape, f32)
    extra, aliases = [], {}
    if prev is not None:
        extra = list(prev)
        aliases = {4 + len(grads) + i: i for i in range(3)}
    n = rb * count * unit * len(grads)
    return pl.pallas_call(
        functools.partial(adam_kernel, rate, two),
        grid_spec=pltpu.PrefetchScalarGridSpec(
            num_scalar_prefetch=1,
            grid=grid,
            in_specs=[whole] * 3 + [half] * len(grads) + [pl.BlockSpec(memory_space=pl.ANY)] * len(extra),
            out_specs=[whole] * 3,
        ),
        out_shape=[out] * 3,
        input_output_aliases=aliases,
        compiler_params=pltpu.CompilerParams(vmem_limit_bytes=32 * 1024 * 1024),
        cost_estimate=pl.CostEstimate(flops=20 * n, bytes_accessed=28 * n, transcendentals=0),
    )(core, w, m, v, *grads, *extra)


def attend_kernel(kept_ref, got_ref, bias_ref, cos_ref, sin_ref, prow_ref, pcol_ref, qkv_ref, out_ref, peak_ref, total_ref):
    cos, sin = cos_ref[0], sin_ref[0]
    half = ROTARY // 2
    parts = []
    for i in range(3):
        v = kept_ref[i, 0].astype(f32) + got_ref[i, 0].astype(f32) + bias_ref[i, 0]
        if i < 2:
            a, b = v[:half], v[half:ROTARY]
            v = jnp.concatenate([a * cos - b * sin, b * cos + a * sin, v[ROTARY:]], axis=0)
        v = v.astype(bf16)
        qkv_ref[i, 0] = v
        parts.append(v)
    q, k, v = parts
    scores = dot(k, q, FIRST) * score_scale
    scores = jnp.where(pcol_ref[0] <= prow_ref[0], scores, masked_score)
    peak = jnp.max(scores, axis=0, keepdims=True)
    e = jnp.exp(scores - peak)
    total = jnp.sum(e, axis=0, keepdims=True)
    p = (e / total).astype(bf16)
    out_ref[0] = dot(v, p, PLAIN).astype(bf16)
    peak_ref[0, 0] = peak
    total_ref[0, 0] = total


def attend(kept, got, bias, cos, sin, prow, pcol):
    _, heads, hd, t = kept.shape
    seqs, _, seq = prow.shape
    big = pl.BlockSpec((3, 1, hd, seq), lambda s, h: (0, h, 0, s))
    table = pl.BlockSpec((1, ROTARY // 2, seq), lambda s, h: (s, 0, 0))
    stat = pl.BlockSpec((1, 1, 1, seq), lambda s, h: (s, h, 0, 0))
    return pl.pallas_call(
        attend_kernel,
        grid=(seqs, heads),
        in_specs=[
            big,
            big,
            pl.BlockSpec((3, 1, hd, 1), lambda s, h: (0, h, 0, 0)),
            table,
            table,
            pl.BlockSpec((1, 1, seq), lambda s, h: (s, 0, 0)),
            pl.BlockSpec((1, seq, 1), lambda s, h: (s, 0, 0)),
        ],
        out_specs=[big, pl.BlockSpec((1, hd, seq), lambda s, h: (h, 0, s)), stat, stat],
        out_shape=[
            jax.ShapeDtypeStruct((3, heads, hd, t), bf16),
            jax.ShapeDtypeStruct((heads, hd, t), bf16),
            jax.ShapeDtypeStruct((seqs, heads, 1, seq), f32),
            jax.ShapeDtypeStruct((seqs, heads, 1, seq), f32),
        ],
        compiler_params=pltpu.CompilerParams(vmem_limit_bytes=32 * 1024 * 1024),
        cost_estimate=pl.CostEstimate(
            flops=4 * seqs * heads * seq * seq * hd,
            bytes_accessed=16 * 3 * heads * hd * t,
            transcendentals=seqs * heads * seq * seq,
        ),
    )(kept, got, bias, cos, sin, prow, pcol)


def attend_back_kernel(qkv_ref, dout_ref, peak_ref, total_ref, cos_ref, sin_ref, prow_ref, pcol_ref, out_ref):
    cos, sin = cos_ref[0], sin_ref[0]
    half = ROTARY // 2
    q, k, v = qkv_ref[0, 0], qkv_ref[1, 0], qkv_ref[2, 0]
    dout = dout_ref[0]
    scores = dot(k, q, FIRST) * score_scale
    scores = jnp.where(pcol_ref[0] <= prow_ref[0], scores, masked_score)
    p = jnp.exp(scores - peak_ref[0, 0]) / total_ref[0, 0]
    dp = dot(v, dout, FIRST)
    inner = jnp.sum(p * dp, axis=0, keepdims=True)
    ds = (p * (dp - inner)).astype(bf16)

    def back(x):
        a, b = x[:half], x[half:ROTARY]
        return jnp.concatenate([a * cos + b * sin, b * cos - a * sin, x[ROTARY:]], axis=0)

    out_ref[0, 0] = back(dot(k, ds, PLAIN) * score_scale).astype(bf16)
    out_ref[1, 0] = back(dot(q, ds, LAST) * score_scale).astype(bf16)
    out_ref[2, 0] = dot(dout, p.astype(bf16), LAST).astype(bf16)


def attend_back(qkv, dout, peak, total, cos, sin, prow, pcol):
    _, heads, hd, t = qkv.shape
    seqs, _, seq = prow.shape
    big = pl.BlockSpec((3, 1, hd, seq), lambda s, h: (0, h, 0, s))
    table = pl.BlockSpec((1, ROTARY // 2, seq), lambda s, h: (s, 0, 0))
    stat = pl.BlockSpec((1, 1, 1, seq), lambda s, h: (s, h, 0, 0))
    return pl.pallas_call(
        attend_back_kernel,
        grid=(seqs, heads),
        in_specs=[
            big,
            pl.BlockSpec((1, hd, seq), lambda s, h: (h, 0, s)),
            stat,
            stat,
            table,
            table,
            pl.BlockSpec((1, 1, seq), lambda s, h: (s, 0, 0)),
            pl.BlockSpec((1, seq, 1), lambda s, h: (s, 0, 0)),
        ],
        out_specs=big,
        out_shape=jax.ShapeDtypeStruct((3, heads, hd, t), bf16),
        compiler_params=pltpu.CompilerParams(vmem_limit_bytes=32 * 1024 * 1024),
        cost_estimate=pl.CostEstimate(
            flops=10 * seqs * heads * seq * seq * hd,
            bytes_accessed=16 * 3 * heads * hd * t,
            transcendentals=seqs * heads * seq * seq,
        ),
    )(qkv, dout, peak, total, cos, sin, prow, pcol)


def body(
    tokens,
    cotangent,
    span_order,
    w_qkv,
    w_out,
    w_up,
    w_down,
    norm_params,
    m_qkv,
    v_qkv,
    m_out,
    v_out,
    m_up,
    v_up,
    m_down,
    v_down,
    m_norm,
    v_norm,
):
    at = Plane()
    do = Order()
    reps = RepSum(do)
    width = tokens.shape[3]
    rows = tokens.shape[1]
    S, Y, nb = at.s_size, at.y_size, at.blocks
    plane = ("ctx", "shard")
    blk = width // nb
    ffb = FF // nb
    heads = blk // HEAD_DIM
    seq = rows * at.ctx_size
    T = S * seq
    H = T // 2
    first = at.c == 0
    core = at.c.reshape(1)
    my_block = at.ctx * S + at.s
    halves = (slice(0, H), slice(H, T))
    seqs = (slice(0, S // 2), slice(S // 2, S))

    def pick(x, axis, which):
        return lax.dynamic_index_in_dim(x, which, axis, keepdims=False)

    def in_order(mine, theirs, axis):
        return jnp.stack([jnp.where(first, mine, theirs), jnp.where(first, theirs, mine)], axis=axis)

    def join(a, b):
        return jnp.concatenate([a, b], axis=0)

    x_rows = tokens.reshape(rows, width)
    order = span_order.reshape(-1).astype(f32)
    span = rows // 2

    def pack(x, order):
        xf = x.astype(f32)
        mean = jnp.mean(xf, axis=1)
        centred = xf - mean[:, None]
        inv = lax.rsqrt(jnp.mean(centred * centred, axis=1) + eps_norm)
        mine = lax.dynamic_slice_in_dim(order, 2 * at.ctx, 2)
        place = jnp.repeat(mine, span)
        terms = []
        for v in (mean, inv):
            for _ in range(3):
                t = lax.reduce_precision(v, 8, 7)
                terms.append(t)
                v = v - t
        extra = jnp.stack(terms + [place] + [jnp.zeros_like(place)] * 9).astype(bf16)
        blocks = x.T.reshape(nb, blk, rows)
        return jnp.concatenate([blocks, jnp.broadcast_to(extra[None], (nb, 16, rows))], axis=1)

    packed = do(pack, x_rows, order)
    got = lax.all_to_all(packed, plane, split_axis=0, concat_axis=0, tiled=True)

    def chip_rows(w, lead, unit, count):
        mine, theirs = do(lambda w: split_columns(w, core, lead, unit, count), w)
        return mine, at.core(theirs)

    def lanes(a, b):
        return jnp.concatenate([a, b], axis=1)

    wq_parts = chip_rows(w_qkv, 0, S * blk, 3 * Y)
    norm_cols = norm_params.reshape(7, nb, blk).transpose(1, 2, 0)
    own_cols = pick(norm_cols, 0, my_block)
    other_cols = pick(norm_cols, 0, (at.ctx ^ 1) * S + at.s)
    pair_cols = join(own_cols, other_cols)
    bias = own_cols[:, 4:7].T.reshape(3, heads, HEAD_DIM, 1)
    wq = do(lanes, *wq_parts)

    def first_step(flip):
        axis, step = at.steps(flip)[0]
        return axis, step, {"y": 1, "s": 2}[axis], (at.index(axis) // step) % 2

    def send_keep(w, pre, unit, flip):
        _, step, ax, bit = first_step(flip)
        w = w.reshape(pre, Y, S, unit, w.shape[1])
        cut = [lax.dynamic_slice_in_dim(w, b * step, step, ax) for b in (1 - bit, bit)]
        return [c.reshape(-1, c.shape[-1]) for c in cut]

    wq_cut = [do(lambda w, k=k: send_keep(w, 3, blk, bool(k)), wq) for k in range(2)]

    def arrange(got):
        x = got.reshape(at.ctx_size, S, blk + 16, rows).transpose(2, 1, 0, 3).reshape(blk + 16, T)
        x_own, extra = x[:blk], x[blk:].astype(f32)
        mean = extra[0:1] + extra[1:2] + extra[2:3]
        inv = extra[3:4] + extra[4:5] + extra[5:6]
        return x_own, mean, inv, extra[6:7]

    x_own, mean1, inv1, place = do(arrange, got)
    x_other = at.core(x_own)

    def first_norm(mine, theirs, mean, inv, cols):
        x = join(mine, theirs).astype(f32)
        return ((x - mean) * inv * cols[:, 0:1] + cols[:, 1:2]).astype(bf16)

    xn1 = do(first_norm, x_own, x_other, mean1, inv1, pair_cols)

    def send_products(cut, xs, shapes):
        got = []
        for k in range(2):
            axis, step, _, _ = first_step(bool(k))
            p = do(lambda w, x: dot(w, x, PLAIN).astype(bf16), cut[k][0], xs[k]).reshape(shapes[k])
            got.append(at.along(p, axis, step))
        kept = []
        for k in range(2):
            p = do(lambda w, x: dot(w, x, PLAIN).astype(bf16), cut[k][1], xs[k])
            kept.append(p.reshape(shapes[k]))
        return list(zip(kept, got))

    def half_shape(pre, unit, t, flip):
        _, step, ax, _ = first_step(flip)
        shape = [pre, Y, S, unit, t]
        shape[ax] = step
        return tuple(shape)

    def scatter_rest(pairs):
        for i in range(1, len(at.steps(False))):
            out = []
            for k in range(2):
                kept, got = pairs[k]
                axis, step = at.steps(bool(k))[i]
                ax = {"y": 1, "s": 2}[axis]
                bit = (at.index(axis) // step) % 2

                def cut(a, b):
                    p = (a.astype(f32) + b.astype(f32)).astype(bf16)
                    return [lax.dynamic_slice_in_dim(p, n * step, step, ax) for n in (1 - bit, bit)]

                send, kept = do(cut, kept, got)
                out.append((kept, at.along(send, axis, step)))
            pairs = out
        return [(kept[:, 0, 0], got[:, 0, 0]) for kept, got in pairs]

    flying = send_products(
        wq_cut, [xn1[:, h] for h in halves], [half_shape(3, blk, H, bool(k)) for k in range(2)]
    )

    wo_parts = chip_rows(w_out, 0, S * blk, Y)
    wg_parts = chip_rows(w_up, 0, S * ffb, Y)
    wo = do(lanes, *wo_parts)
    wu_parts = chip_rows(w_up, Y, S * ffb, Y)
    wg = do(lanes, *wg_parts)
    wg_cut = do(lambda w: send_keep(w, 1, ffb, False), wg)

    def positions(place):
        pos = place.reshape(S, seq) * span + (jnp.arange(seq) % span).astype(f32)[None, :]
        prow, pcol = pos.reshape(S, 1, seq), pos.reshape(S, seq, 1)
        exponent = jnp.arange(ROTARY // 2, dtype=f32)
        inverse = 10000.0 ** (-2.0 * exponent / ROTARY)
        angles = prow * inverse[None, :, None]
        return jnp.cos(angles), jnp.sin(angles), prow, pcol

    cos, sin, prow, pcol = do(positions, place)
    flying = scatter_rest(flying)
    wu = do(lanes, *wu_parts)
    wu_cut = do(lambda w: send_keep(w, 1, ffb, True), wu)

    def gather_steps(parts, row_axis):
        n = len(at.steps(False))
        state = {"parts": list(parts)}

        def start(i):
            state["got"] = []
            state["at"] = []
            for k in range(2):
                axis, step = list(reversed(at.steps(bool(k))))[i]
                state["at"].append((axis, step))
                state["got"].append(at.along(state["parts"][k], axis, step))

        def finish():
            def put(parts, got):
                out = []
                for k in range(2):
                    axis, step = state["at"][k]
                    ax = {"y": 0, "s": 1}[axis]
                    low = (at.index(axis) // step) % 2 == 0
                    a, b = parts[k], got[k]
                    out.append(jnp.concatenate([jnp.where(low, a, b), jnp.where(low, b, a)], ax))
                return out

            state["parts"] = do(put, state["parts"], state["got"])

        def result():
            return jnp.concatenate(state["parts"], axis=row_axis)

        return n, start, finish, result

    qkvs, attns, attn_got, peaks, totals = [], [], [], [], []
    for k in range(2):
        sq = seqs[k]
        shape = (3, heads, HEAD_DIM, H)
        qkv, attn, peak, total = do(
            attend, flying[k][0].reshape(shape), flying[k][1].reshape(shape), bias, cos[sq], sin[sq], prow[sq], pcol[sq]
        )
        qkvs.append(qkv)
        attns.append(attn.reshape(blk, H))
        attn_got.append(at.core(attns[k]))
        peaks.append(peak)
        totals.append(total)

    wo5 = wo.reshape(1, Y, S, blk, wo.shape[1])
    flying = []
    for k in range(2):
        axis, step, ax, bit = first_step(bool(k))

        def product(w, a, b):
            p = dot(w, join(a, b), PLAIN).astype(bf16).reshape(1, Y, S, blk, H)
            return [lax.dynamic_slice_in_dim(p, n * step, step, ax) for n in (1 - bit, bit)]

        send, kept = do(product, wo, attns[k], attn_got[k])
        flying.append((kept, at.along(send, axis, step)))
    flying = scatter_rest(flying)
    cot = cotangent.reshape(2, rows // 2, width)
    cot_pair, _ = lax.optimization_barrier((cot, flying[1][0]))
    cot_n, cot_start, cot_finish, cot_done = gather_steps([cot_pair[k][None, None] for k in range(2)], 2)

    def residual(x, a0, b0, a1, b1):
        a, b = lanes(a0[0], a1[0]), lanes(b0[0], b1[0])
        hidden = x.astype(f32) + (a.astype(f32) + b.astype(f32))
        local_mean = jnp.mean(hidden, axis=0, keepdims=True)
        dev = hidden - local_mean
        return hidden, join(local_mean, jnp.sum(dev * dev, axis=0, keepdims=True))

    hidden, moments = do(residual, x_own, *flying[0], *flying[1])
    cot_start(0)
    count = blk
    for axis, step in at.steps(False) + [("core", 1)]:
        other = at.core(moments) if axis == "core" else at.along(moments, axis, step)

        def merge(a, b):
            gap = a[0:1] - b[0:1]
            return join(0.5 * (a[0:1] + b[0:1]), a[1:2] + b[1:2] + gap * gap * (count / 2.0))

        moments = do(merge, moments, other)
        count *= 2

    def second_norm(hidden, moments, cols):
        inv2 = lax.rsqrt(moments[1:2] / width + eps_norm)
        z2 = (hidden - moments[0:1]) * inv2
        return (z2 * cols[:, 2:3] + cols[:, 3:4]).astype(bf16), z2, inv2

    xn2_own, z2, inv2 = do(second_norm, hidden, moments, own_cols)
    xn2 = do(join, xn2_own, at.core(xn2_own))

    flying = send_products(
        [wg_cut, wu_cut], [xn2, xn2], [half_shape(1, ffb, T, bool(k)) for k in range(2)]
    )

    for i in range(1, cot_n):
        cot_finish()
        cot_start(i)
    wo_own = do(lambda w: w.astype(bf16), w_out)
    wd_own = do(lambda w: w.astype(bf16), w_down)

    def gain_products(wg, wu, cols):
        g, b = cols[:, 2], cols[:, 3]
        terms = []
        for v in (g, b):
            t = lax.reduce_precision(v, 8, 7)
            terms += [t, v - t]
        terms = jnp.stack(terms).astype(bf16)
        out = []
        for w in (wg, wu):
            p = dot(w, terms, LAST)
            out.append(jnp.stack([p[:, 0] + p[:, 1], p[:, 2] + p[:, 3]]).reshape(2, Y, S, ffb))
        return jnp.concatenate(out, axis=0)

    gains = do(gain_products, wg, wu, pair_cols)
    for axis, step in at.steps(False):
        ax = {"y": 1, "s": 2}[axis]
        bit = (at.index(axis) // step) % 2
        send = lax.dynamic_slice_in_dim(gains, (1 - bit) * step, step, ax)
        kept = lax.dynamic_slice_in_dim(gains, bit * step, step, ax)
        gains = do(lambda a, b: a + b, kept, at.along(send, axis, step))
    gains = do(lambda g: g.reshape(4, ffb, 1), gains)
    cot_finish()
    cot_c = do(lambda x: x, cot_done())

    def all_cotangents(mine, theirs):
        both = in_order(mine.reshape(Y, S, rows, width), theirs.reshape(Y, S, rows, width), 2)
        return both.transpose(1, 0, 2, 3, 4).reshape(T, width)

    cot_all = do(all_cotangents, cot_c, at.core(cot_c))
    grad_act = do(lambda w, c: dot(w, c, LAST), wd_own, cot_all)
    cot_cols = do(lambda c: lax.dynamic_slice_in_dim(c, my_block * blk, blk, 1).T, cot_all)
    flying = scatter_rest(flying)

    def gated(ga, gb, ua, ub, grad_act, gains):
        gate = ga[0].astype(f32) + gb[0].astype(f32)
        up = ua[0].astype(f32) + ub[0].astype(f32)
        sig = jax.nn.sigmoid(gate)
        silu = gate * sig
        ggate = (grad_act * up * sig * (1.0 + gate * (1.0 - sig))).astype(bf16)
        gup = (grad_act * silu).astype(bf16)
        return ggate, gup, (silu * up).astype(bf16), gate, up

    ggate, gup, act, gate, up = do(gated, *flying[0], *flying[1], grad_act, gains)

    def parts_of(count, want):
        return max(n for n in range(1, want + 1) if count % (16 * n) == 0)

    n_down, n_up, n_out, n_qkv = parts_of(ffb, 4), parts_of(blk, 2), parts_of(blk, 2), parts_of(blk, 4)

    def cut(g, n):
        r = g.shape[0] // n
        return [g[i * r : (i + 1) * r] for i in range(n)]

    def quarter_heads(x):
        return [x[:, h][None, None] for h in halves]

    n, start, finish, gate_all = gather_steps(quarter_heads(ggate), 3)
    start(0)
    g_down = do(lambda a, c: dot(a, c, PLAIN).astype(bf16), act, cot_all)
    for i, g in enumerate(cut(g_down, n_down)):
        reps.push(("down", i), g)
    reps.tick()

    def norm_sums2(ggate, gup, gate, up, gains):
        a, b = ggate.astype(f32), gup.astype(f32)
        e = jnp.sum(a * gains[0] + b * gains[2], axis=0, keepdims=True)
        ez = jnp.sum(a * (gate - gains[1]) + b * (up - gains[3]), axis=0, keepdims=True)
        return join(e, ez)

    sums = do(norm_sums2, ggate, gup, gate, up, gains)
    steps2 = at.steps(False) + [("core", 1)]

    def sum_step(sums, axis, step):
        other = at.core(sums) if axis == "core" else at.along(sums, axis, step)
        return do(lambda a, b: a + b, sums, other)

    finish()
    start(1)
    reps.tick()
    for axis, step in steps2:
        sums = sum_step(sums, axis, step)
    reps.tick()
    for i in range(2, n):
        finish()
        start(i)
    n, start_up, finish_up, up_all = gather_steps(quarter_heads(gup), 3)
    finish()
    start_up(0)
    reps.tick()
    ggate_all = do(lambda x: x.reshape(Y * S * ffb, T), gate_all())
    part_gate = do(lambda w, g: dot(w, g, FIRST), wg, ggate_all)
    g_gate = do(lambda x, g: dot(x, g, LAST).astype(bf16), xn2, ggate_all)

    def push_pairs(name, g, n):
        r = g.shape[0] // (2 * n)
        for i in range(n):
            reps.push((name, "theirs", i), g[(n + i) * r : (n + i + 1) * r])
            reps.push((name, "mine", i), g[i * r : (i + 1) * r])

    push_pairs("gate", g_gate, n_up)
    finish_up()
    for i in range(1, n):
        start_up(i)
        reps.tick()
        if i == 1:
            out_part = do(lambda w, a: dot(w, a, FIRST).astype(bf16), wd_own, act).reshape(Y, 2, S, blk, T)
            reps.tick()
        finish_up()
    gup_all = do(lambda x: x.reshape(Y * S * ffb, T), up_all())
    part = do(lambda w, g, p: dot(w, g, FIRST) + p, wu, gup_all, part_gate)
    part_theirs = at.core(part[blk:])
    reps.tick()

    def branch(a, b, cot, z, scale, gain, sums):
        gxn2 = a + b
        e = gxn2 * gain
        grad_hidden = cot.astype(f32) + scale * (e - sums[0:1] / width - z * (sums[1:2] / width))
        return grad_hidden.astype(bf16), grad_hidden, gxn2

    grad_branch, grad_hidden, gxn2 = do(
        branch, part[:blk], part_theirs, cot_cols, z2, inv2, own_cols[:, 2:3], sums
    )
    n, start, finish, branch_all = gather_steps(quarter_heads(grad_branch), 3)
    start(0)
    g_up = do(lambda x, g: dot(x, g, LAST).astype(bf16), xn2, gup_all)
    push_pairs("up", g_up, n_up)
    finish()
    for i in range(1, n):
        start(i)
        if i == 1:
            reps.tick()
        finish()
    gbr_c = do(lambda x: x, branch_all())
    gbr_o = at.core(gbr_c)
    gbr = do(lambda a, b: in_order(a, b, 1).reshape(width, T), gbr_c, gbr_o)
    grad_attn = do(lambda w, g: dot(w, g, PLAIN).astype(bf16), wo_own, gbr)

    gqkvs = []
    for k in range(2):
        sq = seqs[k]
        gqkvs.append(
            do(
                attend_back,
                qkvs[k],
                grad_attn[:, halves[k]].reshape(heads, HEAD_DIM, H),
                peaks[k],
                totals[k],
                cos[sq],
                sin[sq],
                prow[sq],
                pcol[sq],
            ).reshape(3, blk, H)
        )
        if k == 0:
            reps.tick()
    n, start, finish, gqkv_done = gather_steps([g.reshape(1, 1, 3 * blk, H) for g in gqkvs], 3)
    start(0)
    attn = lanes(*attns)
    g_out = do(lambda a, g: dot(a, g, LAST).astype(bf16), attn, gbr)
    for i, g in enumerate(cut(g_out, n_out)):
        reps.push(("out", i), g)
    reps.tick()
    finish()
    for i in range(1, n):
        start(i)
        if i == 1:
            reps.tick()
            reps.tick()
        finish()

    def qkv_columns(x):
        return x.reshape(Y, S, 3, blk, T).transpose(2, 0, 1, 3, 4).reshape(3 * Y * S * blk, T)

    gqkv = do(qkv_columns, gqkv_done())
    g_qkv = do(lambda x, g: dot(x, g, LAST).astype(bf16), xn1, gqkv)
    push_pairs("qkv", g_qkv, n_qkv)
    reps.tick()
    part = do(lambda w, g: dot(w, g, FIRST), wq, gqkv)
    part_theirs = at.core(part[blk:])

    jobs = []
    results = {"down": None, "out": None, "up": None, "qkv": None}
    states = {
        "down": (w_down, m_down, v_down),
        "out": (w_out, m_out, v_out),
        "up": (w_up, m_up, v_up),
        "qkv": (w_qkv, m_qkv, v_qkv),
    }
    rates = {"down": 0.02, "out": 0.2, "up": 0.03, "qkv": 0.03}
    received = {}
    for i in range(n_down):
        jobs.append(("down", [("down", i)], i, 0, min(512, width)))
    for part_name, lead in (("gate", 0), ("up", Y)):
        for i in range(n_up):
            jobs.append(("up", [(part_name, "mine", i), (part_name, "theirs", i)], i, lead, S * ffb))
    for i in range(n_out):
        jobs.append(("out", [("out", i)], i, 0, min(512, width)))
    for i in range(n_qkv):
        jobs.append(("qkv", [("qkv", "mine", i), ("qkv", "theirs", i)], i, 0, S * blk))

    def exchange():
        for name in list(reps.done):
            if name[1] == "theirs" and name not in received:
                received[name] = at.core(reps.done[name])

    def update(limit):
        exchange()
        while jobs and limit:
            name, needs, i, lead, unit = jobs[0]
            if not all(k in reps.done for k in needs):
                return
            grads = [received[k] if k[1] == "theirs" else reps.done[k] for k in needs]
            results[name] = do(
                lambda s, g, prev: adam_part(s, g, core, rates[name], prev, i, lead, unit),
                states[name],
                grads,
                results[name],
            )
            jobs.pop(0)
            limit -= 1

    reps.tick()

    def first_back(a, b, x, mean, inv, gain, gxn2, z2, gqkv0, gqkv1):
        gxn1 = a + b
        z1 = (x.astype(f32) - mean) * inv
        e = gxn1 * gain
        sums = join(jnp.sum(e, axis=0, keepdims=True), jnp.sum(e * z1, axis=0, keepdims=True))
        small = jnp.concatenate(
            [
                jnp.sum(gxn1 * z1, axis=1)[None],
                jnp.sum(gxn1, axis=1)[None],
                jnp.sum(gxn2 * z2, axis=1)[None],
                jnp.sum(gxn2, axis=1)[None],
                jnp.sum(gqkv0.astype(f32), axis=2) + jnp.sum(gqkv1.astype(f32), axis=2),
            ],
            axis=0,
        )
        return sums, small, gxn1, z1

    sums, small, gxn1, z1 = do(
        first_back, part[:blk], part_theirs, x_own, mean1, inv1, own_cols[:, 0:1], gxn2, z2, *gqkvs
    )
    for axis, step in steps2:
        sums = sum_step(sums, axis, step)
    input_grad = do(
        lambda h, grad, z, scale, gain, sums: h
        + scale * (grad * gain - sums[0:1] / width - z * (sums[1:2] / width)),
        grad_hidden,
        gxn1,
        z1,
        inv1,
        own_cols[:, 0:1],
        sums,
    )
    reps.tick()

    def to_rows(cols):
        split = do(lambda c: c.reshape(blk, S, at.ctx_size, rows).transpose(2, 1, 0, 3).reshape(nb, blk, rows), cols)
        got = lax.all_to_all(split, plane, split_axis=0, concat_axis=0, tiled=True)
        return do(lambda g: g.reshape(width, rows).T, got)

    out_theirs = at.core(pick(out_part, 1, 1 - at.c))
    input_rows = to_rows(input_grad)
    reps.tick()
    update(2)
    flying = []
    out_sum = do(
        lambda a, b: (a.astype(f32) + b.astype(f32)).astype(bf16)[None], pick(out_part, 1, at.c), out_theirs
    )
    for k in range(2):
        axis, step, ax, bit = first_step(bool(k))
        p = out_sum[..., halves[k]]
        send = lax.dynamic_slice_in_dim(p, (1 - bit) * step, step, ax)
        flying.append((lax.dynamic_slice_in_dim(p, bit * step, step, ax), at.along(send, axis, step)))
    reps.tick()
    update(2)
    flying = scatter_rest(flying)

    def output(hidden, a0, b0, a1, b1):
        a, b = lanes(a0[0], a1[0]), lanes(b0[0], b1[0])
        return (hidden + (a.astype(f32) + b.astype(f32))).astype(bf16)

    reps.tick()
    update(2)
    block_output = to_rows(do(output, hidden, *flying[0], *flying[1]))
    reps.tick()
    update(2)

    n_rep = lax.axis_size("rep")
    step = 1
    while step < n_rep:
        other = lax.ppermute(small, "rep", [(i, i ^ step) for i in range(n_rep)])
        small = do(lambda a, b: a + b, small, other)
        step *= 2
    reps.tick()
    update(2)
    sent = do(lambda s: jnp.broadcast_to(s.reshape(1, 7, blk), (nb, 7, blk)), small)
    got = lax.all_to_all(sent, plane, split_axis=0, concat_axis=0, tiled=True)
    norm_grad = got.transpose(1, 0, 2).reshape(7, width)
    mn, vn, wn = do(lambda *a: adam_update(*a, 0.3, 0.0), norm_params, m_norm, v_norm, norm_grad)

    while reps.busy():
        reps.tick()
        update(2)
    update(len(jobs))
    return (
        (block_output.reshape(tokens.shape), input_rows.reshape(tokens.shape))
        + tuple(results["qkv"])
        + tuple(results["out"])
        + tuple(results["up"])
        + tuple(results["down"])
        + (mn, vn, wn)
    )


def solution(mesh):
    tok = P("rep", "ctx", "shard", None)
    row = P(("ctx", "shard"), None)
    placed = (tok, tok, P("rep", "shard", None)) + (row,) * 4 + (P(),) + (row,) * 8 + (P(), P())
    return jax.shard_map(
        body,
        mesh=mesh,
        in_specs=placed,
        out_specs=(tok, tok) + (row,) * 12 + (P(),) * 3,
        check_vma=False,
    )
```

```python
import functools

import jax
import jax.numpy as jnp
from jax import lax
from jax.experimental import pallas as pl
from jax.experimental.pallas import tpu as pltpu
from jax.sharding import PartitionSpec as P

HEADS = 32
HEAD_DIM = 64
FF = 5632
ROTARY = 16
STEP = 10

eps_norm = 1e-05
masked_score = -1e30
beta_one = 0.9
beta_two = 0.999
adam_eps = 1e-08
weight_decay = 0.1
score_scale = HEAD_DIM ** (-0.5)
FIRST = (((0,), (0,)), ((), ()))
LAST = (((1,), (1,)), ((), ()))
PLAIN = (((1,), (0,)), ((), ()))
bf16 = jnp.bfloat16
f32 = jnp.float32


def dot(a, b, dims):
    return lax.dot_general(a, b, dims, preferred_element_type=f32)


def adam_update(weight, moment_one, moment_two, grad, step_rate, decay_rate):
    first_new = beta_one * moment_one + (1.0 - beta_one) * grad
    second_new = beta_two * moment_two + (1.0 - beta_two) * grad * grad
    first_hat = first_new / (1.0 - beta_one**STEP)
    second_hat = second_new / (1.0 - beta_two**STEP)
    weight_new = weight - step_rate * (
        first_hat / (jnp.sqrt(second_hat) + adam_eps) + decay_rate * weight
    )
    return (first_new, second_new, weight_new)


class Plane:
    def __init__(self):
        self.s_size = lax.axis_size("shard")
        self.ctx_size = lax.axis_size("ctx")
        self.y_size = self.ctx_size // 2
        self.ctx = lax.axis_index("ctx")
        self.s = lax.axis_index("shard")
        self.y = self.ctx // 2
        self.c = self.ctx % 2
        self.blocks = self.ctx_size * self.s_size

    def core(self, x):
        return lax.ppermute(x, "ctx", [(i, i ^ 1) for i in range(self.ctx_size)])

    def along(self, x, axis, step):
        if axis == "y":
            return lax.ppermute(x, "ctx", [(i, i ^ (2 * step)) for i in range(self.ctx_size)])
        return lax.ppermute(x, "shard", [(i, i ^ step) for i in range(self.s_size)])

    def index(self, axis):
        return self.y if axis == "y" else self.s

    def steps(self, flip):
        ys = []
        k = self.y_size // 2
        while k:
            ys.append(("y", k))
            k //= 2
        ss = []
        k = self.s_size // 2
        while k:
            ss.append(("s", k))
            k //= 2
        return ys + ss if flip else ss + ys

    def chip_exchange(self, x, take):
        out = [(self.y, self.s, take(self.y, self.s))]
        for ry in range(self.y_size):
            for rs in range(self.s_size):
                if ry or rs:
                    y, s = self.y ^ ry, self.s ^ rs
                    mask = 2 * ry * self.s_size + rs
                    perm = [(i, i ^ mask) for i in range(self.blocks)]
                    out.append((y, s, lax.ppermute(take(y, s), ("ctx", "shard"), perm)))
        return out

    def sum_all(self, x):
        for axis, step in self.steps(False):
            x = x + self.along(x, axis, step)
        return x + self.core(x)

    def scatter_sum(self, p, flip):
        axes = {"y": 1, "s": 2}
        steps = self.steps(flip)
        kept = got = None
        for n, (axis, step) in enumerate(steps):
            ax = axes[axis]
            bit = (self.index(axis) // step) % 2
            kept = lax.dynamic_slice_in_dim(p, bit * step, step, ax)
            send = lax.dynamic_slice_in_dim(p, (1 - bit) * step, step, ax)
            got = self.along(send, axis, step)
            if n + 1 < len(steps):
                p = (kept.astype(f32) + got.astype(f32)).astype(bf16)
        return kept[:, 0, 0], got[:, 0, 0]

    def gather(self, p, flip):
        axes = {"y": 1, "s": 2}
        p = p[:, None, None]
        for axis, step in reversed(self.steps(flip)):
            ax = axes[axis]
            bit = (self.index(axis) // step) % 2
            got = self.along(p, axis, step)
            first = bit == 0
            p = jnp.concatenate([jnp.where(first, p, got), jnp.where(first, got, p)], ax)
        return p


class Order:
    def __init__(self):
        self.last = None

    def __call__(self, stage, *args):
        if self.last is not None:
            args, self.last = lax.optimization_barrier((args, self.last))
        out = stage(*args)
        self.last = jax.tree.leaves(out)[0]
        return out


SMALL = pl.CostEstimate(flops=1024, bytes_accessed=1024, transcendentals=0)


class RepSum:
    def __init__(self, order):
        self.order = order
        z = lax.axis_index("rep")
        self.end = (z == 0) | (z == lax.axis_size("rep") - 1)
        self.queue = []
        self.outer = None
        self.inner = None
        self.done = {}

    def push(self, name, g):
        self.queue.append((name, g))

    def busy(self):
        return bool(self.queue or self.outer or self.inner)

    def tick(self):
        outer, inner = self.outer, self.inner
        new = self.queue.pop(0) if self.queue else None
        values = {}
        if outer and outer["in"]:
            values["g"], values["g_got"] = outer["in"][1], outer["in_got"]
        if outer and outer["out"]:
            values["t"], values["t_got"] = outer["out"][1], outer["out_got"]
        if inner:
            values["s"], values["s_got"] = inner[1], inner[2]
        if new:
            values["new"] = new[1]
        both = new and inner and new[1].shape == inner[1].shape

        def stage(v):
            def add(a, b):
                return lax.reduce_precision(a.astype(f32) + b.astype(f32), 8, 7).astype(bf16)

            out = {}
            if "s" in v:
                out["total"] = add(v["s"], v["s_got"])
            if "g" in v:
                out["sum"] = add(v["g"], v["g_got"])
            if "t" in v:
                out["out"] = jnp.where(self.end, v["t_got"], v["t"])
            if both:
                out["send"] = jnp.where(self.end, v["new"], out["total"])
            elif "new" in v:
                out["new"] = v["new"]
            return out

        out = self.order(stage, values)
        if outer and outer["out"]:
            self.done[outer["out"][0]] = out["out"]
        self.outer = None
        if new or inner:
            o = {"in": None, "out": None}
            if both:
                o["in_got"] = o["out_got"] = lax.ppermute(out["send"], "rep", [(0, 1), (1, 0), (2, 3), (3, 2)])
            else:
                if new:
                    o["in_got"] = lax.ppermute(out["new"], "rep", [(0, 1), (3, 2)])
                if inner:
                    o["out_got"] = lax.ppermute(out["total"], "rep", [(1, 0), (2, 3)])
            if new:
                o["in"] = new
            if inner:
                o["out"] = (inner[0], out["total"])
            self.outer = o
        self.inner = None
        if outer and outer["in"]:
            self.inner = (outer["in"][0], out["sum"], lax.ppermute(out["sum"], "rep", [(1, 2), (2, 1)]))


def split_kernel(core_ref, w_ref, mine_ref, theirs_ref):
    unit = mine_ref.shape[0]
    first = core_ref[0] == 0
    a, b = w_ref[:, :unit], w_ref[:, unit:]
    mine_ref[...] = jnp.where(first, a, b).T.astype(bf16)
    theirs_ref[...] = jnp.where(first, b, a).T.astype(bf16)


def split_columns(w, core, lead, unit, count):
    rows = w.shape[0]
    half = pl.BlockSpec((unit, rows), lambda j, core: (j, 0))
    out = jax.ShapeDtypeStruct((count * unit, rows), bf16)
    return pl.pallas_call(
        split_kernel,
        grid_spec=pltpu.PrefetchScalarGridSpec(
            num_scalar_prefetch=1,
            grid=(count,),
            in_specs=[pl.BlockSpec((rows, 2 * unit), lambda j, core: (0, lead + j))],
            out_specs=[half, half],
        ),
        out_shape=[out, out],
        compiler_params=pltpu.CompilerParams(vmem_limit_bytes=32 * 1024 * 1024),
        cost_estimate=SMALL,
    )(core, w)


def arrange_kernel(at_ref, a_ref, b_ref, c_ref, d_ref, send_ref, keep_ref):
    send_ref[...] = jnp.concatenate([a_ref[...], b_ref[...]], axis=1)
    keep_ref[...] = jnp.concatenate([c_ref[...], d_ref[...]], axis=1)


def arrange(mine, got, place, pre, y_size, s_size, unit, flip):
    r = mine.shape[1]
    half = pre * y_size * s_size // 2

    def block(i, place, keep):
        p = i % pre
        i = i // pre
        if flip:
            s, y = i % s_size, i // s_size
            bit = place[0] // (y_size // 2)
            bit = bit if keep else 1 - bit
            y = y + bit * (y_size // 2)
        else:
            y, s = i % y_size, i // y_size
            bit = place[1] // (s_size // 2)
            bit = bit if keep else 1 - bit
            s = s + bit * (s_size // 2)
        return ((p * y_size + y) * s_size + s, 0)

    def spec(keep):
        return pl.BlockSpec((unit, r), lambda i, place: block(i, place, keep))

    out = jax.ShapeDtypeStruct((half * unit, 2 * r), bf16)
    out_spec = pl.BlockSpec((unit, 2 * r), lambda i, place: (i, 0))
    return pl.pallas_call(
        arrange_kernel,
        grid_spec=pltpu.PrefetchScalarGridSpec(
            num_scalar_prefetch=1,
            grid=(half,),
            in_specs=[spec(False), spec(False), spec(True), spec(True)],
            out_specs=[out_spec, out_spec],
        ),
        out_shape=[out, out],
        compiler_params=pltpu.CompilerParams(vmem_limit_bytes=32 * 1024 * 1024),
        cost_estimate=SMALL,
    )(place, mine, got, mine, got)


def add_split_kernel(bit_ref, a_ref, b_ref, c_ref, d_ref, send_ref, keep_ref):
    send_ref[...] = (a_ref[...].astype(f32) + b_ref[...].astype(f32)).astype(bf16)
    keep_ref[...] = (c_ref[...].astype(f32) + d_ref[...].astype(f32)).astype(bf16)


def add_split(kept, got, bit):
    rows, t = kept.shape
    half = rows // 2
    n = max(n for n in (1, 2, 3, 4) if half % (16 * n) == 0)
    rb = half // n
    away = pl.BlockSpec((rb, t), lambda i, bit: ((1 - bit[0]) * n + i, 0))
    here = pl.BlockSpec((rb, t), lambda i, bit: (bit[0] * n + i, 0))
    out = jax.ShapeDtypeStruct((half, t), bf16)
    out_spec = pl.BlockSpec((rb, t), lambda i, bit: (i, 0))
    return pl.pallas_call(
        add_split_kernel,
        grid_spec=pltpu.PrefetchScalarGridSpec(
            num_scalar_prefetch=1,
            grid=(n,),
            in_specs=[away, away, here, here],
            out_specs=[out_spec, out_spec],
        ),
        out_shape=[out, out],
        compiler_params=pltpu.CompilerParams(vmem_limit_bytes=48 * 1024 * 1024),
        cost_estimate=SMALL,
    )(bit, kept, got, kept, got)


def token_rows_kernel(core_ref, a_ref, b_ref, c_ref, d_ref, out_ref):
    mine = core_ref[0] == pl.program_id(2)
    half = out_ref.shape[0] // 2
    out_ref[:half] = jnp.where(mine, a_ref[0, 0], c_ref[0, 0])
    out_ref[half:] = jnp.where(mine, b_ref[0, 0], d_ref[0, 0])


def token_rows(mine, theirs, core):
    y_size, s_size, rows, width = mine[0].shape
    part = pl.BlockSpec((1, 1, rows, width), lambda s, y, c, core: (y, s, 0, 0))
    return pl.pallas_call(
        token_rows_kernel,
        grid_spec=pltpu.PrefetchScalarGridSpec(
            num_scalar_prefetch=1,
            grid=(s_size, y_size, 2),
            in_specs=[part] * 4,
            out_specs=pl.BlockSpec((2 * rows, width), lambda s, y, c, core: ((s * y_size + y) * 2 + c, 0)),
        ),
        out_shape=jax.ShapeDtypeStruct((s_size * y_size * 4 * rows, width), bf16),
        compiler_params=pltpu.CompilerParams(vmem_limit_bytes=32 * 1024 * 1024),
        cost_estimate=SMALL,
    )(core, *mine, *theirs)


def adam_kernel(rate, two, core_ref, w_ref, m_ref, v_ref, *refs):
    grad = refs[0][...].astype(f32)
    if two:
        other = refs[1][...].astype(f32)
        mine = core_ref[0] == 0
        grad = jnp.concatenate([jnp.where(mine, grad, other), jnp.where(mine, other, grad)], axis=1)
    new_m_ref, new_v_ref, new_w_ref = refs[-3:]
    new_m, new_v, new_w = adam_update(w_ref[...], m_ref[...], v_ref[...], grad, rate, weight_decay)
    new_m_ref[...] = new_m
    new_v_ref[...] = new_v
    new_w_ref[...] = new_w


def adam_part(state, grads, core, rate, prev, row_block, col_first, unit):
    w, m, v = state
    two = len(grads) == 2
    rb = grads[0].shape[0]
    count = grads[0].shape[1] // unit
    whole = pl.BlockSpec((rb, unit * len(grads)), lambda g, core: (row_block, col_first + g))
    half = pl.BlockSpec((rb, unit), lambda g, core: (0, g))
    out = jax.ShapeDtypeStruct(w.shape, f32)
    extra, aliases = [], {}
    if prev is not None:
        extra = list(prev)
        aliases = {4 + len(grads) + i: i for i in range(3)}
    return pl.pallas_call(
        functools.partial(adam_kernel, rate, two),
        grid_spec=pltpu.PrefetchScalarGridSpec(
            num_scalar_prefetch=1,
            grid=(count,),
            in_specs=[whole] * 3 + [half] * len(grads) + [pl.BlockSpec(memory_space=pl.ANY)] * len(extra),
            out_specs=[whole] * 3,
        ),
        out_shape=[out] * 3,
        input_output_aliases=aliases,
        compiler_params=pltpu.CompilerParams(vmem_limit_bytes=48 * 1024 * 1024),
        cost_estimate=SMALL,
    )(core, w, m, v, *grads, *extra)


def attend_kernel(kept_ref, got_ref, bias_ref, table_ref, qkv_ref, out_ref, stat_ref):
    half = ROTARY // 2
    cos, sin, pos = table_ref[0, :half], table_ref[0, half:ROTARY], table_ref[0, ROTARY:]
    parts = []
    for i in range(3):
        v = kept_ref[i, 0].astype(f32) + got_ref[i, 0].astype(f32) + bias_ref[i, 0]
        if i < 2:
            a, b = v[:half], v[half:ROTARY]
            v = jnp.concatenate([a * cos - b * sin, b * cos + a * sin, v[ROTARY:]], axis=0)
        v = v.astype(bf16)
        qkv_ref[i, 0] = v
        parts.append(v)
    q, k, v = parts
    scores = dot(k, q, FIRST) * score_scale
    scores = jnp.where(pos.T[:, :1] <= pos[:1], scores, masked_score)
    peak = jnp.max(scores, axis=0, keepdims=True)
    e = jnp.exp(scores - peak)
    total = jnp.sum(e, axis=0, keepdims=True)
    p = (e / total).astype(bf16)
    out_ref[0] = dot(v, p, PLAIN).astype(bf16)
    stat_ref[0, 0] = jnp.concatenate([peak, total], axis=0)


def attend(kept, got, bias, table):
    _, heads, hd, t = kept.shape
    seqs, _, seq = table.shape
    big = pl.BlockSpec((3, 1, hd, seq), lambda s, h: (0, h, 0, s))
    table_spec = pl.BlockSpec((1, table.shape[1], seq), lambda s, h: (s, 0, 0))
    stat = pl.BlockSpec((1, 1, 2, seq), lambda s, h: (s, h, 0, 0))
    return pl.pallas_call(
        attend_kernel,
        grid=(seqs, heads),
        in_specs=[
            big,
            big,
            pl.BlockSpec((3, 1, hd, 1), lambda s, h: (0, h, 0, 0)),
            table_spec,
        ],
        out_specs=[big, pl.BlockSpec((1, hd, seq), lambda s, h: (h, 0, s)), stat],
        out_shape=[
            jax.ShapeDtypeStruct((3, heads, hd, t), bf16),
            jax.ShapeDtypeStruct((heads, hd, t), bf16),
            jax.ShapeDtypeStruct((seqs, heads, 2, seq), f32),
        ],
        compiler_params=pltpu.CompilerParams(vmem_limit_bytes=32 * 1024 * 1024),
        cost_estimate=SMALL,
    )(kept, got, bias, table)


def attend_back_kernel(qkv_ref, dout_ref, stat_ref, table_ref, out_ref):
    half = ROTARY // 2
    cos, sin, pos = table_ref[0, :half], table_ref[0, half:ROTARY], table_ref[0, ROTARY:]
    q, k, v = qkv_ref[0, 0], qkv_ref[1, 0], qkv_ref[2, 0]
    dout = dout_ref[0]
    scores = dot(k, q, FIRST) * score_scale
    scores = jnp.where(pos.T[:, :1] <= pos[:1], scores, masked_score)
    p = jnp.exp(scores - stat_ref[0, 0, :1]) / stat_ref[0, 0, 1:]
    dp = dot(v, dout, FIRST)
    inner = jnp.sum(p * dp, axis=0, keepdims=True)
    ds = (p * (dp - inner)).astype(bf16)

    def back(x):
        a, b = x[:half], x[half:ROTARY]
        return jnp.concatenate([a * cos + b * sin, b * cos - a * sin, x[ROTARY:]], axis=0)

    out_ref[0, 0] = back(dot(k, ds, PLAIN) * score_scale).astype(bf16)
    out_ref[1, 0] = back(dot(q, ds, LAST) * score_scale).astype(bf16)
    out_ref[2, 0] = dot(dout, p.astype(bf16), LAST).astype(bf16)


def attend_back(qkv, dout, stats, table):
    _, heads, hd, t = qkv.shape
    seqs, _, seq = table.shape
    big = pl.BlockSpec((3, 1, hd, seq), lambda s, h: (0, h, 0, s))
    table_spec = pl.BlockSpec((1, table.shape[1], seq), lambda s, h: (s, 0, 0))
    stat = pl.BlockSpec((1, 1, 2, seq), lambda s, h: (s, h, 0, 0))
    return pl.pallas_call(
        attend_back_kernel,
        grid=(seqs, heads),
        in_specs=[
            big,
            pl.BlockSpec((1, hd, seq), lambda s, h: (h, 0, s)),
            stat,
            table_spec,
        ],
        out_specs=big,
        out_shape=jax.ShapeDtypeStruct((3, heads, hd, t), bf16),
        compiler_params=pltpu.CompilerParams(vmem_limit_bytes=32 * 1024 * 1024),
        cost_estimate=SMALL,
    )(qkv, dout, stats, table)


def body(
    tokens,
    cotangent,
    span_order,
    w_qkv,
    w_out,
    w_up,
    w_down,
    norm_params,
    m_qkv,
    v_qkv,
    m_out,
    v_out,
    m_up,
    v_up,
    m_down,
    v_down,
    m_norm,
    v_norm,
):
    at = Plane()
    do = Order()
    reps = RepSum(do)
    width = tokens.shape[3]
    rows = tokens.shape[1]
    S, Y, nb = at.s_size, at.y_size, at.blocks
    plane = ("ctx", "shard")
    blk = width // nb
    ffb = FF // nb
    heads = blk // HEAD_DIM
    seq = rows * at.ctx_size
    T = S * seq
    H = T // 2
    first = at.c == 0
    core = at.c.reshape(1)
    my_block = at.ctx * S + at.s
    halves = (slice(0, H), slice(H, T))
    seqs = (slice(0, S // 2), slice(S // 2, S))

    def pick(x, axis, which):
        return lax.dynamic_index_in_dim(x, which, axis, keepdims=False)

    def in_order(mine, theirs, axis):
        return jnp.stack([jnp.where(first, mine, theirs), jnp.where(first, theirs, mine)], axis=axis)

    def join(a, b):
        return jnp.concatenate([a, b], axis=0)

    def lanes(a, b):
        return jnp.concatenate([a, b], axis=1)

    x_rows = tokens.reshape(rows, width)
    order = span_order.reshape(-1).astype(f32)
    span = rows // 2

    def pack(x, order):
        xf = x.astype(f32)
        mean = jnp.mean(xf, axis=1)
        centred = xf - mean[:, None]
        inv = lax.rsqrt(jnp.mean(centred * centred, axis=1) + eps_norm)
        mine = lax.dynamic_slice_in_dim(order, 2 * at.ctx, 2)
        place = jnp.repeat(mine, span)
        terms = []
        for v in (mean, inv):
            for _ in range(3):
                t = lax.reduce_precision(v, 8, 7)
                terms.append(t)
                v = v - t
        extra = jnp.stack(terms + [place] + [jnp.zeros_like(place)] * 9).astype(bf16)
        blocks = x.T.reshape(nb, blk, rows)
        return jnp.concatenate([blocks, jnp.broadcast_to(extra[None], (nb, 16, rows))], axis=1)

    packed = do(pack, x_rows, order)
    got = lax.all_to_all(packed, plane, split_axis=0, concat_axis=0, tiled=True)

    def chip_rows(w, lead, unit, count):
        mine, theirs = do(lambda w: split_columns(w, core, lead, unit, count), w)
        return mine, at.core(theirs)

    wq_parts = chip_rows(w_qkv, 0, S * blk, 3 * Y)
    norm_cols = norm_params.reshape(7, nb, blk).transpose(1, 2, 0)
    own_cols = pick(norm_cols, 0, my_block)
    other_cols = pick(norm_cols, 0, (at.ctx ^ 1) * S + at.s)
    pair_cols = join(own_cols, other_cols)
    bias = own_cols[:, 4:7].T.reshape(3, heads, HEAD_DIM, 1)
    spot = jnp.stack([at.y, at.s])

    def cut_weights(parts, pre, unit, flip):
        return do(lambda a, b: arrange(a, b, spot, pre, Y, S, unit, flip), *parts)

    wq_cut = [cut_weights(wq_parts, 3, blk, bool(k)) for k in range(2)]

    def columns(got):
        x = got.reshape(at.ctx_size, S, blk + 16, rows).transpose(2, 1, 0, 3).reshape(blk + 16, T)
        x_own, extra = x[:blk], x[blk:].astype(f32)
        mean = extra[0:1] + extra[1:2] + extra[2:3]
        inv = extra[3:4] + extra[4:5] + extra[5:6]
        return x_own, mean, inv, extra[6:7]

    x_own, mean1, inv1, place = do(columns, got)
    x_other = at.core(x_own)

    def first_norm(mine, theirs, mean, inv, cols):
        x = join(mine, theirs).astype(f32)
        return ((x - mean) * inv * cols[:, 0:1] + cols[:, 1:2]).astype(bf16)

    xn1 = do(first_norm, x_own, x_other, mean1, inv1, pair_cols)

    def send_products(cut, xs):
        got, kept = [], []
        for k in range(2):
            axis, step = at.steps(bool(k))[0]
            p = do(lambda w, x: dot(w, x, PLAIN).astype(bf16), cut[k][0], xs[k])
            got.append(at.along(p, axis, step))
        for k in range(2):
            kept.append(do(lambda w, x: dot(w, x, PLAIN).astype(bf16), cut[k][1], xs[k]))
        return list(zip(kept, got))

    def scatter_rest(pairs):
        for i in range(1, len(at.steps(False))):
            out = []
            for k in range(2):
                axis, step = at.steps(bool(k))[i]
                bit = (at.index(axis) // step) % 2
                send, kept = do(lambda a, b: add_split(a, b, bit.reshape(1)), *pairs[k])
                out.append((kept, at.along(send, axis, step)))
            pairs = out
        return pairs

    flying = send_products(wq_cut, [xn1[:, h] for h in halves])

    wo_parts = chip_rows(w_out, 0, S * blk, Y)
    wg_parts = chip_rows(w_up, 0, S * ffb, Y)
    wu_parts = chip_rows(w_up, Y, S * ffb, Y)
    wo_cut = [cut_weights(wo_parts, 1, blk, bool(k)) for k in range(2)]

    def positions(place):
        pos = place.reshape(S, seq) * span + (jnp.arange(seq) % span).astype(f32)[None, :]
        prow = pos.reshape(S, 1, seq)
        exponent = jnp.arange(ROTARY // 2, dtype=f32)
        inverse = 10000.0 ** (-2.0 * exponent / ROTARY)
        angles = prow * inverse[None, :, None]
        return jnp.concatenate([jnp.cos(angles), jnp.sin(angles), jnp.broadcast_to(prow, (S, 8, seq))], axis=1)

    table = do(positions, place)
    flying = scatter_rest(flying)
    wg_cut = cut_weights(wg_parts, 1, ffb, False)
    wu_cut = cut_weights(wu_parts, 1, ffb, True)

    def gather_steps(parts, row_axis):
        n = len(at.steps(False))
        state = {"parts": list(parts)}

        def start(i):
            state["got"] = []
            state["at"] = []
            for k in range(2):
                axis, step = list(reversed(at.steps(bool(k))))[i]
                state["at"].append((axis, step))
                state["got"].append(at.along(state["parts"][k], axis, step))

        def finish():
            def put(parts, got):
                out = []
                for k in range(2):
                    axis, step = state["at"][k]
                    ax = {"y": 0, "s": 1}[axis]
                    low = (at.index(axis) // step) % 2 == 0
                    a, b = parts[k], got[k]
                    out.append(jnp.concatenate([jnp.where(low, a, b), jnp.where(low, b, a)], ax))
                return out

            state["parts"] = do(put, state["parts"], state["got"])

        def result():
            return jnp.concatenate(state["parts"], axis=row_axis)

        return n, start, finish, state if row_axis is None else result

    qkvs, attns, attn_got, stats = [], [], [], []
    for k in range(2):
        shape = (3, heads, HEAD_DIM, H)
        qkv, attn, stat = do(attend, flying[k][0].reshape(shape), flying[k][1].reshape(shape), bias, table[seqs[k]])
        qkvs.append(qkv)
        attns.append(attn.reshape(blk, H))
        attn_got.append(at.core(attns[k]))
        stats.append(stat)

    pairs = [do(join, attns[k], attn_got[k]) for k in range(2)]
    flying = scatter_rest(send_products(wo_cut, pairs))
    cot = cotangent.reshape(2, rows // 2, width)
    cot_pair, _ = lax.optimization_barrier((cot, flying[1][0]))
    cot_n, cot_start, cot_finish, cot_state = gather_steps([cot_pair[k][None, None] for k in range(2)], None)

    def residual(x, a0, b0, a1, b1):
        a, b = lanes(a0, a1), lanes(b0, b1)
        hidden = x.astype(f32) + (a.astype(f32) + b.astype(f32))
        local_mean = jnp.mean(hidden, axis=0, keepdims=True)
        dev = hidden - local_mean
        return hidden, join(local_mean, jnp.sum(dev * dev, axis=0, keepdims=True))

    hidden, moments = do(residual, x_own, *flying[0], *flying[1])
    cot_start(0)
    count = blk
    for axis, step in at.steps(False) + [("core", 1)]:
        other = at.core(moments) if axis == "core" else at.along(moments, axis, step)

        def merge(a, b):
            gap = a[0:1] - b[0:1]
            return join(0.5 * (a[0:1] + b[0:1]), a[1:2] + b[1:2] + gap * gap * (count / 2.0))

        moments = do(merge, moments, other)
        count *= 2

    def second_norm(hidden, moments, cols):
        inv2 = lax.rsqrt(moments[1:2] / width + eps_norm)
        z2 = (hidden - moments[0:1]) * inv2
        return (z2 * cols[:, 2:3] + cols[:, 3:4]).astype(bf16), z2, inv2

    xn2_own, z2, inv2 = do(second_norm, hidden, moments, own_cols)
    xn2 = do(join, xn2_own, at.core(xn2_own))

    flying = send_products([wg_cut, wu_cut], [xn2, xn2])

    for i in range(1, cot_n):
        cot_finish()
        cot_start(i)
    wo_own = do(lambda w: w.astype(bf16), w_out)
    wd_own = do(lambda w: w.astype(bf16), w_down)
    wq = do(lanes, *wq_parts)

    wg = do(lanes, *wg_parts)
    wu = do(lanes, *wu_parts)

    def gain_products(wg, wu, cols):
        g, b = cols[:, 2], cols[:, 3]
        terms = []
        for v in (g, b):
            t = lax.reduce_precision(v, 8, 7)
            terms += [t, v - t]
        terms = jnp.stack(terms).astype(bf16)
        out = []
        for w in (wg, wu):
            p = dot(w, terms, LAST)
            out.append(jnp.stack([p[:, 0] + p[:, 1], p[:, 2] + p[:, 3]]).reshape(2, Y, S, ffb))
        return jnp.concatenate(out, axis=0)

    gains = do(gain_products, wg, wu, pair_cols)
    for axis, step in at.steps(False):
        ax = {"y": 1, "s": 2}[axis]
        bit = (at.index(axis) // step) % 2
        send = lax.dynamic_slice_in_dim(gains, (1 - bit) * step, step, ax)
        kept = lax.dynamic_slice_in_dim(gains, bit * step, step, ax)
        gains = do(lambda a, b: a + b, kept, at.along(send, axis, step))
    gains = do(lambda g: g.reshape(4, ffb, 1), gains)
    cot_finish()
    cot_theirs = [at.core(p) for p in cot_state["parts"]]
    cot_all = do(lambda a, b: token_rows(a, b, core), cot_state["parts"], cot_theirs)
    grad_act = do(lambda w, c: dot(w, c, LAST), wd_own, cot_all)
    cot_cols = do(lambda c: lax.dynamic_slice_in_dim(c, my_block * blk, blk, 1).T, cot_all)
    flying = scatter_rest(flying)

    def gated(ga, gb, ua, ub, grad_act, gains):
        gate = ga.astype(f32) + gb.astype(f32)
        up = ua.astype(f32) + ub.astype(f32)
        sig = jax.nn.sigmoid(gate)
        silu = gate * sig
        ggate = (grad_act * up * sig * (1.0 + gate * (1.0 - sig))).astype(bf16)
        gup = (grad_act * silu).astype(bf16)
        return ggate, gup, (silu * up).astype(bf16), gate, up

    ggate, gup, act, gate, up = do(gated, *flying[0], *flying[1], grad_act, gains)

    def parts_of(count, want):
        return max(n for n in range(1, want + 1) if count % (16 * n) == 0)

    def even(count, want):
        n = parts_of(count, want)
        return [(k * (count // n), count // n) for k in range(n)]

    down_rows, up_rows, out_rows = even(ffb, 4), even(blk, 2), even(blk, 2)
    qkv_rows = [(0, blk // 2), (blk // 2, blk // 4), (3 * blk // 4, blk // 4)]

    def push_rows(name, g, rows):
        for k, (at_row, count) in enumerate(rows):
            reps.push((name, "all", k), g[at_row : at_row + count])

    def push_pairs(name, g, rows):
        for k, (at_row, count) in enumerate(rows):
            reps.push((name, "theirs", k), g[blk + at_row : blk + at_row + count])
            reps.push((name, "mine", k), g[at_row : at_row + count])

    results = {"down": None, "out": None, "up": None, "qkv": None}
    states = {
        "down": (w_down, m_down, v_down),
        "out": (w_out, m_out, v_out),
        "up": (w_up, m_up, v_up),
        "qkv": (w_qkv, m_qkv, v_qkv),
    }
    rates = {"down": 0.02, "out": 0.2, "up": 0.03, "qkv": 0.03}
    jobs = []
    for k, (at_row, count) in enumerate(down_rows):
        jobs.append(("down", [("down", "all", k)], at_row // count, 0, min(512, width)))
    for part_name, lead in (("gate", 0), ("up", Y)):
        for k, (at_row, count) in enumerate(up_rows):
            jobs.append(
                ("up", [(part_name, "mine", k), (part_name, "theirs", k)], at_row // count, lead, S * ffb)
            )
    for k, (at_row, count) in enumerate(out_rows):
        jobs.append(("out", [("out", "all", k)], at_row // count, 0, min(512, width)))
    for k, (at_row, count) in enumerate(qkv_rows):
        jobs.append(("qkv", [("qkv", "mine", k), ("qkv", "theirs", k)], at_row // count, 0, S * blk))
    received = {}

    def update(limit):
        for name in list(reps.done):
            if name[1] == "theirs" and name not in received:
                received[name] = at.core(reps.done[name])
        while jobs and limit:
            name, needs, row_block, lead, unit = jobs[0]
            if not all(k in reps.done for k in needs):
                return
            grads = [received[k] if k[1] == "theirs" else reps.done[k] for k in needs]
            results[name] = do(
                lambda s, g, prev: adam_part(s, g, core, rates[name], prev, row_block, lead, unit),
                states[name],
                grads,
                results[name],
            )
            jobs.pop(0)
            limit -= 1

    def quarter_heads(x):
        return [x[:, h][None, None] for h in halves]

    n, start, finish, gate_all = gather_steps(quarter_heads(ggate), 3)
    start(0)
    g_down = do(lambda a, c: dot(a, c, PLAIN).astype(bf16), act, cot_all)
    push_rows("down", g_down, down_rows)
    reps.tick()

    def norm_sums2(ggate, gup, gate, up, gains):
        a, b = ggate.astype(f32), gup.astype(f32)
        e = jnp.sum(a * gains[0] + b * gains[2], axis=0, keepdims=True)
        ez = jnp.sum(a * (gate - gains[1]) + b * (up - gains[3]), axis=0, keepdims=True)
        return join(e, ez)

    sums = do(norm_sums2, ggate, gup, gate, up, gains)
    steps2 = at.steps(False) + [("core", 1)]

    def sum_step(sums, axis, step):
        other = at.core(sums) if axis == "core" else at.along(sums, axis, step)
        return do(lambda a, b: a + b, sums, other)

    finish()
    start(1)
    reps.tick()
    for axis, step in steps2:
        sums = sum_step(sums, axis, step)
    reps.tick()
    for i in range(2, n):
        finish()
        start(i)
    n, start_up, finish_up, up_all = gather_steps(quarter_heads(gup), 3)
    finish()
    start_up(0)
    reps.tick()
    ggate_all = do(lambda x: x.reshape(Y * S * ffb, T), gate_all())
    part_gate = do(lambda w, g: dot(w, g, FIRST), wg, ggate_all)
    g_gate = do(lambda x, g: dot(x, g, LAST).astype(bf16), xn2, ggate_all)
    push_pairs("gate", g_gate, up_rows)
    finish_up()
    for i in range(1, n):
        start_up(i)
        reps.tick()
        if i == 1:
            out_part = do(lambda w, a: dot(w, a, FIRST).astype(bf16), wd_own, act).reshape(Y, 2, S * blk, T)
            out_theirs = at.core(pick(out_part, 1, 1 - at.c))
            reps.tick()
        finish_up()
    gup_all = do(lambda x: x.reshape(Y * S * ffb, T), up_all())
    part = do(lambda w, g, p: dot(w, g, FIRST) + p, wu, gup_all, part_gate)
    part_theirs = at.core(part[blk:])
    reps.tick()

    def branch(a, b, cot, z, scale, gain, sums):
        gxn2 = a + b
        e = gxn2 * gain
        grad_hidden = cot.astype(f32) + scale * (e - sums[0:1] / width - z * (sums[1:2] / width))
        return grad_hidden.astype(bf16), grad_hidden, gxn2

    grad_branch, grad_hidden, gxn2 = do(
        branch, part[:blk], part_theirs, cot_cols, z2, inv2, own_cols[:, 2:3], sums
    )
    n, start, finish, branch_all = gather_steps(quarter_heads(grad_branch), 3)
    start(0)
    g_up = do(lambda x, g: dot(x, g, LAST).astype(bf16), xn2, gup_all)
    push_pairs("up", g_up, up_rows)
    finish()
    for i in range(1, n):
        start(i)
        if i == 1:
            reps.tick()
        finish()
    gbr_c = do(lambda x: x, branch_all())
    gbr_o = at.core(gbr_c)
    gbr = do(lambda a, b: in_order(a, b, 1).reshape(width, T), gbr_c, gbr_o)
    grad_attn = do(lambda w, g: dot(w, g, PLAIN).astype(bf16), wo_own, gbr)
    reps.tick()

    gqkvs = []
    for k in range(2):
        dout = grad_attn[:, halves[k]].reshape(heads, HEAD_DIM, H)
        gqkvs.append(do(attend_back, qkvs[k], dout, stats[k], table[seqs[k]]).reshape(3, blk, H))
        if k == 0:
            reps.tick()
    n, start, finish, gqkv_done = gather_steps([g.reshape(1, 1, 3 * blk, H) for g in gqkvs], 3)
    start(0)
    attn = lanes(*attns)
    g_out = do(lambda a, g: dot(a, g, LAST).astype(bf16), attn, gbr)
    push_rows("out", g_out, out_rows)
    reps.tick()
    update(2)
    finish()
    for i in range(1, n):
        start(i)
        if i == 1:
            reps.tick()
            update(2)
            reps.tick()
            update(1)
        finish()

    def qkv_columns(x):
        return x.reshape(Y, S, 3, blk, T).transpose(2, 0, 1, 3, 4).reshape(3 * Y * S * blk, T)

    gqkv = do(qkv_columns, gqkv_done())
    reps.tick()
    g_qkv = do(lambda x, g: dot(x, g, LAST).astype(bf16), xn1, gqkv)
    push_pairs("qkv", g_qkv, qkv_rows)
    part = do(lambda w, g: dot(w, g, FIRST), wq, gqkv)
    part_theirs = at.core(part[blk:])
    update(1)
    reps.tick()

    def first_back(a, b, x, mean, inv, gain, gxn2, z2, gqkv0, gqkv1):
        gxn1 = a + b
        z1 = (x.astype(f32) - mean) * inv
        e = gxn1 * gain
        sums = join(jnp.sum(e, axis=0, keepdims=True), jnp.sum(e * z1, axis=0, keepdims=True))
        small = jnp.concatenate(
            [
                jnp.sum(gxn1 * z1, axis=1)[None],
                jnp.sum(gxn1, axis=1)[None],
                jnp.sum(gxn2 * z2, axis=1)[None],
                jnp.sum(gxn2, axis=1)[None],
                jnp.sum(gqkv0.astype(f32), axis=2) + jnp.sum(gqkv1.astype(f32), axis=2),
            ],
            axis=0,
        )
        return sums, small, gxn1, z1

    sums, small, gxn1, z1 = do(
        first_back, part[:blk], part_theirs, x_own, mean1, inv1, own_cols[:, 0:1], gxn2, z2, *gqkvs
    )
    for axis, step in steps2:
        sums = sum_step(sums, axis, step)
    reps.tick()
    input_grad = do(
        lambda h, grad, z, scale, gain, sums: h
        + scale * (grad * gain - sums[0:1] / width - z * (sums[1:2] / width)),
        grad_hidden,
        gxn1,
        z1,
        inv1,
        own_cols[:, 0:1],
        sums,
    )

    def to_rows(cols):
        split = do(lambda c: c.reshape(blk, S, at.ctx_size, rows).transpose(2, 1, 0, 3).reshape(nb, blk, rows), cols)
        got = lax.all_to_all(split, plane, split_axis=0, concat_axis=0, tiled=True)
        return do(lambda g: g.reshape(width, rows).T, got)

    update(1)
    input_rows = to_rows(input_grad)
    reps.tick()
    update(1)

    kept, got = pick(out_part, 1, at.c).reshape(-1, T), out_theirs.reshape(-1, T)
    for k, (axis, step) in enumerate(at.steps(True)):
        bit = (at.index(axis) // step) % 2
        send, kept = do(lambda a, b: add_split(a, b, bit.reshape(1)), kept, got)
        got = at.along(send, axis, step)
        if k < 2:
            reps.tick()
            update(1)
    out_cols = do(
        lambda h, a, b: (h + (a.astype(f32) + b.astype(f32))).astype(bf16), hidden, kept, got
    )
    reps.tick()
    update(1)
    block_output = to_rows(out_cols)
    reps.tick()
    update(1)

    n_rep = lax.axis_size("rep")
    step = 1
    while step < n_rep:
        other = lax.ppermute(small, "rep", [(i, i ^ step) for i in range(n_rep)])
        small = do(lambda a, b: a + b, small, other)
        step *= 2
    sent = do(lambda s: jnp.broadcast_to(s.reshape(1, 7, blk), (nb, 7, blk)), small)
    got = lax.all_to_all(sent, plane, split_axis=0, concat_axis=0, tiled=True)
    norm_grad = got.transpose(1, 0, 2).reshape(7, width)
    mn, vn, wn = do(lambda *a: adam_update(*a, 0.3, 0.0), norm_params, m_norm, v_norm, norm_grad)

    while reps.busy():
        reps.tick()
        update(2)
    update(len(jobs))
    return (
        (block_output.reshape(tokens.shape), input_rows.reshape(tokens.shape))
        + tuple(results["qkv"])
        + tuple(results["out"])
        + tuple(results["up"])
        + tuple(results["down"])
        + (mn, vn, wn)
    )


def solution(mesh):
    tok = P("rep", "ctx", "shard", None)
    row = P(("ctx", "shard"), None)
    placed = (tok, tok, P("rep", "shard", None)) + (row,) * 4 + (P(),) + (row,) * 8 + (P(), P())
    return jax.shard_map(
        body,
        mesh=mesh,
        in_specs=placed,
        out_specs=(tok, tok) + (row,) * 12 + (P(),) * 3,
        check_vma=False,
    )
```

```python
import functools

import jax
import jax.numpy as jnp
from jax import lax
from jax.experimental import pallas as pl
from jax.experimental.pallas import tpu as pltpu
from jax.sharding import PartitionSpec as P

HEADS = 32
HEAD_DIM = 64
FF = 5632
ROTARY = 16
STEP = 10

eps_norm = 1e-05
masked_score = -1e30
beta_one = 0.9
beta_two = 0.999
adam_eps = 1e-08
weight_decay = 0.1
score_scale = HEAD_DIM ** (-0.5)
FIRST = (((0,), (0,)), ((), ()))
LAST = (((1,), (1,)), ((), ()))
PLAIN = (((1,), (0,)), ((), ()))
bf16 = jnp.bfloat16
f32 = jnp.float32


def dot(a, b, dims):
    return lax.dot_general(a, b, dims, preferred_element_type=f32)


def adam_update(weight, moment_one, moment_two, grad, step_rate, decay_rate):
    first_new = beta_one * moment_one + (1.0 - beta_one) * grad
    second_new = beta_two * moment_two + (1.0 - beta_two) * grad * grad
    first_hat = first_new / (1.0 - beta_one**STEP)
    second_hat = second_new / (1.0 - beta_two**STEP)
    weight_new = weight - step_rate * (
        first_hat / (jnp.sqrt(second_hat) + adam_eps) + decay_rate * weight
    )
    return (first_new, second_new, weight_new)


class Plane:
    def __init__(self):
        self.s_size = lax.axis_size("shard")
        self.ctx_size = lax.axis_size("ctx")
        self.y_size = self.ctx_size // 2
        self.ctx = lax.axis_index("ctx")
        self.s = lax.axis_index("shard")
        self.y = self.ctx // 2
        self.c = self.ctx % 2
        self.blocks = self.ctx_size * self.s_size

    def core(self, x):
        return lax.ppermute(x, "ctx", [(i, i ^ 1) for i in range(self.ctx_size)])

    def along(self, x, axis, step):
        if axis == "y":
            return lax.ppermute(x, "ctx", [(i, i ^ (2 * step)) for i in range(self.ctx_size)])
        return lax.ppermute(x, "shard", [(i, i ^ step) for i in range(self.s_size)])

    def index(self, axis):
        return self.y if axis == "y" else self.s

    def steps(self, flip):
        ys = []
        k = self.y_size // 2
        while k:
            ys.append(("y", k))
            k //= 2
        ss = []
        k = self.s_size // 2
        while k:
            ss.append(("s", k))
            k //= 2
        return ys + ss if flip else ss + ys

    def chip_exchange(self, x, take):
        out = [(self.y, self.s, take(self.y, self.s))]
        for ry in range(self.y_size):
            for rs in range(self.s_size):
                if ry or rs:
                    y, s = self.y ^ ry, self.s ^ rs
                    mask = 2 * ry * self.s_size + rs
                    perm = [(i, i ^ mask) for i in range(self.blocks)]
                    out.append((y, s, lax.ppermute(take(y, s), ("ctx", "shard"), perm)))
        return out

    def sum_all(self, x):
        for axis, step in self.steps(False):
            x = x + self.along(x, axis, step)
        return x + self.core(x)

    def scatter_sum(self, p, flip):
        axes = {"y": 1, "s": 2}
        steps = self.steps(flip)
        kept = got = None
        for n, (axis, step) in enumerate(steps):
            ax = axes[axis]
            bit = (self.index(axis) // step) % 2
            kept = lax.dynamic_slice_in_dim(p, bit * step, step, ax)
            send = lax.dynamic_slice_in_dim(p, (1 - bit) * step, step, ax)
            got = self.along(send, axis, step)
            if n + 1 < len(steps):
                p = (kept.astype(f32) + got.astype(f32)).astype(bf16)
        return kept[:, 0, 0], got[:, 0, 0]

    def gather(self, p, flip):
        axes = {"y": 1, "s": 2}
        p = p[:, None, None]
        for axis, step in reversed(self.steps(flip)):
            ax = axes[axis]
            bit = (self.index(axis) // step) % 2
            got = self.along(p, axis, step)
            first = bit == 0
            p = jnp.concatenate([jnp.where(first, p, got), jnp.where(first, got, p)], ax)
        return p


class Order:
    def __init__(self):
        self.last = None

    def __call__(self, stage, *args):
        if self.last is not None:
            args, self.last = lax.optimization_barrier((args, self.last))
        out = stage(*args)
        self.last = jax.tree.leaves(out)[0]
        return out


SMALL = pl.CostEstimate(flops=1024, bytes_accessed=1024, transcendentals=0)


class RepSum:
    def __init__(self, order):
        self.order = order
        z = lax.axis_index("rep")
        self.end = (z == 0) | (z == lax.axis_size("rep") - 1)
        self.queue = []
        self.flight = []
        self.done = {}

    def push(self, name, g):
        self.queue.append((name, g))

    def busy(self):
        return bool(self.queue or self.flight)

    def tick(self):
        old = {}
        if len(self.flight) == 2 or (self.flight and not self.queue):
            old = self.flight.pop(0)
        new = self.queue.pop(0) if self.queue else None
        values = {}
        if "in" in old:
            values["g"], values["g_got"] = old["in"][1], old["in_got"]
        if "mid" in old:
            values["s"], values["s_got"] = old["mid"][1], old["mid_got"]
        if new:
            values["new"] = new[1]
        both = new and "mid" in old and new[1].shape == old["mid"][1].shape
        if "out" in old:
            values["out_got"] = old["out_got"]

        def stage(v):
            def add(a, b):
                return lax.reduce_precision(a.astype(f32) + b.astype(f32), 8, 7).astype(bf16)

            out = {}
            if "g" in v:
                out["a_sum"] = add(v["g"], v["g_got"])
            if "s" in v:
                total = add(v["s"], v["s_got"])
                out["total"] = jnp.where(self.end, v["new"], total) if both else total
            if "new" in v and not both:
                out["new"] = v["new"]
            if "out_got" in v:
                out["z_got"] = v["out_got"]
            return out

        if not values:
            return
        out = self.order(stage, values)
        if "out" in old:
            self.done[old["out"][0]] = (old["out"][1], out["z_got"])
        slot = {}
        if both:
            got = lax.ppermute(out["total"], "rep", [(0, 1), (1, 0), (2, 3), (3, 2)])
            slot = {"in": new, "in_got": got, "out": (old["mid"][0], out["total"]), "out_got": got}
        else:
            if new:
                slot["in"] = new
                slot["in_got"] = lax.ppermute(out["new"], "rep", [(0, 1), (3, 2)])
            if "mid" in old:
                slot["out"] = (old["mid"][0], out["total"])
                slot["out_got"] = lax.ppermute(out["total"], "rep", [(1, 0), (2, 3)])
        if "in" in old:
            slot["mid"] = (old["in"][0], out["a_sum"])
            slot["mid_got"] = lax.ppermute(out["a_sum"], "rep", [(1, 2), (2, 1)])
        if slot:
            self.flight.append(slot)


def cast_kernel(w_ref, out_ref):
    out_ref[...] = w_ref[...].astype(bf16)


def cast(w):
    rows, width = w.shape
    unit = max(n for n in (128, 256, 512, 1024, 1408, 2048, 2816) if width % n == 0)
    spec = pl.BlockSpec((rows, unit), lambda i: (0, i))
    return pl.pallas_call(
        cast_kernel,
        grid=(width // unit,),
        in_specs=[spec],
        out_specs=spec,
        out_shape=jax.ShapeDtypeStruct(w.shape, bf16),
        compiler_params=pltpu.CompilerParams(vmem_limit_bytes=48 * 1024 * 1024),
        cost_estimate=SMALL,
    )(w)


def split_kernel(core_ref, w_ref, mine_ref, theirs_ref):
    unit = mine_ref.shape[0]
    first = core_ref[0] == 0
    a, b = w_ref[:, :unit], w_ref[:, unit:]
    mine_ref[...] = jnp.where(first, a, b).T.astype(bf16)
    theirs_ref[...] = jnp.where(first, b, a).T.astype(bf16)


def split_columns(w, core, lead, unit, count):
    rows = w.shape[0]
    half = pl.BlockSpec((unit, rows), lambda j, core: (j, 0))
    out = jax.ShapeDtypeStruct((count * unit, rows), bf16)
    return pl.pallas_call(
        split_kernel,
        grid_spec=pltpu.PrefetchScalarGridSpec(
            num_scalar_prefetch=1,
            grid=(count,),
            in_specs=[pl.BlockSpec((rows, 2 * unit), lambda j, core: (0, lead + j))],
            out_specs=[half, half],
        ),
        out_shape=[out, out],
        compiler_params=pltpu.CompilerParams(vmem_limit_bytes=32 * 1024 * 1024),
        cost_estimate=SMALL,
    )(core, w)


def arrange_kernel(at_ref, a_ref, b_ref, c_ref, d_ref, send_ref, keep_ref):
    send_ref[...] = jnp.concatenate([a_ref[...], b_ref[...]], axis=1)
    keep_ref[...] = jnp.concatenate([c_ref[...], d_ref[...]], axis=1)


def arrange(mine, got, place, pre, y_size, s_size, unit, flip):
    r = mine.shape[1]
    half = pre * y_size * s_size // 2

    def block(i, place, keep):
        p = i % pre
        i = i // pre
        if flip:
            s, y = i % s_size, i // s_size
            bit = place[0] // (y_size // 2)
            bit = bit if keep else 1 - bit
            y = y + bit * (y_size // 2)
        else:
            y, s = i % y_size, i // y_size
            bit = place[1] // (s_size // 2)
            bit = bit if keep else 1 - bit
            s = s + bit * (s_size // 2)
        return ((p * y_size + y) * s_size + s, 0)

    def spec(keep):
        return pl.BlockSpec((unit, r), lambda i, place: block(i, place, keep))

    out = jax.ShapeDtypeStruct((half * unit, 2 * r), bf16)
    out_spec = pl.BlockSpec((unit, 2 * r), lambda i, place: (i, 0))
    return pl.pallas_call(
        arrange_kernel,
        grid_spec=pltpu.PrefetchScalarGridSpec(
            num_scalar_prefetch=1,
            grid=(half,),
            in_specs=[spec(False), spec(False), spec(True), spec(True)],
            out_specs=[out_spec, out_spec],
        ),
        out_shape=[out, out],
        compiler_params=pltpu.CompilerParams(vmem_limit_bytes=32 * 1024 * 1024),
        cost_estimate=SMALL,
    )(place, mine, got, mine, got)


def add_split_kernel(bit_ref, a_ref, b_ref, c_ref, d_ref, send_ref, keep_ref):
    send_ref[...] = (a_ref[...].astype(f32) + b_ref[...].astype(f32)).astype(bf16)
    keep_ref[...] = (c_ref[...].astype(f32) + d_ref[...].astype(f32)).astype(bf16)


def add_split(kept, got, bit):
    rows, t = kept.shape
    half = rows // 2
    n = max(n for n in (1, 2, 3, 4) if half % (16 * n) == 0)
    rb = half // n
    away = pl.BlockSpec((rb, t), lambda i, bit: ((1 - bit[0]) * n + i, 0))
    here = pl.BlockSpec((rb, t), lambda i, bit: (bit[0] * n + i, 0))
    out = jax.ShapeDtypeStruct((half, t), bf16)
    out_spec = pl.BlockSpec((rb, t), lambda i, bit: (i, 0))
    return pl.pallas_call(
        add_split_kernel,
        grid_spec=pltpu.PrefetchScalarGridSpec(
            num_scalar_prefetch=1,
            grid=(n,),
            in_specs=[away, away, here, here],
            out_specs=[out_spec, out_spec],
        ),
        out_shape=[out, out],
        compiler_params=pltpu.CompilerParams(vmem_limit_bytes=48 * 1024 * 1024),
        cost_estimate=SMALL,
    )(bit, kept, got, kept, got)


def adam_kernel(rate, end_ref, w_ref, m_ref, v_ref, total_ref, got_ref, *refs):
    grad = jnp.where(end_ref[0] == 1, got_ref[...], total_ref[...]).astype(f32)
    new_m_ref, new_v_ref, new_w_ref = refs[-3:]
    new_m, new_v, new_w = adam_update(w_ref[...], m_ref[...], v_ref[...], grad, rate, weight_decay)
    new_m_ref[...] = new_m
    new_v_ref[...] = new_v
    new_w_ref[...] = new_w


def adam_part(state, grads, end, rate, prev, row_block, lead, unit):
    w, m, v = state
    rb, width = grads[0].shape
    whole = pl.BlockSpec((rb, unit), lambda g, end: (row_block, lead + g))
    part = pl.BlockSpec((rb, unit), lambda g, end: (0, g))
    out = jax.ShapeDtypeStruct(w.shape, f32)
    extra, aliases = [], {}
    if prev is not None:
        extra = list(prev)
        aliases = {6 + i: i for i in range(3)}
    return pl.pallas_call(
        functools.partial(adam_kernel, rate),
        grid_spec=pltpu.PrefetchScalarGridSpec(
            num_scalar_prefetch=1,
            grid=(width // unit,),
            in_specs=[whole] * 3 + [part] * 2 + [pl.BlockSpec(memory_space=pl.ANY)] * len(extra),
            out_specs=[whole] * 3,
        ),
        out_shape=[out] * 3,
        input_output_aliases=aliases,
        compiler_params=pltpu.CompilerParams(vmem_limit_bytes=48 * 1024 * 1024),
        cost_estimate=SMALL,
    )(end, w, m, v, *grads, *extra)


def attend_kernel(kept_ref, got_ref, bias_ref, table_ref, qkv_ref, out_ref, stat_ref):
    half = ROTARY // 2
    cos, sin, pos = table_ref[0, :half], table_ref[0, half:ROTARY], table_ref[0, ROTARY:]
    parts = []
    for i in range(3):
        v = kept_ref[i, 0].astype(f32) + got_ref[i, 0].astype(f32) + bias_ref[i, 0]
        if i < 2:
            a, b = v[:half], v[half:ROTARY]
            v = jnp.concatenate([a * cos - b * sin, b * cos + a * sin, v[ROTARY:]], axis=0)
        v = v.astype(bf16)
        qkv_ref[i, 0] = v
        parts.append(v)
    q, k, v = parts
    scores = dot(k, q, FIRST) * score_scale
    scores = jnp.where(pos.T[:, :1] <= pos[:1], scores, masked_score)
    peak = jnp.max(scores, axis=0, keepdims=True)
    e = jnp.exp(scores - peak)
    total = jnp.sum(e, axis=0, keepdims=True)
    p = (e / total).astype(bf16)
    out_ref[0] = dot(v, p, PLAIN).astype(bf16)
    stat_ref[0, 0] = jnp.concatenate([peak, total], axis=0)


def attend(kept, got, bias, table):
    _, heads, hd, t = kept.shape
    seqs, _, seq = table.shape
    big = pl.BlockSpec((3, 1, hd, seq), lambda s, h: (0, h, 0, s))
    table_spec = pl.BlockSpec((1, table.shape[1], seq), lambda s, h: (s, 0, 0))
    stat = pl.BlockSpec((1, 1, 2, seq), lambda s, h: (s, h, 0, 0))
    return pl.pallas_call(
        attend_kernel,
        grid=(seqs, heads),
        in_specs=[
            big,
            big,
            pl.BlockSpec((3, 1, hd, 1), lambda s, h: (0, h, 0, 0)),
            table_spec,
        ],
        out_specs=[big, pl.BlockSpec((1, hd, seq), lambda s, h: (h, 0, s)), stat],
        out_shape=[
            jax.ShapeDtypeStruct((3, heads, hd, t), bf16),
            jax.ShapeDtypeStruct((heads, hd, t), bf16),
            jax.ShapeDtypeStruct((seqs, heads, 2, seq), f32),
        ],
        compiler_params=pltpu.CompilerParams(vmem_limit_bytes=32 * 1024 * 1024),
        cost_estimate=SMALL,
    )(kept, got, bias, table)


def attend_back_kernel(qkv_ref, dout_ref, stat_ref, table_ref, out_ref):
    half = ROTARY // 2
    cos, sin, pos = table_ref[0, :half], table_ref[0, half:ROTARY], table_ref[0, ROTARY:]
    q, k, v = qkv_ref[0, 0], qkv_ref[1, 0], qkv_ref[2, 0]
    dout = dout_ref[0]
    scores = dot(k, q, FIRST) * score_scale
    scores = jnp.where(pos.T[:, :1] <= pos[:1], scores, masked_score)
    p = jnp.exp(scores - stat_ref[0, 0, :1]) / stat_ref[0, 0, 1:]
    dp = dot(v, dout, FIRST)
    inner = jnp.sum(p * dp, axis=0, keepdims=True)
    ds = (p * (dp - inner)).astype(bf16)

    def back(x):
        a, b = x[:half], x[half:ROTARY]
        return jnp.concatenate([a * cos + b * sin, b * cos - a * sin, x[ROTARY:]], axis=0)

    out_ref[0, 0] = back(dot(k, ds, PLAIN) * score_scale).astype(bf16)
    out_ref[1, 0] = back(dot(q, ds, LAST) * score_scale).astype(bf16)
    out_ref[2, 0] = dot(dout, p.astype(bf16), LAST).astype(bf16)


def attend_back(qkv, dout, stats, table):
    _, heads, hd, t = qkv.shape
    seqs, _, seq = table.shape
    big = pl.BlockSpec((3, 1, hd, seq), lambda s, h: (0, h, 0, s))
    table_spec = pl.BlockSpec((1, table.shape[1], seq), lambda s, h: (s, 0, 0))
    stat = pl.BlockSpec((1, 1, 2, seq), lambda s, h: (s, h, 0, 0))
    return pl.pallas_call(
        attend_back_kernel,
        grid=(seqs, heads),
        in_specs=[
            big,
            pl.BlockSpec((1, hd, seq), lambda s, h: (h, 0, s)),
            stat,
            table_spec,
        ],
        out_specs=big,
        out_shape=jax.ShapeDtypeStruct((3, heads, hd, t), bf16),
        compiler_params=pltpu.CompilerParams(vmem_limit_bytes=32 * 1024 * 1024),
        cost_estimate=SMALL,
    )(qkv, dout, stats, table)


def body(
    tokens,
    cotangent,
    span_order,
    w_qkv,
    w_out,
    w_up,
    w_down,
    norm_params,
    m_qkv,
    v_qkv,
    m_out,
    v_out,
    m_up,
    v_up,
    m_down,
    v_down,
    m_norm,
    v_norm,
):
    at = Plane()
    do = Order()
    reps = RepSum(do)
    width = tokens.shape[3]
    rows = tokens.shape[1]
    S, Y, nb = at.s_size, at.y_size, at.blocks
    plane = ("ctx", "shard")
    blk = width // nb
    ffb = FF // nb
    heads = blk // HEAD_DIM
    seq = rows * at.ctx_size
    T = S * seq
    H = T // 2
    first = at.c == 0
    core = at.c.reshape(1)
    my_block = at.ctx * S + at.s
    halves = (slice(0, H), slice(H, T))
    seqs = (slice(0, S // 2), slice(S // 2, S))

    def pick(x, axis, which):
        return lax.dynamic_index_in_dim(x, which, axis, keepdims=False)

    def in_order(mine, theirs, axis):
        return jnp.stack([jnp.where(first, mine, theirs), jnp.where(first, theirs, mine)], axis=axis)

    def join(a, b):
        return jnp.concatenate([a, b], axis=0)

    def lanes(a, b):
        return jnp.concatenate([a, b], axis=1)

    x_rows = tokens.reshape(rows, width)
    order = span_order.reshape(-1).astype(f32)
    span = rows // 2

    def pack(x, order):
        xf = x.astype(f32)
        mean = jnp.mean(xf, axis=1)
        centred = xf - mean[:, None]
        inv = lax.rsqrt(jnp.mean(centred * centred, axis=1) + eps_norm)
        mine = lax.dynamic_slice_in_dim(order, 2 * at.ctx, 2)
        place = jnp.repeat(mine, span)
        terms = []
        for v in (mean, inv):
            for _ in range(3):
                t = lax.reduce_precision(v, 8, 7)
                terms.append(t)
                v = v - t
        extra = jnp.stack(terms + [place] + [jnp.zeros_like(place)] * 9).astype(bf16)
        blocks = x.T.reshape(nb, blk, rows)
        return jnp.concatenate([blocks, jnp.broadcast_to(extra[None], (nb, 16, rows))], axis=1)

    packed = do(pack, x_rows, order)
    cot_all = lax.all_gather(cotangent.reshape(rows, width), ("shard", "ctx"), axis=0, tiled=True)
    got = lax.all_to_all(packed, plane, split_axis=0, concat_axis=0, tiled=True)

    def chip_rows(w, lead, unit, count):
        mine, theirs = do(lambda w: split_columns(w, core, lead, unit, count), w)
        return mine, at.core(theirs)

    wq_parts = chip_rows(w_qkv, 0, S * blk, 3 * Y)
    norm_cols = norm_params.reshape(7, nb, blk).transpose(1, 2, 0)
    own_cols = pick(norm_cols, 0, my_block)
    other_cols = pick(norm_cols, 0, (at.ctx ^ 1) * S + at.s)
    pair_cols = join(own_cols, other_cols)
    bias = own_cols[:, 4:7].T.reshape(3, heads, HEAD_DIM, 1)
    spot = jnp.stack([at.y, at.s])

    def cut_weights(parts, pre, unit, flip):
        return do(lambda a, b: arrange(a, b, spot, pre, Y, S, unit, flip), *parts)

    wq_cut = [cut_weights(wq_parts, 3, blk, bool(k)) for k in range(2)]

    def columns(got):
        x = got.reshape(at.ctx_size, S, blk + 16, rows).transpose(2, 1, 0, 3).reshape(blk + 16, T)
        x_own, extra = x[:blk], x[blk:].astype(f32)
        mean = extra[0:1] + extra[1:2] + extra[2:3]
        inv = extra[3:4] + extra[4:5] + extra[5:6]
        return x_own, mean, inv, extra[6:7]

    x_own, mean1, inv1, place = do(columns, got)
    x_other = at.core(x_own)

    def first_norm(mine, theirs, mean, inv, cols):
        x = join(mine, theirs).astype(f32)
        return ((x - mean) * inv * cols[:, 0:1] + cols[:, 1:2]).astype(bf16)

    xn1 = do(first_norm, x_own, x_other, mean1, inv1, pair_cols)
    xn1_own = xn1[:blk]

    def send_products(cut, xs):
        got, kept = [], []
        for k in range(2):
            axis, step = at.steps(bool(k))[0]
            p = do(lambda w, x: dot(w, x, PLAIN).astype(bf16), cut[k][0], xs[k])
            got.append(at.along(p, axis, step))
        for k in range(2):
            kept.append(do(lambda w, x: dot(w, x, PLAIN).astype(bf16), cut[k][1], xs[k]))
        return list(zip(kept, got))

    def scatter_rest(pairs):
        for i in range(1, len(at.steps(False))):
            out = []
            for k in range(2):
                axis, step = at.steps(bool(k))[i]
                bit = (at.index(axis) // step) % 2
                send, kept = do(lambda a, b: add_split(a, b, bit.reshape(1)), *pairs[k])
                out.append((kept, at.along(send, axis, step)))
            pairs = out
        return pairs

    flying = send_products(wq_cut, [xn1[:, h] for h in halves])

    wo_parts = chip_rows(w_out, 0, S * blk, Y)
    wg_parts = chip_rows(w_up, 0, S * ffb, Y)
    wu_parts = chip_rows(w_up, Y, S * ffb, Y)
    wo_cut = [cut_weights(wo_parts, 1, blk, bool(k)) for k in range(2)]

    def positions(place):
        pos = place.reshape(S, seq) * span + (jnp.arange(seq) % span).astype(f32)[None, :]
        prow = pos.reshape(S, 1, seq)
        exponent = jnp.arange(ROTARY // 2, dtype=f32)
        inverse = 10000.0 ** (-2.0 * exponent / ROTARY)
        angles = prow * inverse[None, :, None]
        return jnp.concatenate([jnp.cos(angles), jnp.sin(angles), jnp.broadcast_to(prow, (S, 8, seq))], axis=1)

    table = do(positions, place)
    flying = scatter_rest(flying)
    wg_cut = cut_weights(wg_parts, 1, ffb, False)
    wu_cut = cut_weights(wu_parts, 1, ffb, True)

    qkvs, attns, attn_got, stats = [], [], [], []
    for k in range(2):
        shape = (3, heads, HEAD_DIM, H)
        qkv, attn, stat = do(attend, flying[k][0].reshape(shape), flying[k][1].reshape(shape), bias, table[seqs[k]])
        qkvs.append(qkv)
        attns.append(attn.reshape(blk, H))
        attn_got.append(at.core(attns[k]))
        stats.append(stat)

    pairs = [do(join, attns[k], attn_got[k]) for k in range(2)]
    flying = scatter_rest(send_products(wo_cut, pairs))
    def residual(x, a0, b0, a1, b1):
        a, b = lanes(a0, a1), lanes(b0, b1)
        hidden = x.astype(f32) + (a.astype(f32) + b.astype(f32))
        local_mean = jnp.mean(hidden, axis=0, keepdims=True)
        dev = hidden - local_mean
        return hidden, join(local_mean, jnp.sum(dev * dev, axis=0, keepdims=True))

    hidden, moments = do(residual, x_own, *flying[0], *flying[1])
    count = blk
    for axis, step in at.steps(False) + [("core", 1)]:
        other = at.core(moments) if axis == "core" else at.along(moments, axis, step)

        def merge(a, b):
            gap = a[0:1] - b[0:1]
            return join(0.5 * (a[0:1] + b[0:1]), a[1:2] + b[1:2] + gap * gap * (count / 2.0))

        moments = do(merge, moments, other)
        count *= 2

    def second_norm(hidden, moments, cols):
        inv2 = lax.rsqrt(moments[1:2] / width + eps_norm)
        z2 = (hidden - moments[0:1]) * inv2
        return (z2 * cols[:, 2:3] + cols[:, 3:4]).astype(bf16), z2, inv2

    xn2_own, z2, inv2 = do(second_norm, hidden, moments, own_cols)
    xn2 = do(join, xn2_own, at.core(xn2_own))

    flying = send_products([wg_cut, wu_cut], [xn2, xn2])

    wu_nat = do(cast, w_up)

    def gain_products(w, cols):
        terms = []
        for v in (cols[:, 2], cols[:, 3]):
            t = lax.reduce_precision(v, 8, 7)
            terms += [t, v - t]
        p = dot(jnp.stack(terms).astype(bf16), w, PLAIN)
        p = jnp.stack([p[0] + p[1], p[2] + p[3]])
        return p.reshape(2, 2, nb, ffb).transpose(2, 1, 0, 3).reshape(nb, 4, ffb)

    gains = do(gain_products, wu_nat, own_cols)
    gains = lax.psum_scatter(gains, plane, scatter_dimension=0, tiled=True).reshape(4, ffb, 1)
    wd_own = do(cast, w_down)
    grad_act = do(lambda w, c: dot(w, c, LAST), wd_own, cot_all)
    cot_cols = do(lambda c: lax.dynamic_slice_in_dim(c, my_block * blk, blk, 1).T, cot_all)
    wo_own = do(cast, w_out)
    wq_nat = do(cast, w_qkv)
    flying = scatter_rest(flying)

    def gated(ga, gb, ua, ub, grad_act, gains):
        gate = ga.astype(f32) + gb.astype(f32)
        up = ua.astype(f32) + ub.astype(f32)
        sig = jax.nn.sigmoid(gate)
        silu = gate * sig
        ggate = (grad_act * up * sig * (1.0 + gate * (1.0 - sig))).astype(bf16)
        gup = (grad_act * silu).astype(bf16)
        return ggate, gup, (silu * up).astype(bf16), gate, up

    ggate, gup, act, gate, up = do(gated, *flying[0], *flying[1], grad_act, gains)

    def parts_of(count, want):
        return max(n for n in range(1, want + 1) if count % (16 * n) == 0)

    def even(count, want):
        n = parts_of(count, want)
        return [(k * (count // n), count // n) for k in range(n)]

    down_rows, up_rows, out_rows = even(ffb, 4), even(blk, 4), even(blk, 2)
    thirds = {2: even(blk, 2), 1: even(blk, 2), 0: even(blk, 4)}

    def push(name, g, rows):
        for k, (at_row, count) in enumerate(rows):
            reps.push((name, k), g[at_row : at_row + count])

    results = {"down": None, "out": None, "up": None, "qkv": None}
    states = {
        "down": (w_down, m_down, v_down),
        "out": (w_out, m_out, v_out),
        "up": (w_up, m_up, v_up),
        "qkv": (w_qkv, m_qkv, v_qkv),
    }
    rates = {"down": 0.02, "out": 0.2, "up": 0.03, "qkv": 0.03}
    jobs = []
    wide = FF // 4
    for name, state, lead, unit, cuts in (
        [("down", "down", 0, 1024, down_rows), ("gate", "up", 0, wide, up_rows), ("up", "up", FF // wide, wide, up_rows)]
        + [("out", "out", 0, 1024, out_rows)]
        + [(third, "qkv", third * width // 1024, 1024, thirds[third]) for third in (2, 1, 0)]
    ):
        for k, (at_row, count) in enumerate(cuts):
            jobs.append((state, (name, k), at_row // count, lead, unit))
    end = reps.end.astype(jnp.int32).reshape(1)

    def update(limit):
        while jobs and limit and jobs[0][1] in reps.done:
            name, key, row_block, lead, unit = jobs.pop(0)
            results[name] = do(
                lambda s, g, prev: adam_part(s, g, end, rates[name], prev, row_block, lead, unit),
                states[name],
                reps.done[key],
                results[name],
            )
            limit -= 1

    def everywhere(x):
        return lax.all_gather(x, plane, axis=0, tiled=True)

    def ticks(n):
        for _ in range(n):
            reps.tick()

    ggate_all = everywhere(ggate)
    gup_all = everywhere(gup)
    g_down = do(lambda a, c: dot(a, c, PLAIN).astype(bf16), act, cot_all)
    push("down", g_down, down_rows)
    reps.tick()

    def norm_sums2(ggate, gup, gate, up, gains):
        a, b = ggate.astype(f32), gup.astype(f32)
        e = jnp.sum(a * gains[0] + b * gains[2], axis=0, keepdims=True)
        ez = jnp.sum(a * (gate - gains[1]) + b * (up - gains[3]), axis=0, keepdims=True)
        return join(e, ez)

    sums = do(norm_sums2, ggate, gup, gate, up, gains)
    reps.tick()
    steps2 = at.steps(False) + [("core", 1)]

    def sum_step(sums, axis, step):
        other = at.core(sums) if axis == "core" else at.along(sums, axis, step)
        return do(lambda a, b: a + b, sums, other)

    for axis, step in steps2:
        sums = sum_step(sums, axis, step)
    reps.tick()
    out_part = do(lambda w, a: dot(w, a, FIRST).astype(bf16), wd_own, act)
    ticks(2)
    part_gate = do(lambda w, g: dot(w, g, PLAIN), wu_nat[:, :FF], ggate_all)
    g_gate = do(lambda x, g: dot(x, g, LAST).astype(bf16), xn2_own, ggate_all)
    push("gate", g_gate, up_rows)
    ticks(4)
    update(1)
    reps.tick()
    gxn2 = do(lambda w, g, p: dot(w, g, PLAIN) + p, wu_nat[:, FF:], gup_all, part_gate)

    def branch(gxn2, cot, z, scale, gain, sums):
        e = gxn2 * gain
        grad_hidden = cot.astype(f32) + scale * (e - sums[0:1] / width - z * (sums[1:2] / width))
        return grad_hidden.astype(bf16), grad_hidden

    grad_branch, grad_hidden = do(branch, gxn2, cot_cols, z2, inv2, own_cols[:, 2:3], sums)
    gbr = everywhere(grad_branch)
    g_up = do(lambda x, g: dot(x, g, LAST).astype(bf16), xn2_own, gup_all)
    push("up", g_up, up_rows)
    reps.tick()
    update(2)
    reps.tick()
    update(1)
    grad_attn = do(lambda w, g: dot(w, g, PLAIN).astype(bf16), wo_own, gbr)

    gqkvs = []
    for k in range(2):
        dout = grad_attn[:, halves[k]].reshape(heads, HEAD_DIM, H)
        gqkvs.append(do(attend_back, qkvs[k], dout, stats[k], table[seqs[k]]))
        if k == 0:
            reps.tick()
    gqkv_own = do(lambda a, b: [lanes(a[i].reshape(blk, H), b[i].reshape(blk, H)) for i in range(3)], *gqkvs)
    gathered = {third: everywhere(gqkv_own[third]) for third in (2, 1, 0)}
    out_sum = lax.psum_scatter(out_part, plane, scatter_dimension=0, tiled=True)
    attn = lanes(*attns)
    g_out = do(lambda a, g: dot(a, g, LAST).astype(bf16), attn, gbr)
    push("out", g_out, out_rows)
    gxn1 = None
    for third in (2, 1, 0):
        reps.tick()
        update(1)
        reps.tick()
        g_all = gathered[third]
        w_third = wq_nat[:, third * width : (third + 1) * width]
        if gxn1 is None:
            gxn1 = do(lambda w, g: dot(w, g, PLAIN), w_third, g_all)
        else:
            gxn1 = do(lambda w, g, p: dot(w, g, PLAIN) + p, w_third, g_all, gxn1)
        g = do(lambda x, g: dot(x, g, LAST).astype(bf16), xn1_own, g_all)
        push(third, g, thirds[third])
    reps.tick()

    def first_back(gxn1, x, mean, inv, gain, gxn2, z2, parts):
        z1 = (x.astype(f32) - mean) * inv
        e = gxn1 * gain
        sums = join(jnp.sum(e, axis=0, keepdims=True), jnp.sum(e * z1, axis=0, keepdims=True))
        small = [gxn1 * z1, gxn1, gxn2 * z2, gxn2] + [p.astype(f32) for p in parts]
        small = jnp.stack([jnp.sum(p, axis=1) for p in small])
        return sums, small, z1

    sums, small, z1 = do(first_back, gxn1, x_own, mean1, inv1, own_cols[:, 0:1], gxn2, z2, gqkv_own)
    for axis, step in steps2:
        sums = sum_step(sums, axis, step)
    reps.tick()
    update(1)
    input_grad = do(
        lambda h, grad, z, scale, gain, sums: h
        + scale * (grad * gain - sums[0:1] / width - z * (sums[1:2] / width)),
        grad_hidden,
        gxn1,
        z1,
        inv1,
        own_cols[:, 0:1],
        sums,
    )
    out_cols = do(lambda h, a: (h + a.astype(f32)).astype(bf16), hidden, out_sum)
    reps.tick()
    update(1)

    def to_rows(cols):
        split = do(lambda c: c.reshape(blk, S, at.ctx_size, rows).transpose(2, 1, 0, 3).reshape(nb, blk, rows), cols)
        got = lax.all_to_all(split, plane, split_axis=0, concat_axis=0, tiled=True)
        return do(lambda g: g.reshape(width, rows).T, got)

    input_rows = to_rows(input_grad)
    reps.tick()
    update(1)
    block_output = to_rows(out_cols)
    reps.tick()
    update(1)

    n_rep = lax.axis_size("rep")
    step = 1
    while step < n_rep:
        other = lax.ppermute(small, "rep", [(i, i ^ step) for i in range(n_rep)])
        small = do(lambda a, b: a + b, small, other)
        step *= 2
    sent = do(lambda s: jnp.broadcast_to(s.reshape(1, 7, blk), (nb, 7, blk)), small)
    got = lax.all_to_all(sent, plane, split_axis=0, concat_axis=0, tiled=True)
    norm_grad = got.transpose(1, 0, 2).reshape(7, width)
    mn, vn, wn = do(lambda *a: adam_update(*a, 0.3, 0.0), norm_params, m_norm, v_norm, norm_grad)

    while reps.busy():
        reps.tick()
        update(1)
    update(len(jobs))
    return (
        (block_output.reshape(tokens.shape), input_rows.reshape(tokens.shape))
        + tuple(results["qkv"])
        + tuple(results["out"])
        + tuple(results["up"])
        + tuple(results["down"])
        + (mn, vn, wn)
    )


def solution(mesh):
    tok = P("rep", "ctx", "shard", None)
    row = P(("ctx", "shard"), None)
    placed = (tok, tok, P("rep", "shard", None)) + (row,) * 4 + (P(),) + (row,) * 8 + (P(), P())
    return jax.shard_map(
        body,
        mesh=mesh,
        in_specs=placed,
        out_specs=(tok, tok) + (row,) * 12 + (P(),) * 3,
        check_vma=False,
    )
```

```python
import functools

import jax
import jax.numpy as jnp
from jax import lax
from jax.experimental import pallas as pl
from jax.experimental.pallas import tpu as pltpu
from jax.sharding import PartitionSpec as P

HEADS = 32
HEAD_DIM = 64
FF = 5632
ROTARY = 16
STEP = 10

eps_norm = 1e-05
masked_score = -1e30
beta_one = 0.9
beta_two = 0.999
adam_eps = 1e-08
weight_decay = 0.1
score_scale = HEAD_DIM ** (-0.5)
FIRST = (((0,), (0,)), ((), ()))
LAST = (((1,), (1,)), ((), ()))
PLAIN = (((1,), (0,)), ((), ()))
bf16 = jnp.bfloat16
f32 = jnp.float32


def dot(a, b, dims):
    return lax.dot_general(a, b, dims, preferred_element_type=f32)


def adam_update(weight, moment_one, moment_two, grad, step_rate, decay_rate):
    first_new = beta_one * moment_one + (1.0 - beta_one) * grad
    second_new = beta_two * moment_two + (1.0 - beta_two) * grad * grad
    first_hat = first_new / (1.0 - beta_one**STEP)
    second_hat = second_new / (1.0 - beta_two**STEP)
    weight_new = weight - step_rate * (
        first_hat / (jnp.sqrt(second_hat) + adam_eps) + decay_rate * weight
    )
    return (first_new, second_new, weight_new)


class Plane:
    def __init__(self):
        self.s_size = lax.axis_size("shard")
        self.ctx_size = lax.axis_size("ctx")
        self.y_size = self.ctx_size // 2
        self.ctx = lax.axis_index("ctx")
        self.s = lax.axis_index("shard")
        self.y = self.ctx // 2
        self.c = self.ctx % 2
        self.blocks = self.ctx_size * self.s_size

    def core(self, x):
        return lax.ppermute(x, "ctx", [(i, i ^ 1) for i in range(self.ctx_size)])

    def along(self, x, axis, step):
        if axis == "y":
            return lax.ppermute(x, "ctx", [(i, i ^ (2 * step)) for i in range(self.ctx_size)])
        return lax.ppermute(x, "shard", [(i, i ^ step) for i in range(self.s_size)])

    def index(self, axis):
        return self.y if axis == "y" else self.s

    def steps(self, flip):
        ys = []
        k = self.y_size // 2
        while k:
            ys.append(("y", k))
            k //= 2
        ss = []
        k = self.s_size // 2
        while k:
            ss.append(("s", k))
            k //= 2
        return ys + ss if flip else ss + ys

    def chip_exchange(self, x, take):
        out = [(self.y, self.s, take(self.y, self.s))]
        for ry in range(self.y_size):
            for rs in range(self.s_size):
                if ry or rs:
                    y, s = self.y ^ ry, self.s ^ rs
                    mask = 2 * ry * self.s_size + rs
                    perm = [(i, i ^ mask) for i in range(self.blocks)]
                    out.append((y, s, lax.ppermute(take(y, s), ("ctx", "shard"), perm)))
        return out

    def sum_all(self, x):
        for axis, step in self.steps(False):
            x = x + self.along(x, axis, step)
        return x + self.core(x)

    def scatter_sum(self, p, flip):
        axes = {"y": 1, "s": 2}
        steps = self.steps(flip)
        kept = got = None
        for n, (axis, step) in enumerate(steps):
            ax = axes[axis]
            bit = (self.index(axis) // step) % 2
            kept = lax.dynamic_slice_in_dim(p, bit * step, step, ax)
            send = lax.dynamic_slice_in_dim(p, (1 - bit) * step, step, ax)
            got = self.along(send, axis, step)
            if n + 1 < len(steps):
                p = (kept.astype(f32) + got.astype(f32)).astype(bf16)
        return kept[:, 0, 0], got[:, 0, 0]

    def gather(self, p, flip):
        axes = {"y": 1, "s": 2}
        p = p[:, None, None]
        for axis, step in reversed(self.steps(flip)):
            ax = axes[axis]
            bit = (self.index(axis) // step) % 2
            got = self.along(p, axis, step)
            first = bit == 0
            p = jnp.concatenate([jnp.where(first, p, got), jnp.where(first, got, p)], ax)
        return p


class Order:
    def __init__(self):
        self.last = None

    def __call__(self, stage, *args):
        if self.last is not None:
            args, self.last = lax.optimization_barrier((args, self.last))
        out = stage(*args)
        self.last = jax.tree.leaves(out)[0]
        return out


SMALL = pl.CostEstimate(flops=1024, bytes_accessed=1024, transcendentals=0)


class RepSum:
    def __init__(self, order):
        self.order = order
        z = lax.axis_index("rep")
        self.end = (z == 0) | (z == lax.axis_size("rep") - 1)
        self.queue = []
        self.flight = []
        self.done = {}

    def push(self, name, g):
        self.queue.append((name, g))

    def busy(self):
        return bool(self.queue or self.flight)

    def tick(self):
        old = {}
        if len(self.flight) == 2 or (self.flight and not self.queue):
            old = self.flight.pop(0)
        new = self.queue.pop(0) if self.queue else None
        values = {}
        if "in" in old:
            values["g"], values["g_got"] = old["in"][1], old["in_got"]
        if "mid" in old:
            values["s"], values["s_got"] = old["mid"][1], old["mid_got"]
        if new:
            values["new"] = new[1]
        both = new and "mid" in old and new[1].shape == old["mid"][1].shape
        if "out" in old:
            values["out_got"] = old["out_got"]

        def stage(v):
            def add(a, b):
                return lax.reduce_precision(a.astype(f32) + b.astype(f32), 8, 7).astype(bf16)

            out = {}
            if "g" in v:
                out["a_sum"] = add(v["g"], v["g_got"])
            if "s" in v:
                total = add(v["s"], v["s_got"])
                out["total"] = jnp.where(self.end, v["new"], total) if both else total
            if "new" in v and not both:
                out["new"] = v["new"]
            if "out_got" in v:
                out["z_got"] = v["out_got"]
            return out

        if not values:
            return
        out = self.order(stage, values)
        if "out" in old:
            self.done[old["out"][0]] = jnp.where(self.end, out["z_got"], old["out"][1])
        slot = {}
        if both:
            got = lax.ppermute(out["total"], "rep", [(0, 1), (1, 0), (2, 3), (3, 2)])
            slot = {"in": new, "in_got": got, "out": (old["mid"][0], out["total"]), "out_got": got}
        else:
            if new:
                slot["in"] = new
                slot["in_got"] = lax.ppermute(out["new"], "rep", [(0, 1), (3, 2)])
            if "mid" in old:
                slot["out"] = (old["mid"][0], out["total"])
                slot["out_got"] = lax.ppermute(out["total"], "rep", [(1, 0), (2, 3)])
        if "in" in old:
            slot["mid"] = (old["in"][0], out["a_sum"])
            slot["mid_got"] = lax.ppermute(out["a_sum"], "rep", [(1, 2), (2, 1)])
        if slot:
            self.flight.append(slot)


def cast_kernel(w_ref, out_ref):
    out_ref[...] = w_ref[...].astype(bf16)


def cast(w):
    rows, width = w.shape
    unit = max(n for n in (128, 256, 512, 1024, 1408, 2048, 2816) if width % n == 0)
    spec = pl.BlockSpec((rows, unit), lambda i: (0, i))
    return pl.pallas_call(
        cast_kernel,
        grid=(width // unit,),
        in_specs=[spec],
        out_specs=spec,
        out_shape=jax.ShapeDtypeStruct(w.shape, bf16),
        compiler_params=pltpu.CompilerParams(vmem_limit_bytes=48 * 1024 * 1024),
        cost_estimate=SMALL,
    )(w)


def split_kernel(core_ref, w_ref, mine_ref, theirs_ref):
    unit = mine_ref.shape[0]
    first = core_ref[0] == 0
    a, b = w_ref[:, :unit], w_ref[:, unit:]
    mine_ref[...] = jnp.where(first, a, b).T.astype(bf16)
    theirs_ref[...] = jnp.where(first, b, a).T.astype(bf16)


def split_columns(w, core, lead, unit, count):
    rows = w.shape[0]
    half = pl.BlockSpec((unit, rows), lambda j, core: (j, 0))
    out = jax.ShapeDtypeStruct((count * unit, rows), bf16)
    return pl.pallas_call(
        split_kernel,
        grid_spec=pltpu.PrefetchScalarGridSpec(
            num_scalar_prefetch=1,
            grid=(count,),
            in_specs=[pl.BlockSpec((rows, 2 * unit), lambda j, core: (0, lead + j))],
            out_specs=[half, half],
        ),
        out_shape=[out, out],
        compiler_params=pltpu.CompilerParams(vmem_limit_bytes=32 * 1024 * 1024),
        cost_estimate=SMALL,
    )(core, w)


def arrange_kernel(at_ref, a_ref, b_ref, c_ref, d_ref, send_ref, keep_ref):
    send_ref[...] = jnp.concatenate([a_ref[...], b_ref[...]], axis=1)
    keep_ref[...] = jnp.concatenate([c_ref[...], d_ref[...]], axis=1)


def arrange(mine, got, place, pre, y_size, s_size, unit, flip):
    r = mine.shape[1]
    half = pre * y_size * s_size // 2

    def block(i, place, keep):
        p = i % pre
        i = i // pre
        if flip:
            s, y = i % s_size, i // s_size
            bit = place[0] // (y_size // 2)
            bit = bit if keep else 1 - bit
            y = y + bit * (y_size // 2)
        else:
            y, s = i % y_size, i // y_size
            bit = place[1] // (s_size // 2)
            bit = bit if keep else 1 - bit
            s = s + bit * (s_size // 2)
        return ((p * y_size + y) * s_size + s, 0)

    def spec(keep):
        return pl.BlockSpec((unit, r), lambda i, place: block(i, place, keep))

    out = jax.ShapeDtypeStruct((half * unit, 2 * r), bf16)
    out_spec = pl.BlockSpec((unit, 2 * r), lambda i, place: (i, 0))
    return pl.pallas_call(
        arrange_kernel,
        grid_spec=pltpu.PrefetchScalarGridSpec(
            num_scalar_prefetch=1,
            grid=(half,),
            in_specs=[spec(False), spec(False), spec(True), spec(True)],
            out_specs=[out_spec, out_spec],
        ),
        out_shape=[out, out],
        compiler_params=pltpu.CompilerParams(vmem_limit_bytes=32 * 1024 * 1024),
        cost_estimate=SMALL,
    )(place, mine, got, mine, got)


def lanes_kernel(a_ref, b_ref, out_ref):
    out_ref[...] = jnp.concatenate([a_ref[...], b_ref[...]], axis=1)


def side_by_side(a, b):
    rows, width = a.shape
    n = max(n for n in (1, 2, 4, 8) if rows % (16 * n) == 0)
    spec = pl.BlockSpec((rows // n, width), lambda i: (i, 0))
    return pl.pallas_call(
        lanes_kernel,
        grid=(n,),
        in_specs=[spec, spec],
        out_specs=pl.BlockSpec((rows // n, 2 * width), lambda i: (i, 0)),
        out_shape=jax.ShapeDtypeStruct((rows, 2 * width), bf16),
        compiler_params=pltpu.CompilerParams(vmem_limit_bytes=48 * 1024 * 1024),
        cost_estimate=SMALL,
    )(a, b)


def add_split_kernel(bit_ref, a_ref, b_ref, c_ref, d_ref, send_ref, keep_ref):
    send_ref[...] = (a_ref[...].astype(f32) + b_ref[...].astype(f32)).astype(bf16)
    keep_ref[...] = (c_ref[...].astype(f32) + d_ref[...].astype(f32)).astype(bf16)


def add_split(kept, got, bit):
    rows, t = kept.shape
    half = rows // 2
    n = max(n for n in (1, 2, 3, 4) if half % (16 * n) == 0)
    rb = half // n
    away = pl.BlockSpec((rb, t), lambda i, bit: ((1 - bit[0]) * n + i, 0))
    here = pl.BlockSpec((rb, t), lambda i, bit: (bit[0] * n + i, 0))
    out = jax.ShapeDtypeStruct((half, t), bf16)
    out_spec = pl.BlockSpec((rb, t), lambda i, bit: (i, 0))
    return pl.pallas_call(
        add_split_kernel,
        grid_spec=pltpu.PrefetchScalarGridSpec(
            num_scalar_prefetch=1,
            grid=(n,),
            in_specs=[away, away, here, here],
            out_specs=[out_spec, out_spec],
        ),
        out_shape=[out, out],
        compiler_params=pltpu.CompilerParams(vmem_limit_bytes=48 * 1024 * 1024),
        cost_estimate=SMALL,
    )(bit, kept, got, kept, got)


def adam_kernel(rate, two, core_ref, w_ref, m_ref, v_ref, *refs):
    grad = refs[0][...].astype(f32)
    if two:
        other = refs[1][...].astype(f32)
        mine = core_ref[0] == 0
        grad = jnp.concatenate([jnp.where(mine, grad, other), jnp.where(mine, other, grad)], axis=1)
    new_m_ref, new_v_ref, new_w_ref = refs[-3:]
    new_m, new_v, new_w = adam_update(w_ref[...], m_ref[...], v_ref[...], grad, rate, weight_decay)
    new_m_ref[...] = new_m
    new_v_ref[...] = new_v
    new_w_ref[...] = new_w


def adam_part(state, grads, core, rate, prev, row_first, lead, unit, rb):
    w, m, v = state
    two = len(grads) == 2
    rows, width = grads[0].shape
    whole = pl.BlockSpec((rb, unit * len(grads)), lambda i, g, core: (row_first // rb + i, lead + g))
    half = pl.BlockSpec((rb, unit), lambda i, g, core: (i, g))
    out = jax.ShapeDtypeStruct(w.shape, f32)
    extra, aliases = [], {}
    if prev is not None:
        extra = list(prev)
        aliases = {4 + len(grads) + i: i for i in range(3)}
    return pl.pallas_call(
        functools.partial(adam_kernel, rate, two),
        grid_spec=pltpu.PrefetchScalarGridSpec(
            num_scalar_prefetch=1,
            grid=(rows // rb, width // unit),
            in_specs=[whole] * 3 + [half] * len(grads) + [pl.BlockSpec(memory_space=pl.ANY)] * len(extra),
            out_specs=[whole] * 3,
        ),
        out_shape=[out] * 3,
        input_output_aliases=aliases,
        compiler_params=pltpu.CompilerParams(vmem_limit_bytes=48 * 1024 * 1024),
        cost_estimate=SMALL,
    )(core, w, m, v, *grads, *extra)


def attend_kernel(kept_ref, got_ref, bias_ref, table_ref, qkv_ref, out_ref, stat_ref):
    half = ROTARY // 2
    cos, sin, pos = table_ref[0, :half], table_ref[0, half:ROTARY], table_ref[0, ROTARY:]
    parts = []
    for i in range(3):
        v = kept_ref[i, 0].astype(f32) + got_ref[i, 0].astype(f32) + bias_ref[i, 0]
        if i < 2:
            a, b = v[:half], v[half:ROTARY]
            v = jnp.concatenate([a * cos - b * sin, b * cos + a * sin, v[ROTARY:]], axis=0)
        v = v.astype(bf16)
        qkv_ref[i, 0] = v
        parts.append(v)
    q, k, v = parts
    scores = dot(k, q, FIRST) * score_scale
    scores = jnp.where(pos.T[:, :1] <= pos[:1], scores, masked_score)
    peak = jnp.max(scores, axis=0, keepdims=True)
    e = jnp.exp(scores - peak)
    total = jnp.sum(e, axis=0, keepdims=True)
    p = (e / total).astype(bf16)
    out_ref[0] = dot(v, p, PLAIN).astype(bf16)
    stat_ref[0, 0] = jnp.concatenate([peak, total], axis=0)


def attend(kept, got, bias, table):
    _, heads, hd, t = kept.shape
    seqs, _, seq = table.shape
    big = pl.BlockSpec((3, 1, hd, seq), lambda s, h: (0, h, 0, s))
    table_spec = pl.BlockSpec((1, table.shape[1], seq), lambda s, h: (s, 0, 0))
    stat = pl.BlockSpec((1, 1, 2, seq), lambda s, h: (s, h, 0, 0))
    return pl.pallas_call(
        attend_kernel,
        grid=(seqs, heads),
        in_specs=[
            big,
            big,
            pl.BlockSpec((3, 1, hd, 1), lambda s, h: (0, h, 0, 0)),
            table_spec,
        ],
        out_specs=[big, pl.BlockSpec((1, hd, seq), lambda s, h: (h, 0, s)), stat],
        out_shape=[
            jax.ShapeDtypeStruct((3, heads, hd, t), bf16),
            jax.ShapeDtypeStruct((heads, hd, t), bf16),
            jax.ShapeDtypeStruct((seqs, heads, 2, seq), f32),
        ],
        compiler_params=pltpu.CompilerParams(vmem_limit_bytes=32 * 1024 * 1024),
        cost_estimate=SMALL,
    )(kept, got, bias, table)


def attend_back_kernel(qkv_ref, dout_ref, stat_ref, table_ref, out_ref):
    half = ROTARY // 2
    cos, sin, pos = table_ref[0, :half], table_ref[0, half:ROTARY], table_ref[0, ROTARY:]
    q, k, v = qkv_ref[0, 0], qkv_ref[1, 0], qkv_ref[2, 0]
    dout = dout_ref[0]
    scores = dot(k, q, FIRST) * score_scale
    scores = jnp.where(pos.T[:, :1] <= pos[:1], scores, masked_score)
    p = jnp.exp(scores - stat_ref[0, 0, :1]) / stat_ref[0, 0, 1:]
    dp = dot(v, dout, FIRST)
    inner = jnp.sum(p * dp, axis=0, keepdims=True)
    ds = (p * (dp - inner)).astype(bf16)

    def back(x):
        a, b = x[:half], x[half:ROTARY]
        return jnp.concatenate([a * cos + b * sin, b * cos - a * sin, x[ROTARY:]], axis=0)

    out_ref[0, 0] = back(dot(k, ds, PLAIN) * score_scale).astype(bf16)
    out_ref[1, 0] = back(dot(q, ds, LAST) * score_scale).astype(bf16)
    out_ref[2, 0] = dot(dout, p.astype(bf16), LAST).astype(bf16)


def attend_back(qkv, dout, stats, table):
    _, heads, hd, t = qkv.shape
    seqs, _, seq = table.shape
    big = pl.BlockSpec((3, 1, hd, seq), lambda s, h: (0, h, 0, s))
    table_spec = pl.BlockSpec((1, table.shape[1], seq), lambda s, h: (s, 0, 0))
    stat = pl.BlockSpec((1, 1, 2, seq), lambda s, h: (s, h, 0, 0))
    return pl.pallas_call(
        attend_back_kernel,
        grid=(seqs, heads),
        in_specs=[
            big,
            pl.BlockSpec((1, hd, seq), lambda s, h: (h, 0, s)),
            stat,
            table_spec,
        ],
        out_specs=big,
        out_shape=jax.ShapeDtypeStruct((3, heads, hd, t), bf16),
        compiler_params=pltpu.CompilerParams(vmem_limit_bytes=32 * 1024 * 1024),
        cost_estimate=SMALL,
    )(qkv, dout, stats, table)


def body(
    tokens,
    cotangent,
    span_order,
    w_qkv,
    w_out,
    w_up,
    w_down,
    norm_params,
    m_qkv,
    v_qkv,
    m_out,
    v_out,
    m_up,
    v_up,
    m_down,
    v_down,
    m_norm,
    v_norm,
):
    at = Plane()
    do = Order()
    reps = RepSum(do)
    width = tokens.shape[3]
    rows = tokens.shape[1]
    S, Y, nb = at.s_size, at.y_size, at.blocks
    plane = ("ctx", "shard")
    blk = width // nb
    ffb = FF // nb
    heads = blk // HEAD_DIM
    seq = rows * at.ctx_size
    T = S * seq
    H = T // 2
    first = at.c == 0
    core = at.c.reshape(1)
    my_block = at.ctx * S + at.s
    halves = (slice(0, H), slice(H, T))
    seqs = (slice(0, S // 2), slice(S // 2, S))

    def pick(x, axis, which):
        return lax.dynamic_index_in_dim(x, which, axis, keepdims=False)

    def in_order(mine, theirs, axis):
        return jnp.stack([jnp.where(first, mine, theirs), jnp.where(first, theirs, mine)], axis=axis)

    def join(a, b):
        return jnp.concatenate([a, b], axis=0)

    def lanes(a, b):
        return jnp.concatenate([a, b], axis=1)

    x_rows = tokens.reshape(rows, width)
    order = span_order.reshape(-1).astype(f32)
    span = rows // 2

    def pack(x, order):
        xf = x.astype(f32)
        mean = jnp.mean(xf, axis=1)
        centred = xf - mean[:, None]
        inv = lax.rsqrt(jnp.mean(centred * centred, axis=1) + eps_norm)
        mine = lax.dynamic_slice_in_dim(order, 2 * at.ctx, 2)
        place = jnp.repeat(mine, span)
        terms = []
        for v in (mean, inv):
            for _ in range(3):
                t = lax.reduce_precision(v, 8, 7)
                terms.append(t)
                v = v - t
        extra = jnp.stack(terms + [place] + [jnp.zeros_like(place)] * 9).astype(bf16)
        blocks = x.T.reshape(nb, blk, rows)
        return jnp.concatenate([blocks, jnp.broadcast_to(extra[None], (nb, 16, rows))], axis=1)

    packed = do(pack, x_rows, order)
    cot_all = lax.all_gather(cotangent.reshape(rows, width), ("shard", "ctx"), axis=0, tiled=True)
    got = lax.all_to_all(packed, plane, split_axis=0, concat_axis=0, tiled=True)

    def chip_rows(w, lead, unit, count):
        mine, theirs = do(lambda w: split_columns(w, core, lead, unit, count), w)
        return mine, at.core(theirs)

    wq_parts = chip_rows(w_qkv, 0, S * blk, 3 * Y)
    norm_cols = norm_params.reshape(7, nb, blk).transpose(1, 2, 0)
    own_cols = pick(norm_cols, 0, my_block)
    other_cols = pick(norm_cols, 0, (at.ctx ^ 1) * S + at.s)
    pair_cols = join(own_cols, other_cols)
    bias = own_cols[:, 4:7].T.reshape(3, heads, HEAD_DIM, 1)
    spot = jnp.stack([at.y, at.s])

    def cut_weights(parts, pre, unit, flip):
        return do(lambda a, b: arrange(a, b, spot, pre, Y, S, unit, flip), *parts)

    wq_cut = [cut_weights(wq_parts, 3, blk, bool(k)) for k in range(2)]

    def columns(got):
        x = got.reshape(at.ctx_size, S, blk + 16, rows).transpose(2, 1, 0, 3).reshape(blk + 16, T)
        x_own, extra = x[:blk], x[blk:].astype(f32)
        mean = extra[0:1] + extra[1:2] + extra[2:3]
        inv = extra[3:4] + extra[4:5] + extra[5:6]
        return x_own, mean, inv, extra[6:7]

    x_own, mean1, inv1, place = do(columns, got)
    x_other = at.core(x_own)

    def first_norm(mine, theirs, mean, inv, cols):
        x = join(mine, theirs).astype(f32)
        return ((x - mean) * inv * cols[:, 0:1] + cols[:, 1:2]).astype(bf16)

    xn1 = do(first_norm, x_own, x_other, mean1, inv1, pair_cols)

    def send_products(cut, xs):
        got, kept = [], []
        for k in range(2):
            axis, step = at.steps(bool(k))[0]
            p = do(lambda w, x: dot(w, x, PLAIN).astype(bf16), cut[k][0], xs[k])
            got.append(at.along(p, axis, step))
        for k in range(2):
            kept.append(do(lambda w, x: dot(w, x, PLAIN).astype(bf16), cut[k][1], xs[k]))
        return list(zip(kept, got))

    def scatter_rest(pairs):
        for i in range(1, len(at.steps(False))):
            out = []
            for k in range(2):
                axis, step = at.steps(bool(k))[i]
                bit = (at.index(axis) // step) % 2
                send, kept = do(lambda a, b: add_split(a, b, bit.reshape(1)), *pairs[k])
                out.append((kept, at.along(send, axis, step)))
            pairs = out
        return pairs

    flying = send_products(wq_cut, [xn1[:, h] for h in halves])

    wo_parts = chip_rows(w_out, 0, S * blk, Y)
    wg_parts = chip_rows(w_up, 0, S * ffb, Y)
    wu_parts = chip_rows(w_up, Y, S * ffb, Y)
    wo_cut = [cut_weights(wo_parts, 1, blk, bool(k)) for k in range(2)]

    def positions(place):
        pos = place.reshape(S, seq) * span + (jnp.arange(seq) % span).astype(f32)[None, :]
        prow = pos.reshape(S, 1, seq)
        exponent = jnp.arange(ROTARY // 2, dtype=f32)
        inverse = 10000.0 ** (-2.0 * exponent / ROTARY)
        angles = prow * inverse[None, :, None]
        return jnp.concatenate([jnp.cos(angles), jnp.sin(angles), jnp.broadcast_to(prow, (S, 8, seq))], axis=1)

    table = do(positions, place)
    flying = scatter_rest(flying)
    wg_cut = cut_weights(wg_parts, 1, ffb, False)
    wu_cut = cut_weights(wu_parts, 1, ffb, True)

    def gather_steps(parts, row_axis):
        n = len(at.steps(False))
        state = {"parts": list(parts)}

        def start(i):
            state["got"] = []
            state["at"] = []
            for k in range(2):
                axis, step = list(reversed(at.steps(bool(k))))[i]
                state["at"].append((axis, step))
                state["got"].append(at.along(state["parts"][k], axis, step))

        def finish():
            def put(parts, got):
                out = []
                for k in range(2):
                    axis, step = state["at"][k]
                    ax = {"y": 0, "s": 1}[axis]
                    low = (at.index(axis) // step) % 2 == 0
                    a, b = parts[k], got[k]
                    out.append(jnp.concatenate([jnp.where(low, a, b), jnp.where(low, b, a)], ax))
                return out

            state["parts"] = do(put, state["parts"], state["got"])

        def result():
            return jnp.concatenate(state["parts"], axis=row_axis)

        return n, start, finish, result

    qkvs, attns, attn_got, stats = [], [], [], []
    for k in range(2):
        shape = (3, heads, HEAD_DIM, H)
        qkv, attn, stat = do(attend, flying[k][0].reshape(shape), flying[k][1].reshape(shape), bias, table[seqs[k]])
        qkvs.append(qkv)
        attns.append(attn.reshape(blk, H))
        attn_got.append(at.core(attns[k]))
        stats.append(stat)

    pairs = [do(join, attns[k], attn_got[k]) for k in range(2)]
    flying = scatter_rest(send_products(wo_cut, pairs))
    def residual(x, a0, b0, a1, b1):
        a, b = lanes(a0, a1), lanes(b0, b1)
        hidden = x.astype(f32) + (a.astype(f32) + b.astype(f32))
        local_mean = jnp.mean(hidden, axis=0, keepdims=True)
        dev = hidden - local_mean
        return hidden, join(local_mean, jnp.sum(dev * dev, axis=0, keepdims=True))

    hidden, moments = do(residual, x_own, *flying[0], *flying[1])
    count = blk
    for axis, step in at.steps(False) + [("core", 1)]:
        other = at.core(moments) if axis == "core" else at.along(moments, axis, step)

        def merge(a, b):
            gap = a[0:1] - b[0:1]
            return join(0.5 * (a[0:1] + b[0:1]), a[1:2] + b[1:2] + gap * gap * (count / 2.0))

        moments = do(merge, moments, other)
        count *= 2

    def second_norm(hidden, moments, cols):
        inv2 = lax.rsqrt(moments[1:2] / width + eps_norm)
        z2 = (hidden - moments[0:1]) * inv2
        return (z2 * cols[:, 2:3] + cols[:, 3:4]).astype(bf16), z2, inv2

    xn2_own, z2, inv2 = do(second_norm, hidden, moments, own_cols)
    xn2 = do(join, xn2_own, at.core(xn2_own))

    flying = send_products([wg_cut, wu_cut], [xn2, xn2])

    wd_own = do(cast, w_down)
    wg = do(side_by_side, *wg_parts)
    wu = do(side_by_side, *wu_parts)

    def gain_products(wg, wu, cols):
        g, b = cols[:, 2], cols[:, 3]
        terms = []
        for v in (g, b):
            t = lax.reduce_precision(v, 8, 7)
            terms += [t, v - t]
        terms = jnp.stack(terms).astype(bf16)
        out = []
        for w in (wg, wu):
            p = dot(w, terms, LAST)
            out.append(jnp.stack([p[:, 0] + p[:, 1], p[:, 2] + p[:, 3]]).reshape(2, Y, S, ffb))
        return jnp.concatenate(out, axis=0)

    gains = do(gain_products, wg, wu, pair_cols)
    for axis, step in at.steps(False):
        ax = {"y": 1, "s": 2}[axis]
        bit = (at.index(axis) // step) % 2
        send = lax.dynamic_slice_in_dim(gains, (1 - bit) * step, step, ax)
        kept = lax.dynamic_slice_in_dim(gains, bit * step, step, ax)
        gains = do(lambda a, b: a + b, kept, at.along(send, axis, step))
    gains = do(lambda g: g.reshape(4, ffb, 1), gains)
    grad_act = do(lambda w, c: dot(w, c, LAST), wd_own, cot_all)
    cot_cols = do(lambda c: lax.dynamic_slice_in_dim(c, my_block * blk, blk, 1).T, cot_all)
    wo_own = do(cast, w_out)
    wq = do(side_by_side, *wq_parts)
    flying = scatter_rest(flying)

    def gated(ga, gb, ua, ub, grad_act, gains):
        gate = ga.astype(f32) + gb.astype(f32)
        up = ua.astype(f32) + ub.astype(f32)
        sig = jax.nn.sigmoid(gate)
        silu = gate * sig
        ggate = (grad_act * up * sig * (1.0 + gate * (1.0 - sig))).astype(bf16)
        gup = (grad_act * silu).astype(bf16)
        return ggate, gup, (silu * up).astype(bf16), gate, up

    ggate, gup, act, gate, up = do(gated, *flying[0], *flying[1], grad_act, gains)

    def parts_of(count, want):
        return max(n for n in range(1, want + 1) if count % (16 * n) == 0)

    def even(count, want):
        n = parts_of(count, want)
        return [(k * (count // n), count // n) for k in range(n)]

    out_rows = even(blk, 2)
    qkv_rows = [(0, blk // 2), (blk // 2, blk // 4), (3 * blk // 4, blk // 4)]

    def push_pairs(name, g, rows):
        for k, (at_row, count) in enumerate(rows):
            reps.push((name, "theirs", k), g[blk + at_row : blk + at_row + count])
            reps.push((name, "mine", k), g[at_row : at_row + count])

    results = {"down": None, "out": None, "up": None, "qkv": None}
    states = {
        "down": (w_down, m_down, v_down),
        "out": (w_out, m_out, v_out),
        "up": (w_up, m_up, v_up),
        "qkv": (w_qkv, m_qkv, v_qkv),
    }
    rates = {"down": 0.02, "out": 0.2, "up": 0.03, "qkv": 0.03}

    def adam(name, grads, row_first, lead, unit, rb):
        results[name] = do(
            lambda s, g, prev: adam_part(s, g, core, rates[name], prev, row_first, lead, unit, rb),
            states[name],
            grads,
            results[name],
        )

    jobs = []
    for k, (at_row, count) in enumerate(out_rows):
        jobs.append(("out", [("out", k)], at_row, count, 1024))
    for k, (at_row, count) in enumerate(qkv_rows):
        jobs.append(("qkv", [("qkv", "mine", k), ("qkv", "theirs", k)], at_row, count, S * blk))
    received = {}

    def update(limit):
        for name in list(reps.done):
            if name[1] == "theirs" and name not in received:
                received[name] = at.core(reps.done[name])
        while jobs and limit and all(k in reps.done for k in jobs[0][1]):
            name, needs, at_row, count, unit = jobs.pop(0)
            adam(name, [received[k] if k[1] == "theirs" else reps.done[k] for k in needs], at_row, 0, unit, count)
            limit -= 1

    def ticks(n):
        for _ in range(n):
            reps.tick()

    def rep_scatter(g):
        return lax.psum_scatter(g, "rep", scatter_dimension=0, tiled=True)

    def rep_gather(g):
        return lax.all_gather(do(lambda g: g, g), "rep", axis=0, tiled=True)

    def quarter_heads(x):
        return [x[:, h][None, None] for h in halves]

    n, start, finish, gate_all = gather_steps(quarter_heads(ggate), 3)
    start(0)
    g_down = do(lambda a, c: dot(a, c, PLAIN).astype(bf16), act, cot_all)
    g_down = rep_scatter(g_down)

    def norm_sums2(ggate, gup, gate, up, gains):
        a, b = ggate.astype(f32), gup.astype(f32)
        e = jnp.sum(a * gains[0] + b * gains[2], axis=0, keepdims=True)
        ez = jnp.sum(a * (gate - gains[1]) + b * (up - gains[3]), axis=0, keepdims=True)
        return join(e, ez)

    sums = do(norm_sums2, ggate, gup, gate, up, gains)
    steps2 = at.steps(False) + [("core", 1)]

    def sum_step(sums, axis, step):
        other = at.core(sums) if axis == "core" else at.along(sums, axis, step)
        return do(lambda a, b: a + b, sums, other)

    finish()
    start(1)
    for axis, step in steps2:
        sums = sum_step(sums, axis, step)
    for i in range(2, n):
        finish()
        start(i)
    n, start_up, finish_up, up_all = gather_steps(quarter_heads(gup), 3)
    finish()
    start_up(0)
    ggate_all = do(lambda x: x.reshape(Y * S * ffb, T), gate_all())
    finish_up()
    for i in range(1, n):
        start_up(i)
        if i == 1:
            g_gate = do(lambda x, g: dot(x, g, LAST).astype(bf16), xn2, ggate_all)
            g_down = rep_gather(g_down)
            g_gate = rep_scatter(do(lambda g: g, g_gate))
            part_gate = do(lambda w, g: dot(w, g, FIRST), wg, ggate_all)
            out_part = do(lambda w, a: dot(w, a, FIRST).astype(bf16), wd_own, act).reshape(Y, 2, S * blk, T)
            out_theirs = at.core(pick(out_part, 1, 1 - at.c))
        finish_up()
    gup_all = do(lambda x: x.reshape(Y * S * ffb, T), up_all())
    part = do(lambda w, g, p: dot(w, g, FIRST) + p, wu, gup_all, part_gate)
    part_theirs = at.core(part[blk:])

    def branch(a, b, cot, z, scale, gain, sums):
        gxn2 = a + b
        e = gxn2 * gain
        grad_hidden = cot.astype(f32) + scale * (e - sums[0:1] / width - z * (sums[1:2] / width))
        return grad_hidden.astype(bf16), grad_hidden, gxn2

    grad_branch, grad_hidden, gxn2 = do(
        branch, part[:blk], part_theirs, cot_cols, z2, inv2, own_cols[:, 2:3], sums
    )
    n, start, finish, branch_all = gather_steps(quarter_heads(grad_branch), 3)
    start(0)
    g_up = do(lambda x, g: dot(x, g, LAST).astype(bf16), xn2, gup_all)
    finish()
    for i in range(1, n):
        start(i)
        finish()
    gbr_c = do(lambda x: x, branch_all())
    gbr_o = at.core(gbr_c)
    gbr = do(lambda a, b: in_order(a, b, 1).reshape(width, T), gbr_c, gbr_o)
    grad_attn = do(lambda w, g: dot(w, g, PLAIN).astype(bf16), wo_own, gbr)

    gqkvs = []
    for k in range(2):
        dout = grad_attn[:, halves[k]].reshape(heads, HEAD_DIM, H)
        gqkvs.append(do(attend_back, qkvs[k], dout, stats[k], table[seqs[k]]).reshape(3, blk, H))
    n, start, finish, gqkv_done = gather_steps([g.reshape(1, 1, 3 * blk, H) for g in gqkvs], 3)
    start(0)
    attn = lanes(*attns)
    g_out = do(lambda a, g: dot(a, g, LAST).astype(bf16), attn, gbr)
    for k, (at_row, count) in enumerate(out_rows):
        reps.push(("out", k), g_out[at_row : at_row + count])
    adam("down", [g_down], 0, 0, 1024, ffb // 4 if ffb % 64 == 0 else ffb)
    finish()
    for i in range(1, n):
        start(i)
        if i == 1:
            g_gate = rep_gather(g_gate)
            g_up = rep_scatter(do(lambda g: g, g_up))
            reps.tick()
        finish()

    def qkv_columns(x):
        return x.reshape(Y, S, 3, blk, T).transpose(2, 0, 1, 3, 4).reshape(3 * Y * S * blk, T)

    gqkv = do(qkv_columns, gqkv_done())
    g_qkv = do(lambda x, g: dot(x, g, LAST).astype(bf16), xn1, gqkv)
    push_pairs("qkv", g_qkv, qkv_rows)
    ticks(1)
    part = do(lambda w, g: dot(w, g, FIRST), wq, gqkv)
    part_theirs = at.core(part[blk:])
    ticks(1)

    def split_rows(g):
        return do(lambda g: (g[:blk], g[blk:]), g)

    def adam_ff(g, lead):
        mine, theirs = split_rows(g)
        adam("up", [mine, at.core(theirs)], 0, lead, S * ffb, min(blk, 128))

    adam_ff(g_gate, 0)
    ticks(1)

    def first_back(a, b, x, mean, inv, gain, gxn2, z2, gqkv0, gqkv1):
        gxn1 = a + b
        z1 = (x.astype(f32) - mean) * inv
        e = gxn1 * gain
        sums = join(jnp.sum(e, axis=0, keepdims=True), jnp.sum(e * z1, axis=0, keepdims=True))
        small = jnp.concatenate(
            [
                jnp.sum(gxn1 * z1, axis=1)[None],
                jnp.sum(gxn1, axis=1)[None],
                jnp.sum(gxn2 * z2, axis=1)[None],
                jnp.sum(gxn2, axis=1)[None],
                jnp.sum(gqkv0.astype(f32), axis=2) + jnp.sum(gqkv1.astype(f32), axis=2),
            ],
            axis=0,
        )
        return sums, small, gxn1, z1

    sums, small, gxn1, z1 = do(
        first_back, part[:blk], part_theirs, x_own, mean1, inv1, own_cols[:, 0:1], gxn2, z2, *gqkvs
    )
    for axis, step in steps2:
        sums = sum_step(sums, axis, step)
    ticks(1)
    input_grad = do(
        lambda h, grad, z, scale, gain, sums: h
        + scale * (grad * gain - sums[0:1] / width - z * (sums[1:2] / width)),
        grad_hidden,
        gxn1,
        z1,
        inv1,
        own_cols[:, 0:1],
        sums,
    )

    def to_rows(cols):
        split = do(lambda c: c.reshape(blk, S, at.ctx_size, rows).transpose(2, 1, 0, 3).reshape(nb, blk, rows), cols)
        got = lax.all_to_all(split, plane, split_axis=0, concat_axis=0, tiled=True)
        return do(lambda g: g.reshape(width, rows).T, got)

    update(1)
    input_rows = to_rows(input_grad)
    g_up = rep_gather(g_up)
    reps.tick()
    update(1)

    kept, got = pick(out_part, 1, at.c).reshape(-1, T), out_theirs.reshape(-1, T)
    for k, (axis, step) in enumerate(at.steps(True)):
        bit = (at.index(axis) // step) % 2
        send, kept = do(lambda a, b: add_split(a, b, bit.reshape(1)), kept, got)
        got = at.along(send, axis, step)
        if k < 2:
            reps.tick()
            update(1)
    out_cols = do(
        lambda h, a, b: (h + (a.astype(f32) + b.astype(f32))).astype(bf16), hidden, kept, got
    )
    reps.tick()
    update(1)
    block_output = to_rows(out_cols)
    reps.tick()
    update(1)

    n_rep = lax.axis_size("rep")
    step = 1
    while step < n_rep:
        other = lax.ppermute(small, "rep", [(i, i ^ step) for i in range(n_rep)])
        small = do(lambda a, b: a + b, small, other)
        step *= 2
    sent = do(lambda s: jnp.broadcast_to(s.reshape(1, 7, blk), (nb, 7, blk)), small)
    got = lax.all_to_all(sent, plane, split_axis=0, concat_axis=0, tiled=True)
    norm_grad = got.transpose(1, 0, 2).reshape(7, width)
    mn, vn, wn = do(lambda *a: adam_update(*a, 0.3, 0.0), norm_params, m_norm, v_norm, norm_grad)

    ticks(2)
    adam_ff(g_up, Y)
    while reps.busy():
        reps.tick()
        update(1)
    update(len(jobs))
    return (
        (block_output.reshape(tokens.shape), input_rows.reshape(tokens.shape))
        + tuple(results["qkv"])
        + tuple(results["out"])
        + tuple(results["up"])
        + tuple(results["down"])
        + (mn, vn, wn)
    )


def solution(mesh):
    tok = P("rep", "ctx", "shard", None)
    row = P(("ctx", "shard"), None)
    placed = (tok, tok, P("rep", "shard", None)) + (row,) * 4 + (P(),) + (row,) * 8 + (P(), P())
    return jax.shard_map(
        body,
        mesh=mesh,
        in_specs=placed,
        out_specs=(tok, tok) + (row,) * 12 + (P(),) * 3,
        check_vma=False,
    )
```

```python
import functools

import jax
import jax.numpy as jnp
from jax import lax
from jax.experimental import pallas as pl
from jax.experimental.pallas import tpu as pltpu
from jax.sharding import PartitionSpec as P

HEADS = 32
HEAD_DIM = 64
FF = 5632
ROTARY = 16
STEP = 10

eps_norm = 1e-05
masked_score = -1e30
beta_one = 0.9
beta_two = 0.999
adam_eps = 1e-08
weight_decay = 0.1
score_scale = HEAD_DIM ** (-0.5)
FIRST = (((0,), (0,)), ((), ()))
LAST = (((1,), (1,)), ((), ()))
PLAIN = (((1,), (0,)), ((), ()))
bf16 = jnp.bfloat16
f32 = jnp.float32


def dot(a, b, dims):
    return lax.dot_general(a, b, dims, preferred_element_type=f32)


def adam_update(weight, moment_one, moment_two, grad, step_rate, decay_rate):
    first_new = beta_one * moment_one + (1.0 - beta_one) * grad
    second_new = beta_two * moment_two + (1.0 - beta_two) * grad * grad
    first_hat = first_new / (1.0 - beta_one**STEP)
    second_hat = second_new / (1.0 - beta_two**STEP)
    weight_new = weight - step_rate * (
        first_hat / (jnp.sqrt(second_hat) + adam_eps) + decay_rate * weight
    )
    return (first_new, second_new, weight_new)


class Plane:
    def __init__(self):
        self.s_size = lax.axis_size("shard")
        self.ctx_size = lax.axis_size("ctx")
        self.y_size = self.ctx_size // 2
        self.ctx = lax.axis_index("ctx")
        self.s = lax.axis_index("shard")
        self.y = self.ctx // 2
        self.c = self.ctx % 2
        self.blocks = self.ctx_size * self.s_size

    def core(self, x):
        return lax.ppermute(x, "ctx", [(i, i ^ 1) for i in range(self.ctx_size)])

    def along(self, x, axis, step):
        if axis == "y":
            return lax.ppermute(x, "ctx", [(i, i ^ (2 * step)) for i in range(self.ctx_size)])
        return lax.ppermute(x, "shard", [(i, i ^ step) for i in range(self.s_size)])

    def index(self, axis):
        return self.y if axis == "y" else self.s

    def steps(self, flip):
        ys = []
        k = self.y_size // 2
        while k:
            ys.append(("y", k))
            k //= 2
        ss = []
        k = self.s_size // 2
        while k:
            ss.append(("s", k))
            k //= 2
        return ys + ss if flip else ss + ys

    def chip_exchange(self, x, take):
        out = [(self.y, self.s, take(self.y, self.s))]
        for ry in range(self.y_size):
            for rs in range(self.s_size):
                if ry or rs:
                    y, s = self.y ^ ry, self.s ^ rs
                    mask = 2 * ry * self.s_size + rs
                    perm = [(i, i ^ mask) for i in range(self.blocks)]
                    out.append((y, s, lax.ppermute(take(y, s), ("ctx", "shard"), perm)))
        return out

    def sum_all(self, x):
        for axis, step in self.steps(False):
            x = x + self.along(x, axis, step)
        return x + self.core(x)

    def scatter_sum(self, p, flip):
        axes = {"y": 1, "s": 2}
        steps = self.steps(flip)
        kept = got = None
        for n, (axis, step) in enumerate(steps):
            ax = axes[axis]
            bit = (self.index(axis) // step) % 2
            kept = lax.dynamic_slice_in_dim(p, bit * step, step, ax)
            send = lax.dynamic_slice_in_dim(p, (1 - bit) * step, step, ax)
            got = self.along(send, axis, step)
            if n + 1 < len(steps):
                p = (kept.astype(f32) + got.astype(f32)).astype(bf16)
        return kept[:, 0, 0], got[:, 0, 0]

    def gather(self, p, flip):
        axes = {"y": 1, "s": 2}
        p = p[:, None, None]
        for axis, step in reversed(self.steps(flip)):
            ax = axes[axis]
            bit = (self.index(axis) // step) % 2
            got = self.along(p, axis, step)
            first = bit == 0
            p = jnp.concatenate([jnp.where(first, p, got), jnp.where(first, got, p)], ax)
        return p


class Order:
    def __init__(self):
        self.last = None

    def __call__(self, stage, *args):
        if self.last is not None:
            args, self.last = lax.optimization_barrier((args, self.last))
        out = stage(*args)
        self.last = jax.tree.leaves(out)[0]
        return out


SMALL = pl.CostEstimate(flops=1024, bytes_accessed=1024, transcendentals=0)


class RepSum:
    def __init__(self, order):
        self.order = order
        z = lax.axis_index("rep")
        self.end = (z == 0) | (z == lax.axis_size("rep") - 1)
        self.queue = []
        self.flight = []
        self.depth = 1
        self.done = {}

    def push(self, name, g):
        self.queue.append((name, g))

    def busy(self):
        return bool(self.queue or self.flight)

    def tick(self):
        old = {}
        if len(self.flight) >= self.depth or (self.flight and not self.queue):
            old = self.flight.pop(0)
        new = self.queue.pop(0) if self.queue else None
        values = {}
        if "in" in old:
            values["g"], values["g_got"] = old["in"][1], old["in_got"]
        if "mid" in old:
            values["s"], values["s_got"] = old["mid"][1], old["mid_got"]
        if new:
            values["new"] = new[1]
        both = new and "mid" in old and new[1].shape == old["mid"][1].shape
        if "out" in old:
            values["out_got"] = old["out_got"]

        def stage(v):
            def add(a, b):
                return lax.reduce_precision(a.astype(f32) + b.astype(f32), 8, 7).astype(bf16)

            out = {}
            if "g" in v:
                out["a_sum"] = add(v["g"], v["g_got"])
            if "s" in v:
                total = add(v["s"], v["s_got"])
                out["total"] = jnp.where(self.end, v["new"], total) if both else total
            if "new" in v and not both:
                out["new"] = v["new"]
            if "out_got" in v:
                out["z_got"] = v["out_got"]
            return out

        if not values:
            return
        out = self.order(stage, values)
        if "out" in old:
            self.done[old["out"][0]] = jnp.where(self.end, out["z_got"], old["out"][1])
        slot = {}
        if both:
            got = lax.ppermute(out["total"], "rep", [(0, 1), (1, 0), (2, 3), (3, 2)])
            slot = {"in": new, "in_got": got, "out": (old["mid"][0], out["total"]), "out_got": got}
        else:
            if new:
                slot["in"] = new
                slot["in_got"] = lax.ppermute(out["new"], "rep", [(0, 1), (3, 2)])
            if "mid" in old:
                slot["out"] = (old["mid"][0], out["total"])
                slot["out_got"] = lax.ppermute(out["total"], "rep", [(1, 0), (2, 3)])
        if "in" in old:
            slot["mid"] = (old["in"][0], out["a_sum"])
            slot["mid_got"] = lax.ppermute(out["a_sum"], "rep", [(1, 2), (2, 1)])
        if slot:
            self.flight.append(slot)


def cast_kernel(w_ref, out_ref):
    out_ref[...] = w_ref[...].astype(bf16)


def cast(w):
    rows, width = w.shape
    unit = max(n for n in (128, 256, 512, 1024, 1408, 2048, 2816) if width % n == 0)
    spec = pl.BlockSpec((rows, unit), lambda i: (0, i))
    return pl.pallas_call(
        cast_kernel,
        grid=(width // unit,),
        in_specs=[spec],
        out_specs=spec,
        out_shape=jax.ShapeDtypeStruct(w.shape, bf16),
        compiler_params=pltpu.CompilerParams(vmem_limit_bytes=48 * 1024 * 1024),
        cost_estimate=SMALL,
    )(w)


def split_kernel(core_ref, w_ref, mine_ref, theirs_ref):
    unit = mine_ref.shape[0]
    first = core_ref[0] == 0
    a, b = w_ref[:, :unit], w_ref[:, unit:]
    mine_ref[...] = jnp.where(first, a, b).T.astype(bf16)
    theirs_ref[...] = jnp.where(first, b, a).T.astype(bf16)


def split_columns(w, core, lead, unit, count):
    rows = w.shape[0]
    half = pl.BlockSpec((unit, rows), lambda j, core: (j, 0))
    out = jax.ShapeDtypeStruct((count * unit, rows), bf16)
    return pl.pallas_call(
        split_kernel,
        grid_spec=pltpu.PrefetchScalarGridSpec(
            num_scalar_prefetch=1,
            grid=(count,),
            in_specs=[pl.BlockSpec((rows, 2 * unit), lambda j, core: (0, lead + j))],
            out_specs=[half, half],
        ),
        out_shape=[out, out],
        compiler_params=pltpu.CompilerParams(vmem_limit_bytes=32 * 1024 * 1024),
        cost_estimate=SMALL,
    )(core, w)


def arrange_kernel(at_ref, a_ref, b_ref, c_ref, d_ref, send_ref, keep_ref):
    send_ref[...] = jnp.concatenate([a_ref[...], b_ref[...]], axis=1)
    keep_ref[...] = jnp.concatenate([c_ref[...], d_ref[...]], axis=1)


def arrange(mine, got, place, pre, y_size, s_size, unit, flip):
    r = mine.shape[1]
    half = pre * y_size * s_size // 2

    def block(i, place, keep):
        p = i % pre
        i = i // pre
        if flip:
            s, y = i % s_size, i // s_size
            bit = place[0] // (y_size // 2)
            bit = bit if keep else 1 - bit
            y = y + bit * (y_size // 2)
        else:
            y, s = i % y_size, i // y_size
            bit = place[1] // (s_size // 2)
            bit = bit if keep else 1 - bit
            s = s + bit * (s_size // 2)
        return ((p * y_size + y) * s_size + s, 0)

    def spec(keep):
        return pl.BlockSpec((unit, r), lambda i, place: block(i, place, keep))

    out = jax.ShapeDtypeStruct((half * unit, 2 * r), bf16)
    out_spec = pl.BlockSpec((unit, 2 * r), lambda i, place: (i, 0))
    return pl.pallas_call(
        arrange_kernel,
        grid_spec=pltpu.PrefetchScalarGridSpec(
            num_scalar_prefetch=1,
            grid=(half,),
            in_specs=[spec(False), spec(False), spec(True), spec(True)],
            out_specs=[out_spec, out_spec],
        ),
        out_shape=[out, out],
        compiler_params=pltpu.CompilerParams(vmem_limit_bytes=32 * 1024 * 1024),
        cost_estimate=SMALL,
    )(place, mine, got, mine, got)


def lanes_kernel(a_ref, b_ref, out_ref):
    out_ref[...] = jnp.concatenate([a_ref[...], b_ref[...]], axis=1)


def side_by_side(a, b):
    rows, width = a.shape
    n = max(n for n in (1, 2, 4, 8) if rows % (16 * n) == 0)
    spec = pl.BlockSpec((rows // n, width), lambda i: (i, 0))
    return pl.pallas_call(
        lanes_kernel,
        grid=(n,),
        in_specs=[spec, spec],
        out_specs=pl.BlockSpec((rows // n, 2 * width), lambda i: (i, 0)),
        out_shape=jax.ShapeDtypeStruct((rows, 2 * width), bf16),
        compiler_params=pltpu.CompilerParams(vmem_limit_bytes=48 * 1024 * 1024),
        cost_estimate=SMALL,
    )(a, b)


def add_split_kernel(bit_ref, a_ref, b_ref, c_ref, d_ref, send_ref, keep_ref):
    send_ref[...] = (a_ref[...].astype(f32) + b_ref[...].astype(f32)).astype(bf16)
    keep_ref[...] = (c_ref[...].astype(f32) + d_ref[...].astype(f32)).astype(bf16)


def add_split(kept, got, bit):
    rows, t = kept.shape
    half = rows // 2
    n = max(n for n in (1, 2, 3, 4) if half % (16 * n) == 0)
    rb = half // n
    away = pl.BlockSpec((rb, t), lambda i, bit: ((1 - bit[0]) * n + i, 0))
    here = pl.BlockSpec((rb, t), lambda i, bit: (bit[0] * n + i, 0))
    out = jax.ShapeDtypeStruct((half, t), bf16)
    out_spec = pl.BlockSpec((rb, t), lambda i, bit: (i, 0))
    return pl.pallas_call(
        add_split_kernel,
        grid_spec=pltpu.PrefetchScalarGridSpec(
            num_scalar_prefetch=1,
            grid=(n,),
            in_specs=[away, away, here, here],
            out_specs=[out_spec, out_spec],
        ),
        out_shape=[out, out],
        compiler_params=pltpu.CompilerParams(vmem_limit_bytes=48 * 1024 * 1024),
        cost_estimate=SMALL,
    )(bit, kept, got, kept, got)


def adam_kernel(rate, two, core_ref, w_ref, m_ref, v_ref, *refs):
    grad = refs[0][...].astype(f32)
    if two:
        other = refs[1][...].astype(f32)
        mine = core_ref[0] == 0
        grad = jnp.concatenate([jnp.where(mine, grad, other), jnp.where(mine, other, grad)], axis=1)
    new_m_ref, new_v_ref, new_w_ref = refs[-3:]
    new_m, new_v, new_w = adam_update(w_ref[...], m_ref[...], v_ref[...], grad, rate, weight_decay)
    new_m_ref[...] = new_m
    new_v_ref[...] = new_v
    new_w_ref[...] = new_w


def adam_part(state, grads, core, rate, prev, row_first, lead, unit, rb):
    w, m, v = state
    two = len(grads) == 2
    rows, width = grads[0].shape
    whole = pl.BlockSpec((rb, unit * len(grads)), lambda i, g, core: (row_first // rb + i, lead + g))
    half = pl.BlockSpec((rb, unit), lambda i, g, core: (i, g))
    out = jax.ShapeDtypeStruct(w.shape, f32)
    extra, aliases = [], {}
    if prev is not None:
        extra = list(prev)
        aliases = {4 + len(grads) + i: i for i in range(3)}
    return pl.pallas_call(
        functools.partial(adam_kernel, rate, two),
        grid_spec=pltpu.PrefetchScalarGridSpec(
            num_scalar_prefetch=1,
            grid=(rows // rb, width // unit),
            in_specs=[whole] * 3 + [half] * len(grads) + [pl.BlockSpec(memory_space=pl.ANY)] * len(extra),
            out_specs=[whole] * 3,
        ),
        out_shape=[out] * 3,
        input_output_aliases=aliases,
        compiler_params=pltpu.CompilerParams(vmem_limit_bytes=48 * 1024 * 1024),
        cost_estimate=SMALL,
    )(core, w, m, v, *grads, *extra)


def attend_kernel(kept_ref, got_ref, bias_ref, table_ref, qkv_ref, out_ref, stat_ref):
    half = ROTARY // 2
    cos, sin, pos = table_ref[0, :half], table_ref[0, half:ROTARY], table_ref[0, ROTARY:]
    parts = []
    for i in range(3):
        v = kept_ref[i, 0].astype(f32) + got_ref[i, 0].astype(f32) + bias_ref[i, 0]
        if i < 2:
            a, b = v[:half], v[half:ROTARY]
            v = jnp.concatenate([a * cos - b * sin, b * cos + a * sin, v[ROTARY:]], axis=0)
        v = v.astype(bf16)
        qkv_ref[i, 0] = v
        parts.append(v)
    q, k, v = parts
    scores = dot(k, q, FIRST) * score_scale
    scores = jnp.where(pos.T[:, :1] <= pos[:1], scores, masked_score)
    peak = jnp.max(scores, axis=0, keepdims=True)
    e = jnp.exp(scores - peak)
    total = jnp.sum(e, axis=0, keepdims=True)
    p = (e / total).astype(bf16)
    out_ref[0] = dot(v, p, PLAIN).astype(bf16)
    stat_ref[0, 0] = jnp.concatenate([peak, total], axis=0)


def attend(kept, got, bias, table):
    _, heads, hd, t = kept.shape
    seqs, _, seq = table.shape
    big = pl.BlockSpec((3, 1, hd, seq), lambda s, h: (0, h, 0, s))
    table_spec = pl.BlockSpec((1, table.shape[1], seq), lambda s, h: (s, 0, 0))
    stat = pl.BlockSpec((1, 1, 2, seq), lambda s, h: (s, h, 0, 0))
    return pl.pallas_call(
        attend_kernel,
        grid=(seqs, heads),
        in_specs=[
            big,
            big,
            pl.BlockSpec((3, 1, hd, 1), lambda s, h: (0, h, 0, 0)),
            table_spec,
        ],
        out_specs=[big, pl.BlockSpec((1, hd, seq), lambda s, h: (h, 0, s)), stat],
        out_shape=[
            jax.ShapeDtypeStruct((3, heads, hd, t), bf16),
            jax.ShapeDtypeStruct((heads, hd, t), bf16),
            jax.ShapeDtypeStruct((seqs, heads, 2, seq), f32),
        ],
        compiler_params=pltpu.CompilerParams(vmem_limit_bytes=32 * 1024 * 1024),
        cost_estimate=SMALL,
    )(kept, got, bias, table)


def attend_back_kernel(qkv_ref, dout_ref, stat_ref, table_ref, out_ref):
    half = ROTARY // 2
    cos, sin, pos = table_ref[0, :half], table_ref[0, half:ROTARY], table_ref[0, ROTARY:]
    q, k, v = qkv_ref[0, 0], qkv_ref[1, 0], qkv_ref[2, 0]
    dout = dout_ref[0]
    scores = dot(k, q, FIRST) * score_scale
    scores = jnp.where(pos.T[:, :1] <= pos[:1], scores, masked_score)
    p = jnp.exp(scores - stat_ref[0, 0, :1]) / stat_ref[0, 0, 1:]
    dp = dot(v, dout, FIRST)
    inner = jnp.sum(p * dp, axis=0, keepdims=True)
    ds = (p * (dp - inner)).astype(bf16)

    def back(x):
        a, b = x[:half], x[half:ROTARY]
        return jnp.concatenate([a * cos + b * sin, b * cos - a * sin, x[ROTARY:]], axis=0)

    out_ref[0, 0] = back(dot(k, ds, PLAIN) * score_scale).astype(bf16)
    out_ref[1, 0] = back(dot(q, ds, LAST) * score_scale).astype(bf16)
    out_ref[2, 0] = dot(dout, p.astype(bf16), LAST).astype(bf16)


def attend_back(qkv, dout, stats, table):
    _, heads, hd, t = qkv.shape
    seqs, _, seq = table.shape
    big = pl.BlockSpec((3, 1, hd, seq), lambda s, h: (0, h, 0, s))
    table_spec = pl.BlockSpec((1, table.shape[1], seq), lambda s, h: (s, 0, 0))
    stat = pl.BlockSpec((1, 1, 2, seq), lambda s, h: (s, h, 0, 0))
    return pl.pallas_call(
        attend_back_kernel,
        grid=(seqs, heads),
        in_specs=[
            big,
            pl.BlockSpec((1, hd, seq), lambda s, h: (h, 0, s)),
            stat,
            table_spec,
        ],
        out_specs=big,
        out_shape=jax.ShapeDtypeStruct((3, heads, hd, t), bf16),
        compiler_params=pltpu.CompilerParams(vmem_limit_bytes=32 * 1024 * 1024),
        cost_estimate=SMALL,
    )(qkv, dout, stats, table)


def body(
    tokens,
    cotangent,
    span_order,
    w_qkv,
    w_out,
    w_up,
    w_down,
    norm_params,
    m_qkv,
    v_qkv,
    m_out,
    v_out,
    m_up,
    v_up,
    m_down,
    v_down,
    m_norm,
    v_norm,
):
    at = Plane()
    do = Order()
    reps = RepSum(do)
    width = tokens.shape[3]
    rows = tokens.shape[1]
    S, Y, nb = at.s_size, at.y_size, at.blocks
    plane = ("ctx", "shard")
    blk = width // nb
    ffb = FF // nb
    heads = blk // HEAD_DIM
    seq = rows * at.ctx_size
    T = S * seq
    H = T // 2
    first = at.c == 0
    core = at.c.reshape(1)
    my_block = at.ctx * S + at.s
    halves = (slice(0, H), slice(H, T))
    seqs = (slice(0, S // 2), slice(S // 2, S))

    def pick(x, axis, which):
        return lax.dynamic_index_in_dim(x, which, axis, keepdims=False)

    def in_order(mine, theirs, axis):
        return jnp.stack([jnp.where(first, mine, theirs), jnp.where(first, theirs, mine)], axis=axis)

    def join(a, b):
        return jnp.concatenate([a, b], axis=0)

    def lanes(a, b):
        return jnp.concatenate([a, b], axis=1)

    x_rows = tokens.reshape(rows, width)
    order = span_order.reshape(-1).astype(f32)
    span = rows // 2

    def pack(x, order):
        xf = x.astype(f32)
        mean = jnp.mean(xf, axis=1)
        centred = xf - mean[:, None]
        inv = lax.rsqrt(jnp.mean(centred * centred, axis=1) + eps_norm)
        mine = lax.dynamic_slice_in_dim(order, 2 * at.ctx, 2)
        place = jnp.repeat(mine, span)
        terms = []
        for v in (mean, inv):
            for _ in range(3):
                t = lax.reduce_precision(v, 8, 7)
                terms.append(t)
                v = v - t
        extra = jnp.stack(terms + [place] + [jnp.zeros_like(place)] * 9).astype(bf16)
        blocks = x.T.reshape(nb, blk, rows)
        return jnp.concatenate([blocks, jnp.broadcast_to(extra[None], (nb, 16, rows))], axis=1)

    packed = do(pack, x_rows, order)
    cot_all = lax.all_gather(cotangent.reshape(rows, width), ("shard", "ctx"), axis=0, tiled=True)
    got = lax.all_to_all(packed, plane, split_axis=0, concat_axis=0, tiled=True)

    def chip_rows(w, lead, unit, count):
        mine, theirs = do(lambda w: split_columns(w, core, lead, unit, count), w)
        return mine, at.core(theirs)

    wq_parts = chip_rows(w_qkv, 0, S * blk, 3 * Y)
    norm_cols = norm_params.reshape(7, nb, blk).transpose(1, 2, 0)
    own_cols = pick(norm_cols, 0, my_block)
    other_cols = pick(norm_cols, 0, (at.ctx ^ 1) * S + at.s)
    pair_cols = join(own_cols, other_cols)
    bias = own_cols[:, 4:7].T.reshape(3, heads, HEAD_DIM, 1)
    spot = jnp.stack([at.y, at.s])

    def cut_weights(parts, pre, unit, flip):
        return do(lambda a, b: arrange(a, b, spot, pre, Y, S, unit, flip), *parts)

    wq_cut = [cut_weights(wq_parts, 3, blk, bool(k)) for k in range(2)]

    def columns(got):
        x = got.reshape(at.ctx_size, S, blk + 16, rows).transpose(2, 1, 0, 3).reshape(blk + 16, T)
        x_own, extra = x[:blk], x[blk:].astype(f32)
        mean = extra[0:1] + extra[1:2] + extra[2:3]
        inv = extra[3:4] + extra[4:5] + extra[5:6]
        return x_own, mean, inv, extra[6:7]

    x_own, mean1, inv1, place = do(columns, got)
    x_other = at.core(x_own)

    def first_norm(mine, theirs, mean, inv, cols):
        x = join(mine, theirs).astype(f32)
        return ((x - mean) * inv * cols[:, 0:1] + cols[:, 1:2]).astype(bf16)

    xn1 = do(first_norm, x_own, x_other, mean1, inv1, pair_cols)

    def send_products(cut, xs):
        got, kept = [], []
        for k in range(2):
            axis, step = at.steps(bool(k))[0]
            p = do(lambda w, x: dot(w, x, PLAIN).astype(bf16), cut[k][0], xs[k])
            got.append(at.along(p, axis, step))
        for k in range(2):
            kept.append(do(lambda w, x: dot(w, x, PLAIN).astype(bf16), cut[k][1], xs[k]))
        return list(zip(kept, got))

    def scatter_rest(pairs):
        for i in range(1, len(at.steps(False))):
            out = []
            for k in range(2):
                axis, step = at.steps(bool(k))[i]
                bit = (at.index(axis) // step) % 2
                send, kept = do(lambda a, b: add_split(a, b, bit.reshape(1)), *pairs[k])
                out.append((kept, at.along(send, axis, step)))
            pairs = out
        return pairs

    flying = send_products(wq_cut, [xn1[:, h] for h in halves])

    wo_parts = chip_rows(w_out, 0, S * blk, Y)
    wg_parts = chip_rows(w_up, 0, S * ffb, Y)
    wu_parts = chip_rows(w_up, Y, S * ffb, Y)
    wo_cut = [cut_weights(wo_parts, 1, blk, bool(k)) for k in range(2)]

    def positions(place):
        pos = place.reshape(S, seq) * span + (jnp.arange(seq) % span).astype(f32)[None, :]
        prow = pos.reshape(S, 1, seq)
        exponent = jnp.arange(ROTARY // 2, dtype=f32)
        inverse = 10000.0 ** (-2.0 * exponent / ROTARY)
        angles = prow * inverse[None, :, None]
        return jnp.concatenate([jnp.cos(angles), jnp.sin(angles), jnp.broadcast_to(prow, (S, 8, seq))], axis=1)

    table = do(positions, place)
    flying = scatter_rest(flying)
    wg_cut = cut_weights(wg_parts, 1, ffb, False)
    wu_cut = cut_weights(wu_parts, 1, ffb, True)

    def gather_steps(parts, row_axis):
        n = len(at.steps(False))
        state = {"parts": list(parts)}

        def start(i):
            state["got"] = []
            state["at"] = []
            for k in range(2):
                axis, step = list(reversed(at.steps(bool(k))))[i]
                state["at"].append((axis, step))
                state["got"].append(at.along(state["parts"][k], axis, step))

        def finish():
            def put(parts, got):
                out = []
                for k in range(2):
                    axis, step = state["at"][k]
                    ax = {"y": 0, "s": 1}[axis]
                    low = (at.index(axis) // step) % 2 == 0
                    a, b = parts[k], got[k]
                    out.append(jnp.concatenate([jnp.where(low, a, b), jnp.where(low, b, a)], ax))
                return out

            state["parts"] = do(put, state["parts"], state["got"])

        def result():
            return jnp.concatenate(state["parts"], axis=row_axis)

        return n, start, finish, result

    def gain_products(wg, wu, cols):
        terms = []
        for v in (cols[:, 2], cols[:, 3]):
            t = lax.reduce_precision(v, 8, 7)
            terms += [t, v - t]
        terms = jnp.stack(terms).astype(bf16)
        out = []
        for mine, theirs in (wg, wu):
            p = dot(terms[:, :blk], mine, LAST) + dot(terms[:, blk:], theirs, LAST)
            out.append(jnp.stack([p[0] + p[1], p[2] + p[3]]).reshape(2, Y, S, ffb))
        return jnp.concatenate(out, axis=0)

    gains = do(gain_products, wg_parts, wu_parts, pair_cols)
    gain_steps = list(at.steps(False))

    def gain_step(gains):
        axis, step = gain_steps.pop(0)
        ax = {"y": 1, "s": 2}[axis]
        bit = (at.index(axis) // step) % 2
        send = lax.dynamic_slice_in_dim(gains, (1 - bit) * step, step, ax)
        kept = lax.dynamic_slice_in_dim(gains, bit * step, step, ax)
        return kept, at.along(send, axis, step)

    gains = gain_step(gains)

    qkvs, attns, attn_got, stats = [], [], [], []
    for k in range(2):
        shape = (3, heads, HEAD_DIM, H)
        qkv, attn, stat = do(attend, flying[k][0].reshape(shape), flying[k][1].reshape(shape), bias, table[seqs[k]])
        qkvs.append(qkv)
        attns.append(attn.reshape(blk, H))
        attn_got.append(at.core(attns[k]))
        stats.append(stat)
        gains = do(lambda a, b: a + b, *gains)
        if gain_steps:
            gains = gain_step(gains)
        else:
            gains = (gains, jnp.zeros_like(gains))
    while gain_steps:
        gains = gain_step(do(lambda a, b: a + b, *gains))
    gains = do(lambda a, b: (a + b).reshape(4, ffb, 1), *gains)

    pairs = [do(join, attns[k], attn_got[k]) for k in range(2)]
    flying = scatter_rest(send_products(wo_cut, pairs))
    def residual(x, a0, b0, a1, b1):
        a, b = lanes(a0, a1), lanes(b0, b1)
        hidden = x.astype(f32) + (a.astype(f32) + b.astype(f32))
        local_mean = jnp.mean(hidden, axis=0, keepdims=True)
        dev = hidden - local_mean
        return hidden, join(local_mean, jnp.sum(dev * dev, axis=0, keepdims=True))

    hidden, moments = do(residual, x_own, *flying[0], *flying[1])
    count = blk
    for axis, step in at.steps(False) + [("core", 1)]:
        other = at.core(moments) if axis == "core" else at.along(moments, axis, step)

        def merge(a, b):
            gap = a[0:1] - b[0:1]
            return join(0.5 * (a[0:1] + b[0:1]), a[1:2] + b[1:2] + gap * gap * (count / 2.0))

        moments = do(merge, moments, other)
        count *= 2

    def second_norm(hidden, moments, cols):
        inv2 = lax.rsqrt(moments[1:2] / width + eps_norm)
        z2 = (hidden - moments[0:1]) * inv2
        return (z2 * cols[:, 2:3] + cols[:, 3:4]).astype(bf16), z2, inv2

    xn2_own, z2, inv2 = do(second_norm, hidden, moments, own_cols)
    xn2 = do(join, xn2_own, at.core(xn2_own))

    flying = send_products([wg_cut, wu_cut], [xn2, xn2])

    wd_own = do(cast, w_down)
    grad_act = do(lambda w, c: dot(w, c, LAST), wd_own, cot_all)
    cot_cols = do(lambda c: lax.dynamic_slice_in_dim(c, my_block * blk, blk, 1).T, cot_all)
    wo_own = do(cast, w_out)
    wg = do(side_by_side, *wg_parts)
    wu = do(side_by_side, *wu_parts)
    wq = do(side_by_side, *wq_parts)
    flying = scatter_rest(flying)

    def gated(ga, gb, ua, ub, grad_act, gains):
        gate = ga.astype(f32) + gb.astype(f32)
        up = ua.astype(f32) + ub.astype(f32)
        sig = jax.nn.sigmoid(gate)
        silu = gate * sig
        ggate = (grad_act * up * sig * (1.0 + gate * (1.0 - sig))).astype(bf16)
        gup = (grad_act * silu).astype(bf16)
        return ggate, gup, (silu * up).astype(bf16), gate, up

    ggate, gup, act, gate, up = do(gated, *flying[0], *flying[1], grad_act, gains)

    def parts_of(count, want):
        return max(n for n in range(1, want + 1) if count % (16 * n) == 0)

    def even(count, want):
        n = parts_of(count, want)
        return [(k * (count // n), count // n) for k in range(n)]

    down_rows, up_rows, out_rows = even(ffb, 2), [(0, blk)], [(0, blk)]
    qkv_rows = [(0, blk // 2), (blk // 2, blk // 4), (3 * blk // 4, blk // 4)]

    def push_pairs(name, g, rows):
        for k, (at_row, count) in enumerate(rows):
            reps.push((name, "theirs", k), g[blk + at_row : blk + at_row + count])
            reps.push((name, "mine", k), g[at_row : at_row + count])

    results = {"down": None, "out": None, "up": None, "qkv": None}
    states = {
        "down": (w_down, m_down, v_down),
        "out": (w_out, m_out, v_out),
        "up": (w_up, m_up, v_up),
        "qkv": (w_qkv, m_qkv, v_qkv),
    }
    rates = {"down": 0.02, "out": 0.2, "up": 0.03, "qkv": 0.03}

    def adam(name, grads, row_first, lead, unit, rb):
        results[name] = do(
            lambda s, g, prev: adam_part(s, g, core, rates[name], prev, row_first, lead, unit, rb),
            states[name],
            grads,
            results[name],
        )

    jobs = []
    for k, (at_row, count) in enumerate(down_rows):
        jobs.append(("down", [("down", k)], at_row, 0, count, 1024))
    for name, lead in (("gate", 0), ("up", Y)):
        for k, (at_row, count) in enumerate(up_rows):
            jobs.append(("up", [(name, "mine", k), (name, "theirs", k)], at_row, lead, count, S * ffb))
    for k, (at_row, count) in enumerate(out_rows):
        jobs.append(("out", [("out", k)], at_row, 0, count, 1024))
    for k, (at_row, count) in enumerate(qkv_rows):
        jobs.append(("qkv", [("qkv", "mine", k), ("qkv", "theirs", k)], at_row, 0, count, S * blk))
    received = {}

    def update(limit):
        for name in list(reps.done):
            if name[1] == "theirs" and name not in received:
                received[name] = at.core(reps.done[name])
        while jobs and limit and all(k in reps.done for k in jobs[0][1]):
            name, needs, at_row, lead, count, unit = jobs.pop(0)
            rb = max(n for n in range(8, min(count, 176) + 1, 8) if count % n == 0 and at_row % n == 0)
            adam(name, [received[k] if k[1] == "theirs" else reps.done[k] for k in needs], at_row, lead, unit, rb)
            limit -= 1

    def ticks(n):
        for _ in range(n):
            reps.tick()

    def quarter_heads(x):
        return [x[:, h][None, None] for h in halves]

    n, start, finish, gate_all = gather_steps(quarter_heads(ggate), 3)
    start(0)
    g_down = do(lambda a, c: dot(a, c, PLAIN).astype(bf16), act, cot_all)
    for k, (at_row, count) in enumerate(down_rows):
        reps.push(("down", k), g_down[at_row : at_row + count])
    ticks(1)

    def norm_sums2(ggate, gup, gate, up, gains):
        a, b = ggate.astype(f32), gup.astype(f32)
        e = jnp.sum(a * gains[0] + b * gains[2], axis=0, keepdims=True)
        ez = jnp.sum(a * (gate - gains[1]) + b * (up - gains[3]), axis=0, keepdims=True)
        return join(e, ez)

    sums = do(norm_sums2, ggate, gup, gate, up, gains)
    steps2 = at.steps(False) + [("core", 1)]

    def sum_send(sums, axis, step):
        return at.core(sums) if axis == "core" else at.along(sums, axis, step)

    def sum_step(sums, axis, step):
        return do(lambda a, b: a + b, sums, sum_send(sums, axis, step))

    tiny = list(steps2)
    sums_got = sum_send(sums, *tiny[0])
    for i in range(1, n):
        finish()
        sums = do(lambda a, b: a + b, sums, sums_got)
        tiny.pop(0)
        start(i)
        sums_got = sum_send(sums, *tiny[0])
        ticks(1)
    n, start_up, finish_up, up_all = gather_steps(quarter_heads(gup), 3)
    finish()
    for axis, step in tiny:
        sums = do(lambda a, b: a + b, sums, sums_got)
        if (axis, step) != tiny[-1]:
            sums_got = sum_send(sums, *tiny[tiny.index((axis, step)) + 1])
    start_up(0)
    ggate_all = do(lambda x: x.reshape(Y * S * ffb, T), gate_all())
    finish_up()
    for i in range(1, n):
        start_up(i)
        if i == 1:
            g_gate = do(lambda x, g: dot(x, g, LAST).astype(bf16), xn2, ggate_all)
            push_pairs("gate", g_gate, up_rows)
            part_gate = do(lambda w, g: dot(w, g, FIRST), wg, ggate_all)
            out_part = do(lambda w, a: dot(w, a, FIRST).astype(bf16), wd_own, act)
            ticks(1)
        finish_up()
    gup_all = do(lambda x: x.reshape(Y * S * ffb, T), up_all())
    part = do(lambda w, g, p: dot(w, g, FIRST) + p, wu, gup_all, part_gate)
    part_theirs = at.core(part[blk:])

    def branch(a, b, cot, z, scale, gain, sums):
        gxn2 = a + b
        e = gxn2 * gain
        grad_hidden = cot.astype(f32) + scale * (e - sums[0:1] / width - z * (sums[1:2] / width))
        return grad_hidden.astype(bf16), grad_hidden, gxn2

    grad_branch, grad_hidden, gxn2 = do(
        branch, part[:blk], part_theirs, cot_cols, z2, inv2, own_cols[:, 2:3], sums
    )
    n, start, finish, branch_all = gather_steps(quarter_heads(grad_branch), 3)
    start(0)
    g_up = do(lambda x, g: dot(x, g, LAST).astype(bf16), xn2, gup_all)
    push_pairs("up", g_up, up_rows)
    finish()
    for i in range(1, n):
        start(i)
        if i == 1:
            ticks(1)
        finish()
    gbr_c = do(lambda x: x, branch_all())
    gbr_o = at.core(gbr_c)
    gbr = do(lambda a, b: in_order(a, b, 1).reshape(width, T), gbr_c, gbr_o)
    grad_attn = do(lambda w, g: dot(w, g, PLAIN).astype(bf16), wo_own, gbr)

    gqkvs = []
    for k in range(2):
        dout = grad_attn[:, halves[k]].reshape(heads, HEAD_DIM, H)
        gqkvs.append(do(attend_back, qkvs[k], dout, stats[k], table[seqs[k]]).reshape(3, blk, H))
    n, start, finish, gqkv_done = gather_steps([g.reshape(1, 1, 3 * blk, H) for g in gqkvs], 3)
    start(0)
    attn = lanes(*attns)
    g_out = do(lambda a, g: dot(a, g, LAST).astype(bf16), attn, gbr)
    for k, (at_row, count) in enumerate(out_rows):
        reps.push(("out", k), g_out[at_row : at_row + count])
    ticks(1)
    finish()
    for i in range(1, n):
        start(i)
        if i == 1:
            update(1)
            ticks(1)
            update(1)
        finish()

    def qkv_columns(x):
        return x.reshape(Y, S, 3, blk, T).transpose(2, 0, 1, 3, 4).reshape(3 * Y * S * blk, T)

    gqkv = do(qkv_columns, gqkv_done())
    g_qkv = do(lambda x, g: dot(x, g, LAST).astype(bf16), xn1, gqkv)
    push_pairs("qkv", g_qkv, qkv_rows)
    part = do(lambda w, g: dot(w, g, FIRST), wq, gqkv)
    part_theirs = at.core(part[blk:])
    out_sum = lax.psum_scatter(out_part, plane, scatter_dimension=0, tiled=True)
    reps.depth = 2
    ticks(1)
    update(1)
    ticks(1)

    def first_back(a, b, x, mean, inv, gain, gxn2, z2, gqkv0, gqkv1):
        gxn1 = a + b
        z1 = (x.astype(f32) - mean) * inv
        e = gxn1 * gain
        sums = join(jnp.sum(e, axis=0, keepdims=True), jnp.sum(e * z1, axis=0, keepdims=True))
        small = jnp.concatenate(
            [
                jnp.sum(gxn1 * z1, axis=1)[None],
                jnp.sum(gxn1, axis=1)[None],
                jnp.sum(gxn2 * z2, axis=1)[None],
                jnp.sum(gxn2, axis=1)[None],
                jnp.sum(gqkv0.astype(f32), axis=2) + jnp.sum(gqkv1.astype(f32), axis=2),
            ],
            axis=0,
        )
        return sums, small, gxn1, z1

    sums, small, gxn1, z1 = do(
        first_back, part[:blk], part_theirs, x_own, mean1, inv1, own_cols[:, 0:1], gxn2, z2, *gqkvs
    )
    for axis, step in steps2:
        sums = sum_step(sums, axis, step)
    ticks(1)
    input_grad = do(
        lambda h, grad, z, scale, gain, sums: h
        + scale * (grad * gain - sums[0:1] / width - z * (sums[1:2] / width)),
        grad_hidden,
        gxn1,
        z1,
        inv1,
        own_cols[:, 0:1],
        sums,
    )

    def to_rows(cols):
        split = do(lambda c: c.reshape(blk, S, at.ctx_size, rows).transpose(2, 1, 0, 3).reshape(nb, blk, rows), cols)
        got = lax.all_to_all(split, plane, split_axis=0, concat_axis=0, tiled=True)
        return do(lambda g: g.reshape(width, rows).T, got)

    input_rows = to_rows(input_grad)
    ticks(1)
    update(1)
    ticks(1)
    everyone = ("rep",) + plane
    small_all = lax.all_gather(small[None], everyone, axis=0, tiled=True)
    update(1)
    ticks(1)

    out_cols = do(lambda h, a: (h + a.astype(f32)).astype(bf16), hidden, out_sum)
    block_output = to_rows(out_cols)
    ticks(1)
    update(1)
    ticks(1)
    update(1)

    def norm_update(every, *a):
        every = every.reshape(lax.axis_size("rep"), nb, 7, blk)
        total = every[0]
        for k in range(1, every.shape[0]):
            total = total + every[k]
        return adam_update(*a, total.transpose(1, 0, 2).reshape(7, width), 0.3, 0.0)

    mn, vn, wn = do(norm_update, small_all, norm_params, m_norm, v_norm)
    while reps.busy():
        reps.tick()
        update(1)
    update(len(jobs))
    return (
        (block_output.reshape(tokens.shape), input_rows.reshape(tokens.shape))
        + tuple(results["qkv"])
        + tuple(results["out"])
        + tuple(results["up"])
        + tuple(results["down"])
        + (mn, vn, wn)
    )


def solution(mesh):
    tok = P("rep", "ctx", "shard", None)
    row = P(("ctx", "shard"), None)
    placed = (tok, tok, P("rep", "shard", None)) + (row,) * 4 + (P(),) + (row,) * 8 + (P(), P())
    return jax.shard_map(
        body,
        mesh=mesh,
        in_specs=placed,
        out_specs=(tok, tok) + (row,) * 12 + (P(),) * 3,
        check_vma=False,
    )
```

```python
import functools

import jax
import jax.numpy as jnp
from jax import lax
from jax.experimental import pallas as pl
from jax.experimental.pallas import tpu as pltpu
from jax.sharding import PartitionSpec as P

HEADS = 32
HEAD_DIM = 64
FF = 5632
ROTARY = 16
STEP = 10

eps_norm = 1e-05
masked_score = -1e30
beta_one = 0.9
beta_two = 0.999
adam_eps = 1e-08
weight_decay = 0.1
score_scale = HEAD_DIM ** (-0.5)
FIRST = (((0,), (0,)), ((), ()))
LAST = (((1,), (1,)), ((), ()))
PLAIN = (((1,), (0,)), ((), ()))
bf16 = jnp.bfloat16
f32 = jnp.float32


def dot(a, b, dims):
    return lax.dot_general(a, b, dims, preferred_element_type=f32)


def adam_update(weight, moment_one, moment_two, grad, step_rate, decay_rate):
    first_new = beta_one * moment_one + (1.0 - beta_one) * grad
    second_new = beta_two * moment_two + (1.0 - beta_two) * grad * grad
    first_hat = first_new / (1.0 - beta_one**STEP)
    second_hat = second_new / (1.0 - beta_two**STEP)
    weight_new = weight - step_rate * (
        first_hat / (jnp.sqrt(second_hat) + adam_eps) + decay_rate * weight
    )
    return (first_new, second_new, weight_new)


class Plane:
    def __init__(self):
        self.s_size = lax.axis_size("shard")
        self.ctx_size = lax.axis_size("ctx")
        self.y_size = self.ctx_size // 2
        self.ctx = lax.axis_index("ctx")
        self.s = lax.axis_index("shard")
        self.y = self.ctx // 2
        self.c = self.ctx % 2
        self.blocks = self.ctx_size * self.s_size

    def core(self, x):
        return lax.ppermute(x, "ctx", [(i, i ^ 1) for i in range(self.ctx_size)])

    def along(self, x, axis, step):
        if axis == "y":
            return lax.ppermute(x, "ctx", [(i, i ^ (2 * step)) for i in range(self.ctx_size)])
        return lax.ppermute(x, "shard", [(i, i ^ step) for i in range(self.s_size)])

    def index(self, axis):
        return self.y if axis == "y" else self.s

    def steps(self, flip):
        ys = []
        k = self.y_size // 2
        while k:
            ys.append(("y", k))
            k //= 2
        ss = []
        k = self.s_size // 2
        while k:
            ss.append(("s", k))
            k //= 2
        return ys + ss if flip else ss + ys

    def chip_exchange(self, x, take):
        out = [(self.y, self.s, take(self.y, self.s))]
        for ry in range(self.y_size):
            for rs in range(self.s_size):
                if ry or rs:
                    y, s = self.y ^ ry, self.s ^ rs
                    mask = 2 * ry * self.s_size + rs
                    perm = [(i, i ^ mask) for i in range(self.blocks)]
                    out.append((y, s, lax.ppermute(take(y, s), ("ctx", "shard"), perm)))
        return out

    def sum_all(self, x):
        for axis, step in self.steps(False):
            x = x + self.along(x, axis, step)
        return x + self.core(x)

    def scatter_sum(self, p, flip):
        axes = {"y": 1, "s": 2}
        steps = self.steps(flip)
        kept = got = None
        for n, (axis, step) in enumerate(steps):
            ax = axes[axis]
            bit = (self.index(axis) // step) % 2
            kept = lax.dynamic_slice_in_dim(p, bit * step, step, ax)
            send = lax.dynamic_slice_in_dim(p, (1 - bit) * step, step, ax)
            got = self.along(send, axis, step)
            if n + 1 < len(steps):
                p = (kept.astype(f32) + got.astype(f32)).astype(bf16)
        return kept[:, 0, 0], got[:, 0, 0]

    def gather(self, p, flip):
        axes = {"y": 1, "s": 2}
        p = p[:, None, None]
        for axis, step in reversed(self.steps(flip)):
            ax = axes[axis]
            bit = (self.index(axis) // step) % 2
            got = self.along(p, axis, step)
            first = bit == 0
            p = jnp.concatenate([jnp.where(first, p, got), jnp.where(first, got, p)], ax)
        return p


class Order:
    def __init__(self):
        self.last = None

    def __call__(self, stage, *args):
        if self.last is not None:
            args, self.last = lax.optimization_barrier((args, self.last))
        out = stage(*args)
        self.last = jax.tree.leaves(out)[0]
        return out


SMALL = pl.CostEstimate(flops=1024, bytes_accessed=1024, transcendentals=0)


class RepSum:
    def __init__(self, order):
        self.order = order
        z = lax.axis_index("rep")
        self.end = (z == 0) | (z == lax.axis_size("rep") - 1)
        self.queue = []
        self.flight = []
        self.depth = 1
        self.done = {}

    def push(self, name, g):
        self.queue.append((name, g))

    def busy(self):
        return bool(self.queue or self.flight)

    def tick(self):
        old = {}
        if len(self.flight) >= self.depth or (self.flight and not self.queue):
            old = self.flight.pop(0)
        new = self.queue.pop(0) if self.queue else None
        values = {}
        if "in" in old:
            values["g"], values["g_got"] = old["in"][1], old["in_got"]
        if "mid" in old:
            values["s"], values["s_got"] = old["mid"][1], old["mid_got"]
        if new:
            values["new"] = new[1]
        both = new and "mid" in old and new[1].shape == old["mid"][1].shape
        if "out" in old:
            values["out_got"] = old["out_got"]

        def stage(v):
            def add(a, b):
                return lax.reduce_precision(a.astype(f32) + b.astype(f32), 8, 7).astype(bf16)

            out = {}
            if "g" in v:
                out["a_sum"] = add(v["g"], v["g_got"])
            if "s" in v:
                total = add(v["s"], v["s_got"])
                out["total"] = jnp.where(self.end, v["new"], total) if both else total
            if "new" in v and not both:
                out["new"] = v["new"]
            if "out_got" in v:
                out["z_got"] = v["out_got"]
            return out

        if not values:
            return
        out = self.order(stage, values)
        if "out" in old:
            self.done[old["out"][0]] = jnp.where(self.end, out["z_got"], old["out"][1])
        slot = {}
        if both:
            got = lax.ppermute(out["total"], "rep", [(0, 1), (1, 0), (2, 3), (3, 2)])
            slot = {"in": new, "in_got": got, "out": (old["mid"][0], out["total"]), "out_got": got}
        else:
            if new:
                slot["in"] = new
                slot["in_got"] = lax.ppermute(out["new"], "rep", [(0, 1), (3, 2)])
            if "mid" in old:
                slot["out"] = (old["mid"][0], out["total"])
                slot["out_got"] = lax.ppermute(out["total"], "rep", [(1, 0), (2, 3)])
        if "in" in old:
            slot["mid"] = (old["in"][0], out["a_sum"])
            slot["mid_got"] = lax.ppermute(out["a_sum"], "rep", [(1, 2), (2, 1)])
        if slot:
            self.flight.append(slot)


def cast_kernel(w_ref, out_ref):
    out_ref[...] = w_ref[...].astype(bf16)


def cast(w):
    rows, width = w.shape
    unit = max(n for n in (128, 256, 512, 1024, 1408, 2048, 2816) if width % n == 0)
    spec = pl.BlockSpec((rows, unit), lambda i: (0, i))
    return pl.pallas_call(
        cast_kernel,
        grid=(width // unit,),
        in_specs=[spec],
        out_specs=spec,
        out_shape=jax.ShapeDtypeStruct(w.shape, bf16),
        compiler_params=pltpu.CompilerParams(vmem_limit_bytes=48 * 1024 * 1024),
        cost_estimate=SMALL,
    )(w)


def split_kernel(core_ref, w_ref, mine_ref, theirs_ref):
    unit = mine_ref.shape[0]
    first = core_ref[0] == 0
    a, b = w_ref[:, :unit], w_ref[:, unit:]
    mine_ref[...] = jnp.where(first, a, b).T.astype(bf16)
    theirs_ref[...] = jnp.where(first, b, a).T.astype(bf16)


def split_columns(w, core, lead, unit, count):
    rows = w.shape[0]
    half = pl.BlockSpec((unit, rows), lambda j, core: (j, 0))
    out = jax.ShapeDtypeStruct((count * unit, rows), bf16)
    return pl.pallas_call(
        split_kernel,
        grid_spec=pltpu.PrefetchScalarGridSpec(
            num_scalar_prefetch=1,
            grid=(count,),
            in_specs=[pl.BlockSpec((rows, 2 * unit), lambda j, core: (0, lead + j))],
            out_specs=[half, half],
        ),
        out_shape=[out, out],
        compiler_params=pltpu.CompilerParams(vmem_limit_bytes=32 * 1024 * 1024),
        cost_estimate=SMALL,
    )(core, w)


def arrange_kernel(at_ref, a_ref, b_ref, c_ref, d_ref, send_ref, keep_ref):
    send_ref[...] = jnp.concatenate([a_ref[...], b_ref[...]], axis=1)
    keep_ref[...] = jnp.concatenate([c_ref[...], d_ref[...]], axis=1)


def arrange(mine, got, place, pre, y_size, s_size, unit, flip):
    r = mine.shape[1]
    half = pre * y_size * s_size // 2

    def block(i, place, keep):
        p = i % pre
        i = i // pre
        if flip:
            s, y = i % s_size, i // s_size
            bit = place[0] // (y_size // 2)
            bit = bit if keep else 1 - bit
            y = y + bit * (y_size // 2)
        else:
            y, s = i % y_size, i // y_size
            bit = place[1] // (s_size // 2)
            bit = bit if keep else 1 - bit
            s = s + bit * (s_size // 2)
        return ((p * y_size + y) * s_size + s, 0)

    def spec(keep):
        return pl.BlockSpec((unit, r), lambda i, place: block(i, place, keep))

    out = jax.ShapeDtypeStruct((half * unit, 2 * r), bf16)
    out_spec = pl.BlockSpec((unit, 2 * r), lambda i, place: (i, 0))
    return pl.pallas_call(
        arrange_kernel,
        grid_spec=pltpu.PrefetchScalarGridSpec(
            num_scalar_prefetch=1,
            grid=(half,),
            in_specs=[spec(False), spec(False), spec(True), spec(True)],
            out_specs=[out_spec, out_spec],
        ),
        out_shape=[out, out],
        compiler_params=pltpu.CompilerParams(vmem_limit_bytes=32 * 1024 * 1024),
        cost_estimate=SMALL,
    )(place, mine, got, mine, got)


def product_kernel(dims, a_ref, b_ref, *refs):
    p = dot(a_ref[...], b_ref[...], dims)
    if len(refs) == 2:
        p = p + refs[0][...]
    refs[-1][...] = p.astype(refs[-1].dtype)


def mm(a, b, dims, dtype, tm=None, tn=None, add=None):
    (ca,), (cb,) = dims[0]
    m, k, n = a.shape[1 - ca], a.shape[ca], b.shape[1 - cb]
    tm, tn = tm or m, tn or n
    a_block = [0, 0]
    a_block[ca], a_block[1 - ca] = k, tm
    b_block = [0, 0]
    b_block[cb], b_block[1 - cb] = k, tn
    out = pl.BlockSpec((tm, tn), lambda i, j: (i, j))
    return pl.pallas_call(
        functools.partial(product_kernel, dims),
        grid=(m // tm, n // tn),
        in_specs=[
            pl.BlockSpec(tuple(a_block), (lambda i, j: (0, i)) if ca == 0 else (lambda i, j: (i, 0))),
            pl.BlockSpec(tuple(b_block), (lambda i, j: (0, j)) if cb == 0 else (lambda i, j: (j, 0))),
        ]
        + ([] if add is None else [out]),
        out_specs=out,
        out_shape=jax.ShapeDtypeStruct((m, n), dtype),
        compiler_params=pltpu.CompilerParams(vmem_limit_bytes=48 * 1024 * 1024),
        cost_estimate=SMALL,
    )(*((a, b) if add is None else (a, b, add)))


def last_step_kernel(bits_ref, own0_ref, got0_ref, own1_ref, got1_ref, out_ref):
    y, s = pl.program_id(1), pl.program_id(2)
    half = own0_ref.shape[3]
    ys, ss = bits_ref[2], bits_ref[3]
    a = jnp.where(s // ss == bits_ref[1], own0_ref[0, 0], got0_ref[0, 0])
    b = jnp.where(y // ys == bits_ref[0], own1_ref[0, 0], got1_ref[0, 0])
    out_ref[0, 0, 0, :, :half] = a
    out_ref[0, 0, 0, :, half:] = b


def last_step(parts, got, bits, pre, y_size, s_size):
    rows, half = parts[0].shape[2] // pre, parts[0].shape[3]
    along_s = pl.BlockSpec((1, 1, rows, half), lambda p, y, s, bits: (y, s % (s_size // 2), p, 0))
    along_y = pl.BlockSpec((1, 1, rows, half), lambda p, y, s, bits: (y % (y_size // 2), s, p, 0))
    return pl.pallas_call(
        last_step_kernel,
        grid_spec=pltpu.PrefetchScalarGridSpec(
            num_scalar_prefetch=1,
            grid=(pre, y_size, s_size),
            in_specs=[along_s, along_s, along_y, along_y],
            out_specs=pl.BlockSpec((1, 1, 1, rows, 2 * half), lambda p, y, s, bits: (p, y, s, 0, 0)),
        ),
        out_shape=jax.ShapeDtypeStruct((pre, y_size, s_size, rows, 2 * half), bf16),
        compiler_params=pltpu.CompilerParams(vmem_limit_bytes=48 * 1024 * 1024),
        cost_estimate=SMALL,
    )(bits, parts[0], got[0], parts[1], got[1])


def stack_turned_kernel(a_ref, b_ref, out_ref):
    r = a_ref.shape[1]
    out_ref[:r] = a_ref[...].T
    out_ref[r:] = b_ref[...].T


def stack_turned(a, b):
    rows, width = a.shape
    n = max(n for n in (1, 2, 4, 6, 8, 11) if rows % (128 * n) == 0)
    spec = pl.BlockSpec((rows // n, width), lambda i: (i, 0))
    return pl.pallas_call(
        stack_turned_kernel,
        grid=(n,),
        in_specs=[spec, spec],
        out_specs=pl.BlockSpec((2 * width, rows // n), lambda i: (0, i)),
        out_shape=jax.ShapeDtypeStruct((2 * width, rows), bf16),
        compiler_params=pltpu.CompilerParams(vmem_limit_bytes=48 * 1024 * 1024),
        cost_estimate=SMALL,
    )(a, b)


def add_split_kernel(bit_ref, a_ref, b_ref, c_ref, d_ref, send_ref, keep_ref):
    send_ref[...] = (a_ref[...].astype(f32) + b_ref[...].astype(f32)).astype(bf16)
    keep_ref[...] = (c_ref[...].astype(f32) + d_ref[...].astype(f32)).astype(bf16)


def add_split(kept, got, bit):
    rows, t = kept.shape
    half = rows // 2
    n = max(n for n in (1, 2, 3, 4) if half % (16 * n) == 0)
    rb = half // n
    away = pl.BlockSpec((rb, t), lambda i, bit: ((1 - bit[0]) * n + i, 0))
    here = pl.BlockSpec((rb, t), lambda i, bit: (bit[0] * n + i, 0))
    out = jax.ShapeDtypeStruct((half, t), bf16)
    out_spec = pl.BlockSpec((rb, t), lambda i, bit: (i, 0))
    return pl.pallas_call(
        add_split_kernel,
        grid_spec=pltpu.PrefetchScalarGridSpec(
            num_scalar_prefetch=1,
            grid=(n,),
            in_specs=[away, away, here, here],
            out_specs=[out_spec, out_spec],
        ),
        out_shape=[out, out],
        compiler_params=pltpu.CompilerParams(vmem_limit_bytes=48 * 1024 * 1024),
        cost_estimate=SMALL,
    )(bit, kept, got, kept, got)


def adam_kernel(rate, two, core_ref, w_ref, m_ref, v_ref, *refs):
    grad = refs[0][...].astype(f32)
    if two:
        other = refs[1][...].astype(f32)
        mine = core_ref[0] == 0
        grad = jnp.concatenate([jnp.where(mine, grad, other), jnp.where(mine, other, grad)], axis=1)
    new_m_ref, new_v_ref, new_w_ref = refs[-3:]
    new_m, new_v, new_w = adam_update(w_ref[...], m_ref[...], v_ref[...], grad, rate, weight_decay)
    new_m_ref[...] = new_m
    new_v_ref[...] = new_v
    new_w_ref[...] = new_w


def adam_part(state, grads, core, rate, prev, row_first, lead, unit, rb):
    w, m, v = state
    two = len(grads) == 2
    rows, width = grads[0].shape
    whole = pl.BlockSpec((rb, unit * len(grads)), lambda i, g, core: (row_first // rb + i, lead + g))
    half = pl.BlockSpec((rb, unit), lambda i, g, core: (i, g))
    out = jax.ShapeDtypeStruct(w.shape, f32)
    extra, aliases = [], {}
    if prev is not None:
        extra = list(prev)
        aliases = {4 + len(grads) + i: i for i in range(3)}
    return pl.pallas_call(
        functools.partial(adam_kernel, rate, two),
        grid_spec=pltpu.PrefetchScalarGridSpec(
            num_scalar_prefetch=1,
            grid=(rows // rb, width // unit),
            in_specs=[whole] * 3 + [half] * len(grads) + [pl.BlockSpec(memory_space=pl.ANY)] * len(extra),
            out_specs=[whole] * 3,
        ),
        out_shape=[out] * 3,
        input_output_aliases=aliases,
        compiler_params=pltpu.CompilerParams(vmem_limit_bytes=48 * 1024 * 1024),
        cost_estimate=SMALL,
    )(core, w, m, v, *grads, *extra)


def attend_kernel(kept_ref, got_ref, bias_ref, table_ref, qkv_ref, out_ref, stat_ref):
    half = ROTARY // 2
    cos, sin, pos = table_ref[0, :half], table_ref[0, half:ROTARY], table_ref[0, ROTARY:]
    parts = []
    for i in range(3):
        v = kept_ref[i, 0].astype(f32) + got_ref[i, 0].astype(f32) + bias_ref[i, 0]
        if i < 2:
            a, b = v[:half], v[half:ROTARY]
            v = jnp.concatenate([a * cos - b * sin, b * cos + a * sin, v[ROTARY:]], axis=0)
        v = v.astype(bf16)
        qkv_ref[i, 0] = v
        parts.append(v)
    q, k, v = parts
    scores = dot(k, q, FIRST) * score_scale
    scores = jnp.where(pos.T[:, :1] <= pos[:1], scores, masked_score)
    peak = jnp.max(scores, axis=0, keepdims=True)
    e = jnp.exp(scores - peak)
    total = jnp.sum(e, axis=0, keepdims=True)
    p = (e / total).astype(bf16)
    out_ref[0] = dot(v, p, PLAIN).astype(bf16)
    stat_ref[0, 0] = jnp.concatenate([peak, total], axis=0)


def attend(kept, got, bias, table):
    _, heads, hd, t = kept.shape
    seqs, _, seq = table.shape
    big = pl.BlockSpec((3, 1, hd, seq), lambda s, h: (0, h, 0, s))
    table_spec = pl.BlockSpec((1, table.shape[1], seq), lambda s, h: (s, 0, 0))
    stat = pl.BlockSpec((1, 1, 2, seq), lambda s, h: (s, h, 0, 0))
    return pl.pallas_call(
        attend_kernel,
        grid=(seqs, heads),
        in_specs=[
            big,
            big,
            pl.BlockSpec((3, 1, hd, 1), lambda s, h: (0, h, 0, 0)),
            table_spec,
        ],
        out_specs=[big, pl.BlockSpec((1, hd, seq), lambda s, h: (h, 0, s)), stat],
        out_shape=[
            jax.ShapeDtypeStruct((3, heads, hd, t), bf16),
            jax.ShapeDtypeStruct((heads, hd, t), bf16),
            jax.ShapeDtypeStruct((seqs, heads, 2, seq), f32),
        ],
        compiler_params=pltpu.CompilerParams(vmem_limit_bytes=32 * 1024 * 1024),
        cost_estimate=SMALL,
    )(kept, got, bias, table)


def attend_back_kernel(qkv_ref, dout_ref, stat_ref, table_ref, out_ref):
    half = ROTARY // 2
    cos, sin, pos = table_ref[0, :half], table_ref[0, half:ROTARY], table_ref[0, ROTARY:]
    q, k, v = qkv_ref[0, 0], qkv_ref[1, 0], qkv_ref[2, 0]
    dout = dout_ref[0]
    scores = dot(k, q, FIRST) * score_scale
    scores = jnp.where(pos.T[:, :1] <= pos[:1], scores, masked_score)
    p = jnp.exp(scores - stat_ref[0, 0, :1]) / stat_ref[0, 0, 1:]
    dp = dot(v, dout, FIRST)
    inner = jnp.sum(p * dp, axis=0, keepdims=True)
    ds = (p * (dp - inner)).astype(bf16)

    def back(x):
        a, b = x[:half], x[half:ROTARY]
        return jnp.concatenate([a * cos + b * sin, b * cos - a * sin, x[ROTARY:]], axis=0)

    out_ref[0, 0] = back(dot(k, ds, PLAIN) * score_scale).astype(bf16)
    out_ref[1, 0] = back(dot(q, ds, LAST) * score_scale).astype(bf16)
    out_ref[2, 0] = dot(dout, p.astype(bf16), LAST).astype(bf16)


def attend_back(qkv, dout, stats, table):
    _, heads, hd, t = qkv.shape
    seqs, _, seq = table.shape
    big = pl.BlockSpec((3, 1, hd, seq), lambda s, h: (0, h, 0, s))
    table_spec = pl.BlockSpec((1, table.shape[1], seq), lambda s, h: (s, 0, 0))
    stat = pl.BlockSpec((1, 1, 2, seq), lambda s, h: (s, h, 0, 0))
    return pl.pallas_call(
        attend_back_kernel,
        grid=(seqs, heads),
        in_specs=[
            big,
            pl.BlockSpec((1, hd, seq), lambda s, h: (h, 0, s)),
            stat,
            table_spec,
        ],
        out_specs=big,
        out_shape=jax.ShapeDtypeStruct((3, heads, hd, t), bf16),
        compiler_params=pltpu.CompilerParams(vmem_limit_bytes=32 * 1024 * 1024),
        cost_estimate=SMALL,
    )(qkv, dout, stats, table)


def body(
    tokens,
    cotangent,
    span_order,
    w_qkv,
    w_out,
    w_up,
    w_down,
    norm_params,
    m_qkv,
    v_qkv,
    m_out,
    v_out,
    m_up,
    v_up,
    m_down,
    v_down,
    m_norm,
    v_norm,
):
    at = Plane()
    do = Order()
    reps = RepSum(do)
    width = tokens.shape[3]
    rows = tokens.shape[1]
    S, Y, nb = at.s_size, at.y_size, at.blocks
    plane = ("ctx", "shard")
    blk = width // nb
    ffb = FF // nb
    heads = blk // HEAD_DIM
    seq = rows * at.ctx_size
    T = S * seq
    H = T // 2
    first = at.c == 0
    core = at.c.reshape(1)
    my_block = at.ctx * S + at.s
    halves = (slice(0, H), slice(H, T))
    seqs = (slice(0, S // 2), slice(S // 2, S))

    def pick(x, axis, which):
        return lax.dynamic_index_in_dim(x, which, axis, keepdims=False)

    def in_order(mine, theirs, axis):
        return jnp.stack([jnp.where(first, mine, theirs), jnp.where(first, theirs, mine)], axis=axis)

    def join(a, b):
        return jnp.concatenate([a, b], axis=0)

    def lanes(a, b):
        return jnp.concatenate([a, b], axis=1)

    x_rows = tokens.reshape(rows, width)
    order = span_order.reshape(-1).astype(f32)
    span = rows // 2

    def pack(x, order):
        xf = x.astype(f32)
        mean = jnp.mean(xf, axis=1)
        centred = xf - mean[:, None]
        inv = lax.rsqrt(jnp.mean(centred * centred, axis=1) + eps_norm)
        mine = lax.dynamic_slice_in_dim(order, 2 * at.ctx, 2)
        place = jnp.repeat(mine, span)
        terms = []
        for v in (mean, inv):
            for _ in range(3):
                t = lax.reduce_precision(v, 8, 7)
                terms.append(t)
                v = v - t
        extra = jnp.stack(terms + [place] + [jnp.zeros_like(place)] * 9).astype(bf16)
        blocks = x.T.reshape(nb, blk, rows)
        return jnp.concatenate([blocks, jnp.broadcast_to(extra[None], (nb, 16, rows))], axis=1)

    packed = do(pack, x_rows, order)
    cot_all = lax.all_gather(cotangent.reshape(rows, width), ("shard", "ctx"), axis=0, tiled=True)
    got = lax.all_to_all(packed, plane, split_axis=0, concat_axis=0, tiled=True)

    def chip_rows(w, lead, unit, count):
        mine, theirs = do(lambda w: split_columns(w, core, lead, unit, count), w)
        return mine, at.core(theirs)

    wq_parts = chip_rows(w_qkv, 0, S * blk, 3 * Y)
    norm_cols = norm_params.reshape(7, nb, blk).transpose(1, 2, 0)
    own_cols = pick(norm_cols, 0, my_block)
    other_cols = pick(norm_cols, 0, (at.ctx ^ 1) * S + at.s)
    pair_cols = join(own_cols, other_cols)
    bias = own_cols[:, 4:7].T.reshape(3, heads, HEAD_DIM, 1)
    spot = jnp.stack([at.y, at.s])

    def cut_weights(parts, pre, unit, flip):
        return do(lambda a, b: arrange(a, b, spot, pre, Y, S, unit, flip), *parts)

    wq_cut = [cut_weights(wq_parts, 3, blk, bool(k)) for k in range(2)]

    def columns(got):
        x = got.reshape(at.ctx_size, S, blk + 16, rows).transpose(2, 1, 0, 3).reshape(blk + 16, T)
        x_own, extra = x[:blk], x[blk:].astype(f32)
        mean = extra[0:1] + extra[1:2] + extra[2:3]
        inv = extra[3:4] + extra[4:5] + extra[5:6]
        return x_own, mean, inv, extra[6:7]

    x_own, mean1, inv1, place = do(columns, got)
    x_other = at.core(x_own)

    def first_norm(mine, theirs, mean, inv, cols):
        x = join(mine, theirs).astype(f32)
        return ((x - mean) * inv * cols[:, 0:1] + cols[:, 1:2]).astype(bf16)

    xn1 = do(first_norm, x_own, x_other, mean1, inv1, pair_cols)

    def send_products(cut, xs):
        got, kept = [], []
        for k in range(2):
            axis, step = at.steps(bool(k))[0]
            p = do(lambda w, x: dot(w, x, PLAIN).astype(bf16), cut[k][0], xs[k])
            got.append(at.along(p, axis, step))
        for k in range(2):
            kept.append(do(lambda w, x: dot(w, x, PLAIN).astype(bf16), cut[k][1], xs[k]))
        return list(zip(kept, got))

    def scatter_rest(pairs):
        for i in range(1, len(at.steps(False))):
            out = []
            for k in range(2):
                axis, step = at.steps(bool(k))[i]
                bit = (at.index(axis) // step) % 2
                send, kept = do(lambda a, b: add_split(a, b, bit.reshape(1)), *pairs[k])
                out.append((kept, at.along(send, axis, step)))
            pairs = out
        return pairs

    flying = send_products(wq_cut, [xn1[:, h] for h in halves])

    wo_parts = chip_rows(w_out, 0, S * blk, Y)
    wg_parts = chip_rows(w_up, 0, S * ffb, Y)
    wu_parts = chip_rows(w_up, Y, S * ffb, Y)
    wo_cut = [cut_weights(wo_parts, 1, blk, bool(k)) for k in range(2)]

    def positions(place):
        pos = place.reshape(S, seq) * span + (jnp.arange(seq) % span).astype(f32)[None, :]
        prow = pos.reshape(S, 1, seq)
        exponent = jnp.arange(ROTARY // 2, dtype=f32)
        inverse = 10000.0 ** (-2.0 * exponent / ROTARY)
        angles = prow * inverse[None, :, None]
        return jnp.concatenate([jnp.cos(angles), jnp.sin(angles), jnp.broadcast_to(prow, (S, 8, seq))], axis=1)

    table = do(positions, place)
    flying = scatter_rest(flying)

    def gather_steps(parts, pre):
        n = len(at.steps(False))
        state = {"parts": list(parts)}

        def start(i, after=None):
            if after is not None:
                state["parts"], _ = lax.optimization_barrier((state["parts"], after))
            state["got"] = []
            state["at"] = []
            for k in range(2):
                axis, step = list(reversed(at.steps(bool(k))))[i]
                state["at"].append((axis, step))
                state["got"].append(at.along(state["parts"][k], axis, step))

        def finish():
            def put(parts, got):
                out = []
                for k in range(2):
                    axis, step = state["at"][k]
                    ax = {"y": 0, "s": 1}[axis]
                    low = (at.index(axis) // step) % 2 == 0
                    a, b = parts[k], got[k]
                    out.append(jnp.concatenate([jnp.where(low, a, b), jnp.where(low, b, a)], ax))
                return out

            state["parts"] = do(put, state["parts"], state["got"])

        def result():
            ys, ss = Y // 2, S // 2
            bits = jnp.stack([at.y // ys, at.s // ss, jnp.int32(ys), jnp.int32(ss)]).astype(jnp.int32)
            return do(lambda p, g: last_step(p, g, bits, pre, Y, S), state["parts"], state["got"])

        return n, start, finish, result

    qkvs, attns, attn_got, stats = [], [], [], []
    for k in range(2):
        shape = (3, heads, HEAD_DIM, H)
        qkv, attn, stat = do(attend, flying[k][0].reshape(shape), flying[k][1].reshape(shape), bias, table[seqs[k]])
        qkvs.append(qkv)
        attns.append(attn.reshape(blk, H))
        attn_got.append(at.core(attns[k]))
        stats.append(stat)
    pairs = [do(join, attns[k], attn_got[k]) for k in range(2)]
    flying = send_products(wo_cut, pairs)
    wg_cut = cut_weights(wg_parts, 1, ffb, False)
    wu_cut = cut_weights(wu_parts, 1, ffb, True)

    def gain_products(wg, wu, cols):
        terms = []
        for v in (cols[:, 2], cols[:, 3]):
            t = lax.reduce_precision(v, 8, 7)
            terms += [t, v - t]
        terms = jnp.stack(terms).astype(bf16)
        out = []
        for mine, theirs in (wg, wu):
            p = dot(terms[:, :blk], mine, LAST) + dot(terms[:, blk:], theirs, LAST)
            out.append(jnp.stack([p[0] + p[1], p[2] + p[3]]).reshape(2, Y, S, ffb))
        return jnp.concatenate(out, axis=0)

    gains = do(gain_products, wg_parts, wu_parts, pair_cols)
    gain_steps = list(at.steps(False))

    def gain_step(gains):
        axis, step = gain_steps.pop(0)
        ax = {"y": 1, "s": 2}[axis]
        bit = (at.index(axis) // step) % 2
        send = lax.dynamic_slice_in_dim(gains, (1 - bit) * step, step, ax)
        kept = lax.dynamic_slice_in_dim(gains, bit * step, step, ax)
        return kept, at.along(send, axis, step)

    flying = scatter_rest(flying)
    def residual(x, a0, b0, a1, b1):
        a, b = lanes(a0, a1), lanes(b0, b1)
        hidden = x.astype(f32) + (a.astype(f32) + b.astype(f32))
        local_mean = jnp.mean(hidden, axis=0, keepdims=True)
        dev = hidden - local_mean
        return hidden, join(local_mean, jnp.sum(dev * dev, axis=0, keepdims=True))

    hidden, moments = do(residual, x_own, *flying[0], *flying[1])
    count = blk
    for axis, step in at.steps(False) + [("core", 1)]:
        other = at.core(moments) if axis == "core" else at.along(moments, axis, step)

        def merge(a, b):
            gap = a[0:1] - b[0:1]
            return join(0.5 * (a[0:1] + b[0:1]), a[1:2] + b[1:2] + gap * gap * (count / 2.0))

        moments = do(merge, moments, other)
        count *= 2

    def second_norm(hidden, moments, cols):
        inv2 = lax.rsqrt(moments[1:2] / width + eps_norm)
        z2 = (hidden - moments[0:1]) * inv2
        return (z2 * cols[:, 2:3] + cols[:, 3:4]).astype(bf16), z2, inv2

    gains = gain_step(gains)
    xn2_own, z2, inv2 = do(second_norm, hidden, moments, own_cols)
    xn2 = do(join, xn2_own, at.core(xn2_own))

    flying = send_products([wg_cut, wu_cut], [xn2, xn2])

    wd_own = do(cast, w_down)
    wg = do(stack_turned, *wg_parts)
    wu = do(stack_turned, *wu_parts)
    grad_act = do(lambda w, c: mm(w, c, LAST, f32, tn=256), wd_own, cot_all)
    cot_cols = do(lambda c: lax.dynamic_slice_in_dim(c, my_block * blk, blk, 1).T, cot_all)
    wo_own = do(cast, w_out)
    wq = do(stack_turned, *wq_parts)
    gains = do(lambda a, b: a + b, *gains)
    while gain_steps:
        gains = do(lambda a, b: a + b, *gain_step(gains))
    gains = do(lambda g: g.reshape(4, ffb, 1), gains)
    flying = scatter_rest(flying)

    def gated(ga, gb, ua, ub, grad_act, gains):
        gate = ga.astype(f32) + gb.astype(f32)
        up = ua.astype(f32) + ub.astype(f32)
        sig = jax.nn.sigmoid(gate)
        silu = gate * sig
        ggate = (grad_act * up * sig * (1.0 + gate * (1.0 - sig))).astype(bf16)
        gup = (grad_act * silu).astype(bf16)
        return ggate, gup, (silu * up).astype(bf16), gate, up

    ggate, gup, act, gate, up = do(gated, *flying[0], *flying[1], grad_act, gains)

    def parts_of(count, want):
        return max(n for n in range(1, want + 1) if count % (16 * n) == 0)

    def even(count, want):
        n = parts_of(count, want)
        return [(k * (count // n), count // n) for k in range(n)]

    down_rows, up_rows = even(ffb, 2), [(0, blk)]

    def push_pairs(name, g, rows):
        for k, (at_row, count) in enumerate(rows):
            reps.push((name, "theirs", k), g[blk + at_row : blk + at_row + count])
            reps.push((name, "mine", k), g[at_row : at_row + count])

    results = {"down": None, "out": None, "up": None, "qkv": None}
    states = {
        "down": (w_down, m_down, v_down),
        "out": (w_out, m_out, v_out),
        "up": (w_up, m_up, v_up),
        "qkv": (w_qkv, m_qkv, v_qkv),
    }
    rates = {"down": 0.02, "out": 0.2, "up": 0.03, "qkv": 0.03}

    def adam(name, grads, row_first, lead, unit, rb):
        results[name] = do(
            lambda s, g, prev: adam_part(s, g, core, rates[name], prev, row_first, lead, unit, rb),
            states[name],
            grads,
            results[name],
        )

    jobs = []
    for k, (at_row, count) in enumerate(down_rows):
        jobs.append(("down", [("down", k)], at_row, 0, count, 1024))
    for name, lead in (("gate", 0), ("up", Y)):
        for k, (at_row, count) in enumerate(up_rows):
            jobs.append(("up", [(name, "mine", k), (name, "theirs", k)], at_row, lead, count, S * ffb))
    for k in range(2):
        jobs.append(("out", [("out", k)], 0, k, blk, width // 2))
    for third in (2, 1, 0):
        for k, (at_row, count) in enumerate(up_rows):
            jobs.append(
                ("qkv", [(third, "mine", k), (third, "theirs", k)], at_row, third * Y, count, S * blk)
            )
    received = {}

    def update(limit):
        for name in list(reps.done):
            if name[1] == "theirs" and name not in received:
                received[name] = at.core(reps.done[name])
        while jobs and limit and all(k in reps.done for k in jobs[0][1]):
            name, needs, at_row, lead, count, unit = jobs.pop(0)
            rb = max(n for n in range(8, min(count, 176) + 1, 8) if count % n == 0 and at_row % n == 0)
            adam(name, [received[k] if k[1] == "theirs" else reps.done[k] for k in needs], at_row, lead, unit, rb)
            limit -= 1

    def ticks(n):
        for _ in range(n):
            reps.tick()

    wide = 2 * FF // 8

    def quarter_heads(x):
        return [x[:, h][None, None] for h in halves]

    n, start, finish, gate_all = gather_steps(quarter_heads(ggate), 1)
    start(0)
    g_down = do(lambda a, c: mm(a, c, PLAIN, bf16, tn=512), act, cot_all)
    for k, (at_row, count) in enumerate(down_rows):
        reps.push(("down", k), g_down[at_row : at_row + count])
    ticks(1)

    def norm_sums2(ggate, gup, gate, up, gains):
        a, b = ggate.astype(f32), gup.astype(f32)
        e = jnp.sum(a * gains[0] + b * gains[2], axis=0, keepdims=True)
        ez = jnp.sum(a * (gate - gains[1]) + b * (up - gains[3]), axis=0, keepdims=True)
        return join(e, ez)

    sums = do(norm_sums2, ggate, gup, gate, up, gains)
    steps2 = at.steps(False) + [("core", 1)]

    def sum_send(sums, axis, step):
        return at.core(sums) if axis == "core" else at.along(sums, axis, step)

    def sum_step(sums, axis, step):
        return do(lambda a, b: a + b, sums, sum_send(sums, axis, step))

    tiny = list(steps2)
    sums_got = sum_send(sums, *tiny.pop(0))
    for i in range(1, n):
        finish()
        sums = do(lambda a, b: a + b, sums, sums_got)
        sums_got = sum_send(sums, *tiny.pop(0))
        start(i, sums)
        ticks(1)
    n, start_up, finish_up, up_all = gather_steps(quarter_heads(gup), 1)
    ggate_all = gate_all().reshape(Y * S * ffb, T)
    sums = do(lambda a, b: a + b, sums, sums_got)
    start_up(0, sums)
    while tiny:
        sums = sum_step(sums, *tiny.pop(0))
    g_gate = do(lambda x, g: mm(x, g, LAST, bf16, tn=wide), xn2, ggate_all)
    push_pairs("gate", g_gate, up_rows)
    finish_up()
    for i in range(1, n):
        start_up(i)
        if i == 1:
            ticks(1)
            part_gate = do(lambda w, g: mm(w, g, PLAIN, f32, tn=256), wg, ggate_all)
            out_part = do(lambda w, a: mm(w, a, FIRST, bf16, tm=512), wd_own, act)
            update(1)
        if i < n - 1:
            finish_up()
    gup_all = up_all().reshape(Y * S * ffb, T)
    part = do(lambda w, g, p: dot(w, g, PLAIN) + p, wu, gup_all, part_gate)
    part_theirs = at.core(part[blk:])
    ticks(1)

    def branch(a, b, cot, z, scale, gain, sums):
        gxn2 = a + b
        e = gxn2 * gain
        grad_hidden = cot.astype(f32) + scale * (e - sums[0:1] / width - z * (sums[1:2] / width))
        return grad_hidden.astype(bf16), grad_hidden, gxn2

    grad_branch, grad_hidden, gxn2 = do(
        branch, part[:blk], part_theirs, cot_cols, z2, inv2, own_cols[:, 2:3], sums
    )
    n, start, finish, branch_all = gather_steps(quarter_heads(grad_branch), 1)
    start(0)
    g_up = do(lambda x, g: mm(x, g, LAST, bf16, tn=wide), xn2, gup_all)
    push_pairs("up", g_up, up_rows)
    finish()
    for i in range(1, n):
        start(i)
        if i == 1:
            ticks(1)
        if i < n - 1:
            finish()
    gbr_c = branch_all()[0]
    gbr_o = at.core(gbr_c)
    gbr = do(lambda a, b: in_order(a, b, 1).reshape(width, T), gbr_c, gbr_o)
    grad_attn = do(lambda w, g: dot(w, g, PLAIN).astype(bf16), wo_own, gbr)

    gqkvs = []
    for k in range(2):
        dout = grad_attn[:, halves[k]].reshape(heads, HEAD_DIM, H)
        gqkvs.append(do(attend_back, qkvs[k], dout, stats[k], table[seqs[k]]).reshape(3, blk, H))
    n, start, finish, gqkv_done = gather_steps([g.reshape(1, 1, 3 * blk, H) for g in gqkvs], 3)
    start(0)
    attn = lanes(*attns)
    for k in range(2):
        g_out = do(lambda a, g: mm(a, g, LAST, bf16, tn=512), attn, gbr[k * width // 2 : (k + 1) * width // 2])
        reps.push(("out", k), g_out)
    ticks(1)
    finish()
    for i in range(1, n):
        start(i)
        if i == 1:
            update(1)
            ticks(1)
            update(1)
        if i < n - 1:
            finish()
    gqkv = gqkv_done().reshape(3, Y * S * blk, T)
    for third in (2, 1, 0):
        g = do(lambda x, g: dot(x, g, LAST).astype(bf16), xn1, gqkv[third])
        push_pairs(third, g, up_rows)
        if third == 2:
            ticks(1)
    part = do(lambda w, g: dot(w, g, PLAIN), wq, gqkv.reshape(3 * Y * S * blk, T))
    part_theirs = at.core(part[blk:])
    out_sum = lax.psum_scatter(out_part, plane, scatter_dimension=0, tiled=True)
    reps.depth = 2
    ticks(1)
    update(1)
    ticks(1)

    def first_back(a, b, x, mean, inv, gain, gxn2, z2, gqkv0, gqkv1):
        gxn1 = a + b
        z1 = (x.astype(f32) - mean) * inv
        e = gxn1 * gain
        sums = join(jnp.sum(e, axis=0, keepdims=True), jnp.sum(e * z1, axis=0, keepdims=True))
        small = jnp.concatenate(
            [
                jnp.sum(gxn1 * z1, axis=1)[None],
                jnp.sum(gxn1, axis=1)[None],
                jnp.sum(gxn2 * z2, axis=1)[None],
                jnp.sum(gxn2, axis=1)[None],
                jnp.sum(gqkv0.astype(f32), axis=2) + jnp.sum(gqkv1.astype(f32), axis=2),
            ],
            axis=0,
        )
        return sums, small, gxn1, z1

    sums, small, gxn1, z1 = do(
        first_back, part[:blk], part_theirs, x_own, mean1, inv1, own_cols[:, 0:1], gxn2, z2, *gqkvs
    )
    for axis, step in steps2:
        sums = sum_step(sums, axis, step)
    ticks(1)
    input_grad = do(
        lambda h, grad, z, scale, gain, sums: h
        + scale * (grad * gain - sums[0:1] / width - z * (sums[1:2] / width)),
        grad_hidden,
        gxn1,
        z1,
        inv1,
        own_cols[:, 0:1],
        sums,
    )

    def to_rows(cols):
        split = do(lambda c: c.reshape(blk, S, at.ctx_size, rows).transpose(2, 1, 0, 3).reshape(nb, blk, rows), cols)
        got = lax.all_to_all(split, plane, split_axis=0, concat_axis=0, tiled=True)
        return do(lambda g: g.reshape(width, rows).T, got)

    input_rows = to_rows(input_grad)
    ticks(1)
    update(1)
    ticks(1)
    n_rep = lax.axis_size("rep")
    step = 1
    while step < n_rep:
        other = lax.ppermute(small, "rep", [(i, i ^ step) for i in range(n_rep)])
        small = do(lambda a, b: a + b, small, other)
        step *= 2
    update(1)
    ticks(1)
    sent = do(lambda s: jnp.broadcast_to(s.reshape(1, 7, blk), (nb, 7, blk)), small)
    small_all = lax.all_to_all(sent, plane, split_axis=0, concat_axis=0, tiled=True)

    out_cols = do(lambda h, a: (h + a.astype(f32)).astype(bf16), hidden, out_sum)
    block_output = to_rows(out_cols)
    ticks(1)
    update(1)
    ticks(1)
    update(1)

    def norm_update(every, *a):
        return adam_update(*a, every.transpose(1, 0, 2).reshape(7, width), 0.3, 0.0)

    mn, vn, wn = do(norm_update, small_all, norm_params, m_norm, v_norm)
    while reps.busy():
        reps.tick()
        update(1)
    update(len(jobs))
    return (
        (block_output.reshape(tokens.shape), input_rows.reshape(tokens.shape))
        + tuple(results["qkv"])
        + tuple(results["out"])
        + tuple(results["up"])
        + tuple(results["down"])
        + (mn, vn, wn)
    )


def solution(mesh):
    tok = P("rep", "ctx", "shard", None)
    row = P(("ctx", "shard"), None)
    placed = (tok, tok, P("rep", "shard", None)) + (row,) * 4 + (P(),) + (row,) * 8 + (P(), P())
    return jax.shard_map(
        body,
        mesh=mesh,
        in_specs=placed,
        out_specs=(tok, tok) + (row,) * 12 + (P(),) * 3,
        check_vma=False,
    )
```

```python
import functools

import jax
import jax.numpy as jnp
from jax import lax
from jax.experimental import pallas as pl
from jax.experimental.pallas import tpu as pltpu
from jax.sharding import PartitionSpec as P

HEADS = 32
HEAD_DIM = 64
FF = 5632
ROTARY = 16
STEP = 10

eps_norm = 1e-05
masked_score = -1e30
beta_one = 0.9
beta_two = 0.999
adam_eps = 1e-08
weight_decay = 0.1
score_scale = HEAD_DIM ** (-0.5)
FIRST = (((0,), (0,)), ((), ()))
LAST = (((1,), (1,)), ((), ()))
PLAIN = (((1,), (0,)), ((), ()))
bf16 = jnp.bfloat16
f32 = jnp.float32


def dot(a, b, dims):
    return lax.dot_general(a, b, dims, preferred_element_type=f32)


def adam_update(weight, moment_one, moment_two, grad, step_rate, decay_rate):
    first_new = beta_one * moment_one + (1.0 - beta_one) * grad
    second_new = beta_two * moment_two + (1.0 - beta_two) * grad * grad
    first_hat = first_new / (1.0 - beta_one**STEP)
    second_hat = second_new / (1.0 - beta_two**STEP)
    weight_new = weight - step_rate * (
        first_hat / (jnp.sqrt(second_hat) + adam_eps) + decay_rate * weight
    )
    return (first_new, second_new, weight_new)


class Plane:
    def __init__(self):
        self.s_size = lax.axis_size("shard")
        self.ctx_size = lax.axis_size("ctx")
        self.y_size = self.ctx_size // 2
        self.ctx = lax.axis_index("ctx")
        self.s = lax.axis_index("shard")
        self.y = self.ctx // 2
        self.c = self.ctx % 2
        self.blocks = self.ctx_size * self.s_size

    def core(self, x):
        return lax.ppermute(x, "ctx", [(i, i ^ 1) for i in range(self.ctx_size)])

    def along(self, x, axis, step):
        if axis == "y":
            return lax.ppermute(x, "ctx", [(i, i ^ (2 * step)) for i in range(self.ctx_size)])
        return lax.ppermute(x, "shard", [(i, i ^ step) for i in range(self.s_size)])

    def index(self, axis):
        return self.y if axis == "y" else self.s

    def steps(self, flip):
        ys = []
        k = self.y_size // 2
        while k:
            ys.append(("y", k))
            k //= 2
        ss = []
        k = self.s_size // 2
        while k:
            ss.append(("s", k))
            k //= 2
        return ys + ss if flip else ss + ys

    def chip_exchange(self, x, take):
        out = [(self.y, self.s, take(self.y, self.s))]
        for ry in range(self.y_size):
            for rs in range(self.s_size):
                if ry or rs:
                    y, s = self.y ^ ry, self.s ^ rs
                    mask = 2 * ry * self.s_size + rs
                    perm = [(i, i ^ mask) for i in range(self.blocks)]
                    out.append((y, s, lax.ppermute(take(y, s), ("ctx", "shard"), perm)))
        return out

    def sum_all(self, x):
        for axis, step in self.steps(False):
            x = x + self.along(x, axis, step)
        return x + self.core(x)

    def scatter_sum(self, p, flip):
        axes = {"y": 1, "s": 2}
        steps = self.steps(flip)
        kept = got = None
        for n, (axis, step) in enumerate(steps):
            ax = axes[axis]
            bit = (self.index(axis) // step) % 2
            kept = lax.dynamic_slice_in_dim(p, bit * step, step, ax)
            send = lax.dynamic_slice_in_dim(p, (1 - bit) * step, step, ax)
            got = self.along(send, axis, step)
            if n + 1 < len(steps):
                p = (kept.astype(f32) + got.astype(f32)).astype(bf16)
        return kept[:, 0, 0], got[:, 0, 0]

    def gather(self, p, flip):
        axes = {"y": 1, "s": 2}
        p = p[:, None, None]
        for axis, step in reversed(self.steps(flip)):
            ax = axes[axis]
            bit = (self.index(axis) // step) % 2
            got = self.along(p, axis, step)
            first = bit == 0
            p = jnp.concatenate([jnp.where(first, p, got), jnp.where(first, got, p)], ax)
        return p


class Order:
    def __init__(self):
        self.last = None

    def __call__(self, stage, *args):
        if self.last is not None:
            args, self.last = lax.optimization_barrier((args, self.last))
        out = stage(*args)
        self.last = jax.tree.leaves(out)[0]
        return out


SMALL = pl.CostEstimate(flops=1024, bytes_accessed=1024, transcendentals=0)


class RepSum:
    def __init__(self, order):
        self.order = order
        z = lax.axis_index("rep")
        self.end = (z == 0) | (z == lax.axis_size("rep") - 1)
        self.queue = []
        self.flight = []
        self.depth = 1
        self.done = {}

    def push(self, name, g):
        self.queue.append((name, g))

    def busy(self):
        return bool(self.queue or self.flight)

    def tick(self):
        old = {}
        if len(self.flight) >= self.depth or (self.flight and not self.queue):
            old = self.flight.pop(0)
        new = self.queue.pop(0) if self.queue else None
        values = {}
        if "in" in old:
            values["g"], values["g_got"] = old["in"][1], old["in_got"]
        if "mid" in old:
            values["s"], values["s_got"] = old["mid"][1], old["mid_got"]
        if new:
            values["new"] = new[1]
        both = new and "mid" in old and new[1].shape == old["mid"][1].shape
        if "out" in old:
            values["out_got"] = old["out_got"]

        def stage(v):
            def add(a, b):
                return lax.reduce_precision(a.astype(f32) + b.astype(f32), 8, 7).astype(bf16)

            out = {}
            if "g" in v:
                out["a_sum"] = add(v["g"], v["g_got"])
            if "s" in v:
                total = add(v["s"], v["s_got"])
                out["total"] = jnp.where(self.end, v["new"], total) if both else total
            if "new" in v and not both:
                out["new"] = v["new"]
            if "out_got" in v:
                out["z_got"] = v["out_got"]
            return out

        if not values:
            return
        out = self.order(stage, values)
        if "out" in old:
            self.done[old["out"][0]] = jnp.where(self.end, out["z_got"], old["out"][1])
        slot = {}
        if both:
            got = lax.ppermute(out["total"], "rep", [(0, 1), (1, 0), (2, 3), (3, 2)])
            slot = {"in": new, "in_got": got, "out": (old["mid"][0], out["total"]), "out_got": got}
        else:
            if new:
                slot["in"] = new
                slot["in_got"] = lax.ppermute(out["new"], "rep", [(0, 1), (3, 2)])
            if "mid" in old:
                slot["out"] = (old["mid"][0], out["total"])
                slot["out_got"] = lax.ppermute(out["total"], "rep", [(1, 0), (2, 3)])
        if "in" in old:
            slot["mid"] = (old["in"][0], out["a_sum"])
            slot["mid_got"] = lax.ppermute(out["a_sum"], "rep", [(1, 2), (2, 1)])
        if slot:
            self.flight.append(slot)


def cast_kernel(w_ref, out_ref):
    out_ref[...] = w_ref[...].astype(bf16)


def cast(w):
    rows, width = w.shape
    unit = max(n for n in (128, 256, 512, 1024, 1408, 2048, 2816) if width % n == 0)
    spec = pl.BlockSpec((rows, unit), lambda i: (0, i))
    return pl.pallas_call(
        cast_kernel,
        grid=(width // unit,),
        in_specs=[spec],
        out_specs=spec,
        out_shape=jax.ShapeDtypeStruct(w.shape, bf16),
        compiler_params=pltpu.CompilerParams(vmem_limit_bytes=48 * 1024 * 1024),
        cost_estimate=SMALL,
    )(w)


class PairSum:
    def __init__(self, order, g):
        self.order = order
        self.even = lax.axis_index("rep") % 2 == 0
        half = g.shape[0] // 2

        def cut(g):
            a, b = g[:half], g[half:]
            return jnp.where(self.even, b, a), jnp.where(self.even, a, b)

        send, self.kept = order(cut, g)
        self.got = self.exchange(send, 1)
        self.stage = 0

    def exchange(self, x, step):
        return lax.ppermute(x, "rep", [(i, i ^ step) for i in range(lax.axis_size("rep"))])

    def step(self):
        def add(a, b):
            return lax.reduce_precision(a.astype(f32) + b.astype(f32), 8, 7).astype(bf16)

        def put(a, b):
            return jnp.where(self.even, a, b), jnp.where(self.even, b, a)

        if self.stage < 2:
            self.kept = self.order(add, self.kept, self.got)
            self.got = self.exchange(self.kept, 2 - self.stage)
        else:
            self.done = self.order(put, self.kept, self.got)
        self.stage += 1


def gated_kernel(ga_ref, gb_ref, ua_ref, ub_ref, grad_ref, gains_ref, g0_ref, g1_ref, u0_ref, u1_ref, act_ref, sums_ref):
    half = g0_ref.shape[1]
    gate = ga_ref[...].astype(f32) + gb_ref[...].astype(f32)
    up = ua_ref[...].astype(f32) + ub_ref[...].astype(f32)
    sig = jax.nn.sigmoid(gate)
    silu = gate * sig
    grad = grad_ref[...]
    act_ref[...] = (silu * up).astype(bf16)
    ggate = (grad * up * sig * (1.0 + gate * (1.0 - sig))).astype(bf16)
    gup = (grad * silu).astype(bf16)
    g0_ref[...] = ggate[:, :half]
    g1_ref[...] = ggate[:, half:]
    u0_ref[...] = gup[:, :half]
    u1_ref[...] = gup[:, half:]
    a, b = ggate.astype(f32), gup.astype(f32)
    e = jnp.sum(a * gains_ref[0] + b * gains_ref[2], axis=0, keepdims=True)
    ez = jnp.sum(a * (gate - gains_ref[1]) + b * (up - gains_ref[3]), axis=0, keepdims=True)
    both = jnp.concatenate([e, ez], axis=0)

    @pl.when(pl.program_id(0) == 0)
    def _():
        sums_ref[...] = both

    @pl.when(pl.program_id(0) > 0)
    def _():
        sums_ref[...] += both


def gated(ga, gb, ua, ub, grad_act, gains):
    rows, t = grad_act.shape
    n = max(n for n in (1, 2, 4) if rows % (16 * n) == 0)
    whole = pl.BlockSpec((rows // n, t), lambda i: (i, 0))
    half = pl.BlockSpec((rows // n, t // 2), lambda i: (i, 0))
    out_half = jax.ShapeDtypeStruct((rows, t // 2), bf16)
    return pl.pallas_call(
        gated_kernel,
        grid=(n,),
        in_specs=[whole] * 5 + [pl.BlockSpec((4, rows // n, 1), lambda i: (0, i, 0))],
        out_specs=[half] * 4 + [whole, pl.BlockSpec((2, t), lambda i: (0, 0))],
        out_shape=[out_half] * 4 + [jax.ShapeDtypeStruct((rows, t), bf16), jax.ShapeDtypeStruct((2, t), f32)],
        compiler_params=pltpu.CompilerParams(vmem_limit_bytes=56 * 1024 * 1024),
        cost_estimate=SMALL,
    )(ga, gb, ua, ub, grad_act, gains)


def split_kernel(core_ref, w_ref, mine_ref, theirs_ref):
    unit = mine_ref.shape[0]
    first = core_ref[0] == 0
    a, b = w_ref[:, :unit], w_ref[:, unit:]
    mine_ref[...] = jnp.where(first, a, b).T.astype(bf16)
    theirs_ref[...] = jnp.where(first, b, a).T.astype(bf16)


def split_columns(w, core, lead, unit, count):
    rows = w.shape[0]
    half = pl.BlockSpec((unit, rows), lambda j, core: (j, 0))
    out = jax.ShapeDtypeStruct((count * unit, rows), bf16)
    return pl.pallas_call(
        split_kernel,
        grid_spec=pltpu.PrefetchScalarGridSpec(
            num_scalar_prefetch=1,
            grid=(count,),
            in_specs=[pl.BlockSpec((rows, 2 * unit), lambda j, core: (0, lead + j))],
            out_specs=[half, half],
        ),
        out_shape=[out, out],
        compiler_params=pltpu.CompilerParams(vmem_limit_bytes=32 * 1024 * 1024),
        cost_estimate=SMALL,
    )(core, w)


def arrange_kernel(at_ref, a_ref, b_ref, c_ref, d_ref, send_ref, keep_ref):
    send_ref[...] = jnp.concatenate([a_ref[...], b_ref[...]], axis=1)
    keep_ref[...] = jnp.concatenate([c_ref[...], d_ref[...]], axis=1)


def arrange(mine, got, place, pre, y_size, s_size, unit, flip):
    r = mine.shape[1]
    half = pre * y_size * s_size // 2

    def block(i, place, keep):
        p = i % pre
        i = i // pre
        if flip:
            s, y = i % s_size, i // s_size
            bit = place[0] // (y_size // 2)
            bit = bit if keep else 1 - bit
            y = y + bit * (y_size // 2)
        else:
            y, s = i % y_size, i // y_size
            bit = place[1] // (s_size // 2)
            bit = bit if keep else 1 - bit
            s = s + bit * (s_size // 2)
        return ((p * y_size + y) * s_size + s, 0)

    def spec(keep):
        return pl.BlockSpec((unit, r), lambda i, place: block(i, place, keep))

    out = jax.ShapeDtypeStruct((half * unit, 2 * r), bf16)
    out_spec = pl.BlockSpec((unit, 2 * r), lambda i, place: (i, 0))
    return pl.pallas_call(
        arrange_kernel,
        grid_spec=pltpu.PrefetchScalarGridSpec(
            num_scalar_prefetch=1,
            grid=(half,),
            in_specs=[spec(False), spec(False), spec(True), spec(True)],
            out_specs=[out_spec, out_spec],
        ),
        out_shape=[out, out],
        compiler_params=pltpu.CompilerParams(vmem_limit_bytes=32 * 1024 * 1024),
        cost_estimate=SMALL,
    )(place, mine, got, mine, got)


def product_kernel(dims, a_ref, b_ref, *refs):
    p = dot(a_ref[...], b_ref[...], dims)
    if len(refs) == 2:
        p = p + refs[0][...]
    refs[-1][...] = p.astype(refs[-1].dtype)


def mm(a, b, dims, dtype, tm=None, tn=None, add=None):
    (ca,), (cb,) = dims[0]
    m, k, n = a.shape[1 - ca], a.shape[ca], b.shape[1 - cb]
    tm, tn = tm or m, tn or n
    a_block = [0, 0]
    a_block[ca], a_block[1 - ca] = k, tm
    b_block = [0, 0]
    b_block[cb], b_block[1 - cb] = k, tn
    out = pl.BlockSpec((tm, tn), lambda i, j: (i, j))
    return pl.pallas_call(
        functools.partial(product_kernel, dims),
        grid=(m // tm, n // tn),
        in_specs=[
            pl.BlockSpec(tuple(a_block), (lambda i, j: (0, i)) if ca == 0 else (lambda i, j: (i, 0))),
            pl.BlockSpec(tuple(b_block), (lambda i, j: (0, j)) if cb == 0 else (lambda i, j: (j, 0))),
        ]
        + ([] if add is None else [out]),
        out_specs=out,
        out_shape=jax.ShapeDtypeStruct((m, n), dtype),
        compiler_params=pltpu.CompilerParams(vmem_limit_bytes=48 * 1024 * 1024),
        cost_estimate=SMALL,
    )(*((a, b) if add is None else (a, b, add)))


def last_step_kernel(bits_ref, own0_ref, got0_ref, own1_ref, got1_ref, out_ref):
    y, s = pl.program_id(1), pl.program_id(2)
    half = own0_ref.shape[3]
    ys, ss = bits_ref[2], bits_ref[3]
    a = jnp.where(s // ss == bits_ref[1], own0_ref[0, 0], got0_ref[0, 0])
    b = jnp.where(y // ys == bits_ref[0], own1_ref[0, 0], got1_ref[0, 0])
    out_ref[0, 0, 0, :, :half] = a
    out_ref[0, 0, 0, :, half:] = b


def last_step(parts, got, bits, pre, y_size, s_size):
    rows, half = parts[0].shape[2] // pre, parts[0].shape[3]
    along_s = pl.BlockSpec((1, 1, rows, half), lambda p, y, s, bits: (y, s % (s_size // 2), p, 0))
    along_y = pl.BlockSpec((1, 1, rows, half), lambda p, y, s, bits: (y % (y_size // 2), s, p, 0))
    return pl.pallas_call(
        last_step_kernel,
        grid_spec=pltpu.PrefetchScalarGridSpec(
            num_scalar_prefetch=1,
            grid=(pre, y_size, s_size),
            in_specs=[along_s, along_s, along_y, along_y],
            out_specs=pl.BlockSpec((1, 1, 1, rows, 2 * half), lambda p, y, s, bits: (p, y, s, 0, 0)),
        ),
        out_shape=jax.ShapeDtypeStruct((pre, y_size, s_size, rows, 2 * half), bf16),
        compiler_params=pltpu.CompilerParams(vmem_limit_bytes=48 * 1024 * 1024),
        cost_estimate=SMALL,
    )(bits, parts[0], got[0], parts[1], got[1])


def stack_turned_kernel(a_ref, b_ref, out_ref):
    r = a_ref.shape[1]
    out_ref[:r] = a_ref[...].T
    out_ref[r:] = b_ref[...].T


def stack_turned(a, b):
    rows, width = a.shape
    n = max(n for n in (1, 2, 4, 6, 8, 11) if rows % (128 * n) == 0)
    spec = pl.BlockSpec((rows // n, width), lambda i: (i, 0))
    return pl.pallas_call(
        stack_turned_kernel,
        grid=(n,),
        in_specs=[spec, spec],
        out_specs=pl.BlockSpec((2 * width, rows // n), lambda i: (0, i)),
        out_shape=jax.ShapeDtypeStruct((2 * width, rows), bf16),
        compiler_params=pltpu.CompilerParams(vmem_limit_bytes=48 * 1024 * 1024),
        cost_estimate=SMALL,
    )(a, b)


def add_split_kernel(bit_ref, a_ref, b_ref, c_ref, d_ref, send_ref, keep_ref):
    send_ref[...] = (a_ref[...].astype(f32) + b_ref[...].astype(f32)).astype(bf16)
    keep_ref[...] = (c_ref[...].astype(f32) + d_ref[...].astype(f32)).astype(bf16)


def add_split(kept, got, bit):
    rows, t = kept.shape
    half = rows // 2
    n = max(n for n in (1, 2, 3, 4) if half % (16 * n) == 0)
    rb = half // n
    away = pl.BlockSpec((rb, t), lambda i, bit: ((1 - bit[0]) * n + i, 0))
    here = pl.BlockSpec((rb, t), lambda i, bit: (bit[0] * n + i, 0))
    out = jax.ShapeDtypeStruct((half, t), bf16)
    out_spec = pl.BlockSpec((rb, t), lambda i, bit: (i, 0))
    return pl.pallas_call(
        add_split_kernel,
        grid_spec=pltpu.PrefetchScalarGridSpec(
            num_scalar_prefetch=1,
            grid=(n,),
            in_specs=[away, away, here, here],
            out_specs=[out_spec, out_spec],
        ),
        out_shape=[out, out],
        compiler_params=pltpu.CompilerParams(vmem_limit_bytes=48 * 1024 * 1024),
        cost_estimate=SMALL,
    )(bit, kept, got, kept, got)


def adam_kernel(rate, two, core_ref, w_ref, m_ref, v_ref, *refs):
    grad = refs[0][...].astype(f32)
    if two:
        other = refs[1][...].astype(f32)
        mine = core_ref[0] == 0
        grad = jnp.concatenate([jnp.where(mine, grad, other), jnp.where(mine, other, grad)], axis=1)
    new_m_ref, new_v_ref, new_w_ref = refs[-3:]
    new_m, new_v, new_w = adam_update(w_ref[...], m_ref[...], v_ref[...], grad, rate, weight_decay)
    new_m_ref[...] = new_m
    new_v_ref[...] = new_v
    new_w_ref[...] = new_w


def adam_part(state, grads, core, rate, prev, row_first, lead, unit, rb):
    w, m, v = state
    two = len(grads) == 2
    rows, width = grads[0].shape
    whole = pl.BlockSpec((rb, unit * len(grads)), lambda i, g, core: (row_first // rb + i, lead + g))
    half = pl.BlockSpec((rb, unit), lambda i, g, core: (i, g))
    out = jax.ShapeDtypeStruct(w.shape, f32)
    extra, aliases = [], {}
    if prev is not None:
        extra = list(prev)
        aliases = {4 + len(grads) + i: i for i in range(3)}
    return pl.pallas_call(
        functools.partial(adam_kernel, rate, two),
        grid_spec=pltpu.PrefetchScalarGridSpec(
            num_scalar_prefetch=1,
            grid=(rows // rb, width // unit),
            in_specs=[whole] * 3 + [half] * len(grads) + [pl.BlockSpec(memory_space=pl.ANY)] * len(extra),
            out_specs=[whole] * 3,
        ),
        out_shape=[out] * 3,
        input_output_aliases=aliases,
        compiler_params=pltpu.CompilerParams(vmem_limit_bytes=48 * 1024 * 1024),
        cost_estimate=SMALL,
    )(core, w, m, v, *grads, *extra)


def attend_kernel(kept_ref, got_ref, bias_ref, table_ref, qkv_ref, out_ref, stat_ref):
    half = ROTARY // 2
    cos, sin, pos = table_ref[0, :half], table_ref[0, half:ROTARY], table_ref[0, ROTARY:]
    parts = []
    for i in range(3):
        v = kept_ref[i, 0].astype(f32) + got_ref[i, 0].astype(f32) + bias_ref[i, 0]
        if i < 2:
            a, b = v[:half], v[half:ROTARY]
            v = jnp.concatenate([a * cos - b * sin, b * cos + a * sin, v[ROTARY:]], axis=0)
        v = v.astype(bf16)
        qkv_ref[i, 0] = v
        parts.append(v)
    q, k, v = parts
    scores = dot(k, q, FIRST) * score_scale
    scores = jnp.where(pos.T[:, :1] <= pos[:1], scores, masked_score)
    peak = jnp.max(scores, axis=0, keepdims=True)
    e = jnp.exp(scores - peak)
    total = jnp.sum(e, axis=0, keepdims=True)
    p = (e / total).astype(bf16)
    out_ref[0] = dot(v, p, PLAIN).astype(bf16)
    stat_ref[0, 0] = jnp.concatenate([peak, total], axis=0)


def attend(kept, got, bias, table):
    _, heads, hd, t = kept.shape
    seqs, _, seq = table.shape
    big = pl.BlockSpec((3, 1, hd, seq), lambda s, h: (0, h, 0, s))
    table_spec = pl.BlockSpec((1, table.shape[1], seq), lambda s, h: (s, 0, 0))
    stat = pl.BlockSpec((1, 1, 2, seq), lambda s, h: (s, h, 0, 0))
    return pl.pallas_call(
        attend_kernel,
        grid=(seqs, heads),
        in_specs=[
            big,
            big,
            pl.BlockSpec((3, 1, hd, 1), lambda s, h: (0, h, 0, 0)),
            table_spec,
        ],
        out_specs=[big, pl.BlockSpec((1, hd, seq), lambda s, h: (h, 0, s)), stat],
        out_shape=[
            jax.ShapeDtypeStruct((3, heads, hd, t), bf16),
            jax.ShapeDtypeStruct((heads, hd, t), bf16),
            jax.ShapeDtypeStruct((seqs, heads, 2, seq), f32),
        ],
        compiler_params=pltpu.CompilerParams(vmem_limit_bytes=32 * 1024 * 1024),
        cost_estimate=SMALL,
    )(kept, got, bias, table)


def attend_back_kernel(qkv_ref, dout_ref, stat_ref, table_ref, out_ref):
    half = ROTARY // 2
    cos, sin, pos = table_ref[0, :half], table_ref[0, half:ROTARY], table_ref[0, ROTARY:]
    q, k, v = qkv_ref[0, 0], qkv_ref[1, 0], qkv_ref[2, 0]
    dout = dout_ref[0]
    scores = dot(k, q, FIRST) * score_scale
    scores = jnp.where(pos.T[:, :1] <= pos[:1], scores, masked_score)
    p = jnp.exp(scores - stat_ref[0, 0, :1]) / stat_ref[0, 0, 1:]
    dp = dot(v, dout, FIRST)
    inner = jnp.sum(p * dp, axis=0, keepdims=True)
    ds = (p * (dp - inner)).astype(bf16)

    def back(x):
        a, b = x[:half], x[half:ROTARY]
        return jnp.concatenate([a * cos + b * sin, b * cos - a * sin, x[ROTARY:]], axis=0)

    out_ref[0, 0] = back(dot(k, ds, PLAIN) * score_scale).astype(bf16)
    out_ref[1, 0] = back(dot(q, ds, LAST) * score_scale).astype(bf16)
    out_ref[2, 0] = dot(dout, p.astype(bf16), LAST).astype(bf16)


def attend_back(qkv, dout, stats, table):
    _, heads, hd, t = qkv.shape
    seqs, _, seq = table.shape
    big = pl.BlockSpec((3, 1, hd, seq), lambda s, h: (0, h, 0, s))
    table_spec = pl.BlockSpec((1, table.shape[1], seq), lambda s, h: (s, 0, 0))
    stat = pl.BlockSpec((1, 1, 2, seq), lambda s, h: (s, h, 0, 0))
    return pl.pallas_call(
        attend_back_kernel,
        grid=(seqs, heads),
        in_specs=[
            big,
            pl.BlockSpec((1, hd, seq), lambda s, h: (h, 0, s)),
            stat,
            table_spec,
        ],
        out_specs=big,
        out_shape=jax.ShapeDtypeStruct((3, heads, hd, t), bf16),
        compiler_params=pltpu.CompilerParams(vmem_limit_bytes=32 * 1024 * 1024),
        cost_estimate=SMALL,
    )(qkv, dout, stats, table)


def body(
    tokens,
    cotangent,
    span_order,
    w_qkv,
    w_out,
    w_up,
    w_down,
    norm_params,
    m_qkv,
    v_qkv,
    m_out,
    v_out,
    m_up,
    v_up,
    m_down,
    v_down,
    m_norm,
    v_norm,
):
    at = Plane()
    do = Order()
    reps = RepSum(do)
    width = tokens.shape[3]
    rows = tokens.shape[1]
    S, Y, nb = at.s_size, at.y_size, at.blocks
    plane = ("ctx", "shard")
    blk = width // nb
    ffb = FF // nb
    heads = blk // HEAD_DIM
    seq = rows * at.ctx_size
    T = S * seq
    H = T // 2
    first = at.c == 0
    core = at.c.reshape(1)
    my_block = at.ctx * S + at.s
    halves = (slice(0, H), slice(H, T))
    seqs = (slice(0, S // 2), slice(S // 2, S))

    def pick(x, axis, which):
        return lax.dynamic_index_in_dim(x, which, axis, keepdims=False)

    def in_order(mine, theirs, axis):
        return jnp.stack([jnp.where(first, mine, theirs), jnp.where(first, theirs, mine)], axis=axis)

    def join(a, b):
        return jnp.concatenate([a, b], axis=0)

    def lanes(a, b):
        return jnp.concatenate([a, b], axis=1)

    x_rows = tokens.reshape(rows, width)
    order = span_order.reshape(-1).astype(f32)
    span = rows // 2

    def pack(x, order):
        xf = x.astype(f32)
        mean = jnp.mean(xf, axis=1)
        centred = xf - mean[:, None]
        inv = lax.rsqrt(jnp.mean(centred * centred, axis=1) + eps_norm)
        mine = lax.dynamic_slice_in_dim(order, 2 * at.ctx, 2)
        place = jnp.repeat(mine, span)
        terms = []
        for v in (mean, inv):
            for _ in range(3):
                t = lax.reduce_precision(v, 8, 7)
                terms.append(t)
                v = v - t
        extra = jnp.stack(terms + [place] + [jnp.zeros_like(place)] * 9).astype(bf16)
        blocks = x.T.reshape(nb, blk, rows)
        return jnp.concatenate([blocks, jnp.broadcast_to(extra[None], (nb, 16, rows))], axis=1)

    packed = do(pack, x_rows, order)
    cot_all = lax.all_gather(cotangent.reshape(rows, width), ("shard", "ctx"), axis=0, tiled=True)
    got = lax.all_to_all(packed, plane, split_axis=0, concat_axis=0, tiled=True)

    def chip_rows(w, lead, unit, count):
        mine, theirs = do(lambda w: split_columns(w, core, lead, unit, count), w)
        return mine, at.core(theirs)

    wq_parts = chip_rows(w_qkv, 0, S * blk, 3 * Y)
    norm_cols = norm_params.reshape(7, nb, blk).transpose(1, 2, 0)
    own_cols = pick(norm_cols, 0, my_block)
    other_cols = pick(norm_cols, 0, (at.ctx ^ 1) * S + at.s)
    pair_cols = join(own_cols, other_cols)
    bias = own_cols[:, 4:7].T.reshape(3, heads, HEAD_DIM, 1)
    spot = jnp.stack([at.y, at.s])

    def cut_weights(parts, pre, unit, flip):
        return do(lambda a, b: arrange(a, b, spot, pre, Y, S, unit, flip), *parts)

    wq_cut = [cut_weights(wq_parts, 3, blk, bool(k)) for k in range(2)]

    def columns(got):
        x = got.reshape(at.ctx_size, S, blk + 16, rows).transpose(2, 1, 0, 3).reshape(blk + 16, T)
        x_own, extra = x[:blk], x[blk:].astype(f32)
        mean = extra[0:1] + extra[1:2] + extra[2:3]
        inv = extra[3:4] + extra[4:5] + extra[5:6]
        return x_own, mean, inv, extra[6:7]

    x_own, mean1, inv1, place = do(columns, got)
    x_other = at.core(x_own)

    def first_norm(mine, theirs, mean, inv, cols):
        x = join(mine, theirs).astype(f32)
        return ((x - mean) * inv * cols[:, 0:1] + cols[:, 1:2]).astype(bf16)

    xn1 = do(first_norm, x_own, x_other, mean1, inv1, pair_cols)

    def send_products(cut, xs):
        got, kept = [], []
        for k in range(2):
            axis, step = at.steps(bool(k))[0]
            p = do(lambda w, x: dot(w, x, PLAIN).astype(bf16), cut[k][0], xs[k])
            got.append(at.along(p, axis, step))
        for k in range(2):
            kept.append(do(lambda w, x: dot(w, x, PLAIN).astype(bf16), cut[k][1], xs[k]))
        return list(zip(kept, got))

    def scatter_rest(pairs):
        for i in range(1, len(at.steps(False))):
            out = []
            for k in range(2):
                axis, step = at.steps(bool(k))[i]
                bit = (at.index(axis) // step) % 2
                send, kept = do(lambda a, b: add_split(a, b, bit.reshape(1)), *pairs[k])
                out.append((kept, at.along(send, axis, step)))
            pairs = out
        return pairs

    flying = send_products(wq_cut, [xn1[:, h] for h in halves])

    wo_parts = chip_rows(w_out, 0, S * blk, Y)
    wg_parts = chip_rows(w_up, 0, S * ffb, Y)
    wu_parts = chip_rows(w_up, Y, S * ffb, Y)
    wo_cut = [cut_weights(wo_parts, 1, blk, bool(k)) for k in range(2)]

    def positions(place):
        pos = place.reshape(S, seq) * span + (jnp.arange(seq) % span).astype(f32)[None, :]
        prow = pos.reshape(S, 1, seq)
        exponent = jnp.arange(ROTARY // 2, dtype=f32)
        inverse = 10000.0 ** (-2.0 * exponent / ROTARY)
        angles = prow * inverse[None, :, None]
        return jnp.concatenate([jnp.cos(angles), jnp.sin(angles), jnp.broadcast_to(prow, (S, 8, seq))], axis=1)

    table = do(positions, place)
    flying = scatter_rest(flying)

    def gather_steps(parts, pre):
        n = len(at.steps(False))
        state = {"parts": list(parts)}

        def start(i, after=None):
            if after is not None:
                state["parts"], _ = lax.optimization_barrier((state["parts"], after))
            state["got"] = []
            state["at"] = []
            for k in range(2):
                axis, step = list(reversed(at.steps(bool(k))))[i]
                state["at"].append((axis, step))
                state["got"].append(at.along(state["parts"][k], axis, step))

        def finish():
            def put(parts, got):
                out = []
                for k in range(2):
                    axis, step = state["at"][k]
                    ax = {"y": 0, "s": 1}[axis]
                    low = (at.index(axis) // step) % 2 == 0
                    a, b = parts[k], got[k]
                    out.append(jnp.concatenate([jnp.where(low, a, b), jnp.where(low, b, a)], ax))
                return out

            state["parts"] = do(put, state["parts"], state["got"])

        def result():
            ys, ss = Y // 2, S // 2
            bits = jnp.stack([at.y // ys, at.s // ss, jnp.int32(ys), jnp.int32(ss)]).astype(jnp.int32)
            return do(lambda p, g: last_step(p, g, bits, pre, Y, S), state["parts"], state["got"])

        return n, start, finish, result

    qkvs, attns, attn_got, stats = [], [], [], []
    for k in range(2):
        shape = (3, heads, HEAD_DIM, H)
        qkv, attn, stat = do(attend, flying[k][0].reshape(shape), flying[k][1].reshape(shape), bias, table[seqs[k]])
        qkvs.append(qkv)
        attns.append(attn.reshape(blk, H))
        attn_got.append(at.core(attns[k]))
        stats.append(stat)
    pairs = [do(join, attns[k], attn_got[k]) for k in range(2)]
    flying = send_products(wo_cut, pairs)
    wg_cut = cut_weights(wg_parts, 1, ffb, False)
    wu_cut = cut_weights(wu_parts, 1, ffb, True)

    def gain_products(wg, wu, cols):
        terms = []
        for v in (cols[:, 2], cols[:, 3]):
            t = lax.reduce_precision(v, 8, 7)
            terms += [t, v - t]
        terms = jnp.stack(terms).astype(bf16)
        out = []
        for mine, theirs in (wg, wu):
            p = dot(terms[:, :blk], mine, LAST) + dot(terms[:, blk:], theirs, LAST)
            out.append(jnp.stack([p[0] + p[1], p[2] + p[3]]).reshape(2, Y, S, ffb))
        return jnp.concatenate(out, axis=0)

    gains = do(gain_products, wg_parts, wu_parts, pair_cols)
    gain_steps = list(at.steps(False))

    def gain_step(gains):
        axis, step = gain_steps.pop(0)
        ax = {"y": 1, "s": 2}[axis]
        bit = (at.index(axis) // step) % 2
        send = lax.dynamic_slice_in_dim(gains, (1 - bit) * step, step, ax)
        kept = lax.dynamic_slice_in_dim(gains, bit * step, step, ax)
        return kept, at.along(send, axis, step)

    flying = scatter_rest(flying)
    def residual(x, a0, b0, a1, b1):
        a, b = lanes(a0, a1), lanes(b0, b1)
        hidden = x.astype(f32) + (a.astype(f32) + b.astype(f32))
        local_mean = jnp.mean(hidden, axis=0, keepdims=True)
        dev = hidden - local_mean
        return hidden, join(local_mean, jnp.sum(dev * dev, axis=0, keepdims=True))

    hidden, moments = do(residual, x_own, *flying[0], *flying[1])
    count = blk
    for axis, step in at.steps(False) + [("core", 1)]:
        other = at.core(moments) if axis == "core" else at.along(moments, axis, step)

        def merge(a, b):
            gap = a[0:1] - b[0:1]
            return join(0.5 * (a[0:1] + b[0:1]), a[1:2] + b[1:2] + gap * gap * (count / 2.0))

        moments = do(merge, moments, other)
        count *= 2

    def second_norm(hidden, moments, cols):
        inv2 = lax.rsqrt(moments[1:2] / width + eps_norm)
        z2 = (hidden - moments[0:1]) * inv2
        return (z2 * cols[:, 2:3] + cols[:, 3:4]).astype(bf16), z2, inv2

    gains = gain_step(gains)
    xn2_own, z2, inv2 = do(second_norm, hidden, moments, own_cols)
    xn2 = do(join, xn2_own, at.core(xn2_own))

    flying = send_products([wg_cut, wu_cut], [xn2, xn2])

    wd_own = do(cast, w_down)
    wg = do(stack_turned, *wg_parts)
    wu = do(stack_turned, *wu_parts)
    cot_all = do(lambda c: c, cot_all)
    grad_act = do(lambda w, c: mm(w, c, LAST, f32, tn=256), wd_own, cot_all)
    cot_cols = do(lambda c: lax.dynamic_slice_in_dim(c, my_block * blk, blk, 1).T, cot_all)
    wo_own = do(cast, w_out)
    wq = do(stack_turned, *wq_parts)
    gains = do(lambda a, b: a + b, *gains)
    while gain_steps:
        gains = do(lambda a, b: a + b, *gain_step(gains))
    gains = do(lambda g: g.reshape(4, ffb, 1), gains)
    flying = scatter_rest(flying)

    gate0, gate1, up0, up1, act, sums = do(gated, *flying[0], *flying[1], grad_act, gains)

    def parts_of(count, want):
        return max(n for n in range(1, want + 1) if count % (16 * n) == 0)

    def even(count, want):
        n = parts_of(count, want)
        return [(k * (count // n), count // n) for k in range(n)]

    down_rows, up_rows = even(ffb, 2), [(0, blk)]

    def push_pairs(name, g, rows):
        for k, (at_row, count) in enumerate(rows):
            reps.push((name, "theirs", k), g[blk + at_row : blk + at_row + count])
            reps.push((name, "mine", k), g[at_row : at_row + count])

    results = {"down": None, "out": None, "up": None, "qkv": None}
    states = {
        "down": (w_down, m_down, v_down),
        "out": (w_out, m_out, v_out),
        "up": (w_up, m_up, v_up),
        "qkv": (w_qkv, m_qkv, v_qkv),
    }
    rates = {"down": 0.02, "out": 0.2, "up": 0.03, "qkv": 0.03}

    def adam(name, grads, row_first, lead, unit, rb):
        results[name] = do(
            lambda s, g, prev: adam_part(s, g, core, rates[name], prev, row_first, lead, unit, rb),
            states[name],
            grads,
            results[name],
        )

    jobs = []
    for k, (at_row, count) in enumerate(down_rows):
        jobs.append(("down", [("down", k)], at_row, 0, count, 1024))
    for name, lead in (("gate", 0), ("up", Y)):
        for k, (at_row, count) in enumerate(up_rows):
            jobs.append(("up", [(name, "mine", k), (name, "theirs", k)], at_row, lead, count, S * ffb))
    received = {}

    def update(limit):
        for name in list(reps.done):
            if name[1] == "theirs" and name not in received:
                received[name] = at.core(reps.done[name])
        while jobs and limit and all(k in reps.done for k in jobs[0][1]):
            name, needs, at_row, lead, count, unit = jobs.pop(0)
            rb = max(n for n in range(8, min(count, 176) + 1, 8) if count % n == 0 and at_row % n == 0)
            adam(name, [received[k] if k[1] == "theirs" else reps.done[k] for k in needs], at_row, lead, unit, rb)
            limit -= 1

    def ticks(n):
        for _ in range(n):
            reps.tick()

    wide = 2 * FF // 8

    def quarter_heads(x):
        return [x[:, h][None, None] for h in halves]

    n, start, finish, gate_all = gather_steps([gate0[None, None], gate1[None, None]], 1)
    start(0)
    g_down = do(lambda a, c: mm(a, c, PLAIN, bf16, tn=512), act, cot_all)
    for k, (at_row, count) in enumerate(down_rows):
        reps.push(("down", k), g_down[at_row : at_row + count])
    ticks(1)

    steps2 = at.steps(False) + [("core", 1)]

    def sum_send(sums, axis, step):
        return at.core(sums) if axis == "core" else at.along(sums, axis, step)

    def sum_step(sums, axis, step):
        return do(lambda a, b: a + b, sums, sum_send(sums, axis, step))

    tiny = list(steps2)
    sums_got = sum_send(sums, *tiny.pop(0))
    for i in range(1, n):
        finish()
        sums = do(lambda a, b: a + b, sums, sums_got)
        sums_got = sum_send(sums, *tiny.pop(0))
        start(i, sums)
        ticks(1)
    n, start_up, finish_up, up_all = gather_steps([up0[None, None], up1[None, None]], 1)
    ggate_all = gate_all().reshape(Y * S * ffb, T)
    sums = do(lambda a, b: a + b, sums, sums_got)
    start_up(0, sums)
    while tiny:
        sums = sum_step(sums, *tiny.pop(0))
    g_gate = do(lambda x, g: mm(x, g, LAST, bf16, tn=wide), xn2, ggate_all)
    push_pairs("gate", g_gate, up_rows)
    finish_up()
    for i in range(1, n):
        start_up(i)
        if i == 1:
            ticks(1)
            part_gate = do(lambda w, g: mm(w, g, PLAIN, f32, tn=256), wg, ggate_all)
            out_part = do(lambda w, a: mm(w, a, FIRST, bf16, tm=512), wd_own, act)
            update(1)
        if i < n - 1:
            finish_up()
    gup_all = up_all().reshape(Y * S * ffb, T)
    part = do(lambda w, g, p: dot(w, g, PLAIN) + p, wu, gup_all, part_gate)
    part_theirs = at.core(part[blk:])

    def branch(a, b, cot, z, scale, gain, sums):
        gxn2 = a + b
        e = gxn2 * gain
        grad_hidden = cot.astype(f32) + scale * (e - sums[0:1] / width - z * (sums[1:2] / width))
        return grad_hidden.astype(bf16), grad_hidden, gxn2

    grad_branch, grad_hidden, gxn2 = do(
        branch, part[:blk], part_theirs, cot_cols, z2, inv2, own_cols[:, 2:3], sums
    )
    n, start, finish, branch_all = gather_steps(quarter_heads(grad_branch), 1)
    start(0)
    ticks(1)
    g_up = do(lambda x, g: mm(x, g, LAST, bf16, tn=wide), xn2, gup_all)
    push_pairs("up", g_up, up_rows)
    finish()
    for i in range(1, n):
        start(i)
        if i == 1:
            ticks(1)
        if i < n - 1:
            finish()
    gbr_c = branch_all()[0]
    gbr_o = at.core(gbr_c)
    gbr = do(lambda a, b: in_order(a, b, 1).reshape(width, T), gbr_c, gbr_o)
    grad_attn = do(lambda w, g: dot(w, g, PLAIN).astype(bf16), wo_own, gbr)

    gqkvs = []
    for k in range(2):
        dout = grad_attn[:, halves[k]].reshape(heads, HEAD_DIM, H)
        gqkvs.append(do(attend_back, qkvs[k], dout, stats[k], table[seqs[k]]).reshape(3, blk, H))
    n, start, finish, gqkv_done = gather_steps([g.reshape(1, 1, 3 * blk, H) for g in gqkvs], 3)
    start(0)
    attn = lanes(*attns)
    g_out = do(lambda a, g: mm(a, g, LAST, bf16, tn=512), attn, gbr)
    out_pair = PairSum(do, g_out)
    ticks(1)
    finish()
    for i in range(1, n):
        start(i)
        if i == 1:
            out_pair.step()
            update(1)
            ticks(1)
            out_pair.step()
            update(1)
        if i < n - 1:
            finish()
    gqkv = gqkv_done().reshape(3, Y * S * blk, T)
    pairs = []
    for third in (2, 1, 0):
        g = do(lambda x, g: dot(x, g, LAST).astype(bf16), xn1, gqkv[third])
        pairs.append(PairSum(do, g))
    ticks(1)
    part = do(lambda w, g: dot(w, g, PLAIN), wq, gqkv.reshape(3 * Y * S * blk, T))
    part_theirs = at.core(part[blk:])
    pairs[0].step()
    out_pair.step()
    out_sum = lax.psum_scatter(out_part, plane, scatter_dimension=0, tiled=True)

    def first_back(a, b, x, mean, inv, gain, gxn2, z2, gqkv0, gqkv1):
        gxn1 = a + b
        z1 = (x.astype(f32) - mean) * inv
        e = gxn1 * gain
        sums = join(jnp.sum(e, axis=0, keepdims=True), jnp.sum(e * z1, axis=0, keepdims=True))
        small = jnp.concatenate(
            [
                jnp.sum(gxn1 * z1, axis=1)[None],
                jnp.sum(gxn1, axis=1)[None],
                jnp.sum(gxn2 * z2, axis=1)[None],
                jnp.sum(gxn2, axis=1)[None],
                jnp.sum(gqkv0.astype(f32), axis=2) + jnp.sum(gqkv1.astype(f32), axis=2),
            ],
            axis=0,
        )
        return sums, small, gxn1, z1

    sums, small, gxn1, z1 = do(
        first_back, part[:blk], part_theirs, x_own, mean1, inv1, own_cols[:, 0:1], gxn2, z2, *gqkvs
    )
    sums = sum_step(sums, *steps2[0])
    pairs[1].step()
    for axis, step in steps2[1:]:
        sums = sum_step(sums, axis, step)
    pairs[2].step()
    input_grad = do(
        lambda h, grad, z, scale, gain, sums: h
        + scale * (grad * gain - sums[0:1] / width - z * (sums[1:2] / width)),
        grad_hidden,
        gxn1,
        z1,
        inv1,
        own_cols[:, 0:1],
        sums,
    )

    def to_rows(cols):
        split = do(lambda c: c.reshape(blk, S, at.ctx_size, rows).transpose(2, 1, 0, 3).reshape(nb, blk, rows), cols)
        got = lax.all_to_all(split, plane, split_axis=0, concat_axis=0, tiled=True)
        return do(lambda g: g.reshape(width, rows).T, got)

    def adam_qkv(third, pair):
        mine, theirs = pair.done
        adam("qkv", [mine, at.core(theirs)], 0, third * Y, S * blk, min(blk, 128))

    ticks(1)
    update(1)
    pairs[0].step()
    n_rep = lax.axis_size("rep")
    step = 1
    while step < n_rep:
        other = lax.ppermute(small, "rep", [(i, i ^ step) for i in range(n_rep)])
        small = do(lambda a, b: a + b, small, other)
        step *= 2
    for k, g in enumerate(out_pair.done):
        adam("out", [g], k * blk // 2, 0, width // 2, blk // 2)
    ticks(1)
    input_rows = to_rows(input_grad)
    pairs[1].step()
    update(1)
    while reps.busy():
        reps.tick()
        update(1)
    out_cols = do(lambda h, a: (h + a.astype(f32)).astype(bf16), hidden, out_sum)
    pairs[0].step()
    adam_qkv(2, pairs[0])
    pairs[2].step()
    pairs[1].step()
    update(len(jobs))
    block_output = to_rows(out_cols)
    adam_qkv(1, pairs[1])
    sent = do(lambda s: jnp.broadcast_to(s.reshape(1, 7, blk), (nb, 7, blk)), small)
    small_all = lax.all_to_all(sent, plane, split_axis=0, concat_axis=0, tiled=True)

    def norm_update(every, *a):
        return adam_update(*a, every.transpose(1, 0, 2).reshape(7, width), 0.3, 0.0)

    mn, vn, wn = do(norm_update, small_all, norm_params, m_norm, v_norm)
    pairs[2].step()
    adam_qkv(0, pairs[2])
    return (
        (block_output.reshape(tokens.shape), input_rows.reshape(tokens.shape))
        + tuple(results["qkv"])
        + tuple(results["out"])
        + tuple(results["up"])
        + tuple(results["down"])
        + (mn, vn, wn)
    )


def solution(mesh):
    tok = P("rep", "ctx", "shard", None)
    row = P(("ctx", "shard"), None)
    placed = (tok, tok, P("rep", "shard", None)) + (row,) * 4 + (P(),) + (row,) * 8 + (P(), P())
    return jax.shard_map(
        body,
        mesh=mesh,
        in_specs=placed,
        out_specs=(tok, tok) + (row,) * 12 + (P(),) * 3,
        check_vma=False,
    )
```

```python
import functools

import jax
import jax.numpy as jnp
from jax import lax
from jax.experimental import pallas as pl
from jax.experimental.pallas import tpu as pltpu
from jax.sharding import PartitionSpec as P

HEADS = 32
HEAD_DIM = 64
FF = 5632
ROTARY = 16
STEP = 10

eps_norm = 1e-05
masked_score = -1e30
beta_one = 0.9
beta_two = 0.999
adam_eps = 1e-08
weight_decay = 0.1
score_scale = HEAD_DIM ** (-0.5)
FIRST = (((0,), (0,)), ((), ()))
LAST = (((1,), (1,)), ((), ()))
PLAIN = (((1,), (0,)), ((), ()))
bf16 = jnp.bfloat16
f32 = jnp.float32


def dot(a, b, dims):
    return lax.dot_general(a, b, dims, preferred_element_type=f32)


def adam_update(weight, moment_one, moment_two, grad, step_rate, decay_rate):
    first_new = beta_one * moment_one + (1.0 - beta_one) * grad
    second_new = beta_two * moment_two + (1.0 - beta_two) * grad * grad
    first_hat = first_new / (1.0 - beta_one**STEP)
    second_hat = second_new / (1.0 - beta_two**STEP)
    weight_new = weight - step_rate * (
        first_hat / (jnp.sqrt(second_hat) + adam_eps) + decay_rate * weight
    )
    return (first_new, second_new, weight_new)


class Plane:
    def __init__(self):
        self.s_size = lax.axis_size("shard")
        self.ctx_size = lax.axis_size("ctx")
        self.y_size = self.ctx_size // 2
        self.ctx = lax.axis_index("ctx")
        self.s = lax.axis_index("shard")
        self.y = self.ctx // 2
        self.c = self.ctx % 2
        self.blocks = self.ctx_size * self.s_size

    def core(self, x):
        return lax.ppermute(x, "ctx", [(i, i ^ 1) for i in range(self.ctx_size)])

    def along(self, x, axis, step):
        if axis == "y":
            return lax.ppermute(x, "ctx", [(i, i ^ (2 * step)) for i in range(self.ctx_size)])
        return lax.ppermute(x, "shard", [(i, i ^ step) for i in range(self.s_size)])

    def index(self, axis):
        return self.y if axis == "y" else self.s

    def steps(self, flip):
        ys = []
        k = self.y_size // 2
        while k:
            ys.append(("y", k))
            k //= 2
        ss = []
        k = self.s_size // 2
        while k:
            ss.append(("s", k))
            k //= 2
        return ys + ss if flip else ss + ys

    def chip_exchange(self, x, take):
        out = [(self.y, self.s, take(self.y, self.s))]
        for ry in range(self.y_size):
            for rs in range(self.s_size):
                if ry or rs:
                    y, s = self.y ^ ry, self.s ^ rs
                    mask = 2 * ry * self.s_size + rs
                    perm = [(i, i ^ mask) for i in range(self.blocks)]
                    out.append((y, s, lax.ppermute(take(y, s), ("ctx", "shard"), perm)))
        return out

    def sum_all(self, x):
        for axis, step in self.steps(False):
            x = x + self.along(x, axis, step)
        return x + self.core(x)

    def scatter_sum(self, p, flip):
        axes = {"y": 1, "s": 2}
        steps = self.steps(flip)
        kept = got = None
        for n, (axis, step) in enumerate(steps):
            ax = axes[axis]
            bit = (self.index(axis) // step) % 2
            kept = lax.dynamic_slice_in_dim(p, bit * step, step, ax)
            send = lax.dynamic_slice_in_dim(p, (1 - bit) * step, step, ax)
            got = self.along(send, axis, step)
            if n + 1 < len(steps):
                p = (kept.astype(f32) + got.astype(f32)).astype(bf16)
        return kept[:, 0, 0], got[:, 0, 0]

    def gather(self, p, flip):
        axes = {"y": 1, "s": 2}
        p = p[:, None, None]
        for axis, step in reversed(self.steps(flip)):
            ax = axes[axis]
            bit = (self.index(axis) // step) % 2
            got = self.along(p, axis, step)
            first = bit == 0
            p = jnp.concatenate([jnp.where(first, p, got), jnp.where(first, got, p)], ax)
        return p


class Order:
    def __init__(self):
        self.last = None

    def __call__(self, stage, *args):
        if self.last is not None:
            args, self.last = lax.optimization_barrier((args, self.last))
        out = stage(*args)
        self.last = jax.tree.leaves(out)[0]
        return out


SMALL = pl.CostEstimate(flops=1024, bytes_accessed=1024, transcendentals=0)


def cast_kernel(w_ref, out_ref):
    out_ref[...] = w_ref[...].astype(bf16)


def cast(w):
    rows, width = w.shape
    unit = max(n for n in (128, 256, 512, 1024, 1408, 2048, 2816) if width % n == 0)
    spec = pl.BlockSpec((rows, unit), lambda i: (0, i))
    return pl.pallas_call(
        cast_kernel,
        grid=(width // unit,),
        in_specs=[spec],
        out_specs=spec,
        out_shape=jax.ShapeDtypeStruct(w.shape, bf16),
        compiler_params=pltpu.CompilerParams(vmem_limit_bytes=48 * 1024 * 1024),
        cost_estimate=SMALL,
    )(w)


class PairSum:
    def __init__(self, order, g):
        self.order = order
        self.even = lax.axis_index("rep") % 2 == 0
        half = g.shape[0] // 2

        def cut(g):
            a, b = g[:half], g[half:]
            return jnp.where(self.even, b, a), jnp.where(self.even, a, b)

        send, self.kept = order(cut, g)
        self.got = self.exchange(send, 1)
        self.stage = 0

    def exchange(self, x, step):
        return lax.ppermute(x, "rep", [(i, i ^ step) for i in range(lax.axis_size("rep"))])

    def step(self):
        def add(a, b):
            return lax.reduce_precision(a.astype(f32) + b.astype(f32), 8, 7).astype(bf16)

        def put(a, b):
            return jnp.where(self.even, a, b), jnp.where(self.even, b, a)

        if self.stage < 2:
            self.kept = self.order(add, self.kept, self.got)
            self.got = self.exchange(self.kept, 2 - self.stage)
        else:
            self.done = self.order(put, self.kept, self.got)
        self.stage += 1


def gated_kernel(ga_ref, gb_ref, ua_ref, ub_ref, grad_ref, gains_ref, g0_ref, g1_ref, u0_ref, u1_ref, act_ref, sums_ref):
    half = g0_ref.shape[1]
    gate = ga_ref[...].astype(f32) + gb_ref[...].astype(f32)
    up = ua_ref[...].astype(f32) + ub_ref[...].astype(f32)
    sig = jax.nn.sigmoid(gate)
    silu = gate * sig
    grad = grad_ref[...]
    act_ref[...] = (silu * up).astype(bf16)
    ggate = (grad * up * sig * (1.0 + gate * (1.0 - sig))).astype(bf16)
    gup = (grad * silu).astype(bf16)
    g0_ref[...] = ggate[:, :half]
    g1_ref[...] = ggate[:, half:]
    u0_ref[...] = gup[:, :half]
    u1_ref[...] = gup[:, half:]
    a, b = ggate.astype(f32), gup.astype(f32)
    e = jnp.sum(a * gains_ref[:, 0:1] + b * gains_ref[:, 2:3], axis=0, keepdims=True)
    ez = jnp.sum(a * (gate - gains_ref[:, 1:2]) + b * (up - gains_ref[:, 3:4]), axis=0, keepdims=True)
    both = jnp.concatenate([e, ez], axis=0)

    @pl.when(pl.program_id(0) == 0)
    def _():
        sums_ref[...] = both

    @pl.when(pl.program_id(0) > 0)
    def _():
        sums_ref[...] += both


def gated(ga, gb, ua, ub, grad_act, gains):
    rows, t = grad_act.shape
    n = max(n for n in (1, 2, 4) if rows % (16 * n) == 0)
    whole = pl.BlockSpec((rows // n, t), lambda i: (i, 0))
    half = pl.BlockSpec((rows // n, t // 2), lambda i: (i, 0))
    out_half = jax.ShapeDtypeStruct((rows, t // 2), bf16)
    return pl.pallas_call(
        gated_kernel,
        grid=(n,),
        in_specs=[whole] * 5 + [pl.BlockSpec((rows // n, 4), lambda i: (i, 0))],
        out_specs=[half] * 4 + [whole, pl.BlockSpec((2, t), lambda i: (0, 0))],
        out_shape=[out_half] * 4 + [jax.ShapeDtypeStruct((rows, t), bf16), jax.ShapeDtypeStruct((2, t), f32)],
        compiler_params=pltpu.CompilerParams(vmem_limit_bytes=56 * 1024 * 1024),
        cost_estimate=SMALL,
    )(ga, gb, ua, ub, grad_act, gains)


def split_kernel(core_ref, w_ref, mine_ref, theirs_ref):
    unit = mine_ref.shape[0]
    first = core_ref[0] == 0
    a, b = w_ref[:, :unit], w_ref[:, unit:]
    mine_ref[...] = jnp.where(first, a, b).T.astype(bf16)
    theirs_ref[...] = jnp.where(first, b, a).T.astype(bf16)


def split_columns(w, core, lead, unit, count):
    rows = w.shape[0]
    half = pl.BlockSpec((unit, rows), lambda j, core: (j, 0))
    out = jax.ShapeDtypeStruct((count * unit, rows), bf16)
    return pl.pallas_call(
        split_kernel,
        grid_spec=pltpu.PrefetchScalarGridSpec(
            num_scalar_prefetch=1,
            grid=(count,),
            in_specs=[pl.BlockSpec((rows, 2 * unit), lambda j, core: (0, lead + j))],
            out_specs=[half, half],
        ),
        out_shape=[out, out],
        compiler_params=pltpu.CompilerParams(vmem_limit_bytes=32 * 1024 * 1024),
        cost_estimate=SMALL,
    )(core, w)


def arrange_kernel(at_ref, a_ref, b_ref, c_ref, d_ref, send_ref, keep_ref):
    send_ref[...] = jnp.concatenate([a_ref[...], b_ref[...]], axis=1)
    keep_ref[...] = jnp.concatenate([c_ref[...], d_ref[...]], axis=1)


def arrange(mine, got, place, pre, y_size, s_size, unit, flip):
    r = mine.shape[1]
    half = pre * y_size * s_size // 2

    def block(i, place, keep):
        p = i % pre
        i = i // pre
        if flip:
            s, y = i % s_size, i // s_size
            bit = place[0] // (y_size // 2)
            bit = bit if keep else 1 - bit
            y = y + bit * (y_size // 2)
        else:
            y, s = i % y_size, i // y_size
            bit = place[1] // (s_size // 2)
            bit = bit if keep else 1 - bit
            s = s + bit * (s_size // 2)
        return ((p * y_size + y) * s_size + s, 0)

    def spec(keep):
        return pl.BlockSpec((unit, r), lambda i, place: block(i, place, keep))

    out = jax.ShapeDtypeStruct((half * unit, 2 * r), bf16)
    out_spec = pl.BlockSpec((unit, 2 * r), lambda i, place: (i, 0))
    return pl.pallas_call(
        arrange_kernel,
        grid_spec=pltpu.PrefetchScalarGridSpec(
            num_scalar_prefetch=1,
            grid=(half,),
            in_specs=[spec(False), spec(False), spec(True), spec(True)],
            out_specs=[out_spec, out_spec],
        ),
        out_shape=[out, out],
        compiler_params=pltpu.CompilerParams(vmem_limit_bytes=32 * 1024 * 1024),
        cost_estimate=SMALL,
    )(place, mine, got, mine, got)


def product_kernel(dims, a_ref, b_ref, *refs):
    p = dot(a_ref[...], b_ref[...], dims)
    if len(refs) == 2:
        p = p + refs[0][...]
    refs[-1][...] = p.astype(refs[-1].dtype)


def mm(a, b, dims, dtype, tm=None, tn=None, add=None):
    (ca,), (cb,) = dims[0]
    m, k, n = a.shape[1 - ca], a.shape[ca], b.shape[1 - cb]
    tm, tn = tm or m, tn or n
    a_block = [0, 0]
    a_block[ca], a_block[1 - ca] = k, tm
    b_block = [0, 0]
    b_block[cb], b_block[1 - cb] = k, tn
    out = pl.BlockSpec((tm, tn), lambda i, j: (i, j))
    return pl.pallas_call(
        functools.partial(product_kernel, dims),
        grid=(m // tm, n // tn),
        in_specs=[
            pl.BlockSpec(tuple(a_block), (lambda i, j: (0, i)) if ca == 0 else (lambda i, j: (i, 0))),
            pl.BlockSpec(tuple(b_block), (lambda i, j: (0, j)) if cb == 0 else (lambda i, j: (j, 0))),
        ]
        + ([] if add is None else [out]),
        out_specs=out,
        out_shape=jax.ShapeDtypeStruct((m, n), dtype),
        compiler_params=pltpu.CompilerParams(vmem_limit_bytes=48 * 1024 * 1024),
        cost_estimate=SMALL,
    )(*((a, b) if add is None else (a, b, add)))


def stack_turned_kernel(a_ref, b_ref, out_ref):
    r = a_ref.shape[1]
    out_ref[:r] = a_ref[...].T
    out_ref[r:] = b_ref[...].T


def stack_turned(a, b):
    rows, width = a.shape
    n = max(n for n in (1, 2, 4, 6, 8, 11) if rows % (128 * n) == 0)
    spec = pl.BlockSpec((rows // n, width), lambda i: (i, 0))
    return pl.pallas_call(
        stack_turned_kernel,
        grid=(n,),
        in_specs=[spec, spec],
        out_specs=pl.BlockSpec((2 * width, rows // n), lambda i: (0, i)),
        out_shape=jax.ShapeDtypeStruct((2 * width, rows), bf16),
        compiler_params=pltpu.CompilerParams(vmem_limit_bytes=48 * 1024 * 1024),
        cost_estimate=SMALL,
    )(a, b)


def add_split_kernel(bit_ref, a_ref, b_ref, c_ref, d_ref, send_ref, keep_ref):
    send_ref[...] = (a_ref[...].astype(f32) + b_ref[...].astype(f32)).astype(bf16)
    keep_ref[...] = (c_ref[...].astype(f32) + d_ref[...].astype(f32)).astype(bf16)


def add_split(kept, got, bit):
    rows, t = kept.shape
    half = rows // 2
    n = max(n for n in (1, 2, 3, 4) if half % (16 * n) == 0)
    rb = half // n
    away = pl.BlockSpec((rb, t), lambda i, bit: ((1 - bit[0]) * n + i, 0))
    here = pl.BlockSpec((rb, t), lambda i, bit: (bit[0] * n + i, 0))
    out = jax.ShapeDtypeStruct((half, t), bf16)
    out_spec = pl.BlockSpec((rb, t), lambda i, bit: (i, 0))
    return pl.pallas_call(
        add_split_kernel,
        grid_spec=pltpu.PrefetchScalarGridSpec(
            num_scalar_prefetch=1,
            grid=(n,),
            in_specs=[away, away, here, here],
            out_specs=[out_spec, out_spec],
        ),
        out_shape=[out, out],
        compiler_params=pltpu.CompilerParams(vmem_limit_bytes=48 * 1024 * 1024),
        cost_estimate=SMALL,
    )(bit, kept, got, kept, got)


def adam_kernel(rate, two, core_ref, w_ref, m_ref, v_ref, *refs):
    grad = refs[0][...].astype(f32)
    if two:
        other = refs[1][...].astype(f32)
        mine = core_ref[0] == 0
        grad = jnp.concatenate([jnp.where(mine, grad, other), jnp.where(mine, other, grad)], axis=1)
    new_m_ref, new_v_ref, new_w_ref = refs[-3:]
    new_m, new_v, new_w = adam_update(w_ref[...], m_ref[...], v_ref[...], grad, rate, weight_decay)
    new_m_ref[...] = new_m
    new_v_ref[...] = new_v
    new_w_ref[...] = new_w


def adam_part(state, grads, core, rate, prev, row_first, lead, unit, rb):
    w, m, v = state
    two = len(grads) == 2
    rows, width = grads[0].shape
    whole = pl.BlockSpec((rb, unit * len(grads)), lambda i, g, core: (row_first // rb + i, lead + g))
    half = pl.BlockSpec((rb, unit), lambda i, g, core: (i, g))
    out = jax.ShapeDtypeStruct(w.shape, f32)
    extra, aliases = [], {}
    if prev is not None:
        extra = list(prev)
        aliases = {4 + len(grads) + i: i for i in range(3)}
    return pl.pallas_call(
        functools.partial(adam_kernel, rate, two),
        grid_spec=pltpu.PrefetchScalarGridSpec(
            num_scalar_prefetch=1,
            grid=(rows // rb, width // unit),
            in_specs=[whole] * 3 + [half] * len(grads) + [pl.BlockSpec(memory_space=pl.ANY)] * len(extra),
            out_specs=[whole] * 3,
        ),
        out_shape=[out] * 3,
        input_output_aliases=aliases,
        compiler_params=pltpu.CompilerParams(vmem_limit_bytes=48 * 1024 * 1024),
        cost_estimate=SMALL,
    )(core, w, m, v, *grads, *extra)


def attend_kernel(kept_ref, got_ref, bias_ref, table_ref, qkv_ref, out_ref, stat_ref):
    half = ROTARY // 2
    cos, sin, pos = table_ref[0, :half], table_ref[0, half:ROTARY], table_ref[0, ROTARY:]
    parts = []
    for i in range(3):
        v = kept_ref[i, 0].astype(f32) + got_ref[i, 0].astype(f32) + bias_ref[i, 0]
        if i < 2:
            a, b = v[:half], v[half:ROTARY]
            v = jnp.concatenate([a * cos - b * sin, b * cos + a * sin, v[ROTARY:]], axis=0)
        v = v.astype(bf16)
        qkv_ref[i, 0] = v
        parts.append(v)
    q, k, v = parts
    scores = dot(k, q, FIRST) * score_scale
    scores = jnp.where(pos.T[:, :1] <= pos[:1], scores, masked_score)
    peak = jnp.max(scores, axis=0, keepdims=True)
    e = jnp.exp(scores - peak)
    total = jnp.sum(e, axis=0, keepdims=True)
    p = (e / total).astype(bf16)
    out_ref[0] = dot(v, p, PLAIN).astype(bf16)
    stat_ref[0, 0] = jnp.concatenate([peak, total], axis=0)


def attend(kept, got, bias, table):
    _, heads, hd, t = kept.shape
    seqs, _, seq = table.shape
    big = pl.BlockSpec((3, 1, hd, seq), lambda s, h: (0, h, 0, s))
    table_spec = pl.BlockSpec((1, table.shape[1], seq), lambda s, h: (s, 0, 0))
    stat = pl.BlockSpec((1, 1, 2, seq), lambda s, h: (s, h, 0, 0))
    return pl.pallas_call(
        attend_kernel,
        grid=(seqs, heads),
        in_specs=[
            big,
            big,
            pl.BlockSpec((3, 1, hd, 1), lambda s, h: (0, h, 0, 0)),
            table_spec,
        ],
        out_specs=[big, pl.BlockSpec((1, hd, seq), lambda s, h: (h, 0, s)), stat],
        out_shape=[
            jax.ShapeDtypeStruct((3, heads, hd, t), bf16),
            jax.ShapeDtypeStruct((heads, hd, t), bf16),
            jax.ShapeDtypeStruct((seqs, heads, 2, seq), f32),
        ],
        compiler_params=pltpu.CompilerParams(vmem_limit_bytes=32 * 1024 * 1024),
        cost_estimate=SMALL,
    )(kept, got, bias, table)


def attend_back_kernel(qkv_ref, dout_ref, stat_ref, table_ref, out_ref):
    half = ROTARY // 2
    cos, sin, pos = table_ref[0, :half], table_ref[0, half:ROTARY], table_ref[0, ROTARY:]
    q, k, v = qkv_ref[0, 0], qkv_ref[1, 0], qkv_ref[2, 0]
    dout = dout_ref[0]
    scores = dot(k, q, FIRST) * score_scale
    scores = jnp.where(pos.T[:, :1] <= pos[:1], scores, masked_score)
    p = jnp.exp(scores - stat_ref[0, 0, :1]) / stat_ref[0, 0, 1:]
    dp = dot(v, dout, FIRST)
    inner = jnp.sum(p * dp, axis=0, keepdims=True)
    ds = (p * (dp - inner)).astype(bf16)

    def back(x):
        a, b = x[:half], x[half:ROTARY]
        return jnp.concatenate([a * cos + b * sin, b * cos - a * sin, x[ROTARY:]], axis=0)

    out_ref[0, 0] = back(dot(k, ds, PLAIN) * score_scale).astype(bf16)
    out_ref[1, 0] = back(dot(q, ds, LAST) * score_scale).astype(bf16)
    out_ref[2, 0] = dot(dout, p.astype(bf16), LAST).astype(bf16)


def attend_back(qkv, dout, stats, table):
    _, heads, hd, t = qkv.shape
    seqs, _, seq = table.shape
    big = pl.BlockSpec((3, 1, hd, seq), lambda s, h: (0, h, 0, s))
    table_spec = pl.BlockSpec((1, table.shape[1], seq), lambda s, h: (s, 0, 0))
    stat = pl.BlockSpec((1, 1, 2, seq), lambda s, h: (s, h, 0, 0))
    return pl.pallas_call(
        attend_back_kernel,
        grid=(seqs, heads),
        in_specs=[
            big,
            pl.BlockSpec((1, hd, seq), lambda s, h: (h, 0, s)),
            stat,
            table_spec,
        ],
        out_specs=big,
        out_shape=jax.ShapeDtypeStruct((3, heads, hd, t), bf16),
        compiler_params=pltpu.CompilerParams(vmem_limit_bytes=32 * 1024 * 1024),
        cost_estimate=SMALL,
    )(qkv, dout, stats, table)


def body(
    tokens,
    cotangent,
    span_order,
    w_qkv,
    w_out,
    w_up,
    w_down,
    norm_params,
    m_qkv,
    v_qkv,
    m_out,
    v_out,
    m_up,
    v_up,
    m_down,
    v_down,
    m_norm,
    v_norm,
):
    at = Plane()
    do = Order()
    width = tokens.shape[3]
    rows = tokens.shape[1]
    S, Y, nb = at.s_size, at.y_size, at.blocks
    plane = ("ctx", "shard")
    blk = width // nb
    ffb = FF // nb
    heads = blk // HEAD_DIM
    seq = rows * at.ctx_size
    T = S * seq
    H = T // 2
    first = at.c == 0
    core = at.c.reshape(1)
    my_block = at.ctx * S + at.s
    halves = (slice(0, H), slice(H, T))
    seqs = (slice(0, S // 2), slice(S // 2, S))

    def pick(x, axis, which):
        return lax.dynamic_index_in_dim(x, which, axis, keepdims=False)

    def in_order(mine, theirs, axis):
        return jnp.stack([jnp.where(first, mine, theirs), jnp.where(first, theirs, mine)], axis=axis)

    def join(a, b):
        return jnp.concatenate([a, b], axis=0)

    def lanes(a, b):
        return jnp.concatenate([a, b], axis=1)

    x_rows = tokens.reshape(rows, width)
    order = span_order.reshape(-1).astype(f32)
    span = rows // 2

    def pack(x, order):
        xf = x.astype(f32)
        mean = jnp.mean(xf, axis=1)
        centred = xf - mean[:, None]
        inv = lax.rsqrt(jnp.mean(centred * centred, axis=1) + eps_norm)
        mine = lax.dynamic_slice_in_dim(order, 2 * at.ctx, 2)
        place = jnp.repeat(mine, span)
        terms = []
        for v in (mean, inv):
            for _ in range(3):
                t = lax.reduce_precision(v, 8, 7)
                terms.append(t)
                v = v - t
        extra = jnp.stack(terms + [place] + [jnp.zeros_like(place)] * 9).astype(bf16)
        blocks = x.T.reshape(nb, blk, rows)
        return jnp.concatenate([blocks, jnp.broadcast_to(extra[None], (nb, 16, rows))], axis=1)

    packed = do(pack, x_rows, order)
    cot_all = lax.all_gather(do(cast, cotangent.reshape(rows, width)), ("shard", "ctx"), axis=0, tiled=True)
    got = lax.all_to_all(packed, plane, split_axis=0, concat_axis=0, tiled=True)

    def chip_rows(w, lead, unit, count):
        mine, theirs = do(lambda w: split_columns(w, core, lead, unit, count), w)
        return mine, at.core(theirs)

    wq_parts = chip_rows(w_qkv, 0, S * blk, 3 * Y)
    norm_cols = norm_params.reshape(7, nb, blk).transpose(1, 2, 0)
    own_cols = pick(norm_cols, 0, my_block)
    other_cols = pick(norm_cols, 0, (at.ctx ^ 1) * S + at.s)
    pair_cols = join(own_cols, other_cols)
    bias = own_cols[:, 4:7].T.reshape(3, heads, HEAD_DIM, 1)
    spot = jnp.stack([at.y, at.s])

    def cut_weights(parts, pre, unit, flip):
        return do(lambda a, b: arrange(a, b, spot, pre, Y, S, unit, flip), *parts)

    wq_cut = [cut_weights(wq_parts, 3, blk, bool(k)) for k in range(2)]

    def columns(got):
        x = got.reshape(at.ctx_size, S, blk + 16, rows).transpose(2, 1, 0, 3).reshape(blk + 16, T)
        x_own, extra = x[:blk], x[blk:].astype(f32)
        mean = extra[0:1] + extra[1:2] + extra[2:3]
        inv = extra[3:4] + extra[4:5] + extra[5:6]
        return x_own, mean, inv, extra[6:7]

    x_own, mean1, inv1, place = do(columns, got)
    x_other = at.core(x_own)

    def first_norm(mine, theirs, mean, inv, cols):
        x = join(mine, theirs).astype(f32)
        return ((x - mean) * inv * cols[:, 0:1] + cols[:, 1:2]).astype(bf16)

    xn1 = do(first_norm, x_own, x_other, mean1, inv1, pair_cols)

    def send_products(cut, xs):
        got, kept = [], []
        for k in range(2):
            axis, step = at.steps(bool(k))[0]
            p = do(lambda w, x: dot(w, x, PLAIN).astype(bf16), cut[k][0], xs[k])
            got.append(at.along(p, axis, step))
        for k in range(2):
            kept.append(do(lambda w, x: dot(w, x, PLAIN).astype(bf16), cut[k][1], xs[k]))
        return list(zip(kept, got))

    def scatter_rest(pairs):
        for i in range(1, len(at.steps(False))):
            out = []
            for k in range(2):
                axis, step = at.steps(bool(k))[i]
                bit = (at.index(axis) // step) % 2
                send, kept = do(lambda a, b: add_split(a, b, bit.reshape(1)), *pairs[k])
                out.append((kept, at.along(send, axis, step)))
            pairs = out
        return pairs

    flying = send_products(wq_cut, [xn1[:, h] for h in halves])

    wo_parts = chip_rows(w_out, 0, S * blk, Y)
    wg_parts = chip_rows(w_up, 0, S * ffb, Y)
    wu_parts = chip_rows(w_up, Y, S * ffb, Y)
    wo_cut = [cut_weights(wo_parts, 1, blk, bool(k)) for k in range(2)]

    def positions(place):
        pos = place.reshape(S, seq) * span + (jnp.arange(seq) % span).astype(f32)[None, :]
        prow = pos.reshape(S, 1, seq)
        exponent = jnp.arange(ROTARY // 2, dtype=f32)
        inverse = 10000.0 ** (-2.0 * exponent / ROTARY)
        angles = prow * inverse[None, :, None]
        return jnp.concatenate([jnp.cos(angles), jnp.sin(angles), jnp.broadcast_to(prow, (S, 8, seq))], axis=1)

    table = do(positions, place)
    flying = scatter_rest(flying)

    def gather_steps(parts, pre):
        n = len(at.steps(False))
        state = {"parts": list(parts)}

        def start(i, after=None):
            if after is not None:
                state["parts"], _ = lax.optimization_barrier((state["parts"], after))
            state["got"] = []
            state["at"] = []
            for k in range(2):
                axis, step = list(reversed(at.steps(bool(k))))[i]
                state["at"].append((axis, step))
                state["got"].append(at.along(state["parts"][k], axis, step))

        def finish():
            def put(parts, got):
                out = []
                for k in range(2):
                    axis, step = state["at"][k]
                    ax = {"y": 0, "s": 1}[axis]
                    low = (at.index(axis) // step) % 2 == 0
                    a, b = parts[k], got[k]
                    out.append(jnp.concatenate([jnp.where(low, a, b), jnp.where(low, b, a)], ax))
                return out

            state["parts"] = do(put, state["parts"], state["got"])

        def result():
            finish()
            return do(
                lambda a, b: jnp.concatenate([a, b], axis=3)
                .reshape(Y, S, pre, -1, T)
                .transpose(2, 0, 1, 3, 4),
                *state["parts"],
            )

        return n, start, finish, result

    qkvs, attns, attn_got, stats = [], [], [], []
    for k in range(2):
        shape = (3, heads, HEAD_DIM, H)
        qkv, attn, stat = do(attend, flying[k][0].reshape(shape), flying[k][1].reshape(shape), bias, table[seqs[k]])
        qkvs.append(qkv)
        attns.append(attn.reshape(blk, H))
        attn_got.append(at.core(attns[k]))
        stats.append(stat)
    pairs = [do(join, attns[k], attn_got[k]) for k in range(2)]
    flying = send_products(wo_cut, pairs)
    wg_cut = cut_weights(wg_parts, 1, ffb, False)
    wu_cut = cut_weights(wu_parts, 1, ffb, True)

    def gain_products(wg, wu, cols):
        terms = []
        for v in (cols[:, 2], cols[:, 3]):
            t = lax.reduce_precision(v, 8, 7)
            terms += [t, v - t]
        terms = jnp.stack(terms).astype(bf16)
        out = []
        for mine, theirs in (wg, wu):
            p = dot(terms[:, :blk], mine, LAST) + dot(terms[:, blk:], theirs, LAST)
            out.append(jnp.stack([p[0] + p[1], p[2] + p[3]]).reshape(2, Y, S, ffb))
        return jnp.concatenate(out, axis=0)

    gains = do(gain_products, wg_parts, wu_parts, pair_cols)
    gain_steps = list(at.steps(False))

    def gain_step(gains):
        axis, step = gain_steps.pop(0)
        ax = {"y": 1, "s": 2}[axis]
        bit = (at.index(axis) // step) % 2
        send = lax.dynamic_slice_in_dim(gains, (1 - bit) * step, step, ax)
        kept = lax.dynamic_slice_in_dim(gains, bit * step, step, ax)
        return kept, at.along(send, axis, step)

    flying = scatter_rest(flying)
    def residual(x, a0, b0, a1, b1):
        a, b = lanes(a0, a1), lanes(b0, b1)
        hidden = x.astype(f32) + (a.astype(f32) + b.astype(f32))
        local_mean = jnp.mean(hidden, axis=0, keepdims=True)
        dev = hidden - local_mean
        return hidden, join(local_mean, jnp.sum(dev * dev, axis=0, keepdims=True))

    hidden, moments = do(residual, x_own, *flying[0], *flying[1])
    count = blk
    for axis, step in at.steps(False) + [("core", 1)]:
        other = at.core(moments) if axis == "core" else at.along(moments, axis, step)

        def merge(a, b):
            gap = a[0:1] - b[0:1]
            return join(0.5 * (a[0:1] + b[0:1]), a[1:2] + b[1:2] + gap * gap * (count / 2.0))

        moments = do(merge, moments, other)
        count *= 2

    def second_norm(hidden, moments, cols):
        inv2 = lax.rsqrt(moments[1:2] / width + eps_norm)
        z2 = (hidden - moments[0:1]) * inv2
        return (z2 * cols[:, 2:3] + cols[:, 3:4]).astype(bf16), z2, inv2

    gains = gain_step(gains)
    xn2_own, z2, inv2 = do(second_norm, hidden, moments, own_cols)
    xn2 = do(join, xn2_own, at.core(xn2_own))

    flying = send_products([wg_cut, wu_cut], [xn2, xn2])

    wd_own = do(cast, w_down)
    wg = do(stack_turned, *wg_parts)
    wu = do(stack_turned, *wu_parts)
    grad_act = do(lambda w, c: mm(w, c, LAST, f32, tn=256), wd_own, cot_all)
    cot_cols = do(lambda c: lax.dynamic_slice_in_dim(c, my_block * blk, blk, 1).T, cot_all)
    wo_own = do(cast, w_out)
    wq = do(stack_turned, *wq_parts)
    gains = do(lambda a, b: a + b, *gains)
    while gain_steps:
        gains = do(lambda a, b: a + b, *gain_step(gains))
    gains = do(lambda g: g.reshape(4, ffb).T, gains)
    flying = scatter_rest(flying)

    gate0, gate1, up0, up1, act, sums = do(gated, *flying[0], *flying[1], grad_act, gains)

    def parts_of(count, want):
        return max(n for n in range(1, want + 1) if count % (16 * n) == 0)

    def even(count, want):
        n = parts_of(count, want)
        return [(k * (count // n), count // n) for k in range(n)]

    results = {"down": None, "out": None, "up": None, "qkv": None}
    states = {
        "down": (w_down, m_down, v_down),
        "out": (w_out, m_out, v_out),
        "up": (w_up, m_up, v_up),
        "qkv": (w_qkv, m_qkv, v_qkv),
    }
    rates = {"down": 0.02, "out": 0.2, "up": 0.03, "qkv": 0.03}

    def adam(name, grads, row_first, lead, unit, rb):
        results[name] = do(
            lambda s, g, prev: adam_part(s, g, core, rates[name], prev, row_first, lead, unit, rb),
            states[name],
            grads,
            results[name],
        )

    def adam_own(name, pair):
        half = pair.done[0].shape[0]
        rb = max(n for n in range(8, min(half, 176) + 1, 8) if half % n == 0)
        for k, g in enumerate(pair.done):
            adam(name, [g], k * half, 0, width // 2, rb)

    def adam_both(name, pair, lead, unit):
        mine, theirs = pair.done
        adam(name, [mine, at.core(theirs)], 0, lead, unit, min(blk, 128))

    wide = 2 * FF // 8

    def quarter_heads(x):
        return [x[:, h][None, None] for h in halves]

    n, start, finish, gate_all = gather_steps([gate0[None, None], gate1[None, None]], 1)
    start(0)
    g_down = do(lambda a, c: mm(a, c, PLAIN, bf16, tn=512), act, cot_all)
    p_down = PairSum(do, g_down)

    steps2 = at.steps(False) + [("core", 1)]

    def sum_send(sums, axis, step):
        return at.core(sums) if axis == "core" else at.along(sums, axis, step)

    def sum_step(sums, axis, step):
        return do(lambda a, b: a + b, sums, sum_send(sums, axis, step))

    tiny = list(steps2)
    sums_got = sum_send(sums, *tiny.pop(0))
    for i in range(1, n):
        finish()
        sums = do(lambda a, b: a + b, sums, sums_got)
        sums_got = sum_send(sums, *tiny.pop(0))
        start(i, sums)
    n, start_up, finish_up, up_all = gather_steps([up0[None, None], up1[None, None]], 1)
    ggate_all = gate_all().reshape(Y * S * ffb, T)
    sums = do(lambda a, b: a + b, sums, sums_got)
    start_up(0, sums)
    while tiny:
        sums = sum_step(sums, *tiny.pop(0))
    g_gate = do(lambda x, g: mm(x, g, LAST, bf16, tn=wide), xn2, ggate_all)
    p_down.step()
    p_gate = PairSum(do, g_gate)
    finish_up()
    for i in range(1, n):
        start_up(i)
        if i == 1:
            part_gate = do(lambda w, g: mm(w, g, PLAIN, f32, tn=256), wg, ggate_all)
            out_part = do(lambda w, a: mm(w, a, FIRST, bf16, tm=512), wd_own, act)
        if i < n - 1:
            finish_up()
    gup_all = up_all().reshape(Y * S * ffb, T)
    part = do(lambda w, g, p: dot(w, g, PLAIN) + p, wu, gup_all, part_gate)
    part_theirs = at.core(part[blk:])

    def branch(a, b, cot, z, scale, gain, sums):
        gxn2 = a + b
        e = gxn2 * gain
        grad_hidden = cot.astype(f32) + scale * (e - sums[0:1] / width - z * (sums[1:2] / width))
        return grad_hidden.astype(bf16), grad_hidden, gxn2

    grad_branch, grad_hidden, gxn2 = do(
        branch, part[:blk], part_theirs, cot_cols, z2, inv2, own_cols[:, 2:3], sums
    )
    n, start, finish, branch_all = gather_steps(quarter_heads(grad_branch), 1)
    start(0)
    p_down.step()
    p_gate.step()
    g_up = do(lambda x, g: mm(x, g, LAST, bf16, tn=wide), xn2, gup_all)
    p_up = PairSum(do, g_up)
    finish()
    for i in range(1, n):
        start(i)
        if i < n - 1:
            finish()
    gbr_c = branch_all()[0]
    gbr_o = at.core(gbr_c)
    gbr = do(lambda a, b: in_order(a, b, 1).reshape(width, T), gbr_c, gbr_o)
    grad_attn = do(lambda w, g: dot(w, g, PLAIN).astype(bf16), wo_own, gbr)

    gqkvs = []
    for k in range(2):
        dout = grad_attn[:, halves[k]].reshape(heads, HEAD_DIM, H)
        gqkvs.append(do(attend_back, qkvs[k], dout, stats[k], table[seqs[k]]).reshape(3, blk, H))
    n, start, finish, gqkv_done = gather_steps([g.reshape(1, 1, 3 * blk, H) for g in gqkvs], 3)
    start(0)
    attn = lanes(*attns)
    g_out = do(lambda a, g: mm(a, g, LAST, bf16, tn=512), attn, gbr)
    p_out = PairSum(do, g_out)
    p_down.step()
    p_up.step()
    finish()
    for i in range(1, n):
        start(i)
        if i == 1:
            p_gate.step()
            p_out.step()
            adam_own("down", p_down)
        if i < n - 1:
            finish()
    gqkv = gqkv_done().reshape(3, Y * S * blk, T)
    p_qkv = {}
    for third in (2, 1, 0):
        g = do(lambda x, g: dot(x, g, LAST).astype(bf16), xn1, gqkv[third])
        p_qkv[third] = PairSum(do, g)
    part = do(lambda w, g: dot(w, g, PLAIN), wq, gqkv.reshape(3 * Y * S * blk, T))
    part_theirs = at.core(part[blk:])
    out_sum = lax.psum_scatter(out_part, plane, scatter_dimension=0, tiled=True)
    p_gate.step()
    p_up.step()
    p_qkv[2].step()

    def first_back(a, b, x, mean, inv, gain, gxn2, z2, gqkv0, gqkv1):
        gxn1 = a + b
        z1 = (x.astype(f32) - mean) * inv
        e = gxn1 * gain
        sums = join(jnp.sum(e, axis=0, keepdims=True), jnp.sum(e * z1, axis=0, keepdims=True))
        small = jnp.concatenate(
            [
                jnp.sum(gxn1 * z1, axis=1)[None],
                jnp.sum(gxn1, axis=1)[None],
                jnp.sum(gxn2 * z2, axis=1)[None],
                jnp.sum(gxn2, axis=1)[None],
                jnp.sum(gqkv0.astype(f32), axis=2) + jnp.sum(gqkv1.astype(f32), axis=2),
            ],
            axis=0,
        )
        return sums, small, gxn1, z1

    sums, small, gxn1, z1 = do(
        first_back, part[:blk], part_theirs, x_own, mean1, inv1, own_cols[:, 0:1], gxn2, z2, *gqkvs
    )
    adam_both("up", p_gate, 0, S * ffb)
    p_out.step()
    p_qkv[1].step()
    for axis, step in steps2:
        sums = sum_step(sums, axis, step)
    input_grad = do(
        lambda h, grad, z, scale, gain, sums: h
        + scale * (grad * gain - sums[0:1] / width - z * (sums[1:2] / width)),
        grad_hidden,
        gxn1,
        z1,
        inv1,
        own_cols[:, 0:1],
        sums,
    )

    def to_rows(cols):
        split = do(lambda c: c.reshape(blk, S, at.ctx_size, rows).transpose(2, 1, 0, 3).reshape(nb, blk, rows), cols)
        got = lax.all_to_all(split, plane, split_axis=0, concat_axis=0, tiled=True)
        return do(lambda g: g.reshape(width, rows).T, got)

    p_up.step()
    p_qkv[2].step()
    p_qkv[0].step()
    input_rows = to_rows(input_grad)
    p_out.step()
    adam_both("up", p_up, Y, S * ffb)
    p_qkv[1].step()
    p_qkv[2].step()
    adam_own("out", p_out)
    adam_both("qkv", p_qkv[2], 2 * Y, S * blk)
    p_qkv[0].step()
    p_qkv[1].step()
    n_rep = lax.axis_size("rep")
    step = 1
    while step < n_rep:
        other = lax.ppermute(small, "rep", [(i, i ^ step) for i in range(n_rep)])
        small = do(lambda a, b: a + b, small, other)
        step *= 2
    out_cols = do(lambda h, a: (h + a.astype(f32)).astype(bf16), hidden, out_sum)
    adam_both("qkv", p_qkv[1], Y, S * blk)
    block_output = to_rows(out_cols)
    sent = do(lambda s: jnp.broadcast_to(s.reshape(1, 7, blk), (nb, 7, blk)), small)
    small_all = lax.all_to_all(sent, plane, split_axis=0, concat_axis=0, tiled=True)

    def norm_update(every, *a):
        return adam_update(*a, every.transpose(1, 0, 2).reshape(7, width), 0.3, 0.0)

    mn, vn, wn = do(norm_update, small_all, norm_params, m_norm, v_norm)
    p_qkv[0].step()
    adam_both("qkv", p_qkv[0], 0, S * blk)
    return (
        (block_output.reshape(tokens.shape), input_rows.reshape(tokens.shape))
        + tuple(results["qkv"])
        + tuple(results["out"])
        + tuple(results["up"])
        + tuple(results["down"])
        + (mn, vn, wn)
    )


def solution(mesh):
    tok = P("rep", "ctx", "shard", None)
    row = P(("ctx", "shard"), None)
    placed = (tok, tok, P("rep", "shard", None)) + (row,) * 4 + (P(),) + (row,) * 8 + (P(), P())
    return jax.shard_map(
        body,
        mesh=mesh,
        in_specs=placed,
        out_specs=(tok, tok) + (row,) * 12 + (P(),) * 3,
        check_vma=False,
    )
```

```python
import functools

import jax
import jax.numpy as jnp
from jax import lax
from jax.experimental import pallas as pl
from jax.experimental.pallas import tpu as pltpu
from jax.sharding import PartitionSpec as P

HEADS = 32
HEAD_DIM = 64
FF = 5632
ROTARY = 16
STEP = 10

eps_norm = 1e-05
masked_score = -1e30
beta_one = 0.9
beta_two = 0.999
adam_eps = 1e-08
weight_decay = 0.1
score_scale = HEAD_DIM ** (-0.5)
FIRST = (((0,), (0,)), ((), ()))
LAST = (((1,), (1,)), ((), ()))
PLAIN = (((1,), (0,)), ((), ()))
bf16 = jnp.bfloat16
f32 = jnp.float32


def dot(a, b, dims):
    return lax.dot_general(a, b, dims, preferred_element_type=f32)


def adam_update(weight, moment_one, moment_two, grad, step_rate, decay_rate):
    first_new = beta_one * moment_one + (1.0 - beta_one) * grad
    second_new = beta_two * moment_two + (1.0 - beta_two) * grad * grad
    first_hat = first_new / (1.0 - beta_one**STEP)
    second_hat = second_new / (1.0 - beta_two**STEP)
    weight_new = weight - step_rate * (
        first_hat / (jnp.sqrt(second_hat) + adam_eps) + decay_rate * weight
    )
    return (first_new, second_new, weight_new)


class Plane:
    def __init__(self):
        self.s_size = lax.axis_size("shard")
        self.ctx_size = lax.axis_size("ctx")
        self.y_size = self.ctx_size // 2
        self.ctx = lax.axis_index("ctx")
        self.s = lax.axis_index("shard")
        self.y = self.ctx // 2
        self.c = self.ctx % 2
        self.blocks = self.ctx_size * self.s_size

    def core(self, x):
        return lax.ppermute(x, "ctx", [(i, i ^ 1) for i in range(self.ctx_size)])

    def along(self, x, axis, step):
        if axis == "y":
            return lax.ppermute(x, "ctx", [(i, i ^ (2 * step)) for i in range(self.ctx_size)])
        return lax.ppermute(x, "shard", [(i, i ^ step) for i in range(self.s_size)])

    def index(self, axis):
        return self.y if axis == "y" else self.s

    def steps(self, flip):
        ys = []
        k = self.y_size // 2
        while k:
            ys.append(("y", k))
            k //= 2
        ss = []
        k = self.s_size // 2
        while k:
            ss.append(("s", k))
            k //= 2
        return ys + ss if flip else ss + ys

    def chip_exchange(self, x, take):
        out = [(self.y, self.s, take(self.y, self.s))]
        for ry in range(self.y_size):
            for rs in range(self.s_size):
                if ry or rs:
                    y, s = self.y ^ ry, self.s ^ rs
                    mask = 2 * ry * self.s_size + rs
                    perm = [(i, i ^ mask) for i in range(self.blocks)]
                    out.append((y, s, lax.ppermute(take(y, s), ("ctx", "shard"), perm)))
        return out

    def sum_all(self, x):
        for axis, step in self.steps(False):
            x = x + self.along(x, axis, step)
        return x + self.core(x)

    def scatter_sum(self, p, flip):
        axes = {"y": 1, "s": 2}
        steps = self.steps(flip)
        kept = got = None
        for n, (axis, step) in enumerate(steps):
            ax = axes[axis]
            bit = (self.index(axis) // step) % 2
            kept = lax.dynamic_slice_in_dim(p, bit * step, step, ax)
            send = lax.dynamic_slice_in_dim(p, (1 - bit) * step, step, ax)
            got = self.along(send, axis, step)
            if n + 1 < len(steps):
                p = (kept.astype(f32) + got.astype(f32)).astype(bf16)
        return kept[:, 0, 0], got[:, 0, 0]

    def gather(self, p, flip):
        axes = {"y": 1, "s": 2}
        p = p[:, None, None]
        for axis, step in reversed(self.steps(flip)):
            ax = axes[axis]
            bit = (self.index(axis) // step) % 2
            got = self.along(p, axis, step)
            first = bit == 0
            p = jnp.concatenate([jnp.where(first, p, got), jnp.where(first, got, p)], ax)
        return p


class Order:
    def __init__(self):
        self.last = None

    def __call__(self, stage, *args):
        if self.last is not None:
            args, self.last = lax.optimization_barrier((args, self.last))
        out = stage(*args)
        self.last = jax.tree.leaves(out)[0]
        return out


SMALL = pl.CostEstimate(flops=1024, bytes_accessed=1024, transcendentals=0)


class RepSum:
    def __init__(self, order):
        self.order = order
        z = lax.axis_index("rep")
        self.end = (z == 0) | (z == lax.axis_size("rep") - 1)
        self.queue = []
        self.flight = []
        self.depth = 1
        self.done = {}

    def push(self, name, g):
        self.queue.append((name, g))

    def busy(self):
        return bool(self.queue or self.flight)

    def tick(self):
        old = {}
        if len(self.flight) >= self.depth or (self.flight and not self.queue):
            old = self.flight.pop(0)
        new = self.queue.pop(0) if self.queue else None
        values = {}
        if "in" in old:
            values["g"], values["g_got"] = old["in"][1], old["in_got"]
        if "mid" in old:
            values["s"], values["s_got"] = old["mid"][1], old["mid_got"]
        if new:
            values["new"] = new[1]
        both = new and "mid" in old and new[1].shape == old["mid"][1].shape
        if "out" in old:
            values["out_got"] = old["out_got"]

        def stage(v):
            def add(a, b):
                return lax.reduce_precision(a.astype(f32) + b.astype(f32), 8, 7).astype(bf16)

            out = {}
            if "g" in v:
                out["a_sum"] = add(v["g"], v["g_got"])
            if "s" in v:
                total = add(v["s"], v["s_got"])
                out["total"] = jnp.where(self.end, v["new"], total) if both else total
            if "new" in v and not both:
                out["new"] = v["new"]
            if "out_got" in v:
                out["z_got"] = v["out_got"]
            return out

        if not values:
            return
        out = self.order(stage, values)
        if "out" in old:
            self.done[old["out"][0]] = jnp.where(self.end, out["z_got"], old["out"][1])
        slot = {}
        if both:
            got = lax.ppermute(out["total"], "rep", [(0, 1), (1, 0), (2, 3), (3, 2)])
            slot = {"in": new, "in_got": got, "out": (old["mid"][0], out["total"]), "out_got": got}
        else:
            if new:
                slot["in"] = new
                slot["in_got"] = lax.ppermute(out["new"], "rep", [(0, 1), (3, 2)])
            if "mid" in old:
                slot["out"] = (old["mid"][0], out["total"])
                slot["out_got"] = lax.ppermute(out["total"], "rep", [(1, 0), (2, 3)])
        if "in" in old:
            slot["mid"] = (old["in"][0], out["a_sum"])
            slot["mid_got"] = lax.ppermute(out["a_sum"], "rep", [(1, 2), (2, 1)])
        if slot:
            self.flight.append(slot)


def cast_kernel(w_ref, out_ref):
    out_ref[...] = w_ref[...].astype(bf16)


def cast(w):
    rows, width = w.shape
    unit = max(n for n in (128, 256, 512, 1024, 1408, 2048, 2816) if width % n == 0)
    spec = pl.BlockSpec((rows, unit), lambda i: (0, i))
    return pl.pallas_call(
        cast_kernel,
        grid=(width // unit,),
        in_specs=[spec],
        out_specs=spec,
        out_shape=jax.ShapeDtypeStruct(w.shape, bf16),
        compiler_params=pltpu.CompilerParams(vmem_limit_bytes=48 * 1024 * 1024),
        cost_estimate=SMALL,
    )(w)


class PairSum:
    def __init__(self, order, g):
        self.order = order
        self.even = lax.axis_index("rep") % 2 == 0
        half = g.shape[0] // 2

        def cut(g):
            a, b = g[:half], g[half:]
            return jnp.where(self.even, b, a), jnp.where(self.even, a, b)

        send, self.kept = order(cut, g)
        self.got = self.exchange(send, 1)
        self.stage = 0

    def exchange(self, x, step):
        return lax.ppermute(x, "rep", [(i, i ^ step) for i in range(lax.axis_size("rep"))])

    def step(self):
        def add(a, b):
            return lax.reduce_precision(a.astype(f32) + b.astype(f32), 8, 7).astype(bf16)

        def put(a, b):
            return jnp.where(self.even, a, b), jnp.where(self.even, b, a)

        if self.stage < 2:
            self.kept = self.order(add, self.kept, self.got)
            self.got = self.exchange(self.kept, 2 - self.stage)
        else:
            self.done = self.order(put, self.kept, self.got)
        self.stage += 1


def gated_kernel(ga_ref, gb_ref, ua_ref, ub_ref, grad_ref, gains_ref, g0_ref, g1_ref, u0_ref, u1_ref, act_ref, sums_ref):
    half = g0_ref.shape[1]
    gate = ga_ref[...].astype(f32) + gb_ref[...].astype(f32)
    up = ua_ref[...].astype(f32) + ub_ref[...].astype(f32)
    sig = jax.nn.sigmoid(gate)
    silu = gate * sig
    grad = grad_ref[...]
    act_ref[...] = (silu * up).astype(bf16)
    ggate = (grad * up * sig * (1.0 + gate * (1.0 - sig))).astype(bf16)
    gup = (grad * silu).astype(bf16)
    g0_ref[...] = ggate[:, :half]
    g1_ref[...] = ggate[:, half:]
    u0_ref[...] = gup[:, :half]
    u1_ref[...] = gup[:, half:]
    a, b = ggate.astype(f32), gup.astype(f32)
    e = jnp.sum(a * gains_ref[:, 0:1] + b * gains_ref[:, 2:3], axis=0, keepdims=True)
    ez = jnp.sum(a * (gate - gains_ref[:, 1:2]) + b * (up - gains_ref[:, 3:4]), axis=0, keepdims=True)
    both = jnp.concatenate([e, ez], axis=0)

    @pl.when(pl.program_id(0) == 0)
    def _():
        sums_ref[...] = both

    @pl.when(pl.program_id(0) > 0)
    def _():
        sums_ref[...] += both


def gated(ga, gb, ua, ub, grad_act, gains):
    rows, t = grad_act.shape
    n = max(n for n in (1, 2, 4) if rows % (16 * n) == 0)
    whole = pl.BlockSpec((rows // n, t), lambda i: (i, 0))
    half = pl.BlockSpec((rows // n, t // 2), lambda i: (i, 0))
    out_half = jax.ShapeDtypeStruct((rows, t // 2), bf16)
    return pl.pallas_call(
        gated_kernel,
        grid=(n,),
        in_specs=[whole] * 5 + [pl.BlockSpec((rows // n, 4), lambda i: (i, 0))],
        out_specs=[half] * 4 + [whole, pl.BlockSpec((2, t), lambda i: (0, 0))],
        out_shape=[out_half] * 4 + [jax.ShapeDtypeStruct((rows, t), bf16), jax.ShapeDtypeStruct((2, t), f32)],
        compiler_params=pltpu.CompilerParams(vmem_limit_bytes=56 * 1024 * 1024),
        cost_estimate=SMALL,
    )(ga, gb, ua, ub, grad_act, gains)


def own_columns_kernel(block_ref, x_ref, out_ref):
    out_ref[...] = x_ref[...].T


def own_columns(x, block, width):
    rows = x.shape[0]
    if width % 128:
        return lax.dynamic_slice_in_dim(x, block[0] * width, width, 1).T
    tile = min(rows, 512)
    return pl.pallas_call(
        own_columns_kernel,
        grid_spec=pltpu.PrefetchScalarGridSpec(
            num_scalar_prefetch=1,
            grid=(rows // tile,),
            in_specs=[pl.BlockSpec((tile, width), lambda i, block: (i, block[0]))],
            out_specs=pl.BlockSpec((width, tile), lambda i, block: (0, i)),
        ),
        out_shape=jax.ShapeDtypeStruct((width, rows), bf16),
        compiler_params=pltpu.CompilerParams(vmem_limit_bytes=48 * 1024 * 1024),
        cost_estimate=SMALL,
    )(block, x)


def split_kernel(core_ref, w_ref, mine_ref, theirs_ref):
    unit = mine_ref.shape[0]
    first = core_ref[0] == 0
    a, b = w_ref[:, :unit], w_ref[:, unit:]
    mine_ref[...] = jnp.where(first, a, b).T.astype(bf16)
    theirs_ref[...] = jnp.where(first, b, a).T.astype(bf16)


def split_columns(w, core, lead, unit, count):
    rows = w.shape[0]
    half = pl.BlockSpec((unit, rows), lambda j, core: (j, 0))
    out = jax.ShapeDtypeStruct((count * unit, rows), bf16)
    return pl.pallas_call(
        split_kernel,
        grid_spec=pltpu.PrefetchScalarGridSpec(
            num_scalar_prefetch=1,
            grid=(count,),
            in_specs=[pl.BlockSpec((rows, 2 * unit), lambda j, core: (0, lead + j))],
            out_specs=[half, half],
        ),
        out_shape=[out, out],
        compiler_params=pltpu.CompilerParams(vmem_limit_bytes=32 * 1024 * 1024),
        cost_estimate=SMALL,
    )(core, w)


def arrange_kernel(at_ref, a_ref, b_ref, c_ref, d_ref, send_ref, keep_ref):
    send_ref[...] = jnp.concatenate([a_ref[...], b_ref[...]], axis=1)
    keep_ref[...] = jnp.concatenate([c_ref[...], d_ref[...]], axis=1)


def arrange(mine, got, place, pre, y_size, s_size, unit, flip):
    r = mine.shape[1]
    half = pre * y_size * s_size // 2

    def block(i, place, keep):
        p = i % pre
        i = i // pre
        if flip:
            s, y = i % s_size, i // s_size
            bit = place[0] // (y_size // 2)
            bit = bit if keep else 1 - bit
            y = y + bit * (y_size // 2)
        else:
            y, s = i % y_size, i // y_size
            bit = place[1] // (s_size // 2)
            bit = bit if keep else 1 - bit
            s = s + bit * (s_size // 2)
        return ((p * y_size + y) * s_size + s, 0)

    def spec(keep):
        return pl.BlockSpec((unit, r), lambda i, place: block(i, place, keep))

    out = jax.ShapeDtypeStruct((half * unit, 2 * r), bf16)
    out_spec = pl.BlockSpec((unit, 2 * r), lambda i, place: (i, 0))
    return pl.pallas_call(
        arrange_kernel,
        grid_spec=pltpu.PrefetchScalarGridSpec(
            num_scalar_prefetch=1,
            grid=(half,),
            in_specs=[spec(False), spec(False), spec(True), spec(True)],
            out_specs=[out_spec, out_spec],
        ),
        out_shape=[out, out],
        compiler_params=pltpu.CompilerParams(vmem_limit_bytes=32 * 1024 * 1024),
        cost_estimate=SMALL,
    )(place, mine, got, mine, got)


def product_kernel(dims, a_ref, b_ref, *refs):
    p = dot(a_ref[...], b_ref[...], dims)
    if len(refs) == 2:
        p = p + refs[0][...]
    refs[-1][...] = p.astype(refs[-1].dtype)


def mm(a, b, dims, dtype, tm=None, tn=None, add=None):
    (ca,), (cb,) = dims[0]
    m, k, n = a.shape[1 - ca], a.shape[ca], b.shape[1 - cb]
    tm, tn = tm or m, tn or n
    a_block = [0, 0]
    a_block[ca], a_block[1 - ca] = k, tm
    b_block = [0, 0]
    b_block[cb], b_block[1 - cb] = k, tn
    out = pl.BlockSpec((tm, tn), lambda i, j: (i, j))
    return pl.pallas_call(
        functools.partial(product_kernel, dims),
        grid=(m // tm, n // tn),
        in_specs=[
            pl.BlockSpec(tuple(a_block), (lambda i, j: (0, i)) if ca == 0 else (lambda i, j: (i, 0))),
            pl.BlockSpec(tuple(b_block), (lambda i, j: (0, j)) if cb == 0 else (lambda i, j: (j, 0))),
        ]
        + ([] if add is None else [out]),
        out_specs=out,
        out_shape=jax.ShapeDtypeStruct((m, n), dtype),
        compiler_params=pltpu.CompilerParams(vmem_limit_bytes=48 * 1024 * 1024),
        cost_estimate=SMALL,
    )(*((a, b) if add is None else (a, b, add)))


def last_step_kernel(bits_ref, own0_ref, got0_ref, own1_ref, got1_ref, out_ref):
    y, s = pl.program_id(1), pl.program_id(2)
    half = own0_ref.shape[3]
    ys, ss = bits_ref[2], bits_ref[3]
    a = jnp.where(s // ss == bits_ref[1], own0_ref[0, 0], got0_ref[0, 0])
    b = jnp.where(y // ys == bits_ref[0], own1_ref[0, 0], got1_ref[0, 0])
    out_ref[0, 0, 0, :, :half] = a
    out_ref[0, 0, 0, :, half:] = b


def last_step(parts, got, bits, pre, y_size, s_size):
    rows, half = parts[0].shape[2] // pre, parts[0].shape[3]
    along_s = pl.BlockSpec((1, 1, rows, half), lambda p, y, s, bits: (y, s % (s_size // 2), p, 0))
    along_y = pl.BlockSpec((1, 1, rows, half), lambda p, y, s, bits: (y % (y_size // 2), s, p, 0))
    return pl.pallas_call(
        last_step_kernel,
        grid_spec=pltpu.PrefetchScalarGridSpec(
            num_scalar_prefetch=1,
            grid=(pre, y_size, s_size),
            in_specs=[along_s, along_s, along_y, along_y],
            out_specs=pl.BlockSpec((1, 1, 1, rows, 2 * half), lambda p, y, s, bits: (p, y, s, 0, 0)),
        ),
        out_shape=jax.ShapeDtypeStruct((pre, y_size, s_size, rows, 2 * half), bf16),
        compiler_params=pltpu.CompilerParams(vmem_limit_bytes=48 * 1024 * 1024),
        cost_estimate=SMALL,
    )(bits, parts[0], got[0], parts[1], got[1])


def stack_turned_kernel(a_ref, b_ref, out_ref):
    r = a_ref.shape[1]
    out_ref[:r] = a_ref[...].T
    out_ref[r:] = b_ref[...].T


def stack_turned(a, b):
    rows, width = a.shape
    n = max(n for n in (1, 2, 4, 6, 8, 11) if rows % (128 * n) == 0)
    spec = pl.BlockSpec((rows // n, width), lambda i: (i, 0))
    return pl.pallas_call(
        stack_turned_kernel,
        grid=(n,),
        in_specs=[spec, spec],
        out_specs=pl.BlockSpec((2 * width, rows // n), lambda i: (0, i)),
        out_shape=jax.ShapeDtypeStruct((2 * width, rows), bf16),
        compiler_params=pltpu.CompilerParams(vmem_limit_bytes=48 * 1024 * 1024),
        cost_estimate=SMALL,
    )(a, b)


def add_split_kernel(bit_ref, a_ref, b_ref, c_ref, d_ref, send_ref, keep_ref):
    send_ref[...] = (a_ref[...].astype(f32) + b_ref[...].astype(f32)).astype(bf16)
    keep_ref[...] = (c_ref[...].astype(f32) + d_ref[...].astype(f32)).astype(bf16)


def add_split(kept, got, bit):
    rows, t = kept.shape
    half = rows // 2
    n = max(n for n in (1, 2, 3, 4) if half % (16 * n) == 0)
    rb = half // n
    away = pl.BlockSpec((rb, t), lambda i, bit: ((1 - bit[0]) * n + i, 0))
    here = pl.BlockSpec((rb, t), lambda i, bit: (bit[0] * n + i, 0))
    out = jax.ShapeDtypeStruct((half, t), bf16)
    out_spec = pl.BlockSpec((rb, t), lambda i, bit: (i, 0))
    return pl.pallas_call(
        add_split_kernel,
        grid_spec=pltpu.PrefetchScalarGridSpec(
            num_scalar_prefetch=1,
            grid=(n,),
            in_specs=[away, away, here, here],
            out_specs=[out_spec, out_spec],
        ),
        out_shape=[out, out],
        compiler_params=pltpu.CompilerParams(vmem_limit_bytes=48 * 1024 * 1024),
        cost_estimate=SMALL,
    )(bit, kept, got, kept, got)


def adam_kernel(rate, two, core_ref, w_ref, m_ref, v_ref, *refs):
    grad = refs[0][...].astype(f32)
    if two:
        other = refs[1][...].astype(f32)
        mine = core_ref[0] == 0
        grad = jnp.concatenate([jnp.where(mine, grad, other), jnp.where(mine, other, grad)], axis=1)
    new_m_ref, new_v_ref, new_w_ref = refs[-3:]
    new_m, new_v, new_w = adam_update(w_ref[...], m_ref[...], v_ref[...], grad, rate, weight_decay)
    new_m_ref[...] = new_m
    new_v_ref[...] = new_v
    new_w_ref[...] = new_w


def adam_part(state, grads, core, rate, prev, row_first, lead, unit, rb):
    w, m, v = state
    two = len(grads) == 2
    rows, width = grads[0].shape
    whole = pl.BlockSpec((rb, unit * len(grads)), lambda i, g, core: (row_first // rb + i, lead + g))
    half = pl.BlockSpec((rb, unit), lambda i, g, core: (i, g))
    out = jax.ShapeDtypeStruct(w.shape, f32)
    extra, aliases = [], {}
    if prev is not None:
        extra = list(prev)
        aliases = {4 + len(grads) + i: i for i in range(3)}
    return pl.pallas_call(
        functools.partial(adam_kernel, rate, two),
        grid_spec=pltpu.PrefetchScalarGridSpec(
            num_scalar_prefetch=1,
            grid=(rows // rb, width // unit),
            in_specs=[whole] * 3 + [half] * len(grads) + [pl.BlockSpec(memory_space=pl.ANY)] * len(extra),
            out_specs=[whole] * 3,
        ),
        out_shape=[out] * 3,
        input_output_aliases=aliases,
        compiler_params=pltpu.CompilerParams(vmem_limit_bytes=48 * 1024 * 1024),
        cost_estimate=SMALL,
    )(core, w, m, v, *grads, *extra)


def attend_kernel(kept_ref, got_ref, bias_ref, table_ref, qkv_ref, out_ref, stat_ref):
    half = ROTARY // 2
    cos, sin, pos = table_ref[0, :half], table_ref[0, half:ROTARY], table_ref[0, ROTARY:]
    parts = []
    for i in range(3):
        v = kept_ref[i, 0].astype(f32) + got_ref[i, 0].astype(f32) + bias_ref[i, 0]
        if i < 2:
            a, b = v[:half], v[half:ROTARY]
            v = jnp.concatenate([a * cos - b * sin, b * cos + a * sin, v[ROTARY:]], axis=0)
        v = v.astype(bf16)
        qkv_ref[i, 0] = v
        parts.append(v)
    q, k, v = parts
    scores = dot(k, q, FIRST) * score_scale
    scores = jnp.where(pos.T[:, :1] <= pos[:1], scores, masked_score)
    peak = jnp.max(scores, axis=0, keepdims=True)
    e = jnp.exp(scores - peak)
    total = jnp.sum(e, axis=0, keepdims=True)
    p = (e / total).astype(bf16)
    out_ref[0] = dot(v, p, PLAIN).astype(bf16)
    stat_ref[0, 0] = jnp.concatenate([peak, total], axis=0)


def attend(kept, got, bias, table):
    _, heads, hd, t = kept.shape
    seqs, _, seq = table.shape
    big = pl.BlockSpec((3, 1, hd, seq), lambda s, h: (0, h, 0, s))
    table_spec = pl.BlockSpec((1, table.shape[1], seq), lambda s, h: (s, 0, 0))
    stat = pl.BlockSpec((1, 1, 2, seq), lambda s, h: (s, h, 0, 0))
    return pl.pallas_call(
        attend_kernel,
        grid=(seqs, heads),
        in_specs=[
            big,
            big,
            pl.BlockSpec((3, 1, hd, 1), lambda s, h: (0, h, 0, 0)),
            table_spec,
        ],
        out_specs=[big, pl.BlockSpec((1, hd, seq), lambda s, h: (h, 0, s)), stat],
        out_shape=[
            jax.ShapeDtypeStruct((3, heads, hd, t), bf16),
            jax.ShapeDtypeStruct((heads, hd, t), bf16),
            jax.ShapeDtypeStruct((seqs, heads, 2, seq), f32),
        ],
        compiler_params=pltpu.CompilerParams(vmem_limit_bytes=32 * 1024 * 1024),
        cost_estimate=SMALL,
    )(kept, got, bias, table)


def attend_back_kernel(qkv_ref, dout_ref, stat_ref, table_ref, out_ref):
    half = ROTARY // 2
    cos, sin, pos = table_ref[0, :half], table_ref[0, half:ROTARY], table_ref[0, ROTARY:]
    q, k, v = qkv_ref[0, 0], qkv_ref[1, 0], qkv_ref[2, 0]
    dout = dout_ref[0]
    scores = dot(k, q, FIRST) * score_scale
    scores = jnp.where(pos.T[:, :1] <= pos[:1], scores, masked_score)
    p = jnp.exp(scores - stat_ref[0, 0, :1]) / stat_ref[0, 0, 1:]
    dp = dot(v, dout, FIRST)
    inner = jnp.sum(p * dp, axis=0, keepdims=True)
    ds = (p * (dp - inner)).astype(bf16)

    def back(x):
        a, b = x[:half], x[half:ROTARY]
        return jnp.concatenate([a * cos + b * sin, b * cos - a * sin, x[ROTARY:]], axis=0)

    out_ref[0, 0] = back(dot(k, ds, PLAIN) * score_scale).astype(bf16)
    out_ref[1, 0] = back(dot(q, ds, LAST) * score_scale).astype(bf16)
    out_ref[2, 0] = dot(dout, p.astype(bf16), LAST).astype(bf16)


def attend_back(qkv, dout, stats, table):
    _, heads, hd, t = qkv.shape
    seqs, _, seq = table.shape
    big = pl.BlockSpec((3, 1, hd, seq), lambda s, h: (0, h, 0, s))
    table_spec = pl.BlockSpec((1, table.shape[1], seq), lambda s, h: (s, 0, 0))
    stat = pl.BlockSpec((1, 1, 2, seq), lambda s, h: (s, h, 0, 0))
    return pl.pallas_call(
        attend_back_kernel,
        grid=(seqs, heads),
        in_specs=[
            big,
            pl.BlockSpec((1, hd, seq), lambda s, h: (h, 0, s)),
            stat,
            table_spec,
        ],
        out_specs=big,
        out_shape=jax.ShapeDtypeStruct((3, heads, hd, t), bf16),
        compiler_params=pltpu.CompilerParams(vmem_limit_bytes=32 * 1024 * 1024),
        cost_estimate=SMALL,
    )(qkv, dout, stats, table)


def body(
    tokens,
    cotangent,
    span_order,
    w_qkv,
    w_out,
    w_up,
    w_down,
    norm_params,
    m_qkv,
    v_qkv,
    m_out,
    v_out,
    m_up,
    v_up,
    m_down,
    v_down,
    m_norm,
    v_norm,
):
    at = Plane()
    do = Order()
    reps = RepSum(do)
    width = tokens.shape[3]
    rows = tokens.shape[1]
    S, Y, nb = at.s_size, at.y_size, at.blocks
    plane = ("ctx", "shard")
    blk = width // nb
    ffb = FF // nb
    heads = blk // HEAD_DIM
    seq = rows * at.ctx_size
    T = S * seq
    H = T // 2
    first = at.c == 0
    core = at.c.reshape(1)
    my_block = at.ctx * S + at.s
    halves = (slice(0, H), slice(H, T))
    seqs = (slice(0, S // 2), slice(S // 2, S))

    def pick(x, axis, which):
        return lax.dynamic_index_in_dim(x, which, axis, keepdims=False)

    def in_order(mine, theirs, axis):
        return jnp.stack([jnp.where(first, mine, theirs), jnp.where(first, theirs, mine)], axis=axis)

    def join(a, b):
        return jnp.concatenate([a, b], axis=0)

    def lanes(a, b):
        return jnp.concatenate([a, b], axis=1)

    x_rows = tokens.reshape(rows, width)
    order = span_order.reshape(-1).astype(f32)
    span = rows // 2

    def pack(x, order):
        xf = x.astype(f32)
        mean = jnp.mean(xf, axis=1)
        centred = xf - mean[:, None]
        inv = lax.rsqrt(jnp.mean(centred * centred, axis=1) + eps_norm)
        mine = lax.dynamic_slice_in_dim(order, 2 * at.ctx, 2)
        place = jnp.repeat(mine, span)
        terms = []
        for v in (mean, inv):
            for _ in range(3):
                t = lax.reduce_precision(v, 8, 7)
                terms.append(t)
                v = v - t
        extra = jnp.stack(terms + [place] + [jnp.zeros_like(place)] * 9).astype(bf16)
        blocks = x.T.reshape(nb, blk, rows)
        return jnp.concatenate([blocks, jnp.broadcast_to(extra[None], (nb, 16, rows))], axis=1)

    packed = do(pack, x_rows, order)
    cot_all = lax.all_gather(do(cast, cotangent.reshape(rows, width)), ("shard", "ctx"), axis=0, tiled=True)
    got = lax.all_to_all(packed, plane, split_axis=0, concat_axis=0, tiled=True)

    def chip_rows(w, lead, unit, count):
        mine, theirs = do(lambda w: split_columns(w, core, lead, unit, count), w)
        return mine, at.core(theirs)

    wq_parts = chip_rows(w_qkv, 0, S * blk, 3 * Y)
    norm_cols = norm_params.reshape(7, nb, blk).transpose(1, 2, 0)
    own_cols = pick(norm_cols, 0, my_block)
    other_cols = pick(norm_cols, 0, (at.ctx ^ 1) * S + at.s)
    pair_cols = join(own_cols, other_cols)
    bias = own_cols[:, 4:7].T.reshape(3, heads, HEAD_DIM, 1)
    spot = jnp.stack([at.y, at.s])

    def cut_weights(parts, pre, unit, flip):
        return do(lambda a, b: arrange(a, b, spot, pre, Y, S, unit, flip), *parts)

    wq_cut = [cut_weights(wq_parts, 3, blk, bool(k)) for k in range(2)]

    def columns(got):
        x = got.reshape(at.ctx_size, S, blk + 16, rows).transpose(2, 1, 0, 3).reshape(blk + 16, T)
        x_own, extra = x[:blk], x[blk:].astype(f32)
        mean = extra[0:1] + extra[1:2] + extra[2:3]
        inv = extra[3:4] + extra[4:5] + extra[5:6]
        return x_own, mean, inv, extra[6:7]

    x_own, mean1, inv1, place = do(columns, got)
    x_other = at.core(x_own)

    def first_norm(mine, theirs, mean, inv, cols):
        x = join(mine, theirs).astype(f32)
        return ((x - mean) * inv * cols[:, 0:1] + cols[:, 1:2]).astype(bf16)

    xn1 = do(first_norm, x_own, x_other, mean1, inv1, pair_cols)

    def send_products(cut, xs):
        got, kept = [], []
        for k in range(2):
            axis, step = at.steps(bool(k))[0]
            p = do(lambda w, x: dot(w, x, PLAIN).astype(bf16), cut[k][0], xs[k])
            got.append(at.along(p, axis, step))
        for k in range(2):
            kept.append(do(lambda w, x: dot(w, x, PLAIN).astype(bf16), cut[k][1], xs[k]))
        return list(zip(kept, got))

    def scatter_rest(pairs):
        for i in range(1, len(at.steps(False))):
            out = []
            for k in range(2):
                axis, step = at.steps(bool(k))[i]
                bit = (at.index(axis) // step) % 2
                send, kept = do(lambda a, b: add_split(a, b, bit.reshape(1)), *pairs[k])
                out.append((kept, at.along(send, axis, step)))
            pairs = out
        return pairs

    flying = send_products(wq_cut, [xn1[:, h] for h in halves])

    wo_parts = chip_rows(w_out, 0, S * blk, Y)
    wg_parts = chip_rows(w_up, 0, S * ffb, Y)
    wu_parts = chip_rows(w_up, Y, S * ffb, Y)
    wo_cut = [cut_weights(wo_parts, 1, blk, bool(k)) for k in range(2)]

    def positions(place):
        pos = place.reshape(S, seq) * span + (jnp.arange(seq) % span).astype(f32)[None, :]
        prow = pos.reshape(S, 1, seq)
        exponent = jnp.arange(ROTARY // 2, dtype=f32)
        inverse = 10000.0 ** (-2.0 * exponent / ROTARY)
        angles = prow * inverse[None, :, None]
        return jnp.concatenate([jnp.cos(angles), jnp.sin(angles), jnp.broadcast_to(prow, (S, 8, seq))], axis=1)

    table = do(positions, place)
    flying = scatter_rest(flying)

    def gather_steps(parts, pre):
        n = len(at.steps(False))
        state = {"parts": list(parts)}

        def start(i, after=None):
            if after is not None:
                state["parts"], _ = lax.optimization_barrier((state["parts"], after))
            state["got"] = []
            state["at"] = []
            for k in range(2):
                axis, step = list(reversed(at.steps(bool(k))))[i]
                state["at"].append((axis, step))
                state["got"].append(at.along(state["parts"][k], axis, step))

        def finish():
            def put(parts, got):
                out = []
                for k in range(2):
                    axis, step = state["at"][k]
                    ax = {"y": 0, "s": 1}[axis]
                    low = (at.index(axis) // step) % 2 == 0
                    a, b = parts[k], got[k]
                    out.append(jnp.concatenate([jnp.where(low, a, b), jnp.where(low, b, a)], ax))
                return out

            state["parts"] = do(put, state["parts"], state["got"])

        def result():
            ys, ss = Y // 2, S // 2
            bits = jnp.stack([at.y // ys, at.s // ss, jnp.int32(ys), jnp.int32(ss)]).astype(jnp.int32)
            return do(lambda p, g: last_step(p, g, bits, pre, Y, S), state["parts"], state["got"])

        return n, start, finish, result

    qkvs, attns, attn_got, stats = [], [], [], []
    for k in range(2):
        shape = (3, heads, HEAD_DIM, H)
        qkv, attn, stat = do(attend, flying[k][0].reshape(shape), flying[k][1].reshape(shape), bias, table[seqs[k]])
        qkvs.append(qkv)
        attns.append(attn.reshape(blk, H))
        attn_got.append(at.core(attns[k]))
        stats.append(stat)
    pairs = [do(join, attns[k], attn_got[k]) for k in range(2)]
    flying = send_products(wo_cut, pairs)
    wg_cut = cut_weights(wg_parts, 1, ffb, False)
    wu_cut = cut_weights(wu_parts, 1, ffb, True)

    def gain_products(wg, wu, cols):
        terms = []
        for v in (cols[:, 2], cols[:, 3]):
            t = lax.reduce_precision(v, 8, 7)
            terms += [t, v - t]
        terms = jnp.stack(terms).astype(bf16)
        out = []
        for mine, theirs in (wg, wu):
            p = dot(terms[:, :blk], mine, LAST) + dot(terms[:, blk:], theirs, LAST)
            out.append(jnp.stack([p[0] + p[1], p[2] + p[3]]).reshape(2, Y, S, ffb))
        return jnp.concatenate(out, axis=0)

    gains = do(gain_products, wg_parts, wu_parts, pair_cols)
    gain_steps = list(at.steps(False))

    def gain_step(gains):
        axis, step = gain_steps.pop(0)
        ax = {"y": 1, "s": 2}[axis]
        bit = (at.index(axis) // step) % 2
        send = lax.dynamic_slice_in_dim(gains, (1 - bit) * step, step, ax)
        kept = lax.dynamic_slice_in_dim(gains, bit * step, step, ax)
        return kept, at.along(send, axis, step)

    flying = scatter_rest(flying)
    def residual(x, a0, b0, a1, b1):
        a, b = lanes(a0, a1), lanes(b0, b1)
        hidden = x.astype(f32) + (a.astype(f32) + b.astype(f32))
        local_mean = jnp.mean(hidden, axis=0, keepdims=True)
        dev = hidden - local_mean
        return hidden, join(local_mean, jnp.sum(dev * dev, axis=0, keepdims=True))

    hidden, moments = do(residual, x_own, *flying[0], *flying[1])
    count = blk
    for axis, step in at.steps(False) + [("core", 1)]:
        other = at.core(moments) if axis == "core" else at.along(moments, axis, step)

        def merge(a, b):
            gap = a[0:1] - b[0:1]
            return join(0.5 * (a[0:1] + b[0:1]), a[1:2] + b[1:2] + gap * gap * (count / 2.0))

        moments = do(merge, moments, other)
        count *= 2

    def second_norm(hidden, moments, cols):
        inv2 = lax.rsqrt(moments[1:2] / width + eps_norm)
        z2 = (hidden - moments[0:1]) * inv2
        return (z2 * cols[:, 2:3] + cols[:, 3:4]).astype(bf16), z2, inv2

    gains = gain_step(gains)
    xn2_own, z2, inv2 = do(second_norm, hidden, moments, own_cols)
    xn2 = do(join, xn2_own, at.core(xn2_own))

    flying = send_products([wg_cut, wu_cut], [xn2, xn2])

    wd_own = do(cast, w_down)
    wg = do(stack_turned, *wg_parts)
    wu = do(stack_turned, *wu_parts)
    grad_act = do(lambda w, c: mm(w, c, LAST, f32, tn=256), wd_own, cot_all)
    cot_cols = do(lambda c: own_columns(c, my_block.reshape(1), blk), cot_all)
    wo_own = do(cast, w_out)
    wq = do(stack_turned, *wq_parts)
    gains = do(lambda a, b: a + b, *gains)
    while gain_steps:
        gains = do(lambda a, b: a + b, *gain_step(gains))
    gains = do(lambda g: g.reshape(4, ffb).T, gains)
    flying = scatter_rest(flying)

    gate0, gate1, up0, up1, act, sums = do(gated, *flying[0], *flying[1], grad_act, gains)

    up_rows = [(0, blk)]

    def push_pairs(name, g, rows):
        for k, (at_row, count) in enumerate(rows):
            reps.push((name, "theirs", k), g[blk + at_row : blk + at_row + count])
            reps.push((name, "mine", k), g[at_row : at_row + count])

    results = {"down": None, "out": None, "up": None, "qkv": None}
    states = {
        "down": (w_down, m_down, v_down),
        "out": (w_out, m_out, v_out),
        "up": (w_up, m_up, v_up),
        "qkv": (w_qkv, m_qkv, v_qkv),
    }
    rates = {"down": 0.02, "out": 0.2, "up": 0.03, "qkv": 0.03}

    def adam(name, grads, row_first, lead, unit, rb):
        results[name] = do(
            lambda s, g, prev: adam_part(s, g, core, rates[name], prev, row_first, lead, unit, rb),
            states[name],
            grads,
            results[name],
        )

    def adam_both(name, mine, theirs, lead, unit):
        adam(name, [mine, theirs], 0, lead, unit, min(blk, 128))

    def ticks(n):
        for _ in range(n):
            reps.tick()

    wide = 2 * FF // 8

    def quarter_heads(x):
        return [x[:, h][None, None] for h in halves]

    n, start, finish, gate_all = gather_steps([gate0[None, None], gate1[None, None]], 1)
    start(0)
    g_down = do(lambda a, c: mm(a, c, PLAIN, bf16, tn=512), act, cot_all)
    g_down = lax.psum_scatter(g_down, "rep", scatter_dimension=0, tiled=True)

    steps2 = at.steps(False) + [("core", 1)]

    def sum_send(sums, axis, step):
        return at.core(sums) if axis == "core" else at.along(sums, axis, step)

    def sum_step(sums, axis, step):
        return do(lambda a, b: a + b, sums, sum_send(sums, axis, step))

    tiny = list(steps2)
    sums_got = sum_send(sums, *tiny.pop(0))
    for i in range(1, n):
        finish()
        sums = do(lambda a, b: a + b, sums, sums_got)
        sums_got = sum_send(sums, *tiny.pop(0))
        start(i, sums)
    n, start_up, finish_up, up_all = gather_steps([up0[None, None], up1[None, None]], 1)
    ggate_all = gate_all().reshape(Y * S * ffb, T)
    sums = do(lambda a, b: a + b, sums, sums_got)
    start_up(0, sums)
    while tiny:
        sums = sum_step(sums, *tiny.pop(0))
    g_gate = do(lambda x, g: mm(x, g, LAST, bf16, tn=wide), xn2, ggate_all)
    push_pairs("gate", g_gate, up_rows)
    ticks(1)
    finish_up()
    for i in range(1, n):
        start_up(i)
        if i == 1:
            g_down = lax.all_gather(do(lambda g: g, g_down), "rep", axis=0, tiled=True)
            part_gate = do(lambda w, g: mm(w, g, PLAIN, f32, tn=256), wg, ggate_all)
            out_part = do(lambda w, a: mm(w, a, FIRST, bf16, tm=512), wd_own, act)
            ticks(1)
        if i < n - 1:
            finish_up()
    gup_all = up_all().reshape(Y * S * ffb, T)
    part = do(lambda w, g, p: dot(w, g, PLAIN) + p, wu, gup_all, part_gate)
    part_theirs = at.core(part[blk:])

    def branch(a, b, cot, z, scale, gain, sums):
        gxn2 = a + b
        e = gxn2 * gain
        grad_hidden = cot.astype(f32) + scale * (e - sums[0:1] / width - z * (sums[1:2] / width))
        return grad_hidden.astype(bf16), grad_hidden, gxn2

    grad_branch, grad_hidden, gxn2 = do(
        branch, part[:blk], part_theirs, cot_cols, z2, inv2, own_cols[:, 2:3], sums
    )
    n, start, finish, branch_all = gather_steps(quarter_heads(grad_branch), 1)
    start(0)
    g_up = do(lambda x, g: mm(x, g, LAST, bf16, tn=wide), xn2, gup_all)
    push_pairs("up", g_up, up_rows)
    finish()
    for i in range(1, n):
        start(i)
        if i == 1:
            ticks(1)
        if i < n - 1:
            finish()
    gbr_c = branch_all()[0]
    gbr_o = at.core(gbr_c)
    gbr = do(lambda a, b: in_order(a, b, 1).reshape(width, T), gbr_c, gbr_o)
    grad_attn = do(lambda w, g: dot(w, g, PLAIN).astype(bf16), wo_own, gbr)

    gqkvs = []
    for k in range(2):
        dout = grad_attn[:, halves[k]].reshape(heads, HEAD_DIM, H)
        gqkvs.append(do(attend_back, qkvs[k], dout, stats[k], table[seqs[k]]).reshape(3, blk, H))
    n, start, finish, gqkv_done = gather_steps([g.reshape(1, 1, 3 * blk, H) for g in gqkvs], 3)
    start(0)
    attn = lanes(*attns)
    g_out = do(lambda a, g: mm(a, g, LAST, bf16, tn=512), attn, gbr)
    p_out = PairSum(do, g_out)
    ticks(1)
    finish()
    for i in range(1, n):
        start(i)
        if i == 1:
            p_out.step()
            adam("down", [g_down], 0, 0, width // 2, 176)
            ticks(1)
            p_out.step()
        if i < n - 1:
            finish()
    gqkv = gqkv_done().reshape(3, Y * S * blk, T)
    p_qkv = {}
    for third in (2, 1, 0):
        g = do(lambda x, g: mm(x, g, LAST, bf16, tn=512), xn1, gqkv[third])
        p_qkv[third] = PairSum(do, g)
    gate_theirs = at.core(reps.done[("gate", "theirs", 0)])
    part = do(lambda w, g: dot(w, g, PLAIN), wq, gqkv.reshape(3 * Y * S * blk, T))
    part_theirs = at.core(part[blk:])
    ticks(1)
    p_qkv[2].step()
    out_sum = lax.psum_scatter(out_part, plane, scatter_dimension=0, tiled=True)

    def first_back(a, b, x, mean, inv, gain, gxn2, z2, gqkv0, gqkv1):
        gxn1 = a + b
        z1 = (x.astype(f32) - mean) * inv
        e = gxn1 * gain
        sums = join(jnp.sum(e, axis=0, keepdims=True), jnp.sum(e * z1, axis=0, keepdims=True))
        small = jnp.concatenate(
            [
                jnp.sum(gxn1 * z1, axis=1)[None],
                jnp.sum(gxn1, axis=1)[None],
                jnp.sum(gxn2 * z2, axis=1)[None],
                jnp.sum(gxn2, axis=1)[None],
                jnp.sum(gqkv0.astype(f32), axis=2) + jnp.sum(gqkv1.astype(f32), axis=2),
            ],
            axis=0,
        )
        return sums, small, gxn1, z1

    sums, small, gxn1, z1 = do(
        first_back, part[:blk], part_theirs, x_own, mean1, inv1, own_cols[:, 0:1], gxn2, z2, *gqkvs
    )
    p_qkv[1].step()
    p_qkv[0].step()
    adam_both("up", reps.done[("gate", "mine", 0)], gate_theirs, 0, S * ffb)
    p_out.step()
    sums = sum_step(sums, *steps2[0])
    p_qkv[2].step()
    for axis, step in steps2[1:]:
        sums = sum_step(sums, axis, step)
    input_grad = do(
        lambda h, grad, z, scale, gain, sums: h
        + scale * (grad * gain - sums[0:1] / width - z * (sums[1:2] / width)),
        grad_hidden,
        gxn1,
        z1,
        inv1,
        own_cols[:, 0:1],
        sums,
    )
    while reps.busy():
        reps.tick()
    up_theirs = at.core(reps.done[("up", "theirs", 0)])

    def to_rows(cols):
        split = do(lambda c: c.reshape(blk, S, at.ctx_size, rows).transpose(2, 1, 0, 3).reshape(nb, blk, rows), cols)
        got = lax.all_to_all(split, plane, split_axis=0, concat_axis=0, tiled=True)
        return do(lambda g: g.reshape(width, rows).T, got)

    def adam_qkv(third):
        mine, theirs = p_qkv[third].done
        adam_both("qkv", mine, at.core(theirs), third * Y, S * blk)

    p_qkv[1].step()
    input_rows = to_rows(input_grad)
    p_qkv[0].step()
    adam_both("up", reps.done[("up", "mine", 0)], up_theirs, Y, S * ffb)
    for k, g in enumerate(p_out.done):
        adam("out", [g], k * blk // 2, 0, width // 2, blk // 2)
    p_qkv[2].step()
    adam_qkv(2)
    n_rep = lax.axis_size("rep")
    step = 1
    while step < n_rep:
        other = lax.ppermute(small, "rep", [(i, i ^ step) for i in range(n_rep)])
        small = do(lambda a, b: a + b, small, other)
        step *= 2
    p_qkv[1].step()
    adam_qkv(1)
    out_cols = do(lambda h, a: (h + a.astype(f32)).astype(bf16), hidden, out_sum)
    block_output = to_rows(out_cols)
    sent = do(lambda s: jnp.broadcast_to(s.reshape(1, 7, blk), (nb, 7, blk)), small)
    small_all = lax.all_to_all(sent, plane, split_axis=0, concat_axis=0, tiled=True)

    def norm_update(every, *a):
        return adam_update(*a, every.transpose(1, 0, 2).reshape(7, width), 0.3, 0.0)

    mn, vn, wn = do(norm_update, small_all, norm_params, m_norm, v_norm)
    p_qkv[0].step()
    adam_qkv(0)
    return (
        (block_output.reshape(tokens.shape), input_rows.reshape(tokens.shape))
        + tuple(results["qkv"])
        + tuple(results["out"])
        + tuple(results["up"])
        + tuple(results["down"])
        + (mn, vn, wn)
    )


def solution(mesh):
    tok = P("rep", "ctx", "shard", None)
    row = P(("ctx", "shard"), None)
    placed = (tok, tok, P("rep", "shard", None)) + (row,) * 4 + (P(),) + (row,) * 8 + (P(), P())
    return jax.shard_map(
        body,
        mesh=mesh,
        in_specs=placed,
        out_specs=(tok, tok) + (row,) * 12 + (P(),) * 3,
        check_vma=False,
    )
```

```python
import functools

import jax
import jax.numpy as jnp
from jax import lax
from jax.experimental import pallas as pl
from jax.experimental.pallas import tpu as pltpu
from jax.sharding import PartitionSpec as P

HEADS = 32
HEAD_DIM = 64
FF = 5632
ROTARY = 16
STEP = 10

eps_norm = 1e-05
masked_score = -1e30
beta_one = 0.9
beta_two = 0.999
adam_eps = 1e-08
weight_decay = 0.1
score_scale = HEAD_DIM ** (-0.5)
FIRST = (((0,), (0,)), ((), ()))
LAST = (((1,), (1,)), ((), ()))
PLAIN = (((1,), (0,)), ((), ()))
bf16 = jnp.bfloat16
f32 = jnp.float32


def dot(a, b, dims):
    return lax.dot_general(a, b, dims, preferred_element_type=f32)


def adam_update(weight, moment_one, moment_two, grad, step_rate, decay_rate):
    first_new = beta_one * moment_one + (1.0 - beta_one) * grad
    second_new = beta_two * moment_two + (1.0 - beta_two) * grad * grad
    first_hat = first_new / (1.0 - beta_one**STEP)
    second_hat = second_new / (1.0 - beta_two**STEP)
    weight_new = weight - step_rate * (
        first_hat / (jnp.sqrt(second_hat) + adam_eps) + decay_rate * weight
    )
    return (first_new, second_new, weight_new)


class Plane:
    def __init__(self):
        self.s_size = lax.axis_size("shard")
        self.ctx_size = lax.axis_size("ctx")
        self.y_size = self.ctx_size // 2
        self.ctx = lax.axis_index("ctx")
        self.s = lax.axis_index("shard")
        self.y = self.ctx // 2
        self.c = self.ctx % 2
        self.blocks = self.ctx_size * self.s_size

    def core(self, x):
        return lax.ppermute(x, "ctx", [(i, i ^ 1) for i in range(self.ctx_size)])

    def along(self, x, axis, step):
        if axis == "y":
            return lax.ppermute(x, "ctx", [(i, i ^ (2 * step)) for i in range(self.ctx_size)])
        return lax.ppermute(x, "shard", [(i, i ^ step) for i in range(self.s_size)])

    def index(self, axis):
        return self.y if axis == "y" else self.s

    def steps(self, flip):
        ys = []
        k = self.y_size // 2
        while k:
            ys.append(("y", k))
            k //= 2
        ss = []
        k = self.s_size // 2
        while k:
            ss.append(("s", k))
            k //= 2
        return ys + ss if flip else ss + ys

    def chip_exchange(self, x, take):
        out = [(self.y, self.s, take(self.y, self.s))]
        for ry in range(self.y_size):
            for rs in range(self.s_size):
                if ry or rs:
                    y, s = self.y ^ ry, self.s ^ rs
                    mask = 2 * ry * self.s_size + rs
                    perm = [(i, i ^ mask) for i in range(self.blocks)]
                    out.append((y, s, lax.ppermute(take(y, s), ("ctx", "shard"), perm)))
        return out

    def sum_all(self, x):
        for axis, step in self.steps(False):
            x = x + self.along(x, axis, step)
        return x + self.core(x)

    def scatter_sum(self, p, flip):
        axes = {"y": 1, "s": 2}
        steps = self.steps(flip)
        kept = got = None
        for n, (axis, step) in enumerate(steps):
            ax = axes[axis]
            bit = (self.index(axis) // step) % 2
            kept = lax.dynamic_slice_in_dim(p, bit * step, step, ax)
            send = lax.dynamic_slice_in_dim(p, (1 - bit) * step, step, ax)
            got = self.along(send, axis, step)
            if n + 1 < len(steps):
                p = (kept.astype(f32) + got.astype(f32)).astype(bf16)
        return kept[:, 0, 0], got[:, 0, 0]

    def gather(self, p, flip):
        axes = {"y": 1, "s": 2}
        p = p[:, None, None]
        for axis, step in reversed(self.steps(flip)):
            ax = axes[axis]
            bit = (self.index(axis) // step) % 2
            got = self.along(p, axis, step)
            first = bit == 0
            p = jnp.concatenate([jnp.where(first, p, got), jnp.where(first, got, p)], ax)
        return p


class Order:
    def __init__(self):
        self.last = None

    def __call__(self, stage, *args):
        if self.last is not None:
            args, self.last = lax.optimization_barrier((args, self.last))
        out = stage(*args)
        self.last = jax.tree.leaves(out)[0]
        return out


SMALL = pl.CostEstimate(flops=1024, bytes_accessed=1024, transcendentals=0)


class RepSum:
    def __init__(self, order):
        self.order = order
        z = lax.axis_index("rep")
        self.end = (z == 0) | (z == lax.axis_size("rep") - 1)
        self.queue = []
        self.flight = []
        self.depth = 1
        self.done = {}

    def push(self, name, g):
        self.queue.append((name, g))

    def busy(self):
        return bool(self.queue or self.flight)

    def tick(self):
        old = {}
        if len(self.flight) >= self.depth or (self.flight and not self.queue):
            old = self.flight.pop(0)
        new = self.queue.pop(0) if self.queue else None
        values = {}
        if "in" in old:
            values["g"], values["g_got"] = old["in"][1], old["in_got"]
        if "mid" in old:
            values["s"], values["s_got"] = old["mid"][1], old["mid_got"]
        if new:
            values["new"] = new[1]
        both = new and "mid" in old and new[1].shape == old["mid"][1].shape
        if "out" in old:
            values["out_got"] = old["out_got"]

        def stage(v):
            def add(a, b):
                return lax.reduce_precision(a.astype(f32) + b.astype(f32), 8, 7).astype(bf16)

            out = {}
            if "g" in v:
                out["a_sum"] = add(v["g"], v["g_got"])
            if "s" in v:
                total = add(v["s"], v["s_got"])
                out["total"] = jnp.where(self.end, v["new"], total) if both else total
            if "new" in v and not both:
                out["new"] = v["new"]
            if "out_got" in v:
                out["z_got"] = v["out_got"]
            return out

        if not values:
            return
        out = self.order(stage, values)
        if "out" in old:
            self.done[old["out"][0]] = jnp.where(self.end, out["z_got"], old["out"][1])
        slot = {}
        if both:
            got = lax.ppermute(out["total"], "rep", [(0, 1), (1, 0), (2, 3), (3, 2)])
            slot = {"in": new, "in_got": got, "out": (old["mid"][0], out["total"]), "out_got": got}
        else:
            if new:
                slot["in"] = new
                slot["in_got"] = lax.ppermute(out["new"], "rep", [(0, 1), (3, 2)])
            if "mid" in old:
                slot["out"] = (old["mid"][0], out["total"])
                slot["out_got"] = lax.ppermute(out["total"], "rep", [(1, 0), (2, 3)])
        if "in" in old:
            slot["mid"] = (old["in"][0], out["a_sum"])
            slot["mid_got"] = lax.ppermute(out["a_sum"], "rep", [(1, 2), (2, 1)])
        if slot:
            self.flight.append(slot)


def cast_kernel(w_ref, out_ref):
    out_ref[...] = w_ref[...].astype(bf16)


def cast(w):
    rows, width = w.shape
    unit = max(n for n in (128, 256, 512, 1024, 1408, 2048, 2816) if width % n == 0)
    spec = pl.BlockSpec((rows, unit), lambda i: (0, i))
    return pl.pallas_call(
        cast_kernel,
        grid=(width // unit,),
        in_specs=[spec],
        out_specs=spec,
        out_shape=jax.ShapeDtypeStruct(w.shape, bf16),
        compiler_params=pltpu.CompilerParams(vmem_limit_bytes=48 * 1024 * 1024),
        cost_estimate=SMALL,
    )(w)


def gated_kernel(ga_ref, gb_ref, ua_ref, ub_ref, grad_ref, gains_ref, ggate_ref, gup_ref, act_ref, sums_ref):
    gate = ga_ref[...].astype(f32) + gb_ref[...].astype(f32)
    up = ua_ref[...].astype(f32) + ub_ref[...].astype(f32)
    sig = jax.nn.sigmoid(gate)
    silu = gate * sig
    grad = grad_ref[...]
    act_ref[...] = (silu * up).astype(bf16)
    ggate = (grad * up * sig * (1.0 + gate * (1.0 - sig))).astype(bf16)
    gup = (grad * silu).astype(bf16)
    ggate_ref[...] = ggate
    gup_ref[...] = gup
    a, b = ggate.astype(f32), gup.astype(f32)
    e = jnp.sum(a * gains_ref[:, 0:1] + b * gains_ref[:, 2:3], axis=0, keepdims=True)
    ez = jnp.sum(a * (gate - gains_ref[:, 1:2]) + b * (up - gains_ref[:, 3:4]), axis=0, keepdims=True)
    both = jnp.concatenate([e, ez], axis=0)

    @pl.when(pl.program_id(0) == 0)
    def _():
        sums_ref[...] = both

    @pl.when(pl.program_id(0) > 0)
    def _():
        sums_ref[...] += both


def gated(ga, gb, ua, ub, grad_act, gains):
    rows, t = grad_act.shape
    n = max(n for n in (1, 2, 4) if rows % (16 * n) == 0)
    whole = pl.BlockSpec((rows // n, t), lambda i: (i, 0))
    out = jax.ShapeDtypeStruct((rows, t), bf16)
    return pl.pallas_call(
        gated_kernel,
        grid=(n,),
        in_specs=[whole] * 5 + [pl.BlockSpec((rows // n, 4), lambda i: (i, 0))],
        out_specs=[whole] * 3 + [pl.BlockSpec((2, t), lambda i: (0, 0))],
        out_shape=[out] * 3 + [jax.ShapeDtypeStruct((2, t), f32)],
        compiler_params=pltpu.CompilerParams(vmem_limit_bytes=56 * 1024 * 1024),
        cost_estimate=SMALL,
    )(ga, gb, ua, ub, grad_act, gains)


def own_columns_kernel(block_ref, x_ref, out_ref):
    out_ref[...] = x_ref[...].T


def own_columns(x, block, width):
    rows = x.shape[0]
    if width % 128:
        return lax.dynamic_slice_in_dim(x, block[0] * width, width, 1).T
    tile = min(rows, 512)
    return pl.pallas_call(
        own_columns_kernel,
        grid_spec=pltpu.PrefetchScalarGridSpec(
            num_scalar_prefetch=1,
            grid=(rows // tile,),
            in_specs=[pl.BlockSpec((tile, width), lambda i, block: (i, block[0]))],
            out_specs=pl.BlockSpec((width, tile), lambda i, block: (0, i)),
        ),
        out_shape=jax.ShapeDtypeStruct((width, rows), bf16),
        compiler_params=pltpu.CompilerParams(vmem_limit_bytes=48 * 1024 * 1024),
        cost_estimate=SMALL,
    )(block, x)


def split_kernel(core_ref, w_ref, mine_ref, theirs_ref):
    unit = mine_ref.shape[0]
    first = core_ref[0] == 0
    a, b = w_ref[:, :unit], w_ref[:, unit:]
    mine_ref[...] = jnp.where(first, a, b).T.astype(bf16)
    theirs_ref[...] = jnp.where(first, b, a).T.astype(bf16)


def split_columns(w, core, lead, unit, count):
    rows = w.shape[0]
    half = pl.BlockSpec((unit, rows), lambda j, core: (j, 0))
    out = jax.ShapeDtypeStruct((count * unit, rows), bf16)
    return pl.pallas_call(
        split_kernel,
        grid_spec=pltpu.PrefetchScalarGridSpec(
            num_scalar_prefetch=1,
            grid=(count,),
            in_specs=[pl.BlockSpec((rows, 2 * unit), lambda j, core: (0, lead + j))],
            out_specs=[half, half],
        ),
        out_shape=[out, out],
        compiler_params=pltpu.CompilerParams(vmem_limit_bytes=32 * 1024 * 1024),
        cost_estimate=SMALL,
    )(core, w)


def arrange_kernel(at_ref, a_ref, b_ref, c_ref, d_ref, send_ref, keep_ref):
    send_ref[...] = jnp.concatenate([a_ref[...], b_ref[...]], axis=1)
    keep_ref[...] = jnp.concatenate([c_ref[...], d_ref[...]], axis=1)


def arrange(mine, got, place, pre, y_size, s_size, unit, flip):
    r = mine.shape[1]
    half = pre * y_size * s_size // 2

    def block(i, place, keep):
        p = i % pre
        i = i // pre
        if flip:
            s, y = i % s_size, i // s_size
            bit = place[0] // (y_size // 2)
            bit = bit if keep else 1 - bit
            y = y + bit * (y_size // 2)
        else:
            y, s = i % y_size, i // y_size
            bit = place[1] // (s_size // 2)
            bit = bit if keep else 1 - bit
            s = s + bit * (s_size // 2)
        return ((p * y_size + y) * s_size + s, 0)

    def spec(keep):
        return pl.BlockSpec((unit, r), lambda i, place: block(i, place, keep))

    out = jax.ShapeDtypeStruct((half * unit, 2 * r), bf16)
    out_spec = pl.BlockSpec((unit, 2 * r), lambda i, place: (i, 0))
    return pl.pallas_call(
        arrange_kernel,
        grid_spec=pltpu.PrefetchScalarGridSpec(
            num_scalar_prefetch=1,
            grid=(half,),
            in_specs=[spec(False), spec(False), spec(True), spec(True)],
            out_specs=[out_spec, out_spec],
        ),
        out_shape=[out, out],
        compiler_params=pltpu.CompilerParams(vmem_limit_bytes=32 * 1024 * 1024),
        cost_estimate=SMALL,
    )(place, mine, got, mine, got)


def product_kernel(dims, a_ref, b_ref, *refs):
    p = dot(a_ref[...], b_ref[...], dims)
    if len(refs) == 2:
        p = p + refs[0][...]
    refs[-1][...] = p.astype(refs[-1].dtype)


def mm(a, b, dims, dtype, tm=None, tn=None, add=None):
    (ca,), (cb,) = dims[0]
    m, k, n = a.shape[1 - ca], a.shape[ca], b.shape[1 - cb]
    tm, tn = tm or m, tn or n
    a_block = [0, 0]
    a_block[ca], a_block[1 - ca] = k, tm
    b_block = [0, 0]
    b_block[cb], b_block[1 - cb] = k, tn
    out = pl.BlockSpec((tm, tn), lambda i, j: (i, j))
    return pl.pallas_call(
        functools.partial(product_kernel, dims),
        grid=(m // tm, n // tn),
        in_specs=[
            pl.BlockSpec(tuple(a_block), (lambda i, j: (0, i)) if ca == 0 else (lambda i, j: (i, 0))),
            pl.BlockSpec(tuple(b_block), (lambda i, j: (0, j)) if cb == 0 else (lambda i, j: (j, 0))),
        ]
        + ([] if add is None else [out]),
        out_specs=out,
        out_shape=jax.ShapeDtypeStruct((m, n), dtype),
        compiler_params=pltpu.CompilerParams(vmem_limit_bytes=48 * 1024 * 1024),
        cost_estimate=SMALL,
    )(*((a, b) if add is None else (a, b, add)))


def stack_turned_kernel(a_ref, b_ref, out_ref):
    r = a_ref.shape[1]
    out_ref[:r] = a_ref[...].T
    out_ref[r:] = b_ref[...].T


def stack_turned(a, b):
    rows, width = a.shape
    n = max(n for n in (1, 2, 4, 6, 8, 11) if rows % (128 * n) == 0)
    spec = pl.BlockSpec((rows // n, width), lambda i: (i, 0))
    return pl.pallas_call(
        stack_turned_kernel,
        grid=(n,),
        in_specs=[spec, spec],
        out_specs=pl.BlockSpec((2 * width, rows // n), lambda i: (0, i)),
        out_shape=jax.ShapeDtypeStruct((2 * width, rows), bf16),
        compiler_params=pltpu.CompilerParams(vmem_limit_bytes=48 * 1024 * 1024),
        cost_estimate=SMALL,
    )(a, b)


def add_split_kernel(bit_ref, a_ref, b_ref, c_ref, d_ref, send_ref, keep_ref):
    send_ref[...] = (a_ref[...].astype(f32) + b_ref[...].astype(f32)).astype(bf16)
    keep_ref[...] = (c_ref[...].astype(f32) + d_ref[...].astype(f32)).astype(bf16)


def add_split(kept, got, bit):
    rows, t = kept.shape
    half = rows // 2
    n = max(n for n in (1, 2, 3, 4) if half % (16 * n) == 0)
    rb = half // n
    away = pl.BlockSpec((rb, t), lambda i, bit: ((1 - bit[0]) * n + i, 0))
    here = pl.BlockSpec((rb, t), lambda i, bit: (bit[0] * n + i, 0))
    out = jax.ShapeDtypeStruct((half, t), bf16)
    out_spec = pl.BlockSpec((rb, t), lambda i, bit: (i, 0))
    return pl.pallas_call(
        add_split_kernel,
        grid_spec=pltpu.PrefetchScalarGridSpec(
            num_scalar_prefetch=1,
            grid=(n,),
            in_specs=[away, away, here, here],
            out_specs=[out_spec, out_spec],
        ),
        out_shape=[out, out],
        compiler_params=pltpu.CompilerParams(vmem_limit_bytes=48 * 1024 * 1024),
        cost_estimate=SMALL,
    )(bit, kept, got, kept, got)


def adam_kernel(rate, two, core_ref, w_ref, m_ref, v_ref, *refs):
    grad = refs[0][...].astype(f32)
    if two:
        other = refs[1][...].astype(f32)
        mine = core_ref[0] == 0
        grad = jnp.concatenate([jnp.where(mine, grad, other), jnp.where(mine, other, grad)], axis=1)
    new_m_ref, new_v_ref, new_w_ref = refs[-3:]
    new_m, new_v, new_w = adam_update(w_ref[...], m_ref[...], v_ref[...], grad, rate, weight_decay)
    new_m_ref[...] = new_m
    new_v_ref[...] = new_v
    new_w_ref[...] = new_w


def adam_part(state, grads, core, rate, prev, row_first, lead, unit, rb):
    w, m, v = state
    two = len(grads) == 2
    rows, width = grads[0].shape
    whole = pl.BlockSpec((rb, unit * len(grads)), lambda i, g, core: (row_first // rb + i, lead + g))
    half = pl.BlockSpec((rb, unit), lambda i, g, core: (i, g))
    out = jax.ShapeDtypeStruct(w.shape, f32)
    extra, aliases = [], {}
    if prev is not None:
        extra = list(prev)
        aliases = {4 + len(grads) + i: i for i in range(3)}
    return pl.pallas_call(
        functools.partial(adam_kernel, rate, two),
        grid_spec=pltpu.PrefetchScalarGridSpec(
            num_scalar_prefetch=1,
            grid=(rows // rb, width // unit),
            in_specs=[whole] * 3 + [half] * len(grads) + [pl.BlockSpec(memory_space=pl.ANY)] * len(extra),
            out_specs=[whole] * 3,
        ),
        out_shape=[out] * 3,
        input_output_aliases=aliases,
        compiler_params=pltpu.CompilerParams(vmem_limit_bytes=48 * 1024 * 1024),
        cost_estimate=SMALL,
    )(core, w, m, v, *grads, *extra)


def attend_kernel(kept_ref, got_ref, bias_ref, table_ref, qkv_ref, out_ref, stat_ref):
    half = ROTARY // 2
    cos, sin, pos = table_ref[0, :half], table_ref[0, half:ROTARY], table_ref[0, ROTARY:]
    parts = []
    for i in range(3):
        v = kept_ref[i, 0].astype(f32) + got_ref[i, 0].astype(f32) + bias_ref[i, 0]
        if i < 2:
            a, b = v[:half], v[half:ROTARY]
            v = jnp.concatenate([a * cos - b * sin, b * cos + a * sin, v[ROTARY:]], axis=0)
        v = v.astype(bf16)
        qkv_ref[i, 0] = v
        parts.append(v)
    q, k, v = parts
    scores = dot(k, q, FIRST) * score_scale
    scores = jnp.where(pos.T[:, :1] <= pos[:1], scores, masked_score)
    peak = jnp.max(scores, axis=0, keepdims=True)
    e = jnp.exp(scores - peak)
    total = jnp.sum(e, axis=0, keepdims=True)
    p = (e / total).astype(bf16)
    out_ref[0] = dot(v, p, PLAIN).astype(bf16)
    stat_ref[0, 0] = jnp.concatenate([peak, total], axis=0)


def attend(kept, got, bias, table):
    _, heads, hd, t = kept.shape
    seqs, _, seq = table.shape
    big = pl.BlockSpec((3, 1, hd, seq), lambda s, h: (0, h, 0, s))
    table_spec = pl.BlockSpec((1, table.shape[1], seq), lambda s, h: (s, 0, 0))
    stat = pl.BlockSpec((1, 1, 2, seq), lambda s, h: (s, h, 0, 0))
    return pl.pallas_call(
        attend_kernel,
        grid=(seqs, heads),
        in_specs=[
            big,
            big,
            pl.BlockSpec((3, 1, hd, 1), lambda s, h: (0, h, 0, 0)),
            table_spec,
        ],
        out_specs=[big, pl.BlockSpec((1, hd, seq), lambda s, h: (h, 0, s)), stat],
        out_shape=[
            jax.ShapeDtypeStruct((3, heads, hd, t), bf16),
            jax.ShapeDtypeStruct((heads, hd, t), bf16),
            jax.ShapeDtypeStruct((seqs, heads, 2, seq), f32),
        ],
        compiler_params=pltpu.CompilerParams(vmem_limit_bytes=32 * 1024 * 1024),
        cost_estimate=SMALL,
    )(kept, got, bias, table)


def attend_back_kernel(qkv_ref, dout_ref, stat_ref, table_ref, out_ref):
    half = ROTARY // 2
    cos, sin, pos = table_ref[0, :half], table_ref[0, half:ROTARY], table_ref[0, ROTARY:]
    q, k, v = qkv_ref[0, 0], qkv_ref[1, 0], qkv_ref[2, 0]
    dout = dout_ref[0]
    scores = dot(k, q, FIRST) * score_scale
    scores = jnp.where(pos.T[:, :1] <= pos[:1], scores, masked_score)
    p = jnp.exp(scores - stat_ref[0, 0, :1]) / stat_ref[0, 0, 1:]
    dp = dot(v, dout, FIRST)
    inner = jnp.sum(p * dp, axis=0, keepdims=True)
    ds = (p * (dp - inner)).astype(bf16)

    def back(x):
        a, b = x[:half], x[half:ROTARY]
        return jnp.concatenate([a * cos + b * sin, b * cos - a * sin, x[ROTARY:]], axis=0)

    out_ref[0, 0] = back(dot(k, ds, PLAIN) * score_scale).astype(bf16)
    out_ref[1, 0] = back(dot(q, ds, LAST) * score_scale).astype(bf16)
    out_ref[2, 0] = dot(dout, p.astype(bf16), LAST).astype(bf16)


def attend_back(qkv, dout, stats, table):
    _, heads, hd, t = qkv.shape
    seqs, _, seq = table.shape
    big = pl.BlockSpec((3, 1, hd, seq), lambda s, h: (0, h, 0, s))
    table_spec = pl.BlockSpec((1, table.shape[1], seq), lambda s, h: (s, 0, 0))
    stat = pl.BlockSpec((1, 1, 2, seq), lambda s, h: (s, h, 0, 0))
    return pl.pallas_call(
        attend_back_kernel,
        grid=(seqs, heads),
        in_specs=[
            big,
            pl.BlockSpec((1, hd, seq), lambda s, h: (h, 0, s)),
            stat,
            table_spec,
        ],
        out_specs=big,
        out_shape=jax.ShapeDtypeStruct((3, heads, hd, t), bf16),
        compiler_params=pltpu.CompilerParams(vmem_limit_bytes=32 * 1024 * 1024),
        cost_estimate=SMALL,
    )(qkv, dout, stats, table)


def body(
    tokens,
    cotangent,
    span_order,
    w_qkv,
    w_out,
    w_up,
    w_down,
    norm_params,
    m_qkv,
    v_qkv,
    m_out,
    v_out,
    m_up,
    v_up,
    m_down,
    v_down,
    m_norm,
    v_norm,
):
    at = Plane()
    do = Order()
    reps = RepSum(do)
    width = tokens.shape[3]
    rows = tokens.shape[1]
    S, Y, nb = at.s_size, at.y_size, at.blocks
    plane = ("ctx", "shard")
    blk = width // nb
    ffb = FF // nb
    heads = blk // HEAD_DIM
    seq = rows * at.ctx_size
    T = S * seq
    H = T // 2
    first = at.c == 0
    core = at.c.reshape(1)
    my_block = at.ctx * S + at.s
    halves = (slice(0, H), slice(H, T))
    seqs = (slice(0, S // 2), slice(S // 2, S))

    def pick(x, axis, which):
        return lax.dynamic_index_in_dim(x, which, axis, keepdims=False)

    def in_order(mine, theirs, axis):
        return jnp.stack([jnp.where(first, mine, theirs), jnp.where(first, theirs, mine)], axis=axis)

    def join(a, b):
        return jnp.concatenate([a, b], axis=0)

    def lanes(a, b):
        return jnp.concatenate([a, b], axis=1)

    x_rows = tokens.reshape(rows, width)
    order = span_order.reshape(-1).astype(f32)
    span = rows // 2

    def pack(x, order):
        xf = x.astype(f32)
        mean = jnp.mean(xf, axis=1)
        centred = xf - mean[:, None]
        inv = lax.rsqrt(jnp.mean(centred * centred, axis=1) + eps_norm)
        mine = lax.dynamic_slice_in_dim(order, 2 * at.ctx, 2)
        place = jnp.repeat(mine, span)
        terms = []
        for v in (mean, inv):
            for _ in range(3):
                t = lax.reduce_precision(v, 8, 7)
                terms.append(t)
                v = v - t
        extra = jnp.stack(terms + [place] + [jnp.zeros_like(place)] * 9).astype(bf16)
        blocks = x.T.reshape(nb, blk, rows)
        return jnp.concatenate([blocks, jnp.broadcast_to(extra[None], (nb, 16, rows))], axis=1)

    packed = do(pack, x_rows, order)
    cot_all = lax.all_gather(do(cast, cotangent.reshape(rows, width)), ("shard", "ctx"), axis=0, tiled=True)
    got = lax.all_to_all(packed, plane, split_axis=0, concat_axis=0, tiled=True)

    def chip_rows(w, lead, unit, count):
        mine, theirs = do(lambda w: split_columns(w, core, lead, unit, count), w)
        return mine, at.core(theirs)

    wq_parts = chip_rows(w_qkv, 0, S * blk, 3 * Y)
    norm_cols = norm_params.reshape(7, nb, blk).transpose(1, 2, 0)
    own_cols = pick(norm_cols, 0, my_block)
    other_cols = pick(norm_cols, 0, (at.ctx ^ 1) * S + at.s)
    pair_cols = join(own_cols, other_cols)
    bias = own_cols[:, 4:7].T.reshape(3, heads, HEAD_DIM, 1)
    spot = jnp.stack([at.y, at.s])

    def cut_weights(parts, pre, unit, flip):
        return do(lambda a, b: arrange(a, b, spot, pre, Y, S, unit, flip), *parts)

    wq_cut = [cut_weights(wq_parts, 3, blk, bool(k)) for k in range(2)]

    def columns(got):
        x = got.reshape(at.ctx_size, S, blk + 16, rows).transpose(2, 1, 0, 3).reshape(blk + 16, T)
        x_own, extra = x[:blk], x[blk:].astype(f32)
        mean = extra[0:1] + extra[1:2] + extra[2:3]
        inv = extra[3:4] + extra[4:5] + extra[5:6]
        return x_own, mean, inv, extra[6:7]

    x_own, mean1, inv1, place = do(columns, got)
    x_other = at.core(x_own)

    def first_norm(mine, theirs, mean, inv, cols):
        x = join(mine, theirs).astype(f32)
        return ((x - mean) * inv * cols[:, 0:1] + cols[:, 1:2]).astype(bf16)

    xn1 = do(first_norm, x_own, x_other, mean1, inv1, pair_cols)

    def send_products(cut, xs):
        got, kept = [], []
        for k in range(2):
            axis, step = at.steps(bool(k))[0]
            p = do(lambda w, x: dot(w, x, PLAIN).astype(bf16), cut[k][0], xs[k])
            got.append(at.along(p, axis, step))
        for k in range(2):
            kept.append(do(lambda w, x: dot(w, x, PLAIN).astype(bf16), cut[k][1], xs[k]))
        return list(zip(kept, got))

    def scatter_rest(pairs):
        for i in range(1, len(at.steps(False))):
            out = []
            for k in range(2):
                axis, step = at.steps(bool(k))[i]
                bit = (at.index(axis) // step) % 2
                send, kept = do(lambda a, b: add_split(a, b, bit.reshape(1)), *pairs[k])
                out.append((kept, at.along(send, axis, step)))
            pairs = out
        return pairs

    flying = send_products(wq_cut, [xn1[:, h] for h in halves])

    wo_parts = chip_rows(w_out, 0, S * blk, Y)
    wg_parts = chip_rows(w_up, 0, S * ffb, Y)
    wu_parts = chip_rows(w_up, Y, S * ffb, Y)
    wo_cut = [cut_weights(wo_parts, 1, blk, bool(k)) for k in range(2)]

    def positions(place):
        pos = place.reshape(S, seq) * span + (jnp.arange(seq) % span).astype(f32)[None, :]
        prow = pos.reshape(S, 1, seq)
        exponent = jnp.arange(ROTARY // 2, dtype=f32)
        inverse = 10000.0 ** (-2.0 * exponent / ROTARY)
        angles = prow * inverse[None, :, None]
        return jnp.concatenate([jnp.cos(angles), jnp.sin(angles), jnp.broadcast_to(prow, (S, 8, seq))], axis=1)

    table = do(positions, place)
    flying = scatter_rest(flying)

    qkvs, attns, attn_got, stats = [], [], [], []
    for k in range(2):
        shape = (3, heads, HEAD_DIM, H)
        qkv, attn, stat = do(attend, flying[k][0].reshape(shape), flying[k][1].reshape(shape), bias, table[seqs[k]])
        qkvs.append(qkv)
        attns.append(attn.reshape(blk, H))
        attn_got.append(at.core(attns[k]))
        stats.append(stat)
    pairs = [do(join, attns[k], attn_got[k]) for k in range(2)]
    flying = send_products(wo_cut, pairs)
    wg_cut = cut_weights(wg_parts, 1, ffb, False)
    wu_cut = cut_weights(wu_parts, 1, ffb, True)

    def gain_products(wg, wu, cols):
        terms = []
        for v in (cols[:, 2], cols[:, 3]):
            t = lax.reduce_precision(v, 8, 7)
            terms += [t, v - t]
        terms = jnp.stack(terms).astype(bf16)
        out = []
        for mine, theirs in (wg, wu):
            p = dot(terms[:, :blk], mine, LAST) + dot(terms[:, blk:], theirs, LAST)
            out.append(jnp.stack([p[0] + p[1], p[2] + p[3]]).reshape(2, Y, S, ffb))
        return jnp.concatenate(out, axis=0)

    gains = do(gain_products, wg_parts, wu_parts, pair_cols)
    gain_steps = list(at.steps(False))

    def gain_step(gains):
        axis, step = gain_steps.pop(0)
        ax = {"y": 1, "s": 2}[axis]
        bit = (at.index(axis) // step) % 2
        send = lax.dynamic_slice_in_dim(gains, (1 - bit) * step, step, ax)
        kept = lax.dynamic_slice_in_dim(gains, bit * step, step, ax)
        return kept, at.along(send, axis, step)

    flying = scatter_rest(flying)
    def residual(x, a0, b0, a1, b1):
        a, b = lanes(a0, a1), lanes(b0, b1)
        hidden = x.astype(f32) + (a.astype(f32) + b.astype(f32))
        local_mean = jnp.mean(hidden, axis=0, keepdims=True)
        dev = hidden - local_mean
        return hidden, join(local_mean, jnp.sum(dev * dev, axis=0, keepdims=True))

    hidden, moments = do(residual, x_own, *flying[0], *flying[1])
    count = blk
    for axis, step in at.steps(False) + [("core", 1)]:
        other = at.core(moments) if axis == "core" else at.along(moments, axis, step)

        def merge(a, b):
            gap = a[0:1] - b[0:1]
            return join(0.5 * (a[0:1] + b[0:1]), a[1:2] + b[1:2] + gap * gap * (count / 2.0))

        moments = do(merge, moments, other)
        count *= 2

    def second_norm(hidden, moments, cols):
        inv2 = lax.rsqrt(moments[1:2] / width + eps_norm)
        z2 = (hidden - moments[0:1]) * inv2
        return (z2 * cols[:, 2:3] + cols[:, 3:4]).astype(bf16), z2, inv2

    gains = gain_step(gains)
    xn2_own, z2, inv2 = do(second_norm, hidden, moments, own_cols)
    xn2 = do(join, xn2_own, at.core(xn2_own))

    flying = send_products([wg_cut, wu_cut], [xn2, xn2])

    wd_own = do(cast, w_down)
    wg = do(stack_turned, *wg_parts)
    wu = do(stack_turned, *wu_parts)
    grad_act = do(lambda w, c: mm(w, c, LAST, f32, tn=256), wd_own, cot_all)
    cot_cols = do(lambda c: own_columns(c, my_block.reshape(1), blk), cot_all)
    wo_own = do(cast, w_out)
    wq = do(stack_turned, *wq_parts)
    gains = do(lambda a, b: a + b, *gains)
    while gain_steps:
        gains = do(lambda a, b: a + b, *gain_step(gains))
    gains = do(lambda g: g.reshape(4, ffb).T, gains)
    flying = scatter_rest(flying)

    ggate, gup, act, sums = do(gated, *flying[0], *flying[1], grad_act, gains)

    def parts_of(count, want):
        return max(n for n in range(1, want + 1) if count % (16 * n) == 0)

    def even(count, want):
        n = parts_of(count, want)
        return [(k * (count // n), count // n) for k in range(n)]

    down_rows, up_rows = even(ffb, 2), [(0, blk)]

    def push_pairs(name, g, rows):
        for k, (at_row, count) in enumerate(rows):
            reps.push((name, "theirs", k), g[blk + at_row : blk + at_row + count])
            reps.push((name, "mine", k), g[at_row : at_row + count])

    results = {"down": None, "out": None, "up": None, "qkv": None}
    states = {
        "down": (w_down, m_down, v_down),
        "out": (w_out, m_out, v_out),
        "up": (w_up, m_up, v_up),
        "qkv": (w_qkv, m_qkv, v_qkv),
    }
    rates = {"down": 0.02, "out": 0.2, "up": 0.03, "qkv": 0.03}

    def adam(name, grads, row_first, lead, unit, rb):
        results[name] = do(
            lambda s, g, prev: adam_part(s, g, core, rates[name], prev, row_first, lead, unit, rb),
            states[name],
            grads,
            results[name],
        )

    jobs = []
    for k, (at_row, count) in enumerate(down_rows):
        jobs.append(("down", [("down", k)], at_row, 0, count, 1024))
    for name, lead in (("gate", 0), ("up", Y)):
        for k, (at_row, count) in enumerate(up_rows):
            jobs.append(("up", [(name, "mine", k), (name, "theirs", k)], at_row, lead, count, S * ffb))
    for k in range(2):
        jobs.append(("out", [("out", k)], 0, k, blk, width // 2))
    for third in (2, 1, 0):
        for k, (at_row, count) in enumerate(up_rows):
            jobs.append(
                ("qkv", [(third, "mine", k), (third, "theirs", k)], at_row, third * Y, count, S * blk)
            )
    received = {}

    def update(limit):
        for name in list(reps.done):
            if name[1] == "theirs" and name not in received:
                received[name] = at.core(reps.done[name])
        while jobs and limit and all(k in reps.done for k in jobs[0][1]):
            name, needs, at_row, lead, count, unit = jobs.pop(0)
            rb = max(n for n in range(8, min(count, 176) + 1, 8) if count % n == 0 and at_row % n == 0)
            adam(name, [received[k] if k[1] == "theirs" else reps.done[k] for k in needs], at_row, lead, unit, rb)
            limit -= 1

    def ticks(n):
        for _ in range(n):
            reps.tick()

    same_core = [
        [(2 * y + c) * S + s for y in range(Y) for s in range(S)] for c in range(2)
    ]

    def gather_core(x):
        return lax.all_gather(x, plane, axis=0, tiled=True, axis_index_groups=same_core)

    wide = 2 * FF // 8

    ggate_all = gather_core(ggate)
    gup_all = gather_core(gup)
    g_down = do(lambda a, c: mm(a, c, PLAIN, bf16, tn=512), act, cot_all)
    for k, (at_row, count) in enumerate(down_rows):
        reps.push(("down", k), g_down[at_row : at_row + count])
    ticks(1)
    out_part = do(lambda w, a: mm(w, a, FIRST, bf16, tm=512), wd_own, act)
    steps2 = at.steps(False) + [("core", 1)]

    def sum_send(sums, axis, step):
        return at.core(sums) if axis == "core" else at.along(sums, axis, step)

    def sum_step(sums, axis, step):
        return do(lambda a, b: a + b, sums, sum_send(sums, axis, step))

    for axis, step in steps2:
        sums = sum_step(sums, axis, step)
    ticks(1)
    g_gate = do(lambda x, g: mm(x, g, LAST, bf16, tn=wide), xn2, ggate_all)
    push_pairs("gate", g_gate, up_rows)
    part_gate = do(lambda w, g: mm(w, g, PLAIN, f32, tn=256), wg, ggate_all)
    ticks(2)
    part = do(lambda w, g, p: mm(w, g, PLAIN, f32, tn=256, add=p), wu, gup_all, part_gate)
    part_theirs = at.core(part[blk:])

    def branch(a, b, cot, z, scale, gain, sums):
        gxn2 = a + b
        e = gxn2 * gain
        grad_hidden = cot.astype(f32) + scale * (e - sums[0:1] / width - z * (sums[1:2] / width))
        return grad_hidden.astype(bf16), grad_hidden, gxn2

    grad_branch, grad_hidden, gxn2 = do(
        branch, part[:blk], part_theirs, cot_cols, z2, inv2, own_cols[:, 2:3], sums
    )
    gbr = lax.all_gather(grad_branch, plane, axis=0, tiled=True)
    g_up = do(lambda x, g: mm(x, g, LAST, bf16, tn=wide), xn2, gup_all)
    push_pairs("up", g_up, up_rows)
    ticks(1)
    grad_attn = do(lambda w, g: mm(w, g, PLAIN, bf16, tn=256), wo_own, gbr)

    gqkvs = []
    for k in range(2):
        dout = grad_attn[:, halves[k]].reshape(heads, HEAD_DIM, H)
        gqkvs.append(do(attend_back, qkvs[k], dout, stats[k], table[seqs[k]]).reshape(3, blk, H))
    gqkv_own = do(lambda a, b: jnp.concatenate([a, b], axis=2).reshape(3 * blk, T), *gqkvs)
    gqkv = gather_core(gqkv_own)
    ticks(1)
    attn = lanes(*attns)
    for k in range(2):
        g_out = do(lambda a, g: mm(a, g, LAST, bf16, tn=512), attn, gbr[k * width // 2 : (k + 1) * width // 2])
        reps.push(("out", k), g_out)
    update(1)
    ticks(1)
    update(1)
    ticks(1)
    gqkv = do(lambda g: g.reshape(Y * S, 3, blk, T).transpose(1, 0, 2, 3).reshape(3, Y * S * blk, T), gqkv)
    reps.depth = 2
    for third in (2, 1, 0):
        g = do(lambda x, g: mm(x, g, LAST, bf16, tn=512), xn1, gqkv[third])
        push_pairs(third, g, up_rows)
        if third == 2:
            ticks(1)
    part = do(lambda w, g: mm(w, g, PLAIN, f32, tn=256), wq, gqkv.reshape(3 * Y * S * blk, T))
    part_theirs = at.core(part[blk:])
    out_sum = lax.psum_scatter(do(lambda p: p, out_part), plane, scatter_dimension=0, tiled=True)
    ticks(1)
    update(1)

    def first_back(a, b, x, mean, inv, gain, gxn2, z2, gqkv0, gqkv1):
        gxn1 = a + b
        z1 = (x.astype(f32) - mean) * inv
        e = gxn1 * gain
        sums = join(jnp.sum(e, axis=0, keepdims=True), jnp.sum(e * z1, axis=0, keepdims=True))
        small = jnp.concatenate(
            [
                jnp.sum(gxn1 * z1, axis=1)[None],
                jnp.sum(gxn1, axis=1)[None],
                jnp.sum(gxn2 * z2, axis=1)[None],
                jnp.sum(gxn2, axis=1)[None],
                jnp.sum(gqkv0.astype(f32), axis=2) + jnp.sum(gqkv1.astype(f32), axis=2),
            ],
            axis=0,
        )
        return sums, small, gxn1, z1

    sums, small, gxn1, z1 = do(
        first_back, part[:blk], part_theirs, x_own, mean1, inv1, own_cols[:, 0:1], gxn2, z2, *gqkvs
    )
    for axis, step in steps2:
        sums = sum_step(sums, axis, step)
    ticks(1)
    input_grad = do(
        lambda h, grad, z, scale, gain, sums: h
        + scale * (grad * gain - sums[0:1] / width - z * (sums[1:2] / width)),
        grad_hidden,
        gxn1,
        z1,
        inv1,
        own_cols[:, 0:1],
        sums,
    )

    def to_rows(cols):
        split = do(lambda c: c.reshape(blk, S, at.ctx_size, rows).transpose(2, 1, 0, 3).reshape(nb, blk, rows), cols)
        got = lax.all_to_all(split, plane, split_axis=0, concat_axis=0, tiled=True)
        return do(lambda g: g.reshape(width, rows).T, got)

    input_rows = to_rows(input_grad)
    ticks(1)
    update(1)
    ticks(1)
    n_rep = lax.axis_size("rep")
    step = 1
    while step < n_rep:
        other = lax.ppermute(small, "rep", [(i, i ^ step) for i in range(n_rep)])
        small = do(lambda a, b: a + b, small, other)
        step *= 2
    update(1)
    ticks(1)
    sent = do(lambda s: jnp.broadcast_to(s.reshape(1, 7, blk), (nb, 7, blk)), small)
    small_all = lax.all_to_all(sent, plane, split_axis=0, concat_axis=0, tiled=True)

    out_cols = do(lambda h, a: (h + a.astype(f32)).astype(bf16), hidden, out_sum)
    block_output = to_rows(out_cols)
    ticks(1)
    update(1)
    ticks(1)
    update(1)

    def norm_update(every, *a):
        return adam_update(*a, every.transpose(1, 0, 2).reshape(7, width), 0.3, 0.0)

    mn, vn, wn = do(norm_update, small_all, norm_params, m_norm, v_norm)
    while reps.busy():
        reps.tick()
        update(1)
    update(len(jobs))
    return (
        (block_output.reshape(tokens.shape), input_rows.reshape(tokens.shape))
        + tuple(results["qkv"])
        + tuple(results["out"])
        + tuple(results["up"])
        + tuple(results["down"])
        + (mn, vn, wn)
    )


def solution(mesh):
    tok = P("rep", "ctx", "shard", None)
    row = P(("ctx", "shard"), None)
    placed = (tok, tok, P("rep", "shard", None)) + (row,) * 4 + (P(),) + (row,) * 8 + (P(), P())
    return jax.shard_map(
        body,
        mesh=mesh,
        in_specs=placed,
        out_specs=(tok, tok) + (row,) * 12 + (P(),) * 3,
        check_vma=False,
    )
```

```python
import functools

import jax
import jax.numpy as jnp
from jax import lax
from jax.experimental import pallas as pl
from jax.experimental.pallas import tpu as pltpu
from jax.sharding import PartitionSpec as P

HEADS = 32
HEAD_DIM = 64
FF = 5632
ROTARY = 16
STEP = 10

eps_norm = 1e-05
masked_score = -1e30
beta_one = 0.9
beta_two = 0.999
adam_eps = 1e-08
weight_decay = 0.1
score_scale = HEAD_DIM ** (-0.5)
FIRST = (((0,), (0,)), ((), ()))
LAST = (((1,), (1,)), ((), ()))
PLAIN = (((1,), (0,)), ((), ()))
bf16 = jnp.bfloat16
f32 = jnp.float32


def dot(a, b, dims):
    return lax.dot_general(a, b, dims, preferred_element_type=f32)


def adam_update(weight, moment_one, moment_two, grad, step_rate, decay_rate):
    first_new = beta_one * moment_one + (1.0 - beta_one) * grad
    second_new = beta_two * moment_two + (1.0 - beta_two) * grad * grad
    first_hat = first_new / (1.0 - beta_one**STEP)
    second_hat = second_new / (1.0 - beta_two**STEP)
    weight_new = weight - step_rate * (
        first_hat / (jnp.sqrt(second_hat) + adam_eps) + decay_rate * weight
    )
    return (first_new, second_new, weight_new)


class Plane:
    def __init__(self):
        self.s_size = lax.axis_size("shard")
        self.ctx_size = lax.axis_size("ctx")
        self.y_size = self.ctx_size // 2
        self.ctx = lax.axis_index("ctx")
        self.s = lax.axis_index("shard")
        self.y = self.ctx // 2
        self.c = self.ctx % 2
        self.blocks = self.ctx_size * self.s_size

    def core(self, x):
        return lax.ppermute(x, "ctx", [(i, i ^ 1) for i in range(self.ctx_size)])

    def along(self, x, axis, step):
        if axis == "y":
            return lax.ppermute(x, "ctx", [(i, i ^ (2 * step)) for i in range(self.ctx_size)])
        return lax.ppermute(x, "shard", [(i, i ^ step) for i in range(self.s_size)])

    def index(self, axis):
        return self.y if axis == "y" else self.s

    def steps(self, flip):
        ys = []
        k = self.y_size // 2
        while k:
            ys.append(("y", k))
            k //= 2
        ss = []
        k = self.s_size // 2
        while k:
            ss.append(("s", k))
            k //= 2
        return ys + ss if flip else ss + ys

    def chip_exchange(self, x, take):
        out = [(self.y, self.s, take(self.y, self.s))]
        for ry in range(self.y_size):
            for rs in range(self.s_size):
                if ry or rs:
                    y, s = self.y ^ ry, self.s ^ rs
                    mask = 2 * ry * self.s_size + rs
                    perm = [(i, i ^ mask) for i in range(self.blocks)]
                    out.append((y, s, lax.ppermute(take(y, s), ("ctx", "shard"), perm)))
        return out

    def sum_all(self, x):
        for axis, step in self.steps(False):
            x = x + self.along(x, axis, step)
        return x + self.core(x)

    def scatter_sum(self, p, flip):
        axes = {"y": 1, "s": 2}
        steps = self.steps(flip)
        kept = got = None
        for n, (axis, step) in enumerate(steps):
            ax = axes[axis]
            bit = (self.index(axis) // step) % 2
            kept = lax.dynamic_slice_in_dim(p, bit * step, step, ax)
            send = lax.dynamic_slice_in_dim(p, (1 - bit) * step, step, ax)
            got = self.along(send, axis, step)
            if n + 1 < len(steps):
                p = (kept.astype(f32) + got.astype(f32)).astype(bf16)
        return kept[:, 0, 0], got[:, 0, 0]

    def gather(self, p, flip):
        axes = {"y": 1, "s": 2}
        p = p[:, None, None]
        for axis, step in reversed(self.steps(flip)):
            ax = axes[axis]
            bit = (self.index(axis) // step) % 2
            got = self.along(p, axis, step)
            first = bit == 0
            p = jnp.concatenate([jnp.where(first, p, got), jnp.where(first, got, p)], ax)
        return p


class Order:
    def __init__(self):
        self.last = None

    def __call__(self, stage, *args):
        if self.last is not None:
            args, self.last = lax.optimization_barrier((args, self.last))
        out = stage(*args)
        self.last = jax.tree.leaves(out)[0]
        return out


SMALL = pl.CostEstimate(flops=1024, bytes_accessed=1024, transcendentals=0)


class RepSum:
    def __init__(self, order):
        self.order = order
        z = lax.axis_index("rep")
        self.end = (z == 0) | (z == lax.axis_size("rep") - 1)
        self.queue = []
        self.flight = []
        self.depth = 1
        self.done = {}

    def push(self, name, g):
        self.queue.append((name, g))

    def busy(self):
        return bool(self.queue or self.flight)

    def tick(self):
        old = {}
        if len(self.flight) >= self.depth or (self.flight and not self.queue):
            old = self.flight.pop(0)
        new = self.queue.pop(0) if self.queue else None
        values = {}
        if "in" in old:
            values["g"], values["g_got"] = old["in"][1], old["in_got"]
        if "mid" in old:
            values["s"], values["s_got"] = old["mid"][1], old["mid_got"]
        if new:
            values["new"] = new[1]
        both = new and "mid" in old and new[1].shape == old["mid"][1].shape
        if "out" in old:
            values["out_got"] = old["out_got"]

        def stage(v):
            def add(a, b):
                return lax.reduce_precision(a.astype(f32) + b.astype(f32), 8, 7).astype(bf16)

            out = {}
            if "g" in v:
                out["a_sum"] = add(v["g"], v["g_got"])
            if "s" in v:
                total = add(v["s"], v["s_got"])
                out["total"] = jnp.where(self.end, v["new"], total) if both else total
            if "new" in v and not both:
                out["new"] = v["new"]
            if "out_got" in v:
                out["z_got"] = v["out_got"]
            return out

        if not values:
            return
        out = self.order(stage, values)
        if "out" in old:
            self.done[old["out"][0]] = jnp.where(self.end, out["z_got"], old["out"][1])
        slot = {}
        if both:
            got = lax.ppermute(out["total"], "rep", [(0, 1), (1, 0), (2, 3), (3, 2)])
            slot = {"in": new, "in_got": got, "out": (old["mid"][0], out["total"]), "out_got": got}
        else:
            if new:
                slot["in"] = new
                slot["in_got"] = lax.ppermute(out["new"], "rep", [(0, 1), (3, 2)])
            if "mid" in old:
                slot["out"] = (old["mid"][0], out["total"])
                slot["out_got"] = lax.ppermute(out["total"], "rep", [(1, 0), (2, 3)])
        if "in" in old:
            slot["mid"] = (old["in"][0], out["a_sum"])
            slot["mid_got"] = lax.ppermute(out["a_sum"], "rep", [(1, 2), (2, 1)])
        if slot:
            self.flight.append(slot)


def cast_kernel(w_ref, out_ref):
    out_ref[...] = w_ref[...].astype(bf16)


def cast(w):
    rows, width = w.shape
    unit = max(n for n in (128, 256, 512, 1024, 1408, 2048, 2816) if width % n == 0)
    spec = pl.BlockSpec((rows, unit), lambda i: (0, i))
    return pl.pallas_call(
        cast_kernel,
        grid=(width // unit,),
        in_specs=[spec],
        out_specs=spec,
        out_shape=jax.ShapeDtypeStruct(w.shape, bf16),
        compiler_params=pltpu.CompilerParams(vmem_limit_bytes=60 * 1024 * 1024),
        cost_estimate=SMALL,
    )(w)


def own_columns_kernel(block_ref, x_ref, out_ref):
    out_ref[...] = x_ref[...].T


def own_columns(x, block, width):
    rows = x.shape[0]
    if width % 128:
        return lax.dynamic_slice_in_dim(x, block[0] * width, width, 1).T
    tile = min(rows, 512)
    return pl.pallas_call(
        own_columns_kernel,
        grid_spec=pltpu.PrefetchScalarGridSpec(
            num_scalar_prefetch=1,
            grid=(rows // tile,),
            in_specs=[pl.BlockSpec((tile, width), lambda i, block: (i, block[0]))],
            out_specs=pl.BlockSpec((width, tile), lambda i, block: (0, i)),
        ),
        out_shape=jax.ShapeDtypeStruct((width, rows), bf16),
        compiler_params=pltpu.CompilerParams(vmem_limit_bytes=60 * 1024 * 1024),
        cost_estimate=SMALL,
    )(block, x)


def split_kernel(core_ref, w_ref, mine_ref, theirs_ref):
    unit = mine_ref.shape[0]
    first = core_ref[0] == 0
    a, b = w_ref[:, :unit], w_ref[:, unit:]
    mine_ref[...] = jnp.where(first, a, b).T.astype(bf16)
    theirs_ref[...] = jnp.where(first, b, a).T.astype(bf16)


def split_columns(w, core, lead, unit, count):
    rows = w.shape[0]
    half = pl.BlockSpec((unit, rows), lambda j, core: (j, 0))
    out = jax.ShapeDtypeStruct((count * unit, rows), bf16)
    return pl.pallas_call(
        split_kernel,
        grid_spec=pltpu.PrefetchScalarGridSpec(
            num_scalar_prefetch=1,
            grid=(count,),
            in_specs=[pl.BlockSpec((rows, 2 * unit), lambda j, core: (0, lead + j))],
            out_specs=[half, half],
        ),
        out_shape=[out, out],
        compiler_params=pltpu.CompilerParams(vmem_limit_bytes=60 * 1024 * 1024),
        cost_estimate=SMALL,
    )(core, w)


def arrange_kernel(at_ref, a_ref, b_ref, c_ref, d_ref, send_ref, keep_ref):
    send_ref[...] = jnp.concatenate([a_ref[...], b_ref[...]], axis=1)
    keep_ref[...] = jnp.concatenate([c_ref[...], d_ref[...]], axis=1)


def arrange(mine, got, place, pre, y_size, s_size, unit, flip):
    r = mine.shape[1]
    half = pre * y_size * s_size // 2

    def block(i, place, keep):
        p = i % pre
        i = i // pre
        if flip:
            s, y = i % s_size, i // s_size
            bit = place[0] // (y_size // 2)
            bit = bit if keep else 1 - bit
            y = y + bit * (y_size // 2)
        else:
            y, s = i % y_size, i // y_size
            bit = place[1] // (s_size // 2)
            bit = bit if keep else 1 - bit
            s = s + bit * (s_size // 2)
        return ((p * y_size + y) * s_size + s, 0)

    def spec(keep):
        return pl.BlockSpec((unit, r), lambda i, place: block(i, place, keep))

    out = jax.ShapeDtypeStruct((half * unit, 2 * r), bf16)
    out_spec = pl.BlockSpec((unit, 2 * r), lambda i, place: (i, 0))
    return pl.pallas_call(
        arrange_kernel,
        grid_spec=pltpu.PrefetchScalarGridSpec(
            num_scalar_prefetch=1,
            grid=(half,),
            in_specs=[spec(False), spec(False), spec(True), spec(True)],
            out_specs=[out_spec, out_spec],
        ),
        out_shape=[out, out],
        compiler_params=pltpu.CompilerParams(vmem_limit_bytes=60 * 1024 * 1024),
        cost_estimate=SMALL,
    )(place, mine, got, mine, got)


def product_kernel(dims, a_ref, b_ref, *refs):
    p = dot(a_ref[...], b_ref[...], dims)
    if len(refs) == 2:
        p = p + refs[0][...]
    refs[-1][...] = p.astype(refs[-1].dtype)


def mm(a, b, dims, dtype, tm=None, tn=None, add=None):
    (ca,), (cb,) = dims[0]
    m, k, n = a.shape[1 - ca], a.shape[ca], b.shape[1 - cb]
    tm, tn = tm or m, tn or n
    a_block = [0, 0]
    a_block[ca], a_block[1 - ca] = k, tm
    b_block = [0, 0]
    b_block[cb], b_block[1 - cb] = k, tn
    out = pl.BlockSpec((tm, tn), lambda i, j: (i, j))
    return pl.pallas_call(
        functools.partial(product_kernel, dims),
        grid=(m // tm, n // tn),
        in_specs=[
            pl.BlockSpec(tuple(a_block), (lambda i, j: (0, i)) if ca == 0 else (lambda i, j: (i, 0))),
            pl.BlockSpec(tuple(b_block), (lambda i, j: (0, j)) if cb == 0 else (lambda i, j: (j, 0))),
        ]
        + ([] if add is None else [out]),
        out_specs=out,
        out_shape=jax.ShapeDtypeStruct((m, n), dtype),
        compiler_params=pltpu.CompilerParams(vmem_limit_bytes=60 * 1024 * 1024),
        cost_estimate=SMALL,
    )(*((a, b) if add is None else (a, b, add)))


def last_step_kernel(bits_ref, own0_ref, got0_ref, own1_ref, got1_ref, out_ref):
    y, s = pl.program_id(1), pl.program_id(2)
    half = own0_ref.shape[3]
    ys, ss = bits_ref[2], bits_ref[3]
    a = jnp.where(s // ss == bits_ref[1], own0_ref[0, 0], got0_ref[0, 0])
    b = jnp.where(y // ys == bits_ref[0], own1_ref[0, 0], got1_ref[0, 0])
    out_ref[0, 0, 0, :, :half] = a
    out_ref[0, 0, 0, :, half:] = b


def last_step(parts, got, bits, pre, y_size, s_size):
    rows, half = parts[0].shape[2] // pre, parts[0].shape[3]
    along_s = pl.BlockSpec((1, 1, rows, half), lambda p, y, s, bits: (y, s % (s_size // 2), p, 0))
    along_y = pl.BlockSpec((1, 1, rows, half), lambda p, y, s, bits: (y % (y_size // 2), s, p, 0))
    return pl.pallas_call(
        last_step_kernel,
        grid_spec=pltpu.PrefetchScalarGridSpec(
            num_scalar_prefetch=1,
            grid=(pre, y_size, s_size),
            in_specs=[along_s, along_s, along_y, along_y],
            out_specs=pl.BlockSpec((1, 1, 1, rows, 2 * half), lambda p, y, s, bits: (p, y, s, 0, 0)),
        ),
        out_shape=jax.ShapeDtypeStruct((pre, y_size, s_size, rows, 2 * half), bf16),
        compiler_params=pltpu.CompilerParams(vmem_limit_bytes=60 * 1024 * 1024),
        cost_estimate=SMALL,
    )(bits, parts[0], got[0], parts[1], got[1])


def stack_turned_kernel(a_ref, b_ref, out_ref):
    r = a_ref.shape[1]
    out_ref[:r] = a_ref[...].T
    out_ref[r:] = b_ref[...].T


def stack_turned(a, b):
    rows, width = a.shape
    n = max(n for n in (1, 2, 4, 6, 8, 11) if rows % (128 * n) == 0)
    spec = pl.BlockSpec((rows // n, width), lambda i: (i, 0))
    return pl.pallas_call(
        stack_turned_kernel,
        grid=(n,),
        in_specs=[spec, spec],
        out_specs=pl.BlockSpec((2 * width, rows // n), lambda i: (0, i)),
        out_shape=jax.ShapeDtypeStruct((2 * width, rows), bf16),
        compiler_params=pltpu.CompilerParams(vmem_limit_bytes=60 * 1024 * 1024),
        cost_estimate=SMALL,
    )(a, b)


def add_split_kernel(bit_ref, a_ref, b_ref, c_ref, d_ref, send_ref, keep_ref):
    send_ref[...] = (a_ref[...].astype(f32) + b_ref[...].astype(f32)).astype(bf16)
    keep_ref[...] = (c_ref[...].astype(f32) + d_ref[...].astype(f32)).astype(bf16)


def add_split(kept, got, bit):
    rows, t = kept.shape
    half = rows // 2
    n = max(n for n in (1, 2, 3, 4) if half % (16 * n) == 0)
    rb = half // n
    away = pl.BlockSpec((rb, t), lambda i, bit: ((1 - bit[0]) * n + i, 0))
    here = pl.BlockSpec((rb, t), lambda i, bit: (bit[0] * n + i, 0))
    out = jax.ShapeDtypeStruct((half, t), bf16)
    out_spec = pl.BlockSpec((rb, t), lambda i, bit: (i, 0))
    return pl.pallas_call(
        add_split_kernel,
        grid_spec=pltpu.PrefetchScalarGridSpec(
            num_scalar_prefetch=1,
            grid=(n,),
            in_specs=[away, away, here, here],
            out_specs=[out_spec, out_spec],
        ),
        out_shape=[out, out],
        compiler_params=pltpu.CompilerParams(vmem_limit_bytes=60 * 1024 * 1024),
        cost_estimate=SMALL,
    )(bit, kept, got, kept, got)


def adam_kernel(rate, two, core_ref, w_ref, m_ref, v_ref, *refs):
    grad = refs[0][...].astype(f32)
    if two:
        other = refs[1][...].astype(f32)
        mine = core_ref[0] == 0
        grad = jnp.concatenate([jnp.where(mine, grad, other), jnp.where(mine, other, grad)], axis=1)
    new_m_ref, new_v_ref, new_w_ref = refs[-3:]
    new_m, new_v, new_w = adam_update(w_ref[...], m_ref[...], v_ref[...], grad, rate, weight_decay)
    new_m_ref[...] = new_m
    new_v_ref[...] = new_v
    new_w_ref[...] = new_w


def adam_part(state, grads, core, rate, prev, row_first, lead, unit, rb):
    w, m, v = state
    two = len(grads) == 2
    rows, width = grads[0].shape
    whole = pl.BlockSpec((rb, unit * len(grads)), lambda i, g, core: (row_first // rb + i, lead + g))
    half = pl.BlockSpec((rb, unit), lambda i, g, core: (i, g))
    out = jax.ShapeDtypeStruct(w.shape, f32)
    extra, aliases = [], {}
    if prev is not None:
        extra = list(prev)
        aliases = {4 + len(grads) + i: i for i in range(3)}
    return pl.pallas_call(
        functools.partial(adam_kernel, rate, two),
        grid_spec=pltpu.PrefetchScalarGridSpec(
            num_scalar_prefetch=1,
            grid=(rows // rb, width // unit),
            in_specs=[whole] * 3 + [half] * len(grads) + [pl.BlockSpec(memory_space=pl.ANY)] * len(extra),
            out_specs=[whole] * 3,
        ),
        out_shape=[out] * 3,
        input_output_aliases=aliases,
        compiler_params=pltpu.CompilerParams(vmem_limit_bytes=60 * 1024 * 1024),
        cost_estimate=SMALL,
    )(core, w, m, v, *grads, *extra)


def attend_kernel(kept_ref, got_ref, bias_ref, table_ref, qkv_ref, out_ref, stat_ref):
    half = ROTARY // 2
    cos, sin, pos = table_ref[0, :half], table_ref[0, half:ROTARY], table_ref[0, ROTARY:]
    parts = []
    for i in range(3):
        v = kept_ref[i, 0].astype(f32) + got_ref[i, 0].astype(f32) + bias_ref[i, 0]
        if i < 2:
            a, b = v[:half], v[half:ROTARY]
            v = jnp.concatenate([a * cos - b * sin, b * cos + a * sin, v[ROTARY:]], axis=0)
        v = v.astype(bf16)
        qkv_ref[i, 0] = v
        parts.append(v)
    q, k, v = parts
    scores = dot(k, q, FIRST) * score_scale
    scores = jnp.where(pos.T[:, :1] <= pos[:1], scores, masked_score)
    peak = jnp.max(scores, axis=0, keepdims=True)
    e = jnp.exp(scores - peak)
    total = jnp.sum(e, axis=0, keepdims=True)
    p = (e / total).astype(bf16)
    out_ref[0] = dot(v, p, PLAIN).astype(bf16)
    stat_ref[0, 0] = jnp.concatenate([peak, total], axis=0)


def attend(kept, got, bias, table):
    _, heads, hd, t = kept.shape
    seqs, _, seq = table.shape
    big = pl.BlockSpec((3, 1, hd, seq), lambda s, h: (0, h, 0, s))
    table_spec = pl.BlockSpec((1, table.shape[1], seq), lambda s, h: (s, 0, 0))
    stat = pl.BlockSpec((1, 1, 2, seq), lambda s, h: (s, h, 0, 0))
    return pl.pallas_call(
        attend_kernel,
        grid=(seqs, heads),
        in_specs=[
            big,
            big,
            pl.BlockSpec((3, 1, hd, 1), lambda s, h: (0, h, 0, 0)),
            table_spec,
        ],
        out_specs=[big, pl.BlockSpec((1, hd, seq), lambda s, h: (h, 0, s)), stat],
        out_shape=[
            jax.ShapeDtypeStruct((3, heads, hd, t), bf16),
            jax.ShapeDtypeStruct((heads, hd, t), bf16),
            jax.ShapeDtypeStruct((seqs, heads, 2, seq), f32),
        ],
        compiler_params=pltpu.CompilerParams(vmem_limit_bytes=60 * 1024 * 1024),
        cost_estimate=SMALL,
    )(kept, got, bias, table)


def attend_back_kernel(qkv_ref, dout_ref, stat_ref, table_ref, out_ref):
    half = ROTARY // 2
    cos, sin, pos = table_ref[0, :half], table_ref[0, half:ROTARY], table_ref[0, ROTARY:]
    q, k, v = qkv_ref[0, 0], qkv_ref[1, 0], qkv_ref[2, 0]
    dout = dout_ref[0]
    scores = dot(k, q, FIRST) * score_scale
    scores = jnp.where(pos.T[:, :1] <= pos[:1], scores, masked_score)
    p = jnp.exp(scores - stat_ref[0, 0, :1]) / stat_ref[0, 0, 1:]
    dp = dot(v, dout, FIRST)
    inner = jnp.sum(p * dp, axis=0, keepdims=True)
    ds = (p * (dp - inner)).astype(bf16)

    def back(x):
        a, b = x[:half], x[half:ROTARY]
        return jnp.concatenate([a * cos + b * sin, b * cos - a * sin, x[ROTARY:]], axis=0)

    out_ref[0, 0] = back(dot(k, ds, PLAIN) * score_scale).astype(bf16)
    out_ref[1, 0] = back(dot(q, ds, LAST) * score_scale).astype(bf16)
    out_ref[2, 0] = dot(dout, p.astype(bf16), LAST).astype(bf16)


def attend_back(qkv, dout, stats, table):
    _, heads, hd, t = qkv.shape
    seqs, _, seq = table.shape
    big = pl.BlockSpec((3, 1, hd, seq), lambda s, h: (0, h, 0, s))
    table_spec = pl.BlockSpec((1, table.shape[1], seq), lambda s, h: (s, 0, 0))
    stat = pl.BlockSpec((1, 1, 2, seq), lambda s, h: (s, h, 0, 0))
    return pl.pallas_call(
        attend_back_kernel,
        grid=(seqs, heads),
        in_specs=[
            big,
            pl.BlockSpec((1, hd, seq), lambda s, h: (h, 0, s)),
            stat,
            table_spec,
        ],
        out_specs=big,
        out_shape=jax.ShapeDtypeStruct((3, heads, hd, t), bf16),
        compiler_params=pltpu.CompilerParams(vmem_limit_bytes=60 * 1024 * 1024),
        cost_estimate=SMALL,
    )(qkv, dout, stats, table)


def body(
    tokens,
    cotangent,
    span_order,
    w_qkv,
    w_out,
    w_up,
    w_down,
    norm_params,
    m_qkv,
    v_qkv,
    m_out,
    v_out,
    m_up,
    v_up,
    m_down,
    v_down,
    m_norm,
    v_norm,
):
    at = Plane()
    do = Order()
    reps = RepSum(do)
    width = tokens.shape[3]
    rows = tokens.shape[1]
    S, Y, nb = at.s_size, at.y_size, at.blocks
    plane = ("ctx", "shard")
    blk = width // nb
    ffb = FF // nb
    heads = blk // HEAD_DIM
    seq = rows * at.ctx_size
    T = S * seq
    H = T // 2
    first = at.c == 0
    core = at.c.reshape(1)
    my_block = at.ctx * S + at.s
    halves = (slice(0, H), slice(H, T))
    seqs = (slice(0, S // 2), slice(S // 2, S))

    def pick(x, axis, which):
        return lax.dynamic_index_in_dim(x, which, axis, keepdims=False)

    def in_order(mine, theirs, axis):
        return jnp.stack([jnp.where(first, mine, theirs), jnp.where(first, theirs, mine)], axis=axis)

    def join(a, b):
        return jnp.concatenate([a, b], axis=0)

    def lanes(a, b):
        return jnp.concatenate([a, b], axis=1)

    x_rows = tokens.reshape(rows, width)
    order = span_order.reshape(-1).astype(f32)
    span = rows // 2

    def pack(x, order):
        xf = x.astype(f32)
        mean = jnp.mean(xf, axis=1)
        centred = xf - mean[:, None]
        inv = lax.rsqrt(jnp.mean(centred * centred, axis=1) + eps_norm)
        mine = lax.dynamic_slice_in_dim(order, 2 * at.ctx, 2)
        place = jnp.repeat(mine, span)
        terms = []
        for v in (mean, inv):
            for _ in range(3):
                t = lax.reduce_precision(v, 8, 7)
                terms.append(t)
                v = v - t
        extra = jnp.stack(terms + [place] + [jnp.zeros_like(place)] * 9).astype(bf16)
        blocks = x.T.reshape(nb, blk, rows)
        return jnp.concatenate([blocks, jnp.broadcast_to(extra[None], (nb, 16, rows))], axis=1)

    packed = do(pack, x_rows, order)
    cot_all = lax.all_gather(do(cast, cotangent.reshape(rows, width)), ("shard", "ctx"), axis=0, tiled=True)
    got = lax.all_to_all(packed, plane, split_axis=0, concat_axis=0, tiled=True)

    def chip_rows(w, lead, unit, count):
        mine, theirs = do(lambda w: split_columns(w, core, lead, unit, count), w)
        return mine, at.core(theirs)

    wq_parts = chip_rows(w_qkv, 0, S * blk, 3 * Y)
    norm_cols = norm_params.reshape(7, nb, blk).transpose(1, 2, 0)
    own_cols = pick(norm_cols, 0, my_block)
    other_cols = pick(norm_cols, 0, (at.ctx ^ 1) * S + at.s)
    pair_cols = join(own_cols, other_cols)
    bias = own_cols[:, 4:7].T.reshape(3, heads, HEAD_DIM, 1)
    spot = jnp.stack([at.y, at.s])

    def cut_weights(parts, pre, unit, flip):
        return do(lambda a, b: arrange(a, b, spot, pre, Y, S, unit, flip), *parts)

    wq_cut = [cut_weights(wq_parts, 3, blk, bool(k)) for k in range(2)]

    def columns(got):
        x = got.reshape(at.ctx_size, S, blk + 16, rows).transpose(2, 1, 0, 3).reshape(blk + 16, T)
        x_own, extra = x[:blk], x[blk:].astype(f32)
        mean = extra[0:1] + extra[1:2] + extra[2:3]
        inv = extra[3:4] + extra[4:5] + extra[5:6]
        return x_own, mean, inv, extra[6:7]

    x_own, mean1, inv1, place = do(columns, got)
    x_other = at.core(x_own)

    def first_norm(mine, theirs, mean, inv, cols):
        x = join(mine, theirs).astype(f32)
        return ((x - mean) * inv * cols[:, 0:1] + cols[:, 1:2]).astype(bf16)

    xn1 = do(first_norm, x_own, x_other, mean1, inv1, pair_cols)

    def send_products(cut, xs):
        got, kept = [], []
        for k in range(2):
            axis, step = at.steps(bool(k))[0]
            p = do(lambda w, x: dot(w, x, PLAIN).astype(bf16), cut[k][0], xs[k])
            got.append(at.along(p, axis, step))
        for k in range(2):
            kept.append(do(lambda w, x: dot(w, x, PLAIN).astype(bf16), cut[k][1], xs[k]))
        return list(zip(kept, got))

    def scatter_rest(pairs):
        for i in range(1, len(at.steps(False))):
            out = []
            for k in range(2):
                axis, step = at.steps(bool(k))[i]
                bit = (at.index(axis) // step) % 2
                send, kept = do(lambda a, b: add_split(a, b, bit.reshape(1)), *pairs[k])
                out.append((kept, at.along(send, axis, step)))
            pairs = out
        return pairs

    flying = send_products(wq_cut, [xn1[:, h] for h in halves])

    wo_parts = chip_rows(w_out, 0, S * blk, Y)
    wg_parts = chip_rows(w_up, 0, S * ffb, Y)
    wu_parts = chip_rows(w_up, Y, S * ffb, Y)
    wo_cut = [cut_weights(wo_parts, 1, blk, bool(k)) for k in range(2)]

    def positions(place):
        pos = place.reshape(S, seq) * span + (jnp.arange(seq) % span).astype(f32)[None, :]
        prow = pos.reshape(S, 1, seq)
        exponent = jnp.arange(ROTARY // 2, dtype=f32)
        inverse = 10000.0 ** (-2.0 * exponent / ROTARY)
        angles = prow * inverse[None, :, None]
        return jnp.concatenate([jnp.cos(angles), jnp.sin(angles), jnp.broadcast_to(prow, (S, 8, seq))], axis=1)

    table = do(positions, place)
    flying = scatter_rest(flying)

    def gather_steps(parts, pre):
        n = len(at.steps(False))
        state = {"parts": list(parts)}

        def start(i, after=None):
            if after is not None:
                state["parts"], _ = lax.optimization_barrier((state["parts"], after))
            state["got"] = []
            state["at"] = []
            for k in range(2):
                axis, step = list(reversed(at.steps(bool(k))))[i]
                state["at"].append((axis, step))
                state["got"].append(at.along(state["parts"][k], axis, step))

        def finish():
            def put(parts, got):
                out = []
                for k in range(2):
                    axis, step = state["at"][k]
                    ax = {"y": 0, "s": 1}[axis]
                    low = (at.index(axis) // step) % 2 == 0
                    a, b = parts[k], got[k]
                    out.append(jnp.concatenate([jnp.where(low, a, b), jnp.where(low, b, a)], ax))
                return out

            state["parts"] = do(put, state["parts"], state["got"])

        def result():
            ys, ss = Y // 2, S // 2
            bits = jnp.stack([at.y // ys, at.s // ss, jnp.int32(ys), jnp.int32(ss)]).astype(jnp.int32)
            return do(lambda p, g: last_step(p, g, bits, pre, Y, S), state["parts"], state["got"])

        return n, start, finish, result

    qkvs, attns, attn_got, stats = [], [], [], []
    for k in range(2):
        shape = (3, heads, HEAD_DIM, H)
        qkv, attn, stat = do(attend, flying[k][0].reshape(shape), flying[k][1].reshape(shape), bias, table[seqs[k]])
        qkvs.append(qkv)
        attns.append(attn.reshape(blk, H))
        attn_got.append(at.core(attns[k]))
        stats.append(stat)
    pairs = [do(join, attns[k], attn_got[k]) for k in range(2)]
    flying = send_products(wo_cut, pairs)
    wg_cut = cut_weights(wg_parts, 1, ffb, False)
    wu_cut = cut_weights(wu_parts, 1, ffb, True)

    def gain_products(wg, wu, cols):
        terms = []
        for v in (cols[:, 2], cols[:, 3]):
            t = lax.reduce_precision(v, 8, 7)
            terms += [t, v - t]
        terms = jnp.stack(terms).astype(bf16)
        out = []
        for mine, theirs in (wg, wu):
            p = dot(terms[:, :blk], mine, LAST) + dot(terms[:, blk:], theirs, LAST)
            out.append(jnp.stack([p[0] + p[1], p[2] + p[3]]).reshape(2, Y, S, ffb))
        return jnp.concatenate(out, axis=0)

    gains = do(gain_products, wg_parts, wu_parts, pair_cols)
    gain_steps = list(at.steps(False))

    def gain_step(gains):
        axis, step = gain_steps.pop(0)
        ax = {"y": 1, "s": 2}[axis]
        bit = (at.index(axis) // step) % 2
        send = lax.dynamic_slice_in_dim(gains, (1 - bit) * step, step, ax)
        kept = lax.dynamic_slice_in_dim(gains, bit * step, step, ax)
        return kept, at.along(send, axis, step)

    flying = scatter_rest(flying)
    def residual(x, a0, b0, a1, b1):
        a, b = lanes(a0, a1), lanes(b0, b1)
        hidden = x.astype(f32) + (a.astype(f32) + b.astype(f32))
        local_mean = jnp.mean(hidden, axis=0, keepdims=True)
        dev = hidden - local_mean
        return hidden, join(local_mean, jnp.sum(dev * dev, axis=0, keepdims=True))

    hidden, moments = do(residual, x_own, *flying[0], *flying[1])
    count = blk
    for axis, step in at.steps(False) + [("core", 1)]:
        other = at.core(moments) if axis == "core" else at.along(moments, axis, step)

        def merge(a, b):
            gap = a[0:1] - b[0:1]
            return join(0.5 * (a[0:1] + b[0:1]), a[1:2] + b[1:2] + gap * gap * (count / 2.0))

        moments = do(merge, moments, other)
        count *= 2

    def second_norm(hidden, moments, cols):
        inv2 = lax.rsqrt(moments[1:2] / width + eps_norm)
        z2 = (hidden - moments[0:1]) * inv2
        return (z2 * cols[:, 2:3] + cols[:, 3:4]).astype(bf16), z2, inv2

    gains = gain_step(gains)
    xn2_own, z2, inv2 = do(second_norm, hidden, moments, own_cols)
    xn2 = do(join, xn2_own, at.core(xn2_own))

    flying = send_products([wg_cut, wu_cut], [xn2, xn2])

    wd_own = do(cast, w_down)
    wg = do(stack_turned, *wg_parts)
    wu = do(stack_turned, *wu_parts)
    grad_act = do(lambda w, c: mm(w, c, LAST, f32, tn=256), wd_own, cot_all)
    cot_cols = do(lambda c: own_columns(c, my_block.reshape(1), blk), cot_all)
    wo_own = do(cast, w_out)
    wq = do(stack_turned, *wq_parts)
    gains = do(lambda a, b: a + b, *gains)
    while gain_steps:
        gains = do(lambda a, b: a + b, *gain_step(gains))
    gains = do(lambda g: g.reshape(4, ffb, 1), gains)
    flying = scatter_rest(flying)

    def gated(ga, gb, ua, ub, grad_act, gains):
        gate = ga.astype(f32) + gb.astype(f32)
        up = ua.astype(f32) + ub.astype(f32)
        sig = jax.nn.sigmoid(gate)
        silu = gate * sig
        ggate = (grad_act * up * sig * (1.0 + gate * (1.0 - sig))).astype(bf16)
        gup = (grad_act * silu).astype(bf16)
        return ggate, gup, (silu * up).astype(bf16), gate, up

    ggate, gup, act, gate, up = do(gated, *flying[0], *flying[1], grad_act, gains)

    def parts_of(count, want):
        return max(n for n in range(1, want + 1) if count % (16 * n) == 0)

    def even(count, want):
        n = parts_of(count, want)
        return [(k * (count // n), count // n) for k in range(n)]

    down_rows, up_rows = even(ffb, 2), [(0, blk)]

    def push_pairs(name, g, rows):
        for k, (at_row, count) in enumerate(rows):
            reps.push((name, "theirs", k), g[blk + at_row : blk + at_row + count])
            reps.push((name, "mine", k), g[at_row : at_row + count])

    results = {"down": None, "out": None, "up": None, "qkv": None}
    states = {
        "down": (w_down, m_down, v_down),
        "out": (w_out, m_out, v_out),
        "up": (w_up, m_up, v_up),
        "qkv": (w_qkv, m_qkv, v_qkv),
    }
    rates = {"down": 0.02, "out": 0.2, "up": 0.03, "qkv": 0.03}

    def adam(name, grads, row_first, lead, unit, rb):
        results[name] = do(
            lambda s, g, prev: adam_part(s, g, core, rates[name], prev, row_first, lead, unit, rb),
            states[name],
            grads,
            results[name],
        )

    jobs = []
    for k, (at_row, count) in enumerate(down_rows):
        jobs.append(("down", [("down", k)], at_row, 0, count, 1024))
    for name, lead in (("gate", 0), ("up", Y)):
        for k, (at_row, count) in enumerate(up_rows):
            jobs.append(("up", [(name, "mine", k), (name, "theirs", k)], at_row, lead, count, S * ffb))
    for k in range(2):
        jobs.append(("out", [("out", k)], 0, k, blk, width // 2))
    for third in (2, 1, 0):
        jobs.append(("qkv", [(third, 0), (third, 1, "theirs")], 0, third * Y, blk, S * blk))
    received = {}

    def update(limit):
        for name in list(reps.done):
            if name in ("out", 0, 1, 2):
                g = reps.done.pop(name)
                half = g.shape[0] // 2
                reps.done[(name, 0)] = g[:half]
                reps.done[(name, 1) if name == "out" else (name, 1, "theirs")] = g[half:]
        for name in list(reps.done):
            if "theirs" in name and name not in received:
                received[name] = at.core(reps.done[name])
        while jobs and limit and all(k in reps.done for k in jobs[0][1]):
            name, needs, at_row, lead, count, unit = jobs.pop(0)
            rb = max(n for n in range(8, min(count, 176) + 1, 8) if count % n == 0 and at_row % n == 0)
            adam(name, [received[k] if "theirs" in k else reps.done[k] for k in needs], at_row, lead, unit, rb)
            limit -= 1

    def ticks(n):
        for _ in range(n):
            reps.tick()

    wide = 2 * FF // 8

    def quarter_heads(x):
        return [x[:, h][None, None] for h in halves]

    n, start, finish, gate_all = gather_steps(quarter_heads(ggate), 1)
    start(0)
    g_down = do(lambda a, c: mm(a, c, PLAIN, bf16, tn=512), act, cot_all)
    for k, (at_row, count) in enumerate(down_rows):
        reps.push(("down", k), g_down[at_row : at_row + count])
    ticks(1)

    def norm_sums2(ggate, gup, gate, up, gains):
        a, b = ggate.astype(f32), gup.astype(f32)
        e = jnp.sum(a * gains[0] + b * gains[2], axis=0, keepdims=True)
        ez = jnp.sum(a * (gate - gains[1]) + b * (up - gains[3]), axis=0, keepdims=True)
        return join(e, ez)

    sums = do(norm_sums2, ggate, gup, gate, up, gains)
    steps2 = at.steps(False) + [("core", 1)]

    def sum_send(sums, axis, step):
        return at.core(sums) if axis == "core" else at.along(sums, axis, step)

    def sum_step(sums, axis, step):
        return do(lambda a, b: a + b, sums, sum_send(sums, axis, step))

    tiny = list(steps2)
    sums_got = sum_send(sums, *tiny.pop(0))
    for i in range(1, n):
        finish()
        sums = do(lambda a, b: a + b, sums, sums_got)
        sums_got = sum_send(sums, *tiny.pop(0))
        start(i, sums)
        ticks(1)
    n, start_up, finish_up, up_all = gather_steps(quarter_heads(gup), 1)
    ggate_all = gate_all().reshape(Y * S * ffb, T)
    sums = do(lambda a, b: a + b, sums, sums_got)
    start_up(0, sums)
    while tiny:
        sums = sum_step(sums, *tiny.pop(0))
    g_gate = do(lambda x, g: mm(x, g, LAST, bf16, tn=wide), xn2, ggate_all)
    push_pairs("gate", g_gate, up_rows)
    finish_up()
    for i in range(1, n):
        start_up(i)
        if i == 1:
            ticks(1)
            part_gate = do(lambda w, g: mm(w, g, PLAIN, f32, tn=256), wg, ggate_all)
            out_part = do(lambda w, a: mm(w, a, FIRST, bf16, tm=512), wd_own, act)
            update(1)
        if i < n - 1:
            finish_up()
    gup_all = up_all().reshape(Y * S * ffb, T)
    part = do(lambda w, g, p: dot(w, g, PLAIN) + p, wu, gup_all, part_gate)
    part_theirs = at.core(part[blk:])
    ticks(1)

    def branch(a, b, cot, z, scale, gain, sums):
        gxn2 = a + b
        e = gxn2 * gain
        grad_hidden = cot.astype(f32) + scale * (e - sums[0:1] / width - z * (sums[1:2] / width))
        return grad_hidden.astype(bf16), grad_hidden, gxn2

    grad_branch, grad_hidden, gxn2 = do(
        branch, part[:blk], part_theirs, cot_cols, z2, inv2, own_cols[:, 2:3], sums
    )
    n, start, finish, branch_all = gather_steps(quarter_heads(grad_branch), 1)
    start(0)
    g_up = do(lambda x, g: mm(x, g, LAST, bf16, tn=wide), xn2, gup_all)
    push_pairs("up", g_up, up_rows)
    finish()
    for i in range(1, n):
        start(i)
        if i == 1:
            ticks(1)
        if i < n - 1:
            finish()
    gbr_c = branch_all()[0]
    gbr_o = at.core(gbr_c)
    gbr = do(lambda a, b: in_order(a, b, 1).reshape(width, T), gbr_c, gbr_o)
    grad_attn = do(lambda w, g: dot(w, g, PLAIN).astype(bf16), wo_own, gbr)

    gqkvs = []
    for k in range(2):
        dout = grad_attn[:, halves[k]].reshape(heads, HEAD_DIM, H)
        gqkvs.append(do(attend_back, qkvs[k], dout, stats[k], table[seqs[k]]).reshape(3, blk, H))
    n, start, finish, gqkv_done = gather_steps([g.reshape(1, 1, 3 * blk, H) for g in gqkvs], 3)
    start(0)
    attn = lanes(*attns)
    g_out = do(
        lambda a, g: join(*[mm(a, g[k * width // 2 : (k + 1) * width // 2], LAST, bf16, tn=512) for k in range(2)]),
        attn,
        gbr,
    )
    reps.push("out", g_out)
    ticks(1)
    finish()
    for i in range(1, n):
        start(i)
        if i == 1:
            update(1)
            ticks(1)
            update(1)
        if i < n - 1:
            finish()
    gqkv = gqkv_done().reshape(3, Y * S * blk, T)
    for third in (2, 1, 0):
        g = do(lambda x, g: dot(x, g, LAST).astype(bf16), xn1, gqkv[third])
        reps.push(third, g)
        if third == 2:
            ticks(1)
    part = do(lambda w, g: dot(w, g, PLAIN), wq, gqkv.reshape(3 * Y * S * blk, T))
    part_theirs = at.core(part[blk:])
    out_sum = lax.psum_scatter(out_part, plane, scatter_dimension=0, tiled=True)
    reps.depth = 2
    ticks(1)
    update(1)
    ticks(1)

    def first_back(a, b, x, mean, inv, gain, gxn2, z2, gqkv0, gqkv1):
        gxn1 = a + b
        z1 = (x.astype(f32) - mean) * inv
        e = gxn1 * gain
        sums = join(jnp.sum(e, axis=0, keepdims=True), jnp.sum(e * z1, axis=0, keepdims=True))
        small = jnp.concatenate(
            [
                jnp.sum(gxn1 * z1, axis=1)[None],
                jnp.sum(gxn1, axis=1)[None],
                jnp.sum(gxn2 * z2, axis=1)[None],
                jnp.sum(gxn2, axis=1)[None],
                jnp.sum(gqkv0.astype(f32), axis=2) + jnp.sum(gqkv1.astype(f32), axis=2),
            ],
            axis=0,
        )
        return sums, small, gxn1, z1

    sums, small, gxn1, z1 = do(
        first_back, part[:blk], part_theirs, x_own, mean1, inv1, own_cols[:, 0:1], gxn2, z2, *gqkvs
    )
    for axis, step in steps2:
        sums = sum_step(sums, axis, step)
    ticks(1)
    input_grad = do(
        lambda h, grad, z, scale, gain, sums: h
        + scale * (grad * gain - sums[0:1] / width - z * (sums[1:2] / width)),
        grad_hidden,
        gxn1,
        z1,
        inv1,
        own_cols[:, 0:1],
        sums,
    )

    def to_rows(cols):
        split = do(lambda c: c.reshape(blk, S, at.ctx_size, rows).transpose(2, 1, 0, 3).reshape(nb, blk, rows), cols)
        got = lax.all_to_all(split, plane, split_axis=0, concat_axis=0, tiled=True)
        return do(lambda g: g.reshape(width, rows).T, got)

    input_rows = to_rows(input_grad)
    ticks(1)
    update(1)
    ticks(1)
    n_rep = lax.axis_size("rep")
    step = 1
    while step < n_rep:
        other = lax.ppermute(small, "rep", [(i, i ^ step) for i in range(n_rep)])
        small = do(lambda a, b: a + b, small, other)
        step *= 2
    update(1)
    ticks(1)
    sent = do(lambda s: jnp.broadcast_to(s.reshape(1, 7, blk), (nb, 7, blk)), small)
    small_all = lax.all_to_all(sent, plane, split_axis=0, concat_axis=0, tiled=True)

    out_cols = do(lambda h, a: (h + a.astype(f32)).astype(bf16), hidden, out_sum)
    block_output = to_rows(out_cols)
    ticks(1)
    update(1)
    ticks(1)
    update(1)

    def norm_update(every, *a):
        return adam_update(*a, every.transpose(1, 0, 2).reshape(7, width), 0.3, 0.0)

    mn, vn, wn = do(norm_update, small_all, norm_params, m_norm, v_norm)
    while reps.busy():
        reps.tick()
        update(1)
    update(len(jobs))
    return (
        (block_output.reshape(tokens.shape), input_rows.reshape(tokens.shape))
        + tuple(results["qkv"])
        + tuple(results["out"])
        + tuple(results["up"])
        + tuple(results["down"])
        + (mn, vn, wn)
    )


def solution(mesh):
    tok = P("rep", "ctx", "shard", None)
    row = P(("ctx", "shard"), None)
    placed = (tok, tok, P("rep", "shard", None)) + (row,) * 4 + (P(),) + (row,) * 8 + (P(), P())
    return jax.shard_map(
        body,
        mesh=mesh,
        in_specs=placed,
        out_specs=(tok, tok) + (row,) * 12 + (P(),) * 3,
        check_vma=False,
    )
```

```python
import functools

import jax
import jax.numpy as jnp
from jax import lax
from jax.experimental import pallas as pl
from jax.experimental.pallas import tpu as pltpu
from jax.sharding import PartitionSpec as P

HEADS = 32
HEAD_DIM = 64
FF = 5632
ROTARY = 16
STEP = 10

eps_norm = 1e-05
masked_score = -1e30
beta_one = 0.9
beta_two = 0.999
adam_eps = 1e-08
weight_decay = 0.1
score_scale = HEAD_DIM ** (-0.5)
FIRST = (((0,), (0,)), ((), ()))
LAST = (((1,), (1,)), ((), ()))
PLAIN = (((1,), (0,)), ((), ()))
bf16 = jnp.bfloat16
f32 = jnp.float32


def dot(a, b, dims):
    return lax.dot_general(a, b, dims, preferred_element_type=f32)


def adam_update(weight, moment_one, moment_two, grad, step_rate, decay_rate):
    first_new = beta_one * moment_one + (1.0 - beta_one) * grad
    second_new = beta_two * moment_two + (1.0 - beta_two) * grad * grad
    first_hat = first_new / (1.0 - beta_one**STEP)
    second_hat = second_new / (1.0 - beta_two**STEP)
    weight_new = weight - step_rate * (
        first_hat / (jnp.sqrt(second_hat) + adam_eps) + decay_rate * weight
    )
    return (first_new, second_new, weight_new)


class Plane:
    def __init__(self):
        self.s_size = lax.axis_size("shard")
        self.ctx_size = lax.axis_size("ctx")
        self.y_size = self.ctx_size // 2
        self.ctx = lax.axis_index("ctx")
        self.s = lax.axis_index("shard")
        self.y = self.ctx // 2
        self.c = self.ctx % 2
        self.blocks = self.ctx_size * self.s_size

    def core(self, x):
        return lax.ppermute(x, "ctx", [(i, i ^ 1) for i in range(self.ctx_size)])

    def along(self, x, axis, step):
        if axis == "y":
            return lax.ppermute(x, "ctx", [(i, i ^ (2 * step)) for i in range(self.ctx_size)])
        return lax.ppermute(x, "shard", [(i, i ^ step) for i in range(self.s_size)])

    def index(self, axis):
        return self.y if axis == "y" else self.s

    def steps(self, flip):
        ys = []
        k = self.y_size // 2
        while k:
            ys.append(("y", k))
            k //= 2
        ss = []
        k = self.s_size // 2
        while k:
            ss.append(("s", k))
            k //= 2
        return ys + ss if flip else ss + ys

    def chip_exchange(self, x, take):
        out = [(self.y, self.s, take(self.y, self.s))]
        for ry in range(self.y_size):
            for rs in range(self.s_size):
                if ry or rs:
                    y, s = self.y ^ ry, self.s ^ rs
                    mask = 2 * ry * self.s_size + rs
                    perm = [(i, i ^ mask) for i in range(self.blocks)]
                    out.append((y, s, lax.ppermute(take(y, s), ("ctx", "shard"), perm)))
        return out

    def sum_all(self, x):
        for axis, step in self.steps(False):
            x = x + self.along(x, axis, step)
        return x + self.core(x)

    def scatter_sum(self, p, flip):
        axes = {"y": 1, "s": 2}
        steps = self.steps(flip)
        kept = got = None
        for n, (axis, step) in enumerate(steps):
            ax = axes[axis]
            bit = (self.index(axis) // step) % 2
            kept = lax.dynamic_slice_in_dim(p, bit * step, step, ax)
            send = lax.dynamic_slice_in_dim(p, (1 - bit) * step, step, ax)
            got = self.along(send, axis, step)
            if n + 1 < len(steps):
                p = (kept.astype(f32) + got.astype(f32)).astype(bf16)
        return kept[:, 0, 0], got[:, 0, 0]

    def gather(self, p, flip):
        axes = {"y": 1, "s": 2}
        p = p[:, None, None]
        for axis, step in reversed(self.steps(flip)):
            ax = axes[axis]
            bit = (self.index(axis) // step) % 2
            got = self.along(p, axis, step)
            first = bit == 0
            p = jnp.concatenate([jnp.where(first, p, got), jnp.where(first, got, p)], ax)
        return p


class Order:
    def __init__(self):
        self.last = None

    def __call__(self, stage, *args):
        if self.last is not None:
            args, self.last = lax.optimization_barrier((args, self.last))
        out = stage(*args)
        self.last = jax.tree.leaves(out)[0]
        return out


SMALL = pl.CostEstimate(flops=1024, bytes_accessed=1024, transcendentals=0)


class RepSum:
    def __init__(self, order):
        self.order = order
        z = lax.axis_index("rep")
        self.end = (z == 0) | (z == lax.axis_size("rep") - 1)
        self.queue = []
        self.flight = []
        self.depth = 1
        self.done = {}

    def push(self, name, g):
        self.queue.append((name, g))

    def busy(self):
        return bool(self.queue or self.flight)

    def tick(self):
        old = {}
        if len(self.flight) >= self.depth or (self.flight and not self.queue):
            old = self.flight.pop(0)
        new = self.queue.pop(0) if self.queue else None
        values = {}
        if "in" in old:
            values["g"], values["g_got"] = old["in"][1], old["in_got"]
        if "mid" in old:
            values["s"], values["s_got"] = old["mid"][1], old["mid_got"]
        if new:
            values["new"] = new[1]
        both = new and "mid" in old and new[1].shape == old["mid"][1].shape
        if "out" in old:
            values["out_got"] = old["out_got"]

        def stage(v):
            def add(a, b):
                return lax.reduce_precision(a.astype(f32) + b.astype(f32), 8, 7).astype(bf16)

            out = {}
            if "g" in v:
                out["a_sum"] = add(v["g"], v["g_got"])
            if "s" in v:
                total = add(v["s"], v["s_got"])
                out["total"] = jnp.where(self.end, v["new"], total) if both else total
            if "new" in v and not both:
                out["new"] = v["new"]
            if "out_got" in v:
                out["z_got"] = v["out_got"]
            return out

        if not values:
            return
        out = self.order(stage, values)
        if "out" in old:
            self.done[old["out"][0]] = jnp.where(self.end, out["z_got"], old["out"][1])
        slot = {}
        if both:
            got = lax.ppermute(out["total"], "rep", [(0, 1), (1, 0), (2, 3), (3, 2)])
            slot = {"in": new, "in_got": got, "out": (old["mid"][0], out["total"]), "out_got": got}
        else:
            if new:
                slot["in"] = new
                slot["in_got"] = lax.ppermute(out["new"], "rep", [(0, 1), (3, 2)])
            if "mid" in old:
                slot["out"] = (old["mid"][0], out["total"])
                slot["out_got"] = lax.ppermute(out["total"], "rep", [(1, 0), (2, 3)])
        if "in" in old:
            slot["mid"] = (old["in"][0], out["a_sum"])
            slot["mid_got"] = lax.ppermute(out["a_sum"], "rep", [(1, 2), (2, 1)])
        if slot:
            self.flight.append(slot)


def cast_kernel(w_ref, out_ref):
    out_ref[...] = w_ref[...].astype(bf16)


def cast(w):
    rows, width = w.shape
    unit = max(n for n in (128, 256, 512, 1024, 1408, 2048, 2816) if width % n == 0)
    spec = pl.BlockSpec((rows, unit), lambda i: (0, i))
    return pl.pallas_call(
        cast_kernel,
        grid=(width // unit,),
        in_specs=[spec],
        out_specs=spec,
        out_shape=jax.ShapeDtypeStruct(w.shape, bf16),
        compiler_params=pltpu.CompilerParams(vmem_limit_bytes=48 * 1024 * 1024),
        cost_estimate=SMALL,
    )(w)


def gated_kernel(ga_ref, gb_ref, ua_ref, ub_ref, grad_ref, gains_ref, g0_ref, g1_ref, u0_ref, u1_ref, act_ref, sums_ref):
    half = g0_ref.shape[1]
    gate = ga_ref[...].astype(f32) + gb_ref[...].astype(f32)
    up = ua_ref[...].astype(f32) + ub_ref[...].astype(f32)
    sig = jax.nn.sigmoid(gate)
    silu = gate * sig
    grad = grad_ref[...]
    act_ref[...] = (silu * up).astype(bf16)
    ggate = (grad * up * sig * (1.0 + gate * (1.0 - sig))).astype(bf16)
    gup = (grad * silu).astype(bf16)
    g0_ref[...] = ggate[:, :half]
    g1_ref[...] = ggate[:, half:]
    u0_ref[...] = gup[:, :half]
    u1_ref[...] = gup[:, half:]
    a, b = ggate.astype(f32), gup.astype(f32)
    e = jnp.sum(a * gains_ref[:, 0:1] + b * gains_ref[:, 2:3], axis=0, keepdims=True)
    ez = jnp.sum(a * (gate - gains_ref[:, 1:2]) + b * (up - gains_ref[:, 3:4]), axis=0, keepdims=True)
    both = jnp.concatenate([e, ez], axis=0)

    @pl.when(pl.program_id(0) == 0)
    def _():
        sums_ref[...] = both

    @pl.when(pl.program_id(0) > 0)
    def _():
        sums_ref[...] += both


def gated(ga, gb, ua, ub, grad_act, gains):
    rows, t = grad_act.shape
    n = max(n for n in (1, 2, 4) if rows % (16 * n) == 0)
    whole = pl.BlockSpec((rows // n, t), lambda i: (i, 0))
    half = pl.BlockSpec((rows // n, t // 2), lambda i: (i, 0))
    out_half = jax.ShapeDtypeStruct((rows, t // 2), bf16)
    return pl.pallas_call(
        gated_kernel,
        grid=(n,),
        in_specs=[whole] * 5 + [pl.BlockSpec((rows // n, 4), lambda i: (i, 0))],
        out_specs=[half] * 4 + [whole, pl.BlockSpec((2, t), lambda i: (0, 0))],
        out_shape=[out_half] * 4 + [jax.ShapeDtypeStruct((rows, t), bf16), jax.ShapeDtypeStruct((2, t), f32)],
        compiler_params=pltpu.CompilerParams(vmem_limit_bytes=56 * 1024 * 1024),
        cost_estimate=SMALL,
    )(ga, gb, ua, ub, grad_act, gains)


def own_columns_kernel(block_ref, x_ref, out_ref):
    out_ref[...] = x_ref[...].T


def own_columns(x, block, width):
    rows = x.shape[0]
    if width % 128:
        return lax.dynamic_slice_in_dim(x, block[0] * width, width, 1).T
    tile = min(rows, 512)
    return pl.pallas_call(
        own_columns_kernel,
        grid_spec=pltpu.PrefetchScalarGridSpec(
            num_scalar_prefetch=1,
            grid=(rows // tile,),
            in_specs=[pl.BlockSpec((tile, width), lambda i, block: (i, block[0]))],
            out_specs=pl.BlockSpec((width, tile), lambda i, block: (0, i)),
        ),
        out_shape=jax.ShapeDtypeStruct((width, rows), bf16),
        compiler_params=pltpu.CompilerParams(vmem_limit_bytes=48 * 1024 * 1024),
        cost_estimate=SMALL,
    )(block, x)


def split_kernel(core_ref, w_ref, mine_ref, theirs_ref):
    unit = mine_ref.shape[0]
    first = core_ref[0] == 0
    a, b = w_ref[:, :unit], w_ref[:, unit:]
    mine_ref[...] = jnp.where(first, a, b).T.astype(bf16)
    theirs_ref[...] = jnp.where(first, b, a).T.astype(bf16)


def split_columns(w, core, lead, unit, count):
    rows = w.shape[0]
    half = pl.BlockSpec((unit, rows), lambda j, core: (j, 0))
    out = jax.ShapeDtypeStruct((count * unit, rows), bf16)
    return pl.pallas_call(
        split_kernel,
        grid_spec=pltpu.PrefetchScalarGridSpec(
            num_scalar_prefetch=1,
            grid=(count,),
            in_specs=[pl.BlockSpec((rows, 2 * unit), lambda j, core: (0, lead + j))],
            out_specs=[half, half],
        ),
        out_shape=[out, out],
        compiler_params=pltpu.CompilerParams(vmem_limit_bytes=32 * 1024 * 1024),
        cost_estimate=SMALL,
    )(core, w)


def arrange_kernel(at_ref, a_ref, b_ref, c_ref, d_ref, send_ref, keep_ref):
    send_ref[...] = jnp.concatenate([a_ref[...], b_ref[...]], axis=1)
    keep_ref[...] = jnp.concatenate([c_ref[...], d_ref[...]], axis=1)


def arrange(mine, got, place, pre, y_size, s_size, unit, flip):
    r = mine.shape[1]
    half = pre * y_size * s_size // 2

    def block(i, place, keep):
        p = i % pre
        i = i // pre
        if flip:
            s, y = i % s_size, i // s_size
            bit = place[0] // (y_size // 2)
            bit = bit if keep else 1 - bit
            y = y + bit * (y_size // 2)
        else:
            y, s = i % y_size, i // y_size
            bit = place[1] // (s_size // 2)
            bit = bit if keep else 1 - bit
            s = s + bit * (s_size // 2)
        return ((p * y_size + y) * s_size + s, 0)

    def spec(keep):
        return pl.BlockSpec((unit, r), lambda i, place: block(i, place, keep))

    out = jax.ShapeDtypeStruct((half * unit, 2 * r), bf16)
    out_spec = pl.BlockSpec((unit, 2 * r), lambda i, place: (i, 0))
    return pl.pallas_call(
        arrange_kernel,
        grid_spec=pltpu.PrefetchScalarGridSpec(
            num_scalar_prefetch=1,
            grid=(half,),
            in_specs=[spec(False), spec(False), spec(True), spec(True)],
            out_specs=[out_spec, out_spec],
        ),
        out_shape=[out, out],
        compiler_params=pltpu.CompilerParams(vmem_limit_bytes=32 * 1024 * 1024),
        cost_estimate=SMALL,
    )(place, mine, got, mine, got)


def product_kernel(dims, a_ref, b_ref, *refs):
    p = dot(a_ref[...], b_ref[...], dims)
    if len(refs) == 2:
        p = p + refs[0][...]
    refs[-1][...] = p.astype(refs[-1].dtype)


def mm(a, b, dims, dtype, tm=None, tn=None, add=None):
    (ca,), (cb,) = dims[0]
    m, k, n = a.shape[1 - ca], a.shape[ca], b.shape[1 - cb]
    tm, tn = tm or m, tn or n
    a_block = [0, 0]
    a_block[ca], a_block[1 - ca] = k, tm
    b_block = [0, 0]
    b_block[cb], b_block[1 - cb] = k, tn
    out = pl.BlockSpec((tm, tn), lambda i, j: (i, j))
    return pl.pallas_call(
        functools.partial(product_kernel, dims),
        grid=(m // tm, n // tn),
        in_specs=[
            pl.BlockSpec(tuple(a_block), (lambda i, j: (0, i)) if ca == 0 else (lambda i, j: (i, 0))),
            pl.BlockSpec(tuple(b_block), (lambda i, j: (0, j)) if cb == 0 else (lambda i, j: (j, 0))),
        ]
        + ([] if add is None else [out]),
        out_specs=out,
        out_shape=jax.ShapeDtypeStruct((m, n), dtype),
        compiler_params=pltpu.CompilerParams(vmem_limit_bytes=48 * 1024 * 1024),
        cost_estimate=SMALL,
    )(*((a, b) if add is None else (a, b, add)))


def last_step_kernel(bits_ref, own0_ref, got0_ref, own1_ref, got1_ref, out_ref):
    y, s = pl.program_id(1), pl.program_id(2)
    half = own0_ref.shape[3]
    ys, ss = bits_ref[2], bits_ref[3]
    a = jnp.where(s // ss == bits_ref[1], own0_ref[0, 0], got0_ref[0, 0])
    b = jnp.where(y // ys == bits_ref[0], own1_ref[0, 0], got1_ref[0, 0])
    out_ref[0, 0, 0, :, :half] = a
    out_ref[0, 0, 0, :, half:] = b


def last_step(parts, got, bits, pre, y_size, s_size):
    rows, half = parts[0].shape[2] // pre, parts[0].shape[3]
    along_s = pl.BlockSpec((1, 1, rows, half), lambda p, y, s, bits: (y, s % (s_size // 2), p, 0))
    along_y = pl.BlockSpec((1, 1, rows, half), lambda p, y, s, bits: (y % (y_size // 2), s, p, 0))
    return pl.pallas_call(
        last_step_kernel,
        grid_spec=pltpu.PrefetchScalarGridSpec(
            num_scalar_prefetch=1,
            grid=(pre, y_size, s_size),
            in_specs=[along_s, along_s, along_y, along_y],
            out_specs=pl.BlockSpec((1, 1, 1, rows, 2 * half), lambda p, y, s, bits: (p, y, s, 0, 0)),
        ),
        out_shape=jax.ShapeDtypeStruct((pre, y_size, s_size, rows, 2 * half), bf16),
        compiler_params=pltpu.CompilerParams(vmem_limit_bytes=48 * 1024 * 1024),
        cost_estimate=SMALL,
    )(bits, parts[0], got[0], parts[1], got[1])


def stack_turned_kernel(a_ref, b_ref, out_ref):
    r = a_ref.shape[1]
    out_ref[:r] = a_ref[...].T
    out_ref[r:] = b_ref[...].T


def stack_turned(a, b):
    rows, width = a.shape
    n = max(n for n in (1, 2, 4, 6, 8, 11) if rows % (128 * n) == 0)
    spec = pl.BlockSpec((rows // n, width), lambda i: (i, 0))
    return pl.pallas_call(
        stack_turned_kernel,
        grid=(n,),
        in_specs=[spec, spec],
        out_specs=pl.BlockSpec((2 * width, rows // n), lambda i: (0, i)),
        out_shape=jax.ShapeDtypeStruct((2 * width, rows), bf16),
        compiler_params=pltpu.CompilerParams(vmem_limit_bytes=48 * 1024 * 1024),
        cost_estimate=SMALL,
    )(a, b)


def add_split_kernel(bit_ref, a_ref, b_ref, c_ref, d_ref, send_ref, keep_ref):
    send_ref[...] = (a_ref[...].astype(f32) + b_ref[...].astype(f32)).astype(bf16)
    keep_ref[...] = (c_ref[...].astype(f32) + d_ref[...].astype(f32)).astype(bf16)


def add_split(kept, got, bit):
    rows, t = kept.shape
    half = rows // 2
    n = max(n for n in (1, 2, 3, 4) if half % (16 * n) == 0)
    rb = half // n
    away = pl.BlockSpec((rb, t), lambda i, bit: ((1 - bit[0]) * n + i, 0))
    here = pl.BlockSpec((rb, t), lambda i, bit: (bit[0] * n + i, 0))
    out = jax.ShapeDtypeStruct((half, t), bf16)
    out_spec = pl.BlockSpec((rb, t), lambda i, bit: (i, 0))
    return pl.pallas_call(
        add_split_kernel,
        grid_spec=pltpu.PrefetchScalarGridSpec(
            num_scalar_prefetch=1,
            grid=(n,),
            in_specs=[away, away, here, here],
            out_specs=[out_spec, out_spec],
        ),
        out_shape=[out, out],
        compiler_params=pltpu.CompilerParams(vmem_limit_bytes=48 * 1024 * 1024),
        cost_estimate=SMALL,
    )(bit, kept, got, kept, got)


def adam_kernel(rate, two, core_ref, w_ref, m_ref, v_ref, *refs):
    grad = refs[0][...].astype(f32)
    if two:
        other = refs[1][...].astype(f32)
        mine = core_ref[0] == 0
        grad = jnp.concatenate([jnp.where(mine, grad, other), jnp.where(mine, other, grad)], axis=1)
    new_m_ref, new_v_ref, new_w_ref = refs[-3:]
    new_m, new_v, new_w = adam_update(w_ref[...], m_ref[...], v_ref[...], grad, rate, weight_decay)
    new_m_ref[...] = new_m
    new_v_ref[...] = new_v
    new_w_ref[...] = new_w


def adam_part(state, grads, core, rate, prev, row_first, lead, unit, rb):
    w, m, v = state
    two = len(grads) == 2
    rows, width = grads[0].shape
    whole = pl.BlockSpec((rb, unit * len(grads)), lambda i, g, core: (row_first // rb + i, lead + g))
    half = pl.BlockSpec((rb, unit), lambda i, g, core: (i, g))
    out = jax.ShapeDtypeStruct(w.shape, f32)
    extra, aliases = [], {}
    if prev is not None:
        extra = list(prev)
        aliases = {4 + len(grads) + i: i for i in range(3)}
    return pl.pallas_call(
        functools.partial(adam_kernel, rate, two),
        grid_spec=pltpu.PrefetchScalarGridSpec(
            num_scalar_prefetch=1,
            grid=(rows // rb, width // unit),
            in_specs=[whole] * 3 + [half] * len(grads) + [pl.BlockSpec(memory_space=pl.ANY)] * len(extra),
            out_specs=[whole] * 3,
        ),
        out_shape=[out] * 3,
        input_output_aliases=aliases,
        compiler_params=pltpu.CompilerParams(vmem_limit_bytes=48 * 1024 * 1024),
        cost_estimate=SMALL,
    )(core, w, m, v, *grads, *extra)


def attend_kernel(kept_ref, got_ref, bias_ref, table_ref, qkv_ref, out_ref, stat_ref):
    half = ROTARY // 2
    cos, sin, pos = table_ref[0, :half], table_ref[0, half:ROTARY], table_ref[0, ROTARY:]
    parts = []
    for i in range(3):
        v = kept_ref[i, 0].astype(f32) + got_ref[i, 0].astype(f32) + bias_ref[i, 0]
        if i < 2:
            a, b = v[:half], v[half:ROTARY]
            v = jnp.concatenate([a * cos - b * sin, b * cos + a * sin, v[ROTARY:]], axis=0)
        v = v.astype(bf16)
        qkv_ref[i, 0] = v
        parts.append(v)
    q, k, v = parts
    scores = dot(k, q, FIRST) * score_scale
    scores = jnp.where(pos.T[:, :1] <= pos[:1], scores, masked_score)
    peak = jnp.max(scores, axis=0, keepdims=True)
    e = jnp.exp(scores - peak)
    total = jnp.sum(e, axis=0, keepdims=True)
    p = (e / total).astype(bf16)
    out_ref[0] = dot(v, p, PLAIN).astype(bf16)
    stat_ref[0, 0] = jnp.concatenate([peak, total], axis=0)


def attend(kept, got, bias, table):
    _, heads, hd, t = kept.shape
    seqs, _, seq = table.shape
    big = pl.BlockSpec((3, 1, hd, seq), lambda s, h: (0, h, 0, s))
    table_spec = pl.BlockSpec((1, table.shape[1], seq), lambda s, h: (s, 0, 0))
    stat = pl.BlockSpec((1, 1, 2, seq), lambda s, h: (s, h, 0, 0))
    return pl.pallas_call(
        attend_kernel,
        grid=(seqs, heads),
        in_specs=[
            big,
            big,
            pl.BlockSpec((3, 1, hd, 1), lambda s, h: (0, h, 0, 0)),
            table_spec,
        ],
        out_specs=[big, pl.BlockSpec((1, hd, seq), lambda s, h: (h, 0, s)), stat],
        out_shape=[
            jax.ShapeDtypeStruct((3, heads, hd, t), bf16),
            jax.ShapeDtypeStruct((heads, hd, t), bf16),
            jax.ShapeDtypeStruct((seqs, heads, 2, seq), f32),
        ],
        compiler_params=pltpu.CompilerParams(vmem_limit_bytes=32 * 1024 * 1024),
        cost_estimate=SMALL,
    )(kept, got, bias, table)


def attend_back_kernel(qkv_ref, dout_ref, stat_ref, table_ref, out_ref):
    half = ROTARY // 2
    cos, sin, pos = table_ref[0, :half], table_ref[0, half:ROTARY], table_ref[0, ROTARY:]
    q, k, v = qkv_ref[0, 0], qkv_ref[1, 0], qkv_ref[2, 0]
    dout = dout_ref[0]
    scores = dot(k, q, FIRST) * score_scale
    scores = jnp.where(pos.T[:, :1] <= pos[:1], scores, masked_score)
    p = jnp.exp(scores - stat_ref[0, 0, :1]) / stat_ref[0, 0, 1:]
    dp = dot(v, dout, FIRST)
    inner = jnp.sum(p * dp, axis=0, keepdims=True)
    ds = (p * (dp - inner)).astype(bf16)

    def back(x):
        a, b = x[:half], x[half:ROTARY]
        return jnp.concatenate([a * cos + b * sin, b * cos - a * sin, x[ROTARY:]], axis=0)

    out_ref[0, 0] = back(dot(k, ds, PLAIN) * score_scale).astype(bf16)
    out_ref[1, 0] = back(dot(q, ds, LAST) * score_scale).astype(bf16)
    out_ref[2, 0] = dot(dout, p.astype(bf16), LAST).astype(bf16)


def attend_back(qkv, dout, stats, table):
    _, heads, hd, t = qkv.shape
    seqs, _, seq = table.shape
    big = pl.BlockSpec((3, 1, hd, seq), lambda s, h: (0, h, 0, s))
    table_spec = pl.BlockSpec((1, table.shape[1], seq), lambda s, h: (s, 0, 0))
    stat = pl.BlockSpec((1, 1, 2, seq), lambda s, h: (s, h, 0, 0))
    return pl.pallas_call(
        attend_back_kernel,
        grid=(seqs, heads),
        in_specs=[
            big,
            pl.BlockSpec((1, hd, seq), lambda s, h: (h, 0, s)),
            stat,
            table_spec,
        ],
        out_specs=big,
        out_shape=jax.ShapeDtypeStruct((3, heads, hd, t), bf16),
        compiler_params=pltpu.CompilerParams(vmem_limit_bytes=32 * 1024 * 1024),
        cost_estimate=SMALL,
    )(qkv, dout, stats, table)


def body(
    tokens,
    cotangent,
    span_order,
    w_qkv,
    w_out,
    w_up,
    w_down,
    norm_params,
    m_qkv,
    v_qkv,
    m_out,
    v_out,
    m_up,
    v_up,
    m_down,
    v_down,
    m_norm,
    v_norm,
):
    at = Plane()
    do = Order()
    reps = RepSum(do)
    width = tokens.shape[3]
    rows = tokens.shape[1]
    S, Y, nb = at.s_size, at.y_size, at.blocks
    plane = ("ctx", "shard")
    blk = width // nb
    ffb = FF // nb
    heads = blk // HEAD_DIM
    seq = rows * at.ctx_size
    T = S * seq
    H = T // 2
    first = at.c == 0
    core = at.c.reshape(1)
    my_block = at.ctx * S + at.s
    halves = (slice(0, H), slice(H, T))
    seqs = (slice(0, S // 2), slice(S // 2, S))

    def pick(x, axis, which):
        return lax.dynamic_index_in_dim(x, which, axis, keepdims=False)

    def in_order(mine, theirs, axis):
        return jnp.stack([jnp.where(first, mine, theirs), jnp.where(first, theirs, mine)], axis=axis)

    def join(a, b):
        return jnp.concatenate([a, b], axis=0)

    def lanes(a, b):
        return jnp.concatenate([a, b], axis=1)

    x_rows = tokens.reshape(rows, width)
    order = span_order.reshape(-1).astype(f32)
    span = rows // 2

    def pack(x, order):
        xf = x.astype(f32)
        mean = jnp.mean(xf, axis=1)
        centred = xf - mean[:, None]
        inv = lax.rsqrt(jnp.mean(centred * centred, axis=1) + eps_norm)
        mine = lax.dynamic_slice_in_dim(order, 2 * at.ctx, 2)
        place = jnp.repeat(mine, span)
        terms = []
        for v in (mean, inv):
            for _ in range(3):
                t = lax.reduce_precision(v, 8, 7)
                terms.append(t)
                v = v - t
        extra = jnp.stack(terms + [place] + [jnp.zeros_like(place)] * 9).astype(bf16)
        blocks = x.T.reshape(nb, blk, rows)
        return jnp.concatenate([blocks, jnp.broadcast_to(extra[None], (nb, 16, rows))], axis=1)

    packed = do(pack, x_rows, order)
    cot_all = lax.all_gather(do(cast, cotangent.reshape(rows, width)), ("shard", "ctx"), axis=0, tiled=True)
    got = lax.all_to_all(packed, plane, split_axis=0, concat_axis=0, tiled=True)

    def chip_rows(w, lead, unit, count):
        mine, theirs = do(lambda w: split_columns(w, core, lead, unit, count), w)
        return mine, at.core(theirs)

    wq_parts = chip_rows(w_qkv, 0, S * blk, 3 * Y)
    norm_cols = norm_params.reshape(7, nb, blk).transpose(1, 2, 0)
    own_cols = pick(norm_cols, 0, my_block)
    other_cols = pick(norm_cols, 0, (at.ctx ^ 1) * S + at.s)
    pair_cols = join(own_cols, other_cols)
    bias = own_cols[:, 4:7].T.reshape(3, heads, HEAD_DIM, 1)
    spot = jnp.stack([at.y, at.s])

    def cut_weights(parts, pre, unit, flip):
        return do(lambda a, b: arrange(a, b, spot, pre, Y, S, unit, flip), *parts)

    wq_cut = [cut_weights(wq_parts, 3, blk, bool(k)) for k in range(2)]

    def columns(got):
        x = got.reshape(at.ctx_size, S, blk + 16, rows).transpose(2, 1, 0, 3).reshape(blk + 16, T)
        x_own, extra = x[:blk], x[blk:].astype(f32)
        mean = extra[0:1] + extra[1:2] + extra[2:3]
        inv = extra[3:4] + extra[4:5] + extra[5:6]
        return x_own, mean, inv, extra[6:7]

    x_own, mean1, inv1, place = do(columns, got)
    x_other = at.core(x_own)

    def first_norm(mine, theirs, mean, inv, cols):
        x = join(mine, theirs).astype(f32)
        return ((x - mean) * inv * cols[:, 0:1] + cols[:, 1:2]).astype(bf16)

    xn1 = do(first_norm, x_own, x_other, mean1, inv1, pair_cols)

    def send_products(cut, xs):
        got, kept = [], []
        for k in range(2):
            axis, step = at.steps(bool(k))[0]
            p = do(lambda w, x: dot(w, x, PLAIN).astype(bf16), cut[k][0], xs[k])
            got.append(at.along(p, axis, step))
        for k in range(2):
            kept.append(do(lambda w, x: dot(w, x, PLAIN).astype(bf16), cut[k][1], xs[k]))
        return list(zip(kept, got))

    def scatter_rest(pairs):
        for i in range(1, len(at.steps(False))):
            out = []
            for k in range(2):
                axis, step = at.steps(bool(k))[i]
                bit = (at.index(axis) // step) % 2
                send, kept = do(lambda a, b: add_split(a, b, bit.reshape(1)), *pairs[k])
                out.append((kept, at.along(send, axis, step)))
            pairs = out
        return pairs

    flying = send_products(wq_cut, [xn1[:, h] for h in halves])

    wo_parts = chip_rows(w_out, 0, S * blk, Y)
    wg_parts = chip_rows(w_up, 0, S * ffb, Y)
    wu_parts = chip_rows(w_up, Y, S * ffb, Y)
    wo_cut = [cut_weights(wo_parts, 1, blk, bool(k)) for k in range(2)]

    def positions(place):
        pos = place.reshape(S, seq) * span + (jnp.arange(seq) % span).astype(f32)[None, :]
        prow = pos.reshape(S, 1, seq)
        exponent = jnp.arange(ROTARY // 2, dtype=f32)
        inverse = 10000.0 ** (-2.0 * exponent / ROTARY)
        angles = prow * inverse[None, :, None]
        return jnp.concatenate([jnp.cos(angles), jnp.sin(angles), jnp.broadcast_to(prow, (S, 8, seq))], axis=1)

    table = do(positions, place)
    flying = scatter_rest(flying)

    def gather_steps(parts, pre):
        n = len(at.steps(False))
        state = {"parts": list(parts)}

        def start(i, after=None):
            if after is not None:
                state["parts"], _ = lax.optimization_barrier((state["parts"], after))
            state["got"] = []
            state["at"] = []
            for k in range(2):
                axis, step = list(reversed(at.steps(bool(k))))[i]
                state["at"].append((axis, step))
                state["got"].append(at.along(state["parts"][k], axis, step))

        def finish():
            def put(parts, got):
                out = []
                for k in range(2):
                    axis, step = state["at"][k]
                    ax = {"y": 0, "s": 1}[axis]
                    low = (at.index(axis) // step) % 2 == 0
                    a, b = parts[k], got[k]
                    out.append(jnp.concatenate([jnp.where(low, a, b), jnp.where(low, b, a)], ax))
                return out

            state["parts"] = do(put, state["parts"], state["got"])

        def result():
            ys, ss = Y // 2, S // 2
            bits = jnp.stack([at.y // ys, at.s // ss, jnp.int32(ys), jnp.int32(ss)]).astype(jnp.int32)
            return do(lambda p, g: last_step(p, g, bits, pre, Y, S), state["parts"], state["got"])

        return n, start, finish, result

    qkvs, attns, attn_got, stats = [], [], [], []
    for k in range(2):
        shape = (3, heads, HEAD_DIM, H)
        qkv, attn, stat = do(attend, flying[k][0].reshape(shape), flying[k][1].reshape(shape), bias, table[seqs[k]])
        qkvs.append(qkv)
        attns.append(attn.reshape(blk, H))
        attn_got.append(at.core(attns[k]))
        stats.append(stat)
    pairs = [do(join, attns[k], attn_got[k]) for k in range(2)]
    flying = send_products(wo_cut, pairs)
    wg_cut = cut_weights(wg_parts, 1, ffb, False)
    wu_cut = cut_weights(wu_parts, 1, ffb, True)

    def gain_products(wg, wu, cols):
        terms = []
        for v in (cols[:, 2], cols[:, 3]):
            t = lax.reduce_precision(v, 8, 7)
            terms += [t, v - t]
        terms = jnp.stack(terms).astype(bf16)
        out = []
        for mine, theirs in (wg, wu):
            p = dot(terms[:, :blk], mine, LAST) + dot(terms[:, blk:], theirs, LAST)
            out.append(jnp.stack([p[0] + p[1], p[2] + p[3]]).reshape(2, Y, S, ffb))
        return jnp.concatenate(out, axis=0)

    gains = do(gain_products, wg_parts, wu_parts, pair_cols)
    gain_steps = list(at.steps(False))

    def gain_step(gains):
        axis, step = gain_steps.pop(0)
        ax = {"y": 1, "s": 2}[axis]
        bit = (at.index(axis) // step) % 2
        send = lax.dynamic_slice_in_dim(gains, (1 - bit) * step, step, ax)
        kept = lax.dynamic_slice_in_dim(gains, bit * step, step, ax)
        return kept, at.along(send, axis, step)

    flying = scatter_rest(flying)
    def residual(x, a0, b0, a1, b1):
        a, b = lanes(a0, a1), lanes(b0, b1)
        hidden = x.astype(f32) + (a.astype(f32) + b.astype(f32))
        local_mean = jnp.mean(hidden, axis=0, keepdims=True)
        dev = hidden - local_mean
        return hidden, join(local_mean, jnp.sum(dev * dev, axis=0, keepdims=True))

    hidden, moments = do(residual, x_own, *flying[0], *flying[1])
    count = blk
    for axis, step in at.steps(False) + [("core", 1)]:
        other = at.core(moments) if axis == "core" else at.along(moments, axis, step)

        def merge(a, b):
            gap = a[0:1] - b[0:1]
            return join(0.5 * (a[0:1] + b[0:1]), a[1:2] + b[1:2] + gap * gap * (count / 2.0))

        moments = do(merge, moments, other)
        count *= 2

    def second_norm(hidden, moments, cols):
        inv2 = lax.rsqrt(moments[1:2] / width + eps_norm)
        z2 = (hidden - moments[0:1]) * inv2
        return (z2 * cols[:, 2:3] + cols[:, 3:4]).astype(bf16), z2, inv2

    gains = gain_step(gains)
    xn2_own, z2, inv2 = do(second_norm, hidden, moments, own_cols)
    xn2 = do(join, xn2_own, at.core(xn2_own))

    flying = send_products([wg_cut, wu_cut], [xn2, xn2])

    wd_own = do(cast, w_down)
    wg = do(stack_turned, *wg_parts)
    wu = do(stack_turned, *wu_parts)
    grad_act = do(lambda w, c: mm(w, c, LAST, f32, tn=256), wd_own, cot_all)
    cot_cols = do(lambda c: own_columns(c, my_block.reshape(1), blk), cot_all)
    wo_own = do(cast, w_out)
    wq = do(stack_turned, *wq_parts)
    gains = do(lambda a, b: a + b, *gains)
    while gain_steps:
        gains = do(lambda a, b: a + b, *gain_step(gains))
    gains = do(lambda g: g.reshape(4, ffb).T, gains)
    flying = scatter_rest(flying)

    gate0, gate1, up0, up1, act, sums = do(gated, *flying[0], *flying[1], grad_act, gains)

    def parts_of(count, want):
        return max(n for n in range(1, want + 1) if count % (16 * n) == 0)

    def even(count, want):
        n = parts_of(count, want)
        return [(k * (count // n), count // n) for k in range(n)]

    down_rows, up_rows = even(ffb, 2), [(0, blk)]

    def push_pairs(name, g, rows):
        for k, (at_row, count) in enumerate(rows):
            reps.push((name, "theirs", k), g[blk + at_row : blk + at_row + count])
            reps.push((name, "mine", k), g[at_row : at_row + count])

    results = {"down": None, "out": None, "up": None, "qkv": None}
    states = {
        "down": (w_down, m_down, v_down),
        "out": (w_out, m_out, v_out),
        "up": (w_up, m_up, v_up),
        "qkv": (w_qkv, m_qkv, v_qkv),
    }
    rates = {"down": 0.02, "out": 0.2, "up": 0.03, "qkv": 0.03}

    def adam(name, grads, row_first, lead, unit, rb):
        results[name] = do(
            lambda s, g, prev: adam_part(s, g, core, rates[name], prev, row_first, lead, unit, rb),
            states[name],
            grads,
            results[name],
        )

    jobs = []
    for k, (at_row, count) in enumerate(down_rows):
        jobs.append(("down", [("down", k)], at_row, 0, count, 1024))
    for name, lead in (("gate", 0), ("up", Y)):
        for k, (at_row, count) in enumerate(up_rows):
            jobs.append(("up", [(name, "mine", k), (name, "theirs", k)], at_row, lead, count, S * ffb))
    for k in range(2):
        jobs.append(("out", [("out", k)], 0, k, blk, width // 2))
    for third in (2, 1, 0):
        jobs.append(("qkv", [(third, 0), (third, 1, "theirs")], 0, third * Y, blk, S * blk))
    received = {}

    def update(limit):
        for name in list(reps.done):
            if name in ("out", 0, 1, 2):
                g = reps.done.pop(name)
                half = g.shape[0] // 2
                reps.done[(name, 0)] = g[:half]
                reps.done[(name, 1) if name == "out" else (name, 1, "theirs")] = g[half:]
        for name in list(reps.done):
            if "theirs" in name and name not in received:
                received[name] = at.core(reps.done[name])
        while jobs and limit and all(k in reps.done for k in jobs[0][1]):
            name, needs, at_row, lead, count, unit = jobs.pop(0)
            rb = max(n for n in range(8, min(count, 176) + 1, 8) if count % n == 0 and at_row % n == 0)
            adam(name, [received[k] if "theirs" in k else reps.done[k] for k in needs], at_row, lead, unit, rb)
            limit -= 1

    def ticks(n):
        for _ in range(n):
            reps.tick()

    wide = 2 * FF // 8

    def quarter_heads(x):
        return [x[:, h][None, None] for h in halves]

    n, start, finish, gate_all = gather_steps([gate0[None, None], gate1[None, None]], 1)
    start(0)
    g_down = do(lambda a, c: mm(a, c, PLAIN, bf16, tn=512), act, cot_all)
    for k, (at_row, count) in enumerate(down_rows):
        reps.push(("down", k), g_down[at_row : at_row + count])
    ticks(1)

    steps2 = at.steps(False) + [("core", 1)]

    def sum_send(sums, axis, step):
        return at.core(sums) if axis == "core" else at.along(sums, axis, step)

    def sum_step(sums, axis, step):
        return do(lambda a, b: a + b, sums, sum_send(sums, axis, step))

    tiny = list(steps2)
    sums_got = sum_send(sums, *tiny.pop(0))
    for i in range(1, n):
        finish()
        sums = do(lambda a, b: a + b, sums, sums_got)
        sums_got = sum_send(sums, *tiny.pop(0))
        start(i, sums)
        ticks(1)
    n, start_up, finish_up, up_all = gather_steps([up0[None, None], up1[None, None]], 1)
    ggate_all = gate_all().reshape(Y * S * ffb, T)
    sums = do(lambda a, b: a + b, sums, sums_got)
    start_up(0, sums)
    while tiny:
        sums = sum_step(sums, *tiny.pop(0))
    g_gate = do(lambda x, g: mm(x, g, LAST, bf16, tn=wide), xn2, ggate_all)
    push_pairs("gate", g_gate, up_rows)
    finish_up()
    for i in range(1, n):
        start_up(i)
        if i == 1:
            ticks(1)
            part_gate = do(lambda w, g: mm(w, g, PLAIN, f32, tn=256), wg, ggate_all)
            out_part = do(lambda w, a: mm(w, a, FIRST, bf16, tm=512), wd_own, act)
        if i < n - 1:
            finish_up()
    gup_all = up_all().reshape(Y * S * ffb, T)
    part = do(lambda w, g, p: dot(w, g, PLAIN) + p, wu, gup_all, part_gate)
    part_theirs = at.core(part[blk:])
    ticks(1)

    def branch(a, b, cot, z, scale, gain, sums):
        gxn2 = a + b
        e = gxn2 * gain
        grad_hidden = cot.astype(f32) + scale * (e - sums[0:1] / width - z * (sums[1:2] / width))
        return grad_hidden.astype(bf16), grad_hidden, gxn2

    grad_branch, grad_hidden, gxn2 = do(
        branch, part[:blk], part_theirs, cot_cols, z2, inv2, own_cols[:, 2:3], sums
    )
    n, start, finish, branch_all = gather_steps(quarter_heads(grad_branch), 1)
    start(0)
    g_up = do(lambda x, g: mm(x, g, LAST, bf16, tn=wide), xn2, gup_all)
    push_pairs("up", g_up, up_rows)
    finish()
    for i in range(1, n):
        start(i)
        if i == 1:
            update(1)
            ticks(1)
        if i < n - 1:
            finish()
    gbr_c = branch_all()[0]
    gbr_o = at.core(gbr_c)
    gbr = do(lambda a, b: in_order(a, b, 1).reshape(width, T), gbr_c, gbr_o)
    grad_attn = do(lambda w, g: dot(w, g, PLAIN).astype(bf16), wo_own, gbr)

    gqkvs = []
    for k in range(2):
        dout = grad_attn[:, halves[k]].reshape(heads, HEAD_DIM, H)
        gqkvs.append(do(attend_back, qkvs[k], dout, stats[k], table[seqs[k]]).reshape(3, blk, H))
    n, start, finish, gqkv_done = gather_steps([g.reshape(1, 1, 3 * blk, H) for g in gqkvs], 3)
    start(0)
    attn = lanes(*attns)
    g_out = do(
        lambda a, g: join(*[mm(a, g[k * width // 2 : (k + 1) * width // 2], LAST, bf16, tn=512) for k in range(2)]),
        attn,
        gbr,
    )
    reps.push("out", g_out)
    update(1)
    ticks(1)
    finish()
    for i in range(1, n):
        start(i)
        if i == 1:
            update(1)
            ticks(1)
            update(1)
        if i < n - 1:
            finish()
    gqkv = gqkv_done().reshape(3, Y * S * blk, T)
    out_sum = lax.psum_scatter(do(lambda p: p, out_part), plane, scatter_dimension=0, tiled=True)
    for third in (2, 1, 0):
        g = do(lambda x, g: dot(x, g, LAST).astype(bf16), xn1, gqkv[third])
        reps.push(third, g)
        if third == 2:
            ticks(1)
    part = do(lambda w, g: dot(w, g, PLAIN), wq, gqkv.reshape(3 * Y * S * blk, T))
    part_theirs = at.core(part[blk:])

    def first_back(a, b, x, mean, inv, gain, gxn2, z2, gqkv0, gqkv1):
        gxn1 = a + b
        z1 = (x.astype(f32) - mean) * inv
        e = gxn1 * gain
        sums = join(jnp.sum(e, axis=0, keepdims=True), jnp.sum(e * z1, axis=0, keepdims=True))
        small = jnp.concatenate(
            [
                jnp.sum(gxn1 * z1, axis=1)[None],
                jnp.sum(gxn1, axis=1)[None],
                jnp.sum(gxn2 * z2, axis=1)[None],
                jnp.sum(gxn2, axis=1)[None],
                jnp.sum(gqkv0.astype(f32), axis=2) + jnp.sum(gqkv1.astype(f32), axis=2),
            ],
            axis=0,
        )
        return sums, small, gxn1, z1

    sums, small, gxn1, z1 = do(
        first_back, part[:blk], part_theirs, x_own, mean1, inv1, own_cols[:, 0:1], gxn2, z2, *gqkvs
    )
    for axis, step in steps2:
        sums = sum_step(sums, axis, step)
    ticks(1)
    input_grad = do(
        lambda h, grad, z, scale, gain, sums: (
            h + scale * (grad * gain - sums[0:1] / width - z * (sums[1:2] / width))
        ).astype(bf16),
        grad_hidden,
        gxn1,
        z1,
        inv1,
        own_cols[:, 0:1],
        sums,
    )

    def to_rows(cols):
        split = do(lambda c: c.reshape(blk, S, at.ctx_size, rows).transpose(2, 1, 0, 3).reshape(nb, blk, rows), cols)
        got = lax.all_to_all(split, plane, split_axis=0, concat_axis=0, tiled=True)
        return do(lambda g: g.reshape(width, rows).T, got)

    input_rows = to_rows(input_grad).astype(f32)
    update(1)
    ticks(1)
    n_rep = lax.axis_size("rep")
    step = 1
    while step < n_rep:
        other = lax.ppermute(small, "rep", [(i, i ^ step) for i in range(n_rep)])
        small = do(lambda a, b: a + b, small, other)
        step *= 2
    sent = do(lambda s: jnp.broadcast_to(s.reshape(1, 7, blk), (nb, 7, blk)), small)
    small_all = lax.all_to_all(sent, plane, split_axis=0, concat_axis=0, tiled=True)

    def norm_update(every, *a):
        return adam_update(*a, every.transpose(1, 0, 2).reshape(7, width), 0.3, 0.0)

    mn, vn, wn = do(norm_update, small_all, norm_params, m_norm, v_norm)
    update(1)
    ticks(1)
    update(2)
    ticks(1)
    update(1)
    out_cols = do(lambda h, a: (h + a.astype(f32)).astype(bf16), hidden, out_sum)
    block_output = to_rows(out_cols)
    while reps.busy():
        reps.tick()
        update(2)
    update(len(jobs))
    return (
        (block_output.reshape(tokens.shape), input_rows.reshape(tokens.shape))
        + tuple(results["qkv"])
        + tuple(results["out"])
        + tuple(results["up"])
        + tuple(results["down"])
        + (mn, vn, wn)
    )


def solution(mesh):
    tok = P("rep", "ctx", "shard", None)
    row = P(("ctx", "shard"), None)
    placed = (tok, tok, P("rep", "shard", None)) + (row,) * 4 + (P(),) + (row,) * 8 + (P(), P())
    return jax.shard_map(
        body,
        mesh=mesh,
        in_specs=placed,
        out_specs=(tok, tok) + (row,) * 12 + (P(),) * 3,
        check_vma=False,
    )
```

```python
import functools

import jax
import jax.numpy as jnp
from jax import lax
from jax.experimental import pallas as pl
from jax.experimental.pallas import tpu as pltpu
from jax.sharding import PartitionSpec as P

HEADS = 32
HEAD_DIM = 64
FF = 5632
ROTARY = 16
STEP = 10

eps_norm = 1e-05
masked_score = -1e30
beta_one = 0.9
beta_two = 0.999
adam_eps = 1e-08
weight_decay = 0.1
score_scale = HEAD_DIM ** (-0.5)
FIRST = (((0,), (0,)), ((), ()))
LAST = (((1,), (1,)), ((), ()))
PLAIN = (((1,), (0,)), ((), ()))
bf16 = jnp.bfloat16
f32 = jnp.float32


def dot(a, b, dims):
    return lax.dot_general(a, b, dims, preferred_element_type=f32)


def adam_update(weight, moment_one, moment_two, grad, step_rate, decay_rate):
    first_new = beta_one * moment_one + (1.0 - beta_one) * grad
    second_new = beta_two * moment_two + (1.0 - beta_two) * grad * grad
    first_hat = first_new / (1.0 - beta_one**STEP)
    second_hat = second_new / (1.0 - beta_two**STEP)
    weight_new = weight - step_rate * (
        first_hat / (jnp.sqrt(second_hat) + adam_eps) + decay_rate * weight
    )
    return (first_new, second_new, weight_new)


class Plane:
    def __init__(self):
        self.s_size = lax.axis_size("shard")
        self.ctx_size = lax.axis_size("ctx")
        self.y_size = self.ctx_size // 2
        self.ctx = lax.axis_index("ctx")
        self.s = lax.axis_index("shard")
        self.y = self.ctx // 2
        self.c = self.ctx % 2
        self.blocks = self.ctx_size * self.s_size

    def core(self, x):
        return lax.ppermute(x, "ctx", [(i, i ^ 1) for i in range(self.ctx_size)])

    def along(self, x, axis, step):
        if axis == "y":
            return lax.ppermute(x, "ctx", [(i, i ^ (2 * step)) for i in range(self.ctx_size)])
        return lax.ppermute(x, "shard", [(i, i ^ step) for i in range(self.s_size)])

    def index(self, axis):
        return self.y if axis == "y" else self.s

    def steps(self, flip):
        ys = []
        k = self.y_size // 2
        while k:
            ys.append(("y", k))
            k //= 2
        ss = []
        k = self.s_size // 2
        while k:
            ss.append(("s", k))
            k //= 2
        return ys + ss if flip else ss + ys

    def chip_exchange(self, x, take):
        out = [(self.y, self.s, take(self.y, self.s))]
        for ry in range(self.y_size):
            for rs in range(self.s_size):
                if ry or rs:
                    y, s = self.y ^ ry, self.s ^ rs
                    mask = 2 * ry * self.s_size + rs
                    perm = [(i, i ^ mask) for i in range(self.blocks)]
                    out.append((y, s, lax.ppermute(take(y, s), ("ctx", "shard"), perm)))
        return out

    def sum_all(self, x):
        for axis, step in self.steps(False):
            x = x + self.along(x, axis, step)
        return x + self.core(x)

    def scatter_sum(self, p, flip):
        axes = {"y": 1, "s": 2}
        steps = self.steps(flip)
        kept = got = None
        for n, (axis, step) in enumerate(steps):
            ax = axes[axis]
            bit = (self.index(axis) // step) % 2
            kept = lax.dynamic_slice_in_dim(p, bit * step, step, ax)
            send = lax.dynamic_slice_in_dim(p, (1 - bit) * step, step, ax)
            got = self.along(send, axis, step)
            if n + 1 < len(steps):
                p = (kept.astype(f32) + got.astype(f32)).astype(bf16)
        return kept[:, 0, 0], got[:, 0, 0]

    def gather(self, p, flip):
        axes = {"y": 1, "s": 2}
        p = p[:, None, None]
        for axis, step in reversed(self.steps(flip)):
            ax = axes[axis]
            bit = (self.index(axis) // step) % 2
            got = self.along(p, axis, step)
            first = bit == 0
            p = jnp.concatenate([jnp.where(first, p, got), jnp.where(first, got, p)], ax)
        return p


class Order:
    def __init__(self):
        self.token = lax.create_token()

    def __call__(self, stage, *args):
        args, token = lax.optimization_barrier((args, self.token))
        out, self.token = lax.optimization_barrier((stage(*args), token))
        return out


SMALL = pl.CostEstimate(flops=1024, bytes_accessed=1024, transcendentals=0)


class RepSum:
    def __init__(self, order):
        self.order = order
        z = lax.axis_index("rep")
        self.end = (z == 0) | (z == lax.axis_size("rep") - 1)
        self.queue = []
        self.flight = []
        self.depth = 1
        self.done = {}

    def push(self, name, g):
        self.queue.append((name, g))

    def busy(self):
        return bool(self.queue or self.flight)

    def tick(self):
        old = {}
        if len(self.flight) >= self.depth or (self.flight and not self.queue):
            old = self.flight.pop(0)
        new = self.queue.pop(0) if self.queue else None
        values = {}
        if "in" in old:
            values["g"], values["g_got"] = old["in"][1], old["in_got"]
        if "mid" in old:
            values["s"], values["s_got"] = old["mid"][1], old["mid_got"]
        if new:
            values["new"] = new[1]
        both = new and "mid" in old and new[1].shape == old["mid"][1].shape
        if "out" in old:
            values["out_got"] = old["out_got"]

        def stage(v):
            def add(a, b):
                return lax.reduce_precision(a.astype(f32) + b.astype(f32), 8, 7).astype(bf16)

            out = {}
            if "g" in v:
                out["a_sum"] = add(v["g"], v["g_got"])
            if "s" in v:
                total = add(v["s"], v["s_got"])
                out["total"] = jnp.where(self.end, v["new"], total) if both else total
            if "new" in v and not both:
                out["new"] = v["new"]
            if "out_got" in v:
                out["z_got"] = v["out_got"]
            return out

        if not values:
            return
        out = self.order(stage, values)
        if "out" in old:
            self.done[old["out"][0]] = jnp.where(self.end, out["z_got"], old["out"][1])
        slot = {}
        if both:
            got = lax.ppermute(out["total"], "rep", [(0, 1), (1, 0), (2, 3), (3, 2)])
            slot = {"in": new, "in_got": got, "out": (old["mid"][0], out["total"]), "out_got": got}
        else:
            if new:
                slot["in"] = new
                slot["in_got"] = lax.ppermute(out["new"], "rep", [(0, 1), (3, 2)])
            if "mid" in old:
                slot["out"] = (old["mid"][0], out["total"])
                slot["out_got"] = lax.ppermute(out["total"], "rep", [(1, 0), (2, 3)])
        if "in" in old:
            slot["mid"] = (old["in"][0], out["a_sum"])
            slot["mid_got"] = lax.ppermute(out["a_sum"], "rep", [(1, 2), (2, 1)])
        if slot:
            self.flight.append(slot)


def cast_kernel(w_ref, out_ref):
    out_ref[...] = w_ref[...].astype(bf16)


def cast(w):
    rows, width = w.shape
    unit = max(n for n in (128, 256, 512, 1024, 1408, 2048, 2816) if width % n == 0)
    spec = pl.BlockSpec((rows, unit), lambda i: (0, i))
    return pl.pallas_call(
        cast_kernel,
        grid=(width // unit,),
        in_specs=[spec],
        out_specs=spec,
        out_shape=jax.ShapeDtypeStruct(w.shape, bf16),
        compiler_params=pltpu.CompilerParams(vmem_limit_bytes=48 * 1024 * 1024),
        cost_estimate=SMALL,
    )(w)


def gated_kernel(ga_ref, gb_ref, ua_ref, ub_ref, grad_ref, gains_ref, g0_ref, g1_ref, u0_ref, u1_ref, act_ref, sums_ref):
    half = g0_ref.shape[1]
    gate = ga_ref[...].astype(f32) + gb_ref[...].astype(f32)
    up = ua_ref[...].astype(f32) + ub_ref[...].astype(f32)
    sig = jax.nn.sigmoid(gate)
    silu = gate * sig
    grad = grad_ref[...]
    act_ref[...] = (silu * up).astype(bf16)
    ggate = (grad * up * sig * (1.0 + gate * (1.0 - sig))).astype(bf16)
    gup = (grad * silu).astype(bf16)
    g0_ref[...] = ggate[:, :half]
    g1_ref[...] = ggate[:, half:]
    u0_ref[...] = gup[:, :half]
    u1_ref[...] = gup[:, half:]
    a, b = ggate.astype(f32), gup.astype(f32)
    e = jnp.sum(a * gains_ref[:, 0:1] + b * gains_ref[:, 2:3], axis=0, keepdims=True)
    ez = jnp.sum(a * (gate - gains_ref[:, 1:2]) + b * (up - gains_ref[:, 3:4]), axis=0, keepdims=True)
    both = jnp.concatenate([e, ez], axis=0)

    @pl.when(pl.program_id(0) == 0)
    def _():
        sums_ref[...] = both

    @pl.when(pl.program_id(0) > 0)
    def _():
        sums_ref[...] += both


def gated(ga, gb, ua, ub, grad_act, gains):
    rows, t = grad_act.shape
    n = max(n for n in (1, 2, 4) if rows % (16 * n) == 0)
    whole = pl.BlockSpec((rows // n, t), lambda i: (i, 0))
    half = pl.BlockSpec((rows // n, t // 2), lambda i: (i, 0))
    out_half = jax.ShapeDtypeStruct((rows, t // 2), bf16)
    return pl.pallas_call(
        gated_kernel,
        grid=(n,),
        in_specs=[whole] * 5 + [pl.BlockSpec((rows // n, 4), lambda i: (i, 0))],
        out_specs=[half] * 4 + [whole, pl.BlockSpec((2, t), lambda i: (0, 0))],
        out_shape=[out_half] * 4 + [jax.ShapeDtypeStruct((rows, t), bf16), jax.ShapeDtypeStruct((2, t), f32)],
        compiler_params=pltpu.CompilerParams(vmem_limit_bytes=56 * 1024 * 1024),
        cost_estimate=SMALL,
    )(ga, gb, ua, ub, grad_act, gains)


def own_columns_kernel(block_ref, x_ref, out_ref):
    out_ref[...] = x_ref[...].T


def own_columns(x, block, width):
    rows = x.shape[0]
    if width % 128:
        return lax.dynamic_slice_in_dim(x, block[0] * width, width, 1).T
    tile = min(rows, 512)
    return pl.pallas_call(
        own_columns_kernel,
        grid_spec=pltpu.PrefetchScalarGridSpec(
            num_scalar_prefetch=1,
            grid=(rows // tile,),
            in_specs=[pl.BlockSpec((tile, width), lambda i, block: (i, block[0]))],
            out_specs=pl.BlockSpec((width, tile), lambda i, block: (0, i)),
        ),
        out_shape=jax.ShapeDtypeStruct((width, rows), bf16),
        compiler_params=pltpu.CompilerParams(vmem_limit_bytes=48 * 1024 * 1024),
        cost_estimate=SMALL,
    )(block, x)


def split_kernel(core_ref, w_ref, mine_ref, theirs_ref):
    unit = mine_ref.shape[0]
    first = core_ref[0] == 0
    a, b = w_ref[:, :unit], w_ref[:, unit:]
    mine_ref[...] = jnp.where(first, a, b).T.astype(bf16)
    theirs_ref[...] = jnp.where(first, b, a).T.astype(bf16)


def split_columns(w, core, lead, unit, count):
    rows = w.shape[0]
    half = pl.BlockSpec((unit, rows), lambda j, core: (j, 0))
    out = jax.ShapeDtypeStruct((count * unit, rows), bf16)
    return pl.pallas_call(
        split_kernel,
        grid_spec=pltpu.PrefetchScalarGridSpec(
            num_scalar_prefetch=1,
            grid=(count,),
            in_specs=[pl.BlockSpec((rows, 2 * unit), lambda j, core: (0, lead + j))],
            out_specs=[half, half],
        ),
        out_shape=[out, out],
        compiler_params=pltpu.CompilerParams(vmem_limit_bytes=32 * 1024 * 1024),
        cost_estimate=SMALL,
    )(core, w)


def arrange_kernel(at_ref, a_ref, b_ref, c_ref, d_ref, send_ref, keep_ref):
    send_ref[...] = jnp.concatenate([a_ref[...], b_ref[...]], axis=1)
    keep_ref[...] = jnp.concatenate([c_ref[...], d_ref[...]], axis=1)


def arrange(mine, got, place, pre, y_size, s_size, unit, flip):
    r = mine.shape[1]
    half = pre * y_size * s_size // 2

    def block(i, place, keep):
        p = i % pre
        i = i // pre
        if flip:
            s, y = i % s_size, i // s_size
            bit = place[0] // (y_size // 2)
            bit = bit if keep else 1 - bit
            y = y + bit * (y_size // 2)
        else:
            y, s = i % y_size, i // y_size
            bit = place[1] // (s_size // 2)
            bit = bit if keep else 1 - bit
            s = s + bit * (s_size // 2)
        return ((p * y_size + y) * s_size + s, 0)

    def spec(keep):
        return pl.BlockSpec((unit, r), lambda i, place: block(i, place, keep))

    out = jax.ShapeDtypeStruct((half * unit, 2 * r), bf16)
    out_spec = pl.BlockSpec((unit, 2 * r), lambda i, place: (i, 0))
    return pl.pallas_call(
        arrange_kernel,
        grid_spec=pltpu.PrefetchScalarGridSpec(
            num_scalar_prefetch=1,
            grid=(half,),
            in_specs=[spec(False), spec(False), spec(True), spec(True)],
            out_specs=[out_spec, out_spec],
        ),
        out_shape=[out, out],
        compiler_params=pltpu.CompilerParams(vmem_limit_bytes=32 * 1024 * 1024),
        cost_estimate=SMALL,
    )(place, mine, got, mine, got)


def product_kernel(dims, a_ref, b_ref, *refs):
    p = dot(a_ref[...], b_ref[...], dims)
    if len(refs) == 2:
        p = p + refs[0][...]
    refs[-1][...] = p.astype(refs[-1].dtype)


def mm(a, b, dims, dtype, tm=None, tn=None, add=None):
    (ca,), (cb,) = dims[0]
    m, k, n = a.shape[1 - ca], a.shape[ca], b.shape[1 - cb]
    tm, tn = tm or m, tn or n
    a_block = [0, 0]
    a_block[ca], a_block[1 - ca] = k, tm
    b_block = [0, 0]
    b_block[cb], b_block[1 - cb] = k, tn
    out = pl.BlockSpec((tm, tn), lambda i, j: (i, j))
    return pl.pallas_call(
        functools.partial(product_kernel, dims),
        grid=(m // tm, n // tn),
        in_specs=[
            pl.BlockSpec(tuple(a_block), (lambda i, j: (0, i)) if ca == 0 else (lambda i, j: (i, 0))),
            pl.BlockSpec(tuple(b_block), (lambda i, j: (0, j)) if cb == 0 else (lambda i, j: (j, 0))),
        ]
        + ([] if add is None else [out]),
        out_specs=out,
        out_shape=jax.ShapeDtypeStruct((m, n), dtype),
        compiler_params=pltpu.CompilerParams(vmem_limit_bytes=48 * 1024 * 1024),
        cost_estimate=SMALL,
    )(*((a, b) if add is None else (a, b, add)))


def last_step_kernel(bits_ref, own0_ref, got0_ref, own1_ref, got1_ref, out_ref):
    y, s = pl.program_id(1), pl.program_id(2)
    half = own0_ref.shape[3]
    ys, ss = bits_ref[2], bits_ref[3]
    a = jnp.where(s // ss == bits_ref[1], own0_ref[0, 0], got0_ref[0, 0])
    b = jnp.where(y // ys == bits_ref[0], own1_ref[0, 0], got1_ref[0, 0])
    out_ref[0, 0, 0, :, :half] = a
    out_ref[0, 0, 0, :, half:] = b


def last_step(parts, got, bits, pre, y_size, s_size):
    rows, half = parts[0].shape[2] // pre, parts[0].shape[3]
    along_s = pl.BlockSpec((1, 1, rows, half), lambda p, y, s, bits: (y, s % (s_size // 2), p, 0))
    along_y = pl.BlockSpec((1, 1, rows, half), lambda p, y, s, bits: (y % (y_size // 2), s, p, 0))
    return pl.pallas_call(
        last_step_kernel,
        grid_spec=pltpu.PrefetchScalarGridSpec(
            num_scalar_prefetch=1,
            grid=(pre, y_size, s_size),
            in_specs=[along_s, along_s, along_y, along_y],
            out_specs=pl.BlockSpec((1, 1, 1, rows, 2 * half), lambda p, y, s, bits: (p, y, s, 0, 0)),
        ),
        out_shape=jax.ShapeDtypeStruct((pre, y_size, s_size, rows, 2 * half), bf16),
        compiler_params=pltpu.CompilerParams(vmem_limit_bytes=48 * 1024 * 1024),
        cost_estimate=SMALL,
    )(bits, parts[0], got[0], parts[1], got[1])


def stack_turned_kernel(a_ref, b_ref, out_ref):
    r = a_ref.shape[1]
    out_ref[:r] = a_ref[...].T
    out_ref[r:] = b_ref[...].T


def stack_turned(a, b):
    rows, width = a.shape
    n = max(n for n in (1, 2, 4, 6, 8, 11) if rows % (128 * n) == 0)
    spec = pl.BlockSpec((rows // n, width), lambda i: (i, 0))
    return pl.pallas_call(
        stack_turned_kernel,
        grid=(n,),
        in_specs=[spec, spec],
        out_specs=pl.BlockSpec((2 * width, rows // n), lambda i: (0, i)),
        out_shape=jax.ShapeDtypeStruct((2 * width, rows), bf16),
        compiler_params=pltpu.CompilerParams(vmem_limit_bytes=48 * 1024 * 1024),
        cost_estimate=SMALL,
    )(a, b)


def add_split_kernel(bit_ref, a_ref, b_ref, c_ref, d_ref, send_ref, keep_ref):
    send_ref[...] = (a_ref[...].astype(f32) + b_ref[...].astype(f32)).astype(bf16)
    keep_ref[...] = (c_ref[...].astype(f32) + d_ref[...].astype(f32)).astype(bf16)


def add_split(kept, got, bit):
    rows, t = kept.shape
    half = rows // 2
    n = max(n for n in (1, 2, 3, 4) if half % (16 * n) == 0)
    rb = half // n
    away = pl.BlockSpec((rb, t), lambda i, bit: ((1 - bit[0]) * n + i, 0))
    here = pl.BlockSpec((rb, t), lambda i, bit: (bit[0] * n + i, 0))
    out = jax.ShapeDtypeStruct((half, t), bf16)
    out_spec = pl.BlockSpec((rb, t), lambda i, bit: (i, 0))
    return pl.pallas_call(
        add_split_kernel,
        grid_spec=pltpu.PrefetchScalarGridSpec(
            num_scalar_prefetch=1,
            grid=(n,),
            in_specs=[away, away, here, here],
            out_specs=[out_spec, out_spec],
        ),
        out_shape=[out, out],
        compiler_params=pltpu.CompilerParams(vmem_limit_bytes=48 * 1024 * 1024),
        cost_estimate=SMALL,
    )(bit, kept, got, kept, got)


def adam_kernel(rate, two, core_ref, w_ref, m_ref, v_ref, *refs):
    grad = refs[0][...].astype(f32)
    if two:
        other = refs[1][...].astype(f32)
        mine = core_ref[0] == 0
        grad = jnp.concatenate([jnp.where(mine, grad, other), jnp.where(mine, other, grad)], axis=1)
    new_m_ref, new_v_ref, new_w_ref = refs[-3:]
    new_m, new_v, new_w = adam_update(w_ref[...], m_ref[...], v_ref[...], grad, rate, weight_decay)
    new_m_ref[...] = new_m
    new_v_ref[...] = new_v
    new_w_ref[...] = new_w


def adam_part(state, grads, core, rate, prev, row_first, lead, unit, rb):
    w, m, v = state
    two = len(grads) == 2
    rows, width = grads[0].shape
    whole = pl.BlockSpec((rb, unit * len(grads)), lambda i, g, core: (row_first // rb + i, lead + g))
    half = pl.BlockSpec((rb, unit), lambda i, g, core: (i, g))
    out = jax.ShapeDtypeStruct(w.shape, f32)
    extra, aliases = [], {}
    if prev is not None:
        extra = list(prev)
        aliases = {4 + len(grads) + i: i for i in range(3)}
    return pl.pallas_call(
        functools.partial(adam_kernel, rate, two),
        grid_spec=pltpu.PrefetchScalarGridSpec(
            num_scalar_prefetch=1,
            grid=(rows // rb, width // unit),
            in_specs=[whole] * 3 + [half] * len(grads) + [pl.BlockSpec(memory_space=pl.ANY)] * len(extra),
            out_specs=[whole] * 3,
        ),
        out_shape=[out] * 3,
        input_output_aliases=aliases,
        compiler_params=pltpu.CompilerParams(vmem_limit_bytes=48 * 1024 * 1024),
        cost_estimate=SMALL,
    )(core, w, m, v, *grads, *extra)


def attend_kernel(kept_ref, got_ref, bias_ref, table_ref, qkv_ref, out_ref, stat_ref):
    half = ROTARY // 2
    cos, sin, pos = table_ref[0, :half], table_ref[0, half:ROTARY], table_ref[0, ROTARY:]
    parts = []
    for i in range(3):
        v = kept_ref[i, 0].astype(f32) + got_ref[i, 0].astype(f32) + bias_ref[i, 0]
        if i < 2:
            a, b = v[:half], v[half:ROTARY]
            v = jnp.concatenate([a * cos - b * sin, b * cos + a * sin, v[ROTARY:]], axis=0)
        v = v.astype(bf16)
        qkv_ref[i, 0] = v
        parts.append(v)
    q, k, v = parts
    scores = dot(k, q, FIRST) * score_scale
    scores = jnp.where(pos.T[:, :1] <= pos[:1], scores, masked_score)
    peak = jnp.max(scores, axis=0, keepdims=True)
    e = jnp.exp(scores - peak)
    total = jnp.sum(e, axis=0, keepdims=True)
    p = (e / total).astype(bf16)
    out_ref[0] = dot(v, p, PLAIN).astype(bf16)
    stat_ref[0, 0] = jnp.concatenate([peak, total], axis=0)


def attend(kept, got, bias, table):
    _, heads, hd, t = kept.shape
    seqs, _, seq = table.shape
    big = pl.BlockSpec((3, 1, hd, seq), lambda s, h: (0, h, 0, s))
    table_spec = pl.BlockSpec((1, table.shape[1], seq), lambda s, h: (s, 0, 0))
    stat = pl.BlockSpec((1, 1, 2, seq), lambda s, h: (s, h, 0, 0))
    return pl.pallas_call(
        attend_kernel,
        grid=(seqs, heads),
        in_specs=[
            big,
            big,
            pl.BlockSpec((3, 1, hd, 1), lambda s, h: (0, h, 0, 0)),
            table_spec,
        ],
        out_specs=[big, pl.BlockSpec((1, hd, seq), lambda s, h: (h, 0, s)), stat],
        out_shape=[
            jax.ShapeDtypeStruct((3, heads, hd, t), bf16),
            jax.ShapeDtypeStruct((heads, hd, t), bf16),
            jax.ShapeDtypeStruct((seqs, heads, 2, seq), f32),
        ],
        compiler_params=pltpu.CompilerParams(vmem_limit_bytes=32 * 1024 * 1024),
        cost_estimate=SMALL,
    )(kept, got, bias, table)


def attend_back_kernel(qkv_ref, dout_ref, stat_ref, table_ref, out_ref):
    half = ROTARY // 2
    cos, sin, pos = table_ref[0, :half], table_ref[0, half:ROTARY], table_ref[0, ROTARY:]
    q, k, v = qkv_ref[0, 0], qkv_ref[1, 0], qkv_ref[2, 0]
    dout = dout_ref[0]
    scores = dot(k, q, FIRST) * score_scale
    scores = jnp.where(pos.T[:, :1] <= pos[:1], scores, masked_score)
    p = jnp.exp(scores - stat_ref[0, 0, :1]) / stat_ref[0, 0, 1:]
    dp = dot(v, dout, FIRST)
    inner = jnp.sum(p * dp, axis=0, keepdims=True)
    ds = (p * (dp - inner)).astype(bf16)

    def back(x):
        a, b = x[:half], x[half:ROTARY]
        return jnp.concatenate([a * cos + b * sin, b * cos - a * sin, x[ROTARY:]], axis=0)

    out_ref[0, 0] = back(dot(k, ds, PLAIN) * score_scale).astype(bf16)
    out_ref[1, 0] = back(dot(q, ds, LAST) * score_scale).astype(bf16)
    out_ref[2, 0] = dot(dout, p.astype(bf16), LAST).astype(bf16)


def attend_back(qkv, dout, stats, table):
    _, heads, hd, t = qkv.shape
    seqs, _, seq = table.shape
    big = pl.BlockSpec((3, 1, hd, seq), lambda s, h: (0, h, 0, s))
    table_spec = pl.BlockSpec((1, table.shape[1], seq), lambda s, h: (s, 0, 0))
    stat = pl.BlockSpec((1, 1, 2, seq), lambda s, h: (s, h, 0, 0))
    return pl.pallas_call(
        attend_back_kernel,
        grid=(seqs, heads),
        in_specs=[
            big,
            pl.BlockSpec((1, hd, seq), lambda s, h: (h, 0, s)),
            stat,
            table_spec,
        ],
        out_specs=big,
        out_shape=jax.ShapeDtypeStruct((3, heads, hd, t), bf16),
        compiler_params=pltpu.CompilerParams(vmem_limit_bytes=32 * 1024 * 1024),
        cost_estimate=SMALL,
    )(qkv, dout, stats, table)


def body(
    tokens,
    cotangent,
    span_order,
    w_qkv,
    w_out,
    w_up,
    w_down,
    norm_params,
    m_qkv,
    v_qkv,
    m_out,
    v_out,
    m_up,
    v_up,
    m_down,
    v_down,
    m_norm,
    v_norm,
):
    at = Plane()
    do = Order()
    reps = RepSum(do)
    width = tokens.shape[3]
    rows = tokens.shape[1]
    S, Y, nb = at.s_size, at.y_size, at.blocks
    plane = ("ctx", "shard")
    blk = width // nb
    ffb = FF // nb
    heads = blk // HEAD_DIM
    seq = rows * at.ctx_size
    T = S * seq
    H = T // 2
    first = at.c == 0
    core = at.c.reshape(1)
    my_block = at.ctx * S + at.s
    halves = (slice(0, H), slice(H, T))
    seqs = (slice(0, S // 2), slice(S // 2, S))

    def pick(x, axis, which):
        return lax.dynamic_index_in_dim(x, which, axis, keepdims=False)

    def in_order(mine, theirs, axis):
        return jnp.stack([jnp.where(first, mine, theirs), jnp.where(first, theirs, mine)], axis=axis)

    def join(a, b):
        return jnp.concatenate([a, b], axis=0)

    def lanes(a, b):
        return jnp.concatenate([a, b], axis=1)

    x_rows = tokens.reshape(rows, width)
    order = span_order.reshape(-1).astype(f32)
    span = rows // 2

    def pack(x, order):
        xf = x.astype(f32)
        mean = jnp.mean(xf, axis=1)
        centred = xf - mean[:, None]
        inv = lax.rsqrt(jnp.mean(centred * centred, axis=1) + eps_norm)
        mine = lax.dynamic_slice_in_dim(order, 2 * at.ctx, 2)
        place = jnp.repeat(mine, span)
        terms = []
        for v in (mean, inv):
            for _ in range(3):
                t = lax.reduce_precision(v, 8, 7)
                terms.append(t)
                v = v - t
        extra = jnp.stack(terms + [place] + [jnp.zeros_like(place)] * 9).astype(bf16)
        blocks = x.T.reshape(nb, blk, rows)
        return jnp.concatenate([blocks, jnp.broadcast_to(extra[None], (nb, 16, rows))], axis=1)

    packed = do(pack, x_rows, order)
    cot_all = lax.all_gather(do(cast, cotangent.reshape(rows, width)), ("shard", "ctx"), axis=0, tiled=True)
    got = lax.all_to_all(packed, plane, split_axis=0, concat_axis=0, tiled=True)

    def chip_rows(w, lead, unit, count):
        mine, theirs = do(lambda w: split_columns(w, core, lead, unit, count), w)
        return mine, at.core(theirs)

    wq_parts = chip_rows(w_qkv, 0, S * blk, 3 * Y)
    norm_cols = norm_params.reshape(7, nb, blk).transpose(1, 2, 0)
    own_cols = pick(norm_cols, 0, my_block)
    other_cols = pick(norm_cols, 0, (at.ctx ^ 1) * S + at.s)
    pair_cols = join(own_cols, other_cols)
    bias = own_cols[:, 4:7].T.reshape(3, heads, HEAD_DIM, 1)
    spot = jnp.stack([at.y, at.s])

    def cut_weights(parts, pre, unit, flip):
        return do(lambda a, b: arrange(a, b, spot, pre, Y, S, unit, flip), *parts)

    wq_cut = [cut_weights(wq_parts, 3, blk, bool(k)) for k in range(2)]

    def columns(got):
        x = got.reshape(at.ctx_size, S, blk + 16, rows).transpose(2, 1, 0, 3).reshape(blk + 16, T)
        x_own, extra = x[:blk], x[blk:].astype(f32)
        mean = extra[0:1] + extra[1:2] + extra[2:3]
        inv = extra[3:4] + extra[4:5] + extra[5:6]
        return x_own, mean, inv, extra[6:7]

    x_own, mean1, inv1, place = do(columns, got)
    x_other = at.core(x_own)

    def first_norm(mine, theirs, mean, inv, cols):
        x = join(mine, theirs).astype(f32)
        return ((x - mean) * inv * cols[:, 0:1] + cols[:, 1:2]).astype(bf16)

    xn1 = do(first_norm, x_own, x_other, mean1, inv1, pair_cols)

    def send_products(cut, xs):
        got, kept = [], []
        for k in range(2):
            axis, step = at.steps(bool(k))[0]
            p = do(lambda w, x: dot(w, x, PLAIN).astype(bf16), cut[k][0], xs[k])
            got.append(at.along(p, axis, step))
        for k in range(2):
            kept.append(do(lambda w, x: dot(w, x, PLAIN).astype(bf16), cut[k][1], xs[k]))
        return list(zip(kept, got))

    def scatter_rest(pairs):
        for i in range(1, len(at.steps(False))):
            out = []
            for k in range(2):
                axis, step = at.steps(bool(k))[i]
                bit = (at.index(axis) // step) % 2
                send, kept = do(lambda a, b: add_split(a, b, bit.reshape(1)), *pairs[k])
                out.append((kept, at.along(send, axis, step)))
            pairs = out
        return pairs

    flying = send_products(wq_cut, [xn1[:, h] for h in halves])

    wo_parts = chip_rows(w_out, 0, S * blk, Y)
    wg_parts = chip_rows(w_up, 0, S * ffb, Y)
    wu_parts = chip_rows(w_up, Y, S * ffb, Y)
    wo_cut = [cut_weights(wo_parts, 1, blk, bool(k)) for k in range(2)]

    def positions(place):
        pos = place.reshape(S, seq) * span + (jnp.arange(seq) % span).astype(f32)[None, :]
        prow = pos.reshape(S, 1, seq)
        exponent = jnp.arange(ROTARY // 2, dtype=f32)
        inverse = 10000.0 ** (-2.0 * exponent / ROTARY)
        angles = prow * inverse[None, :, None]
        return jnp.concatenate([jnp.cos(angles), jnp.sin(angles), jnp.broadcast_to(prow, (S, 8, seq))], axis=1)

    table = do(positions, place)
    flying = scatter_rest(flying)

    def gather_steps(parts, pre):
        n = len(at.steps(False))
        state = {"parts": list(parts)}

        def start(i, after=None):
            if after is not None:
                state["parts"], _ = lax.optimization_barrier((state["parts"], after))
            state["got"] = []
            state["at"] = []
            for k in range(2):
                axis, step = list(reversed(at.steps(bool(k))))[i]
                state["at"].append((axis, step))
                state["got"].append(at.along(state["parts"][k], axis, step))

        def finish():
            def put(parts, got):
                out = []
                for k in range(2):
                    axis, step = state["at"][k]
                    ax = {"y": 0, "s": 1}[axis]
                    low = (at.index(axis) // step) % 2 == 0
                    a, b = parts[k], got[k]
                    out.append(jnp.concatenate([jnp.where(low, a, b), jnp.where(low, b, a)], ax))
                return out

            state["parts"] = do(put, state["parts"], state["got"])

        def result():
            ys, ss = Y // 2, S // 2
            bits = jnp.stack([at.y // ys, at.s // ss, jnp.int32(ys), jnp.int32(ss)]).astype(jnp.int32)
            return do(lambda p, g: last_step(p, g, bits, pre, Y, S), state["parts"], state["got"])

        return n, start, finish, result

    qkvs, attns, attn_got, stats = [], [], [], []
    for k in range(2):
        shape = (3, heads, HEAD_DIM, H)
        qkv, attn, stat = do(attend, flying[k][0].reshape(shape), flying[k][1].reshape(shape), bias, table[seqs[k]])
        qkvs.append(qkv)
        attns.append(attn.reshape(blk, H))
        attn_got.append(at.core(attns[k]))
        stats.append(stat)
    pairs = [do(join, attns[k], attn_got[k]) for k in range(2)]
    flying = send_products(wo_cut, pairs)
    wg_cut = cut_weights(wg_parts, 1, ffb, False)
    wu_cut = cut_weights(wu_parts, 1, ffb, True)

    def gain_products(wg, wu, cols):
        terms = []
        for v in (cols[:, 2], cols[:, 3]):
            t = lax.reduce_precision(v, 8, 7)
            terms += [t, v - t]
        terms = jnp.stack(terms).astype(bf16)
        out = []
        for mine, theirs in (wg, wu):
            p = dot(terms[:, :blk], mine, LAST) + dot(terms[:, blk:], theirs, LAST)
            out.append(jnp.stack([p[0] + p[1], p[2] + p[3]]).reshape(2, Y, S, ffb))
        return jnp.concatenate(out, axis=0)

    gains = do(gain_products, wg_parts, wu_parts, pair_cols)
    gain_steps = list(at.steps(False))

    def gain_step(gains):
        axis, step = gain_steps.pop(0)
        ax = {"y": 1, "s": 2}[axis]
        bit = (at.index(axis) // step) % 2
        send = lax.dynamic_slice_in_dim(gains, (1 - bit) * step, step, ax)
        kept = lax.dynamic_slice_in_dim(gains, bit * step, step, ax)
        return kept, at.along(send, axis, step)

    flying = scatter_rest(flying)
    def residual(x, a0, b0, a1, b1):
        a, b = lanes(a0, a1), lanes(b0, b1)
        hidden = x.astype(f32) + (a.astype(f32) + b.astype(f32))
        local_mean = jnp.mean(hidden, axis=0, keepdims=True)
        dev = hidden - local_mean
        return hidden, join(local_mean, jnp.sum(dev * dev, axis=0, keepdims=True))

    hidden, moments = do(residual, x_own, *flying[0], *flying[1])
    count = blk
    for axis, step in at.steps(False) + [("core", 1)]:
        other = at.core(moments) if axis == "core" else at.along(moments, axis, step)

        def merge(a, b):
            gap = a[0:1] - b[0:1]
            return join(0.5 * (a[0:1] + b[0:1]), a[1:2] + b[1:2] + gap * gap * (count / 2.0))

        moments = do(merge, moments, other)
        count *= 2

    def second_norm(hidden, moments, cols):
        inv2 = lax.rsqrt(moments[1:2] / width + eps_norm)
        z2 = (hidden - moments[0:1]) * inv2
        return (z2 * cols[:, 2:3] + cols[:, 3:4]).astype(bf16), z2, inv2

    gains = gain_step(gains)
    xn2_own, z2, inv2 = do(second_norm, hidden, moments, own_cols)
    xn2 = do(join, xn2_own, at.core(xn2_own))

    flying = send_products([wg_cut, wu_cut], [xn2, xn2])

    wd_own = do(cast, w_down)
    wg = do(stack_turned, *wg_parts)
    wu = do(stack_turned, *wu_parts)
    grad_act = do(lambda w, c: mm(w, c, LAST, f32, tn=256), wd_own, cot_all)
    cot_cols = do(lambda c: own_columns(c, my_block.reshape(1), blk), cot_all)
    wo_own = do(cast, w_out)
    wq = do(stack_turned, *wq_parts)
    gains = do(lambda a, b: a + b, *gains)
    while gain_steps:
        gains = do(lambda a, b: a + b, *gain_step(gains))
    gains = do(lambda g: g.reshape(4, ffb).T, gains)
    flying = scatter_rest(flying)

    gate0, gate1, up0, up1, act, sums = do(gated, *flying[0], *flying[1], grad_act, gains)

    def parts_of(count, want):
        return max(n for n in range(1, want + 1) if count % (16 * n) == 0)

    def even(count, want):
        n = parts_of(count, want)
        return [(k * (count // n), count // n) for k in range(n)]

    down_rows, up_rows = even(ffb, 2), [(0, blk)]

    def push_pairs(name, g, rows):
        for k, (at_row, count) in enumerate(rows):
            reps.push((name, "theirs", k), g[blk + at_row : blk + at_row + count])
            reps.push((name, "mine", k), g[at_row : at_row + count])

    results = {"down": None, "out": None, "up": None, "qkv": None}
    states = {
        "down": (w_down, m_down, v_down),
        "out": (w_out, m_out, v_out),
        "up": (w_up, m_up, v_up),
        "qkv": (w_qkv, m_qkv, v_qkv),
    }
    rates = {"down": 0.02, "out": 0.2, "up": 0.03, "qkv": 0.03}

    def adam(name, grads, row_first, lead, unit, rb):
        results[name] = do(
            lambda s, g, prev: adam_part(s, g, core, rates[name], prev, row_first, lead, unit, rb),
            states[name],
            grads,
            results[name],
        )

    jobs = []
    for k, (at_row, count) in enumerate(down_rows):
        jobs.append(("down", [("down", k)], at_row, 0, count, 1024))
    for name, lead in (("gate", 0), ("up", Y)):
        for k, (at_row, count) in enumerate(up_rows):
            jobs.append(("up", [(name, "mine", k), (name, "theirs", k)], at_row, lead, count, S * ffb))
    for k in range(2):
        jobs.append(("out", [("out", k)], 0, k, blk, width // 2))
    for third in (2, 1, 0):
        jobs.append(("qkv", [(third, 0), (third, 1, "theirs")], 0, third * Y, blk, S * blk))
    received = {}

    def update(limit):
        for name in list(reps.done):
            if name in ("out", 0, 1, 2):
                g = reps.done.pop(name)
                half = g.shape[0] // 2
                reps.done[(name, 0)] = g[:half]
                reps.done[(name, 1) if name == "out" else (name, 1, "theirs")] = g[half:]
        for name in list(reps.done):
            if "theirs" in name and name not in received:
                received[name] = at.core(reps.done[name])
        while jobs and limit and all(k in reps.done for k in jobs[0][1]):
            name, needs, at_row, lead, count, unit = jobs.pop(0)
            rb = max(n for n in range(8, min(count, 176) + 1, 8) if count % n == 0 and at_row % n == 0)
            adam(name, [received[k] if "theirs" in k else reps.done[k] for k in needs], at_row, lead, unit, rb)
            limit -= 1

    def ticks(n):
        for _ in range(n):
            reps.tick()

    wide = 2 * FF // 8

    def quarter_heads(x):
        return [x[:, h][None, None] for h in halves]

    n, start, finish, gate_all = gather_steps([gate0[None, None], gate1[None, None]], 1)
    start(0)
    g_down = do(lambda a, c: mm(a, c, PLAIN, bf16, tn=512), act, cot_all)
    for k, (at_row, count) in enumerate(down_rows):
        reps.push(("down", k), g_down[at_row : at_row + count])
    ticks(1)

    steps2 = at.steps(False) + [("core", 1)]

    def sum_send(sums, axis, step):
        return at.core(sums) if axis == "core" else at.along(sums, axis, step)

    def sum_step(sums, axis, step):
        return do(lambda a, b: a + b, sums, sum_send(sums, axis, step))

    tiny = list(steps2)
    sums_got = sum_send(sums, *tiny.pop(0))
    for i in range(1, n):
        finish()
        sums = do(lambda a, b: a + b, sums, sums_got)
        sums_got = sum_send(sums, *tiny.pop(0))
        start(i, sums)
        ticks(1)
    n, start_up, finish_up, up_all = gather_steps([up0[None, None], up1[None, None]], 1)
    ggate_all = gate_all().reshape(Y * S * ffb, T)
    sums = do(lambda a, b: a + b, sums, sums_got)
    start_up(0, sums)
    while tiny:
        sums = sum_step(sums, *tiny.pop(0))
    g_gate = do(lambda x, g: mm(x, g, LAST, bf16, tn=wide), xn2, ggate_all)
    push_pairs("gate", g_gate, up_rows)
    finish_up()
    for i in range(1, n):
        start_up(i)
        if i == 1:
            ticks(1)
            part_gate = do(lambda w, g: mm(w, g, PLAIN, f32, tn=256), wg, ggate_all)
            out_part = do(lambda w, a: mm(w, a, FIRST, bf16, tm=512), wd_own, act)
        if i < n - 1:
            finish_up()
    gup_all = up_all().reshape(Y * S * ffb, T)
    part = do(lambda w, g, p: dot(w, g, PLAIN) + p, wu, gup_all, part_gate)
    part_theirs = at.core(part[blk:])
    ticks(1)

    def branch(a, b, cot, z, scale, gain, sums):
        gxn2 = a + b
        e = gxn2 * gain
        grad_hidden = cot.astype(f32) + scale * (e - sums[0:1] / width - z * (sums[1:2] / width))
        return grad_hidden.astype(bf16), grad_hidden, gxn2

    grad_branch, grad_hidden, gxn2 = do(
        branch, part[:blk], part_theirs, cot_cols, z2, inv2, own_cols[:, 2:3], sums
    )
    n, start, finish, branch_all = gather_steps(quarter_heads(grad_branch), 1)
    start(0)
    g_up = do(lambda x, g: mm(x, g, LAST, bf16, tn=wide), xn2, gup_all)
    push_pairs("up", g_up, up_rows)
    finish()
    for i in range(1, n):
        start(i)
        if i == 1:
            update(1)
            ticks(1)
        if i < n - 1:
            finish()
    gbr_c = branch_all()[0]
    gbr_o = at.core(gbr_c)
    gbr = do(lambda a, b: in_order(a, b, 1).reshape(width, T), gbr_c, gbr_o)
    grad_attn = do(lambda w, g: dot(w, g, PLAIN).astype(bf16), wo_own, gbr)

    gqkvs = []
    for k in range(2):
        dout = grad_attn[:, halves[k]].reshape(heads, HEAD_DIM, H)
        gqkvs.append(do(attend_back, qkvs[k], dout, stats[k], table[seqs[k]]).reshape(3, blk, H))
    n, start, finish, gqkv_done = gather_steps([g.reshape(1, 1, 3 * blk, H) for g in gqkvs], 3)
    start(0)
    attn = lanes(*attns)
    g_out = do(
        lambda a, g: join(*[mm(a, g[k * width // 2 : (k + 1) * width // 2], LAST, bf16, tn=512) for k in range(2)]),
        attn,
        gbr,
    )
    reps.push("out", g_out)
    update(1)
    ticks(1)
    finish()
    for i in range(1, n):
        start(i)
        if i == 1:
            update(1)
            ticks(1)
            update(1)
        if i < n - 1:
            finish()
    gqkv = gqkv_done().reshape(3, Y * S * blk, T)
    out_sum = lax.psum_scatter(do(lambda p: p, out_part), plane, scatter_dimension=0, tiled=True)
    for third in (2, 1, 0):
        g = do(lambda x, g: dot(x, g, LAST).astype(bf16), xn1, gqkv[third])
        reps.push(third, g)
        if third == 2:
            ticks(1)
    part = do(lambda w, g: dot(w, g, PLAIN), wq, gqkv.reshape(3 * Y * S * blk, T))
    part_theirs = at.core(part[blk:])

    def first_back(a, b, x, mean, inv, gain, gxn2, z2, gqkv0, gqkv1):
        gxn1 = a + b
        z1 = (x.astype(f32) - mean) * inv
        e = gxn1 * gain
        sums = join(jnp.sum(e, axis=0, keepdims=True), jnp.sum(e * z1, axis=0, keepdims=True))
        small = jnp.concatenate(
            [
                jnp.sum(gxn1 * z1, axis=1)[None],
                jnp.sum(gxn1, axis=1)[None],
                jnp.sum(gxn2 * z2, axis=1)[None],
                jnp.sum(gxn2, axis=1)[None],
                jnp.sum(gqkv0.astype(f32), axis=2) + jnp.sum(gqkv1.astype(f32), axis=2),
            ],
            axis=0,
        )
        return sums, small, gxn1, z1

    sums, small, gxn1, z1 = do(
        first_back, part[:blk], part_theirs, x_own, mean1, inv1, own_cols[:, 0:1], gxn2, z2, *gqkvs
    )
    for axis, step in steps2:
        sums = sum_step(sums, axis, step)
    ticks(1)
    input_grad = do(
        lambda h, grad, z, scale, gain, sums: (
            h + scale * (grad * gain - sums[0:1] / width - z * (sums[1:2] / width))
        ).astype(bf16),
        grad_hidden,
        gxn1,
        z1,
        inv1,
        own_cols[:, 0:1],
        sums,
    )

    def to_rows(cols):
        split = do(lambda c: c.reshape(blk, S, at.ctx_size, rows).transpose(2, 1, 0, 3).reshape(nb, blk, rows), cols)
        got = lax.all_to_all(split, plane, split_axis=0, concat_axis=0, tiled=True)
        return do(lambda g: g.reshape(width, rows).T, got)

    input_rows = to_rows(input_grad).astype(f32)
    update(1)
    ticks(1)
    n_rep = lax.axis_size("rep")
    step = 1
    while step < n_rep:
        other = lax.ppermute(small, "rep", [(i, i ^ step) for i in range(n_rep)])
        small = do(lambda a, b: a + b, small, other)
        step *= 2
    sent = do(lambda s: jnp.broadcast_to(s.reshape(1, 7, blk), (nb, 7, blk)), small)
    small_all = lax.all_to_all(sent, plane, split_axis=0, concat_axis=0, tiled=True)

    def norm_update(every, *a):
        return adam_update(*a, every.transpose(1, 0, 2).reshape(7, width), 0.3, 0.0)

    mn, vn, wn = do(norm_update, small_all, norm_params, m_norm, v_norm)
    update(1)
    ticks(1)
    update(2)
    ticks(1)
    update(1)
    out_cols = do(lambda h, a: (h + a.astype(f32)).astype(bf16), hidden, out_sum)
    block_output = to_rows(out_cols)
    while reps.busy():
        reps.tick()
        update(2)
    update(len(jobs))
    return (
        (block_output.reshape(tokens.shape), input_rows.reshape(tokens.shape))
        + tuple(results["qkv"])
        + tuple(results["out"])
        + tuple(results["up"])
        + tuple(results["down"])
        + (mn, vn, wn)
    )


def solution(mesh):
    tok = P("rep", "ctx", "shard", None)
    row = P(("ctx", "shard"), None)
    placed = (tok, tok, P("rep", "shard", None)) + (row,) * 4 + (P(),) + (row,) * 8 + (P(), P())
    return jax.shard_map(
        body,
        mesh=mesh,
        in_specs=placed,
        out_specs=(tok, tok) + (row,) * 12 + (P(),) * 3,
        check_vma=False,
    )
```

```python
import functools

import jax
import jax.numpy as jnp
from jax import lax
from jax.experimental import pallas as pl
from jax.experimental.pallas import tpu as pltpu
from jax.sharding import PartitionSpec as P

HEADS = 32
HEAD_DIM = 64
FF = 5632
ROTARY = 16
STEP = 10

eps_norm = 1e-05
masked_score = -1e30
beta_one = 0.9
beta_two = 0.999
adam_eps = 1e-08
weight_decay = 0.1
score_scale = HEAD_DIM ** (-0.5)
FIRST = (((0,), (0,)), ((), ()))
LAST = (((1,), (1,)), ((), ()))
PLAIN = (((1,), (0,)), ((), ()))
bf16 = jnp.bfloat16
f32 = jnp.float32


def dot(a, b, dims):
    return lax.dot_general(a, b, dims, preferred_element_type=f32)


def adam_update(weight, moment_one, moment_two, grad, step_rate, decay_rate):
    first_new = beta_one * moment_one + (1.0 - beta_one) * grad
    second_new = beta_two * moment_two + (1.0 - beta_two) * grad * grad
    first_hat = first_new / (1.0 - beta_one**STEP)
    second_hat = second_new / (1.0 - beta_two**STEP)
    weight_new = weight - step_rate * (
        first_hat / (jnp.sqrt(second_hat) + adam_eps) + decay_rate * weight
    )
    return (first_new, second_new, weight_new)


class Plane:
    def __init__(self):
        self.s_size = lax.axis_size("shard")
        self.ctx_size = lax.axis_size("ctx")
        self.y_size = self.ctx_size // 2
        self.ctx = lax.axis_index("ctx")
        self.s = lax.axis_index("shard")
        self.y = self.ctx // 2
        self.c = self.ctx % 2
        self.blocks = self.ctx_size * self.s_size

    def core(self, x):
        return lax.ppermute(x, "ctx", [(i, i ^ 1) for i in range(self.ctx_size)])

    def along(self, x, axis, step):
        if axis == "y":
            return lax.ppermute(x, "ctx", [(i, i ^ (2 * step)) for i in range(self.ctx_size)])
        return lax.ppermute(x, "shard", [(i, i ^ step) for i in range(self.s_size)])

    def index(self, axis):
        return self.y if axis == "y" else self.s

    def steps(self, flip):
        ys = []
        k = self.y_size // 2
        while k:
            ys.append(("y", k))
            k //= 2
        ss = []
        k = self.s_size // 2
        while k:
            ss.append(("s", k))
            k //= 2
        return ys + ss if flip else ss + ys

    def chip_exchange(self, x, take):
        out = [(self.y, self.s, take(self.y, self.s))]
        for ry in range(self.y_size):
            for rs in range(self.s_size):
                if ry or rs:
                    y, s = self.y ^ ry, self.s ^ rs
                    mask = 2 * ry * self.s_size + rs
                    perm = [(i, i ^ mask) for i in range(self.blocks)]
                    out.append((y, s, lax.ppermute(take(y, s), ("ctx", "shard"), perm)))
        return out

    def sum_all(self, x):
        for axis, step in self.steps(False):
            x = x + self.along(x, axis, step)
        return x + self.core(x)

    def scatter_sum(self, p, flip):
        axes = {"y": 1, "s": 2}
        steps = self.steps(flip)
        kept = got = None
        for n, (axis, step) in enumerate(steps):
            ax = axes[axis]
            bit = (self.index(axis) // step) % 2
            kept = lax.dynamic_slice_in_dim(p, bit * step, step, ax)
            send = lax.dynamic_slice_in_dim(p, (1 - bit) * step, step, ax)
            got = self.along(send, axis, step)
            if n + 1 < len(steps):
                p = (kept.astype(f32) + got.astype(f32)).astype(bf16)
        return kept[:, 0, 0], got[:, 0, 0]

    def gather(self, p, flip):
        axes = {"y": 1, "s": 2}
        p = p[:, None, None]
        for axis, step in reversed(self.steps(flip)):
            ax = axes[axis]
            bit = (self.index(axis) // step) % 2
            got = self.along(p, axis, step)
            first = bit == 0
            p = jnp.concatenate([jnp.where(first, p, got), jnp.where(first, got, p)], ax)
        return p


class Order:
    def __init__(self):
        self.token = lax.create_token()

    def __call__(self, stage, *args):
        args, token = lax.optimization_barrier((args, self.token))
        out, self.token = lax.optimization_barrier((stage(*args), token))
        return out


SMALL = pl.CostEstimate(flops=1024, bytes_accessed=1024, transcendentals=0)


class RepSum:
    def __init__(self, order):
        self.order = order
        z = lax.axis_index("rep")
        self.end = (z == 0) | (z == lax.axis_size("rep") - 1)
        self.queue = []
        self.flight = []
        self.depth = 1
        self.done = {}

    def push(self, name, g):
        self.queue.append((name, g))

    def busy(self):
        return bool(self.queue or self.flight)

    def tick(self, between=None):
        old = {}
        if len(self.flight) >= self.depth or (self.flight and not self.queue):
            old = self.flight.pop(0)
        new = self.queue.pop(0) if self.queue else None
        values = {}
        if "in" in old:
            values["g"], values["g_got"] = old["in"][1], old["in_got"]
        if "mid" in old:
            values["s"], values["s_got"] = old["mid"][1], old["mid_got"]
        if new:
            values["new"] = new[1]
        both = new and "mid" in old and new[1].shape == old["mid"][1].shape
        if "out" in old:
            values["out_got"] = old["out_got"]

        def stage(v):
            def add(a, b):
                return lax.reduce_precision(a.astype(f32) + b.astype(f32), 8, 7).astype(bf16)

            out = {}
            if "g" in v:
                out["a_sum"] = add(v["g"], v["g_got"])
            if "s" in v:
                total = add(v["s"], v["s_got"])
                out["total"] = jnp.where(self.end, v["new"], total) if both else total
            if "new" in v and not both:
                out["new"] = v["new"]
            if "out_got" in v:
                out["z_got"] = v["out_got"]
            return out

        if not values:
            return
        out = self.order(stage, values)
        if between is not None:
            out, _ = lax.optimization_barrier((out, between()))
        if "out" in old:
            self.done[old["out"][0]] = jnp.where(self.end, out["z_got"], old["out"][1])
        slot = {}
        if both:
            got = lax.ppermute(out["total"], "rep", [(0, 1), (1, 0), (2, 3), (3, 2)])
            slot = {"in": new, "in_got": got, "out": (old["mid"][0], out["total"]), "out_got": got}
        else:
            if new:
                slot["in"] = new
                slot["in_got"] = lax.ppermute(out["new"], "rep", [(0, 1), (3, 2)])
            if "mid" in old:
                slot["out"] = (old["mid"][0], out["total"])
                slot["out_got"] = lax.ppermute(out["total"], "rep", [(1, 0), (2, 3)])
        if "in" in old:
            slot["mid"] = (old["in"][0], out["a_sum"])
            slot["mid_got"] = lax.ppermute(out["a_sum"], "rep", [(1, 2), (2, 1)])
        if slot:
            self.flight.append(slot)


def cast_kernel(w_ref, out_ref):
    out_ref[...] = w_ref[...].astype(bf16)


def cast(w):
    rows, width = w.shape
    unit = max(n for n in (128, 256, 512, 1024, 1408, 2048, 2816) if width % n == 0)
    spec = pl.BlockSpec((rows, unit), lambda i: (0, i))
    return pl.pallas_call(
        cast_kernel,
        grid=(width // unit,),
        in_specs=[spec],
        out_specs=spec,
        out_shape=jax.ShapeDtypeStruct(w.shape, bf16),
        compiler_params=pltpu.CompilerParams(vmem_limit_bytes=48 * 1024 * 1024),
        cost_estimate=SMALL,
    )(w)


def gated_kernel(ga_ref, gb_ref, ua_ref, ub_ref, grad_ref, gains_ref, g0_ref, g1_ref, u0_ref, u1_ref, act_ref, sums_ref):
    half = g0_ref.shape[1]
    gate = ga_ref[...].astype(f32) + gb_ref[...].astype(f32)
    up = ua_ref[...].astype(f32) + ub_ref[...].astype(f32)
    sig = jax.nn.sigmoid(gate)
    silu = gate * sig
    grad = grad_ref[...]
    act_ref[...] = (silu * up).astype(bf16)
    ggate = (grad * up * sig * (1.0 + gate * (1.0 - sig))).astype(bf16)
    gup = (grad * silu).astype(bf16)
    g0_ref[...] = ggate[:, :half]
    g1_ref[...] = ggate[:, half:]
    u0_ref[...] = gup[:, :half]
    u1_ref[...] = gup[:, half:]
    a, b = ggate.astype(f32), gup.astype(f32)
    e = jnp.sum(a * gains_ref[:, 0:1] + b * gains_ref[:, 2:3], axis=0, keepdims=True)
    ez = jnp.sum(a * (gate - gains_ref[:, 1:2]) + b * (up - gains_ref[:, 3:4]), axis=0, keepdims=True)
    both = jnp.concatenate([e, ez], axis=0)

    @pl.when(pl.program_id(0) == 0)
    def _():
        sums_ref[...] = both

    @pl.when(pl.program_id(0) > 0)
    def _():
        sums_ref[...] += both


def gated(ga, gb, ua, ub, grad_act, gains):
    rows, t = grad_act.shape
    n = max(n for n in (1, 2, 4) if rows % (16 * n) == 0)
    whole = pl.BlockSpec((rows // n, t), lambda i: (i, 0))
    half = pl.BlockSpec((rows // n, t // 2), lambda i: (i, 0))
    out_half = jax.ShapeDtypeStruct((rows, t // 2), bf16)
    return pl.pallas_call(
        gated_kernel,
        grid=(n,),
        in_specs=[whole] * 5 + [pl.BlockSpec((rows // n, 4), lambda i: (i, 0))],
        out_specs=[half] * 4 + [whole, pl.BlockSpec((2, t), lambda i: (0, 0))],
        out_shape=[out_half] * 4 + [jax.ShapeDtypeStruct((rows, t), bf16), jax.ShapeDtypeStruct((2, t), f32)],
        compiler_params=pltpu.CompilerParams(vmem_limit_bytes=56 * 1024 * 1024),
        cost_estimate=SMALL,
    )(ga, gb, ua, ub, grad_act, gains)


def own_columns_kernel(block_ref, x_ref, out_ref):
    out_ref[...] = x_ref[...].T


def own_columns(x, block, width):
    rows = x.shape[0]
    if width % 128:
        return lax.dynamic_slice_in_dim(x, block[0] * width, width, 1).T
    tile = min(rows, 512)
    return pl.pallas_call(
        own_columns_kernel,
        grid_spec=pltpu.PrefetchScalarGridSpec(
            num_scalar_prefetch=1,
            grid=(rows // tile,),
            in_specs=[pl.BlockSpec((tile, width), lambda i, block: (i, block[0]))],
            out_specs=pl.BlockSpec((width, tile), lambda i, block: (0, i)),
        ),
        out_shape=jax.ShapeDtypeStruct((width, rows), bf16),
        compiler_params=pltpu.CompilerParams(vmem_limit_bytes=48 * 1024 * 1024),
        cost_estimate=SMALL,
    )(block, x)


def split_kernel(core_ref, w_ref, mine_ref, theirs_ref):
    unit = mine_ref.shape[0]
    first = core_ref[0] == 0
    a, b = w_ref[:, :unit], w_ref[:, unit:]
    mine_ref[...] = jnp.where(first, a, b).T.astype(bf16)
    theirs_ref[...] = jnp.where(first, b, a).T.astype(bf16)


def split_columns(w, core, lead, unit, count):
    rows = w.shape[0]
    half = pl.BlockSpec((unit, rows), lambda j, core: (j, 0))
    out = jax.ShapeDtypeStruct((count * unit, rows), bf16)
    return pl.pallas_call(
        split_kernel,
        grid_spec=pltpu.PrefetchScalarGridSpec(
            num_scalar_prefetch=1,
            grid=(count,),
            in_specs=[pl.BlockSpec((rows, 2 * unit), lambda j, core: (0, lead + j))],
            out_specs=[half, half],
        ),
        out_shape=[out, out],
        compiler_params=pltpu.CompilerParams(vmem_limit_bytes=32 * 1024 * 1024),
        cost_estimate=SMALL,
    )(core, w)


def arrange_kernel(at_ref, a_ref, b_ref, c_ref, d_ref, send_ref, keep_ref):
    send_ref[...] = jnp.concatenate([a_ref[...], b_ref[...]], axis=1)
    keep_ref[...] = jnp.concatenate([c_ref[...], d_ref[...]], axis=1)


def arrange(mine, got, place, pre, y_size, s_size, unit, flip):
    r = mine.shape[1]
    half = pre * y_size * s_size // 2

    def block(i, place, keep):
        p = i % pre
        i = i // pre
        if flip:
            s, y = i % s_size, i // s_size
            bit = place[0] // (y_size // 2)
            bit = bit if keep else 1 - bit
            y = y + bit * (y_size // 2)
        else:
            y, s = i % y_size, i // y_size
            bit = place[1] // (s_size // 2)
            bit = bit if keep else 1 - bit
            s = s + bit * (s_size // 2)
        return ((p * y_size + y) * s_size + s, 0)

    def spec(keep):
        return pl.BlockSpec((unit, r), lambda i, place: block(i, place, keep))

    out = jax.ShapeDtypeStruct((half * unit, 2 * r), bf16)
    out_spec = pl.BlockSpec((unit, 2 * r), lambda i, place: (i, 0))
    return pl.pallas_call(
        arrange_kernel,
        grid_spec=pltpu.PrefetchScalarGridSpec(
            num_scalar_prefetch=1,
            grid=(half,),
            in_specs=[spec(False), spec(False), spec(True), spec(True)],
            out_specs=[out_spec, out_spec],
        ),
        out_shape=[out, out],
        compiler_params=pltpu.CompilerParams(vmem_limit_bytes=32 * 1024 * 1024),
        cost_estimate=SMALL,
    )(place, mine, got, mine, got)


def product_kernel(dims, a_ref, b_ref, *refs):
    p = dot(a_ref[...], b_ref[...], dims)
    if len(refs) == 2:
        p = p + refs[0][...]
    refs[-1][...] = p.astype(refs[-1].dtype)


def mm(a, b, dims, dtype, tm=None, tn=None, add=None):
    (ca,), (cb,) = dims[0]
    m, k, n = a.shape[1 - ca], a.shape[ca], b.shape[1 - cb]
    tm, tn = tm or m, tn or n
    a_block = [0, 0]
    a_block[ca], a_block[1 - ca] = k, tm
    b_block = [0, 0]
    b_block[cb], b_block[1 - cb] = k, tn
    out = pl.BlockSpec((tm, tn), lambda i, j: (i, j))
    return pl.pallas_call(
        functools.partial(product_kernel, dims),
        grid=(m // tm, n // tn),
        in_specs=[
            pl.BlockSpec(tuple(a_block), (lambda i, j: (0, i)) if ca == 0 else (lambda i, j: (i, 0))),
            pl.BlockSpec(tuple(b_block), (lambda i, j: (0, j)) if cb == 0 else (lambda i, j: (j, 0))),
        ]
        + ([] if add is None else [out]),
        out_specs=out,
        out_shape=jax.ShapeDtypeStruct((m, n), dtype),
        compiler_params=pltpu.CompilerParams(vmem_limit_bytes=48 * 1024 * 1024),
        cost_estimate=SMALL,
    )(*((a, b) if add is None else (a, b, add)))


def last_step_kernel(bits_ref, own0_ref, got0_ref, own1_ref, got1_ref, out_ref):
    y, s = pl.program_id(1), pl.program_id(2)
    half = own0_ref.shape[3]
    ys, ss = bits_ref[2], bits_ref[3]
    a = jnp.where(s // ss == bits_ref[1], own0_ref[0, 0], got0_ref[0, 0])
    b = jnp.where(y // ys == bits_ref[0], own1_ref[0, 0], got1_ref[0, 0])
    out_ref[0, 0, 0, :, :half] = a
    out_ref[0, 0, 0, :, half:] = b


def last_step(parts, got, bits, pre, y_size, s_size):
    rows, half = parts[0].shape[2] // pre, parts[0].shape[3]
    along_s = pl.BlockSpec((1, 1, rows, half), lambda p, y, s, bits: (y, s % (s_size // 2), p, 0))
    along_y = pl.BlockSpec((1, 1, rows, half), lambda p, y, s, bits: (y % (y_size // 2), s, p, 0))
    return pl.pallas_call(
        last_step_kernel,
        grid_spec=pltpu.PrefetchScalarGridSpec(
            num_scalar_prefetch=1,
            grid=(pre, y_size, s_size),
            in_specs=[along_s, along_s, along_y, along_y],
            out_specs=pl.BlockSpec((1, 1, 1, rows, 2 * half), lambda p, y, s, bits: (p, y, s, 0, 0)),
        ),
        out_shape=jax.ShapeDtypeStruct((pre, y_size, s_size, rows, 2 * half), bf16),
        compiler_params=pltpu.CompilerParams(vmem_limit_bytes=48 * 1024 * 1024),
        cost_estimate=SMALL,
    )(bits, parts[0], got[0], parts[1], got[1])


def stack_turned_kernel(a_ref, b_ref, out_ref):
    r = a_ref.shape[1]
    out_ref[:r] = a_ref[...].T
    out_ref[r:] = b_ref[...].T


def stack_turned(a, b):
    rows, width = a.shape
    n = max(n for n in (1, 2, 4, 6, 8, 11) if rows % (128 * n) == 0)
    spec = pl.BlockSpec((rows // n, width), lambda i: (i, 0))
    return pl.pallas_call(
        stack_turned_kernel,
        grid=(n,),
        in_specs=[spec, spec],
        out_specs=pl.BlockSpec((2 * width, rows // n), lambda i: (0, i)),
        out_shape=jax.ShapeDtypeStruct((2 * width, rows), bf16),
        compiler_params=pltpu.CompilerParams(vmem_limit_bytes=48 * 1024 * 1024),
        cost_estimate=SMALL,
    )(a, b)


def add_split_kernel(bit_ref, a_ref, b_ref, c_ref, d_ref, send_ref, keep_ref):
    send_ref[...] = (a_ref[...].astype(f32) + b_ref[...].astype(f32)).astype(bf16)
    keep_ref[...] = (c_ref[...].astype(f32) + d_ref[...].astype(f32)).astype(bf16)


def add_split(kept, got, bit):
    rows, t = kept.shape
    half = rows // 2
    n = max(n for n in (1, 2, 3, 4) if half % (16 * n) == 0)
    rb = half // n
    away = pl.BlockSpec((rb, t), lambda i, bit: ((1 - bit[0]) * n + i, 0))
    here = pl.BlockSpec((rb, t), lambda i, bit: (bit[0] * n + i, 0))
    out = jax.ShapeDtypeStruct((half, t), bf16)
    out_spec = pl.BlockSpec((rb, t), lambda i, bit: (i, 0))
    return pl.pallas_call(
        add_split_kernel,
        grid_spec=pltpu.PrefetchScalarGridSpec(
            num_scalar_prefetch=1,
            grid=(n,),
            in_specs=[away, away, here, here],
            out_specs=[out_spec, out_spec],
        ),
        out_shape=[out, out],
        compiler_params=pltpu.CompilerParams(vmem_limit_bytes=48 * 1024 * 1024),
        cost_estimate=SMALL,
    )(bit, kept, got, kept, got)


def adam_kernel(rate, two, core_ref, w_ref, m_ref, v_ref, *refs):
    grad = refs[0][...].astype(f32)
    if two:
        other = refs[1][...].astype(f32)
        mine = core_ref[0] == 0
        grad = jnp.concatenate([jnp.where(mine, grad, other), jnp.where(mine, other, grad)], axis=1)
    new_m_ref, new_v_ref, new_w_ref = refs[-3:]
    new_m, new_v, new_w = adam_update(w_ref[...], m_ref[...], v_ref[...], grad, rate, weight_decay)
    new_m_ref[...] = new_m
    new_v_ref[...] = new_v
    new_w_ref[...] = new_w


def adam_part(state, grads, core, rate, prev, row_first, lead, unit, rb):
    w, m, v = state
    two = len(grads) == 2
    rows, width = grads[0].shape
    whole = pl.BlockSpec((rb, unit * len(grads)), lambda i, g, core: (row_first // rb + i, lead + g))
    half = pl.BlockSpec((rb, unit), lambda i, g, core: (i, g))
    out = jax.ShapeDtypeStruct(w.shape, f32)
    extra, aliases = [], {}
    if prev is not None:
        extra = list(prev)
        aliases = {4 + len(grads) + i: i for i in range(3)}
    return pl.pallas_call(
        functools.partial(adam_kernel, rate, two),
        grid_spec=pltpu.PrefetchScalarGridSpec(
            num_scalar_prefetch=1,
            grid=(rows // rb, width // unit),
            in_specs=[whole] * 3 + [half] * len(grads) + [pl.BlockSpec(memory_space=pl.ANY)] * len(extra),
            out_specs=[whole] * 3,
        ),
        out_shape=[out] * 3,
        input_output_aliases=aliases,
        compiler_params=pltpu.CompilerParams(vmem_limit_bytes=48 * 1024 * 1024),
        cost_estimate=SMALL,
    )(core, w, m, v, *grads, *extra)


def attend_kernel(kept_ref, got_ref, bias_ref, table_ref, qkv_ref, out_ref, stat_ref):
    half = ROTARY // 2
    cos, sin, pos = table_ref[0, :half], table_ref[0, half:ROTARY], table_ref[0, ROTARY:]
    parts = []
    for i in range(3):
        v = kept_ref[i, 0].astype(f32) + got_ref[i, 0].astype(f32) + bias_ref[i, 0]
        if i < 2:
            a, b = v[:half], v[half:ROTARY]
            v = jnp.concatenate([a * cos - b * sin, b * cos + a * sin, v[ROTARY:]], axis=0)
        v = v.astype(bf16)
        qkv_ref[i, 0] = v
        parts.append(v)
    q, k, v = parts
    scores = dot(k, q, FIRST) * score_scale
    scores = jnp.where(pos.T[:, :1] <= pos[:1], scores, masked_score)
    peak = jnp.max(scores, axis=0, keepdims=True)
    e = jnp.exp(scores - peak)
    total = jnp.sum(e, axis=0, keepdims=True)
    p = (e / total).astype(bf16)
    out_ref[0] = dot(v, p, PLAIN).astype(bf16)
    stat_ref[0, 0] = jnp.concatenate([peak, total], axis=0)


def attend(kept, got, bias, table):
    _, heads, hd, t = kept.shape
    seqs, _, seq = table.shape
    big = pl.BlockSpec((3, 1, hd, seq), lambda s, h: (0, h, 0, s))
    table_spec = pl.BlockSpec((1, table.shape[1], seq), lambda s, h: (s, 0, 0))
    stat = pl.BlockSpec((1, 1, 2, seq), lambda s, h: (s, h, 0, 0))
    return pl.pallas_call(
        attend_kernel,
        grid=(seqs, heads),
        in_specs=[
            big,
            big,
            pl.BlockSpec((3, 1, hd, 1), lambda s, h: (0, h, 0, 0)),
            table_spec,
        ],
        out_specs=[big, pl.BlockSpec((1, hd, seq), lambda s, h: (h, 0, s)), stat],
        out_shape=[
            jax.ShapeDtypeStruct((3, heads, hd, t), bf16),
            jax.ShapeDtypeStruct((heads, hd, t), bf16),
            jax.ShapeDtypeStruct((seqs, heads, 2, seq), f32),
        ],
        compiler_params=pltpu.CompilerParams(vmem_limit_bytes=32 * 1024 * 1024),
        cost_estimate=SMALL,
    )(kept, got, bias, table)


def attend_back_kernel(qkv_ref, dout_ref, stat_ref, table_ref, out_ref):
    half = ROTARY // 2
    cos, sin, pos = table_ref[0, :half], table_ref[0, half:ROTARY], table_ref[0, ROTARY:]
    q, k, v = qkv_ref[0, 0], qkv_ref[1, 0], qkv_ref[2, 0]
    dout = dout_ref[0]
    scores = dot(k, q, FIRST) * score_scale
    scores = jnp.where(pos.T[:, :1] <= pos[:1], scores, masked_score)
    p = jnp.exp(scores - stat_ref[0, 0, :1]) / stat_ref[0, 0, 1:]
    dp = dot(v, dout, FIRST)
    inner = jnp.sum(p * dp, axis=0, keepdims=True)
    ds = (p * (dp - inner)).astype(bf16)

    def back(x):
        a, b = x[:half], x[half:ROTARY]
        return jnp.concatenate([a * cos + b * sin, b * cos - a * sin, x[ROTARY:]], axis=0)

    out_ref[0, 0] = back(dot(k, ds, PLAIN) * score_scale).astype(bf16)
    out_ref[1, 0] = back(dot(q, ds, LAST) * score_scale).astype(bf16)
    out_ref[2, 0] = dot(dout, p.astype(bf16), LAST).astype(bf16)


def attend_back(qkv, dout, stats, table):
    _, heads, hd, t = qkv.shape
    seqs, _, seq = table.shape
    big = pl.BlockSpec((3, 1, hd, seq), lambda s, h: (0, h, 0, s))
    table_spec = pl.BlockSpec((1, table.shape[1], seq), lambda s, h: (s, 0, 0))
    stat = pl.BlockSpec((1, 1, 2, seq), lambda s, h: (s, h, 0, 0))
    return pl.pallas_call(
        attend_back_kernel,
        grid=(seqs, heads),
        in_specs=[
            big,
            pl.BlockSpec((1, hd, seq), lambda s, h: (h, 0, s)),
            stat,
            table_spec,
        ],
        out_specs=big,
        out_shape=jax.ShapeDtypeStruct((3, heads, hd, t), bf16),
        compiler_params=pltpu.CompilerParams(vmem_limit_bytes=32 * 1024 * 1024),
        cost_estimate=SMALL,
    )(qkv, dout, stats, table)


def body(
    tokens,
    cotangent,
    span_order,
    w_qkv,
    w_out,
    w_up,
    w_down,
    norm_params,
    m_qkv,
    v_qkv,
    m_out,
    v_out,
    m_up,
    v_up,
    m_down,
    v_down,
    m_norm,
    v_norm,
):
    at = Plane()
    do = Order()
    reps = RepSum(do)
    width = tokens.shape[3]
    rows = tokens.shape[1]
    S, Y, nb = at.s_size, at.y_size, at.blocks
    plane = ("ctx", "shard")
    blk = width // nb
    ffb = FF // nb
    heads = blk // HEAD_DIM
    seq = rows * at.ctx_size
    T = S * seq
    H = T // 2
    first = at.c == 0
    core = at.c.reshape(1)
    my_block = at.ctx * S + at.s
    halves = (slice(0, H), slice(H, T))
    seqs = (slice(0, S // 2), slice(S // 2, S))

    def pick(x, axis, which):
        return lax.dynamic_index_in_dim(x, which, axis, keepdims=False)

    def in_order(mine, theirs, axis):
        return jnp.stack([jnp.where(first, mine, theirs), jnp.where(first, theirs, mine)], axis=axis)

    def join(a, b):
        return jnp.concatenate([a, b], axis=0)

    def lanes(a, b):
        return jnp.concatenate([a, b], axis=1)

    x_rows = tokens.reshape(rows, width)
    order = span_order.reshape(-1).astype(f32)
    span = rows // 2

    def pack(x, order):
        xf = x.astype(f32)
        mean = jnp.mean(xf, axis=1)
        centred = xf - mean[:, None]
        inv = lax.rsqrt(jnp.mean(centred * centred, axis=1) + eps_norm)
        mine = lax.dynamic_slice_in_dim(order, 2 * at.ctx, 2)
        place = jnp.repeat(mine, span)
        terms = []
        for v in (mean, inv):
            for _ in range(3):
                t = lax.reduce_precision(v, 8, 7)
                terms.append(t)
                v = v - t
        extra = jnp.stack(terms + [place] + [jnp.zeros_like(place)] * 9).astype(bf16)
        blocks = x.T.reshape(nb, blk, rows)
        return jnp.concatenate([blocks, jnp.broadcast_to(extra[None], (nb, 16, rows))], axis=1)

    packed = do(pack, x_rows, order)
    cot_all = lax.all_gather(do(cast, cotangent.reshape(rows, width)), ("shard", "ctx"), axis=0, tiled=True)
    got = lax.all_to_all(packed, plane, split_axis=0, concat_axis=0, tiled=True)

    def chip_rows(w, lead, unit, count):
        mine, theirs = do(lambda w: split_columns(w, core, lead, unit, count), w)
        return mine, at.core(theirs)

    wq_parts = chip_rows(w_qkv, 0, S * blk, 3 * Y)
    norm_cols = norm_params.reshape(7, nb, blk).transpose(1, 2, 0)
    own_cols = pick(norm_cols, 0, my_block)
    other_cols = pick(norm_cols, 0, (at.ctx ^ 1) * S + at.s)
    pair_cols = join(own_cols, other_cols)
    bias = own_cols[:, 4:7].T.reshape(3, heads, HEAD_DIM, 1)
    spot = jnp.stack([at.y, at.s])

    def cut_weights(parts, pre, unit, flip):
        return do(lambda a, b: arrange(a, b, spot, pre, Y, S, unit, flip), *parts)

    wq_cut = [cut_weights(wq_parts, 3, blk, bool(k)) for k in range(2)]

    def columns(got):
        x = got.reshape(at.ctx_size, S, blk + 16, rows).transpose(2, 1, 0, 3).reshape(blk + 16, T)
        x_own, extra = x[:blk], x[blk:].astype(f32)
        mean = extra[0:1] + extra[1:2] + extra[2:3]
        inv = extra[3:4] + extra[4:5] + extra[5:6]
        return x_own, mean, inv, extra[6:7]

    x_own, mean1, inv1, place = do(columns, got)
    x_other = at.core(x_own)

    def first_norm(mine, theirs, mean, inv, cols):
        x = join(mine, theirs).astype(f32)
        return ((x - mean) * inv * cols[:, 0:1] + cols[:, 1:2]).astype(bf16)

    xn1 = do(first_norm, x_own, x_other, mean1, inv1, pair_cols)

    def send_products(cut, xs):
        got, kept = [], []
        for k in range(2):
            axis, step = at.steps(bool(k))[0]
            p = do(lambda w, x: dot(w, x, PLAIN).astype(bf16), cut[k][0], xs[k])
            got.append(at.along(p, axis, step))
        for k in range(2):
            kept.append(do(lambda w, x: dot(w, x, PLAIN).astype(bf16), cut[k][1], xs[k]))
        return list(zip(kept, got))

    def scatter_rest(pairs):
        for i in range(1, len(at.steps(False))):
            out = []
            for k in range(2):
                axis, step = at.steps(bool(k))[i]
                bit = (at.index(axis) // step) % 2
                send, kept = do(lambda a, b: add_split(a, b, bit.reshape(1)), *pairs[k])
                out.append((kept, at.along(send, axis, step)))
            pairs = out
        return pairs

    flying = send_products(wq_cut, [xn1[:, h] for h in halves])

    wo_parts = chip_rows(w_out, 0, S * blk, Y)
    wg_parts = chip_rows(w_up, 0, S * ffb, Y)
    wu_parts = chip_rows(w_up, Y, S * ffb, Y)
    wo_cut = [cut_weights(wo_parts, 1, blk, bool(k)) for k in range(2)]

    def positions(place):
        pos = place.reshape(S, seq) * span + (jnp.arange(seq) % span).astype(f32)[None, :]
        prow = pos.reshape(S, 1, seq)
        exponent = jnp.arange(ROTARY // 2, dtype=f32)
        inverse = 10000.0 ** (-2.0 * exponent / ROTARY)
        angles = prow * inverse[None, :, None]
        return jnp.concatenate([jnp.cos(angles), jnp.sin(angles), jnp.broadcast_to(prow, (S, 8, seq))], axis=1)

    table = do(positions, place)
    flying = scatter_rest(flying)

    def gather_steps(parts, pre):
        n = len(at.steps(False))
        state = {"parts": list(parts)}

        def start(i, after=None):
            if after is not None:
                state["parts"], _ = lax.optimization_barrier((state["parts"], after))
            state["got"] = []
            state["at"] = []
            for k in range(2):
                axis, step = list(reversed(at.steps(bool(k))))[i]
                state["at"].append((axis, step))
                state["got"].append(at.along(state["parts"][k], axis, step))

        def finish():
            def put(parts, got):
                out = []
                for k in range(2):
                    axis, step = state["at"][k]
                    ax = {"y": 0, "s": 1}[axis]
                    low = (at.index(axis) // step) % 2 == 0
                    a, b = parts[k], got[k]
                    out.append(jnp.concatenate([jnp.where(low, a, b), jnp.where(low, b, a)], ax))
                return out

            state["parts"] = do(put, state["parts"], state["got"])

        def result():
            ys, ss = Y // 2, S // 2
            bits = jnp.stack([at.y // ys, at.s // ss, jnp.int32(ys), jnp.int32(ss)]).astype(jnp.int32)
            return do(lambda p, g: last_step(p, g, bits, pre, Y, S), state["parts"], state["got"])

        return n, start, finish, result

    qkvs, attns, attn_got, stats = [], [], [], []
    for k in range(2):
        shape = (3, heads, HEAD_DIM, H)
        qkv, attn, stat = do(attend, flying[k][0].reshape(shape), flying[k][1].reshape(shape), bias, table[seqs[k]])
        qkvs.append(qkv)
        attns.append(attn.reshape(blk, H))
        attn_got.append(at.core(attns[k]))
        stats.append(stat)
    pairs = [do(join, attns[k], attn_got[k]) for k in range(2)]
    flying = send_products(wo_cut, pairs)
    wg_cut = cut_weights(wg_parts, 1, ffb, False)
    wu_cut = cut_weights(wu_parts, 1, ffb, True)

    def gain_products(wg, wu, cols):
        terms = []
        for v in (cols[:, 2], cols[:, 3]):
            t = lax.reduce_precision(v, 8, 7)
            terms += [t, v - t]
        terms = jnp.stack(terms).astype(bf16)
        out = []
        for mine, theirs in (wg, wu):
            p = dot(terms[:, :blk], mine, LAST) + dot(terms[:, blk:], theirs, LAST)
            out.append(jnp.stack([p[0] + p[1], p[2] + p[3]]).reshape(2, Y, S, ffb))
        return jnp.concatenate(out, axis=0)

    gains = do(gain_products, wg_parts, wu_parts, pair_cols)
    gain_steps = list(at.steps(False))

    def gain_step(gains):
        axis, step = gain_steps.pop(0)
        ax = {"y": 1, "s": 2}[axis]
        bit = (at.index(axis) // step) % 2
        send = lax.dynamic_slice_in_dim(gains, (1 - bit) * step, step, ax)
        kept = lax.dynamic_slice_in_dim(gains, bit * step, step, ax)
        return kept, at.along(send, axis, step)

    flying = scatter_rest(flying)
    def residual(x, a0, b0, a1, b1):
        a, b = lanes(a0, a1), lanes(b0, b1)
        hidden = x.astype(f32) + (a.astype(f32) + b.astype(f32))
        local_mean = jnp.mean(hidden, axis=0, keepdims=True)
        dev = hidden - local_mean
        return hidden, join(local_mean, jnp.sum(dev * dev, axis=0, keepdims=True))

    hidden, moments = do(residual, x_own, *flying[0], *flying[1])
    count = blk
    for axis, step in at.steps(False) + [("core", 1)]:
        other = at.core(moments) if axis == "core" else at.along(moments, axis, step)

        gain_got = gain_step(gains) if axis != "core" else (gains, None)

        def merge(a, b, gains, more):
            gap = a[0:1] - b[0:1]
            total = join(0.5 * (a[0:1] + b[0:1]), a[1:2] + b[1:2] + gap * gap * (count / 2.0))
            return total, gains if more is None else gains + more

        moments, gains = do(merge, moments, other, *gain_got)
        count *= 2

    def second_norm(hidden, moments, cols):
        inv2 = lax.rsqrt(moments[1:2] / width + eps_norm)
        z2 = (hidden - moments[0:1]) * inv2
        return (z2 * cols[:, 2:3] + cols[:, 3:4]).astype(bf16), z2, inv2

    xn2_own, z2, inv2 = do(second_norm, hidden, moments, own_cols)
    xn2 = do(join, xn2_own, at.core(xn2_own))

    flying = send_products([wg_cut, wu_cut], [xn2, xn2])

    wd_own = do(cast, w_down)
    wg = do(stack_turned, *wg_parts)
    wu = do(stack_turned, *wu_parts)
    grad_act = do(lambda w, c: mm(w, c, LAST, f32, tn=256), wd_own, cot_all)
    cot_cols = do(lambda c: own_columns(c, my_block.reshape(1), blk), cot_all)
    wo_own = do(cast, w_out)
    wq = do(stack_turned, *wq_parts)
    gains = do(lambda g: g.reshape(4, ffb).T, gains)
    flying = scatter_rest(flying)

    gate0, gate1, up0, up1, act, sums = do(gated, *flying[0], *flying[1], grad_act, gains)

    def parts_of(count, want):
        return max(n for n in range(1, want + 1) if count % (16 * n) == 0)

    def even(count, want):
        n = parts_of(count, want)
        return [(k * (count // n), count // n) for k in range(n)]

    down_rows, up_rows = even(ffb, 2), [(0, blk)]

    def push_pairs(name, g, rows):
        for k, (at_row, count) in enumerate(rows):
            reps.push((name, "theirs", k), g[blk + at_row : blk + at_row + count])
            reps.push((name, "mine", k), g[at_row : at_row + count])

    results = {"down": None, "out": None, "up": None, "qkv": None}
    states = {
        "down": (w_down, m_down, v_down),
        "out": (w_out, m_out, v_out),
        "up": (w_up, m_up, v_up),
        "qkv": (w_qkv, m_qkv, v_qkv),
    }
    rates = {"down": 0.02, "out": 0.2, "up": 0.03, "qkv": 0.03}

    def adam(name, grads, row_first, lead, unit, rb):
        results[name] = do(
            lambda s, g, prev: adam_part(s, g, core, rates[name], prev, row_first, lead, unit, rb),
            states[name],
            grads,
            results[name],
        )

    jobs = []
    for k, (at_row, count) in enumerate(down_rows):
        jobs.append(("down", [("down", k)], at_row, 0, count, 1024))
    for name, lead in (("gate", 0), ("up", Y)):
        for k, (at_row, count) in enumerate(up_rows):
            jobs.append(("up", [(name, "mine", k), (name, "theirs", k)], at_row, lead, count, S * ffb))
    for k in range(2):
        jobs.append(("out", [("out", k)], 0, k, blk, width // 2))
    for third in (2, 1, 0):
        jobs.append(("qkv", [(third, 0), (third, 1, "theirs")], 0, third * Y, blk, S * blk))
    received = {}

    def update(limit):
        for name in list(reps.done):
            if name in ("out", 0, 1, 2):
                g = reps.done.pop(name)
                half = g.shape[0] // 2
                reps.done[(name, 0)] = g[:half]
                reps.done[(name, 1) if name == "out" else (name, 1, "theirs")] = g[half:]
        for name in list(reps.done):
            if "theirs" in name and name not in received:
                received[name] = at.core(reps.done[name])
        while jobs and limit and all(k in reps.done for k in jobs[0][1]):
            name, needs, at_row, lead, count, unit = jobs.pop(0)
            rb = max(n for n in range(8, min(count, 176) + 1, 8) if count % n == 0 and at_row % n == 0)
            adam(name, [received[k] if "theirs" in k else reps.done[k] for k in needs], at_row, lead, unit, rb)
            limit -= 1

    def ticks(n):
        for _ in range(n):
            reps.tick()

    wide = 2 * FF // 8

    def quarter_heads(x):
        return [x[:, h][None, None] for h in halves]

    n, start, finish, gate_all = gather_steps([gate0[None, None], gate1[None, None]], 1)
    start(0)
    g_down = do(lambda a, c: mm(a, c, PLAIN, bf16, tn=512), act, cot_all)
    for k, (at_row, count) in enumerate(down_rows):
        reps.push(("down", k), g_down[at_row : at_row + count])
    ticks(1)

    steps2 = at.steps(False) + [("core", 1)]

    def sum_send(sums, axis, step):
        return at.core(sums) if axis == "core" else at.along(sums, axis, step)

    def sum_step(sums, axis, step):
        return do(lambda a, b: a + b, sums, sum_send(sums, axis, step))

    tiny = list(steps2)
    sums_got = sum_send(sums, *tiny.pop(0))
    for i in range(1, n):
        finish()
        sums = do(lambda a, b: a + b, sums, sums_got)
        sums_got = sum_send(sums, *tiny.pop(0))
        start(i, sums)
        ticks(1)
    n, start_up, finish_up, up_all = gather_steps([up0[None, None], up1[None, None]], 1)
    ggate_all = gate_all().reshape(Y * S * ffb, T)
    sums = do(lambda a, b: a + b, sums, sums_got)
    start_up(0, sums)
    while tiny:
        sums = sum_step(sums, *tiny.pop(0))
    g_gate = do(lambda x, g: mm(x, g, LAST, bf16, tn=wide), xn2, ggate_all)
    push_pairs("gate", g_gate, up_rows)
    finish_up()
    for i in range(1, n):
        start_up(i)
        if i == 1:
            part_gate = do(lambda w, g: mm(w, g, PLAIN, f32, tn=256), wg, ggate_all)
            out_part = do(lambda w, a: mm(w, a, FIRST, bf16, tm=512), wd_own, act)
            ticks(1)
        if i < n - 1:
            finish_up()
    gup_all = up_all().reshape(Y * S * ffb, T)
    part = do(lambda w, g, p: dot(w, g, PLAIN) + p, wu, gup_all, part_gate)
    part_theirs = at.core(part[blk:])

    def branch(a, b, cot, z, scale, gain, sums):
        gxn2 = a + b
        e = gxn2 * gain
        grad_hidden = cot.astype(f32) + scale * (e - sums[0:1] / width - z * (sums[1:2] / width))
        return grad_hidden.astype(bf16), grad_hidden, gxn2

    grad_branch, grad_hidden, gxn2 = do(
        branch, part[:blk], part_theirs, cot_cols, z2, inv2, own_cols[:, 2:3], sums
    )
    n, start, finish, branch_all = gather_steps(quarter_heads(grad_branch), 1)
    start(0)
    g_up = do(lambda x, g: mm(x, g, LAST, bf16, tn=wide), xn2, gup_all)
    push_pairs("up", g_up, up_rows)
    finish()
    for i in range(1, n):
        start(i)
        if i == 1:
            ticks(1)
        if i < n - 1:
            finish()
    gbr_c = branch_all()[0]
    gbr_o = at.core(gbr_c)
    gbr = do(lambda a, b: in_order(a, b, 1).reshape(width, T), gbr_c, gbr_o)
    grad_attn = do(lambda w, g: dot(w, g, PLAIN).astype(bf16), wo_own, gbr)

    gqkvs = []
    for k in range(2):
        dout = grad_attn[:, halves[k]].reshape(heads, HEAD_DIM, H)
        gqkvs.append(do(attend_back, qkvs[k], dout, stats[k], table[seqs[k]]).reshape(3, blk, H))
    n, start, finish, gqkv_done = gather_steps([g.reshape(1, 1, 3 * blk, H) for g in gqkvs], 3)
    start(0)
    attn = lanes(*attns)
    g_out = do(
        lambda a, g: join(*[mm(a, g[k * width // 2 : (k + 1) * width // 2], LAST, bf16, tn=512) for k in range(2)]),
        attn,
        gbr,
    )
    reps.push("out", g_out)
    update(1)
    ticks(1)
    finish()
    for i in range(1, n):
        start(i)
        if i == 1:
            update(1)
            ticks(1)
        if i < n - 1:
            finish()
    gqkv = gqkv_done().reshape(3, Y * S * blk, T)
    out_sum = lax.psum_scatter(do(lambda p: p, out_part), plane, scatter_dimension=0, tiled=True)
    g = do(lambda x, g: mm(x, g, LAST, bf16, tn=512), xn1, gqkv[2])
    reps.push(2, g)
    ticks(1)
    for third in (1, 0):
        g = do(lambda x, g: mm(x, g, LAST, bf16, tn=512), xn1, gqkv[third])
        reps.push(third, g)
    part = do(lambda w, g: mm(w, g, PLAIN, f32, tn=256), wq, gqkv.reshape(3 * Y * S * blk, T))
    part_theirs = at.core(part[blk:])

    def first_back(a, b, x, mean, inv, gain, gxn2, z2, gqkv0, gqkv1):
        gxn1 = a + b
        z1 = (x.astype(f32) - mean) * inv
        e = gxn1 * gain
        sums = join(jnp.sum(e, axis=0, keepdims=True), jnp.sum(e * z1, axis=0, keepdims=True))
        small = jnp.concatenate(
            [
                jnp.sum(gxn1 * z1, axis=1)[None],
                jnp.sum(gxn1, axis=1)[None],
                jnp.sum(gxn2 * z2, axis=1)[None],
                jnp.sum(gxn2, axis=1)[None],
                jnp.sum(gqkv0.astype(f32), axis=2) + jnp.sum(gqkv1.astype(f32), axis=2),
            ],
            axis=0,
        )
        return sums, small, gxn1, z1

    sums, small, gxn1, z1 = do(
        first_back, part[:blk], part_theirs, x_own, mean1, inv1, own_cols[:, 0:1], gxn2, z2, *gqkvs
    )
    for axis, step in steps2:
        sums = sum_step(sums, axis, step)
    ticks(1)
    input_grad = do(
        lambda h, grad, z, scale, gain, sums: (
            h + scale * (grad * gain - sums[0:1] / width - z * (sums[1:2] / width))
        ).astype(bf16),
        grad_hidden,
        gxn1,
        z1,
        inv1,
        own_cols[:, 0:1],
        sums,
    )

    def to_rows(cols):
        split = do(lambda c: c.reshape(blk, S, at.ctx_size, rows).transpose(2, 1, 0, 3).reshape(nb, blk, rows), cols)
        got = lax.all_to_all(split, plane, split_axis=0, concat_axis=0, tiled=True)
        return do(lambda g: g.reshape(width, rows).T, got)

    input_rows = to_rows(input_grad).astype(f32)
    steps_rep = []
    step = 1
    while step < lax.axis_size("rep"):
        steps_rep.append(step)
        step *= 2

    def small_step():
        nonlocal small
        k = steps_rep.pop(0)
        other = lax.ppermute(small, "rep", [(i, i ^ k) for i in range(lax.axis_size("rep"))])
        small = do(lambda a, b: a + b, small, other)
        return small

    reps.tick(small_step)
    update(1)
    reps.tick(small_step)
    sent = do(lambda s: jnp.broadcast_to(s.reshape(1, 7, blk), (nb, 7, blk)), small)
    small_all = lax.all_to_all(sent, plane, split_axis=0, concat_axis=0, tiled=True)

    def norm_update(every, *a):
        return adam_update(*a, every.transpose(1, 0, 2).reshape(7, width), 0.3, 0.0)

    mn, vn, wn = do(norm_update, small_all, norm_params, m_norm, v_norm)
    update(2)
    ticks(1)
    update(1)
    out_cols = do(lambda h, a: (h + a.astype(f32)).astype(bf16), hidden, out_sum)
    block_output = to_rows(out_cols)
    while reps.busy():
        reps.tick()
        update(2)
    update(len(jobs))
    return (
        (block_output.reshape(tokens.shape), input_rows.reshape(tokens.shape))
        + tuple(results["qkv"])
        + tuple(results["out"])
        + tuple(results["up"])
        + tuple(results["down"])
        + (mn, vn, wn)
    )


def solution(mesh):
    tok = P("rep", "ctx", "shard", None)
    row = P(("ctx", "shard"), None)
    placed = (tok, tok, P("rep", "shard", None)) + (row,) * 4 + (P(),) + (row,) * 8 + (P(), P())
    return jax.shard_map(
        body,
        mesh=mesh,
        in_specs=placed,
        out_specs=(tok, tok) + (row,) * 12 + (P(),) * 3,
        check_vma=False,
    )
```

```python
import functools

import jax
import jax.numpy as jnp
from jax import lax
from jax.experimental import pallas as pl
from jax.experimental.pallas import tpu as pltpu
from jax.sharding import PartitionSpec as P

HEADS = 32
HEAD_DIM = 64
FF = 5632
ROTARY = 16
STEP = 10

eps_norm = 1e-05
masked_score = -1e30
beta_one = 0.9
beta_two = 0.999
adam_eps = 1e-08
weight_decay = 0.1
score_scale = HEAD_DIM ** (-0.5)
FIRST = (((0,), (0,)), ((), ()))
LAST = (((1,), (1,)), ((), ()))
PLAIN = (((1,), (0,)), ((), ()))
bf16 = jnp.bfloat16
f32 = jnp.float32


def dot(a, b, dims):
    return lax.dot_general(a, b, dims, preferred_element_type=f32)


def adam_update(weight, moment_one, moment_two, grad, step_rate, decay_rate):
    first_new = beta_one * moment_one + (1.0 - beta_one) * grad
    second_new = beta_two * moment_two + (1.0 - beta_two) * grad * grad
    first_hat = first_new / (1.0 - beta_one**STEP)
    second_hat = second_new / (1.0 - beta_two**STEP)
    weight_new = weight - step_rate * (
        first_hat / (jnp.sqrt(second_hat) + adam_eps) + decay_rate * weight
    )
    return (first_new, second_new, weight_new)


class Plane:
    def __init__(self):
        self.s_size = lax.axis_size("shard")
        self.ctx_size = lax.axis_size("ctx")
        self.y_size = self.ctx_size // 2
        self.ctx = lax.axis_index("ctx")
        self.s = lax.axis_index("shard")
        self.y = self.ctx // 2
        self.c = self.ctx % 2
        self.blocks = self.ctx_size * self.s_size

    def core(self, x):
        return lax.ppermute(x, "ctx", [(i, i ^ 1) for i in range(self.ctx_size)])

    def along(self, x, axis, step):
        if axis == "y":
            return lax.ppermute(x, "ctx", [(i, i ^ (2 * step)) for i in range(self.ctx_size)])
        return lax.ppermute(x, "shard", [(i, i ^ step) for i in range(self.s_size)])

    def index(self, axis):
        return self.y if axis == "y" else self.s

    def steps(self, flip):
        ys = []
        k = self.y_size // 2
        while k:
            ys.append(("y", k))
            k //= 2
        ss = []
        k = self.s_size // 2
        while k:
            ss.append(("s", k))
            k //= 2
        return ys + ss if flip else ss + ys

    def chip_exchange(self, x, take):
        out = [(self.y, self.s, take(self.y, self.s))]
        for ry in range(self.y_size):
            for rs in range(self.s_size):
                if ry or rs:
                    y, s = self.y ^ ry, self.s ^ rs
                    mask = 2 * ry * self.s_size + rs
                    perm = [(i, i ^ mask) for i in range(self.blocks)]
                    out.append((y, s, lax.ppermute(take(y, s), ("ctx", "shard"), perm)))
        return out

    def sum_all(self, x):
        for axis, step in self.steps(False):
            x = x + self.along(x, axis, step)
        return x + self.core(x)

    def scatter_sum(self, p, flip):
        axes = {"y": 1, "s": 2}
        steps = self.steps(flip)
        kept = got = None
        for n, (axis, step) in enumerate(steps):
            ax = axes[axis]
            bit = (self.index(axis) // step) % 2
            kept = lax.dynamic_slice_in_dim(p, bit * step, step, ax)
            send = lax.dynamic_slice_in_dim(p, (1 - bit) * step, step, ax)
            got = self.along(send, axis, step)
            if n + 1 < len(steps):
                p = (kept.astype(f32) + got.astype(f32)).astype(bf16)
        return kept[:, 0, 0], got[:, 0, 0]

    def gather(self, p, flip):
        axes = {"y": 1, "s": 2}
        p = p[:, None, None]
        for axis, step in reversed(self.steps(flip)):
            ax = axes[axis]
            bit = (self.index(axis) // step) % 2
            got = self.along(p, axis, step)
            first = bit == 0
            p = jnp.concatenate([jnp.where(first, p, got), jnp.where(first, got, p)], ax)
        return p


class Order:
    def __init__(self):
        self.last = None

    def __call__(self, stage, *args):
        if self.last is not None:
            args, self.last = lax.optimization_barrier((args, self.last))
        out = stage(*args)
        self.last = jax.tree.leaves(out)[0]
        return out


SMALL = pl.CostEstimate(flops=1024, bytes_accessed=1024, transcendentals=0)


class RepSum:
    def __init__(self, order):
        self.order = order
        z = lax.axis_index("rep")
        self.end = (z == 0) | (z == lax.axis_size("rep") - 1)
        self.queue = []
        self.flight = []
        self.depth = 1
        self.done = {}

    def push(self, name, g):
        self.queue.append((name, g))

    def busy(self):
        return bool(self.queue or self.flight)

    def tick(self, between=None):
        old = {}
        if len(self.flight) >= self.depth or (self.flight and not self.queue):
            old = self.flight.pop(0)
        new = self.queue.pop(0) if self.queue else None
        values = {}
        if "in" in old:
            values["g"], values["g_got"] = old["in"][1], old["in_got"]
        if "mid" in old:
            values["s"], values["s_got"] = old["mid"][1], old["mid_got"]
        if new:
            values["new"] = new[1]
        both = new and "mid" in old and new[1].shape == old["mid"][1].shape
        if "out" in old:
            values["out_got"] = old["out_got"]

        def stage(v):
            def add(a, b):
                return lax.reduce_precision(a.astype(f32) + b.astype(f32), 8, 7).astype(bf16)

            out = {}
            if "g" in v:
                out["a_sum"] = add(v["g"], v["g_got"])
            if "s" in v:
                total = add(v["s"], v["s_got"])
                out["total"] = jnp.where(self.end, v["new"], total) if both else total
            if "new" in v and not both:
                out["new"] = v["new"]
            if "out_got" in v:
                out["z_got"] = v["out_got"]
            return out

        if not values:
            return
        out = self.order(stage, values)
        if between is not None:
            out, self.kept = lax.optimization_barrier((out, between()))
        if "out" in old:
            self.done[old["out"][0]] = jnp.where(self.end, out["z_got"], old["out"][1])
        slot = {}
        if both:
            got = lax.ppermute(out["total"], "rep", [(0, 1), (1, 0), (2, 3), (3, 2)])
            slot = {"in": new, "in_got": got, "out": (old["mid"][0], out["total"]), "out_got": got}
        else:
            if new:
                slot["in"] = new
                slot["in_got"] = lax.ppermute(out["new"], "rep", [(0, 1), (3, 2)])
            if "mid" in old:
                slot["out"] = (old["mid"][0], out["total"])
                slot["out_got"] = lax.ppermute(out["total"], "rep", [(1, 0), (2, 3)])
        if "in" in old:
            slot["mid"] = (old["in"][0], out["a_sum"])
            slot["mid_got"] = lax.ppermute(out["a_sum"], "rep", [(1, 2), (2, 1)])
        if slot:
            self.flight.append(slot)


def cast_kernel(w_ref, out_ref):
    out_ref[...] = w_ref[...].astype(bf16)


def cast(w):
    rows, width = w.shape
    unit = max(n for n in (128, 256, 512, 1024, 1408, 2048, 2816) if width % n == 0)
    spec = pl.BlockSpec((rows, unit), lambda i: (0, i))
    return pl.pallas_call(
        cast_kernel,
        grid=(width // unit,),
        in_specs=[spec],
        out_specs=spec,
        out_shape=jax.ShapeDtypeStruct(w.shape, bf16),
        compiler_params=pltpu.CompilerParams(vmem_limit_bytes=48 * 1024 * 1024),
        cost_estimate=SMALL,
    )(w)


def gated_kernel(ga_ref, gb_ref, ua_ref, ub_ref, grad_ref, gains_ref, g0_ref, g1_ref, u0_ref, u1_ref, act_ref, sums_ref):
    half = g0_ref.shape[1]
    gate = ga_ref[...].astype(f32) + gb_ref[...].astype(f32)
    up = ua_ref[...].astype(f32) + ub_ref[...].astype(f32)
    sig = jax.nn.sigmoid(gate)
    silu = gate * sig
    grad = grad_ref[...]
    act_ref[...] = (silu * up).astype(bf16)
    ggate = (grad * up * sig * (1.0 + gate * (1.0 - sig))).astype(bf16)
    gup = (grad * silu).astype(bf16)
    g0_ref[...] = ggate[:, :half]
    g1_ref[...] = ggate[:, half:]
    u0_ref[...] = gup[:, :half]
    u1_ref[...] = gup[:, half:]
    a, b = ggate.astype(f32), gup.astype(f32)
    e = jnp.sum(a * gains_ref[:, 0:1] + b * gains_ref[:, 2:3], axis=0, keepdims=True)
    ez = jnp.sum(a * (gate - gains_ref[:, 1:2]) + b * (up - gains_ref[:, 3:4]), axis=0, keepdims=True)
    both = jnp.concatenate([e, ez], axis=0)

    @pl.when(pl.program_id(0) == 0)
    def _():
        sums_ref[...] = both

    @pl.when(pl.program_id(0) > 0)
    def _():
        sums_ref[...] += both


def gated(ga, gb, ua, ub, grad_act, gains):
    rows, t = grad_act.shape
    n = max(n for n in (1, 2, 4) if rows % (16 * n) == 0)
    whole = pl.BlockSpec((rows // n, t), lambda i: (i, 0))
    half = pl.BlockSpec((rows // n, t // 2), lambda i: (i, 0))
    out_half = jax.ShapeDtypeStruct((rows, t // 2), bf16)
    return pl.pallas_call(
        gated_kernel,
        grid=(n,),
        in_specs=[whole] * 5 + [pl.BlockSpec((rows // n, 4), lambda i: (i, 0))],
        out_specs=[half] * 4 + [whole, pl.BlockSpec((2, t), lambda i: (0, 0))],
        out_shape=[out_half] * 4 + [jax.ShapeDtypeStruct((rows, t), bf16), jax.ShapeDtypeStruct((2, t), f32)],
        compiler_params=pltpu.CompilerParams(vmem_limit_bytes=56 * 1024 * 1024),
        cost_estimate=SMALL,
    )(ga, gb, ua, ub, grad_act, gains)


def own_columns_kernel(block_ref, x_ref, out_ref):
    out_ref[...] = x_ref[...].T


def own_columns(x, block, width):
    rows = x.shape[0]
    if width % 128:
        return lax.dynamic_slice_in_dim(x, block[0] * width, width, 1).T
    tile = min(rows, 512)
    return pl.pallas_call(
        own_columns_kernel,
        grid_spec=pltpu.PrefetchScalarGridSpec(
            num_scalar_prefetch=1,
            grid=(rows // tile,),
            in_specs=[pl.BlockSpec((tile, width), lambda i, block: (i, block[0]))],
            out_specs=pl.BlockSpec((width, tile), lambda i, block: (0, i)),
        ),
        out_shape=jax.ShapeDtypeStruct((width, rows), bf16),
        compiler_params=pltpu.CompilerParams(vmem_limit_bytes=48 * 1024 * 1024),
        cost_estimate=SMALL,
    )(block, x)


def split_kernel(core_ref, w_ref, mine_ref, theirs_ref):
    unit = mine_ref.shape[0]
    first = core_ref[0] == 0
    a, b = w_ref[:, :unit], w_ref[:, unit:]
    mine_ref[...] = jnp.where(first, a, b).T.astype(bf16)
    theirs_ref[...] = jnp.where(first, b, a).T.astype(bf16)


def split_columns(w, core, lead, unit, count):
    rows = w.shape[0]
    half = pl.BlockSpec((unit, rows), lambda j, core: (j, 0))
    out = jax.ShapeDtypeStruct((count * unit, rows), bf16)
    return pl.pallas_call(
        split_kernel,
        grid_spec=pltpu.PrefetchScalarGridSpec(
            num_scalar_prefetch=1,
            grid=(count,),
            in_specs=[pl.BlockSpec((rows, 2 * unit), lambda j, core: (0, lead + j))],
            out_specs=[half, half],
        ),
        out_shape=[out, out],
        compiler_params=pltpu.CompilerParams(vmem_limit_bytes=32 * 1024 * 1024),
        cost_estimate=SMALL,
    )(core, w)


def arrange_kernel(at_ref, a_ref, b_ref, c_ref, d_ref, send_ref, keep_ref):
    send_ref[...] = jnp.concatenate([a_ref[...], b_ref[...]], axis=1)
    keep_ref[...] = jnp.concatenate([c_ref[...], d_ref[...]], axis=1)


def arrange(mine, got, place, pre, y_size, s_size, unit, flip):
    r = mine.shape[1]
    half = pre * y_size * s_size // 2

    def block(i, place, keep):
        p = i % pre
        i = i // pre
        if flip:
            s, y = i % s_size, i // s_size
            bit = place[0] // (y_size // 2)
            bit = bit if keep else 1 - bit
            y = y + bit * (y_size // 2)
        else:
            y, s = i % y_size, i // y_size
            bit = place[1] // (s_size // 2)
            bit = bit if keep else 1 - bit
            s = s + bit * (s_size // 2)
        return ((p * y_size + y) * s_size + s, 0)

    def spec(keep):
        return pl.BlockSpec((unit, r), lambda i, place: block(i, place, keep))

    out = jax.ShapeDtypeStruct((half * unit, 2 * r), bf16)
    out_spec = pl.BlockSpec((unit, 2 * r), lambda i, place: (i, 0))
    return pl.pallas_call(
        arrange_kernel,
        grid_spec=pltpu.PrefetchScalarGridSpec(
            num_scalar_prefetch=1,
            grid=(half,),
            in_specs=[spec(False), spec(False), spec(True), spec(True)],
            out_specs=[out_spec, out_spec],
        ),
        out_shape=[out, out],
        compiler_params=pltpu.CompilerParams(vmem_limit_bytes=32 * 1024 * 1024),
        cost_estimate=SMALL,
    )(place, mine, got, mine, got)


def product_kernel(dims, a_ref, b_ref, *refs):
    p = dot(a_ref[...], b_ref[...], dims)
    if len(refs) == 2:
        p = p + refs[0][...]
    refs[-1][...] = p.astype(refs[-1].dtype)


def mm(a, b, dims, dtype, tm=None, tn=None, add=None):
    (ca,), (cb,) = dims[0]
    m, k, n = a.shape[1 - ca], a.shape[ca], b.shape[1 - cb]
    tm, tn = tm or m, tn or n
    a_block = [0, 0]
    a_block[ca], a_block[1 - ca] = k, tm
    b_block = [0, 0]
    b_block[cb], b_block[1 - cb] = k, tn
    out = pl.BlockSpec((tm, tn), lambda i, j: (i, j))
    return pl.pallas_call(
        functools.partial(product_kernel, dims),
        grid=(m // tm, n // tn),
        in_specs=[
            pl.BlockSpec(tuple(a_block), (lambda i, j: (0, i)) if ca == 0 else (lambda i, j: (i, 0))),
            pl.BlockSpec(tuple(b_block), (lambda i, j: (0, j)) if cb == 0 else (lambda i, j: (j, 0))),
        ]
        + ([] if add is None else [out]),
        out_specs=out,
        out_shape=jax.ShapeDtypeStruct((m, n), dtype),
        compiler_params=pltpu.CompilerParams(vmem_limit_bytes=48 * 1024 * 1024),
        cost_estimate=SMALL,
    )(*((a, b) if add is None else (a, b, add)))


def last_step_kernel(bits_ref, own0_ref, got0_ref, own1_ref, got1_ref, out_ref):
    y, s = pl.program_id(1), pl.program_id(2)
    half = own0_ref.shape[3]
    ys, ss = bits_ref[2], bits_ref[3]
    a = jnp.where(s // ss == bits_ref[1], own0_ref[0, 0], got0_ref[0, 0])
    b = jnp.where(y // ys == bits_ref[0], own1_ref[0, 0], got1_ref[0, 0])
    out_ref[0, 0, 0, :, :half] = a
    out_ref[0, 0, 0, :, half:] = b


def last_step(parts, got, bits, pre, y_size, s_size):
    rows, half = parts[0].shape[2] // pre, parts[0].shape[3]
    along_s = pl.BlockSpec((1, 1, rows, half), lambda p, y, s, bits: (y, s % (s_size // 2), p, 0))
    along_y = pl.BlockSpec((1, 1, rows, half), lambda p, y, s, bits: (y % (y_size // 2), s, p, 0))
    return pl.pallas_call(
        last_step_kernel,
        grid_spec=pltpu.PrefetchScalarGridSpec(
            num_scalar_prefetch=1,
            grid=(pre, y_size, s_size),
            in_specs=[along_s, along_s, along_y, along_y],
            out_specs=pl.BlockSpec((1, 1, 1, rows, 2 * half), lambda p, y, s, bits: (p, y, s, 0, 0)),
        ),
        out_shape=jax.ShapeDtypeStruct((pre, y_size, s_size, rows, 2 * half), bf16),
        compiler_params=pltpu.CompilerParams(vmem_limit_bytes=48 * 1024 * 1024),
        cost_estimate=SMALL,
    )(bits, parts[0], got[0], parts[1], got[1])


def stack_turned_kernel(a_ref, b_ref, out_ref):
    r = a_ref.shape[1]
    out_ref[:r] = a_ref[...].T
    out_ref[r:] = b_ref[...].T


def stack_turned(a, b):
    rows, width = a.shape
    n = max(n for n in (1, 2, 4, 6, 8, 11) if rows % (128 * n) == 0)
    spec = pl.BlockSpec((rows // n, width), lambda i: (i, 0))
    return pl.pallas_call(
        stack_turned_kernel,
        grid=(n,),
        in_specs=[spec, spec],
        out_specs=pl.BlockSpec((2 * width, rows // n), lambda i: (0, i)),
        out_shape=jax.ShapeDtypeStruct((2 * width, rows), bf16),
        compiler_params=pltpu.CompilerParams(vmem_limit_bytes=48 * 1024 * 1024),
        cost_estimate=SMALL,
    )(a, b)


def add_split_kernel(bit_ref, a_ref, b_ref, c_ref, d_ref, send_ref, keep_ref):
    send_ref[...] = (a_ref[...].astype(f32) + b_ref[...].astype(f32)).astype(bf16)
    keep_ref[...] = (c_ref[...].astype(f32) + d_ref[...].astype(f32)).astype(bf16)


def add_split(kept, got, bit):
    rows, t = kept.shape
    half = rows // 2
    n = max(n for n in (1, 2, 3, 4) if half % (16 * n) == 0)
    rb = half // n
    away = pl.BlockSpec((rb, t), lambda i, bit: ((1 - bit[0]) * n + i, 0))
    here = pl.BlockSpec((rb, t), lambda i, bit: (bit[0] * n + i, 0))
    out = jax.ShapeDtypeStruct((half, t), bf16)
    out_spec = pl.BlockSpec((rb, t), lambda i, bit: (i, 0))
    return pl.pallas_call(
        add_split_kernel,
        grid_spec=pltpu.PrefetchScalarGridSpec(
            num_scalar_prefetch=1,
            grid=(n,),
            in_specs=[away, away, here, here],
            out_specs=[out_spec, out_spec],
        ),
        out_shape=[out, out],
        compiler_params=pltpu.CompilerParams(vmem_limit_bytes=48 * 1024 * 1024),
        cost_estimate=SMALL,
    )(bit, kept, got, kept, got)


def token_rows_kernel(core_ref, a_ref, b_ref, c_ref, d_ref, out_ref):
    mine = core_ref[0] == pl.program_id(2)
    half = out_ref.shape[0] // 2
    out_ref[:half] = jnp.where(mine, a_ref[0, 0], c_ref[0, 0])
    out_ref[half:] = jnp.where(mine, b_ref[0, 0], d_ref[0, 0])


def token_rows(mine, theirs, core):
    y_size, s_size, rows, width = mine[0].shape
    part = pl.BlockSpec((1, 1, rows, width), lambda s, y, c, core: (y, s, 0, 0))
    return pl.pallas_call(
        token_rows_kernel,
        grid_spec=pltpu.PrefetchScalarGridSpec(
            num_scalar_prefetch=1,
            grid=(s_size, y_size, 2),
            in_specs=[part] * 4,
            out_specs=pl.BlockSpec((2 * rows, width), lambda s, y, c, core: ((s * y_size + y) * 2 + c, 0)),
        ),
        out_shape=jax.ShapeDtypeStruct((s_size * y_size * 4 * rows, width), bf16),
        compiler_params=pltpu.CompilerParams(vmem_limit_bytes=32 * 1024 * 1024),
        cost_estimate=SMALL,
    )(core, *mine, *theirs)


def adam_kernel(rate, two, core_ref, w_ref, m_ref, v_ref, *refs):
    grad = refs[0][...].astype(f32)
    if two:
        other = refs[1][...].astype(f32)
        mine = core_ref[0] == 0
        grad = jnp.concatenate([jnp.where(mine, grad, other), jnp.where(mine, other, grad)], axis=1)
    new_m_ref, new_v_ref, new_w_ref = refs[-3:]
    new_m, new_v, new_w = adam_update(w_ref[...], m_ref[...], v_ref[...], grad, rate, weight_decay)
    new_m_ref[...] = new_m
    new_v_ref[...] = new_v
    new_w_ref[...] = new_w


def adam_part(state, grads, core, rate, prev, row_first, lead, unit, rb):
    w, m, v = state
    two = len(grads) == 2
    rows, width = grads[0].shape
    whole = pl.BlockSpec((rb, unit * len(grads)), lambda i, g, core: (row_first // rb + i, lead + g))
    half = pl.BlockSpec((rb, unit), lambda i, g, core: (i, g))
    out = jax.ShapeDtypeStruct(w.shape, f32)
    extra, aliases = [], {}
    if prev is not None:
        extra = list(prev)
        aliases = {4 + len(grads) + i: i for i in range(3)}
    return pl.pallas_call(
        functools.partial(adam_kernel, rate, two),
        grid_spec=pltpu.PrefetchScalarGridSpec(
            num_scalar_prefetch=1,
            grid=(rows // rb, width // unit),
            in_specs=[whole] * 3 + [half] * len(grads) + [pl.BlockSpec(memory_space=pl.ANY)] * len(extra),
            out_specs=[whole] * 3,
        ),
        out_shape=[out] * 3,
        input_output_aliases=aliases,
        compiler_params=pltpu.CompilerParams(vmem_limit_bytes=48 * 1024 * 1024),
        cost_estimate=SMALL,
    )(core, w, m, v, *grads, *extra)


def attend_kernel(kept_ref, got_ref, bias_ref, table_ref, qkv_ref, out_ref, stat_ref):
    half = ROTARY // 2
    cos, sin, pos = table_ref[0, :half], table_ref[0, half:ROTARY], table_ref[0, ROTARY:]
    parts = []
    for i in range(3):
        v = kept_ref[i, 0].astype(f32) + got_ref[i, 0].astype(f32) + bias_ref[i, 0]
        if i < 2:
            a, b = v[:half], v[half:ROTARY]
            v = jnp.concatenate([a * cos - b * sin, b * cos + a * sin, v[ROTARY:]], axis=0)
        v = v.astype(bf16)
        qkv_ref[i, 0] = v
        parts.append(v)
    q, k, v = parts
    scores = dot(k, q, FIRST) * score_scale
    scores = jnp.where(pos.T[:, :1] <= pos[:1], scores, masked_score)
    peak = jnp.max(scores, axis=0, keepdims=True)
    e = jnp.exp(scores - peak)
    total = jnp.sum(e, axis=0, keepdims=True)
    p = (e / total).astype(bf16)
    out_ref[0] = dot(v, p, PLAIN).astype(bf16)
    stat_ref[0, 0] = jnp.concatenate([peak, total], axis=0)


def attend(kept, got, bias, table):
    _, heads, hd, t = kept.shape
    seqs, _, seq = table.shape
    big = pl.BlockSpec((3, 1, hd, seq), lambda s, h: (0, h, 0, s))
    table_spec = pl.BlockSpec((1, table.shape[1], seq), lambda s, h: (s, 0, 0))
    stat = pl.BlockSpec((1, 1, 2, seq), lambda s, h: (s, h, 0, 0))
    return pl.pallas_call(
        attend_kernel,
        grid=(seqs, heads),
        in_specs=[
            big,
            big,
            pl.BlockSpec((3, 1, hd, 1), lambda s, h: (0, h, 0, 0)),
            table_spec,
        ],
        out_specs=[big, pl.BlockSpec((1, hd, seq), lambda s, h: (h, 0, s)), stat],
        out_shape=[
            jax.ShapeDtypeStruct((3, heads, hd, t), bf16),
            jax.ShapeDtypeStruct((heads, hd, t), bf16),
            jax.ShapeDtypeStruct((seqs, heads, 2, seq), f32),
        ],
        compiler_params=pltpu.CompilerParams(vmem_limit_bytes=32 * 1024 * 1024),
        cost_estimate=SMALL,
    )(kept, got, bias, table)


def attend_back_kernel(qkv_ref, dout_ref, stat_ref, table_ref, out_ref):
    half = ROTARY // 2
    cos, sin, pos = table_ref[0, :half], table_ref[0, half:ROTARY], table_ref[0, ROTARY:]
    q, k, v = qkv_ref[0, 0], qkv_ref[1, 0], qkv_ref[2, 0]
    dout = dout_ref[0]
    scores = dot(k, q, FIRST) * score_scale
    scores = jnp.where(pos.T[:, :1] <= pos[:1], scores, masked_score)
    p = jnp.exp(scores - stat_ref[0, 0, :1]) / stat_ref[0, 0, 1:]
    dp = dot(v, dout, FIRST)
    inner = jnp.sum(p * dp, axis=0, keepdims=True)
    ds = (p * (dp - inner)).astype(bf16)

    def back(x):
        a, b = x[:half], x[half:ROTARY]
        return jnp.concatenate([a * cos + b * sin, b * cos - a * sin, x[ROTARY:]], axis=0)

    out_ref[0, 0] = back(dot(k, ds, PLAIN) * score_scale).astype(bf16)
    out_ref[1, 0] = back(dot(q, ds, LAST) * score_scale).astype(bf16)
    out_ref[2, 0] = dot(dout, p.astype(bf16), LAST).astype(bf16)


def attend_back(qkv, dout, stats, table):
    _, heads, hd, t = qkv.shape
    seqs, _, seq = table.shape
    big = pl.BlockSpec((3, 1, hd, seq), lambda s, h: (0, h, 0, s))
    table_spec = pl.BlockSpec((1, table.shape[1], seq), lambda s, h: (s, 0, 0))
    stat = pl.BlockSpec((1, 1, 2, seq), lambda s, h: (s, h, 0, 0))
    return pl.pallas_call(
        attend_back_kernel,
        grid=(seqs, heads),
        in_specs=[
            big,
            pl.BlockSpec((1, hd, seq), lambda s, h: (h, 0, s)),
            stat,
            table_spec,
        ],
        out_specs=big,
        out_shape=jax.ShapeDtypeStruct((3, heads, hd, t), bf16),
        compiler_params=pltpu.CompilerParams(vmem_limit_bytes=32 * 1024 * 1024),
        cost_estimate=SMALL,
    )(qkv, dout, stats, table)


def body(
    tokens,
    cotangent,
    span_order,
    w_qkv,
    w_out,
    w_up,
    w_down,
    norm_params,
    m_qkv,
    v_qkv,
    m_out,
    v_out,
    m_up,
    v_up,
    m_down,
    v_down,
    m_norm,
    v_norm,
):
    at = Plane()
    do = Order()
    reps = RepSum(do)
    width = tokens.shape[3]
    rows = tokens.shape[1]
    S, Y, nb = at.s_size, at.y_size, at.blocks
    plane = ("ctx", "shard")
    blk = width // nb
    ffb = FF // nb
    heads = blk // HEAD_DIM
    seq = rows * at.ctx_size
    T = S * seq
    H = T // 2
    first = at.c == 0
    core = at.c.reshape(1)
    my_block = at.ctx * S + at.s
    halves = (slice(0, H), slice(H, T))
    seqs = (slice(0, S // 2), slice(S // 2, S))

    def pick(x, axis, which):
        return lax.dynamic_index_in_dim(x, which, axis, keepdims=False)

    def in_order(mine, theirs, axis):
        return jnp.stack([jnp.where(first, mine, theirs), jnp.where(first, theirs, mine)], axis=axis)

    def join(a, b):
        return jnp.concatenate([a, b], axis=0)

    def lanes(a, b):
        return jnp.concatenate([a, b], axis=1)

    def gather_steps(parts, pre):
        n = len(at.steps(False))
        state = {"parts": list(parts)}

        def start(i, after=None):
            if after is not None:
                state["parts"], _ = lax.optimization_barrier((state["parts"], after))
            state["got"] = []
            state["at"] = []
            for k in range(2):
                axis, step = list(reversed(at.steps(bool(k))))[i]
                state["at"].append((axis, step))
                state["got"].append(at.along(state["parts"][k], axis, step))

        def finish():
            def put(parts, got):
                out = []
                for k in range(2):
                    axis, step = state["at"][k]
                    ax = {"y": 0, "s": 1}[axis]
                    low = (at.index(axis) // step) % 2 == 0
                    a, b = parts[k], got[k]
                    out.append(jnp.concatenate([jnp.where(low, a, b), jnp.where(low, b, a)], ax))
                return out

            state["parts"] = do(put, state["parts"], state["got"])

        def result():
            ys, ss = Y // 2, S // 2
            bits = jnp.stack([at.y // ys, at.s // ss, jnp.int32(ys), jnp.int32(ss)]).astype(jnp.int32)
            return do(lambda p, g: last_step(p, g, bits, pre, Y, S), state["parts"], state["got"])

        return n, start, finish, result if pre else state

    x_rows = tokens.reshape(rows, width)
    order = span_order.reshape(-1).astype(f32)
    span = rows // 2

    def pack(x, order):
        xf = x.astype(f32)
        mean = jnp.mean(xf, axis=1)
        centred = xf - mean[:, None]
        inv = lax.rsqrt(jnp.mean(centred * centred, axis=1) + eps_norm)
        mine = lax.dynamic_slice_in_dim(order, 2 * at.ctx, 2)
        place = jnp.repeat(mine, span)
        terms = []
        for v in (mean, inv):
            for _ in range(3):
                t = lax.reduce_precision(v, 8, 7)
                terms.append(t)
                v = v - t
        extra = jnp.stack(terms + [place] + [jnp.zeros_like(place)] * 9).astype(bf16)
        blocks = x.T.reshape(nb, blk, rows)
        return jnp.concatenate([blocks, jnp.broadcast_to(extra[None], (nb, 16, rows))], axis=1)

    packed = do(pack, x_rows, order)
    got = lax.all_to_all(packed, plane, split_axis=0, concat_axis=0, tiled=True)

    def chip_rows(w, lead, unit, count):
        mine, theirs = do(lambda w: split_columns(w, core, lead, unit, count), w)
        return mine, at.core(theirs)

    wq_parts = chip_rows(w_qkv, 0, S * blk, 3 * Y)
    norm_cols = norm_params.reshape(7, nb, blk).transpose(1, 2, 0)
    own_cols = pick(norm_cols, 0, my_block)
    other_cols = pick(norm_cols, 0, (at.ctx ^ 1) * S + at.s)
    pair_cols = join(own_cols, other_cols)
    bias = own_cols[:, 4:7].T.reshape(3, heads, HEAD_DIM, 1)
    spot = jnp.stack([at.y, at.s])

    def cut_weights(parts, pre, unit, flip):
        return do(lambda a, b: arrange(a, b, spot, pre, Y, S, unit, flip), *parts)

    wq_cut = [cut_weights(wq_parts, 3, blk, bool(k)) for k in range(2)]

    def columns(got):
        x = got.reshape(at.ctx_size, S, blk + 16, rows).transpose(2, 1, 0, 3).reshape(blk + 16, T)
        x_own, extra = x[:blk], x[blk:].astype(f32)
        mean = extra[0:1] + extra[1:2] + extra[2:3]
        inv = extra[3:4] + extra[4:5] + extra[5:6]
        return x_own, mean, inv, extra[6:7]

    x_own, mean1, inv1, place = do(columns, got)
    x_other = at.core(x_own)
    cot = cotangent.reshape(2, 1, 1, rows // 2, width)
    cot_n, cot_start, cot_finish, cot_state = gather_steps([cot[0], cot[1]], 0)
    cot_start(0, x_own)

    def first_norm(mine, theirs, mean, inv, cols):
        x = join(mine, theirs).astype(f32)
        return ((x - mean) * inv * cols[:, 0:1] + cols[:, 1:2]).astype(bf16)

    xn1 = do(first_norm, x_own, x_other, mean1, inv1, pair_cols)

    def send_products(cut, xs):
        got, kept = [], []
        for k in range(2):
            axis, step = at.steps(bool(k))[0]
            p = do(lambda w, x: dot(w, x, PLAIN).astype(bf16), cut[k][0], xs[k])
            got.append(at.along(p, axis, step))
        for k in range(2):
            kept.append(do(lambda w, x: dot(w, x, PLAIN).astype(bf16), cut[k][1], xs[k]))
        return list(zip(kept, got))

    def scatter_rest(pairs):
        for i in range(1, len(at.steps(False))):
            out = []
            for k in range(2):
                axis, step = at.steps(bool(k))[i]
                bit = (at.index(axis) // step) % 2
                send, kept = do(lambda a, b: add_split(a, b, bit.reshape(1)), *pairs[k])
                out.append((kept, at.along(send, axis, step)))
            pairs = out
        return pairs

    flying = send_products(wq_cut, [xn1[:, h] for h in halves])

    for i in range(1, cot_n):
        cot_finish()
        cot_start(i)

    wo_parts = chip_rows(w_out, 0, S * blk, Y)
    wg_parts = chip_rows(w_up, 0, S * ffb, Y)
    wu_parts = chip_rows(w_up, Y, S * ffb, Y)
    wo_cut = [cut_weights(wo_parts, 1, blk, bool(k)) for k in range(2)]

    def positions(place):
        pos = place.reshape(S, seq) * span + (jnp.arange(seq) % span).astype(f32)[None, :]
        prow = pos.reshape(S, 1, seq)
        exponent = jnp.arange(ROTARY // 2, dtype=f32)
        inverse = 10000.0 ** (-2.0 * exponent / ROTARY)
        angles = prow * inverse[None, :, None]
        return jnp.concatenate([jnp.cos(angles), jnp.sin(angles), jnp.broadcast_to(prow, (S, 8, seq))], axis=1)

    table = do(positions, place)
    flying = scatter_rest(flying)

    cot_finish()
    cot_parts = cot_state["parts"]
    cot_theirs = [at.core(p) for p in cot_parts]

    qkvs, attns, attn_got, stats = [], [], [], []
    for k in range(2):
        shape = (3, heads, HEAD_DIM, H)
        qkv, attn, stat = do(attend, flying[k][0].reshape(shape), flying[k][1].reshape(shape), bias, table[seqs[k]])
        qkvs.append(qkv)
        attns.append(attn.reshape(blk, H))
        attn_got.append(at.core(attns[k]))
        stats.append(stat)
    pairs = [do(join, attns[k], attn_got[k]) for k in range(2)]
    flying = send_products(wo_cut, pairs)
    wg_cut = cut_weights(wg_parts, 1, ffb, False)
    wu_cut = cut_weights(wu_parts, 1, ffb, True)

    def gain_products(wg, wu, cols):
        terms = []
        for v in (cols[:, 2], cols[:, 3]):
            t = lax.reduce_precision(v, 8, 7)
            terms += [t, v - t]
        terms = jnp.stack(terms).astype(bf16)
        out = []
        for mine, theirs in (wg, wu):
            p = dot(terms[:, :blk], mine, LAST) + dot(terms[:, blk:], theirs, LAST)
            out.append(jnp.stack([p[0] + p[1], p[2] + p[3]]).reshape(2, Y, S, ffb))
        return jnp.concatenate(out, axis=0)

    gains = do(gain_products, wg_parts, wu_parts, pair_cols)
    gain_steps = list(at.steps(False))

    def gain_step(gains):
        axis, step = gain_steps.pop(0)
        ax = {"y": 1, "s": 2}[axis]
        bit = (at.index(axis) // step) % 2
        send = lax.dynamic_slice_in_dim(gains, (1 - bit) * step, step, ax)
        kept = lax.dynamic_slice_in_dim(gains, bit * step, step, ax)
        return kept, at.along(send, axis, step)

    flying = scatter_rest(flying)
    def residual(x, a0, b0, a1, b1):
        a, b = lanes(a0, a1), lanes(b0, b1)
        hidden = x.astype(f32) + (a.astype(f32) + b.astype(f32))
        local_mean = jnp.mean(hidden, axis=0, keepdims=True)
        dev = hidden - local_mean
        return hidden, join(local_mean, jnp.sum(dev * dev, axis=0, keepdims=True))

    hidden, moments = do(residual, x_own, *flying[0], *flying[1])
    count = blk
    for axis, step in at.steps(False) + [("core", 1)]:
        other = at.core(moments) if axis == "core" else at.along(moments, axis, step)

        def merge(a, b):
            gap = a[0:1] - b[0:1]
            return join(0.5 * (a[0:1] + b[0:1]), a[1:2] + b[1:2] + gap * gap * (count / 2.0))

        moments = do(merge, moments, other)
        count *= 2

    def second_norm(hidden, moments, cols):
        inv2 = lax.rsqrt(moments[1:2] / width + eps_norm)
        z2 = (hidden - moments[0:1]) * inv2
        return (z2 * cols[:, 2:3] + cols[:, 3:4]).astype(bf16), z2, inv2

    gains = gain_step(gains)
    xn2_own, z2, inv2 = do(second_norm, hidden, moments, own_cols)
    xn2 = do(join, xn2_own, at.core(xn2_own))

    flying = send_products([wg_cut, wu_cut], [xn2, xn2])

    wd_own = do(cast, w_down)
    wg = do(stack_turned, *wg_parts)
    wu = do(stack_turned, *wu_parts)
    cot_all = do(lambda a, b: token_rows(a, b, core), cot_parts, cot_theirs)
    grad_act = do(lambda w, c: mm(w, c, LAST, f32, tn=256), wd_own, cot_all)
    cot_cols = do(lambda c: own_columns(c, my_block.reshape(1), blk), cot_all)
    wo_own = do(cast, w_out)
    wq = do(stack_turned, *wq_parts)
    gains = do(lambda a, b: a + b, *gains)
    while gain_steps:
        gains = do(lambda a, b: a + b, *gain_step(gains))
    gains = do(lambda g: g.reshape(4, ffb).T, gains)
    flying = scatter_rest(flying)

    gate0, gate1, up0, up1, act, sums = do(gated, *flying[0], *flying[1], grad_act, gains)

    def parts_of(count, want):
        return max(n for n in range(1, want + 1) if count % (16 * n) == 0)

    def even(count, want):
        n = parts_of(count, want)
        return [(k * (count // n), count // n) for k in range(n)]

    down_rows, up_rows = even(ffb, 2), [(0, blk)]

    def push_pairs(name, g, rows):
        for k, (at_row, count) in enumerate(rows):
            reps.push((name, "theirs", k), g[blk + at_row : blk + at_row + count])
            reps.push((name, "mine", k), g[at_row : at_row + count])

    results = {"down": None, "out": None, "up": None, "qkv": None}
    states = {
        "down": (w_down, m_down, v_down),
        "out": (w_out, m_out, v_out),
        "up": (w_up, m_up, v_up),
        "qkv": (w_qkv, m_qkv, v_qkv),
    }
    rates = {"down": 0.02, "out": 0.2, "up": 0.03, "qkv": 0.03}

    def adam(name, grads, row_first, lead, unit, rb):
        results[name] = do(
            lambda s, g, prev: adam_part(s, g, core, rates[name], prev, row_first, lead, unit, rb),
            states[name],
            grads,
            results[name],
        )

    jobs = []
    for k, (at_row, count) in enumerate(down_rows):
        jobs.append(("down", [("down", k)], at_row, 0, count, 1024))
    for name, lead in (("gate", 0), ("up", Y)):
        for k, (at_row, count) in enumerate(up_rows):
            jobs.append(("up", [(name, "mine", k), (name, "theirs", k)], at_row, lead, count, S * ffb))
    for k in range(2):
        jobs.append(("out", [("out", k)], 0, k, blk, width // 2))
    for third in (2, 1, 0):
        jobs.append(("qkv", [(third, 0), (third, 1, "theirs")], 0, third * Y, blk, S * blk))
    received = {}

    def update(limit):
        for name in list(reps.done):
            if name in ("out", 0, 1, 2):
                g = reps.done.pop(name)
                half = g.shape[0] // 2
                reps.done[(name, 0)] = g[:half]
                reps.done[(name, 1) if name == "out" else (name, 1, "theirs")] = g[half:]
        for name in list(reps.done):
            if "theirs" in name and name not in received:
                received[name] = at.core(reps.done[name])
        while jobs and limit and all(k in reps.done for k in jobs[0][1]):
            name, needs, at_row, lead, count, unit = jobs.pop(0)
            rb = max(n for n in range(8, min(count, 176) + 1, 8) if count % n == 0 and at_row % n == 0)
            adam(name, [received[k] if "theirs" in k else reps.done[k] for k in needs], at_row, lead, unit, rb)
            limit -= 1

    def ticks(n):
        for _ in range(n):
            reps.tick()

    wide = 2 * FF // 8

    def quarter_heads(x):
        return [x[:, h][None, None] for h in halves]

    n, start, finish, gate_all = gather_steps([gate0[None, None], gate1[None, None]], 1)
    start(0)
    g_down = do(lambda a, c: mm(a, c, PLAIN, bf16, tn=512), act, cot_all)
    for k, (at_row, count) in enumerate(down_rows):
        reps.push(("down", k), g_down[at_row : at_row + count])
    ticks(1)

    steps2 = at.steps(False) + [("core", 1)]

    def sum_send(sums, axis, step):
        return at.core(sums) if axis == "core" else at.along(sums, axis, step)

    def sum_step(sums, axis, step):
        return do(lambda a, b: a + b, sums, sum_send(sums, axis, step))

    tiny = list(steps2)
    sums_got = sum_send(sums, *tiny.pop(0))
    for i in range(1, n):
        finish()
        sums = do(lambda a, b: a + b, sums, sums_got)
        sums_got = sum_send(sums, *tiny.pop(0))
        start(i, sums)
        ticks(1)
    n, start_up, finish_up, up_all = gather_steps([up0[None, None], up1[None, None]], 1)
    ggate_all = gate_all().reshape(Y * S * ffb, T)
    sums = do(lambda a, b: a + b, sums, sums_got)
    start_up(0, sums)
    while tiny:
        sums = sum_step(sums, *tiny.pop(0))
    g_gate = do(lambda x, g: mm(x, g, LAST, bf16, tn=wide), xn2, ggate_all)
    push_pairs("gate", g_gate, up_rows)
    finish_up()
    for i in range(1, n):
        start_up(i)
        if i == 1:
            part_gate = do(lambda w, g: mm(w, g, PLAIN, f32, tn=256), wg, ggate_all)
            out_part = do(lambda w, a: mm(w, a, FIRST, bf16, tm=512), wd_own, act)
            ticks(1)
        if i < n - 1:
            finish_up()
    gup_all = up_all().reshape(Y * S * ffb, T)
    part = do(lambda w, g, p: dot(w, g, PLAIN) + p, wu, gup_all, part_gate)
    part_theirs = at.core(part[blk:])

    def branch(a, b, cot, z, scale, gain, sums):
        gxn2 = a + b
        e = gxn2 * gain
        grad_hidden = cot.astype(f32) + scale * (e - sums[0:1] / width - z * (sums[1:2] / width))
        return grad_hidden.astype(bf16), grad_hidden, gxn2

    grad_branch, grad_hidden, gxn2 = do(
        branch, part[:blk], part_theirs, cot_cols, z2, inv2, own_cols[:, 2:3], sums
    )
    n, start, finish, branch_all = gather_steps(quarter_heads(grad_branch), 1)
    start(0)
    g_up = do(lambda x, g: mm(x, g, LAST, bf16, tn=wide), xn2, gup_all)
    push_pairs("up", g_up, up_rows)
    finish()
    for i in range(1, n):
        start(i)
        if i == 1:
            ticks(1)
        if i < n - 1:
            finish()
    gbr_c = branch_all()[0]
    gbr_o = at.core(gbr_c)
    gbr = do(lambda a, b: in_order(a, b, 1).reshape(width, T), gbr_c, gbr_o)
    grad_attn = do(lambda w, g: dot(w, g, PLAIN).astype(bf16), wo_own, gbr)

    gqkvs = []
    for k in range(2):
        dout = grad_attn[:, halves[k]].reshape(heads, HEAD_DIM, H)
        gqkvs.append(do(attend_back, qkvs[k], dout, stats[k], table[seqs[k]]).reshape(3, blk, H))
    n, start, finish, gqkv_done = gather_steps([g.reshape(1, 1, 3 * blk, H) for g in gqkvs], 3)
    start(0)
    attn = lanes(*attns)
    g_out = do(
        lambda a, g: join(*[mm(a, g[k * width // 2 : (k + 1) * width // 2], LAST, bf16, tn=512) for k in range(2)]),
        attn,
        gbr,
    )
    reps.push("out", g_out)
    update(1)
    ticks(1)
    finish()
    for i in range(1, n):
        start(i)
        if i == 1:
            update(1)
            ticks(1)
        if i < n - 1:
            finish()
    gqkv = gqkv_done().reshape(3, Y * S * blk, T)
    out_split = out_part.reshape(Y, 2, S * blk, T)
    out_kept = pick(out_split, 1, at.c).reshape(-1, T)
    out_got = at.core(pick(out_split, 1, 1 - at.c).reshape(-1, T))

    def out_step(axis, step):
        bit = (at.index(axis) // step) % 2
        send, kept = do(lambda a, b: add_split(a, b, bit.reshape(1)), out_kept, out_got)
        return kept, at.along(send, axis, step)

    out_steps = at.steps(True)
    g = do(lambda x, g: mm(x, g, LAST, bf16, tn=512), xn1, gqkv[2])
    reps.push(2, g)
    ticks(1)
    for third in (1, 0):
        g = do(lambda x, g: mm(x, g, LAST, bf16, tn=512), xn1, gqkv[third])
        reps.push(third, g)
    part = do(lambda w, g: mm(w, g, PLAIN, f32, tn=256), wq, gqkv.reshape(3 * Y * S * blk, T))
    part_theirs = at.core(part[blk:])

    def first_back(a, b, x, mean, inv, gain, gxn2, z2, gqkv0, gqkv1):
        gxn1 = a + b
        z1 = (x.astype(f32) - mean) * inv
        e = gxn1 * gain
        sums = join(jnp.sum(e, axis=0, keepdims=True), jnp.sum(e * z1, axis=0, keepdims=True))
        small = jnp.concatenate(
            [
                jnp.sum(gxn1 * z1, axis=1)[None],
                jnp.sum(gxn1, axis=1)[None],
                jnp.sum(gxn2 * z2, axis=1)[None],
                jnp.sum(gxn2, axis=1)[None],
                jnp.sum(gqkv0.astype(f32), axis=2) + jnp.sum(gqkv1.astype(f32), axis=2),
            ],
            axis=0,
        )
        return sums, small, gxn1, z1

    sums, small, gxn1, z1 = do(
        first_back, part[:blk], part_theirs, x_own, mean1, inv1, own_cols[:, 0:1], gxn2, z2, *gqkvs
    )
    for axis, step in steps2:
        sums = sum_step(sums, axis, step)
    ticks(1)
    input_grad = do(
        lambda h, grad, z, scale, gain, sums: (
            h + scale * (grad * gain - sums[0:1] / width - z * (sums[1:2] / width))
        ).astype(bf16),
        grad_hidden,
        gxn1,
        z1,
        inv1,
        own_cols[:, 0:1],
        sums,
    )

    def to_rows(cols):
        split = do(lambda c: c.reshape(blk, S, at.ctx_size, rows).transpose(2, 1, 0, 3).reshape(nb, blk, rows), cols)
        got = lax.all_to_all(split, plane, split_axis=0, concat_axis=0, tiled=True)
        return do(lambda g: g.reshape(width, rows).T, got)

    input_rows = to_rows(input_grad).astype(f32)
    steps_rep = []
    step = 1
    while step < lax.axis_size("rep"):
        steps_rep.append(step)
        step *= 2

    def small_step():
        nonlocal small
        small = getattr(reps, "kept", small)
        k = steps_rep.pop(0)
        other = lax.ppermute(small, "rep", [(i, i ^ k) for i in range(lax.axis_size("rep"))])
        small = do(lambda a, b: a + b, small, other)
        return small

    out_kept, out_got = out_step(*out_steps[0])
    reps.tick(small_step)
    update(1)
    for axis, step in out_steps[1:]:
        out_kept, out_got = out_step(axis, step)
    reps.tick(small_step)
    sent = do(lambda s: jnp.broadcast_to(s.reshape(1, 7, blk), (nb, 7, blk)), reps.kept)
    small_all = lax.all_to_all(sent, plane, split_axis=0, concat_axis=0, tiled=True)

    def norm_update(every, *a):
        return adam_update(*a, every.transpose(1, 0, 2).reshape(7, width), 0.3, 0.0)

    mn, vn, wn = do(norm_update, small_all, norm_params, m_norm, v_norm)
    update(2)
    ticks(1)
    update(1)
    out_cols = do(
        lambda h, a, b: (h + (a.astype(f32) + b.astype(f32))).astype(bf16), hidden, out_kept, out_got
    )
    block_output = to_rows(out_cols)
    while reps.busy():
        reps.tick()
        update(2)
    update(len(jobs))
    return (
        (block_output.reshape(tokens.shape), input_rows.reshape(tokens.shape))
        + tuple(results["qkv"])
        + tuple(results["out"])
        + tuple(results["up"])
        + tuple(results["down"])
        + (mn, vn, wn)
    )


def solution(mesh):
    tok = P("rep", "ctx", "shard", None)
    row = P(("ctx", "shard"), None)
    placed = (tok, tok, P("rep", "shard", None)) + (row,) * 4 + (P(),) + (row,) * 8 + (P(), P())
    return jax.shard_map(
        body,
        mesh=mesh,
        in_specs=placed,
        out_specs=(tok, tok) + (row,) * 12 + (P(),) * 3,
        check_vma=False,
    )
```

```python
import functools

import jax
import jax.numpy as jnp
from jax import lax
from jax.experimental import pallas as pl
from jax.experimental.pallas import tpu as pltpu
from jax.sharding import PartitionSpec as P

HEADS = 32
HEAD_DIM = 64
FF = 5632
ROTARY = 16
STEP = 10

eps_norm = 1e-05
masked_score = -1e30
beta_one = 0.9
beta_two = 0.999
adam_eps = 1e-08
weight_decay = 0.1
score_scale = HEAD_DIM ** (-0.5)
FIRST = (((0,), (0,)), ((), ()))
LAST = (((1,), (1,)), ((), ()))
PLAIN = (((1,), (0,)), ((), ()))
bf16 = jnp.bfloat16
f32 = jnp.float32


def dot(a, b, dims):
    return lax.dot_general(a, b, dims, preferred_element_type=f32)


def adam_update(weight, moment_one, moment_two, grad, step_rate, decay_rate):
    first_new = beta_one * moment_one + (1.0 - beta_one) * grad
    second_new = beta_two * moment_two + (1.0 - beta_two) * grad * grad
    first_hat = first_new / (1.0 - beta_one**STEP)
    second_hat = second_new / (1.0 - beta_two**STEP)
    weight_new = weight - step_rate * (
        first_hat / (jnp.sqrt(second_hat) + adam_eps) + decay_rate * weight
    )
    return (first_new, second_new, weight_new)


class Plane:
    def __init__(self):
        self.s_size = lax.axis_size("shard")
        self.ctx_size = lax.axis_size("ctx")
        self.y_size = self.ctx_size // 2
        self.ctx = lax.axis_index("ctx")
        self.s = lax.axis_index("shard")
        self.y = self.ctx // 2
        self.c = self.ctx % 2
        self.blocks = self.ctx_size * self.s_size

    def core(self, x):
        return lax.ppermute(x, "ctx", [(i, i ^ 1) for i in range(self.ctx_size)])

    def along(self, x, axis, step):
        if axis == "y":
            return lax.ppermute(x, "ctx", [(i, i ^ (2 * step)) for i in range(self.ctx_size)])
        return lax.ppermute(x, "shard", [(i, i ^ step) for i in range(self.s_size)])

    def index(self, axis):
        return self.y if axis == "y" else self.s

    def steps(self, flip):
        ys = []
        k = self.y_size // 2
        while k:
            ys.append(("y", k))
            k //= 2
        ss = []
        k = self.s_size // 2
        while k:
            ss.append(("s", k))
            k //= 2
        return ys + ss if flip else ss + ys

    def chip_exchange(self, x, take):
        out = [(self.y, self.s, take(self.y, self.s))]
        for ry in range(self.y_size):
            for rs in range(self.s_size):
                if ry or rs:
                    y, s = self.y ^ ry, self.s ^ rs
                    mask = 2 * ry * self.s_size + rs
                    perm = [(i, i ^ mask) for i in range(self.blocks)]
                    out.append((y, s, lax.ppermute(take(y, s), ("ctx", "shard"), perm)))
        return out

    def sum_all(self, x):
        for axis, step in self.steps(False):
            x = x + self.along(x, axis, step)
        return x + self.core(x)

    def scatter_sum(self, p, flip):
        axes = {"y": 1, "s": 2}
        steps = self.steps(flip)
        kept = got = None
        for n, (axis, step) in enumerate(steps):
            ax = axes[axis]
            bit = (self.index(axis) // step) % 2
            kept = lax.dynamic_slice_in_dim(p, bit * step, step, ax)
            send = lax.dynamic_slice_in_dim(p, (1 - bit) * step, step, ax)
            got = self.along(send, axis, step)
            if n + 1 < len(steps):
                p = (kept.astype(f32) + got.astype(f32)).astype(bf16)
        return kept[:, 0, 0], got[:, 0, 0]

    def gather(self, p, flip):
        axes = {"y": 1, "s": 2}
        p = p[:, None, None]
        for axis, step in reversed(self.steps(flip)):
            ax = axes[axis]
            bit = (self.index(axis) // step) % 2
            got = self.along(p, axis, step)
            first = bit == 0
            p = jnp.concatenate([jnp.where(first, p, got), jnp.where(first, got, p)], ax)
        return p


class Order:
    def __init__(self):
        self.token = lax.create_token()

    def __call__(self, stage, *args):
        args, token = lax.optimization_barrier((args, self.token))
        out, self.token = lax.optimization_barrier((stage(*args), token))
        return out


SMALL = pl.CostEstimate(flops=1024, bytes_accessed=1024, transcendentals=0)


class RepSum:
    def __init__(self, order):
        self.order = order
        z = lax.axis_index("rep")
        self.end = (z == 0) | (z == lax.axis_size("rep") - 1)
        self.queue = []
        self.flight = []
        self.depth = 1
        self.done = {}

    def push(self, name, g):
        self.queue.append((name, g))

    def busy(self):
        return bool(self.queue or self.flight)

    def tick(self, between=None):
        old = {}
        if len(self.flight) >= self.depth or (self.flight and not self.queue):
            old = self.flight.pop(0)
        new = self.queue.pop(0) if self.queue else None
        values = {}
        if "in" in old:
            values["g"], values["g_got"] = old["in"][1], old["in_got"]
        if "mid" in old:
            values["s"], values["s_got"] = old["mid"][1], old["mid_got"]
        if new:
            values["new"] = new[1]
        both = new and "mid" in old and new[1].shape == old["mid"][1].shape
        if "out" in old:
            values["out_got"] = old["out_got"]

        def stage(v):
            def add(a, b):
                return lax.reduce_precision(a.astype(f32) + b.astype(f32), 8, 7).astype(bf16)

            out = {}
            if "g" in v:
                out["a_sum"] = add(v["g"], v["g_got"])
            if "s" in v:
                total = add(v["s"], v["s_got"])
                out["total"] = jnp.where(self.end, v["new"], total) if both else total
            if "new" in v and not both:
                out["new"] = v["new"]
            if "out_got" in v:
                out["z_got"] = v["out_got"]
            return out

        if not values:
            return
        out = self.order(stage, values)
        if between is not None:
            out, self.kept = lax.optimization_barrier((out, between()))
        if "out" in old:
            self.done[old["out"][0]] = jnp.where(self.end, out["z_got"], old["out"][1])
        slot = {}
        if both:
            got = lax.ppermute(out["total"], "rep", [(0, 1), (1, 0), (2, 3), (3, 2)])
            slot = {"in": new, "in_got": got, "out": (old["mid"][0], out["total"]), "out_got": got}
        else:
            if new:
                slot["in"] = new
                slot["in_got"] = lax.ppermute(out["new"], "rep", [(0, 1), (3, 2)])
            if "mid" in old:
                slot["out"] = (old["mid"][0], out["total"])
                slot["out_got"] = lax.ppermute(out["total"], "rep", [(1, 0), (2, 3)])
        if "in" in old:
            slot["mid"] = (old["in"][0], out["a_sum"])
            slot["mid_got"] = lax.ppermute(out["a_sum"], "rep", [(1, 2), (2, 1)])
        if slot:
            self.flight.append(slot)


def cast_kernel(w_ref, out_ref):
    out_ref[...] = w_ref[...].astype(bf16)


def cast(w):
    rows, width = w.shape
    unit = max(n for n in (128, 256, 512, 1024, 1408, 2048, 2816) if width % n == 0)
    spec = pl.BlockSpec((rows, unit), lambda i: (0, i))
    return pl.pallas_call(
        cast_kernel,
        grid=(width // unit,),
        in_specs=[spec],
        out_specs=spec,
        out_shape=jax.ShapeDtypeStruct(w.shape, bf16),
        compiler_params=pltpu.CompilerParams(vmem_limit_bytes=48 * 1024 * 1024),
        cost_estimate=SMALL,
    )(w)


def gated_kernel(ga_ref, gb_ref, ua_ref, ub_ref, grad_ref, gains_ref, g0_ref, g1_ref, u0_ref, u1_ref, act_ref, sums_ref):
    half = g0_ref.shape[1]
    gate = ga_ref[...].astype(f32) + gb_ref[...].astype(f32)
    up = ua_ref[...].astype(f32) + ub_ref[...].astype(f32)
    sig = jax.nn.sigmoid(gate)
    silu = gate * sig
    grad = grad_ref[...]
    act_ref[...] = (silu * up).astype(bf16)
    ggate = (grad * up * sig * (1.0 + gate * (1.0 - sig))).astype(bf16)
    gup = (grad * silu).astype(bf16)
    g0_ref[...] = ggate[:, :half]
    g1_ref[...] = ggate[:, half:]
    u0_ref[...] = gup[:, :half]
    u1_ref[...] = gup[:, half:]
    a, b = ggate.astype(f32), gup.astype(f32)
    e = jnp.sum(a * gains_ref[:, 0:1] + b * gains_ref[:, 2:3], axis=0, keepdims=True)
    ez = jnp.sum(a * (gate - gains_ref[:, 1:2]) + b * (up - gains_ref[:, 3:4]), axis=0, keepdims=True)
    both = jnp.concatenate([e, ez], axis=0)

    @pl.when(pl.program_id(0) == 0)
    def _():
        sums_ref[...] = both

    @pl.when(pl.program_id(0) > 0)
    def _():
        sums_ref[...] += both


def gated(ga, gb, ua, ub, grad_act, gains):
    rows, t = grad_act.shape
    n = max(n for n in (1, 2, 4) if rows % (16 * n) == 0)
    whole = pl.BlockSpec((rows // n, t), lambda i: (i, 0))
    half = pl.BlockSpec((rows // n, t // 2), lambda i: (i, 0))
    out_half = jax.ShapeDtypeStruct((rows, t // 2), bf16)
    return pl.pallas_call(
        gated_kernel,
        grid=(n,),
        in_specs=[whole] * 5 + [pl.BlockSpec((rows // n, 4), lambda i: (i, 0))],
        out_specs=[half] * 4 + [whole, pl.BlockSpec((2, t), lambda i: (0, 0))],
        out_shape=[out_half] * 4 + [jax.ShapeDtypeStruct((rows, t), bf16), jax.ShapeDtypeStruct((2, t), f32)],
        compiler_params=pltpu.CompilerParams(vmem_limit_bytes=56 * 1024 * 1024),
        cost_estimate=SMALL,
    )(ga, gb, ua, ub, grad_act, gains)


def own_columns_kernel(block_ref, x_ref, out_ref):
    out_ref[...] = x_ref[...].T


def own_columns(x, block, width):
    rows = x.shape[0]
    if width % 128:
        return lax.dynamic_slice_in_dim(x, block[0] * width, width, 1).T
    tile = min(rows, 512)
    return pl.pallas_call(
        own_columns_kernel,
        grid_spec=pltpu.PrefetchScalarGridSpec(
            num_scalar_prefetch=1,
            grid=(rows // tile,),
            in_specs=[pl.BlockSpec((tile, width), lambda i, block: (i, block[0]))],
            out_specs=pl.BlockSpec((width, tile), lambda i, block: (0, i)),
        ),
        out_shape=jax.ShapeDtypeStruct((width, rows), bf16),
        compiler_params=pltpu.CompilerParams(vmem_limit_bytes=48 * 1024 * 1024),
        cost_estimate=SMALL,
    )(block, x)


def split_kernel(core_ref, w_ref, mine_ref, theirs_ref):
    unit = mine_ref.shape[0]
    first = core_ref[0] == 0
    a, b = w_ref[:, :unit], w_ref[:, unit:]
    mine_ref[...] = jnp.where(first, a, b).T.astype(bf16)
    theirs_ref[...] = jnp.where(first, b, a).T.astype(bf16)


def split_columns(w, core, lead, unit, count):
    rows = w.shape[0]
    half = pl.BlockSpec((unit, rows), lambda j, core: (j, 0))
    out = jax.ShapeDtypeStruct((count * unit, rows), bf16)
    return pl.pallas_call(
        split_kernel,
        grid_spec=pltpu.PrefetchScalarGridSpec(
            num_scalar_prefetch=1,
            grid=(count,),
            in_specs=[pl.BlockSpec((rows, 2 * unit), lambda j, core: (0, lead + j))],
            out_specs=[half, half],
        ),
        out_shape=[out, out],
        compiler_params=pltpu.CompilerParams(vmem_limit_bytes=32 * 1024 * 1024),
        cost_estimate=SMALL,
    )(core, w)


def arrange_kernel(at_ref, a_ref, b_ref, c_ref, d_ref, send_ref, keep_ref):
    send_ref[...] = jnp.concatenate([a_ref[...], b_ref[...]], axis=1)
    keep_ref[...] = jnp.concatenate([c_ref[...], d_ref[...]], axis=1)


def arrange(mine, got, place, pre, y_size, s_size, unit, flip):
    r = mine.shape[1]
    half = pre * y_size * s_size // 2

    def block(i, place, keep):
        p = i % pre
        i = i // pre
        if flip:
            s, y = i % s_size, i // s_size
            bit = place[0] // (y_size // 2)
            bit = bit if keep else 1 - bit
            y = y + bit * (y_size // 2)
        else:
            y, s = i % y_size, i // y_size
            bit = place[1] // (s_size // 2)
            bit = bit if keep else 1 - bit
            s = s + bit * (s_size // 2)
        return ((p * y_size + y) * s_size + s, 0)

    def spec(keep):
        return pl.BlockSpec((unit, r), lambda i, place: block(i, place, keep))

    out = jax.ShapeDtypeStruct((half * unit, 2 * r), bf16)
    out_spec = pl.BlockSpec((unit, 2 * r), lambda i, place: (i, 0))
    return pl.pallas_call(
        arrange_kernel,
        grid_spec=pltpu.PrefetchScalarGridSpec(
            num_scalar_prefetch=1,
            grid=(half,),
            in_specs=[spec(False), spec(False), spec(True), spec(True)],
            out_specs=[out_spec, out_spec],
        ),
        out_shape=[out, out],
        compiler_params=pltpu.CompilerParams(vmem_limit_bytes=32 * 1024 * 1024),
        cost_estimate=SMALL,
    )(place, mine, got, mine, got)


def product_kernel(dims, a_ref, b_ref, *refs):
    p = dot(a_ref[...], b_ref[...], dims)
    if len(refs) == 2:
        p = p + refs[0][...]
    refs[-1][...] = p.astype(refs[-1].dtype)


def mm(a, b, dims, dtype, tm=None, tn=None, add=None):
    (ca,), (cb,) = dims[0]
    m, k, n = a.shape[1 - ca], a.shape[ca], b.shape[1 - cb]
    tm, tn = tm or m, tn or n
    a_block = [0, 0]
    a_block[ca], a_block[1 - ca] = k, tm
    b_block = [0, 0]
    b_block[cb], b_block[1 - cb] = k, tn
    out = pl.BlockSpec((tm, tn), lambda i, j: (i, j))
    return pl.pallas_call(
        functools.partial(product_kernel, dims),
        grid=(m // tm, n // tn),
        in_specs=[
            pl.BlockSpec(tuple(a_block), (lambda i, j: (0, i)) if ca == 0 else (lambda i, j: (i, 0))),
            pl.BlockSpec(tuple(b_block), (lambda i, j: (0, j)) if cb == 0 else (lambda i, j: (j, 0))),
        ]
        + ([] if add is None else [out]),
        out_specs=out,
        out_shape=jax.ShapeDtypeStruct((m, n), dtype),
        compiler_params=pltpu.CompilerParams(vmem_limit_bytes=48 * 1024 * 1024),
        cost_estimate=SMALL,
    )(*((a, b) if add is None else (a, b, add)))


def last_step_kernel(bits_ref, own0_ref, got0_ref, own1_ref, got1_ref, out_ref):
    y, s = pl.program_id(1), pl.program_id(2)
    half = own0_ref.shape[3]
    ys, ss = bits_ref[2], bits_ref[3]
    a = jnp.where(s // ss == bits_ref[1], own0_ref[0, 0], got0_ref[0, 0])
    b = jnp.where(y // ys == bits_ref[0], own1_ref[0, 0], got1_ref[0, 0])
    out_ref[0, 0, 0, :, :half] = a
    out_ref[0, 0, 0, :, half:] = b


def last_step(parts, got, bits, pre, y_size, s_size):
    rows, half = parts[0].shape[2] // pre, parts[0].shape[3]
    along_s = pl.BlockSpec((1, 1, rows, half), lambda p, y, s, bits: (y, s % (s_size // 2), p, 0))
    along_y = pl.BlockSpec((1, 1, rows, half), lambda p, y, s, bits: (y % (y_size // 2), s, p, 0))
    return pl.pallas_call(
        last_step_kernel,
        grid_spec=pltpu.PrefetchScalarGridSpec(
            num_scalar_prefetch=1,
            grid=(pre, y_size, s_size),
            in_specs=[along_s, along_s, along_y, along_y],
            out_specs=pl.BlockSpec((1, 1, 1, rows, 2 * half), lambda p, y, s, bits: (p, y, s, 0, 0)),
        ),
        out_shape=jax.ShapeDtypeStruct((pre, y_size, s_size, rows, 2 * half), bf16),
        compiler_params=pltpu.CompilerParams(vmem_limit_bytes=48 * 1024 * 1024),
        cost_estimate=SMALL,
    )(bits, parts[0], got[0], parts[1], got[1])


def stack_turned_kernel(a_ref, b_ref, out_ref):
    r = a_ref.shape[1]
    out_ref[:r] = a_ref[...].T
    out_ref[r:] = b_ref[...].T


def stack_turned(a, b):
    rows, width = a.shape
    n = max(n for n in (1, 2, 4, 6, 8, 11) if rows % (128 * n) == 0)
    spec = pl.BlockSpec((rows // n, width), lambda i: (i, 0))
    return pl.pallas_call(
        stack_turned_kernel,
        grid=(n,),
        in_specs=[spec, spec],
        out_specs=pl.BlockSpec((2 * width, rows // n), lambda i: (0, i)),
        out_shape=jax.ShapeDtypeStruct((2 * width, rows), bf16),
        compiler_params=pltpu.CompilerParams(vmem_limit_bytes=48 * 1024 * 1024),
        cost_estimate=SMALL,
    )(a, b)


def add_split_kernel(bit_ref, a_ref, b_ref, c_ref, d_ref, send_ref, keep_ref):
    send_ref[...] = (a_ref[...].astype(f32) + b_ref[...].astype(f32)).astype(bf16)
    keep_ref[...] = (c_ref[...].astype(f32) + d_ref[...].astype(f32)).astype(bf16)


def add_split(kept, got, bit):
    rows, t = kept.shape
    half = rows // 2
    n = max(n for n in (1, 2, 3, 4) if half % (16 * n) == 0)
    rb = half // n
    away = pl.BlockSpec((rb, t), lambda i, bit: ((1 - bit[0]) * n + i, 0))
    here = pl.BlockSpec((rb, t), lambda i, bit: (bit[0] * n + i, 0))
    out = jax.ShapeDtypeStruct((half, t), bf16)
    out_spec = pl.BlockSpec((rb, t), lambda i, bit: (i, 0))
    return pl.pallas_call(
        add_split_kernel,
        grid_spec=pltpu.PrefetchScalarGridSpec(
            num_scalar_prefetch=1,
            grid=(n,),
            in_specs=[away, away, here, here],
            out_specs=[out_spec, out_spec],
        ),
        out_shape=[out, out],
        compiler_params=pltpu.CompilerParams(vmem_limit_bytes=48 * 1024 * 1024),
        cost_estimate=SMALL,
    )(bit, kept, got, kept, got)


def token_rows_kernel(core_ref, a_ref, b_ref, c_ref, d_ref, out_ref):
    mine = core_ref[0] == pl.program_id(2)
    half = out_ref.shape[0] // 2
    out_ref[:half] = jnp.where(mine, a_ref[0, 0], c_ref[0, 0])
    out_ref[half:] = jnp.where(mine, b_ref[0, 0], d_ref[0, 0])


def token_rows(mine, theirs, core):
    y_size, s_size, rows, width = mine[0].shape
    part = pl.BlockSpec((1, 1, rows, width), lambda s, y, c, core: (y, s, 0, 0))
    return pl.pallas_call(
        token_rows_kernel,
        grid_spec=pltpu.PrefetchScalarGridSpec(
            num_scalar_prefetch=1,
            grid=(s_size, y_size, 2),
            in_specs=[part] * 4,
            out_specs=pl.BlockSpec((2 * rows, width), lambda s, y, c, core: ((s * y_size + y) * 2 + c, 0)),
        ),
        out_shape=jax.ShapeDtypeStruct((s_size * y_size * 4 * rows, width), bf16),
        compiler_params=pltpu.CompilerParams(vmem_limit_bytes=32 * 1024 * 1024),
        cost_estimate=SMALL,
    )(core, *mine, *theirs)


def adam_kernel(rate, two, core_ref, w_ref, m_ref, v_ref, *refs):
    grad = refs[0][...].astype(f32)
    if two:
        other = refs[1][...].astype(f32)
        mine = core_ref[0] == 0
        grad = jnp.concatenate([jnp.where(mine, grad, other), jnp.where(mine, other, grad)], axis=1)
    new_m_ref, new_v_ref, new_w_ref = refs[-3:]
    new_m, new_v, new_w = adam_update(w_ref[...], m_ref[...], v_ref[...], grad, rate, weight_decay)
    new_m_ref[...] = new_m
    new_v_ref[...] = new_v
    new_w_ref[...] = new_w


def adam_part(state, grads, core, rate, prev, row_first, lead, unit, rb):
    w, m, v = state
    two = len(grads) == 2
    rows, width = grads[0].shape
    whole = pl.BlockSpec((rb, unit * len(grads)), lambda i, g, core: (row_first // rb + i, lead + g))
    half = pl.BlockSpec((rb, unit), lambda i, g, core: (i, g))
    out = jax.ShapeDtypeStruct(w.shape, f32)
    extra, aliases = [], {}
    if prev is not None:
        extra = list(prev)
        aliases = {4 + len(grads) + i: i for i in range(3)}
    return pl.pallas_call(
        functools.partial(adam_kernel, rate, two),
        grid_spec=pltpu.PrefetchScalarGridSpec(
            num_scalar_prefetch=1,
            grid=(rows // rb, width // unit),
            in_specs=[whole] * 3 + [half] * len(grads) + [pl.BlockSpec(memory_space=pl.ANY)] * len(extra),
            out_specs=[whole] * 3,
        ),
        out_shape=[out] * 3,
        input_output_aliases=aliases,
        compiler_params=pltpu.CompilerParams(vmem_limit_bytes=48 * 1024 * 1024),
        cost_estimate=SMALL,
    )(core, w, m, v, *grads, *extra)


def attend_kernel(kept_ref, got_ref, bias_ref, table_ref, qkv_ref, out_ref, stat_ref):
    half = ROTARY // 2
    cos, sin, pos = table_ref[0, :half], table_ref[0, half:ROTARY], table_ref[0, ROTARY:]
    parts = []
    for i in range(3):
        v = kept_ref[i, 0].astype(f32) + got_ref[i, 0].astype(f32) + bias_ref[i, 0]
        if i < 2:
            a, b = v[:half], v[half:ROTARY]
            v = jnp.concatenate([a * cos - b * sin, b * cos + a * sin, v[ROTARY:]], axis=0)
        v = v.astype(bf16)
        qkv_ref[i, 0] = v
        parts.append(v)
    q, k, v = parts
    scores = dot(k, q, FIRST) * score_scale
    scores = jnp.where(pos.T[:, :1] <= pos[:1], scores, masked_score)
    peak = jnp.max(scores, axis=0, keepdims=True)
    e = jnp.exp(scores - peak)
    total = jnp.sum(e, axis=0, keepdims=True)
    p = (e / total).astype(bf16)
    out_ref[0] = dot(v, p, PLAIN).astype(bf16)
    stat_ref[0, 0] = jnp.concatenate([peak, total], axis=0)


def attend(kept, got, bias, table):
    _, heads, hd, t = kept.shape
    seqs, _, seq = table.shape
    big = pl.BlockSpec((3, 1, hd, seq), lambda s, h: (0, h, 0, s))
    table_spec = pl.BlockSpec((1, table.shape[1], seq), lambda s, h: (s, 0, 0))
    stat = pl.BlockSpec((1, 1, 2, seq), lambda s, h: (s, h, 0, 0))
    return pl.pallas_call(
        attend_kernel,
        grid=(seqs, heads),
        in_specs=[
            big,
            big,
            pl.BlockSpec((3, 1, hd, 1), lambda s, h: (0, h, 0, 0)),
            table_spec,
        ],
        out_specs=[big, pl.BlockSpec((1, hd, seq), lambda s, h: (h, 0, s)), stat],
        out_shape=[
            jax.ShapeDtypeStruct((3, heads, hd, t), bf16),
            jax.ShapeDtypeStruct((heads, hd, t), bf16),
            jax.ShapeDtypeStruct((seqs, heads, 2, seq), f32),
        ],
        compiler_params=pltpu.CompilerParams(vmem_limit_bytes=32 * 1024 * 1024),
        cost_estimate=SMALL,
    )(kept, got, bias, table)


def attend_back_kernel(qkv_ref, dout_ref, stat_ref, table_ref, out_ref):
    half = ROTARY // 2
    cos, sin, pos = table_ref[0, :half], table_ref[0, half:ROTARY], table_ref[0, ROTARY:]
    q, k, v = qkv_ref[0, 0], qkv_ref[1, 0], qkv_ref[2, 0]
    dout = dout_ref[0]
    scores = dot(k, q, FIRST) * score_scale
    scores = jnp.where(pos.T[:, :1] <= pos[:1], scores, masked_score)
    p = jnp.exp(scores - stat_ref[0, 0, :1]) / stat_ref[0, 0, 1:]
    dp = dot(v, dout, FIRST)
    inner = jnp.sum(p * dp, axis=0, keepdims=True)
    ds = (p * (dp - inner)).astype(bf16)

    def back(x):
        a, b = x[:half], x[half:ROTARY]
        return jnp.concatenate([a * cos + b * sin, b * cos - a * sin, x[ROTARY:]], axis=0)

    out_ref[0, 0] = back(dot(k, ds, PLAIN) * score_scale).astype(bf16)
    out_ref[1, 0] = back(dot(q, ds, LAST) * score_scale).astype(bf16)
    out_ref[2, 0] = dot(dout, p.astype(bf16), LAST).astype(bf16)


def attend_back(qkv, dout, stats, table):
    _, heads, hd, t = qkv.shape
    seqs, _, seq = table.shape
    big = pl.BlockSpec((3, 1, hd, seq), lambda s, h: (0, h, 0, s))
    table_spec = pl.BlockSpec((1, table.shape[1], seq), lambda s, h: (s, 0, 0))
    stat = pl.BlockSpec((1, 1, 2, seq), lambda s, h: (s, h, 0, 0))
    return pl.pallas_call(
        attend_back_kernel,
        grid=(seqs, heads),
        in_specs=[
            big,
            pl.BlockSpec((1, hd, seq), lambda s, h: (h, 0, s)),
            stat,
            table_spec,
        ],
        out_specs=big,
        out_shape=jax.ShapeDtypeStruct((3, heads, hd, t), bf16),
        compiler_params=pltpu.CompilerParams(vmem_limit_bytes=32 * 1024 * 1024),
        cost_estimate=SMALL,
    )(qkv, dout, stats, table)


def body(
    tokens,
    cotangent,
    span_order,
    w_qkv,
    w_out,
    w_up,
    w_down,
    norm_params,
    m_qkv,
    v_qkv,
    m_out,
    v_out,
    m_up,
    v_up,
    m_down,
    v_down,
    m_norm,
    v_norm,
):
    at = Plane()
    do = Order()
    reps = RepSum(do)
    width = tokens.shape[3]
    rows = tokens.shape[1]
    S, Y, nb = at.s_size, at.y_size, at.blocks
    plane = ("ctx", "shard")
    blk = width // nb
    ffb = FF // nb
    heads = blk // HEAD_DIM
    seq = rows * at.ctx_size
    T = S * seq
    H = T // 2
    first = at.c == 0
    core = at.c.reshape(1)
    my_block = at.ctx * S + at.s
    halves = (slice(0, H), slice(H, T))
    seqs = (slice(0, S // 2), slice(S // 2, S))

    def pick(x, axis, which):
        return lax.dynamic_index_in_dim(x, which, axis, keepdims=False)

    def in_order(mine, theirs, axis):
        return jnp.stack([jnp.where(first, mine, theirs), jnp.where(first, theirs, mine)], axis=axis)

    def join(a, b):
        return jnp.concatenate([a, b], axis=0)

    def lanes(a, b):
        return jnp.concatenate([a, b], axis=1)

    def gather_steps(parts, pre):
        n = len(at.steps(False))
        state = {"parts": list(parts)}

        def start(i, after=None):
            if after is not None:
                state["parts"], _ = lax.optimization_barrier((state["parts"], after))
            state["got"] = []
            state["at"] = []
            for k in range(2):
                axis, step = list(reversed(at.steps(bool(k))))[i]
                state["at"].append((axis, step))
                state["got"].append(at.along(state["parts"][k], axis, step))

        def finish():
            def put(parts, got):
                out = []
                for k in range(2):
                    axis, step = state["at"][k]
                    ax = {"y": 0, "s": 1}[axis]
                    low = (at.index(axis) // step) % 2 == 0
                    a, b = parts[k], got[k]
                    out.append(jnp.concatenate([jnp.where(low, a, b), jnp.where(low, b, a)], ax))
                return out

            state["parts"] = do(put, state["parts"], state["got"])

        def result():
            ys, ss = Y // 2, S // 2
            bits = jnp.stack([at.y // ys, at.s // ss, jnp.int32(ys), jnp.int32(ss)]).astype(jnp.int32)
            return do(lambda p, g: last_step(p, g, bits, pre, Y, S), state["parts"], state["got"])

        return n, start, finish, result if pre else state

    x_rows = tokens.reshape(rows, width)
    order = span_order.reshape(-1).astype(f32)
    span = rows // 2

    def pack(x, order):
        xf = x.astype(f32)
        mean = jnp.mean(xf, axis=1)
        centred = xf - mean[:, None]
        inv = lax.rsqrt(jnp.mean(centred * centred, axis=1) + eps_norm)
        mine = lax.dynamic_slice_in_dim(order, 2 * at.ctx, 2)
        place = jnp.repeat(mine, span)
        terms = []
        for v in (mean, inv):
            for _ in range(3):
                t = lax.reduce_precision(v, 8, 7)
                terms.append(t)
                v = v - t
        extra = jnp.stack(terms + [place] + [jnp.zeros_like(place)] * 9).astype(bf16)
        blocks = x.T.reshape(nb, blk, rows)
        return jnp.concatenate([blocks, jnp.broadcast_to(extra[None], (nb, 16, rows))], axis=1)

    packed = do(pack, x_rows, order)
    got = lax.all_to_all(packed, plane, split_axis=0, concat_axis=0, tiled=True)

    def chip_rows(w, lead, unit, count):
        mine, theirs = do(lambda w: split_columns(w, core, lead, unit, count), w)
        return mine, at.core(theirs)

    wq_parts = chip_rows(w_qkv, 0, S * blk, 3 * Y)
    norm_cols = norm_params.reshape(7, nb, blk).transpose(1, 2, 0)
    own_cols = pick(norm_cols, 0, my_block)
    other_cols = pick(norm_cols, 0, (at.ctx ^ 1) * S + at.s)
    pair_cols = join(own_cols, other_cols)
    bias = own_cols[:, 4:7].T.reshape(3, heads, HEAD_DIM, 1)
    spot = jnp.stack([at.y, at.s])

    def cut_weights(parts, pre, unit, flip):
        return do(lambda a, b: arrange(a, b, spot, pre, Y, S, unit, flip), *parts)

    wq_cut = [cut_weights(wq_parts, 3, blk, bool(k)) for k in range(2)]

    def columns(got):
        x = got.reshape(at.ctx_size, S, blk + 16, rows).transpose(2, 1, 0, 3).reshape(blk + 16, T)
        x_own, extra = x[:blk], x[blk:].astype(f32)
        mean = extra[0:1] + extra[1:2] + extra[2:3]
        inv = extra[3:4] + extra[4:5] + extra[5:6]
        return x_own, mean, inv, extra[6:7]

    x_own, mean1, inv1, place = do(columns, got)
    x_other = at.core(x_own)
    cot = cotangent.reshape(2, 1, 1, rows // 2, width)
    cot_n, cot_start, cot_finish, cot_state = gather_steps([cot[0], cot[1]], 0)
    cot_start(0, x_own)

    def first_norm(mine, theirs, mean, inv, cols):
        x = join(mine, theirs).astype(f32)
        return ((x - mean) * inv * cols[:, 0:1] + cols[:, 1:2]).astype(bf16)

    xn1 = do(first_norm, x_own, x_other, mean1, inv1, pair_cols)

    def send_products(cut, xs):
        got, kept = [], []
        for k in range(2):
            axis, step = at.steps(bool(k))[0]
            p = do(lambda w, x: dot(w, x, PLAIN).astype(bf16), cut[k][0], xs[k])
            got.append(at.along(p, axis, step))
        for k in range(2):
            kept.append(do(lambda w, x: dot(w, x, PLAIN).astype(bf16), cut[k][1], xs[k]))
        return list(zip(kept, got))

    def scatter_rest(pairs):
        for i in range(1, len(at.steps(False))):
            out = []
            for k in range(2):
                axis, step = at.steps(bool(k))[i]
                bit = (at.index(axis) // step) % 2
                send, kept = do(lambda a, b: add_split(a, b, bit.reshape(1)), *pairs[k])
                out.append((kept, at.along(send, axis, step)))
            pairs = out
        return pairs

    flying = send_products(wq_cut, [xn1[:, h] for h in halves])

    for i in range(1, cot_n):
        cot_finish()
        cot_start(i)

    wo_parts = chip_rows(w_out, 0, S * blk, Y)
    wg_parts = chip_rows(w_up, 0, S * ffb, Y)
    wu_parts = chip_rows(w_up, Y, S * ffb, Y)
    wo_cut = [cut_weights(wo_parts, 1, blk, bool(k)) for k in range(2)]

    def positions(place):
        pos = place.reshape(S, seq) * span + (jnp.arange(seq) % span).astype(f32)[None, :]
        prow = pos.reshape(S, 1, seq)
        exponent = jnp.arange(ROTARY // 2, dtype=f32)
        inverse = 10000.0 ** (-2.0 * exponent / ROTARY)
        angles = prow * inverse[None, :, None]
        return jnp.concatenate([jnp.cos(angles), jnp.sin(angles), jnp.broadcast_to(prow, (S, 8, seq))], axis=1)

    table = do(positions, place)
    flying = scatter_rest(flying)

    cot_finish()
    cot_parts = cot_state["parts"]
    cot_theirs = [at.core(p) for p in cot_parts]

    qkvs, attns, attn_got, stats = [], [], [], []
    for k in range(2):
        shape = (3, heads, HEAD_DIM, H)
        qkv, attn, stat = do(attend, flying[k][0].reshape(shape), flying[k][1].reshape(shape), bias, table[seqs[k]])
        qkvs.append(qkv)
        attns.append(attn.reshape(blk, H))
        attn_got.append(at.core(attns[k]))
        stats.append(stat)
    pairs = [do(join, attns[k], attn_got[k]) for k in range(2)]
    flying = send_products(wo_cut, pairs)
    wg_cut = cut_weights(wg_parts, 1, ffb, False)
    wu_cut = cut_weights(wu_parts, 1, ffb, True)

    def gain_products(wg, wu, cols):
        terms = []
        for v in (cols[:, 2], cols[:, 3]):
            t = lax.reduce_precision(v, 8, 7)
            terms += [t, v - t]
        terms = jnp.stack(terms).astype(bf16)
        out = []
        for mine, theirs in (wg, wu):
            p = dot(terms[:, :blk], mine, LAST) + dot(terms[:, blk:], theirs, LAST)
            out.append(jnp.stack([p[0] + p[1], p[2] + p[3]]).reshape(2, Y, S, ffb))
        return jnp.concatenate(out, axis=0)

    gains = do(gain_products, wg_parts, wu_parts, pair_cols)
    gain_steps = list(at.steps(False))

    def gain_step(gains):
        axis, step = gain_steps.pop(0)
        ax = {"y": 1, "s": 2}[axis]
        bit = (at.index(axis) // step) % 2
        send = lax.dynamic_slice_in_dim(gains, (1 - bit) * step, step, ax)
        kept = lax.dynamic_slice_in_dim(gains, bit * step, step, ax)
        return kept, at.along(send, axis, step)

    flying = scatter_rest(flying)
    def residual(x, a0, b0, a1, b1):
        a, b = lanes(a0, a1), lanes(b0, b1)
        hidden = x.astype(f32) + (a.astype(f32) + b.astype(f32))
        local_mean = jnp.mean(hidden, axis=0, keepdims=True)
        dev = hidden - local_mean
        return hidden, join(local_mean, jnp.sum(dev * dev, axis=0, keepdims=True))

    hidden, moments = do(residual, x_own, *flying[0], *flying[1])
    count = blk
    for axis, step in at.steps(False) + [("core", 1)]:
        other = at.core(moments) if axis == "core" else at.along(moments, axis, step)

        def merge(a, b):
            gap = a[0:1] - b[0:1]
            return join(0.5 * (a[0:1] + b[0:1]), a[1:2] + b[1:2] + gap * gap * (count / 2.0))

        moments = do(merge, moments, other)
        count *= 2

    def second_norm(hidden, moments, cols):
        inv2 = lax.rsqrt(moments[1:2] / width + eps_norm)
        z2 = (hidden - moments[0:1]) * inv2
        return (z2 * cols[:, 2:3] + cols[:, 3:4]).astype(bf16), z2, inv2

    gains = gain_step(gains)
    xn2_own, z2, inv2 = do(second_norm, hidden, moments, own_cols)
    xn2 = do(join, xn2_own, at.core(xn2_own))

    flying = send_products([wg_cut, wu_cut], [xn2, xn2])

    wd_own = do(cast, w_down)
    wg = do(stack_turned, *wg_parts)
    wu = do(stack_turned, *wu_parts)
    cot_all = do(lambda a, b: token_rows(a, b, core), cot_parts, cot_theirs)
    grad_act = do(lambda w, c: mm(w, c, LAST, f32, tn=256), wd_own, cot_all)
    cot_cols = do(lambda c: own_columns(c, my_block.reshape(1), blk), cot_all)
    wo_own = do(cast, w_out)
    wq = do(stack_turned, *wq_parts)
    gains = do(lambda a, b: a + b, *gains)
    while gain_steps:
        gains = do(lambda a, b: a + b, *gain_step(gains))
    gains = do(lambda g: g.reshape(4, ffb).T, gains)
    flying = scatter_rest(flying)

    gate0, gate1, up0, up1, act, sums = do(gated, *flying[0], *flying[1], grad_act, gains)

    def parts_of(count, want):
        return max(n for n in range(1, want + 1) if count % (16 * n) == 0)

    def even(count, want):
        n = parts_of(count, want)
        return [(k * (count // n), count // n) for k in range(n)]

    down_rows, up_rows = even(ffb, 2), [(0, blk)]

    def push_pairs(name, g, rows):
        for k, (at_row, count) in enumerate(rows):
            reps.push((name, "theirs", k), g[blk + at_row : blk + at_row + count])
            reps.push((name, "mine", k), g[at_row : at_row + count])

    results = {"down": None, "out": None, "up": None, "qkv": None}
    states = {
        "down": (w_down, m_down, v_down),
        "out": (w_out, m_out, v_out),
        "up": (w_up, m_up, v_up),
        "qkv": (w_qkv, m_qkv, v_qkv),
    }
    rates = {"down": 0.02, "out": 0.2, "up": 0.03, "qkv": 0.03}

    def adam(name, grads, row_first, lead, unit, rb):
        results[name] = do(
            lambda s, g, prev: adam_part(s, g, core, rates[name], prev, row_first, lead, unit, rb),
            states[name],
            grads,
            results[name],
        )

    jobs = []
    for k, (at_row, count) in enumerate(down_rows):
        jobs.append(("down", [("down", k)], at_row, 0, count, 1024))
    for name, lead in (("gate", 0), ("up", Y)):
        for k, (at_row, count) in enumerate(up_rows):
            jobs.append(("up", [(name, "mine", k), (name, "theirs", k)], at_row, lead, count, S * ffb))
    for k in range(2):
        jobs.append(("out", [("out", k)], 0, k, blk, width // 2))
    for third in (2, 1, 0):
        jobs.append(("qkv", [(third, 0), (third, 1, "theirs")], 0, third * Y, blk, S * blk))
    received = {}

    def update(limit):
        for name in list(reps.done):
            if name in ("out", 0, 1, 2):
                g = reps.done.pop(name)
                half = g.shape[0] // 2
                reps.done[(name, 0)] = g[:half]
                reps.done[(name, 1) if name == "out" else (name, 1, "theirs")] = g[half:]
        for name in list(reps.done):
            if "theirs" in name and name not in received:
                received[name] = at.core(reps.done[name])
        while jobs and limit and all(k in reps.done for k in jobs[0][1]):
            name, needs, at_row, lead, count, unit = jobs.pop(0)
            rb = max(n for n in range(8, min(count, 176) + 1, 8) if count % n == 0 and at_row % n == 0)
            adam(name, [received[k] if "theirs" in k else reps.done[k] for k in needs], at_row, lead, unit, rb)
            limit -= 1

    def ticks(n):
        for _ in range(n):
            reps.tick()

    wide = 2 * FF // 8

    def quarter_heads(x):
        return [x[:, h][None, None] for h in halves]

    n, start, finish, gate_all = gather_steps([gate0[None, None], gate1[None, None]], 1)
    start(0)
    g_down = do(lambda a, c: mm(a, c, PLAIN, bf16, tn=512), act, cot_all)
    for k, (at_row, count) in enumerate(down_rows):
        reps.push(("down", k), g_down[at_row : at_row + count])
    ticks(1)

    steps2 = at.steps(False) + [("core", 1)]

    def sum_send(sums, axis, step):
        return at.core(sums) if axis == "core" else at.along(sums, axis, step)

    def sum_step(sums, axis, step):
        return do(lambda a, b: a + b, sums, sum_send(sums, axis, step))

    tiny = list(steps2)
    sums_got = sum_send(sums, *tiny.pop(0))
    for i in range(1, n):
        finish()
        sums = do(lambda a, b: a + b, sums, sums_got)
        sums_got = sum_send(sums, *tiny.pop(0))
        start(i, sums)
        ticks(1)
    n, start_up, finish_up, up_all = gather_steps([up0[None, None], up1[None, None]], 1)
    ggate_all = gate_all().reshape(Y * S * ffb, T)
    sums = do(lambda a, b: a + b, sums, sums_got)
    start_up(0, sums)
    while tiny:
        sums = sum_step(sums, *tiny.pop(0))
    g_gate = do(lambda x, g: mm(x, g, LAST, bf16, tn=wide), xn2, ggate_all)
    push_pairs("gate", g_gate, up_rows)
    finish_up()
    for i in range(1, n):
        start_up(i)
        if i == 1:
            part_gate = do(lambda w, g: mm(w, g, PLAIN, f32, tn=256), wg, ggate_all)
            out_part = do(lambda w, a: mm(w, a, FIRST, bf16, tm=512), wd_own, act)
            ticks(1)
        if i < n - 1:
            finish_up()
    gup_all = up_all().reshape(Y * S * ffb, T)
    part = do(lambda w, g, p: dot(w, g, PLAIN) + p, wu, gup_all, part_gate)
    part_theirs = at.core(part[blk:])

    def branch(a, b, cot, z, scale, gain, sums):
        gxn2 = a + b
        e = gxn2 * gain
        grad_hidden = cot.astype(f32) + scale * (e - sums[0:1] / width - z * (sums[1:2] / width))
        return grad_hidden.astype(bf16), grad_hidden, gxn2

    grad_branch, grad_hidden, gxn2 = do(
        branch, part[:blk], part_theirs, cot_cols, z2, inv2, own_cols[:, 2:3], sums
    )
    n, start, finish, branch_all = gather_steps(quarter_heads(grad_branch), 1)
    start(0)
    g_up = do(lambda x, g: mm(x, g, LAST, bf16, tn=wide), xn2, gup_all)
    push_pairs("up", g_up, up_rows)
    finish()
    for i in range(1, n):
        start(i)
        if i == 1:
            ticks(1)
        if i < n - 1:
            finish()
    gbr_c = branch_all()[0]
    gbr_o = at.core(gbr_c)
    gbr = do(lambda a, b: in_order(a, b, 1).reshape(width, T), gbr_c, gbr_o)
    grad_attn = do(lambda w, g: dot(w, g, PLAIN).astype(bf16), wo_own, gbr)

    gqkvs = []
    for k in range(2):
        dout = grad_attn[:, halves[k]].reshape(heads, HEAD_DIM, H)
        gqkvs.append(do(attend_back, qkvs[k], dout, stats[k], table[seqs[k]]).reshape(3, blk, H))
    n, start, finish, gqkv_done = gather_steps([g.reshape(1, 1, 3 * blk, H) for g in gqkvs], 3)
    start(0)
    attn = lanes(*attns)
    g_out = do(
        lambda a, g: join(*[mm(a, g[k * width // 2 : (k + 1) * width // 2], LAST, bf16, tn=512) for k in range(2)]),
        attn,
        gbr,
    )
    reps.push("out", g_out)
    update(1)
    ticks(1)
    finish()
    for i in range(1, n):
        start(i)
        if i == 1:
            update(1)
            ticks(1)
        if i < n - 1:
            finish()
    gqkv = gqkv_done().reshape(3, Y * S * blk, T)
    out_split = out_part.reshape(Y, 2, S * blk, T)
    out_kept = pick(out_split, 1, at.c).reshape(-1, T)
    out_got = at.core(pick(out_split, 1, 1 - at.c).reshape(-1, T))

    def out_step(axis, step):
        bit = (at.index(axis) // step) % 2
        send, kept = do(lambda a, b: add_split(a, b, bit.reshape(1)), out_kept, out_got)
        return kept, at.along(send, axis, step)

    out_steps = at.steps(True)
    g = do(lambda x, g: mm(x, g, LAST, bf16, tn=512), xn1, gqkv[2])
    reps.push(2, g)
    ticks(1)
    for third in (1, 0):
        g = do(lambda x, g: mm(x, g, LAST, bf16, tn=512), xn1, gqkv[third])
        reps.push(third, g)
    part = do(lambda w, g: mm(w, g, PLAIN, f32, tn=256), wq, gqkv.reshape(3 * Y * S * blk, T))
    part_theirs = at.core(part[blk:])

    def first_back(a, b, x, mean, inv, gain, gxn2, z2, gqkv0, gqkv1):
        gxn1 = a + b
        z1 = (x.astype(f32) - mean) * inv
        e = gxn1 * gain
        sums = join(jnp.sum(e, axis=0, keepdims=True), jnp.sum(e * z1, axis=0, keepdims=True))
        small = jnp.concatenate(
            [
                jnp.sum(gxn1 * z1, axis=1)[None],
                jnp.sum(gxn1, axis=1)[None],
                jnp.sum(gxn2 * z2, axis=1)[None],
                jnp.sum(gxn2, axis=1)[None],
                jnp.sum(gqkv0.astype(f32), axis=2) + jnp.sum(gqkv1.astype(f32), axis=2),
            ],
            axis=0,
        )
        return sums, small, gxn1, z1

    sums, small, gxn1, z1 = do(
        first_back, part[:blk], part_theirs, x_own, mean1, inv1, own_cols[:, 0:1], gxn2, z2, *gqkvs
    )
    for axis, step in steps2:
        sums = sum_step(sums, axis, step)
    ticks(1)
    input_grad = do(
        lambda h, grad, z, scale, gain, sums: (
            h + scale * (grad * gain - sums[0:1] / width - z * (sums[1:2] / width))
        ).astype(bf16),
        grad_hidden,
        gxn1,
        z1,
        inv1,
        own_cols[:, 0:1],
        sums,
    )

    def to_rows(cols):
        split = do(lambda c: c.reshape(blk, S, at.ctx_size, rows).transpose(2, 1, 0, 3).reshape(nb, blk, rows), cols)
        got = lax.all_to_all(split, plane, split_axis=0, concat_axis=0, tiled=True)
        return do(lambda g: g.reshape(width, rows).T, got)

    input_rows = to_rows(input_grad).astype(f32)
    steps_rep = []
    step = 1
    while step < lax.axis_size("rep"):
        steps_rep.append(step)
        step *= 2

    def small_step():
        nonlocal small
        small = getattr(reps, "kept", small)
        k = steps_rep.pop(0)
        other = lax.ppermute(small, "rep", [(i, i ^ k) for i in range(lax.axis_size("rep"))])
        small = do(lambda a, b: a + b, small, other)
        return small

    out_kept, out_got = out_step(*out_steps[0])
    reps.tick(small_step)
    update(1)
    for axis, step in out_steps[1:]:
        out_kept, out_got = out_step(axis, step)
    reps.tick(small_step)
    sent = do(lambda s: jnp.broadcast_to(s.reshape(1, 7, blk), (nb, 7, blk)), reps.kept)
    small_all = lax.all_to_all(sent, plane, split_axis=0, concat_axis=0, tiled=True)

    def norm_update(every, *a):
        return adam_update(*a, every.transpose(1, 0, 2).reshape(7, width), 0.3, 0.0)

    mn, vn, wn = do(norm_update, small_all, norm_params, m_norm, v_norm)
    update(2)
    ticks(1)
    update(1)
    out_cols = do(
        lambda h, a, b: (h + (a.astype(f32) + b.astype(f32))).astype(bf16), hidden, out_kept, out_got
    )
    block_output = to_rows(out_cols)
    while reps.busy():
        reps.tick()
        update(2)
    update(len(jobs))
    return (
        (block_output.reshape(tokens.shape), input_rows.reshape(tokens.shape))
        + tuple(results["qkv"])
        + tuple(results["out"])
        + tuple(results["up"])
        + tuple(results["down"])
        + (mn, vn, wn)
    )


def solution(mesh):
    tok = P("rep", "ctx", "shard", None)
    row = P(("ctx", "shard"), None)
    placed = (tok, tok, P("rep", "shard", None)) + (row,) * 4 + (P(),) + (row,) * 8 + (P(), P())
    return jax.shard_map(
        body,
        mesh=mesh,
        in_specs=placed,
        out_specs=(tok, tok) + (row,) * 12 + (P(),) * 3,
        check_vma=False,
    )
```

```python
import functools

import jax
import jax.numpy as jnp
from jax import lax
from jax.experimental import pallas as pl
from jax.experimental.pallas import tpu as pltpu
from jax.sharding import PartitionSpec as P

HEADS = 32
HEAD_DIM = 64
FF = 5632
ROTARY = 16
STEP = 10

eps_norm = 1e-05
masked_score = -1e30
beta_one = 0.9
beta_two = 0.999
adam_eps = 1e-08
weight_decay = 0.1
score_scale = HEAD_DIM ** (-0.5)
FIRST = (((0,), (0,)), ((), ()))
LAST = (((1,), (1,)), ((), ()))
PLAIN = (((1,), (0,)), ((), ()))
bf16 = jnp.bfloat16
f32 = jnp.float32


def dot(a, b, dims):
    return lax.dot_general(a, b, dims, preferred_element_type=f32)


def adam_update(weight, moment_one, moment_two, grad, step_rate, decay_rate):
    first_new = beta_one * moment_one + (1.0 - beta_one) * grad
    second_new = beta_two * moment_two + (1.0 - beta_two) * grad * grad
    first_hat = first_new / (1.0 - beta_one**STEP)
    second_hat = second_new / (1.0 - beta_two**STEP)
    weight_new = weight - step_rate * (
        first_hat / (jnp.sqrt(second_hat) + adam_eps) + decay_rate * weight
    )
    return (first_new, second_new, weight_new)


class Plane:
    def __init__(self):
        self.s_size = lax.axis_size("shard")
        self.ctx_size = lax.axis_size("ctx")
        self.y_size = self.ctx_size // 2
        self.ctx = lax.axis_index("ctx")
        self.s = lax.axis_index("shard")
        self.y = self.ctx // 2
        self.c = self.ctx % 2
        self.blocks = self.ctx_size * self.s_size

    def core(self, x):
        return lax.ppermute(x, "ctx", [(i, i ^ 1) for i in range(self.ctx_size)])

    def along(self, x, axis, step):
        if axis == "y":
            return lax.ppermute(x, "ctx", [(i, i ^ (2 * step)) for i in range(self.ctx_size)])
        return lax.ppermute(x, "shard", [(i, i ^ step) for i in range(self.s_size)])

    def index(self, axis):
        return self.y if axis == "y" else self.s

    def steps(self, flip):
        ys = []
        k = self.y_size // 2
        while k:
            ys.append(("y", k))
            k //= 2
        ss = []
        k = self.s_size // 2
        while k:
            ss.append(("s", k))
            k //= 2
        return ys + ss if flip else ss + ys

    def chip_exchange(self, x, take):
        out = [(self.y, self.s, take(self.y, self.s))]
        for ry in range(self.y_size):
            for rs in range(self.s_size):
                if ry or rs:
                    y, s = self.y ^ ry, self.s ^ rs
                    mask = 2 * ry * self.s_size + rs
                    perm = [(i, i ^ mask) for i in range(self.blocks)]
                    out.append((y, s, lax.ppermute(take(y, s), ("ctx", "shard"), perm)))
        return out

    def sum_all(self, x):
        for axis, step in self.steps(False):
            x = x + self.along(x, axis, step)
        return x + self.core(x)

    def scatter_sum(self, p, flip):
        axes = {"y": 1, "s": 2}
        steps = self.steps(flip)
        kept = got = None
        for n, (axis, step) in enumerate(steps):
            ax = axes[axis]
            bit = (self.index(axis) // step) % 2
            kept = lax.dynamic_slice_in_dim(p, bit * step, step, ax)
            send = lax.dynamic_slice_in_dim(p, (1 - bit) * step, step, ax)
            got = self.along(send, axis, step)
            if n + 1 < len(steps):
                p = (kept.astype(f32) + got.astype(f32)).astype(bf16)
        return kept[:, 0, 0], got[:, 0, 0]

    def gather(self, p, flip):
        axes = {"y": 1, "s": 2}
        p = p[:, None, None]
        for axis, step in reversed(self.steps(flip)):
            ax = axes[axis]
            bit = (self.index(axis) // step) % 2
            got = self.along(p, axis, step)
            first = bit == 0
            p = jnp.concatenate([jnp.where(first, p, got), jnp.where(first, got, p)], ax)
        return p


class Order:
    def __init__(self):
        self.token = lax.create_token()

    def __call__(self, stage, *args):
        args, token = lax.optimization_barrier((args, self.token))
        out, self.token = lax.optimization_barrier((stage(*args), token))
        return out


SMALL = pl.CostEstimate(flops=1024, bytes_accessed=1024, transcendentals=0)


class RepSum:
    def __init__(self, order):
        self.order = order
        z = lax.axis_index("rep")
        self.end = (z == 0) | (z == lax.axis_size("rep") - 1)
        self.queue = []
        self.flight = []
        self.depth = 1
        self.done = {}

    def push(self, name, g):
        self.queue.append((name, g))

    def busy(self):
        return bool(self.queue or self.flight)

    def tick(self, between=None):
        old = {}
        if len(self.flight) >= self.depth or (self.flight and not self.queue):
            old = self.flight.pop(0)
        new = self.queue.pop(0) if self.queue else None
        values = {}
        if "in" in old:
            values["g"], values["g_got"] = old["in"][1], old["in_got"]
        if "mid" in old:
            values["s"], values["s_got"] = old["mid"][1], old["mid_got"]
        if new:
            values["new"] = new[1]
        both = new and "mid" in old and new[1].shape == old["mid"][1].shape
        if "out" in old:
            values["out_got"] = old["out_got"]

        def stage(v):
            def add(a, b):
                return lax.reduce_precision(a.astype(f32) + b.astype(f32), 8, 7).astype(bf16)

            out = {}
            if "g" in v:
                out["a_sum"] = add(v["g"], v["g_got"])
            if "s" in v:
                total = add(v["s"], v["s_got"])
                out["total"] = jnp.where(self.end, v["new"], total) if both else total
            if "new" in v and not both:
                out["new"] = v["new"]
            if "out_got" in v:
                out["z_got"] = v["out_got"]
            return out

        if not values:
            return
        out = self.order(stage, values)
        if between is not None:
            out, self.kept = lax.optimization_barrier((out, between()))
        if "out" in old:
            self.done[old["out"][0]] = jnp.where(self.end, out["z_got"], old["out"][1])
        slot = {}
        if both:
            got = lax.ppermute(out["total"], "rep", [(0, 1), (1, 0), (2, 3), (3, 2)])
            slot = {"in": new, "in_got": got, "out": (old["mid"][0], out["total"]), "out_got": got}
        else:
            if new:
                slot["in"] = new
                slot["in_got"] = lax.ppermute(out["new"], "rep", [(0, 1), (3, 2)])
            if "mid" in old:
                slot["out"] = (old["mid"][0], out["total"])
                slot["out_got"] = lax.ppermute(out["total"], "rep", [(1, 0), (2, 3)])
        if "in" in old:
            slot["mid"] = (old["in"][0], out["a_sum"])
            slot["mid_got"] = lax.ppermute(out["a_sum"], "rep", [(1, 2), (2, 1)])
        if slot:
            self.flight.append(slot)


def cast_kernel(w_ref, out_ref):
    out_ref[...] = w_ref[...].astype(bf16)


def cast(w):
    rows, width = w.shape
    unit = max(n for n in (128, 256, 512, 1024, 1408, 2048, 2816) if width % n == 0)
    spec = pl.BlockSpec((rows, unit), lambda i: (0, i))
    return pl.pallas_call(
        cast_kernel,
        grid=(width // unit,),
        in_specs=[spec],
        out_specs=spec,
        out_shape=jax.ShapeDtypeStruct(w.shape, bf16),
        compiler_params=pltpu.CompilerParams(vmem_limit_bytes=48 * 1024 * 1024),
        cost_estimate=SMALL,
    )(w)


def gated_kernel(ga_ref, gb_ref, ua_ref, ub_ref, grad_ref, gains_ref, g0_ref, g1_ref, u0_ref, u1_ref, act_ref, sums_ref):
    half = g0_ref.shape[1]
    gate = ga_ref[...].astype(f32) + gb_ref[...].astype(f32)
    up = ua_ref[...].astype(f32) + ub_ref[...].astype(f32)
    sig = jax.nn.sigmoid(gate)
    silu = gate * sig
    grad = grad_ref[...]
    act_ref[...] = (silu * up).astype(bf16)
    ggate = (grad * up * sig * (1.0 + gate * (1.0 - sig))).astype(bf16)
    gup = (grad * silu).astype(bf16)
    g0_ref[...] = ggate[:, :half]
    g1_ref[...] = ggate[:, half:]
    u0_ref[...] = gup[:, :half]
    u1_ref[...] = gup[:, half:]
    a, b = ggate.astype(f32), gup.astype(f32)
    e = jnp.sum(a * gains_ref[:, 0:1] + b * gains_ref[:, 2:3], axis=0, keepdims=True)
    ez = jnp.sum(a * (gate - gains_ref[:, 1:2]) + b * (up - gains_ref[:, 3:4]), axis=0, keepdims=True)
    both = jnp.concatenate([e, ez], axis=0)

    @pl.when(pl.program_id(0) == 0)
    def _():
        sums_ref[...] = both

    @pl.when(pl.program_id(0) > 0)
    def _():
        sums_ref[...] += both


def gated(ga, gb, ua, ub, grad_act, gains):
    rows, t = grad_act.shape
    n = max(n for n in (1, 2, 4) if rows % (16 * n) == 0)
    whole = pl.BlockSpec((rows // n, t), lambda i: (i, 0))
    half = pl.BlockSpec((rows // n, t // 2), lambda i: (i, 0))
    out_half = jax.ShapeDtypeStruct((rows, t // 2), bf16)
    return pl.pallas_call(
        gated_kernel,
        grid=(n,),
        in_specs=[whole] * 5 + [pl.BlockSpec((rows // n, 4), lambda i: (i, 0))],
        out_specs=[half] * 4 + [whole, pl.BlockSpec((2, t), lambda i: (0, 0))],
        out_shape=[out_half] * 4 + [jax.ShapeDtypeStruct((rows, t), bf16), jax.ShapeDtypeStruct((2, t), f32)],
        compiler_params=pltpu.CompilerParams(vmem_limit_bytes=56 * 1024 * 1024),
        cost_estimate=SMALL,
    )(ga, gb, ua, ub, grad_act, gains)


def own_columns_kernel(block_ref, x_ref, out_ref):
    out_ref[...] = x_ref[...].T


def own_columns(x, block, width):
    rows = x.shape[0]
    if width % 128:
        return lax.dynamic_slice_in_dim(x, block[0] * width, width, 1).T
    tile = min(rows, 512)
    return pl.pallas_call(
        own_columns_kernel,
        grid_spec=pltpu.PrefetchScalarGridSpec(
            num_scalar_prefetch=1,
            grid=(rows // tile,),
            in_specs=[pl.BlockSpec((tile, width), lambda i, block: (i, block[0]))],
            out_specs=pl.BlockSpec((width, tile), lambda i, block: (0, i)),
        ),
        out_shape=jax.ShapeDtypeStruct((width, rows), bf16),
        compiler_params=pltpu.CompilerParams(vmem_limit_bytes=48 * 1024 * 1024),
        cost_estimate=SMALL,
    )(block, x)


def split_kernel(core_ref, w_ref, mine_ref, theirs_ref):
    unit = mine_ref.shape[0]
    first = core_ref[0] == 0
    a, b = w_ref[:, :unit], w_ref[:, unit:]
    mine_ref[...] = jnp.where(first, a, b).T.astype(bf16)
    theirs_ref[...] = jnp.where(first, b, a).T.astype(bf16)


def split_columns(w, core, lead, unit, count):
    rows = w.shape[0]
    half = pl.BlockSpec((unit, rows), lambda j, core: (j, 0))
    out = jax.ShapeDtypeStruct((count * unit, rows), bf16)
    return pl.pallas_call(
        split_kernel,
        grid_spec=pltpu.PrefetchScalarGridSpec(
            num_scalar_prefetch=1,
            grid=(count,),
            in_specs=[pl.BlockSpec((rows, 2 * unit), lambda j, core: (0, lead + j))],
            out_specs=[half, half],
        ),
        out_shape=[out, out],
        compiler_params=pltpu.CompilerParams(vmem_limit_bytes=32 * 1024 * 1024),
        cost_estimate=SMALL,
    )(core, w)


def arrange_kernel(at_ref, a_ref, b_ref, c_ref, d_ref, send_ref, keep_ref):
    send_ref[...] = jnp.concatenate([a_ref[...], b_ref[...]], axis=1)
    keep_ref[...] = jnp.concatenate([c_ref[...], d_ref[...]], axis=1)


def arrange(mine, got, place, pre, y_size, s_size, unit, flip):
    r = mine.shape[1]
    half = pre * y_size * s_size // 2

    def block(i, place, keep):
        p = i % pre
        i = i // pre
        if flip:
            s, y = i % s_size, i // s_size
            bit = place[0] // (y_size // 2)
            bit = bit if keep else 1 - bit
            y = y + bit * (y_size // 2)
        else:
            y, s = i % y_size, i // y_size
            bit = place[1] // (s_size // 2)
            bit = bit if keep else 1 - bit
            s = s + bit * (s_size // 2)
        return ((p * y_size + y) * s_size + s, 0)

    def spec(keep):
        return pl.BlockSpec((unit, r), lambda i, place: block(i, place, keep))

    out = jax.ShapeDtypeStruct((half * unit, 2 * r), bf16)
    out_spec = pl.BlockSpec((unit, 2 * r), lambda i, place: (i, 0))
    return pl.pallas_call(
        arrange_kernel,
        grid_spec=pltpu.PrefetchScalarGridSpec(
            num_scalar_prefetch=1,
            grid=(half,),
            in_specs=[spec(False), spec(False), spec(True), spec(True)],
            out_specs=[out_spec, out_spec],
        ),
        out_shape=[out, out],
        compiler_params=pltpu.CompilerParams(vmem_limit_bytes=32 * 1024 * 1024),
        cost_estimate=SMALL,
    )(place, mine, got, mine, got)


def product_kernel(dims, a_ref, b_ref, *refs):
    p = dot(a_ref[...], b_ref[...], dims)
    if len(refs) == 2:
        p = p + refs[0][...]
    refs[-1][...] = p.astype(refs[-1].dtype)


def mm(a, b, dims, dtype, tm=None, tn=None, add=None):
    (ca,), (cb,) = dims[0]
    m, k, n = a.shape[1 - ca], a.shape[ca], b.shape[1 - cb]
    tm, tn = tm or m, tn or n
    a_block = [0, 0]
    a_block[ca], a_block[1 - ca] = k, tm
    b_block = [0, 0]
    b_block[cb], b_block[1 - cb] = k, tn
    out = pl.BlockSpec((tm, tn), lambda i, j: (i, j))
    return pl.pallas_call(
        functools.partial(product_kernel, dims),
        grid=(m // tm, n // tn),
        in_specs=[
            pl.BlockSpec(tuple(a_block), (lambda i, j: (0, i)) if ca == 0 else (lambda i, j: (i, 0))),
            pl.BlockSpec(tuple(b_block), (lambda i, j: (0, j)) if cb == 0 else (lambda i, j: (j, 0))),
        ]
        + ([] if add is None else [out]),
        out_specs=out,
        out_shape=jax.ShapeDtypeStruct((m, n), dtype),
        compiler_params=pltpu.CompilerParams(vmem_limit_bytes=48 * 1024 * 1024),
        cost_estimate=SMALL,
    )(*((a, b) if add is None else (a, b, add)))


def last_step_kernel(bits_ref, own0_ref, got0_ref, own1_ref, got1_ref, out_ref):
    y, s = pl.program_id(1), pl.program_id(2)
    half = own0_ref.shape[3]
    ys, ss = bits_ref[2], bits_ref[3]
    a = jnp.where(s // ss == bits_ref[1], own0_ref[0, 0], got0_ref[0, 0])
    b = jnp.where(y // ys == bits_ref[0], own1_ref[0, 0], got1_ref[0, 0])
    out_ref[0, 0, 0, :, :half] = a
    out_ref[0, 0, 0, :, half:] = b


def last_step(parts, got, bits, pre, y_size, s_size):
    rows, half = parts[0].shape[2] // pre, parts[0].shape[3]
    along_s = pl.BlockSpec((1, 1, rows, half), lambda p, y, s, bits: (y, s % (s_size // 2), p, 0))
    along_y = pl.BlockSpec((1, 1, rows, half), lambda p, y, s, bits: (y % (y_size // 2), s, p, 0))
    return pl.pallas_call(
        last_step_kernel,
        grid_spec=pltpu.PrefetchScalarGridSpec(
            num_scalar_prefetch=1,
            grid=(pre, y_size, s_size),
            in_specs=[along_s, along_s, along_y, along_y],
            out_specs=pl.BlockSpec((1, 1, 1, rows, 2 * half), lambda p, y, s, bits: (p, y, s, 0, 0)),
        ),
        out_shape=jax.ShapeDtypeStruct((pre, y_size, s_size, rows, 2 * half), bf16),
        compiler_params=pltpu.CompilerParams(vmem_limit_bytes=48 * 1024 * 1024),
        cost_estimate=SMALL,
    )(bits, parts[0], got[0], parts[1], got[1])


def stack_turned_kernel(a_ref, b_ref, out_ref):
    r = a_ref.shape[1]
    out_ref[:r] = a_ref[...].T
    out_ref[r:] = b_ref[...].T


def stack_turned(a, b):
    rows, width = a.shape
    n = max(n for n in (1, 2, 4, 6, 8, 11) if rows % (128 * n) == 0)
    spec = pl.BlockSpec((rows // n, width), lambda i: (i, 0))
    return pl.pallas_call(
        stack_turned_kernel,
        grid=(n,),
        in_specs=[spec, spec],
        out_specs=pl.BlockSpec((2 * width, rows // n), lambda i: (0, i)),
        out_shape=jax.ShapeDtypeStruct((2 * width, rows), bf16),
        compiler_params=pltpu.CompilerParams(vmem_limit_bytes=48 * 1024 * 1024),
        cost_estimate=SMALL,
    )(a, b)


def add_split_kernel(bit_ref, a_ref, b_ref, c_ref, d_ref, send_ref, keep_ref):
    send_ref[...] = (a_ref[...].astype(f32) + b_ref[...].astype(f32)).astype(bf16)
    keep_ref[...] = (c_ref[...].astype(f32) + d_ref[...].astype(f32)).astype(bf16)


def add_split(kept, got, bit):
    rows, t = kept.shape
    half = rows // 2
    n = max(n for n in (1, 2, 3, 4) if half % (16 * n) == 0)
    rb = half // n
    away = pl.BlockSpec((rb, t), lambda i, bit: ((1 - bit[0]) * n + i, 0))
    here = pl.BlockSpec((rb, t), lambda i, bit: (bit[0] * n + i, 0))
    out = jax.ShapeDtypeStruct((half, t), bf16)
    out_spec = pl.BlockSpec((rb, t), lambda i, bit: (i, 0))
    return pl.pallas_call(
        add_split_kernel,
        grid_spec=pltpu.PrefetchScalarGridSpec(
            num_scalar_prefetch=1,
            grid=(n,),
            in_specs=[away, away, here, here],
            out_specs=[out_spec, out_spec],
        ),
        out_shape=[out, out],
        compiler_params=pltpu.CompilerParams(vmem_limit_bytes=48 * 1024 * 1024),
        cost_estimate=SMALL,
    )(bit, kept, got, kept, got)


def token_rows_kernel(core_ref, a_ref, b_ref, c_ref, d_ref, out_ref):
    mine = core_ref[0] == pl.program_id(2)
    half = out_ref.shape[0] // 2
    out_ref[:half] = jnp.where(mine, a_ref[0, 0], c_ref[0, 0])
    out_ref[half:] = jnp.where(mine, b_ref[0, 0], d_ref[0, 0])


def token_rows(mine, theirs, core):
    y_size, s_size, rows, width = mine[0].shape
    part = pl.BlockSpec((1, 1, rows, width), lambda s, y, c, core: (y, s, 0, 0))
    return pl.pallas_call(
        token_rows_kernel,
        grid_spec=pltpu.PrefetchScalarGridSpec(
            num_scalar_prefetch=1,
            grid=(s_size, y_size, 2),
            in_specs=[part] * 4,
            out_specs=pl.BlockSpec((2 * rows, width), lambda s, y, c, core: ((s * y_size + y) * 2 + c, 0)),
        ),
        out_shape=jax.ShapeDtypeStruct((s_size * y_size * 4 * rows, width), bf16),
        compiler_params=pltpu.CompilerParams(vmem_limit_bytes=32 * 1024 * 1024),
        cost_estimate=SMALL,
    )(core, *mine, *theirs)


def adam_kernel(rate, two, core_ref, w_ref, m_ref, v_ref, *refs):
    grad = refs[0][...].astype(f32)
    if two:
        other = refs[1][...].astype(f32)
        mine = core_ref[0] == 0
        grad = jnp.concatenate([jnp.where(mine, grad, other), jnp.where(mine, other, grad)], axis=1)
    new_m_ref, new_v_ref, new_w_ref = refs[-3:]
    new_m, new_v, new_w = adam_update(w_ref[...], m_ref[...], v_ref[...], grad, rate, weight_decay)
    new_m_ref[...] = new_m
    new_v_ref[...] = new_v
    new_w_ref[...] = new_w


def adam_part(state, grads, core, rate, prev, row_first, lead, unit, rb):
    w, m, v = state
    two = len(grads) == 2
    rows, width = grads[0].shape
    whole = pl.BlockSpec((rb, unit * len(grads)), lambda i, g, core: (row_first // rb + i, lead + g))
    half = pl.BlockSpec((rb, unit), lambda i, g, core: (i, g))
    out = jax.ShapeDtypeStruct(w.shape, f32)
    extra, aliases = [], {}
    if prev is not None:
        extra = list(prev)
        aliases = {4 + len(grads) + i: i for i in range(3)}
    return pl.pallas_call(
        functools.partial(adam_kernel, rate, two),
        grid_spec=pltpu.PrefetchScalarGridSpec(
            num_scalar_prefetch=1,
            grid=(rows // rb, width // unit),
            in_specs=[whole] * 3 + [half] * len(grads) + [pl.BlockSpec(memory_space=pl.ANY)] * len(extra),
            out_specs=[whole] * 3,
        ),
        out_shape=[out] * 3,
        input_output_aliases=aliases,
        compiler_params=pltpu.CompilerParams(vmem_limit_bytes=48 * 1024 * 1024),
        cost_estimate=SMALL,
    )(core, w, m, v, *grads, *extra)


def attend_kernel(kept_ref, got_ref, bias_ref, table_ref, qkv_ref, out_ref, stat_ref):
    half = ROTARY // 2
    cos, sin, pos = table_ref[0, :half], table_ref[0, half:ROTARY], table_ref[0, ROTARY:]
    parts = []
    for i in range(3):
        v = kept_ref[i, 0].astype(f32) + got_ref[i, 0].astype(f32) + bias_ref[i, 0]
        if i < 2:
            a, b = v[:half], v[half:ROTARY]
            v = jnp.concatenate([a * cos - b * sin, b * cos + a * sin, v[ROTARY:]], axis=0)
        v = v.astype(bf16)
        qkv_ref[i, 0] = v
        parts.append(v)
    q, k, v = parts
    scores = dot(k, q, FIRST) * score_scale
    scores = jnp.where(pos.T[:, :1] <= pos[:1], scores, masked_score)
    peak = jnp.max(scores, axis=0, keepdims=True)
    e = jnp.exp(scores - peak)
    total = jnp.sum(e, axis=0, keepdims=True)
    p = (e / total).astype(bf16)
    out_ref[0] = dot(v, p, PLAIN).astype(bf16)
    stat_ref[0, 0] = jnp.concatenate([peak, total], axis=0)


def attend(kept, got, bias, table):
    _, heads, hd, t = kept.shape
    seqs, _, seq = table.shape
    big = pl.BlockSpec((3, 1, hd, seq), lambda s, h: (0, h, 0, s))
    table_spec = pl.BlockSpec((1, table.shape[1], seq), lambda s, h: (s, 0, 0))
    stat = pl.BlockSpec((1, 1, 2, seq), lambda s, h: (s, h, 0, 0))
    return pl.pallas_call(
        attend_kernel,
        grid=(seqs, heads),
        in_specs=[
            big,
            big,
            pl.BlockSpec((3, 1, hd, 1), lambda s, h: (0, h, 0, 0)),
            table_spec,
        ],
        out_specs=[big, pl.BlockSpec((1, hd, seq), lambda s, h: (h, 0, s)), stat],
        out_shape=[
            jax.ShapeDtypeStruct((3, heads, hd, t), bf16),
            jax.ShapeDtypeStruct((heads, hd, t), bf16),
            jax.ShapeDtypeStruct((seqs, heads, 2, seq), f32),
        ],
        compiler_params=pltpu.CompilerParams(vmem_limit_bytes=32 * 1024 * 1024),
        cost_estimate=SMALL,
    )(kept, got, bias, table)


def attend_back_kernel(qkv_ref, dout_ref, stat_ref, table_ref, out_ref):
    half = ROTARY // 2
    cos, sin, pos = table_ref[0, :half], table_ref[0, half:ROTARY], table_ref[0, ROTARY:]
    q, k, v = qkv_ref[0, 0], qkv_ref[1, 0], qkv_ref[2, 0]
    dout = dout_ref[0]
    scores = dot(k, q, FIRST) * score_scale
    scores = jnp.where(pos.T[:, :1] <= pos[:1], scores, masked_score)
    p = jnp.exp(scores - stat_ref[0, 0, :1]) / stat_ref[0, 0, 1:]
    dp = dot(v, dout, FIRST)
    inner = jnp.sum(p * dp, axis=0, keepdims=True)
    ds = (p * (dp - inner)).astype(bf16)

    def back(x):
        a, b = x[:half], x[half:ROTARY]
        return jnp.concatenate([a * cos + b * sin, b * cos - a * sin, x[ROTARY:]], axis=0)

    out_ref[0, 0] = back(dot(k, ds, PLAIN) * score_scale).astype(bf16)
    out_ref[1, 0] = back(dot(q, ds, LAST) * score_scale).astype(bf16)
    out_ref[2, 0] = dot(dout, p.astype(bf16), LAST).astype(bf16)


def attend_back(qkv, dout, stats, table):
    _, heads, hd, t = qkv.shape
    seqs, _, seq = table.shape
    big = pl.BlockSpec((3, 1, hd, seq), lambda s, h: (0, h, 0, s))
    table_spec = pl.BlockSpec((1, table.shape[1], seq), lambda s, h: (s, 0, 0))
    stat = pl.BlockSpec((1, 1, 2, seq), lambda s, h: (s, h, 0, 0))
    return pl.pallas_call(
        attend_back_kernel,
        grid=(seqs, heads),
        in_specs=[
            big,
            pl.BlockSpec((1, hd, seq), lambda s, h: (h, 0, s)),
            stat,
            table_spec,
        ],
        out_specs=big,
        out_shape=jax.ShapeDtypeStruct((3, heads, hd, t), bf16),
        compiler_params=pltpu.CompilerParams(vmem_limit_bytes=32 * 1024 * 1024),
        cost_estimate=SMALL,
    )(qkv, dout, stats, table)


def body(
    tokens,
    cotangent,
    span_order,
    w_qkv,
    w_out,
    w_up,
    w_down,
    norm_params,
    m_qkv,
    v_qkv,
    m_out,
    v_out,
    m_up,
    v_up,
    m_down,
    v_down,
    m_norm,
    v_norm,
):
    at = Plane()
    do = Order()
    reps = RepSum(do)
    width = tokens.shape[3]
    rows = tokens.shape[1]
    S, Y, nb = at.s_size, at.y_size, at.blocks
    plane = ("ctx", "shard")
    blk = width // nb
    ffb = FF // nb
    heads = blk // HEAD_DIM
    seq = rows * at.ctx_size
    T = S * seq
    H = T // 2
    first = at.c == 0
    core = at.c.reshape(1)
    my_block = at.ctx * S + at.s
    halves = (slice(0, H), slice(H, T))
    seqs = (slice(0, S // 2), slice(S // 2, S))

    def pick(x, axis, which):
        return lax.dynamic_index_in_dim(x, which, axis, keepdims=False)

    def in_order(mine, theirs, axis):
        return jnp.stack([jnp.where(first, mine, theirs), jnp.where(first, theirs, mine)], axis=axis)

    def join(a, b):
        return jnp.concatenate([a, b], axis=0)

    def lanes(a, b):
        return jnp.concatenate([a, b], axis=1)

    def gather_steps(parts, pre):
        n = len(at.steps(False))
        state = {"parts": list(parts)}

        def start(i, after=None):
            if after is not None:
                state["parts"], _ = lax.optimization_barrier((state["parts"], after))
            state["got"] = []
            state["at"] = []
            for k in range(2):
                axis, step = list(reversed(at.steps(bool(k))))[i]
                state["at"].append((axis, step))
                state["got"].append(at.along(state["parts"][k], axis, step))

        def finish():
            def put(parts, got):
                out = []
                for k in range(2):
                    axis, step = state["at"][k]
                    ax = {"y": 0, "s": 1}[axis]
                    low = (at.index(axis) // step) % 2 == 0
                    a, b = parts[k], got[k]
                    out.append(jnp.concatenate([jnp.where(low, a, b), jnp.where(low, b, a)], ax))
                return out

            state["parts"] = do(put, state["parts"], state["got"])

        def result():
            ys, ss = Y // 2, S // 2
            bits = jnp.stack([at.y // ys, at.s // ss, jnp.int32(ys), jnp.int32(ss)]).astype(jnp.int32)
            return do(lambda p, g: last_step(p, g, bits, pre, Y, S), state["parts"], state["got"])

        return n, start, finish, result if pre else state

    x_rows = tokens.reshape(rows, width)
    order = span_order.reshape(-1).astype(f32)
    span = rows // 2

    def pack(x, order):
        xf = x.astype(f32)
        mean = jnp.mean(xf, axis=1)
        centred = xf - mean[:, None]
        inv = lax.rsqrt(jnp.mean(centred * centred, axis=1) + eps_norm)
        mine = lax.dynamic_slice_in_dim(order, 2 * at.ctx, 2)
        place = jnp.repeat(mine, span)
        terms = []
        for v in (mean, inv):
            for _ in range(3):
                t = lax.reduce_precision(v, 8, 7)
                terms.append(t)
                v = v - t
        extra = jnp.stack(terms + [place] + [jnp.zeros_like(place)] * 9).astype(bf16)
        blocks = x.T.reshape(nb, blk, rows)
        return jnp.concatenate([blocks, jnp.broadcast_to(extra[None], (nb, 16, rows))], axis=1)

    packed = do(pack, x_rows, order)
    got = lax.all_to_all(packed, plane, split_axis=0, concat_axis=0, tiled=True)

    def chip_rows(w, lead, unit, count):
        mine, theirs = do(lambda w: split_columns(w, core, lead, unit, count), w)
        return mine, at.core(theirs)

    wq_parts = chip_rows(w_qkv, 0, S * blk, 3 * Y)
    norm_cols = norm_params.reshape(7, nb, blk).transpose(1, 2, 0)
    own_cols = pick(norm_cols, 0, my_block)
    other_cols = pick(norm_cols, 0, (at.ctx ^ 1) * S + at.s)
    pair_cols = join(own_cols, other_cols)
    bias = own_cols[:, 4:7].T.reshape(3, heads, HEAD_DIM, 1)
    spot = jnp.stack([at.y, at.s])

    def cut_weights(parts, pre, unit, flip):
        return do(lambda a, b: arrange(a, b, spot, pre, Y, S, unit, flip), *parts)

    wq_cut = [cut_weights(wq_parts, 3, blk, bool(k)) for k in range(2)]

    def columns(got):
        x = got.reshape(at.ctx_size, S, blk + 16, rows).transpose(2, 1, 0, 3).reshape(blk + 16, T)
        x_own, extra = x[:blk], x[blk:].astype(f32)
        mean = extra[0:1] + extra[1:2] + extra[2:3]
        inv = extra[3:4] + extra[4:5] + extra[5:6]
        return x_own, mean, inv, extra[6:7]

    x_own, mean1, inv1, place = do(columns, got)
    x_other = at.core(x_own)
    cot = cotangent.reshape(2, 1, 1, rows // 2, width)
    cot_n, cot_start, cot_finish, cot_state = gather_steps([cot[0], cot[1]], 0)
    cot_start(0, x_own)

    def first_norm(mine, theirs, mean, inv, cols):
        x = join(mine, theirs).astype(f32)
        return ((x - mean) * inv * cols[:, 0:1] + cols[:, 1:2]).astype(bf16)

    xn1 = do(first_norm, x_own, x_other, mean1, inv1, pair_cols)

    def send_products(cut, xs):
        got, kept = [], []
        for k in range(2):
            axis, step = at.steps(bool(k))[0]
            p = do(lambda w, x: dot(w, x, PLAIN).astype(bf16), cut[k][0], xs[k])
            got.append(at.along(p, axis, step))
        for k in range(2):
            kept.append(do(lambda w, x: dot(w, x, PLAIN).astype(bf16), cut[k][1], xs[k]))
        return list(zip(kept, got))

    def scatter_rest(pairs):
        for i in range(1, len(at.steps(False))):
            out = []
            for k in range(2):
                axis, step = at.steps(bool(k))[i]
                bit = (at.index(axis) // step) % 2
                send, kept = do(lambda a, b: add_split(a, b, bit.reshape(1)), *pairs[k])
                out.append((kept, at.along(send, axis, step)))
            pairs = out
        return pairs

    flying = send_products(wq_cut, [xn1[:, h] for h in halves])

    for i in range(1, cot_n):
        cot_finish()
        cot_start(i)

    wo_parts = chip_rows(w_out, 0, S * blk, Y)
    wg_parts = chip_rows(w_up, 0, S * ffb, Y)
    wu_parts = chip_rows(w_up, Y, S * ffb, Y)
    wo_cut = [cut_weights(wo_parts, 1, blk, bool(k)) for k in range(2)]

    def positions(place):
        pos = place.reshape(S, seq) * span + (jnp.arange(seq) % span).astype(f32)[None, :]
        prow = pos.reshape(S, 1, seq)
        exponent = jnp.arange(ROTARY // 2, dtype=f32)
        inverse = 10000.0 ** (-2.0 * exponent / ROTARY)
        angles = prow * inverse[None, :, None]
        return jnp.concatenate([jnp.cos(angles), jnp.sin(angles), jnp.broadcast_to(prow, (S, 8, seq))], axis=1)

    table = do(positions, place)
    flying = scatter_rest(flying)

    cot_finish()
    cot_parts = cot_state["parts"]
    cot_theirs = [at.core(p) for p in cot_parts]

    qkvs, attns, attn_got, stats = [], [], [], []
    for k in range(2):
        shape = (3, heads, HEAD_DIM, H)
        qkv, attn, stat = do(attend, flying[k][0].reshape(shape), flying[k][1].reshape(shape), bias, table[seqs[k]])
        qkvs.append(qkv)
        attns.append(attn.reshape(blk, H))
        attn_got.append(at.core(attns[k]))
        stats.append(stat)
    pairs = [do(join, attns[k], attn_got[k]) for k in range(2)]
    flying = send_products(wo_cut, pairs)
    wg_cut = cut_weights(wg_parts, 1, ffb, False)
    wu_cut = cut_weights(wu_parts, 1, ffb, True)

    def gain_products(wg, wu, cols):
        terms = []
        for v in (cols[:, 2], cols[:, 3]):
            t = lax.reduce_precision(v, 8, 7)
            terms += [t, v - t]
        terms = jnp.stack(terms).astype(bf16)
        out = []
        for mine, theirs in (wg, wu):
            p = dot(terms[:, :blk], mine, LAST) + dot(terms[:, blk:], theirs, LAST)
            out.append(jnp.stack([p[0] + p[1], p[2] + p[3]]).reshape(2, Y, S, ffb))
        return jnp.concatenate(out, axis=0)

    gains = do(gain_products, wg_parts, wu_parts, pair_cols)
    gain_steps = list(at.steps(False))

    def gain_step(gains):
        axis, step = gain_steps.pop(0)
        ax = {"y": 1, "s": 2}[axis]
        bit = (at.index(axis) // step) % 2
        send = lax.dynamic_slice_in_dim(gains, (1 - bit) * step, step, ax)
        kept = lax.dynamic_slice_in_dim(gains, bit * step, step, ax)
        return kept, at.along(send, axis, step)

    flying = scatter_rest(flying)
    def residual(x, a0, b0, a1, b1):
        a, b = lanes(a0, a1), lanes(b0, b1)
        hidden = x.astype(f32) + (a.astype(f32) + b.astype(f32))
        local_mean = jnp.mean(hidden, axis=0, keepdims=True)
        dev = hidden - local_mean
        return hidden, join(local_mean, jnp.sum(dev * dev, axis=0, keepdims=True))

    hidden, moments = do(residual, x_own, *flying[0], *flying[1])
    count = blk
    for axis, step in at.steps(False) + [("core", 1)]:
        other = at.core(moments) if axis == "core" else at.along(moments, axis, step)

        def merge(a, b):
            gap = a[0:1] - b[0:1]
            return join(0.5 * (a[0:1] + b[0:1]), a[1:2] + b[1:2] + gap * gap * (count / 2.0))

        moments = do(merge, moments, other)
        count *= 2

    def second_norm(hidden, moments, cols):
        inv2 = lax.rsqrt(moments[1:2] / width + eps_norm)
        z2 = (hidden - moments[0:1]) * inv2
        return (z2 * cols[:, 2:3] + cols[:, 3:4]).astype(bf16), z2, inv2

    gains = gain_step(gains)
    xn2_own, z2, inv2 = do(second_norm, hidden, moments, own_cols)
    xn2 = do(join, xn2_own, at.core(xn2_own))

    flying = send_products([wg_cut, wu_cut], [xn2, xn2])

    wd_own = do(cast, w_down)
    wg = do(stack_turned, *wg_parts)
    wu = do(stack_turned, *wu_parts)
    cot_all = do(lambda a, b: token_rows(a, b, core), cot_parts, cot_theirs)
    grad_act = do(lambda w, c: mm(w, c, LAST, f32, tn=256), wd_own, cot_all)
    cot_cols = do(lambda c: own_columns(c, my_block.reshape(1), blk), cot_all)
    wo_own = do(cast, w_out)
    wq = do(stack_turned, *wq_parts)
    gains = do(lambda a, b: a + b, *gains)
    while gain_steps:
        gains = do(lambda a, b: a + b, *gain_step(gains))
    gains = do(lambda g: g.reshape(4, ffb).T, gains)
    flying = scatter_rest(flying)

    gate0, gate1, up0, up1, act, sums = do(gated, *flying[0], *flying[1], grad_act, gains)

    def parts_of(count, want):
        return max(n for n in range(1, want + 1) if count % (16 * n) == 0)

    def even(count, want):
        n = parts_of(count, want)
        return [(k * (count // n), count // n) for k in range(n)]

    down_rows, up_rows = even(ffb, 2), [(0, blk)]

    def push_pairs(name, g, rows):
        for k, (at_row, count) in enumerate(rows):
            reps.push((name, "theirs", k), g[blk + at_row : blk + at_row + count])
            reps.push((name, "mine", k), g[at_row : at_row + count])

    results = {"down": None, "out": None, "up": None, "qkv": None}
    states = {
        "down": (w_down, m_down, v_down),
        "out": (w_out, m_out, v_out),
        "up": (w_up, m_up, v_up),
        "qkv": (w_qkv, m_qkv, v_qkv),
    }
    rates = {"down": 0.02, "out": 0.2, "up": 0.03, "qkv": 0.03}

    def adam(name, grads, row_first, lead, unit, rb):
        results[name] = do(
            lambda s, g, prev: adam_part(s, g, core, rates[name], prev, row_first, lead, unit, rb),
            states[name],
            grads,
            results[name],
        )

    jobs = []
    for k, (at_row, count) in enumerate(down_rows):
        jobs.append(("down", [("down", k)], at_row, 0, count, 1024))
    for name, lead in (("gate", 0), ("up", Y)):
        for k, (at_row, count) in enumerate(up_rows):
            jobs.append(("up", [(name, "mine", k), (name, "theirs", k)], at_row, lead, count, S * ffb))
    for k in range(2):
        jobs.append(("out", [("out", k)], 0, k, blk, width // 2))
    for third in (2, 1, 0):
        jobs.append(("qkv", [(third, 0), (third, 1, "theirs")], 0, third * Y, blk, S * blk))
    received = {}

    def update(limit):
        for name in list(reps.done):
            if name in ("out", 0, 1, 2):
                g = reps.done.pop(name)
                half = g.shape[0] // 2
                reps.done[(name, 0)] = g[:half]
                reps.done[(name, 1) if name == "out" else (name, 1, "theirs")] = g[half:]
        for name in list(reps.done):
            if "theirs" in name and name not in received:
                received[name] = at.core(reps.done[name])
        while jobs and limit and all(k in reps.done for k in jobs[0][1]):
            name, needs, at_row, lead, count, unit = jobs.pop(0)
            rb = max(n for n in range(8, min(count, 176) + 1, 8) if count % n == 0 and at_row % n == 0)
            adam(name, [received[k] if "theirs" in k else reps.done[k] for k in needs], at_row, lead, unit, rb)
            limit -= 1

    def ticks(n):
        for _ in range(n):
            reps.tick()

    wide = 2 * FF // 8

    def quarter_heads(x):
        return [x[:, h][None, None] for h in halves]

    n, start, finish, gate_all = gather_steps([gate0[None, None], gate1[None, None]], 1)
    start(0)
    g_down = do(lambda a, c: mm(a, c, PLAIN, bf16, tn=512), act, cot_all)
    for k, (at_row, count) in enumerate(down_rows):
        reps.push(("down", k), g_down[at_row : at_row + count])
    ticks(1)

    steps2 = at.steps(False) + [("core", 1)]

    def sum_send(sums, axis, step):
        return at.core(sums) if axis == "core" else at.along(sums, axis, step)

    def sum_step(sums, axis, step):
        return do(lambda a, b: a + b, sums, sum_send(sums, axis, step))

    tiny = list(steps2)
    sums_got = sum_send(sums, *tiny.pop(0))
    for i in range(1, n):
        finish()
        sums = do(lambda a, b: a + b, sums, sums_got)
        sums_got = sum_send(sums, *tiny.pop(0))
        start(i, sums)
        ticks(1)
    n, start_up, finish_up, up_all = gather_steps([up0[None, None], up1[None, None]], 1)
    ggate_all = gate_all().reshape(Y * S * ffb, T)
    sums = do(lambda a, b: a + b, sums, sums_got)
    start_up(0, sums)
    while tiny:
        sums = sum_step(sums, *tiny.pop(0))
    g_gate = do(lambda x, g: mm(x, g, LAST, bf16, tn=wide), xn2, ggate_all)
    push_pairs("gate", g_gate, up_rows)
    finish_up()
    for i in range(1, n):
        start_up(i)
        if i == 1:
            part_gate = do(lambda w, g: mm(w, g, PLAIN, f32, tn=256), wg, ggate_all)
            out_part = do(lambda w, a: mm(w, a, FIRST, bf16, tm=512), wd_own, act)
            ticks(1)
        if i < n - 1:
            finish_up()
    gup_all = up_all().reshape(Y * S * ffb, T)
    part = do(lambda w, g, p: dot(w, g, PLAIN) + p, wu, gup_all, part_gate)
    part_theirs = at.core(part[blk:])

    def branch(a, b, cot, z, scale, gain, sums):
        gxn2 = a + b
        e = gxn2 * gain
        grad_hidden = cot.astype(f32) + scale * (e - sums[0:1] / width - z * (sums[1:2] / width))
        return grad_hidden.astype(bf16), grad_hidden, gxn2

    grad_branch, grad_hidden, gxn2 = do(
        branch, part[:blk], part_theirs, cot_cols, z2, inv2, own_cols[:, 2:3], sums
    )
    n, start, finish, branch_all = gather_steps(quarter_heads(grad_branch), 1)
    start(0)
    g_up = do(lambda x, g: mm(x, g, LAST, bf16, tn=wide), xn2, gup_all)
    push_pairs("up", g_up, up_rows)
    finish()
    for i in range(1, n):
        start(i)
        if i == 1:
            ticks(1)
        if i < n - 1:
            finish()
    gbr_c = branch_all()[0]
    gbr_o = at.core(gbr_c)
    gbr = do(lambda a, b: in_order(a, b, 1).reshape(width, T), gbr_c, gbr_o)
    grad_attn = do(lambda w, g: dot(w, g, PLAIN).astype(bf16), wo_own, gbr)

    gqkvs = []
    for k in range(2):
        dout = grad_attn[:, halves[k]].reshape(heads, HEAD_DIM, H)
        gqkvs.append(do(attend_back, qkvs[k], dout, stats[k], table[seqs[k]]).reshape(3, blk, H))
    n, start, finish, gqkv_done = gather_steps([g.reshape(1, 1, 3 * blk, H) for g in gqkvs], 3)
    start(0)
    attn = lanes(*attns)
    g_out = do(
        lambda a, g: join(*[mm(a, g[k * width // 2 : (k + 1) * width // 2], LAST, bf16, tn=512) for k in range(2)]),
        attn,
        gbr,
    )
    reps.push("out", g_out)
    update(1)
    ticks(1)
    finish()
    for i in range(1, n):
        start(i)
        if i == 1:
            update(1)
            ticks(1)
        if i < n - 1:
            finish()
    gqkv = gqkv_done().reshape(3, Y * S * blk, T)
    out_split = out_part.reshape(Y, 2, S * blk, T)
    out_kept = pick(out_split, 1, at.c).reshape(-1, T)
    out_got = at.core(pick(out_split, 1, 1 - at.c).reshape(-1, T))

    def out_step(axis, step):
        bit = (at.index(axis) // step) % 2
        send, kept = do(lambda a, b: add_split(a, b, bit.reshape(1)), out_kept, out_got)
        return kept, at.along(send, axis, step)

    out_steps = at.steps(True)
    g = do(lambda x, g: mm(x, g, LAST, bf16, tn=512), xn1, gqkv[2])
    reps.push(2, g)
    ticks(1)
    for third in (1, 0):
        g = do(lambda x, g: mm(x, g, LAST, bf16, tn=512), xn1, gqkv[third])
        reps.push(third, g)
    part = do(lambda w, g: mm(w, g, PLAIN, f32, tn=256), wq, gqkv.reshape(3 * Y * S * blk, T))
    part_theirs = at.core(part[blk:])
    ticks(1)

    def first_back(a, b, x, mean, inv, gain, gxn2, z2, gqkv0, gqkv1):
        gxn1 = a + b
        z1 = (x.astype(f32) - mean) * inv
        e = gxn1 * gain
        sums = join(jnp.sum(e, axis=0, keepdims=True), jnp.sum(e * z1, axis=0, keepdims=True))
        small = jnp.concatenate(
            [
                jnp.sum(gxn1 * z1, axis=1)[None],
                jnp.sum(gxn1, axis=1)[None],
                jnp.sum(gxn2 * z2, axis=1)[None],
                jnp.sum(gxn2, axis=1)[None],
                jnp.sum(gqkv0.astype(f32), axis=2) + jnp.sum(gqkv1.astype(f32), axis=2),
            ],
            axis=0,
        )
        return sums, small, gxn1, z1

    sums, small, gxn1, z1 = do(
        first_back, part[:blk], part_theirs, x_own, mean1, inv1, own_cols[:, 0:1], gxn2, z2, *gqkvs
    )
    for axis, step in steps2:
        sums = sum_step(sums, axis, step)
    input_grad = do(
        lambda h, grad, z, scale, gain, sums: (
            h + scale * (grad * gain - sums[0:1] / width - z * (sums[1:2] / width))
        ).astype(bf16),
        grad_hidden,
        gxn1,
        z1,
        inv1,
        own_cols[:, 0:1],
        sums,
    )

    def to_rows(cols):
        split = do(lambda c: c.reshape(blk, S, at.ctx_size, rows).transpose(2, 1, 0, 3).reshape(nb, blk, rows), cols)
        got = lax.all_to_all(split, plane, split_axis=0, concat_axis=0, tiled=True)
        return do(lambda g: g.reshape(width, rows).T, got)

    input_rows = to_rows(input_grad).astype(f32)
    steps_rep = []
    step = 1
    while step < lax.axis_size("rep"):
        steps_rep.append(step)
        step *= 2

    def small_step():
        nonlocal small
        small = getattr(reps, "kept", small)
        k = steps_rep.pop(0)
        other = lax.ppermute(small, "rep", [(i, i ^ k) for i in range(lax.axis_size("rep"))])
        small = do(lambda a, b: a + b, small, other)
        return small

    reps.tick(small_step)
    out_kept, out_got = out_step(*out_steps[0])
    update(1)
    for axis, step in out_steps[1:]:
        out_kept, out_got = out_step(axis, step)
    reps.tick(small_step)
    sent = do(lambda s: jnp.broadcast_to(s.reshape(1, 7, blk), (nb, 7, blk)), reps.kept)
    small_all = lax.all_to_all(sent, plane, split_axis=0, concat_axis=0, tiled=True)

    def norm_update(every, *a):
        return adam_update(*a, every.transpose(1, 0, 2).reshape(7, width), 0.3, 0.0)

    mn, vn, wn = do(norm_update, small_all, norm_params, m_norm, v_norm)
    update(1)
    ticks(1)
    update(2)
    out_cols = do(
        lambda h, a, b: (h + (a.astype(f32) + b.astype(f32))).astype(bf16), hidden, out_kept, out_got
    )
    block_output = to_rows(out_cols)
    update(2)
    while reps.busy():
        reps.tick()
        update(2)
    update(len(jobs))
    return (
        (block_output.reshape(tokens.shape), input_rows.reshape(tokens.shape))
        + tuple(results["qkv"])
        + tuple(results["out"])
        + tuple(results["up"])
        + tuple(results["down"])
        + (mn, vn, wn)
    )


def solution(mesh):
    tok = P("rep", "ctx", "shard", None)
    row = P(("ctx", "shard"), None)
    placed = (tok, tok, P("rep", "shard", None)) + (row,) * 4 + (P(),) + (row,) * 8 + (P(), P())
    return jax.shard_map(
        body,
        mesh=mesh,
        in_specs=placed,
        out_specs=(tok, tok) + (row,) * 12 + (P(),) * 3,
        check_vma=False,
    )
```
